32 devices in a mesh: shard: 2 (over x), ctx: 4 (over z), tp: 4 (over y, core).
Axes of the slice: x: 2, y: 2, z: 4, core: 2. Of those that a mesh axis runs over, the one named last changes fastest.
Arguments:
- tokens: bfloat16 [2, 2560, 1024], P('shard', 'ctx'), may hold values from -6 to 6
- block_tokens: int32 [2, 4], P('shard'), may hold values from 1 to 640, 2048 in all within a row
- ln1_gain: bfloat16 [2, 1024], replicated, may hold values from 0.099609375 to 1.8984375
- ln1_bias: bfloat16 [2, 1024], replicated, may hold values from -1.5 to 1.5
- w_qkv: bfloat16 [2, 1024, 3072], P(None, ('shard', 'ctx'), 'tp'), may hold values from -0.1875 to 0.1875
- b_qv: bfloat16 [2, 2048], P(None, 'tp'), may hold values from -1.5 to 1.5
- w_out: bfloat16 [2, 1024, 1024], P(None, ('shard', 'ctx'), 'tp'), may hold values from -6 to 6
- b_out: bfloat16 [2, 1024], replicated, may hold values from -1.5 to 1.5
- ln2_gain: bfloat16 [2, 1024], replicated, may hold values from 0.099609375 to 1.8984375
- ln2_bias: bfloat16 [2, 1024], replicated, may hold values from -1.5 to 1.5
- w_up: bfloat16 [2, 1024, 4096], P(None, ('shard', 'ctx'), 'tp'), may hold values from -0.1875 to 0.1875
- b_up: bfloat16 [2, 4096], P(None, 'tp'), may hold values from -1.5 to 1.5
- w_down: bfloat16 [2, 1024, 4096], P(None, ('shard', 'ctx'), 'tp'), may hold values from -0.09375 to 0.09375
- b_down: bfloat16 [2, 1024], replicated, may hold values from -1.5 to 1.5
- cotangent: bfloat16 [2, 2560, 1024], P('shard', 'ctx'), may hold values from -6 to 6
Outputs:
- mixed: bfloat16 [2, 2560, 1024], P('shard', 'ctx')
- token_grads: float32 [2, 2560, 1024], P('shard', 'ctx')
- ln1_gain_grad: float32 [2, 1024], replicated
- ln1_bias_grad: float32 [2, 1024], replicated
- qkv_grad: float32 [2, 1024, 3072], P(None, ('shard', 'ctx'), 'tp')
- qv_bias_grad: float32 [2, 2048], P(None, 'tp')
- out_grad: float32 [2, 1024, 1024], P(None, ('shard', 'ctx'), 'tp')
- out_bias_grad: float32 [2, 1024], replicated
- ln2_gain_grad: float32 [2, 1024], replicated
- ln2_bias_grad: float32 [2, 1024], replicated
- up_grad: float32 [2, 1024, 4096], P(None, ('shard', 'ctx'), 'tp')
- up_bias_grad: float32 [2, 4096], P(None, 'tp')
- down_grad: float32 [2, 1024, 4096], P(None, ('shard', 'ctx'), 'tp')
- down_bias_grad: float32 [2, 1024], replicated
The draws below stay inside these ranges and needn't reach their ends.
Inputs may be any that keep to these rules, and one draw needn't show every extreme that they name: block_tokens[i, j] live tokens stand first in the j-th block of 640 slots of image i, the rest of that block is empty; the blocks of an image hold 2048 live tokens together, and one block of each image holds exactly 640.
All inputs are finite; a program needn't handle non-finite values.
Results may differ from the reference program's by a relative error of at most 0.019.
Values may be sent and summed in bfloat16 or wider, within the bound.
A program may use at most 192 MiB of HBM per device.

```python
import math
import jax
import jax.numpy as jnp
import numpy as np
from jax import lax

D = 1024
FF = 4096
HEADS = 16
HEAD_DIM = 64
LAYERS = 2
CAP = 640
IMAGES = 2
SLOTS = 2560
SEQ = 2048
N_CTX = 4


def block_levels(rng, extent, split, least, high):
    level = 1.0
    for position, shards_of in split:
        heights = jax.random.uniform(jax.random.fold_in(jax.random.fold_in(rng, 6), position), (shards_of,), jnp.float32, least / len(split), high / len(split))
        level = level * jnp.repeat(jnp.exp(heights), extent[position] // shards_of).reshape((-1,) + (1,) * (len(extent) - 1 - position))
    return level


def split_up(amount, total, bound, skew):
    weights = [(1 << 20) // math.isqrt(standing ** skew) + 1 for standing in range(2, amount + 1)]
    surplus, holding = total - bound - (amount - 1), [1] * (amount - 1)
    while surplus > 0:
        free = [i for i in range(amount - 1) if holding[i] < bound]
        mass, budget = sum([weights[i] for i in free]), surplus
        for i in free:
            more = min(bound - holding[i], max(1, budget * weights[i] // mass), surplus)
            holding[i] = holding[i] + more
            surplus = surplus - more
    return np.array([bound] + holding)


def uneven_parts(stream_key, amount, total, most, lean):
    if amount == 2:
        one = jax.random.randint(stream_key, (), max(1, total - most), min(most, total - 1) + 1)
        return jnp.stack([one, total - one])
    lengths = jnp.asarray(split_up(amount, total, most, lean), jnp.int32)
    twos = (amount - 1) // 2
    source_of, receiver = lengths[1:1 + 2 * twos:2], lengths[2:2 + 2 * twos:2]
    slack = jnp.minimum(source_of - 1, most - receiver)
    shifted = jax.random.randint(jax.random.fold_in(stream_key, 1), (twos,), 0, 1 << 20) % (slack + 1)
    lengths = lengths.at[1:1 + 2 * twos:2].set(source_of - shifted).at[2:2 + 2 * twos:2].set(receiver + shifted)
    return lengths[jax.random.permutation(jax.random.fold_in(stream_key, 2), amount)]


def noise(rng, shape, scale, reach, pieces=(), dtype=jnp.bfloat16):
    drawn = scale * jax.random.normal(rng, shape, jnp.float32)
    if pieces:
        drawn = drawn * block_levels(rng, shape, pieces, -0.22, 0.18)
    return jnp.clip(drawn, -reach, reach).astype(dtype)


def setup_inputs(seed: int = 0) -> dict:
    splits = jax.random.split(jax.random.key(seed), 16)
    return {
        "tokens": noise(splits[0], (IMAGES, SLOTS, D), 1.0, 6.0, ((0, 2), (1, 4))),
        "block_tokens": jax.vmap(lambda own: uneven_parts(own, N_CTX, SEQ, CAP, 1))(jax.random.split(splits[1], IMAGES)).reshape((IMAGES, N_CTX)).astype(jnp.int32),
        "ln1_gain": jnp.clip(1.0 + 0.18 * jax.random.normal(splits[2], (LAYERS, D), jnp.float32), 0.099609375, 1.8984375).astype(jnp.bfloat16),
        "ln1_bias": noise(splits[3], (LAYERS, D), 0.3, 1.5),
        "w_qkv": noise(splits[4], (LAYERS, D, 3 * D), D ** -0.5, 0.1875, ((1, 8), (2, 4))),
        "b_qv": noise(splits[5], (LAYERS, 2 * D), 0.3, 1.5, ((1, 4),)),
        "w_out": noise(splits[6], (LAYERS, D, D), (max(1, 3 * D // SEQ)) ** -0.5, 6.0, ((1, 8), (2, 4))),
        "b_out": noise(splits[7], (LAYERS, D), 0.3, 1.5),
        "ln2_gain": jnp.clip(1.0 + 0.18 * jax.random.normal(splits[8], (LAYERS, D), jnp.float32), 0.099609375, 1.8984375).astype(jnp.bfloat16),
        "ln2_bias": noise(splits[9], (LAYERS, D), 0.3, 1.5),
        "w_up": noise(splits[10], (LAYERS, D, FF), D ** -0.5, 0.1875, ((1, 8), (2, 4))),
        "b_up": noise(splits[11], (LAYERS, FF), 0.3, 1.5, ((1, 4),)),
        "w_down": noise(splits[12], (LAYERS, D, FF), FF ** -0.5, 0.09375, ((1, 8), (2, 4))),
        "b_down": noise(splits[13], (LAYERS, D), 0.3, 1.5),
        "cotangent": noise(splits[14], (IMAGES, SLOTS, D), 1.0, 6.0, ((0, 2), (1, 4))),
    }


@jax.custom_vjp
def low(v):
    return lax.optimization_barrier(v.astype(jnp.bfloat16)).astype(jnp.float32)

@jax.custom_vjp
def low_back(v):
    return v

def low_keep(v):
    return (low(v), None)

def low_pass(kept, grad):
    return (grad,)

def back_keep(v):
    return (v, None)

def back_low(kept, grad):
    return (low(grad),)
low.defvjp(low_keep, low_pass)
low_back.defvjp(back_keep, back_low)
EPSILON = 1e-06
NEG_LARGE = -1e+30

def product(left, right):
    return jnp.matmul(left, right, precision=lax.Precision.HIGHEST)

def normalize(rows, gain, shift):
    row_mean = lax.optimization_barrier(jnp.mean(rows, axis=-1, keepdims=True))
    centred = rows - row_mean
    variance = lax.optimization_barrier(jnp.mean(centred * centred, axis=-1, keepdims=True))
    return centred * lax.rsqrt(variance + EPSILON) * gain + shift

def head_attend(queries, key_rows, values, live_keys):
    scores = low_back(product(queries, key_rows.T) * HEAD_DIM ** (-0.5))
    scores = jnp.where(live_keys[None, :], scores, NEG_LARGE)
    probability = jax.nn.softmax(scores, axis=-1)
    return product(low(probability), values)

def image_attend(joint_proj, live_keys):
    attend_one = jax.checkpoint(head_attend)
    split_heads = joint_proj.reshape(SLOTS, HEADS, 3, HEAD_DIM).transpose(2, 1, 0, 3)

    def single_head(triple):
        return attend_one(triple[0], triple[1], triple[2], live_keys)
    heads_out = lax.map(single_head, (split_heads[0], split_heads[1], split_heads[2]))
    return heads_out.transpose(1, 0, 2).reshape(SLOTS, HEADS * HEAD_DIM)

def residual_block(stream, live_keys, weights_all):
    ln1_gain, ln1_bias, w_qkv, b_qv, w_out, b_out, ln2_gain, ln2_bias, w_up, b_up, w_down, b_down = weights_all
    norm_first = low(normalize(stream, ln1_gain, ln1_bias))
    bias_pairs = b_qv.reshape(HEADS, 2, HEAD_DIM)
    joint_bias = jnp.stack([bias_pairs[:, 0], jnp.zeros_like(bias_pairs[:, 0]), bias_pairs[:, 1]], axis=1).reshape(3 * D)
    joint_proj = low_back(low(product(norm_first, w_qkv) + joint_bias))
    attended = lax.map(lambda entry: image_attend(entry[0], entry[1]), (joint_proj, live_keys))
    attended = low_back(low(attended))
    middle = stream + low_back(product(attended, w_out.T) + b_out)
    second = low(normalize(middle, ln2_gain, ln2_bias))
    hidden_pre = low_back(product(second, w_up) + b_up)
    hidden = low(jax.nn.gelu(hidden_pre, approximate=False))
    return middle + low_back(product(hidden, w_down.T) + b_down)

def reference(tokens, block_tokens, ln1_gain, ln1_bias, w_qkv, b_qv, w_out, b_out, ln2_gain, ln2_bias, w_up, b_up, w_down, b_down, cotangent):
    slot_index = jnp.arange(SLOTS).astype(jnp.int32)
    owners = (slot_index // CAP).astype(jnp.int32)
    within = slot_index - owners * CAP
    picked = owners[:, None] == jnp.arange(N_CTX).astype(jnp.int32)[None, :]
    live_count = lax.optimization_barrier(jnp.sum(jnp.where(picked[None, :, :], block_tokens[:, None, :], 0), axis=2))
    live_keys = within[None, :] < live_count
    row_mask = live_keys.astype(jnp.float32)[:, :, None]
    weights_all = tuple((weight.astype(jnp.float32) for weight in (ln1_gain, ln1_bias, w_qkv, b_qv, w_out, b_out, ln2_gain, ln2_bias, w_up, b_up, w_down, b_down)))

    def forward(stream, weight_set):
        for layer_index in range(LAYERS):
            stream = residual_block(stream, live_keys, tuple((weight[layer_index] for weight in weight_set)))
        return stream * row_mask
    result, pullback = jax.vjp(forward, tokens.astype(jnp.float32), weights_all)
    token_grads, grads = pullback(cotangent.astype(jnp.float32))
    return (result.astype(jnp.bfloat16), token_grads, grads[0], grads[1], grads[2], grads[3], grads[4], grads[5], grads[6], grads[7], grads[8], grads[9], grads[10], grads[11])
```

```python
import functools
import math

import jax
import jax.numpy as jnp
from jax import lax
from jax.experimental import pallas as pl
from jax.experimental.pallas import tpu as pltpu
from jax.sharding import PartitionSpec as P

HEAD_DIM = 64
EPSILON = 1e-06
NEG_LARGE = -1e30
LOW = jnp.bfloat16
FULL = jnp.float32
PAD = 128


def bits_of(axis):
    size = lax.axis_size(axis)
    assert size & (size - 1) == 0
    return [1 << i for i in range(size.bit_length() - 1)]


def swap(value, axis, bit):
    size = lax.axis_size(axis)
    return lax.ppermute(value, axis, [(i, i ^ bit) for i in range(size)])


def side_of(axis, bit):
    return (lax.axis_index(axis) // bit) % 2


def rows_of(value, start, count, axis=0):
    return lax.dynamic_slice_in_dim(value, start, count, axis)


def halve(axis, bits, partial, total):
    offset, span, received = jnp.int32(0), total, []

    def summed(start, count):
        value = partial(start, count)
        for got, base in received:
            value = value + rows_of(got, start - base, count).astype(FULL)
        return value

    for bit in bits:
        half = span // 2
        side = side_of(axis, bit)
        got = swap(summed(offset + (1 - side) * half, half).astype(LOW), axis, bit)
        offset = offset + side * half
        received.append((got, offset))
        span = half
    return summed(offset, span)


def double(axis, bits, value):
    for bit in bits:
        got = swap(value, axis, bit)
        first = side_of(axis, bit) == 0
        value = jnp.concatenate(
            [jnp.where(first, value, got), jnp.where(first, got, value)], axis=0
        )
    return value


def tp_scatter(partial, total):
    return halve("tp", bits_of("tp"), partial, total)


def tp_gather(value):
    return double("tp", bits_of("tp")[::-1], value)


def tp_offset(total):
    offset, span = jnp.int32(0), total
    for bit in bits_of("tp"):
        span = span // 2
        offset = offset + side_of("tp", bit) * span
    return offset, span


def total_over(axes, value):
    for axis in axes:
        for bit in bits_of(axis):
            value = value + swap(value, axis, bit)
    return value


def gather_weight(piece):
    count = lax.axis_size("ctx")
    place = lax.axis_index("ctx")
    right, left = [piece], [piece]
    for step in range(1, count):
        right.append(
            lax.ppermute(right[-1], "ctx", [(i, i + 1) for i in range(step - 1, count - 1)])
        )
        left.append(
            lax.ppermute(left[-1], "ctx", [(i, i - 1) for i in range(1, count - step + 1)])
        )
    whole = jnp.zeros((count,) + piece.shape, piece.dtype)
    whole = lax.dynamic_update_index_in_dim(whole, piece, place, 0)
    for step in range(1, count):
        block = jnp.where(place >= step, right[step], left[count - step])
        whole = lax.dynamic_update_index_in_dim(whole, block, (place - step) % count, 0)
    whole = whole.reshape((count * piece.shape[0],) + piece.shape[1:])
    return double("shard", bits_of("shard"), whole)


def scatter_weight(partial, total):
    count = lax.axis_size("ctx")
    place = lax.axis_index("ctx")
    mine = halve("shard", bits_of("shard")[::-1], partial, total).astype(LOW)
    mine = mine.reshape((count, mine.shape[0] // count) + mine.shape[1:])

    def block(index):
        return lax.dynamic_index_in_dim(mine, jnp.clip(index, 0, count - 1), 0, False)

    from_left = from_right = None
    for step in range(1, count):
        to_right = block(place + count - step)
        to_left = block(place - count + step)
        if from_left is not None:
            to_right = (to_right.astype(FULL) + from_left.astype(FULL)).astype(LOW)
            to_left = (to_left.astype(FULL) + from_right.astype(FULL)).astype(LOW)
        from_left = lax.ppermute(to_right, "ctx", [(i, i + 1) for i in range(step)])
        from_right = lax.ppermute(
            to_left, "ctx", [(i, i - 1) for i in range(count - step, count)]
        )
    return block(place).astype(FULL) + from_left.astype(FULL) + from_right.astype(FULL)


def heads_out(parts):
    count = lax.axis_size("ctx")
    place = lax.axis_index("ctx")
    got = [lax.dynamic_index_in_dim(parts, place, 0, False)]
    for by in range(1, count):
        given = lax.dynamic_index_in_dim(parts, (place + by) % count, 0, False)
        got.append(lax.ppermute(given, "ctx", [(i, (i + by) % count) for i in range(count)]))
    return got


def heads_back(parts):
    count = lax.axis_size("ctx")
    place = lax.axis_index("ctx")
    whole = jnp.zeros((count,) + parts[0].shape, parts[0].dtype)
    whole = lax.dynamic_update_index_in_dim(whole, parts[0], place, 0)
    for by in range(1, count):
        got = lax.ppermute(parts[by], "ctx", [(i, (i - by) % count) for i in range(count)])
        whole = lax.dynamic_update_index_in_dim(whole, got, (place + by) % count, 0)
    return whole


def dot(left, right, contract):
    return lax.dot_general(
        left, right, ((contract[0], contract[1]), ((), ())), preferred_element_type=FULL
    )


def turned(value):
    return value.astype(FULL).T.astype(LOW)


def attend_kernel(tile, size, qkv_ref, bias_ref, o_ref, olow_ref, lse_ref, k_ref):
    step = pl.program_id(0)
    slots = qkv_ref.shape[1]

    @pl.when(step == 0)
    def _():
        keys = jnp.concatenate(
            [
                qkv_ref[size : 2 * size, :],
                bias_ref[...],
                jnp.zeros((PAD - size - 16, slots), LOW),
            ],
            axis=0,
        )
        k_ref[...] = turned(keys)

    here = pl.ds(pl.multiple_of(step * tile, tile), tile)
    queries = jnp.concatenate(
        [
            (qkv_ref[0:size, here] * (size**-0.5)).astype(LOW),
            jnp.ones((16, tile), LOW),
            jnp.zeros((PAD - size - 16, tile), LOW),
        ],
        axis=0,
    )
    scores = jnp.dot(k_ref[...], queries, preferred_element_type=FULL)
    top = jnp.max(scores, axis=0, keepdims=True)
    weights = jnp.exp(scores - top)
    total = jnp.sum(weights, axis=0, keepdims=True)
    summed = jnp.dot(
        qkv_ref[2 * size : 3 * size, :], weights.astype(LOW), preferred_element_type=FULL
    )
    out = summed / total
    o_ref[...] = out
    olow_ref[...] = out.astype(LOW)
    lse_ref[...] = jnp.broadcast_to(top + jnp.log(total), lse_ref.shape)


def attend(qkv, bias, size):
    slots = qkv.shape[1]
    tile = 256 if slots % 256 == 0 else PAD
    return pl.pallas_call(
        functools.partial(attend_kernel, tile, size),
        grid=(slots // tile,),
        in_specs=[
            pl.BlockSpec((3 * size, slots), lambda i: (0, 0)),
            pl.BlockSpec((16, slots), lambda i: (0, 0)),
        ],
        out_specs=[
            pl.BlockSpec((size, tile), lambda i: (0, i)),
            pl.BlockSpec((size, tile), lambda i: (0, i)),
            pl.BlockSpec((8, tile), lambda i: (0, i)),
        ],
        out_shape=[
            jax.ShapeDtypeStruct((size, slots), FULL),
            jax.ShapeDtypeStruct((size, slots), LOW),
            jax.ShapeDtypeStruct((8, slots), FULL),
        ],
        scratch_shapes=[pltpu.VMEM((slots, PAD), LOW)],
        compiler_params=pltpu.CompilerParams(
            dimension_semantics=("arbitrary",), vmem_limit_bytes=32 * 2**20
        ),
        cost_estimate=pl.CostEstimate(
            flops=2 * slots * slots * 256 * 2,
            bytes_accessed=slots * size * 16,
            transcendentals=slots * slots,
        ),
        name="attend",
    )(qkv, bias)


def attend_back_kernel(
    tile, size, qkv_ref, bias_ref, o_ref, lse_ref, do_ref, dqkv_ref, k_ref, v_ref, dk_ref, dv_ref
):
    step = pl.program_id(0)
    slots = qkv_ref.shape[1]

    @pl.when(step == 0)
    def _():
        keys = jnp.concatenate(
            [
                qkv_ref[size : 2 * size, :],
                bias_ref[...],
                jnp.zeros((PAD - size - 16, slots), LOW),
            ],
            axis=0,
        )
        k_ref[...] = turned(keys)
        v_ref[...] = turned(
            jnp.concatenate(
                [qkv_ref[2 * size : 3 * size, :], jnp.zeros((PAD - size, slots), LOW)], axis=0
            )
        )
        dk_ref[...] = jnp.zeros_like(dk_ref)
        dv_ref[...] = jnp.zeros_like(dv_ref)

    here = pl.ds(pl.multiple_of(step * tile, tile), tile)
    scaled = (qkv_ref[0:size, here] * (size**-0.5)).astype(LOW)
    queries = jnp.concatenate(
        [scaled, jnp.ones((16, tile), LOW), jnp.zeros((PAD - size - 16, tile), LOW)], axis=0
    )
    dout = jnp.concatenate([do_ref[:, here], jnp.zeros((PAD - size, tile), LOW)], axis=0)
    delta = jnp.sum(do_ref[:, here].astype(FULL) * o_ref[:, here], axis=0, keepdims=True)
    scores = jnp.dot(k_ref[...], queries, preferred_element_type=FULL)
    chance = jnp.exp(scores - lse_ref[0:1, here])
    chance_grad = jnp.dot(v_ref[...], dout, preferred_element_type=FULL)
    score_grad = (chance * (chance_grad - delta)).astype(LOW)
    query_grad = jnp.dot(qkv_ref[size : 2 * size, :], score_grad, preferred_element_type=FULL)
    dqkv_ref[0:size, here] = (query_grad * (size**-0.5)).astype(LOW)
    plain_q = turned(jnp.concatenate([scaled, jnp.zeros((PAD - size, tile), LOW)], axis=0))
    dk_ref[...] += jnp.dot(score_grad, plain_q, preferred_element_type=FULL)
    dv_ref[...] += jnp.dot(chance.astype(LOW), turned(dout), preferred_element_type=FULL)

    @pl.when(step == pl.num_programs(0) - 1)
    def _():
        dqkv_ref[size : 2 * size, :] = dk_ref[...].T[0:size].astype(LOW)
        dqkv_ref[2 * size : 3 * size, :] = dv_ref[...].T[0:size].astype(LOW)


def attend_back(qkv, bias, out, lse, dout, size):
    slots = qkv.shape[1]
    tile = 256 if slots % 256 == 0 else PAD
    return pl.pallas_call(
        functools.partial(attend_back_kernel, tile, size),
        grid=(slots // tile,),
        in_specs=[
            pl.BlockSpec((3 * size, slots), lambda i: (0, 0)),
            pl.BlockSpec((16, slots), lambda i: (0, 0)),
            pl.BlockSpec((size, slots), lambda i: (0, 0)),
            pl.BlockSpec((8, slots), lambda i: (0, 0)),
            pl.BlockSpec((size, slots), lambda i: (0, 0)),
        ],
        out_specs=pl.BlockSpec((3 * size, slots), lambda i: (0, 0)),
        out_shape=jax.ShapeDtypeStruct((3 * size, slots), LOW),
        scratch_shapes=[
            pltpu.VMEM((slots, PAD), LOW),
            pltpu.VMEM((slots, PAD), LOW),
            pltpu.VMEM((slots, PAD), FULL),
            pltpu.VMEM((slots, PAD), FULL),
        ],
        compiler_params=pltpu.CompilerParams(
            dimension_semantics=("arbitrary",), vmem_limit_bytes=40 * 2**20
        ),
        cost_estimate=pl.CostEstimate(
            flops=2 * slots * slots * 256 * 5,
            bytes_accessed=slots * size * 24,
            transcendentals=slots * slots,
        ),
        name="attend_back",
    )(qkv, bias, out, lse, dout)


def normalize(rows, gain, shift):
    row_mean = jnp.mean(rows, axis=-1, keepdims=True)
    centred = rows - row_mean
    inverse = lax.rsqrt(jnp.mean(centred * centred, axis=-1, keepdims=True) + EPSILON)
    normed = centred * inverse
    return (normed * gain + shift, normed, inverse)


def normalize_back(grad_out, normed, inverse, gain):
    scaled = grad_out * gain
    mean_grad = jnp.mean(scaled, axis=-1, keepdims=True)
    mean_cross = jnp.mean(scaled * normed, axis=-1, keepdims=True)
    return inverse * (scaled - mean_grad - normed * mean_cross)


def gelu_pair(value):
    spread = 0.5 * (1.0 + lax.erf(value * (0.5**0.5)))
    slope = spread + value * jnp.exp(-0.5 * value * value) * (1.0 / math.sqrt(2.0 * math.pi))
    return (value * spread).astype(LOW), slope.astype(LOW)


def shards(
    tokens,
    block_tokens,
    ln1_gain,
    ln1_bias,
    w_qkv,
    b_qv,
    w_out,
    b_out,
    ln2_gain,
    ln2_bias,
    w_up,
    b_up,
    w_down,
    b_down,
    cotangent,
):
    images, capacity, width = tokens.shape
    assert images == 1
    layers = w_qkv.shape[0]
    size = HEAD_DIM
    ctx_count = lax.axis_size("ctx")
    ctx_place = lax.axis_index("ctx")
    joint_width = w_qkv.shape[2]
    heads = joint_width // (3 * size)
    assert heads == ctx_count
    attn_width = heads * size
    hidden_width = w_up.shape[2]
    offset, span = tp_offset(capacity)

    lengths = block_tokens[0]
    order = (ctx_place - jnp.arange(ctx_count, dtype=jnp.int32)) % ctx_count
    ordered = jnp.sum(
        jnp.where(
            order[:, None] == jnp.arange(ctx_count, dtype=jnp.int32)[None, :], lengths[None, :], 0
        ),
        axis=1,
    )
    usable = jnp.arange(capacity, dtype=jnp.int32)[None, :] < ordered[:, None]
    bias_row = jnp.where(usable, 0.0, NEG_LARGE).astype(LOW).reshape(1, ctx_count * capacity)
    bias = jnp.concatenate([bias_row, jnp.zeros((15, ctx_count * capacity), LOW)], axis=0)
    own_live = ordered[0]
    row_mask = (jnp.arange(capacity, dtype=jnp.int32) < own_live).astype(FULL)[:, None]
    own_mask = rows_of(row_mask, offset, span)

    gathered = []
    for layer in range(layers):
        rest = jnp.concatenate([w_out[layer], w_up[layer], w_down[layer]], axis=1)
        qkv_full = gather_weight(w_qkv[layer])
        rest_full = gather_weight(rest)
        gathered.append(
            (
                qkv_full,
                rest_full[:, :attn_width],
                rest_full[:, attn_width : attn_width + hidden_width],
                rest_full[:, attn_width + hidden_width :],
            )
        )

    whole_stream = tokens[0].astype(FULL)
    stream = rows_of(whole_stream, offset, span)
    saved = []
    for layer in range(layers):
        qkv_full, out_full, up_full, down_full = gathered[layer]
        gain1, shift1 = ln1_gain[layer].astype(FULL), ln1_bias[layer].astype(FULL)
        gain2, shift2 = ln2_gain[layer].astype(FULL), ln2_bias[layer].astype(FULL)
        if layer == 0:
            first = normalize(whole_stream, gain1, shift1)[0].astype(LOW)
        else:
            first = tp_gather(normalize(stream, gain1, shift1)[0].astype(LOW))
        pair = b_qv[layer].astype(FULL).reshape(heads, 2, size)
        joint_bias = jnp.stack(
            [pair[:, 0], jnp.zeros_like(pair[:, 0]), pair[:, 1]], axis=1
        ).reshape(joint_width, 1)
        joint = (dot(qkv_full, first, ((0,), (1,))) + joint_bias).astype(LOW)
        joint = joint.reshape(heads, 3 * size, capacity)
        qkv = jnp.concatenate(heads_out(joint), axis=1)
        head_out, head_low, lse = attend(qkv, bias, size)
        mixed_heads = heads_back(
            [head_low[:, r * capacity : (r + 1) * capacity] for r in range(ctx_count)]
        ).reshape(attn_width, capacity)

        def out_part(start, count, mixed_heads=mixed_heads, out_full=out_full):
            return dot(rows_of(mixed_heads, start, count, 1), out_full, ((0,), (1,)))

        middle = stream + tp_scatter(out_part, capacity) + b_out[layer].astype(FULL)
        second = tp_gather(normalize(middle, gain2, shift2)[0].astype(LOW))
        hidden_pre = dot(second, up_full, ((1,), (0,))) + b_up[layer].astype(FULL)
        hidden, slope = gelu_pair(hidden_pre)

        def down_part(start, count, hidden=hidden, down_full=down_full):
            return dot(rows_of(hidden, start, count), down_full, ((1,), (1,)))

        saved.append((stream, first, qkv, head_out, lse, mixed_heads, middle, second, hidden, slope))
        stream = middle + tp_scatter(down_part, capacity) + b_down[layer].astype(FULL)

    mixed = tp_gather((stream * own_mask).astype(LOW))[None]
    whole_grad = cotangent[0].astype(FULL) * row_mask
    stream_grad = rows_of(whole_grad, offset, span)
    weight_parts = [None] * layers
    small_parts = [None] * layers
    for layer in reversed(range(layers)):
        stream_in, first, qkv, head_out, lse, mixed_heads, middle, second, hidden, slope = saved[
            layer
        ]
        qkv_full, out_full, up_full, down_full = gathered[layer]
        gain1, shift1 = ln1_gain[layer].astype(FULL), ln1_bias[layer].astype(FULL)
        gain2, shift2 = ln2_gain[layer].astype(FULL), ln2_bias[layer].astype(FULL)
        if layer == layers - 1:
            grad_mlp = whole_grad.astype(LOW)
        else:
            grad_mlp = tp_gather(stream_grad.astype(LOW))
        down_bias_grad = jnp.sum(grad_mlp.astype(FULL), axis=0)
        grad_hidden = dot(grad_mlp, down_full, ((1,), (0,)))
        grad_pre = (grad_hidden * slope.astype(FULL)).astype(LOW)
        up_bias_grad = jnp.sum(grad_pre.astype(FULL), axis=0)

        def back_up(start, count, grad_pre=grad_pre, up_full=up_full):
            return dot(rows_of(grad_pre, start, count), up_full, ((1,), (1,)))

        grad_second = tp_scatter(back_up, capacity)

        def mlp_part(start, count, grad_mlp=grad_mlp, hidden=hidden, second=second, grad_pre=grad_pre):
            return jnp.concatenate(
                [
                    dot(rows_of(second, start, count, 1), grad_pre, ((0,), (0,))),
                    dot(rows_of(grad_mlp, start, count, 1), hidden, ((0,), (0,))),
                ],
                axis=1,
            )

        mlp_grads = scatter_weight(mlp_part, width)
        _, second_normed, second_inverse = normalize(middle, gain2, shift2)
        ln2_gain_grad = jnp.sum(grad_second * second_normed, axis=0)
        ln2_bias_grad = jnp.sum(grad_second, axis=0)
        stream_grad = stream_grad + normalize_back(
            grad_second, second_normed, second_inverse, gain2
        )
        grad_attn = tp_gather(stream_grad.astype(LOW))
        out_bias_grad = jnp.sum(grad_attn.astype(FULL), axis=0)
        dout = dot(out_full, grad_attn, ((0,), (1,))).astype(LOW)
        dout = jnp.concatenate(heads_out(dout.reshape(heads, size, capacity)), axis=1)
        dqkv = attend_back(qkv, bias, head_out, lse, dout, size)
        grad_joint = heads_back(
            [dqkv[:, r * capacity : (r + 1) * capacity] for r in range(ctx_count)]
        ).reshape(joint_width, capacity)
        column_sums = jnp.sum(grad_joint.astype(FULL), axis=1).reshape(heads, 3, size)
        qv_bias_grad = jnp.stack([column_sums[:, 0], column_sums[:, 2]], axis=1).reshape(-1)

        def back_qkv(start, count, grad_joint=grad_joint, qkv_full=qkv_full):
            return dot(rows_of(grad_joint, start, count, 1), qkv_full, ((0,), (1,)))

        grad_first = tp_scatter(back_qkv, capacity)

        def attn_part(
            start, count, first=first, grad_joint=grad_joint, grad_attn=grad_attn, heads_low=mixed_heads
        ):
            return jnp.concatenate(
                [
                    dot(rows_of(first, start, count, 1), grad_joint, ((0,), (1,))),
                    dot(rows_of(grad_attn, start, count, 1), heads_low, ((0,), (1,))),
                ],
                axis=1,
            )

        attn_grads = scatter_weight(attn_part, width)
        _, first_normed, first_inverse = normalize(stream_in, gain1, shift1)
        ln1_gain_grad = jnp.sum(grad_first * first_normed, axis=0)
        ln1_bias_grad = jnp.sum(grad_first, axis=0)
        stream_grad = stream_grad + normalize_back(grad_first, first_normed, first_inverse, gain1)
        weight_parts[layer] = (
            attn_grads[:, :joint_width],
            attn_grads[:, joint_width:],
            mlp_grads[:, :hidden_width],
            mlp_grads[:, hidden_width:],
        )
        split = total_over(
            ("tp",),
            jnp.concatenate([ln1_gain_grad, ln1_bias_grad, ln2_gain_grad, ln2_bias_grad]),
        )
        packed = total_over(
            ("shard", "ctx"),
            jnp.concatenate([split, out_bias_grad, down_bias_grad, up_bias_grad, qv_bias_grad]),
        )
        small_parts[layer] = packed

    token_grads = tp_gather(stream_grad.astype(LOW)).astype(FULL)[None]
    small = jnp.stack(small_parts, axis=0)
    cuts = [width * i for i in range(7)] + [width * 6 + hidden_width]
    pieces = [small[:, cuts[i] : cuts[i + 1]] for i in range(7)] + [small[:, cuts[7] :]]
    g_ln1_gain, g_ln1_bias, g_ln2_gain, g_ln2_bias, g_out, g_down, g_up, g_qv = pieces
    stacked = [
        jnp.stack([weight_parts[layer][member] for layer in range(layers)], axis=0)
        for member in range(4)
    ]
    return (
        mixed,
        token_grads,
        g_ln1_gain,
        g_ln1_bias,
        stacked[0],
        g_qv,
        stacked[1],
        g_out,
        g_ln2_gain,
        g_ln2_bias,
        stacked[2],
        g_up,
        stacked[3],
        g_down,
    )


def solution(mesh):
    split_rows = P(None, ("shard", "ctx"), "tp")
    split_tokens = P("shard", "ctx", None)
    return jax.shard_map(
        shards,
        mesh=mesh,
        in_specs=(
            split_tokens,
            P("shard", None),
            P(),
            P(),
            split_rows,
            P(None, "tp"),
            split_rows,
            P(),
            P(),
            P(),
            split_rows,
            P(None, "tp"),
            split_rows,
            P(),
            split_tokens,
        ),
        out_specs=(
            split_tokens,
            split_tokens,
            P(),
            P(),
            split_rows,
            P(None, "tp"),
            split_rows,
            P(),
            P(),
            P(),
            split_rows,
            P(None, "tp"),
            split_rows,
            P(),
        ),
        check_vma=False,
    )
```

```python
import functools
import math

import jax
import jax.numpy as jnp
from jax import lax
from jax.experimental import pallas as pl
from jax.experimental.pallas import tpu as pltpu
from jax.sharding import PartitionSpec as P

HEAD_DIM = 64
EPSILON = 1e-06
NEG_LARGE = -1e30
LOW = jnp.bfloat16
FULL = jnp.float32
PAD = 128


def bits_of(axis):
    size = lax.axis_size(axis)
    assert size & (size - 1) == 0
    return [1 << i for i in range(size.bit_length() - 1)]


def swap(value, axis, bit):
    size = lax.axis_size(axis)
    return lax.ppermute(value, axis, [(i, i ^ bit) for i in range(size)])


def side_of(axis, bit):
    return (lax.axis_index(axis) // bit) % 2


def rows_of(value, start, count, axis=0):
    return lax.dynamic_slice_in_dim(value, start, count, axis)


def halve(axis, bits, partial, total):
    offset, span, received = jnp.int32(0), total, []

    def summed(start, count):
        value = partial(start, count)
        for got, base in received:
            value = value + rows_of(got, start - base, count).astype(FULL)
        return value

    for bit in bits:
        half = span // 2
        side = side_of(axis, bit)
        got = swap(summed(offset + (1 - side) * half, half).astype(LOW), axis, bit)
        offset = offset + side * half
        received.append((got, offset))
        span = half
    return summed(offset, span)


def double(axis, bits, value):
    for bit in bits:
        got = swap(value, axis, bit)
        first = side_of(axis, bit) == 0
        value = jnp.concatenate(
            [jnp.where(first, value, got), jnp.where(first, got, value)], axis=0
        )
    return value


def tp_scatter(partial, total):
    return halve("tp", bits_of("tp"), partial, total)


def tp_gather(value):
    return double("tp", bits_of("tp")[::-1], value)


def tp_offset(total):
    offset, span = jnp.int32(0), total
    for bit in bits_of("tp"):
        span = span // 2
        offset = offset + side_of("tp", bit) * span
    return offset, span


def total_over(axes, value):
    for axis in axes:
        for bit in bits_of(axis):
            value = value + swap(value, axis, bit)
    return value


def ring(value, by):
    count = lax.axis_size("ctx")
    return lax.ppermute(value, "ctx", [(i, (i + by) % count) for i in range(count)])


def gather_weight(piece):
    count = lax.axis_size("ctx")
    place = lax.axis_index("ctx")
    ways = lax.axis_size("shard")
    blocks = [piece] + [ring(piece, by) for by in range(1, count)]
    whole = jnp.zeros((ways * count,) + piece.shape, piece.dtype)
    me = lax.axis_index("shard")
    for by, block in enumerate(blocks):
        at = (place - by) % count
        held = [(jnp.int32(0), block)]
        for bit in bits_of("shard"):
            held = held + [(other ^ bit, swap(value, "shard", bit)) for other, value in held]
        for other, value in held:
            whole = lax.dynamic_update_index_in_dim(whole, value, (me ^ other) * count + at, 0)
    return whole.reshape((ways * count * piece.shape[0],) + piece.shape[1:]), blocks[-1]


def scatter_weight(partial, total):
    count = lax.axis_size("ctx")
    place = lax.axis_index("ctx")
    mine = halve("shard", bits_of("shard")[::-1], partial, total).astype(LOW)
    mine = mine.reshape((count, mine.shape[0] // count) + mine.shape[1:])
    value = lax.dynamic_index_in_dim(mine, place, 0, False).astype(FULL)
    for by in range(1, count):
        given = lax.dynamic_index_in_dim(mine, (place + by) % count, 0, False)
        value = value + ring(given, by).astype(FULL)
    return value


def heads_out(parts):
    count = lax.axis_size("ctx")
    place = lax.axis_index("ctx")
    got = [lax.dynamic_index_in_dim(parts, place, 0, False)]
    for by in range(1, count):
        given = lax.dynamic_index_in_dim(parts, (place + by) % count, 0, False)
        got.append(lax.ppermute(given, "ctx", [(i, (i + by) % count) for i in range(count)]))
    return got


def heads_back(parts):
    count = lax.axis_size("ctx")
    place = lax.axis_index("ctx")
    whole = jnp.zeros((count,) + parts[0].shape, parts[0].dtype)
    whole = lax.dynamic_update_index_in_dim(whole, parts[0], place, 0)
    for by in range(1, count):
        got = lax.ppermute(parts[by], "ctx", [(i, (i - by) % count) for i in range(count)])
        whole = lax.dynamic_update_index_in_dim(whole, got, (place + by) % count, 0)
    return whole


def dot(left, right, contract):
    return lax.dot_general(
        left, right, ((contract[0], contract[1]), ((), ())), preferred_element_type=FULL
    )


def turned(value):
    return value.astype(FULL).T.astype(LOW)


def attend_kernel(tile, size, qkv_ref, bias_ref, o_ref, olow_ref, lse_ref, k_ref):
    step = pl.program_id(0)
    slots = qkv_ref.shape[1]

    @pl.when(step == 0)
    def _():
        keys = jnp.concatenate(
            [
                qkv_ref[size : 2 * size, :],
                bias_ref[...],
                jnp.zeros((PAD - size - 16, slots), LOW),
            ],
            axis=0,
        )
        k_ref[...] = turned(keys)

    here = pl.ds(pl.multiple_of(step * tile, tile), tile)
    queries = jnp.concatenate(
        [
            (qkv_ref[0:size, here] * (size**-0.5)).astype(LOW),
            jnp.ones((16, tile), LOW),
            jnp.zeros((PAD - size - 16, tile), LOW),
        ],
        axis=0,
    )
    scores = jnp.dot(k_ref[...], queries, preferred_element_type=FULL)
    top = jnp.max(scores, axis=0, keepdims=True)
    weights = jnp.exp(scores - top)
    total = jnp.sum(weights, axis=0, keepdims=True)
    summed = jnp.dot(
        qkv_ref[2 * size : 3 * size, :], weights.astype(LOW), preferred_element_type=FULL
    )
    out = summed / total
    o_ref[...] = out
    olow_ref[...] = out.astype(LOW)
    lse_ref[...] = jnp.broadcast_to(top + jnp.log(total), lse_ref.shape)


def attend(qkv, bias, size):
    slots = qkv.shape[1]
    tile = 256 if slots % 256 == 0 else PAD
    return pl.pallas_call(
        functools.partial(attend_kernel, tile, size),
        grid=(slots // tile,),
        in_specs=[
            pl.BlockSpec((3 * size, slots), lambda i: (0, 0)),
            pl.BlockSpec((16, slots), lambda i: (0, 0)),
        ],
        out_specs=[
            pl.BlockSpec((size, tile), lambda i: (0, i)),
            pl.BlockSpec((size, tile), lambda i: (0, i)),
            pl.BlockSpec((8, tile), lambda i: (0, i)),
        ],
        out_shape=[
            jax.ShapeDtypeStruct((size, slots), FULL),
            jax.ShapeDtypeStruct((size, slots), LOW),
            jax.ShapeDtypeStruct((8, slots), FULL),
        ],
        scratch_shapes=[pltpu.VMEM((slots, PAD), LOW)],
        compiler_params=pltpu.CompilerParams(
            dimension_semantics=("arbitrary",), vmem_limit_bytes=32 * 2**20
        ),
        cost_estimate=pl.CostEstimate(
            flops=2 * slots * slots * 256 * 2,
            bytes_accessed=slots * size * 16,
            transcendentals=slots * slots,
        ),
        name="attend",
    )(qkv, bias)


def attend_back_kernel(
    tile, size, qkv_ref, bias_ref, o_ref, lse_ref, do_ref, dqkv_ref, k_ref, v_ref, dk_ref, dv_ref
):
    step = pl.program_id(0)
    slots = qkv_ref.shape[1]

    @pl.when(step == 0)
    def _():
        keys = jnp.concatenate(
            [
                qkv_ref[size : 2 * size, :],
                bias_ref[...],
                jnp.zeros((PAD - size - 16, slots), LOW),
            ],
            axis=0,
        )
        k_ref[...] = turned(keys)
        v_ref[...] = turned(
            jnp.concatenate(
                [qkv_ref[2 * size : 3 * size, :], jnp.zeros((PAD - size, slots), LOW)], axis=0
            )
        )
        dk_ref[...] = jnp.zeros_like(dk_ref)
        dv_ref[...] = jnp.zeros_like(dv_ref)

    here = pl.ds(pl.multiple_of(step * tile, tile), tile)
    scaled = (qkv_ref[0:size, here] * (size**-0.5)).astype(LOW)
    queries = jnp.concatenate(
        [scaled, jnp.ones((16, tile), LOW), jnp.zeros((PAD - size - 16, tile), LOW)], axis=0
    )
    dout = jnp.concatenate([do_ref[:, here], jnp.zeros((PAD - size, tile), LOW)], axis=0)
    delta = jnp.sum(do_ref[:, here].astype(FULL) * o_ref[:, here], axis=0, keepdims=True)
    scores = jnp.dot(k_ref[...], queries, preferred_element_type=FULL)
    chance = jnp.exp(scores - lse_ref[0:1, here])
    chance_grad = jnp.dot(v_ref[...], dout, preferred_element_type=FULL)
    score_grad = (chance * (chance_grad - delta)).astype(LOW)
    query_grad = jnp.dot(qkv_ref[size : 2 * size, :], score_grad, preferred_element_type=FULL)
    dqkv_ref[0:size, here] = (query_grad * (size**-0.5)).astype(LOW)
    plain_q = turned(jnp.concatenate([scaled, jnp.zeros((PAD - size, tile), LOW)], axis=0))
    dk_ref[...] += jnp.dot(score_grad, plain_q, preferred_element_type=FULL)
    dv_ref[...] += jnp.dot(chance.astype(LOW), turned(dout), preferred_element_type=FULL)

    @pl.when(step == pl.num_programs(0) - 1)
    def _():
        dqkv_ref[size : 2 * size, :] = dk_ref[...].T[0:size].astype(LOW)
        dqkv_ref[2 * size : 3 * size, :] = dv_ref[...].T[0:size].astype(LOW)


def attend_back(qkv, bias, out, lse, dout, size):
    slots = qkv.shape[1]
    tile = 256 if slots % 256 == 0 else PAD
    return pl.pallas_call(
        functools.partial(attend_back_kernel, tile, size),
        grid=(slots // tile,),
        in_specs=[
            pl.BlockSpec((3 * size, slots), lambda i: (0, 0)),
            pl.BlockSpec((16, slots), lambda i: (0, 0)),
            pl.BlockSpec((size, slots), lambda i: (0, 0)),
            pl.BlockSpec((8, slots), lambda i: (0, 0)),
            pl.BlockSpec((size, slots), lambda i: (0, 0)),
        ],
        out_specs=pl.BlockSpec((3 * size, slots), lambda i: (0, 0)),
        out_shape=jax.ShapeDtypeStruct((3 * size, slots), LOW),
        scratch_shapes=[
            pltpu.VMEM((slots, PAD), LOW),
            pltpu.VMEM((slots, PAD), LOW),
            pltpu.VMEM((slots, PAD), FULL),
            pltpu.VMEM((slots, PAD), FULL),
        ],
        compiler_params=pltpu.CompilerParams(
            dimension_semantics=("arbitrary",), vmem_limit_bytes=40 * 2**20
        ),
        cost_estimate=pl.CostEstimate(
            flops=2 * slots * slots * 256 * 5,
            bytes_accessed=slots * size * 24,
            transcendentals=slots * slots,
        ),
        name="attend_back",
    )(qkv, bias, out, lse, dout)


def normalize(rows, gain, shift):
    row_mean = jnp.mean(rows, axis=-1, keepdims=True)
    centred = rows - row_mean
    inverse = lax.rsqrt(jnp.mean(centred * centred, axis=-1, keepdims=True) + EPSILON)
    normed = centred * inverse
    return (normed * gain + shift, normed, inverse)


def normalize_back(grad_out, normed, inverse, gain):
    scaled = grad_out * gain
    mean_grad = jnp.mean(scaled, axis=-1, keepdims=True)
    mean_cross = jnp.mean(scaled * normed, axis=-1, keepdims=True)
    return inverse * (scaled - mean_grad - normed * mean_cross)


def gelu_pair(value):
    spread = 0.5 * (1.0 + lax.erf(value * (0.5**0.5)))
    slope = spread + value * jnp.exp(-0.5 * value * value) * (1.0 / math.sqrt(2.0 * math.pi))
    return (value * spread).astype(LOW), slope.astype(LOW)


def shards(
    tokens,
    block_tokens,
    ln1_gain,
    ln1_bias,
    w_qkv,
    b_qv,
    w_out,
    b_out,
    ln2_gain,
    ln2_bias,
    w_up,
    b_up,
    w_down,
    b_down,
    cotangent,
):
    images, capacity, width = tokens.shape
    assert images == 1
    layers = w_qkv.shape[0]
    size = HEAD_DIM
    ctx_count = lax.axis_size("ctx")
    ctx_place = lax.axis_index("ctx")
    joint_width = w_qkv.shape[2]
    heads = joint_width // (3 * size)
    assert heads == ctx_count
    attn_width = heads * size
    hidden_width = w_up.shape[2]
    offset, span = tp_offset(capacity)

    lengths = block_tokens[0]
    order = (ctx_place - jnp.arange(ctx_count, dtype=jnp.int32)) % ctx_count
    ordered = jnp.sum(
        jnp.where(
            order[:, None] == jnp.arange(ctx_count, dtype=jnp.int32)[None, :], lengths[None, :], 0
        ),
        axis=1,
    )
    usable = jnp.arange(capacity, dtype=jnp.int32)[None, :] < ordered[:, None]
    bias_row = jnp.where(usable, 0.0, NEG_LARGE).astype(LOW).reshape(1, ctx_count * capacity)
    bias = jnp.concatenate([bias_row, jnp.zeros((15, ctx_count * capacity), LOW)], axis=0)
    own_live = ordered[0]
    row_mask = (jnp.arange(capacity, dtype=jnp.int32) < own_live).astype(FULL)[:, None]
    own_mask = rows_of(row_mask, offset, span)

    gathered = []
    before = None
    for layer in range(layers):
        first_piece = w_qkv[layer]
        rest = jnp.concatenate([w_out[layer], w_up[layer], w_down[layer]], axis=1)
        if before is not None:
            first_piece, before = lax.optimization_barrier((first_piece, before))
        qkv_full, before = gather_weight(first_piece)
        rest, before = lax.optimization_barrier((rest, before))
        rest_full, before = gather_weight(rest)
        gathered.append(
            (
                qkv_full,
                rest_full[:, :attn_width],
                rest_full[:, attn_width : attn_width + hidden_width],
                rest_full[:, attn_width + hidden_width :],
            )
        )

    whole_stream = tokens[0].astype(FULL)
    stream = rows_of(whole_stream, offset, span)
    saved = []
    for layer in range(layers):
        qkv_full, out_full, up_full, down_full = gathered[layer]
        gain1, shift1 = ln1_gain[layer].astype(FULL), ln1_bias[layer].astype(FULL)
        gain2, shift2 = ln2_gain[layer].astype(FULL), ln2_bias[layer].astype(FULL)
        if layer == 0:
            first = normalize(whole_stream, gain1, shift1)[0].astype(LOW)
        else:
            first = tp_gather(normalize(stream, gain1, shift1)[0].astype(LOW))
        pair = b_qv[layer].astype(FULL).reshape(heads, 2, size)
        joint_bias = jnp.stack(
            [pair[:, 0], jnp.zeros_like(pair[:, 0]), pair[:, 1]], axis=1
        ).reshape(joint_width, 1)
        joint = (dot(qkv_full, first, ((0,), (1,))) + joint_bias).astype(LOW)
        joint = joint.reshape(heads, 3 * size, capacity)
        qkv = jnp.concatenate(heads_out(joint), axis=1)
        head_out, head_low, lse = attend(qkv, bias, size)
        mixed_heads = heads_back(
            [head_low[:, r * capacity : (r + 1) * capacity] for r in range(ctx_count)]
        ).reshape(attn_width, capacity)

        def out_part(start, count, mixed_heads=mixed_heads, out_full=out_full):
            return dot(rows_of(mixed_heads, start, count, 1), out_full, ((0,), (1,)))

        middle = stream + tp_scatter(out_part, capacity) + b_out[layer].astype(FULL)
        second = tp_gather(normalize(middle, gain2, shift2)[0].astype(LOW))
        hidden_pre = dot(second, up_full, ((1,), (0,))) + b_up[layer].astype(FULL)
        hidden, slope = gelu_pair(hidden_pre)

        def down_part(start, count, hidden=hidden, down_full=down_full):
            return dot(rows_of(hidden, start, count), down_full, ((1,), (1,)))

        saved.append((stream, first, qkv, head_out, lse, mixed_heads, middle, second, hidden, slope))
        stream = middle + tp_scatter(down_part, capacity) + b_down[layer].astype(FULL)

    mixed = tp_gather((stream * own_mask).astype(LOW))[None]
    whole_grad = cotangent[0].astype(FULL) * row_mask
    stream_grad = rows_of(whole_grad, offset, span)
    weight_parts = [None] * layers
    small_parts = [None] * layers
    for layer in reversed(range(layers)):
        stream_in, first, qkv, head_out, lse, mixed_heads, middle, second, hidden, slope = saved[
            layer
        ]
        qkv_full, out_full, up_full, down_full = gathered[layer]
        gain1, shift1 = ln1_gain[layer].astype(FULL), ln1_bias[layer].astype(FULL)
        gain2, shift2 = ln2_gain[layer].astype(FULL), ln2_bias[layer].astype(FULL)
        if layer == layers - 1:
            grad_mlp = whole_grad.astype(LOW)
        else:
            grad_mlp = tp_gather(stream_grad.astype(LOW))
        down_bias_grad = jnp.sum(grad_mlp.astype(FULL), axis=0)
        grad_hidden = dot(grad_mlp, down_full, ((1,), (0,)))
        grad_pre = (grad_hidden * slope.astype(FULL)).astype(LOW)
        up_bias_grad = jnp.sum(grad_pre.astype(FULL), axis=0)

        def back_up(start, count, grad_pre=grad_pre, up_full=up_full):
            return dot(rows_of(grad_pre, start, count), up_full, ((1,), (1,)))

        grad_second = tp_scatter(back_up, capacity)

        def down_grad(start, count, grad_mlp=grad_mlp, hidden=hidden):
            return dot(rows_of(grad_mlp, start, count, 1), hidden, ((0,), (0,)))

        def up_grad(start, count, second=second, grad_pre=grad_pre):
            return dot(rows_of(second, start, count, 1), grad_pre, ((0,), (0,)))

        down_parts = scatter_weight(down_grad, width)
        up_parts = scatter_weight(up_grad, width)
        _, second_normed, second_inverse = normalize(middle, gain2, shift2)
        ln2_gain_grad = jnp.sum(grad_second * second_normed, axis=0)
        ln2_bias_grad = jnp.sum(grad_second, axis=0)
        stream_grad = stream_grad + normalize_back(
            grad_second, second_normed, second_inverse, gain2
        )
        grad_attn = tp_gather(stream_grad.astype(LOW))
        out_bias_grad = jnp.sum(grad_attn.astype(FULL), axis=0)
        dout = dot(out_full, grad_attn, ((0,), (1,))).astype(LOW)
        dout = jnp.concatenate(heads_out(dout.reshape(heads, size, capacity)), axis=1)
        dqkv = attend_back(qkv, bias, head_out, lse, dout, size)
        grad_joint = heads_back(
            [dqkv[:, r * capacity : (r + 1) * capacity] for r in range(ctx_count)]
        ).reshape(joint_width, capacity)
        column_sums = jnp.sum(grad_joint.astype(FULL), axis=1).reshape(heads, 3, size)
        qv_bias_grad = jnp.stack([column_sums[:, 0], column_sums[:, 2]], axis=1).reshape(-1)

        def back_qkv(start, count, grad_joint=grad_joint, qkv_full=qkv_full):
            return dot(rows_of(grad_joint, start, count, 1), qkv_full, ((0,), (1,)))

        grad_first = tp_scatter(back_qkv, capacity)

        def out_grad(start, count, grad_attn=grad_attn, heads_low=mixed_heads):
            return dot(rows_of(grad_attn, start, count, 1), heads_low, ((0,), (1,)))

        def qkv_grad(start, count, first=first, grad_joint=grad_joint):
            return dot(rows_of(first, start, count, 1), grad_joint, ((0,), (1,)))

        out_parts = scatter_weight(out_grad, width)
        qkv_parts = scatter_weight(qkv_grad, width)
        _, first_normed, first_inverse = normalize(stream_in, gain1, shift1)
        ln1_gain_grad = jnp.sum(grad_first * first_normed, axis=0)
        ln1_bias_grad = jnp.sum(grad_first, axis=0)
        stream_grad = stream_grad + normalize_back(grad_first, first_normed, first_inverse, gain1)
        weight_parts[layer] = (qkv_parts, out_parts, up_parts, down_parts)
        small_parts[layer] = (
            jnp.concatenate([ln1_gain_grad, ln1_bias_grad, ln2_gain_grad, ln2_bias_grad]),
            jnp.concatenate([out_bias_grad, down_bias_grad, up_bias_grad, qv_bias_grad]),
        )

    token_grads = tp_gather(stream_grad.astype(LOW)).astype(FULL)[None]
    norm_small = total_over(("tp",), jnp.stack([part[0] for part in small_parts], axis=0))
    other_small = jnp.stack([part[1] for part in small_parts], axis=0)
    small = total_over(("shard", "ctx"), jnp.concatenate([norm_small, other_small], axis=1))
    cuts = [width * i for i in range(7)] + [width * 6 + hidden_width]
    pieces = [small[:, cuts[i] : cuts[i + 1]] for i in range(7)] + [small[:, cuts[7] :]]
    g_ln1_gain, g_ln1_bias, g_ln2_gain, g_ln2_bias, g_out, g_down, g_up, g_qv = pieces
    stacked = [
        jnp.stack([weight_parts[layer][member] for layer in range(layers)], axis=0)
        for member in range(4)
    ]
    return (
        mixed,
        token_grads,
        g_ln1_gain,
        g_ln1_bias,
        stacked[0],
        g_qv,
        stacked[1],
        g_out,
        g_ln2_gain,
        g_ln2_bias,
        stacked[2],
        g_up,
        stacked[3],
        g_down,
    )


def solution(mesh):
    split_rows = P(None, ("shard", "ctx"), "tp")
    split_tokens = P("shard", "ctx", None)
    return jax.shard_map(
        shards,
        mesh=mesh,
        in_specs=(
            split_tokens,
            P("shard", None),
            P(),
            P(),
            split_rows,
            P(None, "tp"),
            split_rows,
            P(),
            P(),
            P(),
            split_rows,
            P(None, "tp"),
            split_rows,
            P(),
            split_tokens,
        ),
        out_specs=(
            split_tokens,
            split_tokens,
            P(),
            P(),
            split_rows,
            P(None, "tp"),
            split_rows,
            P(),
            P(),
            P(),
            split_rows,
            P(None, "tp"),
            split_rows,
            P(),
        ),
        check_vma=False,
    )
```

```python
import functools
import math

import jax
import jax.numpy as jnp
from jax import lax
from jax.experimental import pallas as pl
from jax.experimental.pallas import tpu as pltpu
from jax.sharding import PartitionSpec as P

HEAD_DIM = 64
EPSILON = 1e-06
NEG_LARGE = -1e30
LOW = jnp.bfloat16
FULL = jnp.float32
PAD = 128
MESH = pl.DeviceIdType.MESH
ANY = pl.ANY
VMEM = pltpu.VMEM


def bits_of(axis):
    size = lax.axis_size(axis)
    assert size & (size - 1) == 0
    return [1 << i for i in range(size.bit_length() - 1)]


def swap(value, axis, bit):
    size = lax.axis_size(axis)
    return lax.ppermute(value, axis, [(i, i ^ bit) for i in range(size)])


def side_of(axis, bit):
    return (lax.axis_index(axis) // bit) % 2


def rows_of(value, start, count, axis=0):
    return lax.dynamic_slice_in_dim(value, start, count, axis)


def halve(axis, bits, partial, total):
    offset, span, received = jnp.int32(0), total, []

    def summed(start, count):
        value = partial(start, count)
        for got, base in received:
            value = value + rows_of(got, start - base, count).astype(FULL)
        return value

    for bit in bits:
        half = span // 2
        side = side_of(axis, bit)
        got = swap(summed(offset + (1 - side) * half, half).astype(LOW), axis, bit)
        offset = offset + side * half
        received.append((got, offset))
        span = half
    return summed(offset, span)


def double(axis, bits, value):
    for bit in bits:
        got = swap(value, axis, bit)
        first = side_of(axis, bit) == 0
        value = jnp.concatenate(
            [jnp.where(first, value, got), jnp.where(first, got, value)], axis=0
        )
    return value


def tp_scatter(partial, total):
    return halve("tp", bits_of("tp"), partial, total)


def tp_gather(value):
    return double("tp", bits_of("tp")[::-1], value)


def tp_offset(total):
    offset, span = jnp.int32(0), total
    for bit in bits_of("tp"):
        span = span // 2
        offset = offset + side_of("tp", bit) * span
    return offset, span


def total_over(axes, value):
    for axis in axes:
        for bit in bits_of(axis):
            value = value + swap(value, axis, bit)
    return value


def ring(value, by):
    count = lax.axis_size("ctx")
    return lax.ppermute(value, "ctx", [(i, (i + by) % count) for i in range(count)])


def gather_weight(piece):
    count = lax.axis_size("ctx")
    place = lax.axis_index("ctx")
    ways = lax.axis_size("shard")
    blocks = [piece] + [ring(piece, by) for by in range(1, count)]
    whole = jnp.zeros((ways * count,) + piece.shape, piece.dtype)
    me = lax.axis_index("shard")
    for by, block in enumerate(blocks):
        at = (place - by) % count
        held = [(jnp.int32(0), block)]
        for bit in bits_of("shard"):
            held = held + [(other ^ bit, swap(value, "shard", bit)) for other, value in held]
        for other, value in held:
            whole = lax.dynamic_update_index_in_dim(whole, value, (me ^ other) * count + at, 0)
    return whole.reshape((ways * count * piece.shape[0],) + piece.shape[1:]), blocks[-1]


def scatter_weight(partial, total):
    count = lax.axis_size("ctx")
    place = lax.axis_index("ctx")
    mine = halve("shard", bits_of("shard")[::-1], partial, total).astype(LOW)
    mine = mine.reshape((count, mine.shape[0] // count) + mine.shape[1:])
    value = lax.dynamic_index_in_dim(mine, place, 0, False).astype(FULL)
    for by in range(1, count):
        given = lax.dynamic_index_in_dim(mine, (place + by) % count, 0, False)
        value = value + ring(given, by).astype(FULL)
    return value


def dot(left, right, contract):
    return lax.dot_general(
        left, right, ((contract[0], contract[1]), ((), ())), preferred_element_type=FULL
    )


def turned(value):
    return value.astype(FULL).T.astype(LOW)


def normalize(rows, gain, shift):
    row_mean = jnp.mean(rows, axis=-1, keepdims=True)
    centred = rows - row_mean
    inverse = lax.rsqrt(jnp.mean(centred * centred, axis=-1, keepdims=True) + EPSILON)
    normed = centred * inverse
    return (normed * gain + shift, normed, inverse)


def normalize_back(grad_out, normed, inverse, gain):
    scaled = grad_out * gain
    mean_grad = jnp.mean(scaled, axis=-1, keepdims=True)
    mean_cross = jnp.mean(scaled * normed, axis=-1, keepdims=True)
    return inverse * (scaled - mean_grad - normed * mean_cross)


def gelu_pair(value):
    spread = 0.5 * (1.0 + lax.erf(value * (0.5**0.5)))
    slope = spread + value * jnp.exp(-0.5 * value * value) * (1.0 / math.sqrt(2.0 * math.pi))
    return (value * spread).astype(LOW), slope.astype(LOW)


class Mover:
    def __init__(self, sizes, send, recv, local):
        self.ctx_count, self.shard_count = sizes
        self.send, self.recv, self.local = send, recv, local
        self.copies, self.here = [], []
        self.arrived = set()
        self.ctx = lax.axis_index("ctx")
        self.shard = lax.axis_index("shard")

    def go(self, source, target, **device):
        index = len(self.copies)
        copy = pltpu.make_async_remote_copy(
            src_ref=source,
            dst_ref=target,
            send_sem=self.send.at[index],
            recv_sem=self.recv.at[index],
            device_id=device,
            device_id_type=MESH,
        )
        copy.start()
        self.copies.append(copy)
        return index

    def stay(self, source, target):
        copy = pltpu.make_async_copy(source, target, self.local.at[len(self.here)])
        copy.start()
        self.here.append(copy)

    def take(self, index):
        if index not in self.arrived:
            self.arrived.add(index)
            self.copies[index].wait_recv()

    def on(self, by):
        return lax.rem(self.ctx + by, self.ctx_count)

    def back(self, by):
        return lax.rem(self.ctx + self.ctx_count - by, self.ctx_count)

    def settle(self):
        for index, copy in enumerate(self.copies):
            self.take(index)
            copy.wait_send()
        for copy in self.here:
            copy.wait()


class Jobs:
    def __init__(self, mover, kinds, sources, targets):
        self.mover = mover
        self.all = list(zip(kinds, sources, targets))
        self.gathers = []

    def start(self):
        mover = self.mover
        count = mover.ctx_count
        for (kind, layer), source, target in self.all:
            if kind == "gather":
                slot = mover.shard * count + mover.ctx
                mine = source.at[layer]
                mover.go(mine, target.at[slot], shard=1 - mover.shard)
                line = [mover.go(mine, target.at[slot], ctx=mover.on(by)) for by in range(1, count)]
                mover.stay(mine, target.at[slot])
                self.gathers.append((target, line))
            elif kind == "cross":
                part = source.at[pl.ds((1 - mover.shard) * count, count)]
                mover.go(part, target, shard=1 - mover.shard)
            else:
                for by in range(1, count):
                    mover.go(source.at[mover.on(by)], target.at[by - 1], ctx=mover.on(by))

    def hook(self, by):
        mover = self.mover
        if by < mover.ctx_count:
            for target, line in self.gathers:
                mover.take(line[by - 1])
                slot = mover.shard * mover.ctx_count + mover.back(by)
                mover.go(target.at[slot], target.at[slot], shard=1 - mover.shard)


def job_targets(kinds, sources, count):
    shapes = []
    for (kind, layer), source in zip(kinds, sources):
        if kind == "gather":
            shapes.append((2 * count,) + source.shape[1:])
        elif kind == "cross":
            shapes.append((count,) + source.shape[1:])
        else:
            shapes.append((count - 1,) + source.shape[1:])
    return shapes


def job_copies(kinds, count):
    per = {"gather": 2 * count, "cross": 1, "line": count - 1}
    return sum(per[kind] for kind, layer in kinds)


def greet(mover, kinds, ctx, mate_far):
    barrier = pltpu.get_barrier_semaphore()
    peers = []
    names = [kind for kind, layer in kinds]
    if ctx or "gather" in names or "line" in names:
        peers += [dict(ctx=mover.on(by)) for by in range(1, mover.ctx_count)]
    if "gather" in names or "cross" in names:
        peers.append(dict(shard=1 - mover.shard))
    if mate_far:
        peers += [dict(tp=peer) for peer in tp_peers()]
    for peer in peers:
        pl.semaphore_signal(barrier, inc=1, device_id=peer, device_id_type=MESH)
    pl.semaphore_wait(barrier, len(peers))


def tp_peers():
    place = lax.axis_index("tp")
    core, far = lax.rem(place, 2), place // 2
    return place + 1 - 2 * core, place + 2 - 4 * far


def run(kernel, name, ident, inputs, outputs, scratch, copies, jobs, sizes, vmem, flops, extra=()):
    kinds, sources = jobs
    targets = job_targets(kinds, sources, sizes[0])
    n_in, n_out, n_jobs = len(inputs), len(outputs), len(kinds)
    total = copies + job_copies(kinds, sizes[0])
    n_scratch = len(scratch)

    def body(*refs):
        ins, rest = refs[:n_in], refs[n_in:]
        job_in, rest = rest[:n_jobs], rest[n_jobs:]
        outs, rest = rest[:n_out], rest[n_out:]
        job_out, rest = rest[:n_jobs], rest[n_jobs:]
        work, (send, recv, local) = rest[:n_scratch], rest[n_scratch:]
        mover = Mover(sizes, send, recv, local)
        kernel(mover, Jobs(mover, kinds, job_in, job_out), kinds, ins, outs, work)

    results = pl.pallas_call(
        body,
        in_specs=[pl.BlockSpec(memory_space=VMEM)] * n_in + [pl.BlockSpec(memory_space=ANY)] * n_jobs,
        out_specs=[pl.BlockSpec(memory_space=VMEM)] * n_out
        + [pl.BlockSpec(memory_space=ANY)] * n_jobs,
        out_shape=[jax.ShapeDtypeStruct(shape, dtype) for shape, dtype in outputs]
        + [jax.ShapeDtypeStruct(shape, LOW) for shape in targets],
        scratch_shapes=list(scratch)
        + [
            pltpu.SemaphoreType.DMA((max(1, total),)),
            pltpu.SemaphoreType.DMA((max(1, total),)),
            pltpu.SemaphoreType.DMA((max(1, n_jobs),)),
        ],
        compiler_params=pltpu.CompilerParams(
            collective_id=ident, has_side_effects=True, vmem_limit_bytes=vmem * 2**20
        ),
        cost_estimate=pl.CostEstimate(flops=flops, bytes_accessed=2**24, transcendentals=0),
        name=name,
    )(*inputs, *sources)
    return results[:n_out], results[n_out:]


def order_of(block, count):
    return (block + count - 1) % count


def tiles_of(count, capacity, tile):
    ends = [-(-(p + 1) * capacity // tile) for p in range(count)]
    return list(zip([0] + ends[:-1], ends))


def tile_at(t, tile):
    return pl.ds(pl.multiple_of(t * tile, tile), tile)


def attend_kernel(size, tile, mover, jobs, kinds, ins, outs, work):
    parts, bias = ins
    heads, qkv, o_ref, lse = outs
    k_ref, q_ref, v_ref, low_ref = work
    count, _, capacity = parts.shape
    slots = count * capacity
    greet(mover, kinds, True, False)
    sent = [None] + [
        mover.go(parts.at[mover.on(by)], qkv.at[by], ctx=mover.on(by)) for by in range(1, count)
    ]
    jobs.start()
    qkv[0] = parts[mover.ctx]
    q_ref[size:PAD, :] = jnp.concatenate(
        [jnp.ones((16, slots), LOW), jnp.zeros((PAD - size - 16, slots), LOW)], axis=0
    )

    def prepare(r):
        here = slice(r * capacity, (r + 1) * capacity)
        p = order_of(r, count)
        q_ref[0:size, p * capacity : (p + 1) * capacity] = (
            qkv[r, 0:size, :] * (size**-0.5)
        ).astype(LOW)
        v_ref[:, here] = qkv[r, 2 * size : 3 * size, :]
        keys = jnp.concatenate(
            [qkv[r, size : 2 * size, :], bias[:, here], jnp.zeros((PAD - size - 16, capacity), LOW)],
            axis=0,
        )
        k_ref[here, :] = turned(keys)

    prepare(0)
    for by in range(1, count):
        mover.take(sent[by])
        prepare(by)

    def step(t, carry):
        at = tile_at(t, tile)
        scores = jnp.dot(k_ref[...], q_ref[:, at], preferred_element_type=FULL)
        top = jnp.max(scores, axis=0, keepdims=True)
        weights = jnp.exp(scores - top)
        total = jnp.sum(weights, axis=0, keepdims=True)
        summed = jnp.dot(v_ref[...], weights.astype(LOW), preferred_element_type=FULL)
        out = summed / total
        o_ref[:, at] = out
        low_ref[:, at] = out.astype(LOW)
        lse[:, at] = jnp.broadcast_to(top + jnp.log(total), (8, tile))
        return carry

    for p, (low, high) in enumerate(tiles_of(count, capacity, tile)):
        lax.fori_loop(low, high, step, 0)
        done = low_ref.at[:, p * capacity : (p + 1) * capacity]
        if p < count - 1:
            mover.go(done, heads.at[mover.ctx], ctx=mover.back(p + 1))
        else:
            heads[mover.ctx] = low_ref[:, p * capacity : (p + 1) * capacity]
        jobs.hook(p + 1)
    mover.settle()


def attend(parts, bias, size, jobs, sizes, ident):
    count, width, capacity = parts.shape
    slots = count * capacity
    tile = 256 if slots % 256 == 0 else PAD
    return run(
        functools.partial(attend_kernel, size, tile),
        "attend",
        ident,
        [parts, bias],
        [
            ((count, size, capacity), LOW),
            ((count, width, capacity), LOW),
            ((size, slots), FULL),
            ((8, slots), FULL),
        ],
        [
            VMEM((slots, PAD), LOW),
            VMEM((PAD, slots), LOW),
            VMEM((size, slots), LOW),
            VMEM((size, slots), LOW),
        ],
        2 * (count - 1),
        jobs,
        sizes,
        32,
        4 * slots * slots * 256,
    )


def attend_back_kernel(size, tile, mover, jobs, kinds, ins, outs, work):
    parts, bias, qkv, o_ref, lse = ins
    (grads,) = outs
    k_ref, v_ref, q_ref, do_ref, nat_ref, delta_ref, dq_ref, dk_ref, dv_ref, got, back = work
    count, _, capacity = parts.shape
    slots = count * capacity
    greet(mover, kinds, True, False)
    sent = [None] + [
        mover.go(parts.at[mover.on(by)], got.at[by], ctx=mover.on(by)) for by in range(1, count)
    ]
    jobs.start()
    got[0] = parts[mover.ctx]
    q_ref[size:PAD, :] = jnp.concatenate(
        [jnp.ones((16, slots), LOW), jnp.zeros((PAD - size - 16, slots), LOW)], axis=0
    )
    do_ref[size:PAD, :] = jnp.zeros((PAD - size, slots), LOW)
    dq_ref[...] = jnp.zeros_like(dq_ref)
    for r in range(count):
        here = slice(r * capacity, (r + 1) * capacity)
        pad = jnp.zeros((PAD - size - 16, capacity), LOW)
        k_ref[here, :] = turned(
            jnp.concatenate([qkv[r, size : 2 * size, :], bias[:, here], pad], axis=0)
        )
        v_ref[here, :] = turned(
            jnp.concatenate(
                [qkv[r, 2 * size : 3 * size, :], jnp.zeros((PAD - size, capacity), LOW)], axis=0
            )
        )
    for r in range(count):
        if r:
            mover.take(sent[r])
        p = order_of(r, count)
        at = slice(p * capacity, (p + 1) * capacity)
        scaled = (qkv[r, 0:size, :] * (size**-0.5)).astype(LOW)
        dout = got[r]
        q_ref[0:size, at] = scaled
        do_ref[0:size, at] = dout
        nat_ref[at, :] = turned(jnp.concatenate([scaled, dout], axis=0))
        delta = jnp.sum(dout.astype(FULL) * o_ref[:, at], axis=0, keepdims=True)
        delta_ref[:, at] = jnp.broadcast_to(delta, (8, capacity))

    tiles = tiles_of(count, capacity, tile)
    for r in list(range(1, count)) + [0]:
        here = slice(r * capacity, (r + 1) * capacity)
        dk_ref[...] = jnp.zeros_like(dk_ref)
        dv_ref[...] = jnp.zeros_like(dv_ref)

        def step(t, carry, r=r, here=here):
            at = tile_at(t, tile)
            scores = jnp.dot(k_ref[here, :], q_ref[:, at], preferred_element_type=FULL)
            chance = jnp.exp(scores - lse[0:1, at])
            chance_grad = jnp.dot(v_ref[here, :], do_ref[:, at], preferred_element_type=FULL)
            score_grad = (chance * (chance_grad - delta_ref[0:1, at])).astype(LOW)
            dq_ref[:, at] += jnp.dot(
                qkv[r, size : 2 * size, :], score_grad, preferred_element_type=FULL
            )
            dk_ref[...] += jnp.dot(score_grad, nat_ref[at, :], preferred_element_type=FULL)
            dv_ref[...] += jnp.dot(
                chance.astype(LOW), nat_ref[at, :], preferred_element_type=FULL
            )
            return carry

        if r:
            lax.fori_loop(0, tiles[-1][1], step, 0)
        else:
            for p, (low, high) in enumerate(tiles):
                lax.fori_loop(low, high, step, 0)
                at = slice(p * capacity, (p + 1) * capacity)
                value = (dq_ref[:, at] * (size**-0.5)).astype(LOW)
                if p < count - 1:
                    back[p + 1, 0:size, :] = value
                    mover.go(
                        back.at[p + 1, 0:size],
                        grads.at[mover.ctx, 0:size],
                        ctx=mover.back(p + 1),
                    )
                else:
                    grads[mover.ctx, 0:size, :] = value
        keys = dk_ref[...].T[0:size].astype(LOW)
        values = dv_ref[...].T[size : 2 * size].astype(LOW)
        if r:
            back[r, size : 2 * size, :] = keys
            back[r, 2 * size : 3 * size, :] = values
            mover.go(
                back.at[r, size : 3 * size],
                grads.at[mover.ctx, size : 3 * size],
                ctx=mover.back(r),
            )
        else:
            grads[mover.ctx, size : 2 * size, :] = keys
            grads[mover.ctx, 2 * size : 3 * size, :] = values
    mover.settle()


def attend_back(parts, bias, qkv, out, lse, size, jobs, sizes, ident):
    count, _, capacity = parts.shape
    slots = count * capacity
    tile = 256 if slots % 256 == 0 else PAD
    return run(
        functools.partial(attend_back_kernel, size, tile),
        "attend_back",
        ident,
        [parts, bias, qkv, out, lse],
        [((count, 3 * size, capacity), LOW)],
        [
            VMEM((slots, PAD), LOW),
            VMEM((slots, PAD), LOW),
            VMEM((PAD, slots), LOW),
            VMEM((PAD, slots), LOW),
            VMEM((slots, PAD), LOW),
            VMEM((8, slots), FULL),
            VMEM((size, slots), FULL),
            VMEM((capacity, PAD), FULL),
            VMEM((capacity, PAD), FULL),
            VMEM((count, size, capacity), LOW),
            VMEM((count, 3 * size, capacity), LOW),
        ],
        3 * (count - 1),
        jobs,
        sizes,
        32,
        10 * slots * slots * 256,
    )


class Round:
    def __init__(self, mover, rows, full, buffers):
        place = lax.axis_index("tp")
        core, far = lax.rem(place, 2), place // 2
        self.mover, self.full = mover, full
        self.give, self.ra, self.passing, self.rb, self.keep = buffers
        self.span = rows // 4
        self.half = self.span // 2
        self.mate, self.far = tp_peers()

        def quarter(c, f):
            return (c * 2 + f) * self.span

        self.own, self.other = quarter(core, far), quarter(core, 1 - far)
        self.mate_own, self.mate_other = quarter(1 - core, far), quarter(1 - core, 1 - far)

    def rows(self, start, count=None):
        return pl.ds(pl.multiple_of(start, 16), count or self.span)

    def hand(self, slot, value):
        self.give[slot] = value.astype(LOW)
        return self.mover.go(self.give.at[slot], self.ra.at[slot], tp=self.mate)

    def onward(self, value, index):
        self.mover.take(index)
        self.passing[...] = (value + self.ra[1].astype(FULL)).astype(LOW)
        return [
            self.mover.go(self.passing.at[at], self.rb.at[at], tp=self.far)
            for at in (pl.ds(0, self.half), pl.ds(self.half, self.half))
        ]

    def close(self, far_copies, index, finish):
        self.mover.take(index)
        self.keep[...] += self.ra[0].astype(FULL)
        self.to_far, self.to_mate = [], []
        for c in range(2):
            at = pl.ds(c * self.half, self.half)
            self.mover.take(far_copies[c])
            low = finish(at, self.keep[at] + self.rb[at].astype(FULL))
            mine = self.full.at[self.rows(self.own + c * self.half, self.half)]
            mine[...] = low
            self.to_far.append(self.mover.go(mine, mine, tp=self.far))
            self.to_mate.append(self.mover.go(mine, mine, tp=self.mate))

    def eager(self, make, finish):
        first = self.hand(1, make(self.mate_other))
        copies = self.onward(make(self.other), first)
        second = self.hand(0, make(self.mate_own))
        self.keep[...] = make(self.own)
        self.close(copies, second, finish)

    def after(self, before, make, finish):
        before.have_mate_own()
        second = self.hand(0, make(self.mate_own))
        self.keep[...] = make(self.own)
        before.have_other()
        value = make(self.other)
        before.have_mate_other()
        first = self.hand(1, make(self.mate_other))
        self.close(self.onward(value, first), second, finish)

    def have_mate_own(self):
        for copy in self.to_mate:
            self.mover.take(copy)

    def have_other(self):
        self.passed = []
        for c in range(2):
            self.mover.take(self.to_far[c])
            rows = self.full.at[self.rows(self.other + c * self.half, self.half)]
            self.passed.append(self.mover.go(rows, rows, tp=self.mate))

    def have_mate_other(self):
        for copy in self.passed:
            self.mover.take(copy)

    def end(self):
        self.have_other()
        self.mover.settle()


ROUND_COPIES = 10


def round_buffers(rows, width):
    span = rows // 4
    return [
        VMEM((2, span, width), LOW),
        VMEM((2, span, width), LOW),
        VMEM((span, width), LOW),
        VMEM((span, width), LOW),
        VMEM((span, width), FULL),
    ]


def forward_kernel(last, mover, jobs, kinds, ins, outs, work):
    heads, w_out, w_up, w_down, x_ref, vectors, b_up, mask = ins
    middle, second, hidden, slope, stream, following = outs
    nat = work[0]
    rows = heads.shape[1]
    greet(mover, kinds, False, True)
    jobs.start()
    nat[...] = turned(heads[...])
    one = Round(mover, rows, second, work[1:6])
    two = Round(mover, rows, following, work[6:11])
    b_out, gain2, shift2, b_down, gain1, shift1 = [vectors[i : i + 1, :] for i in range(6)]

    def out_part(start):
        return dot(nat[one.rows(start), :], w_out[...], ((1,), (1,)))

    def to_second(at, value):
        value = x_ref[at] + value + b_out
        middle[at] = value
        return normalize(value, gain2, shift2)[0].astype(LOW)

    def mlp_part(start):
        at = two.rows(start)
        pre = jnp.dot(second[at, :], w_up[...], preferred_element_type=FULL) + b_up[0:1, :]
        low, low_slope = gelu_pair(pre)
        hidden[at, :] = low
        slope[at, :] = low_slope
        return dot(low, w_down[...], ((1,), (1,)))

    def to_following(at, value):
        value = middle[at] + value + b_down
        stream[at] = value
        if last:
            return (value * mask[at][:, 0:1]).astype(LOW)
        return normalize(value, gain1, shift1)[0].astype(LOW)

    one.eager(out_part, to_second)
    for by in (1, 2, 3):
        jobs.hook(by)
    two.after(one, mlp_part, to_following)
    two.end()


def forward_block(heads, w_out, w_up, w_down, x, vectors, b_up, mask, last, jobs, sizes, ident):
    rows, width, hidden = heads.shape[1], w_out.shape[0], w_up.shape[1]
    span = rows // 4
    return run(
        functools.partial(forward_kernel, last),
        "forward_block",
        ident,
        [heads, w_out, w_up, w_down, x, vectors, b_up, mask],
        [
            ((span, width), FULL),
            ((rows, width), LOW),
            ((rows, hidden), LOW),
            ((rows, hidden), LOW),
            ((span, width), FULL),
            ((rows, width), LOW),
        ],
        [VMEM((rows, heads.shape[0]), LOW)]
        + round_buffers(rows, width)
        + round_buffers(rows, width),
        2 * ROUND_COPIES,
        jobs,
        sizes,
        40,
        2 * rows * width * (2 * hidden + heads.shape[0]),
    )


def sums_into(sums, at, values):
    for row, value in enumerate(values):
        added = jnp.sum(value, axis=0, keepdims=True)
        sums[row : row + 1, :] = added if at.start == 0 else sums[row : row + 1, :] + added


def mlp_back_kernel(mover, jobs, kinds, ins, outs, work):
    grad, slope, w_up, w_down, middle, x_ref, gain = ins
    pre_grad, stream, full, sums, columns = outs
    rows = grad.shape[0]
    greet(mover, kinds, False, True)
    jobs.start()
    one = Round(mover, rows, full, work)
    columns[...] = jnp.zeros_like(columns)

    def part(start):
        at = one.rows(start)
        pre = jnp.dot(grad[at, :], w_down[...], preferred_element_type=FULL)
        low = (pre * slope[at, :].astype(FULL)).astype(LOW)
        pre_grad[at, :] = low
        columns[0:1, :] += jnp.sum(low.astype(FULL), axis=0, keepdims=True)
        return dot(low, w_up[...], ((1,), (1,)))

    def close(at, value):
        _, normed, inverse = normalize(middle[at], 1.0, 0.0)
        result = x_ref[at] + normalize_back(value, normed, inverse, gain[0:1, :])
        stream[at] = result
        low = result.astype(LOW)
        sums_into(sums, at, (value * normed, value, low.astype(FULL)))
        return low

    one.eager(part, close)
    one.end()


def mlp_back(grad, slope, w_up, w_down, middle, x, gain, jobs, sizes, ident):
    rows, width = grad.shape
    hidden = slope.shape[1]
    span = rows // 4
    return run(
        mlp_back_kernel,
        "mlp_back",
        ident,
        [grad, slope, w_up, w_down, middle, x, gain],
        [
            ((rows, hidden), LOW),
            ((span, width), FULL),
            ((rows, width), LOW),
            ((8, width), FULL),
            ((8, hidden), FULL),
        ],
        round_buffers(rows, width),
        ROUND_COPIES,
        jobs,
        sizes,
        40,
        4 * rows * width * hidden,
    )


def norm_back_kernel(mover, jobs, kinds, ins, outs, work):
    joint, w_qkv, before, x_ref, gain = ins
    stream, full, sums = outs
    nat = work[0]
    rows = joint.shape[1]
    greet(mover, kinds, False, True)
    jobs.start()
    one = Round(mover, rows, full, work[1:])
    nat[...] = turned(joint[...])

    def part(start):
        return dot(nat[one.rows(start), :], w_qkv[...], ((1,), (1,)))

    def close(at, value):
        _, normed, inverse = normalize(before[at], 1.0, 0.0)
        result = x_ref[at] + normalize_back(value, normed, inverse, gain[0:1, :])
        stream[at] = result
        low = result.astype(LOW)
        sums_into(sums, at, (value * normed, value, low.astype(FULL)))
        return low

    one.eager(part, close)
    one.end()


def norm_back(joint, w_qkv, before, x, gain, jobs, sizes, ident):
    rows, width = joint.shape[1], w_qkv.shape[0]
    span = rows // 4
    return run(
        norm_back_kernel,
        "norm_back",
        ident,
        [joint, w_qkv, before, x, gain],
        [((span, width), FULL), ((rows, width), LOW), ((8, width), FULL)],
        [VMEM((rows, joint.shape[0]), LOW)] + round_buffers(rows, width),
        ROUND_COPIES,
        jobs,
        sizes,
        32,
        2 * rows * width * joint.shape[0],
    )


def first_kernel(mover, jobs, kinds, ins, outs, work):
    tokens, vectors = ins
    (first,) = outs
    rows = tokens.shape[0]
    greet(mover, kinds, True, False)
    jobs.start()
    chunk = rows // 5 if rows % 80 == 0 else rows

    def step(i, carry):
        at = pl.ds(pl.multiple_of(i * chunk, 16), chunk)
        value = normalize(tokens[at, :].astype(FULL), vectors[0:1, :], vectors[1:2, :])[0]
        first[at, :] = value.astype(LOW)
        return carry

    lax.fori_loop(0, rows // chunk, step, 0)
    for by in (1, 2, 3):
        jobs.hook(by)
    mover.settle()


def first_norm(tokens, vectors, jobs, sizes, ident):
    return run(
        first_kernel,
        "first_norm",
        ident,
        [tokens, vectors],
        [(tokens.shape, LOW)],
        [],
        0,
        jobs,
        sizes,
        16,
        tokens.size * 16,
    )


def last_kernel(mover, jobs, kinds, ins, outs, work):
    split, whole = ins
    (result,) = outs
    got_tp, got_shard, got_ctx, mine = work
    place = lax.axis_index("tp")
    ways = got_tp.shape[0]
    barrier = pltpu.get_barrier_semaphore()
    peers = [dict(ctx=mover.on(by)) for by in range(1, mover.ctx_count)]
    peers += [dict(shard=1 - mover.shard)]
    peers += [dict(tp=lax.rem(place + by, ways)) for by in range(1, ways)]
    for peer in peers:
        pl.semaphore_signal(barrier, inc=1, device_id=peer, device_id_type=MESH)
    pl.semaphore_wait(barrier, len(peers))
    got_tp[place] = split[...]
    tp_copies = [
        mover.go(split, got_tp.at[place], tp=lax.rem(place + by, ways)) for by in range(1, ways)
    ]
    jobs.start()
    for copy in tp_copies:
        mover.take(copy)
    top = split.shape[0]
    value = got_tp[0]
    for other in range(1, ways):
        value = value + got_tp[other]
    mine[0, 0:top, :] = value
    mine[0, top:, :] = whole[...]
    cross = mover.go(mine.at[0], got_shard, shard=1 - mover.shard)
    mover.take(cross)
    mine[1] = mine[0] + got_shard[...]
    got_ctx[mover.ctx] = mine[1]
    line = [
        mover.go(mine.at[1], got_ctx.at[mover.ctx], ctx=mover.on(by))
        for by in range(1, mover.ctx_count)
    ]
    for copy in line:
        mover.take(copy)
    value = got_ctx[0]
    for other in range(1, mover.ctx_count):
        value = value + got_ctx[other]
    result[...] = value
    mover.settle()


def last_sums(split, whole, jobs, sizes, ident):
    ways = lax.axis_size("tp")
    shape = (split.shape[0] + whole.shape[0], split.shape[1])
    return run(
        last_kernel,
        "last_sums",
        ident,
        [split, whole],
        [(shape, FULL)],
        [
            VMEM((ways,) + split.shape, FULL),
            VMEM(shape, FULL),
            VMEM((sizes[0],) + shape, FULL),
            VMEM((2,) + shape, FULL),
        ],
        ways - 1 + 1 + sizes[0] - 1,
        jobs,
        sizes,
        16,
        2**20,
    )


class Sums:
    def __init__(self, inside):
        self.inside = inside
        self.crossing, self.lining, self.done = [], [], {}

    def add(self, key, value):
        count = lax.axis_size("ctx")
        if not self.inside:
            self.done[key] = scatter_weight(
                lambda start, size: rows_of(value, start, size).astype(FULL), value.shape[0]
            )
            return
        ways = lax.axis_size("shard")
        blocks = value.reshape((ways * count, value.shape[0] // (ways * count)) + value.shape[1:])
        self.crossing.append((key, blocks))

    def jobs(self):
        kinds = [("cross", 0)] * len(self.crossing) + [("line", 0)] * len(self.lining)
        self.riding = (self.crossing, self.lining)
        self.crossing, self.lining = [], []
        return kinds, [value for _, value in self.riding[0] + self.riding[1]]

    def back(self, results):
        count = lax.axis_size("ctx")
        crossed, lined = self.riding
        for (key, blocks), got in zip(crossed, results[: len(crossed)]):
            mine = lax.dynamic_slice_in_dim(blocks, lax.axis_index("shard") * count, count, 0)
            self.lining.append((key, (mine.astype(FULL) + got.astype(FULL)).astype(LOW)))
        for (key, blocks), got in zip(lined, results[len(crossed) :]):
            mine = lax.dynamic_index_in_dim(blocks, lax.axis_index("ctx"), 0, False)
            self.done[key] = mine.astype(FULL) + jnp.sum(got.astype(FULL), axis=0)


def shards(
    tokens,
    block_tokens,
    ln1_gain,
    ln1_bias,
    w_qkv,
    b_qv,
    w_out,
    b_out,
    ln2_gain,
    ln2_bias,
    w_up,
    b_up,
    w_down,
    b_down,
    cotangent,
):
    images, capacity, width = tokens.shape
    assert images == 1
    layers = w_qkv.shape[0]
    size = HEAD_DIM
    ctx_count = lax.axis_size("ctx")
    ctx_place = lax.axis_index("ctx")
    joint_width = w_qkv.shape[2]
    heads = joint_width // (3 * size)
    assert heads == ctx_count
    attn_width = heads * size
    hidden_width = w_up.shape[2]
    offset, span = tp_offset(capacity)

    lengths = block_tokens[0]
    order = (ctx_place - jnp.arange(ctx_count, dtype=jnp.int32)) % ctx_count
    ordered = jnp.sum(
        jnp.where(
            order[:, None] == jnp.arange(ctx_count, dtype=jnp.int32)[None, :], lengths[None, :], 0
        ),
        axis=1,
    )
    usable = jnp.arange(capacity, dtype=jnp.int32)[None, :] < ordered[:, None]
    bias_row = jnp.where(usable, 0.0, NEG_LARGE).astype(LOW).reshape(1, ctx_count * capacity)
    bias = jnp.concatenate([bias_row, jnp.zeros((15, ctx_count * capacity), LOW)], axis=0)
    own_live = ordered[0]
    row_mask = (jnp.arange(capacity, dtype=jnp.int32) < own_live).astype(FULL)[:, None]
    own_mask = rows_of(row_mask, offset, span)

    weights = {"qkv": w_qkv, "out": w_out, "up": w_up, "down": w_down}
    sizes = (ctx_count, lax.axis_size("shard"))
    inside = sizes[1] == 2
    gathered = {}
    plan = {("first", 0): [("qkv", 0)], ("attend", 0): [("out", 0), ("up", 0), ("down", 0)]}
    for layer in range(1, layers):
        plan["block", layer - 1] = [("qkv", layer), ("up", layer)]
        plan["attend", layer] = [("out", layer), ("down", layer)]

    def gathers(at):
        wanted = plan.get(at, []) if inside else []
        return [("gather", layer) for _, layer in wanted], [weights[name] for name, _ in wanted]

    def keep(at, results):
        for (name, layer), value in zip(plan.get(at, []), results):
            gathered[name, layer] = value.reshape((-1, value.shape[2]))

    whole_tokens = tokens[0]
    stream = rows_of(whole_tokens, offset, span).astype(FULL)
    vectors = jnp.stack([ln1_gain[0], ln1_bias[0]]).astype(FULL)
    if inside:
        (first,), results = first_norm(whole_tokens, vectors, gathers(("first", 0)), sizes, 0)
        keep(("first", 0), results)
    else:
        first = normalize(whole_tokens.astype(FULL), vectors[0:1], vectors[1:2])[0].astype(LOW)
        for name, value in weights.items():
            for layer in range(layers):
                gathered[name, layer] = gather_weight(value[layer])[0]
    mask = jnp.broadcast_to(own_mask, (span, PAD))
    saved = []
    for layer in range(layers):
        pair = b_qv[layer].astype(FULL).reshape(heads, 2, size)
        joint_bias = jnp.stack(
            [pair[:, 0], jnp.zeros_like(pair[:, 0]), pair[:, 1]], axis=1
        ).reshape(joint_width, 1)
        joint = (dot(gathered["qkv", layer], first, ((0,), (1,))) + joint_bias).astype(LOW)
        (heads_low, qkv, head_out, lse), results = attend(
            joint.reshape(heads, 3 * size, capacity),
            bias,
            size,
            gathers(("attend", layer)),
            sizes,
            1 + layer,
        )
        keep(("attend", layer), results)
        heads_low = heads_low.reshape(attn_width, capacity)
        after = min(layer + 1, layers - 1)
        vectors = jnp.stack(
            [
                b_out[layer],
                ln2_gain[layer],
                ln2_bias[layer],
                b_down[layer],
                ln1_gain[after],
                ln1_bias[after],
                b_out[layer],
                b_out[layer],
            ]
        ).astype(FULL)
        b_up_rows = jnp.broadcast_to(b_up[layer].astype(FULL)[None], (8, hidden_width))
        (middle, second, hidden, slope, result, following), results = forward_block(
            heads_low,
            gathered["out", layer],
            gathered["up", layer],
            gathered["down", layer],
            stream,
            vectors,
            b_up_rows,
            mask,
            layer == layers - 1,
            gathers(("block", layer)),
            sizes,
            1 + layers + layer,
        )
        keep(("block", layer), results)
        saved.append((stream, first, qkv, head_out, lse, heads_low, middle, second, hidden, slope))
        stream, first = result, following
    mixed = first[None]

    sums = Sums(inside)
    whole_grad = cotangent[0].astype(FULL) * row_mask
    stream = rows_of(whole_grad, offset, span)
    grad = whole_grad.astype(LOW)
    down_sum = jnp.sum(stream, axis=0)
    split_rows = [None] * layers
    local_rows = [None] * layers
    ident = 1 + 2 * layers
    for layer in reversed(range(layers)):
        before, first, qkv, head_out, lse, heads_low, middle, second, hidden, slope = saved[layer]
        sums.add(("down", layer), dot(grad, hidden, ((0,), (0,))).astype(LOW))
        gain2 = jnp.broadcast_to(ln2_gain[layer].astype(FULL)[None], (8, width))
        (pre_grad, stream, grad_attn, sums2, columns), results = mlp_back(
            grad,
            slope,
            gathered["up", layer],
            gathered["down", layer],
            middle,
            stream,
            gain2,
            sums.jobs(),
            sizes,
            ident,
        )
        sums.back(results)
        sums.add(("up", layer), dot(second, pre_grad, ((0,), (0,))).astype(LOW))
        sums.add(("out", layer), dot(grad_attn, heads_low, ((0,), (1,))).astype(LOW))
        dout = dot(gathered["out", layer], grad_attn, ((0,), (1,))).astype(LOW)
        (grad_joint,), results = attend_back(
            dout.reshape(heads, size, capacity),
            bias,
            qkv,
            head_out,
            lse,
            size,
            sums.jobs(),
            sizes,
            ident + 1,
        )
        sums.back(results)
        grad_joint = grad_joint.reshape(joint_width, capacity)
        column_sums = jnp.sum(grad_joint.astype(FULL), axis=1).reshape(heads, 3, size)
        sums.add(("qkv", layer), dot(first, grad_joint, ((0,), (1,))).astype(LOW))
        gain1 = jnp.broadcast_to(ln1_gain[layer].astype(FULL)[None], (8, width))
        (stream, grad, sums1), results = norm_back(
            grad_joint, gathered["qkv", layer], before, stream, gain1, sums.jobs(), sizes, ident + 2
        )
        sums.back(results)
        split_rows[layer] = jnp.stack(
            [sums1[0], sums1[1], sums2[0], sums2[1], sums2[2], down_sum]
        )
        local_rows[layer] = jnp.concatenate(
            [columns[0], jnp.stack([column_sums[:, 0], column_sums[:, 2]], axis=1).reshape(-1)]
        )
        down_sum = sums1[2]
        ident = ident + 3
    token_grads = grad.astype(FULL)[None]

    local = jnp.stack(local_rows, axis=0)
    local_flat = local.reshape(-1)
    local_flat = jnp.pad(local_flat, (0, -local_flat.shape[0] % (8 * width))).reshape(-1, width)
    split = jnp.concatenate(split_rows, axis=0)
    tops = split.shape[0]
    split = jnp.pad(split, ((0, -tops % 8), (0, 0)))
    if inside:
        (totals,), results = last_sums(split, local_flat, sums.jobs(), sizes, ident)
        sums.back(results)
    else:
        totals = jnp.concatenate([total_over(("tp",), split), local_flat], axis=0)
        totals = total_over(("shard", "ctx"), totals)
    named = totals[:tops].reshape(layers, 6, width)
    local = totals[split.shape[0] :].reshape(-1)[: local.size].reshape(local.shape)
    stacked = [
        jnp.stack([sums.done[name, layer] for layer in range(layers)], axis=0)
        for name in ("qkv", "out", "up", "down")
    ]
    return (
        mixed,
        token_grads,
        named[:, 0],
        named[:, 1],
        stacked[0],
        local[:, hidden_width:],
        stacked[1],
        named[:, 4],
        named[:, 2],
        named[:, 3],
        stacked[2],
        local[:, :hidden_width],
        stacked[3],
        named[:, 5],
    )


def solution(mesh):
    split_rows = P(None, ("shard", "ctx"), "tp")
    split_tokens = P("shard", "ctx", None)
    return jax.shard_map(
        shards,
        mesh=mesh,
        in_specs=(
            split_tokens,
            P("shard", None),
            P(),
            P(),
            split_rows,
            P(None, "tp"),
            split_rows,
            P(),
            P(),
            P(),
            split_rows,
            P(None, "tp"),
            split_rows,
            P(),
            split_tokens,
        ),
        out_specs=(
            split_tokens,
            split_tokens,
            P(),
            P(),
            split_rows,
            P(None, "tp"),
            split_rows,
            P(),
            P(),
            P(),
            split_rows,
            P(None, "tp"),
            split_rows,
            P(),
        ),
        check_vma=False,
    )
```

```python
import functools
import math

import jax
import jax.numpy as jnp
from jax import lax
from jax.experimental import pallas as pl
from jax.experimental.pallas import tpu as pltpu
from jax.sharding import PartitionSpec as P

HEAD_DIM = 64
EPSILON = 1e-06
NEG_LARGE = -1e30
LOW = jnp.bfloat16
FULL = jnp.float32
PAD = 128
MESH = pl.DeviceIdType.MESH
ANY = pl.ANY
VMEM = pltpu.VMEM


def bits_of(axis):
    size = lax.axis_size(axis)
    assert size & (size - 1) == 0
    return [1 << i for i in range(size.bit_length() - 1)]


def swap(value, axis, bit):
    size = lax.axis_size(axis)
    return lax.ppermute(value, axis, [(i, i ^ bit) for i in range(size)])


def side_of(axis, bit):
    return (lax.axis_index(axis) // bit) % 2


def rows_of(value, start, count, axis=0):
    return lax.dynamic_slice_in_dim(value, start, count, axis)


def halve(axis, bits, partial, total):
    offset, span, received = jnp.int32(0), total, []

    def summed(start, count):
        value = partial(start, count)
        for got, base in received:
            value = value + rows_of(got, start - base, count).astype(FULL)
        return value

    for bit in bits:
        half = span // 2
        side = side_of(axis, bit)
        got = swap(summed(offset + (1 - side) * half, half).astype(LOW), axis, bit)
        offset = offset + side * half
        received.append((got, offset))
        span = half
    return summed(offset, span)


def double(axis, bits, value):
    for bit in bits:
        got = swap(value, axis, bit)
        first = side_of(axis, bit) == 0
        value = jnp.concatenate(
            [jnp.where(first, value, got), jnp.where(first, got, value)], axis=0
        )
    return value


def tp_scatter(partial, total):
    return halve("tp", bits_of("tp"), partial, total)


def tp_gather(value):
    return double("tp", bits_of("tp")[::-1], value)


def tp_offset(total):
    offset, span = jnp.int32(0), total
    for bit in bits_of("tp"):
        span = span // 2
        offset = offset + side_of("tp", bit) * span
    return offset, span


def total_over(axes, value):
    for axis in axes:
        for bit in bits_of(axis):
            value = value + swap(value, axis, bit)
    return value


def ring(value, by):
    count = lax.axis_size("ctx")
    return lax.ppermute(value, "ctx", [(i, (i + by) % count) for i in range(count)])


def gather_weight(piece):
    count = lax.axis_size("ctx")
    place = lax.axis_index("ctx")
    ways = lax.axis_size("shard")
    blocks = [piece] + [ring(piece, by) for by in range(1, count)]
    whole = jnp.zeros((ways * count,) + piece.shape, piece.dtype)
    me = lax.axis_index("shard")
    for by, block in enumerate(blocks):
        at = (place - by) % count
        held = [(jnp.int32(0), block)]
        for bit in bits_of("shard"):
            held = held + [(other ^ bit, swap(value, "shard", bit)) for other, value in held]
        for other, value in held:
            whole = lax.dynamic_update_index_in_dim(whole, value, (me ^ other) * count + at, 0)
    return whole.reshape((ways * count * piece.shape[0],) + piece.shape[1:]), blocks[-1]


def scatter_weight(partial, total):
    count = lax.axis_size("ctx")
    place = lax.axis_index("ctx")
    mine = halve("shard", bits_of("shard")[::-1], partial, total).astype(LOW)
    mine = mine.reshape((count, mine.shape[0] // count) + mine.shape[1:])
    value = lax.dynamic_index_in_dim(mine, place, 0, False).astype(FULL)
    for by in range(1, count):
        given = lax.dynamic_index_in_dim(mine, (place + by) % count, 0, False)
        value = value + ring(given, by).astype(FULL)
    return value


def dot(left, right, contract):
    return lax.dot_general(
        left, right, ((contract[0], contract[1]), ((), ())), preferred_element_type=FULL
    )


def turned(value):
    return value.astype(FULL).T.astype(LOW)


def normalize(rows, gain, shift):
    row_mean = jnp.mean(rows, axis=-1, keepdims=True)
    centred = rows - row_mean
    inverse = lax.rsqrt(jnp.mean(centred * centred, axis=-1, keepdims=True) + EPSILON)
    normed = centred * inverse
    return (normed * gain + shift, normed, inverse)


def normalize_back(grad_out, normed, inverse, gain):
    scaled = grad_out * gain
    mean_grad = jnp.mean(scaled, axis=-1, keepdims=True)
    mean_cross = jnp.mean(scaled * normed, axis=-1, keepdims=True)
    return inverse * (scaled - mean_grad - normed * mean_cross)


def gelu_pair(value):
    spread = 0.5 * (1.0 + lax.erf(value * (0.5**0.5)))
    slope = spread + value * jnp.exp(-0.5 * value * value) * (1.0 / math.sqrt(2.0 * math.pi))
    return (value * spread).astype(LOW), slope.astype(LOW)


class Mover:
    def __init__(self, sizes, send, recv, local):
        self.ctx_count, self.shard_count = sizes
        self.send, self.recv, self.local = send, recv, local
        self.copies, self.here = [], []
        self.arrived = set()
        self.waited = 0
        self.ctx = lax.axis_index("ctx")
        self.shard = lax.axis_index("shard")

    def go(self, source, target, **device):
        index = len(self.copies)
        copy = pltpu.make_async_remote_copy(
            src_ref=source,
            dst_ref=target,
            send_sem=self.send.at[index],
            recv_sem=self.recv.at[index],
            device_id=device,
            device_id_type=MESH,
        )
        copy.start()
        self.copies.append(copy)
        return index

    def stay(self, source, target):
        copy = pltpu.make_async_copy(source, target, self.local.at[len(self.here)])
        copy.start()
        self.here.append(copy)

    def take(self, index):
        if index not in self.arrived:
            self.arrived.add(index)
            self.copies[index].wait_recv()

    def on(self, by):
        return lax.rem(self.ctx + by, self.ctx_count)

    def back(self, by):
        return lax.rem(self.ctx + self.ctx_count - by, self.ctx_count)

    def have_local(self):
        for copy in self.here[self.waited :]:
            copy.wait()
        self.waited = len(self.here)

    def settle(self):
        for index, copy in enumerate(self.copies):
            self.take(index)
            copy.wait_send()
        self.have_local()


class Gather:
    def __init__(self, mover, source, target):
        self.mover, self.source, self.target = mover, source, target
        self.over = []

    def start(self):
        mover = self.mover
        mine, there = self.source, self.block(mover.ctx)
        self.line = [
            mover.go(mine, there, ctx=mover.on(by)) for by in range(1, mover.ctx_count)
        ]
        self.over.append(mover.go(mine, there, shard=1 - mover.shard))
        mover.stay(mine, there)

    def block(self, ctx):
        mover = self.mover
        rows = self.source.shape[0]
        start = (mover.shard * mover.ctx_count + ctx) * rows
        return self.target.at[pl.ds(pl.multiple_of(start, rows), rows)]

    def pass_on(self, by):
        mover = self.mover
        if by < mover.ctx_count:
            mover.take(self.line[by - 1])
            rows = self.block(mover.back(by))
            self.over.append(mover.go(rows, rows, shard=1 - mover.shard))

    def pass_all(self):
        for by in range(1, self.mover.ctx_count):
            self.pass_on(by)

    def have(self):
        for copy in self.over:
            self.mover.take(copy)
        self.mover.have_local()


class Jobs:
    def __init__(self, mover, kinds, sources, targets):
        self.mover = mover
        self.all = list(zip(kinds, sources, targets))

    def start(self):
        mover = self.mover
        count = mover.ctx_count
        for kind, source, target in self.all:
            if kind == "cross":
                part = source.at[pl.ds((1 - mover.shard) * count, count)]
                mover.go(part, target, shard=1 - mover.shard)
            elif kind == "line":
                for by in range(1, count):
                    mover.go(source.at[mover.on(by)], target.at[by - 1], ctx=mover.on(by))


def job_targets(kinds, sources, count):
    shapes = []
    for kind, source in zip(kinds, sources):
        if kind == "gather":
            shapes.append((2 * count * source.shape[1],) + source.shape[2:])
        elif kind == "cross":
            shapes.append((count,) + source.shape[1:])
        else:
            shapes.append((count - 1,) + source.shape[1:])
    return shapes


def job_copies(kinds, count):
    per = {"gather": 2 * count, "cross": 1, "line": count - 1}
    return sum(per[kind] for kind in kinds)


def greet(mover, kinds, ctx, mate_far):
    barrier = pltpu.get_barrier_semaphore()
    peers = []
    if ctx or "gather" in kinds or "line" in kinds:
        peers += [dict(ctx=mover.on(by)) for by in range(1, mover.ctx_count)]
    if "gather" in kinds or "cross" in kinds:
        peers.append(dict(shard=1 - mover.shard))
    if mate_far:
        peers += [dict(tp=peer) for peer in tp_peers()]
    for peer in peers:
        pl.semaphore_signal(barrier, inc=1, device_id=peer, device_id_type=MESH)
    pl.semaphore_wait(barrier, len(peers))


def tp_peers():
    place = lax.axis_index("tp")
    core, far = lax.rem(place, 2), place // 2
    return place + 1 - 2 * core, place + 2 - 4 * far


def run(kernel, name, ident, inputs, outputs, scratch, copies, jobs, sizes, vmem, flops):
    kinds, sources = jobs
    targets = job_targets(kinds, sources, sizes[0])
    n_in, n_out, n_jobs = len(inputs), len(outputs), len(kinds)
    total = copies + job_copies(kinds, sizes[0])
    n_scratch = len(scratch)

    def body(*refs):
        ins, rest = refs[:n_in], refs[n_in:]
        job_in, rest = rest[:n_jobs], rest[n_jobs:]
        outs, rest = rest[:n_out], rest[n_out:]
        job_out, rest = rest[:n_jobs], rest[n_jobs:]
        work, (send, recv, local) = rest[:n_scratch], rest[n_scratch:]
        mover = Mover(sizes, send, recv, local)
        kernel(mover, kinds, job_in, job_out, ins, outs, work)

    results = pl.pallas_call(
        body,
        in_specs=[pl.BlockSpec(memory_space=VMEM)] * n_in + [pl.BlockSpec(memory_space=ANY)] * n_jobs,
        out_specs=[pl.BlockSpec(memory_space=VMEM)] * n_out
        + [pl.BlockSpec(memory_space=VMEM if kind == "gather" else ANY) for kind in kinds],
        out_shape=[jax.ShapeDtypeStruct(shape, dtype) for shape, dtype in outputs]
        + [jax.ShapeDtypeStruct(shape, LOW) for shape in targets],
        scratch_shapes=list(scratch)
        + [
            pltpu.SemaphoreType.DMA((max(1, total),)),
            pltpu.SemaphoreType.DMA((max(1, total),)),
            pltpu.SemaphoreType.DMA((max(1, n_jobs),)),
        ],
        compiler_params=pltpu.CompilerParams(
            collective_id=ident, has_side_effects=True, vmem_limit_bytes=vmem * 2**20
        ),
        cost_estimate=pl.CostEstimate(flops=flops, bytes_accessed=2**24, transcendentals=0),
        name=name,
    )(*inputs, *sources)
    return results[:n_out], results[n_out:]


def order_of(block, count):
    return (block + count - 1) % count


def tiles_of(count, capacity, tile):
    ends = [-(-(p + 1) * capacity // tile) for p in range(count)]
    return list(zip([0] + ends[:-1], ends))


def tile_at(t, tile):
    return pl.ds(pl.multiple_of(t * tile, tile), tile)


def qkv_part(first, w_qkv, bias, parts, nat):
    rows = first.shape[0]

    def step(i, carry):
        at = pl.ds(pl.multiple_of(i * PAD, PAD), PAD)
        value = jnp.dot(first[at, :], w_qkv[...], preferred_element_type=FULL) + bias[0:1, :]
        nat[:, at] = turned(value.astype(LOW))
        return carry

    lax.fori_loop(0, rows // PAD, step, 0)
    heads, width, _ = parts.shape
    for h in range(heads):
        parts[h] = nat[h * width : (h + 1) * width, :]


def attend_part(size, tile, mover, parts, bias, heads, qkv, o_ref, lse, work, after_send, between):
    k_ref, q_ref, v_ref, low_ref = work
    count, _, capacity = parts.shape
    slots = count * capacity
    sent = [None] + [
        mover.go(parts.at[mover.on(by)], qkv.at[by], ctx=mover.on(by)) for by in range(1, count)
    ]
    after_send()
    qkv[0] = parts[mover.ctx]
    q_ref[size:PAD, :] = jnp.concatenate(
        [jnp.ones((16, slots), LOW), jnp.zeros((PAD - size - 16, slots), LOW)], axis=0
    )

    def prepare(r):
        here = slice(r * capacity, (r + 1) * capacity)
        p = order_of(r, count)
        q_ref[0:size, p * capacity : (p + 1) * capacity] = (
            qkv[r, 0:size, :] * (size**-0.5)
        ).astype(LOW)
        v_ref[:, here] = qkv[r, 2 * size : 3 * size, :]
        keys = jnp.concatenate(
            [qkv[r, size : 2 * size, :], bias[:, here], jnp.zeros((PAD - size - 16, capacity), LOW)],
            axis=0,
        )
        k_ref[here, :] = turned(keys)

    prepare(0)
    for by in range(1, count):
        mover.take(sent[by])
        prepare(by)

    def step(t, carry):
        at = tile_at(t, tile)
        scores = jnp.dot(k_ref[...], q_ref[:, at], preferred_element_type=FULL)
        top = jnp.max(scores, axis=0, keepdims=True)
        weights = jnp.exp(scores - top)
        total = jnp.sum(weights, axis=0, keepdims=True)
        summed = jnp.dot(v_ref[...], weights.astype(LOW), preferred_element_type=FULL)
        out = summed / total
        o_ref[:, at] = out
        low_ref[:, at] = out.astype(LOW)
        lse[:, at] = jnp.broadcast_to(top + jnp.log(total), (8, tile))
        return carry

    arriving = []
    for p, (low, high) in enumerate(tiles_of(count, capacity, tile)):
        lax.fori_loop(low, high, step, 0)
        done = low_ref.at[:, p * capacity : (p + 1) * capacity]
        if p < count - 1:
            arriving.append(mover.go(done, heads.at[mover.ctx], ctx=mover.back(p + 1)))
        else:
            heads[mover.ctx] = low_ref[:, p * capacity : (p + 1) * capacity]
        between(p + 1)
    for copy in arriving:
        mover.take(copy)


def attend_back_kernel(size, tile, mover, kinds, sources, targets, ins, outs, work):
    parts, bias, qkv, o_ref, lse = ins
    (grads,) = outs
    k_ref, v_ref, q_ref, do_ref, nat_ref, delta_ref, dq_ref, dk_ref, dv_ref, got, back = work
    count, _, capacity = parts.shape
    slots = count * capacity
    greet(mover, kinds, True, False)
    sent = [None] + [
        mover.go(parts.at[mover.on(by)], got.at[by], ctx=mover.on(by)) for by in range(1, count)
    ]
    Jobs(mover, kinds, sources, targets).start()
    got[0] = parts[mover.ctx]
    q_ref[size:PAD, :] = jnp.concatenate(
        [jnp.ones((16, slots), LOW), jnp.zeros((PAD - size - 16, slots), LOW)], axis=0
    )
    do_ref[size:PAD, :] = jnp.zeros((PAD - size, slots), LOW)
    dq_ref[...] = jnp.zeros_like(dq_ref)
    for r in range(count):
        here = slice(r * capacity, (r + 1) * capacity)
        pad = jnp.zeros((PAD - size - 16, capacity), LOW)
        k_ref[here, :] = turned(
            jnp.concatenate([qkv[r, size : 2 * size, :], bias[:, here], pad], axis=0)
        )
        v_ref[here, :] = turned(
            jnp.concatenate(
                [qkv[r, 2 * size : 3 * size, :], jnp.zeros((PAD - size, capacity), LOW)], axis=0
            )
        )
    for r in range(count):
        if r:
            mover.take(sent[r])
        p = order_of(r, count)
        at = slice(p * capacity, (p + 1) * capacity)
        scaled = (qkv[r, 0:size, :] * (size**-0.5)).astype(LOW)
        dout = got[r]
        q_ref[0:size, at] = scaled
        do_ref[0:size, at] = dout
        nat_ref[at, :] = turned(jnp.concatenate([scaled, dout], axis=0))
        delta = jnp.sum(dout.astype(FULL) * o_ref[:, at], axis=0, keepdims=True)
        delta_ref[:, at] = jnp.broadcast_to(delta, (8, capacity))

    tiles = tiles_of(count, capacity, tile)
    for r in list(range(1, count)) + [0]:
        here = slice(r * capacity, (r + 1) * capacity)
        dk_ref[...] = jnp.zeros_like(dk_ref)
        dv_ref[...] = jnp.zeros_like(dv_ref)

        def step(t, carry, r=r, here=here):
            at = tile_at(t, tile)
            scores = jnp.dot(k_ref[here, :], q_ref[:, at], preferred_element_type=FULL)
            chance = jnp.exp(scores - lse[0:1, at])
            chance_grad = jnp.dot(v_ref[here, :], do_ref[:, at], preferred_element_type=FULL)
            score_grad = (chance * (chance_grad - delta_ref[0:1, at])).astype(LOW)
            dq_ref[:, at] += jnp.dot(
                qkv[r, size : 2 * size, :], score_grad, preferred_element_type=FULL
            )
            dk_ref[...] += jnp.dot(score_grad, nat_ref[at, :], preferred_element_type=FULL)
            dv_ref[...] += jnp.dot(
                chance.astype(LOW), nat_ref[at, :], preferred_element_type=FULL
            )
            return carry

        if r:
            lax.fori_loop(0, tiles[-1][1], step, 0)
        else:
            for p, (low, high) in enumerate(tiles):
                lax.fori_loop(low, high, step, 0)
                at = slice(p * capacity, (p + 1) * capacity)
                value = (dq_ref[:, at] * (size**-0.5)).astype(LOW)
                if p < count - 1:
                    back[p + 1, 0:size, :] = value
                    mover.go(
                        back.at[p + 1, 0:size],
                        grads.at[mover.ctx, 0:size],
                        ctx=mover.back(p + 1),
                    )
                else:
                    grads[mover.ctx, 0:size, :] = value
        keys = dk_ref[...].T[0:size].astype(LOW)
        values = dv_ref[...].T[size : 2 * size].astype(LOW)
        if r:
            back[r, size : 2 * size, :] = keys
            back[r, 2 * size : 3 * size, :] = values
            mover.go(
                back.at[r, size : 3 * size],
                grads.at[mover.ctx, size : 3 * size],
                ctx=mover.back(r),
            )
        else:
            grads[mover.ctx, size : 2 * size, :] = keys
            grads[mover.ctx, 2 * size : 3 * size, :] = values
    mover.settle()


def attend_back(parts, bias, qkv, out, lse, size, jobs, sizes, ident):
    count, _, capacity = parts.shape
    slots = count * capacity
    tile = 256 if slots % 256 == 0 else PAD
    return run(
        functools.partial(attend_back_kernel, size, tile),
        "attend_back",
        ident,
        [parts, bias, qkv, out, lse],
        [((count, 3 * size, capacity), LOW)],
        [
            VMEM((slots, PAD), LOW),
            VMEM((slots, PAD), LOW),
            VMEM((PAD, slots), LOW),
            VMEM((PAD, slots), LOW),
            VMEM((slots, PAD), LOW),
            VMEM((8, slots), FULL),
            VMEM((size, slots), FULL),
            VMEM((capacity, PAD), FULL),
            VMEM((capacity, PAD), FULL),
            VMEM((count, size, capacity), LOW),
            VMEM((count, 3 * size, capacity), LOW),
        ],
        3 * (count - 1),
        jobs,
        sizes,
        12,
        10 * slots * slots * 256,
    )


class Round:
    def __init__(self, mover, rows, full, buffers):
        place = lax.axis_index("tp")
        core, far = lax.rem(place, 2), place // 2
        self.mover, self.full = mover, full
        self.give, self.ra, self.passing, self.rb, self.keep = buffers
        self.span = rows // 4
        self.half = self.span // 2
        self.mate, self.far = tp_peers()

        def quarter(c, f):
            return (c * 2 + f) * self.span

        self.own, self.other = quarter(core, far), quarter(core, 1 - far)
        self.mate_own, self.mate_other = quarter(1 - core, far), quarter(1 - core, 1 - far)

    def rows(self, start, count=None):
        return pl.ds(pl.multiple_of(start, 16), count or self.span)

    def hand(self, slot, value):
        self.give[slot] = value.astype(LOW)
        return self.mover.go(self.give.at[slot], self.ra.at[slot], tp=self.mate)

    def onward(self, value, index):
        self.mover.take(index)
        self.passing[...] = (value + self.ra[1].astype(FULL)).astype(LOW)
        return [
            self.mover.go(self.passing.at[at], self.rb.at[at], tp=self.far)
            for at in (pl.ds(0, self.half), pl.ds(self.half, self.half))
        ]

    def close(self, far_copies, index, finish):
        self.mover.take(index)
        self.keep[...] += self.ra[0].astype(FULL)
        self.to_far, self.to_mate = [], []
        for c in range(2):
            at = pl.ds(c * self.half, self.half)
            self.mover.take(far_copies[c])
            low = finish(at, self.keep[at] + self.rb[at].astype(FULL))
            mine = self.full.at[self.rows(self.own + c * self.half, self.half)]
            mine[...] = low
            self.to_far.append(self.mover.go(mine, mine, tp=self.far))
            self.to_mate.append(self.mover.go(mine, mine, tp=self.mate))

    def eager(self, make, finish):
        first = self.hand(1, make(self.mate_other))
        copies = self.onward(make(self.other), first)
        second = self.hand(0, make(self.mate_own))
        self.keep[...] = make(self.own)
        self.close(copies, second, finish)

    def after(self, before, make, finish):
        before.have_mate_own()
        second = self.hand(0, make(self.mate_own))
        self.keep[...] = make(self.own)
        before.have_other()
        value = make(self.other)
        before.have_mate_other()
        first = self.hand(1, make(self.mate_other))
        self.close(self.onward(value, first), second, finish)

    def have_mate_own(self):
        for copy in self.to_mate:
            self.mover.take(copy)

    def have_other(self):
        self.passed = []
        for c in range(2):
            self.mover.take(self.to_far[c])
            rows = self.full.at[self.rows(self.other + c * self.half, self.half)]
            self.passed.append(self.mover.go(rows, rows, tp=self.mate))

    def have_mate_other(self):
        for copy in self.passed:
            self.mover.take(copy)

    def end(self):
        self.have_other()
        self.mover.settle()


ROUND_COPIES = 10


def round_buffers(rows, width):
    span = rows // 4
    return [
        VMEM((2, span, width), LOW),
        VMEM((2, span, width), LOW),
        VMEM((span, width), LOW),
        VMEM((span, width), LOW),
        VMEM((span, width), FULL),
    ]


def layer_kernel(last, size, tile, starts, mover, kinds, sources, targets, ins, outs, work):
    stream_in, x_ref, bias, qkv_bias, vectors, b_up, mask = ins[:7]
    qkv, o_ref, lse, heads, middle, second, hidden, slope, stream, following = outs[:10]
    parts, joint, nat = work[:3]
    count, _, capacity = parts.shape
    rows = capacity
    at_entry, at_send, at_block = starts
    held = iter(ins[7:])
    gathers, whole = [], {}
    for (name, layer), source, target in zip(kinds.wanted, sources, targets):
        gathers.append(Gather(mover, source.at[layer], target))
        if layer == kinds.layer:
            whole[name] = gathers[-1]
    for name in ("qkv", "out", "up", "down"):
        if name not in whole:
            whole[name] = next(held)

    def weight(name):
        value = whole[name]
        if isinstance(value, Gather):
            value.have()
            value = value.target
        return value

    def begin(indices):
        for index in indices:
            gathers[index].start()

    greet(mover, list(kinds), True, True)
    b_out, gain2, shift2, b_down, gain1, shift1, gain0, shift0 = [
        vectors[i : i + 1, :] for i in range(8)
    ]
    if at_entry:
        first = outs[10]
        begin(at_entry[0])
        chunk = rows // 5 if rows % 80 == 0 else rows

        def norm_step(i, carry):
            at = pl.ds(pl.multiple_of(i * chunk, 16), chunk)
            value = normalize(stream_in[at, :].astype(FULL), gain0, shift0)[0]
            first[at, :] = value.astype(LOW)
            return carry

        lax.fori_loop(0, rows // chunk, norm_step, 0)
        for index in at_entry[0]:
            gathers[index].pass_all()
        begin(at_entry[1])
        source_rows = first
    else:
        source_rows = stream_in
    qkv_part(source_rows, weight("qkv"), qkv_bias, parts, joint)

    def after_send():
        begin(at_send)
        if at_entry:
            for index in at_entry[1]:
                gathers[index].pass_all()

    def between(p):
        for index in at_send:
            gathers[index].pass_on(p)

    attend_part(
        size, tile, mover, parts, bias, heads, qkv, o_ref, lse, work[3:7], after_send, between
    )
    begin(at_block)
    for h in range(count):
        at = slice(h * size, (h + 1) * size)
        nat[:, at] = heads[h].astype(FULL).T.astype(LOW)
    one = Round(mover, rows, second, work[7:12])
    two = Round(mover, rows, following, work[12:17])

    w_out = weight("out")

    def out_part(start):
        return dot(nat[one.rows(start), :], w_out[...], ((1,), (1,)))

    def to_second(at, value):
        value = x_ref[at] + value + b_out
        middle[at] = value
        return normalize(value, gain2, shift2)[0].astype(LOW)

    one.eager(out_part, to_second)
    w_up, w_down = weight("up"), weight("down")

    def mlp_part(start):
        at = two.rows(start)
        pre = jnp.dot(second[at, :], w_up[...], preferred_element_type=FULL) + b_up[0:1, :]
        low, low_slope = gelu_pair(pre)
        hidden[at, :] = low
        slope[at, :] = low_slope
        return dot(low, w_down[...], ((1,), (1,)))

    def to_following(at, value):
        value = middle[at] + value + b_down
        stream[at] = value
        if last:
            return (value * mask[at][:, 0:1]).astype(LOW)
        return normalize(value, gain1, shift1)[0].astype(LOW)

    two.after(one, mlp_part, to_following)
    for index in at_block:
        gathers[index].pass_all()
    two.end()


class Kinds(list):
    def __init__(self, wanted, layer):
        super().__init__(["gather"] * len(wanted))
        self.wanted, self.layer = wanted, layer


def forward_layer(
    stream_in, x, bias, qkv_bias, vectors, b_up, mask, held, wanted, layer, starts, weights, last, size, sizes, ident
):
    rows, width = stream_in.shape
    count = sizes[0]
    joint = qkv_bias.shape[1]
    hidden = b_up.shape[1]
    heads = joint // (3 * size)
    attn = heads * size
    slots = count * rows
    span = rows // 4
    tile = 256 if slots % 256 == 0 else PAD
    outputs = [
        ((count, 3 * size, rows), LOW),
        ((size, slots), FULL),
        ((8, slots), FULL),
        ((heads, size, rows), LOW),
        ((span, width), FULL),
        ((rows, width), LOW),
        ((rows, hidden), LOW),
        ((rows, hidden), LOW),
        ((span, width), FULL),
        ((rows, width), LOW),
    ]
    if starts[0]:
        outputs.append(((rows, width), LOW))
    scratch = [
        VMEM((heads, 3 * size, rows), LOW),
        VMEM((joint, rows), LOW),
        VMEM((rows, attn), LOW),
        VMEM((slots, PAD), LOW),
        VMEM((PAD, slots), LOW),
        VMEM((size, slots), LOW),
        VMEM((size, slots), LOW),
    ]
    scratch += round_buffers(rows, width) + round_buffers(rows, width)
    return run(
        functools.partial(layer_kernel, last, size, tile, starts),
        "forward_layer",
        ident,
        [stream_in, x, bias, qkv_bias, vectors, b_up, mask] + held,
        outputs,
        scratch,
        2 * (count - 1) + 2 * ROUND_COPIES,
        (Kinds(wanted, layer), [weights[name] for name, _ in wanted]),
        sizes,
        20,
        2 * rows * width * (2 * hidden + attn + joint) + 4 * slots * slots * 256,
    )


def sums_into(sums, at, values):
    for row, value in enumerate(values):
        added = jnp.sum(value, axis=0, keepdims=True)
        sums[row : row + 1, :] = added if at.start == 0 else sums[row : row + 1, :] + added


def mlp_back_kernel(mover, kinds, sources, targets, ins, outs, work):
    grad, slope, w_up, w_down, middle, x_ref, gain = ins
    pre_grad, stream, full, sums, columns = outs
    rows = grad.shape[0]
    greet(mover, kinds, False, True)
    Jobs(mover, kinds, sources, targets).start()
    one = Round(mover, rows, full, work)
    columns[...] = jnp.zeros_like(columns)

    def part(start):
        at = one.rows(start)
        pre = jnp.dot(grad[at, :], w_down[...], preferred_element_type=FULL)
        low = (pre * slope[at, :].astype(FULL)).astype(LOW)
        pre_grad[at, :] = low
        columns[0:1, :] += jnp.sum(low.astype(FULL), axis=0, keepdims=True)
        return dot(low, w_up[...], ((1,), (1,)))

    def close(at, value):
        _, normed, inverse = normalize(middle[at], 1.0, 0.0)
        result = x_ref[at] + normalize_back(value, normed, inverse, gain[0:1, :])
        stream[at] = result
        low = result.astype(LOW)
        sums_into(sums, at, (value * normed, value, low.astype(FULL)))
        return low

    one.eager(part, close)
    one.end()


def mlp_back(grad, slope, w_up, w_down, middle, x, gain, jobs, sizes, ident):
    rows, width = grad.shape
    hidden = slope.shape[1]
    span = rows // 4
    return run(
        mlp_back_kernel,
        "mlp_back",
        ident,
        [grad, slope, w_up, w_down, middle, x, gain],
        [
            ((rows, hidden), LOW),
            ((span, width), FULL),
            ((rows, width), LOW),
            ((8, width), FULL),
            ((8, hidden), FULL),
        ],
        round_buffers(rows, width),
        ROUND_COPIES,
        jobs,
        sizes,
        8,
        4 * rows * width * hidden,
    )


def norm_back_kernel(mover, kinds, sources, targets, ins, outs, work):
    joint, w_qkv, before, x_ref, gain = ins
    stream, full, sums = outs
    nat = work[0]
    rows = joint.shape[1]
    greet(mover, kinds, False, True)
    Jobs(mover, kinds, sources, targets).start()
    one = Round(mover, rows, full, work[1:])
    nat[...] = turned(joint[...])

    def part(start):
        return dot(nat[one.rows(start), :], w_qkv[...], ((1,), (1,)))

    def close(at, value):
        _, normed, inverse = normalize(before[at], 1.0, 0.0)
        result = x_ref[at] + normalize_back(value, normed, inverse, gain[0:1, :])
        stream[at] = result
        low = result.astype(LOW)
        sums_into(sums, at, (value * normed, value, low.astype(FULL)))
        return low

    one.eager(part, close)
    one.end()


def norm_back(joint, w_qkv, before, x, gain, jobs, sizes, ident):
    rows, width = joint.shape[1], w_qkv.shape[0]
    span = rows // 4
    return run(
        norm_back_kernel,
        "norm_back",
        ident,
        [joint, w_qkv, before, x, gain],
        [((span, width), FULL), ((rows, width), LOW), ((8, width), FULL)],
        [VMEM((rows, joint.shape[0]), LOW)] + round_buffers(rows, width),
        ROUND_COPIES,
        jobs,
        sizes,
        8,
        2 * rows * width * joint.shape[0],
    )


def last_kernel(mover, kinds, sources, targets, ins, outs, work):
    split, whole = ins
    (result,) = outs
    got_tp, got_shard, got_ctx, mine = work
    place = lax.axis_index("tp")
    ways = got_tp.shape[0]
    barrier = pltpu.get_barrier_semaphore()
    peers = [dict(ctx=mover.on(by)) for by in range(1, mover.ctx_count)]
    peers += [dict(shard=1 - mover.shard)]
    peers += [dict(tp=lax.rem(place + by, ways)) for by in range(1, ways)]
    for peer in peers:
        pl.semaphore_signal(barrier, inc=1, device_id=peer, device_id_type=MESH)
    pl.semaphore_wait(barrier, len(peers))
    got_tp[place] = split[...]
    tp_copies = [
        mover.go(split, got_tp.at[place], tp=lax.rem(place + by, ways)) for by in range(1, ways)
    ]
    Jobs(mover, kinds, sources, targets).start()
    for copy in tp_copies:
        mover.take(copy)
    top = split.shape[0]
    value = got_tp[0]
    for other in range(1, ways):
        value = value + got_tp[other]
    mine[0, 0:top, :] = value
    mine[0, top:, :] = whole[...]
    cross = mover.go(mine.at[0], got_shard, shard=1 - mover.shard)
    mover.take(cross)
    mine[1] = mine[0] + got_shard[...]
    got_ctx[mover.ctx] = mine[1]
    line = [
        mover.go(mine.at[1], got_ctx.at[mover.ctx], ctx=mover.on(by))
        for by in range(1, mover.ctx_count)
    ]
    for copy in line:
        mover.take(copy)
    value = got_ctx[0]
    for other in range(1, mover.ctx_count):
        value = value + got_ctx[other]
    result[...] = value
    mover.settle()


def last_sums(split, whole, jobs, sizes, ident):
    ways = lax.axis_size("tp")
    shape = (split.shape[0] + whole.shape[0], split.shape[1])
    return run(
        last_kernel,
        "last_sums",
        ident,
        [split, whole],
        [(shape, FULL)],
        [
            VMEM((ways,) + split.shape, FULL),
            VMEM(shape, FULL),
            VMEM((sizes[0],) + shape, FULL),
            VMEM((2,) + shape, FULL),
        ],
        ways - 1 + 1 + sizes[0] - 1,
        jobs,
        sizes,
        4,
        2**20,
    )


class Sums:
    def __init__(self, inside):
        self.inside = inside
        self.crossing, self.lining, self.done = [], [], {}

    def add(self, key, value):
        count = lax.axis_size("ctx")
        if not self.inside:
            self.done[key] = scatter_weight(
                lambda start, size: rows_of(value, start, size).astype(FULL), value.shape[0]
            )
            return
        ways = lax.axis_size("shard")
        blocks = value.reshape((ways * count, value.shape[0] // (ways * count)) + value.shape[1:])
        self.crossing.append((key, blocks))

    def jobs(self):
        kinds = ["cross"] * len(self.crossing) + ["line"] * len(self.lining)
        self.riding = (self.crossing, self.lining)
        self.crossing, self.lining = [], []
        return kinds, [value for _, value in self.riding[0] + self.riding[1]]

    def back(self, results):
        count = lax.axis_size("ctx")
        crossed, lined = self.riding
        for (key, blocks), got in zip(crossed, results[: len(crossed)]):
            mine = lax.dynamic_slice_in_dim(blocks, lax.axis_index("shard") * count, count, 0)
            self.lining.append((key, (mine.astype(FULL) + got.astype(FULL)).astype(LOW)))
        for (key, blocks), got in zip(lined, results[len(crossed) :]):
            mine = lax.dynamic_index_in_dim(blocks, lax.axis_index("ctx"), 0, False)
            self.done[key] = mine.astype(FULL) + jnp.sum(got.astype(FULL), axis=0)


def shards(
    tokens,
    block_tokens,
    ln1_gain,
    ln1_bias,
    w_qkv,
    b_qv,
    w_out,
    b_out,
    ln2_gain,
    ln2_bias,
    w_up,
    b_up,
    w_down,
    b_down,
    cotangent,
):
    images, capacity, width = tokens.shape
    assert images == 1
    layers = w_qkv.shape[0]
    size = HEAD_DIM
    ctx_count = lax.axis_size("ctx")
    ctx_place = lax.axis_index("ctx")
    joint_width = w_qkv.shape[2]
    heads = joint_width // (3 * size)
    assert heads == ctx_count
    attn_width = heads * size
    hidden_width = w_up.shape[2]
    offset, span = tp_offset(capacity)

    lengths = block_tokens[0]
    order = (ctx_place - jnp.arange(ctx_count, dtype=jnp.int32)) % ctx_count
    ordered = jnp.sum(
        jnp.where(
            order[:, None] == jnp.arange(ctx_count, dtype=jnp.int32)[None, :], lengths[None, :], 0
        ),
        axis=1,
    )
    usable = jnp.arange(capacity, dtype=jnp.int32)[None, :] < ordered[:, None]
    bias_row = jnp.where(usable, 0.0, NEG_LARGE).astype(LOW).reshape(1, ctx_count * capacity)
    bias = jnp.concatenate([bias_row, jnp.zeros((15, ctx_count * capacity), LOW)], axis=0)
    own_live = ordered[0]
    row_mask = (jnp.arange(capacity, dtype=jnp.int32) < own_live).astype(FULL)[:, None]
    own_mask = rows_of(row_mask, offset, span)

    weights = {"qkv": w_qkv, "out": w_out, "up": w_up, "down": w_down}
    names = ("qkv", "out", "up", "down")
    sizes = (ctx_count, lax.axis_size("shard"))
    inside = sizes[1] == 2
    gathered = {}
    if not inside:
        for name, value in weights.items():
            for layer in range(layers):
                gathered[name, layer] = gather_weight(value[layer])[0]
    whole_tokens = tokens[0]
    stream = rows_of(whole_tokens, offset, span).astype(FULL)
    source = whole_tokens
    mask = jnp.broadcast_to(own_mask, (span, PAD))
    saved = []
    for layer in range(layers):
        pair = b_qv[layer].astype(FULL).reshape(heads, 2, size)
        joint_bias = jnp.stack(
            [pair[:, 0], jnp.zeros_like(pair[:, 0]), pair[:, 1]], axis=1
        ).reshape(1, joint_width)
        joint_bias = jnp.broadcast_to(joint_bias, (8, joint_width))
        after = min(layer + 1, layers - 1)
        vectors = jnp.stack(
            [
                b_out[layer],
                ln2_gain[layer],
                ln2_bias[layer],
                b_down[layer],
                ln1_gain[after],
                ln1_bias[after],
                ln1_gain[layer],
                ln1_bias[layer],
            ]
        ).astype(FULL)
        b_up_rows = jnp.broadcast_to(b_up[layer].astype(FULL)[None], (8, hidden_width))
        last = layer == layers - 1
        wanted, starts = [], (None, [], [])
        if layer == 0:
            starts = (([], []), [], [])
        if inside:
            if layer == 0:
                wanted = [("qkv", 0), ("out", 0), ("up", 0), ("down", 0)]
                starts = (([0], [1, 2]), [3], [])
            else:
                wanted = [("out", layer), ("down", layer)]
                starts = (None, [0, 1], [])
            if not last:
                ahead = len(wanted)
                wanted = wanted + [("qkv", layer + 1), ("up", layer + 1)]
                starts = (starts[0], starts[1], [ahead, ahead + 1])
        held = [gathered[name, layer] for name in names if (name, layer) not in wanted]
        outs, results = forward_layer(
            source,
            stream,
            bias,
            joint_bias,
            vectors,
            b_up_rows,
            mask,
            held,
            wanted,
            layer,
            starts,
            weights,
            last,
            size,
            sizes,
            1 + layer,
        )
        for key, value in zip(wanted, results):
            gathered[key] = value
        qkv, head_out, lse, heads_low, middle, second, hidden, slope, result, following = outs[:10]
        first = source if layer else outs[10]
        heads_low = heads_low.reshape(attn_width, capacity)
        saved.append((stream, first, qkv, head_out, lse, heads_low, middle, second, hidden, slope))
        stream, source = result, following
    first = source
    mixed = first[None]

    sums = Sums(inside)
    whole_grad = cotangent[0].astype(FULL) * row_mask
    stream = rows_of(whole_grad, offset, span)
    grad = whole_grad.astype(LOW)
    down_sum = jnp.sum(stream, axis=0)
    split_rows = [None] * layers
    local_rows = [None] * layers
    ident = 1 + 2 * layers
    for layer in reversed(range(layers)):
        before, first, qkv, head_out, lse, heads_low, middle, second, hidden, slope = saved[layer]
        sums.add(("down", layer), dot(grad, hidden, ((0,), (0,))).astype(LOW))
        gain2 = jnp.broadcast_to(ln2_gain[layer].astype(FULL)[None], (8, width))
        (pre_grad, stream, grad_attn, sums2, columns), results = mlp_back(
            grad,
            slope,
            gathered["up", layer],
            gathered["down", layer],
            middle,
            stream,
            gain2,
            sums.jobs(),
            sizes,
            ident,
        )
        sums.back(results)
        sums.add(("up", layer), dot(second, pre_grad, ((0,), (0,))).astype(LOW))
        sums.add(("out", layer), dot(grad_attn, heads_low, ((0,), (1,))).astype(LOW))
        dout = dot(gathered["out", layer], grad_attn, ((0,), (1,))).astype(LOW)
        (grad_joint,), results = attend_back(
            dout.reshape(heads, size, capacity),
            bias,
            qkv,
            head_out,
            lse,
            size,
            sums.jobs(),
            sizes,
            ident + 1,
        )
        sums.back(results)
        grad_joint = grad_joint.reshape(joint_width, capacity)
        column_sums = jnp.sum(grad_joint.astype(FULL), axis=1).reshape(heads, 3, size)
        sums.add(("qkv", layer), dot(first, grad_joint, ((0,), (1,))).astype(LOW))
        gain1 = jnp.broadcast_to(ln1_gain[layer].astype(FULL)[None], (8, width))
        (stream, grad, sums1), results = norm_back(
            grad_joint, gathered["qkv", layer], before, stream, gain1, sums.jobs(), sizes, ident + 2
        )
        sums.back(results)
        split_rows[layer] = jnp.stack(
            [sums1[0], sums1[1], sums2[0], sums2[1], sums2[2], down_sum]
        )
        local_rows[layer] = jnp.concatenate(
            [columns[0], jnp.stack([column_sums[:, 0], column_sums[:, 2]], axis=1).reshape(-1)]
        )
        down_sum = sums1[2]
        ident = ident + 3
    token_grads = grad.astype(FULL)[None]

    local = jnp.stack(local_rows, axis=0)
    local_flat = local.reshape(-1)
    local_flat = jnp.pad(local_flat, (0, -local_flat.shape[0] % (8 * width))).reshape(-1, width)
    split = jnp.concatenate(split_rows, axis=0)
    tops = split.shape[0]
    split = jnp.pad(split, ((0, -tops % 8), (0, 0)))
    if inside:
        (totals,), results = last_sums(split, local_flat, sums.jobs(), sizes, ident)
        sums.back(results)
    else:
        totals = jnp.concatenate([total_over(("tp",), split), local_flat], axis=0)
        totals = total_over(("shard", "ctx"), totals)
    named = totals[:tops].reshape(layers, 6, width)
    local = totals[split.shape[0] :].reshape(-1)[: local.size].reshape(local.shape)
    stacked = [
        jnp.stack([sums.done[name, layer] for layer in range(layers)], axis=0)
        for name in ("qkv", "out", "up", "down")
    ]
    return (
        mixed,
        token_grads,
        named[:, 0],
        named[:, 1],
        stacked[0],
        local[:, hidden_width:],
        stacked[1],
        named[:, 4],
        named[:, 2],
        named[:, 3],
        stacked[2],
        local[:, :hidden_width],
        stacked[3],
        named[:, 5],
    )


def solution(mesh):
    split_rows = P(None, ("shard", "ctx"), "tp")
    split_tokens = P("shard", "ctx", None)
    return jax.shard_map(
        shards,
        mesh=mesh,
        in_specs=(
            split_tokens,
            P("shard", None),
            P(),
            P(),
            split_rows,
            P(None, "tp"),
            split_rows,
            P(),
            P(),
            P(),
            split_rows,
            P(None, "tp"),
            split_rows,
            P(),
            split_tokens,
        ),
        out_specs=(
            split_tokens,
            split_tokens,
            P(),
            P(),
            split_rows,
            P(None, "tp"),
            split_rows,
            P(),
            P(),
            P(),
            split_rows,
            P(None, "tp"),
            split_rows,
            P(),
        ),
        check_vma=False,
    )
```

```python
import functools
import math

import jax
import jax.numpy as jnp
from jax import lax
from jax.experimental import pallas as pl
from jax.experimental.pallas import tpu as pltpu
from jax.sharding import PartitionSpec as P

HEAD_DIM = 64
EPSILON = 1e-06
NEG_LARGE = -1e30
LOW = jnp.bfloat16
FULL = jnp.float32
PAD = 128
MESH = pl.DeviceIdType.MESH
VMEM = pltpu.VMEM
HBM = pltpu.HBM


def bits_of(axis):
    size = lax.axis_size(axis)
    assert size & (size - 1) == 0
    return [1 << i for i in range(size.bit_length() - 1)]


def swap(value, axis, bit):
    size = lax.axis_size(axis)
    return lax.ppermute(value, axis, [(i, i ^ bit) for i in range(size)])


def side_of(axis, bit):
    return (lax.axis_index(axis) // bit) % 2


def rows_of(value, start, count, axis=0):
    return lax.dynamic_slice_in_dim(value, start, count, axis)


def halve(axis, bits, partial, total):
    offset, span, received = jnp.int32(0), total, []

    def summed(start, count):
        value = partial(start, count)
        for got, base in received:
            value = value + rows_of(got, start - base, count).astype(FULL)
        return value

    for bit in bits:
        half = span // 2
        side = side_of(axis, bit)
        got = swap(summed(offset + (1 - side) * half, half).astype(LOW), axis, bit)
        offset = offset + side * half
        received.append((got, offset))
        span = half
    return summed(offset, span)


def double(axis, bits, value):
    for bit in bits:
        got = swap(value, axis, bit)
        first = side_of(axis, bit) == 0
        value = jnp.concatenate(
            [jnp.where(first, value, got), jnp.where(first, got, value)], axis=0
        )
    return value


def total_over(axes, value):
    for axis in axes:
        for bit in bits_of(axis):
            value = value + swap(value, axis, bit)
    return value


def ring(value, by):
    count = lax.axis_size("ctx")
    return lax.ppermute(value, "ctx", [(i, (i + by) % count) for i in range(count)])


def gather_weight(piece):
    count = lax.axis_size("ctx")
    place = lax.axis_index("ctx")
    ways = lax.axis_size("shard")
    blocks = [piece] + [ring(piece, by) for by in range(1, count)]
    whole = jnp.zeros((ways * count,) + piece.shape, piece.dtype)
    me = lax.axis_index("shard")
    for by, block in enumerate(blocks):
        at = (place - by) % count
        held = [(jnp.int32(0), block)]
        for bit in bits_of("shard"):
            held = held + [(other ^ bit, swap(value, "shard", bit)) for other, value in held]
        for other, value in held:
            whole = lax.dynamic_update_index_in_dim(whole, value, (me ^ other) * count + at, 0)
    return whole.reshape((ways * count * piece.shape[0],) + piece.shape[1:]), blocks[-1]


def scatter_weight(partial, total):
    count = lax.axis_size("ctx")
    place = lax.axis_index("ctx")
    mine = halve("shard", bits_of("shard")[::-1], partial, total).astype(LOW)
    mine = mine.reshape((count, mine.shape[0] // count) + mine.shape[1:])
    value = lax.dynamic_index_in_dim(mine, place, 0, False).astype(FULL)
    for by in range(1, count):
        given = lax.dynamic_index_in_dim(mine, (place + by) % count, 0, False)
        value = value + ring(given, by).astype(FULL)
    return value


def dot(left, right, contract):
    return lax.dot_general(
        left, right, ((contract[0], contract[1]), ((), ())), preferred_element_type=FULL
    )


def turned(value):
    return value.astype(FULL).T.astype(LOW)


def normalize(rows, gain, shift):
    row_mean = jnp.mean(rows, axis=-1, keepdims=True)
    centred = rows - row_mean
    inverse = lax.rsqrt(jnp.mean(centred * centred, axis=-1, keepdims=True) + EPSILON)
    normed = centred * inverse
    return (normed * gain + shift, normed, inverse)


def normalize_back(grad_out, normed, inverse, gain):
    scaled = grad_out * gain
    mean_grad = jnp.mean(scaled, axis=-1, keepdims=True)
    mean_cross = jnp.mean(scaled * normed, axis=-1, keepdims=True)
    return inverse * (scaled - mean_grad - normed * mean_cross)


def gelu_pair(value):
    spread = 0.5 * (1.0 + lax.erf(value * (0.5**0.5)))
    slope = spread + value * jnp.exp(-0.5 * value * value) * (1.0 / math.sqrt(2.0 * math.pi))
    return (value * spread).astype(LOW), slope.astype(LOW)


class Mover:
    def __init__(self, sizes, send, recv, local):
        self.ctx_count, self.shard_count = sizes
        self.send, self.recv, self.local = send, recv, local
        self.copies, self.here = [], []
        self.arrived = set()
        self.landed = set()
        self.ctx = lax.axis_index("ctx")
        self.shard = lax.axis_index("shard")

    def go(self, source, target, **device):
        index = len(self.copies)
        copy = pltpu.make_async_remote_copy(
            src_ref=source,
            dst_ref=target,
            send_sem=self.send.at[index],
            recv_sem=self.recv.at[index],
            device_id=device,
            device_id_type=MESH,
        )
        copy.start()
        self.copies.append(copy)
        return index

    def stay(self, source, target):
        index = len(self.here)
        copy = pltpu.make_async_copy(source, target, self.local.at[index])
        copy.start()
        self.here.append(copy)
        return index

    def near(self, *indices):
        for index in indices:
            if index not in self.landed:
                self.landed.add(index)
                self.here[index].wait()

    def take(self, index):
        if index not in self.arrived:
            self.arrived.add(index)
            self.copies[index].wait_recv()

    def on(self, by):
        return lax.rem(self.ctx + by, self.ctx_count)

    def back(self, by):
        return lax.rem(self.ctx + self.ctx_count - by, self.ctx_count)

    def settle(self):
        for index, copy in enumerate(self.copies):
            self.take(index)
            copy.wait_send()
        self.near(*range(len(self.here)))


class Gather:
    def __init__(self, mover, source, target):
        self.mover, self.source, self.target = mover, source, target
        self.over = []

    def start(self):
        mover = self.mover
        mine, there = self.source, self.block(mover.ctx)
        self.line = [
            mover.go(mine, there, ctx=mover.on(by)) for by in range(1, mover.ctx_count)
        ]
        self.over.append(mover.go(mine, there, shard=1 - mover.shard))
        self.own = mover.stay(mine, there)

    def block(self, ctx):
        mover = self.mover
        rows = self.source.shape[0]
        start = (mover.shard * mover.ctx_count + ctx) * rows
        return self.target.at[pl.ds(pl.multiple_of(start, rows), rows)]

    def pass_on(self, by):
        mover = self.mover
        if by < mover.ctx_count:
            mover.take(self.line[by - 1])
            rows = self.block(mover.back(by))
            self.over.append(mover.go(rows, rows, shard=1 - mover.shard))

    def pass_all(self):
        for by in range(1, self.mover.ctx_count):
            self.pass_on(by)

    def have(self):
        for copy in self.over:
            self.mover.take(copy)
        self.mover.near(self.own)


class Reduce:
    def __init__(self, mover, buffers, out, lhs, rhs):
        self.mover, self.out, self.lhs, self.rhs = mover, out, lhs, rhs
        self.give, self.got, self.mid, self.line = buffers
        self.half = self.give.shape[0]
        self.block = self.half // mover.ctx_count

    def compute(self, target, shard):
        chunk = min(256, self.half)

        def step(i, carry):
            at = pl.ds(pl.multiple_of(shard * self.half + i * chunk, chunk), chunk)
            here = pl.ds(pl.multiple_of(i * chunk, chunk), chunk)
            target[here, :] = dot(self.lhs[:, at], self.rhs[...], ((0,), (0,))).astype(LOW)
            return carry

        lax.fori_loop(0, self.half // chunk, step, 0)

    def begin(self):
        mover = self.mover
        self.compute(self.give, 1 - mover.shard)
        self.cross = mover.go(self.give, self.got, shard=1 - mover.shard)
        self.compute(self.mid, mover.shard)

    def fold(self):
        self.mover.take(self.cross)
        self.mid[...] = (self.mid[...].astype(FULL) + self.got[...].astype(FULL)).astype(LOW)

    def spread(self):
        mover = self.mover
        self.lines = [
            mover.go(self.rows(mover.on(by)), self.line.at[by - 1], ctx=mover.on(by))
            for by in range(1, mover.ctx_count)
        ]

    def rows(self, ctx):
        return self.mid.at[pl.ds(pl.multiple_of(ctx * self.block, self.block), self.block)]

    def done(self):
        value = self.rows(self.mover.ctx)[...].astype(FULL)
        for index, copy in enumerate(self.lines):
            self.mover.take(copy)
            value = value + self.line[index].astype(FULL)
        self.out[...] = value


def reduce_buffers(half, width, count):
    return [
        VMEM((half, width), LOW),
        VMEM((half, width), LOW),
        VMEM((half, width), LOW),
        VMEM((count - 1, half // count, width), LOW),
    ]


def greet(mover, shard):
    barrier = pltpu.get_barrier_semaphore()
    peers = [dict(ctx=mover.on(by)) for by in range(1, mover.ctx_count)]
    peers += [dict(tp=peer) for peer in tp_peers()]
    if shard:
        peers.append(dict(shard=1 - mover.shard))
    for peer in peers:
        pl.semaphore_signal(barrier, inc=1, device_id=peer, device_id_type=MESH)
    pl.semaphore_wait(barrier, len(peers))


def tp_peers():
    place = lax.axis_index("tp")
    core, far = lax.rem(place, 2), place // 2
    return place + 1 - 2 * core, place + 2 - 4 * far


def run(kernel, name, ident, inputs, outputs, scratch, remote, local, sizes, vmem, flops):
    n_in, n_out, n_scratch = len(inputs), len(outputs), len(scratch)

    def body(*refs):
        ins, outs = refs[:n_in], refs[n_in : n_in + n_out]
        work = refs[n_in + n_out :]
        mover = Mover(sizes, *work[n_scratch:])
        kernel(mover, ins, outs, work[:n_scratch])

    return pl.pallas_call(
        body,
        in_specs=[pl.BlockSpec(memory_space=space) for _, space in inputs],
        out_specs=[pl.BlockSpec(memory_space=space) for _, _, space in outputs],
        out_shape=[jax.ShapeDtypeStruct(shape, dtype) for shape, dtype, _ in outputs],
        scratch_shapes=list(scratch)
        + [
            pltpu.SemaphoreType.DMA((remote,)),
            pltpu.SemaphoreType.DMA((remote,)),
            pltpu.SemaphoreType.DMA((local,)),
        ],
        compiler_params=pltpu.CompilerParams(
            collective_id=ident, has_side_effects=True, vmem_limit_bytes=vmem * 2**20
        ),
        cost_estimate=pl.CostEstimate(flops=flops, bytes_accessed=2**24, transcendentals=0),
        name=name,
    )(*[value for value, _ in inputs])


def order_of(block, count):
    return (block + count - 1) % count


def tiles_of(count, capacity, tile):
    ends = [-(-(p + 1) * capacity // tile) for p in range(count)]
    return list(zip([0] + ends[:-1], ends))


def tile_at(t, tile):
    return pl.ds(pl.multiple_of(t * tile, tile), tile)


def turned_product(left, right, bias, target):
    def step(i, carry):
        at = pl.ds(pl.multiple_of(i * PAD, PAD), PAD)
        value = jnp.dot(left[at, :], right[...], preferred_element_type=FULL)
        if bias is not None:
            value = value + bias[0:1, :]
        target[:, at] = turned(value.astype(LOW))
        return carry

    lax.fori_loop(0, left.shape[0] // PAD, step, 0)


def head_rows(ref, head, width):
    return ref.at[pl.ds(pl.multiple_of(head * width, 16), width)]


def attend_part(size, tile, mover, joint, bias, heads, qkv, o_ref, lse, work, after_send, between):
    k_ref, q_ref, v_ref, low_ref = work
    count, width, capacity = qkv.shape
    slots = count * capacity
    sent = [None] + [
        mover.go(head_rows(joint, mover.on(by), width), qkv.at[by], ctx=mover.on(by))
        for by in range(1, count)
    ]
    after_send()
    qkv[0] = head_rows(joint, mover.ctx, width)[...]
    q_ref[size:PAD, :] = jnp.concatenate(
        [jnp.ones((16, slots), LOW), jnp.zeros((PAD - size - 16, slots), LOW)], axis=0
    )

    def prepare(r):
        here = slice(r * capacity, (r + 1) * capacity)
        p = order_of(r, count)
        q_ref[0:size, p * capacity : (p + 1) * capacity] = (
            qkv[r, 0:size, :] * (size**-0.5)
        ).astype(LOW)
        v_ref[:, here] = qkv[r, 2 * size : 3 * size, :]
        keys = jnp.concatenate(
            [qkv[r, size : 2 * size, :], bias[:, here], jnp.zeros((PAD - size - 16, capacity), LOW)],
            axis=0,
        )
        k_ref[here, :] = turned(keys)

    prepare(0)
    for by in range(1, count):
        mover.take(sent[by])
        prepare(by)

    def step(t, carry):
        at = tile_at(t, tile)
        scores = jnp.dot(k_ref[...], q_ref[:, at], preferred_element_type=FULL)
        top = jnp.max(scores, axis=0, keepdims=True)
        weights = jnp.exp(scores - top)
        total = jnp.sum(weights, axis=0, keepdims=True)
        summed = jnp.dot(v_ref[...], weights.astype(LOW), preferred_element_type=FULL)
        out = summed / total
        o_ref[:, at] = out
        low_ref[:, at] = out.astype(LOW)
        lse[:, at] = jnp.broadcast_to(top + jnp.log(total), (8, tile))
        return carry

    arriving = []
    for p, (low, high) in enumerate(tiles_of(count, capacity, tile)):
        lax.fori_loop(low, high, step, 0)
        done = low_ref.at[:, p * capacity : (p + 1) * capacity]
        if p < count - 1:
            there = head_rows(heads, mover.ctx, size)
            arriving.append(mover.go(done, there, ctx=mover.back(p + 1)))
        else:
            head_rows(heads, mover.ctx, size)[...] = low_ref[:, p * capacity : (p + 1) * capacity]
        between(p + 1)
    for copy in arriving:
        mover.take(copy)


def attend_back_part(size, tile, mover, parts, bias, qkv, o_ref, lse, grads, work, ready, waiting, between):
    k_ref, v_ref, q_ref, do_ref, nat_ref, delta_ref, dq_ref, dk_ref, dv_ref, got, back = work
    count, width, capacity = qkv.shape
    slots = count * capacity
    sent = [None] + [
        mover.go(head_rows(parts, mover.on(by), size), got.at[by], ctx=mover.on(by))
        for by in range(1, count)
    ]
    got[0] = head_rows(parts, mover.ctx, size)[...]
    waiting()
    ready()
    q_ref[size:PAD, :] = jnp.concatenate(
        [jnp.ones((16, slots), LOW), jnp.zeros((PAD - size - 16, slots), LOW)], axis=0
    )
    do_ref[size:PAD, :] = jnp.zeros((PAD - size, slots), LOW)
    dq_ref[...] = jnp.zeros_like(dq_ref)
    for r in range(count):
        here = slice(r * capacity, (r + 1) * capacity)
        pad = jnp.zeros((PAD - size - 16, capacity), LOW)
        k_ref[here, :] = turned(
            jnp.concatenate([qkv[r, size : 2 * size, :], bias[:, here], pad], axis=0)
        )
        v_ref[here, :] = turned(
            jnp.concatenate(
                [qkv[r, 2 * size : 3 * size, :], jnp.zeros((PAD - size, capacity), LOW)], axis=0
            )
        )
    for r in range(count):
        if r:
            mover.take(sent[r])
        p = order_of(r, count)
        at = slice(p * capacity, (p + 1) * capacity)
        scaled = (qkv[r, 0:size, :] * (size**-0.5)).astype(LOW)
        dout = got[r]
        q_ref[0:size, at] = scaled
        do_ref[0:size, at] = dout
        nat_ref[at, :] = turned(jnp.concatenate([scaled, dout], axis=0))
        delta = jnp.sum(dout.astype(FULL) * o_ref[:, at], axis=0, keepdims=True)
        delta_ref[:, at] = jnp.broadcast_to(delta, (8, capacity))

    tiles = tiles_of(count, capacity, tile)
    arriving = []
    mine = head_rows(grads, mover.ctx, width)
    for turn, r in enumerate(list(range(1, count)) + [0]):
        here = slice(r * capacity, (r + 1) * capacity)
        dk_ref[...] = jnp.zeros_like(dk_ref)
        dv_ref[...] = jnp.zeros_like(dv_ref)

        def step(t, carry, r=r, here=here):
            at = tile_at(t, tile)
            scores = jnp.dot(k_ref[here, :], q_ref[:, at], preferred_element_type=FULL)
            chance = jnp.exp(scores - lse[0:1, at])
            chance_grad = jnp.dot(v_ref[here, :], do_ref[:, at], preferred_element_type=FULL)
            score_grad = (chance * (chance_grad - delta_ref[0:1, at])).astype(LOW)
            dq_ref[:, at] += jnp.dot(
                qkv[r, size : 2 * size, :], score_grad, preferred_element_type=FULL
            )
            dk_ref[...] += jnp.dot(score_grad, nat_ref[at, :], preferred_element_type=FULL)
            dv_ref[...] += jnp.dot(
                chance.astype(LOW), nat_ref[at, :], preferred_element_type=FULL
            )
            return carry

        if r:
            lax.fori_loop(0, tiles[-1][1], step, 0)
        else:
            for p, (low, high) in enumerate(tiles):
                lax.fori_loop(low, high, step, 0)
                at = slice(p * capacity, (p + 1) * capacity)
                value = (dq_ref[:, at] * (size**-0.5)).astype(LOW)
                if p < count - 1:
                    back[p + 1, 0:size, :] = value
                    arriving.append(
                        mover.go(
                            back.at[p + 1, 0:size], mine.at[0:size], ctx=mover.back(p + 1)
                        )
                    )
                else:
                    mine[0:size, :] = value
        keys = dk_ref[...].T[0:size].astype(LOW)
        values = dv_ref[...].T[size : 2 * size].astype(LOW)
        if r:
            back[r, size : 2 * size, :] = keys
            back[r, 2 * size : 3 * size, :] = values
            arriving.append(
                mover.go(
                    back.at[r, size : 3 * size], mine.at[size : 3 * size], ctx=mover.back(r)
                )
            )
        else:
            mine[size : 2 * size, :] = keys
            mine[2 * size : 3 * size, :] = values
        between(turn)
    for copy in arriving:
        mover.take(copy)


def attend_back_buffers(size, count, capacity):
    slots = count * capacity
    return [
        VMEM((slots, PAD), LOW),
        VMEM((slots, PAD), LOW),
        VMEM((PAD, slots), LOW),
        VMEM((PAD, slots), LOW),
        VMEM((slots, PAD), LOW),
        VMEM((8, slots), FULL),
        VMEM((size, slots), FULL),
        VMEM((capacity, PAD), FULL),
        VMEM((capacity, PAD), FULL),
        VMEM((count, size, capacity), LOW),
        VMEM((count, 3 * size, capacity), LOW),
    ]


class Round:
    def __init__(self, mover, rows, full, buffers):
        place = lax.axis_index("tp")
        core, far = lax.rem(place, 2), place // 2
        self.mover, self.full = mover, full
        self.give, self.ra, self.passing, self.rb, self.keep = buffers
        self.span = rows // 4
        self.half = self.span // 2
        self.mate, self.far = tp_peers()

        def quarter(c, f):
            return (c * 2 + f) * self.span

        self.own, self.other = quarter(core, far), quarter(core, 1 - far)
        self.mate_own, self.mate_other = quarter(1 - core, far), quarter(1 - core, 1 - far)

    def rows(self, start, count=None):
        return pl.ds(pl.multiple_of(start, 16), count or self.span)

    def hand(self, slot, value):
        self.give[slot] = value.astype(LOW)
        return self.mover.go(self.give.at[slot], self.ra.at[slot], tp=self.mate)

    def onward(self, value, index):
        self.mover.take(index)
        self.passing[...] = (value + self.ra[1].astype(FULL)).astype(LOW)
        return [
            self.mover.go(self.passing.at[at], self.rb.at[at], tp=self.far)
            for at in (pl.ds(0, self.half), pl.ds(self.half, self.half))
        ]

    def close(self, far_copies, index, finish):
        self.mover.take(index)
        self.keep[...] += self.ra[0].astype(FULL)
        self.to_far, self.to_mate = [], []
        for c in range(2):
            at = pl.ds(c * self.half, self.half)
            self.mover.take(far_copies[c])
            low = finish(at, self.keep[at] + self.rb[at].astype(FULL))
            mine = self.full.at[self.rows(self.own + c * self.half, self.half)]
            mine[...] = low
            self.to_far.append(self.mover.go(mine, mine, tp=self.far))
            self.to_mate.append(self.mover.go(mine, mine, tp=self.mate))

    def eager(self, make, finish, meanwhile=None):
        first = self.hand(1, make(self.mate_other))
        copies = self.onward(make(self.other), first)
        second = self.hand(0, make(self.mate_own))
        self.keep[...] = make(self.own)
        if meanwhile:
            meanwhile()
        self.close(copies, second, finish)

    def after(self, before, make, finish, meanwhile=None):
        before.have_mate_own()
        second = self.hand(0, make(self.mate_own))
        self.keep[...] = make(self.own)
        before.have_other()
        value = make(self.other)
        before.have_mate_other()
        first = self.hand(1, make(self.mate_other))
        copies = self.onward(value, first)
        if meanwhile:
            meanwhile()
        self.close(copies, second, finish)

    def have_mate_own(self):
        for copy in self.to_mate:
            self.mover.take(copy)

    def have_other(self):
        self.passed = []
        for c in range(2):
            self.mover.take(self.to_far[c])
            rows = self.full.at[self.rows(self.other + c * self.half, self.half)]
            self.passed.append(self.mover.go(rows, rows, tp=self.mate))

    def have_mate_other(self):
        for copy in self.passed:
            self.mover.take(copy)

    def have(self):
        self.have_mate_own()
        self.have_other()
        self.have_mate_other()


ROUND_COPIES = 10


def round_buffers(rows, width):
    span = rows // 4
    return [
        VMEM((2, span, width), LOW),
        VMEM((2, span, width), LOW),
        VMEM((span, width), LOW),
        VMEM((span, width), LOW),
        VMEM((span, width), FULL),
    ]


NAMES = ("qkv", "out", "up", "down")


def layer_kernel(plan, last, size, tile, mover, ins, outs, work):
    ins, outs, work = iter(ins), iter(outs), iter(work)
    source = next(ins)
    x_ref = None if plan.entry else next(ins)
    bias, qkv_bias, vectors, b_up, mask = [next(ins) for _ in range(5)]
    stream, following = next(outs), next(outs)
    far_qkv, far_o, far_lse, far_heads, far_middle, far_second, far_hidden, far_slope = [
        next(outs) for _ in range(8)
    ]
    far_first = next(outs) if plan.entry else None
    joint, nat, heads, qkv, o_ref, lse, middle, second, hidden, slope = [
        next(work) for _ in range(10)
    ]
    first = next(work) if plan.entry else source
    attend_work = [next(work) for _ in range(4)]
    one_work, two_work = [next(work) for _ in range(5)], [next(work) for _ in range(5)]
    rows = source.shape[0]
    whole = {name: next(work) for name in NAMES}
    gathers, loads = {}, {}
    for name in plan.held:
        loads[name] = (next(ins), whole[name])
    for name in plan.own:
        gathers[name, 0] = Gather(mover, next(ins).at[plan.layer], whole[name])
    for name in plan.ahead:
        gathers[name, 1] = Gather(mover, next(ins).at[plan.layer + 1], next(outs))
    kept = {name: next(outs) for name in plan.own}

    greet(mover, bool(gathers))
    loads = {name: mover.stay(*pair) for name, pair in loads.items()}

    def have(name):
        if name in loads:
            mover.near(loads[name])
        else:
            gathers[name, 0].have()
            mover.stay(whole[name], kept[name])
        return whole[name]

    def begin(keys):
        for key in keys:
            if key in gathers:
                gathers[key].start()

    def pass_on(keys, by):
        for key in keys:
            if key in gathers:
                gathers[key].pass_on(by)

    def pass_all(keys):
        for by in range(1, mover.ctx_count):
            pass_on(keys, by)

    b_out, gain2, shift2, b_down, gain1, shift1, gain0, shift0 = [
        vectors[i : i + 1, :] for i in range(8)
    ]
    one = Round(mover, rows, second, one_work)
    two = Round(mover, rows, following, two_work)
    if plan.entry:
        begin([("qkv", 0)])
        chunk = rows // 5 if rows % 80 == 0 else rows

        def norm_step(i, carry):
            at = pl.ds(pl.multiple_of(i * chunk, 16), chunk)
            value = normalize(source[at, :].astype(FULL), gain0, shift0)[0]
            first[at, :] = value.astype(LOW)
            return carry

        lax.fori_loop(0, rows // chunk, norm_step, 0)
        mover.stay(first, far_first)
        pass_all([("qkv", 0)])
        begin([("out", 0), ("up", 0)])
        turned_product(first, have("qkv"), qkv_bias, joint)
    else:
        turned_product(first, have("qkv"), qkv_bias, joint)

    def after_send():
        if plan.entry:
            pass_all([("out", 0), ("up", 0)])
        else:
            begin([("out", 0), ("down", 0)])

    def between(p):
        if plan.entry and p == 1:
            begin([("down", 0)])
        if not plan.entry:
            pass_on([("out", 0), ("down", 0)], p)

    attend_part(
        size, tile, mover, joint, bias, heads, qkv, o_ref, lse, attend_work, after_send, between
    )
    nat[...] = turned(heads[...])
    mover.stay(qkv, far_qkv)
    mover.stay(o_ref, far_o)
    mover.stay(lse, far_lse)
    mover.stay(nat, far_heads)
    w_out = have("out")

    def out_part(start):
        return dot(nat[one.rows(start), :], w_out[...], ((1,), (1,)))

    def to_second(at, value):
        if plan.entry:
            before = source[one.rows(one.own + at.start, at.size), :].astype(FULL)
        else:
            before = x_ref[at]
        value = before + value + b_out
        middle[at] = value
        return normalize(value, gain2, shift2)[0].astype(LOW)

    if plan.entry:
        one.eager(out_part, to_second, lambda: pass_all([("down", 0)]))
    else:
        one.eager(out_part, to_second)
    begin([("qkv", 1), ("up", 1)])
    w_up, w_down = have("up"), have("down")

    def mlp_part(start):
        at = two.rows(start)
        pre = jnp.dot(second[at, :], w_up[...], preferred_element_type=FULL) + b_up[0:1, :]
        low, low_slope = gelu_pair(pre)
        hidden[at, :] = low
        slope[at, :] = low_slope
        return dot(low, w_down[...], ((1,), (1,)))

    def to_following(at, value):
        value = middle[at] + value + b_down
        stream[at] = value
        if last:
            live = mask[two.rows(two.own + at.start, at.size), 0:1]
            return (value * live).astype(LOW)
        return normalize(value, gain1, shift1)[0].astype(LOW)

    def meanwhile():
        mover.stay(middle, far_middle)
        mover.stay(second, far_second)
        mover.stay(hidden, far_hidden)
        mover.stay(slope, far_slope)
        pass_all([("qkv", 1), ("up", 1)])

    two.after(one, mlp_part, to_following, meanwhile)
    two.have()
    mover.settle()


class Plan:
    def __init__(self, layer, last, inside):
        self.layer, self.entry = layer, layer == 0
        self.own = (NAMES if layer == 0 else ("out", "down")) if inside else ()
        self.ahead = ("qkv", "up") if inside and not last else ()
        self.held = tuple(name for name in NAMES if name not in self.own)


def forward_layer(source, x, bias, qkv_bias, vectors, b_up, mask, gathered, weights, plan, last, size, sizes, ident):
    rows, width = source.shape
    count = sizes[0]
    joint, hidden = qkv_bias.shape[1], b_up.shape[1]
    heads = joint // (3 * size)
    attn, slots, span = heads * size, count * rows, rows // 4
    tile = 256 if slots % 256 == 0 else PAD
    columns = {"qkv": joint, "out": attn, "up": hidden, "down": hidden}
    inputs = [(source, VMEM)] + ([] if plan.entry else [(x, VMEM)])
    inputs += [(value, VMEM) for value in (bias, qkv_bias, vectors, b_up, mask)]
    inputs += [(gathered[name, plan.layer], HBM) for name in plan.held]
    inputs += [(weights[name], HBM) for name in plan.own + plan.ahead]
    saved = [
        ((count, 3 * size, rows), LOW),
        ((size, slots), FULL),
        ((8, slots), FULL),
        ((rows, attn), LOW),
        ((span, width), FULL),
        ((rows, width), LOW),
        ((rows, hidden), LOW),
        ((rows, hidden), LOW),
    ]
    outputs = [((span, width), FULL, VMEM), ((rows, width), LOW, VMEM)]
    outputs += [(shape, dtype, HBM) for shape, dtype in saved]
    if plan.entry:
        outputs.append(((rows, width), LOW, HBM))
    outputs += [((width, columns[name]), LOW, HBM) for name in plan.ahead + plan.own]
    qkv_shape, o_shape, lse_shape, heads_shape = saved[:4]
    scratch = [VMEM((joint, rows), LOW), VMEM((rows, attn), LOW), VMEM((attn, rows), LOW)]
    scratch += [VMEM(*pair) for pair in saved[:3] + saved[4:]]
    if plan.entry:
        scratch.append(VMEM((rows, width), LOW))
    scratch += [
        VMEM((slots, PAD), LOW),
        VMEM((PAD, slots), LOW),
        VMEM((size, slots), LOW),
        VMEM((size, slots), LOW),
    ]
    scratch += round_buffers(rows, width) + round_buffers(rows, width)
    scratch += [VMEM((width, columns[name]), LOW) for name in NAMES]
    results = run(
        functools.partial(layer_kernel, plan, last, size, tile),
        "forward_layer",
        ident,
        inputs,
        outputs,
        scratch,
        2 * (count - 1) + 2 * ROUND_COPIES + 2 * count * len(plan.own + plan.ahead),
        9 + 2 * len(NAMES) + 2,
        sizes,
        48,
        2 * rows * width * (2 * hidden + attn + joint) + 4 * slots * slots * 256,
    )
    stream, following = results[:2]
    kept = results[2 : 11 if plan.entry else 10]
    for name, value in zip(plan.ahead, results[2 + len(kept) :]):
        gathered[name, plan.layer + 1] = value
    for name, value in zip(plan.own, results[2 + len(kept) + len(plan.ahead) :]):
        gathered[name, plan.layer] = value
    return stream, following, kept


def sums_into(sums, first, at, values):
    for index, value in enumerate(values):
        row = first + index
        added = jnp.sum(value, axis=0, keepdims=True)
        width = added.shape[1]
        sums[row : row + 1, 0:width] = (
            added if at.start == 0 else sums[row : row + 1, 0:width] + added
        )


def back_kernel(plan, size, tile, mover, ins, outs, work):
    ins, outs, work = iter(ins), iter(outs), iter(work)
    source = next(ins)
    x_ref = None if plan.last else next(ins)
    bias, vectors, mask = [next(ins) for _ in range(3)]
    far = [next(ins) for _ in range(14)]
    late_far = next(ins) if plan.late else None
    others = [(next(ins), next(ins)) for _ in range(plan.others)]
    stream, following = next(outs), next(outs)
    grad_outs = {name: next(outs) for name in NAMES if plan.inside and (name != "qkv" or plan.final)}
    mid_out = next(outs) if plan.inside and not plan.final else None
    late_out = next(outs) if plan.late else None
    split = local = totals = None
    if plan.joined:
        totals = next(outs)
    else:
        split, local = next(outs), next(outs)
    wholes = {} if plan.inside else {name: next(outs) for name in NAMES}
    near = [next(work) for _ in range(14)]
    slope, w_down, w_up, middle, hidden, second, w_out, heads, qkv, o_ref, lse, first, w_qkv, before = near
    grad = next(work) if plan.last else source
    pre_grad, attn_grad, parts, grads, nat = [next(work) for _ in range(5)]
    attend_work = [next(work) for _ in range(11)]
    one_work, two_work = [next(work) for _ in range(5)], [next(work) for _ in range(5)]
    rows, width = source.shape
    reduces = {}
    if plan.inside:
        pairs = {
            "down": (grad, hidden),
            "up": (second, pre_grad),
            "out": (attn_grad, heads),
            "qkv": (first, nat),
        }
        for name in ("down", "up", "out", "qkv"):
            buffers = [next(work) for _ in range(4)]
            reduces[name] = Reduce(mover, buffers, grad_outs.get(name), *pairs[name])
    late = None
    if plan.late:
        late_mid, late_line = next(work), next(work)
        late = Reduce(mover, (late_mid, None, late_mid, late_line), late_out, None, None)
    if plan.joined:
        split, local = next(work), next(work)
        got_tp, got_shard, got_ctx, mine = [next(work) for _ in range(4)]

    greet(mover, plan.inside)
    load = [mover.stay(there, here) for there, here in zip(far, near)]
    if late:
        mover.near(mover.stay(late_far, late_mid))
        late.spread()
    if plan.last:
        chunk = rows // 5 if rows % 80 == 0 else rows

        def mask_step(i, carry):
            at = pl.ds(pl.multiple_of(i * chunk, 16), chunk)
            grad[at, :] = (source[at, :].astype(FULL) * mask[at, 0:1]).astype(LOW)
            return carry

        lax.fori_loop(0, rows // chunk, mask_step, 0)
    one = Round(mover, rows, attn_grad, one_work)
    two = Round(mover, rows, following, two_work)
    gain2, gain1 = vectors[0:1, :], vectors[1:2, :]
    split[...] = jnp.zeros_like(split)
    local[...] = jnp.zeros_like(local)
    split[5:6, 0:width] = jnp.sum(
        grad[one.rows(one.own), :].astype(FULL), axis=0, keepdims=True
    )
    mover.near(*load[:3])
    hidden_width = slope.shape[1]

    def mlp_part(start):
        at = one.rows(start)
        pre = jnp.dot(grad[at, :], w_down[...], preferred_element_type=FULL)
        low = (pre * slope[at, :].astype(FULL)).astype(LOW)
        pre_grad[at, :] = low
        local[0:1, 0:hidden_width] += jnp.sum(low.astype(FULL), axis=0, keepdims=True)
        return dot(low, w_up[...], ((1,), (1,)))

    def to_attn(at, value):
        if plan.last:
            above = grad[one.rows(one.own + at.start, at.size), :].astype(FULL)
        else:
            above = x_ref[at]
        _, normed, inverse = normalize(middle[at], 1.0, 0.0)
        result = above + normalize_back(value, normed, inverse, gain2)
        stream[at] = result
        low = result.astype(LOW)
        sums_into(split, 2, at, (value * normed, value, low.astype(FULL)))
        return low

    def reduce(name):
        if name in reduces:
            reduces[name].begin()

    def fold(name):
        if name in reduces:
            reduces[name].fold()
            reduces[name].spread()

    def start_down():
        mover.near(load[3], load[4])
        reduce("down")

    one.eager(mlp_part, to_attn, start_down)
    mover.near(load[5])
    reduce("up")
    one.have()
    mover.near(load[6])
    turned_product(attn_grad, w_out, None, parts)

    def waiting():
        mover.near(load[7])
        reduce("out")

    def ready():
        mover.near(load[8], load[9], load[10])

    def between(turn):
        if turn == 0:
            fold("down")
        if turn == 2:
            fold("up")

    attend_back_part(
        size,
        tile,
        mover,
        parts,
        bias,
        qkv,
        o_ref,
        lse,
        grads,
        attend_work,
        ready,
        waiting,
        between,
    )
    nat[...] = turned(grads[...])
    local[1:2, 0 : nat.shape[1]] = jnp.sum(nat[...].astype(FULL), axis=0, keepdims=True)
    mover.near(*load[11:])

    def qkv_part(start):
        return dot(nat[two.rows(start), :], w_qkv[...], ((1,), (1,)))

    def to_following(at, value):
        if plan.final:
            row = before[two.rows(two.own + at.start, at.size), :].astype(FULL)
        else:
            row = before[at]
        _, normed, inverse = normalize(row, 1.0, 0.0)
        result = stream[at] + normalize_back(value, normed, inverse, gain1)
        stream[at] = result
        low = result.astype(LOW)
        sums_into(split, 0, at, (value * normed, value))
        return low

    def start_qkv():
        fold("out")
        reduce("qkv")

    two.eager(qkv_part, to_following, start_qkv)
    if plan.joined:
        place = lax.axis_index("tp")
        ways = got_tp.shape[0]
        top = split.shape[0]
        for index, (other_split, other_local) in enumerate(others):
            at = slice((index + 1) * top, (index + 2) * top)
            mine[0, at] = other_split[...]
            mine[1, at] = other_local[...]
        mine[0, 0:top] = split[...]
        mine[1, 0:top] = local[...]
        got_tp[place] = mine[0]
        tp_copies = [
            mover.go(mine.at[0], got_tp.at[place], tp=lax.rem(place + by, ways))
            for by in range(1, ways)
        ]
    two.have()
    if plan.inside:
        if plan.final:
            fold("qkv")
        else:
            reduces["qkv"].fold()
            mover.stay(reduces["qkv"].mid, mid_out)
    if plan.joined:
        for copy in tp_copies:
            mover.take(copy)
        value = got_tp[0]
        for other in range(1, ways):
            value = value + got_tp[other]
        mine[2] = value
        cross = mover.go(mine.at[pl.ds(1, 2)], got_shard, shard=1 - mover.shard)
        mover.take(cross)
        got_ctx[mover.ctx] = mine[1:3] + got_shard[...]
        there = got_ctx.at[mover.ctx]
        lines = [mover.go(there, there, ctx=mover.on(by)) for by in range(1, mover.ctx_count)]
        for copy in lines:
            mover.take(copy)
        value = got_ctx[0]
        for other in range(1, mover.ctx_count):
            value = value + got_ctx[other]
        totals[...] = value
    for name in ("down", "up", "out"):
        if name in reduces:
            reduces[name].done()
    if late:
        late.done()
    if plan.inside and plan.final:
        reduces["qkv"].done()
    if not plan.inside:
        for name, (lhs, rhs) in {
            "down": (grad, hidden),
            "up": (second, pre_grad),
            "out": (attn_grad, heads),
            "qkv": (first, nat),
        }.items():
            full = Reduce(mover, (wholes[name],) * 4, None, lhs, rhs)
            full.compute(wholes[name], 0)
    mover.settle()


class BackPlan:
    def __init__(self, layer, layers, inside):
        self.inside = inside
        self.last, self.final = layer == layers - 1, layer == 0
        self.late = inside and not self.last
        self.joined = inside and self.final
        self.others = layers - 1 if self.joined else 0


def back_layer(source, x, bias, vectors, mask, saved, late, others, plan, size, sizes, ident):
    rows, width = source.shape
    count = sizes[0]
    slope, w_down, w_up = saved[:3]
    hidden, joint, attn = slope.shape[1], saved[12].shape[1], saved[6].shape[1]
    slots, span = count * rows, rows // 4
    tile = 256 if slots % 256 == 0 else PAD
    wide = max(width, hidden, joint)
    half = width // 2
    block = half // count
    columns = {"qkv": joint, "out": attn, "up": hidden, "down": hidden}
    inputs = [(source, VMEM)] + ([] if plan.last else [(x, VMEM)])
    inputs += [(value, VMEM) for value in (bias, vectors, mask)]
    inputs += [(value, HBM) for value in saved]
    if plan.late:
        inputs.append((late, HBM))
    for pair in others[: plan.others]:
        inputs += [(value, VMEM) for value in pair]
    outputs = [((span, width), FULL, VMEM), ((rows, width), LOW, VMEM)]
    names = [name for name in NAMES if plan.inside and (name != "qkv" or plan.final)]
    outputs += [((block, columns[name]), FULL, VMEM) for name in names]
    if plan.inside and not plan.final:
        outputs.append(((half, joint), LOW, HBM))
    if plan.late:
        outputs.append(((block, joint), FULL, VMEM))
    depth = 8 * (plan.others + 1)
    if plan.joined:
        outputs.append(((2, depth, wide), FULL, VMEM))
    else:
        outputs += [((8, wide), FULL, VMEM)] * 2
    if not plan.inside:
        outputs += [((width, columns[name]), LOW, VMEM) for name in NAMES]
    scratch = [VMEM(value.shape, value.dtype) for value in saved]
    if plan.last:
        scratch.append(VMEM((rows, width), LOW))
    scratch += [
        VMEM((rows, hidden), LOW),
        VMEM((rows, width), LOW),
        VMEM((attn, rows), LOW),
        VMEM((joint, rows), LOW),
        VMEM((rows, joint), LOW),
    ]
    scratch += attend_back_buffers(size, count, rows)
    scratch += round_buffers(rows, width) + round_buffers(rows, width)
    if plan.inside:
        for name in ("down", "up", "out", "qkv"):
            scratch += reduce_buffers(half, columns[name], count)
    if plan.late:
        scratch += [VMEM((half, joint), LOW), VMEM((count - 1, block, joint), LOW)]
    ways = lax.axis_size("tp")
    if plan.joined:
        scratch += [VMEM((8, wide), FULL)] * 2
        scratch += [
            VMEM((ways, depth, wide), FULL),
            VMEM((2, depth, wide), FULL),
            VMEM((count, 2, depth, wide), FULL),
            VMEM((3, depth, wide), FULL),
        ]
    results = run(
        functools.partial(back_kernel, plan, size, tile),
        "back_layer",
        ident,
        inputs,
        outputs,
        scratch,
        3 * (count - 1) + 2 * ROUND_COPIES + 5 * count + ways + count,
        len(saved) + 2,
        sizes,
        58,
        6 * rows * width * (2 * hidden + attn + joint) + 10 * slots * slots * 256,
    )
    return results[:2], names, results[2:]


def shards(
    tokens,
    block_tokens,
    ln1_gain,
    ln1_bias,
    w_qkv,
    b_qv,
    w_out,
    b_out,
    ln2_gain,
    ln2_bias,
    w_up,
    b_up,
    w_down,
    b_down,
    cotangent,
):
    images, capacity, width = tokens.shape
    assert images == 1
    layers = w_qkv.shape[0]
    size = HEAD_DIM
    ctx_count = lax.axis_size("ctx")
    ctx_place = lax.axis_index("ctx")
    joint_width = w_qkv.shape[2]
    heads = joint_width // (3 * size)
    assert heads == ctx_count
    attn_width = heads * size
    hidden_width = w_up.shape[2]
    lengths = block_tokens[0]
    order = (ctx_place - jnp.arange(ctx_count, dtype=jnp.int32)) % ctx_count
    ordered = jnp.sum(
        jnp.where(
            order[:, None] == jnp.arange(ctx_count, dtype=jnp.int32)[None, :], lengths[None, :], 0
        ),
        axis=1,
    )
    usable = jnp.arange(capacity, dtype=jnp.int32)[None, :] < ordered[:, None]
    bias_row = jnp.where(usable, 0.0, NEG_LARGE).astype(LOW).reshape(1, ctx_count * capacity)
    bias = jnp.concatenate([bias_row, jnp.zeros((15, ctx_count * capacity), LOW)], axis=0)
    live = (jnp.arange(capacity, dtype=jnp.int32) < ordered[0]).astype(FULL)
    mask = jnp.broadcast_to(live[:, None], (capacity, PAD))

    weights = {"qkv": w_qkv, "out": w_out, "up": w_up, "down": w_down}
    sizes = (ctx_count, lax.axis_size("shard"))
    inside = sizes[1] == 2
    gathered = {}
    if not inside:
        for name, value in weights.items():
            for layer in range(layers):
                gathered[name, layer] = gather_weight(value[layer])[0]
    source, stream = tokens[0], None
    saved = []
    for layer in range(layers):
        pair = b_qv[layer].astype(FULL).reshape(heads, 2, size)
        joint_bias = jnp.stack(
            [pair[:, 0], jnp.zeros_like(pair[:, 0]), pair[:, 1]], axis=1
        ).reshape(1, joint_width)
        joint_bias = jnp.broadcast_to(joint_bias, (8, joint_width))
        after = min(layer + 1, layers - 1)
        vectors = jnp.stack(
            [
                b_out[layer],
                ln2_gain[layer],
                ln2_bias[layer],
                b_down[layer],
                ln1_gain[after],
                ln1_bias[after],
                ln1_gain[layer],
                ln1_bias[layer],
            ]
        ).astype(FULL)
        b_up_rows = jnp.broadcast_to(b_up[layer].astype(FULL)[None], (8, hidden_width))
        last = layer == layers - 1
        result, following, kept = forward_layer(
            source,
            stream,
            bias,
            joint_bias,
            vectors,
            b_up_rows,
            mask,
            gathered,
            weights,
            Plan(layer, last, inside),
            last,
            size,
            sizes,
            1 + layer,
        )
        before = stream if layer else source
        first = source if layer else kept[8]
        saved.append((before, first) + tuple(kept[:8]))
        source, stream = following, result
    mixed = source[None]

    done, packs = {}, {}
    source, stream, late = cotangent[0], None, None
    for layer in reversed(range(layers)):
        before, first, qkv, head_out, lse, heads_low, middle, second, hidden, slope = saved[layer]
        plan = BackPlan(layer, layers, inside)
        whole = {name: gathered[name, layer] for name in NAMES}
        near = [slope, whole["down"], whole["up"], middle, hidden, second, whole["out"]]
        near += [heads_low, qkv, head_out, lse, first, whole["qkv"], before]
        vectors = jnp.stack([ln2_gain[layer], ln1_gain[layer]] * 4).astype(FULL)
        others = [packs[key] for key in sorted(packs)]
        (stream, source), names, rest = back_layer(
            source, stream, bias, vectors, mask, near, late, others, plan, size, sizes, 1 + layers + layer
        )
        rest = iter(rest)
        for name in names:
            done[name, layer] = next(rest)
        if plan.inside and not plan.final:
            late = next(rest)
        if plan.late:
            done["qkv", layer + 1] = next(rest)
        if plan.joined:
            totals = next(rest)
        else:
            packs[layer] = (next(rest), next(rest))
        if not inside:
            for name in NAMES:
                value = next(rest)
                done[name, layer] = scatter_weight(
                    lambda start, count, value=value: rows_of(value, start, count).astype(FULL),
                    width,
                )
    token_grads = source.astype(FULL)[None]
    if not inside:
        split = total_over(("tp",), jnp.concatenate([packs[l][0] for l in range(layers)]))
        local = jnp.concatenate([packs[l][1] for l in range(layers)])
        totals = total_over(("shard", "ctx"), jnp.stack([local, split]))
    local = totals[0].reshape(layers, 8, -1)
    named = totals[1].reshape(layers, 8, -1)[:, :, :width]
    columns = local[:, 1, :joint_width].reshape(layers, heads, 3, size)
    g_qv = jnp.stack([columns[:, :, 0], columns[:, :, 2]], axis=2).reshape(layers, -1)
    stacked = [
        jnp.stack([done[name, layer] for layer in range(layers)], axis=0) for name in NAMES
    ]
    return (
        mixed,
        token_grads,
        named[:, 0],
        named[:, 1],
        stacked[0],
        g_qv,
        stacked[1],
        named[:, 4],
        named[:, 2],
        named[:, 3],
        stacked[2],
        local[:, 0, :hidden_width],
        stacked[3],
        named[:, 5],
    )


def solution(mesh):
    split_rows = P(None, ("shard", "ctx"), "tp")
    split_tokens = P("shard", "ctx", None)
    return jax.shard_map(
        shards,
        mesh=mesh,
        in_specs=(
            split_tokens,
            P("shard", None),
            P(),
            P(),
            split_rows,
            P(None, "tp"),
            split_rows,
            P(),
            P(),
            P(),
            split_rows,
            P(None, "tp"),
            split_rows,
            P(),
            split_tokens,
        ),
        out_specs=(
            split_tokens,
            split_tokens,
            P(),
            P(),
            split_rows,
            P(None, "tp"),
            split_rows,
            P(),
            P(),
            P(),
            split_rows,
            P(None, "tp"),
            split_rows,
            P(),
        ),
        check_vma=False,
    )
```

```python
import functools
import math

import jax
import jax.numpy as jnp
from jax import lax
from jax.experimental import pallas as pl
from jax.experimental.pallas import tpu as pltpu
from jax.sharding import PartitionSpec as P

HEAD_DIM = 64
EPSILON = 1e-06
NEG_LARGE = -1e30
LOW = jnp.bfloat16
FULL = jnp.float32
PAD = 128
MESH = pl.DeviceIdType.MESH
VMEM = pltpu.VMEM
HBM = pltpu.HBM


def bits_of(axis):
    size = lax.axis_size(axis)
    assert size & (size - 1) == 0
    return [1 << i for i in range(size.bit_length() - 1)]


def swap(value, axis, bit):
    size = lax.axis_size(axis)
    return lax.ppermute(value, axis, [(i, i ^ bit) for i in range(size)])


def side_of(axis, bit):
    return (lax.axis_index(axis) // bit) % 2


def rows_of(value, start, count, axis=0):
    return lax.dynamic_slice_in_dim(value, start, count, axis)


def halve(axis, bits, partial, total):
    offset, span, received = jnp.int32(0), total, []

    def summed(start, count):
        value = partial(start, count)
        for got, base in received:
            value = value + rows_of(got, start - base, count).astype(FULL)
        return value

    for bit in bits:
        half = span // 2
        side = side_of(axis, bit)
        got = swap(summed(offset + (1 - side) * half, half).astype(LOW), axis, bit)
        offset = offset + side * half
        received.append((got, offset))
        span = half
    return summed(offset, span)


def double(axis, bits, value):
    for bit in bits:
        got = swap(value, axis, bit)
        first = side_of(axis, bit) == 0
        value = jnp.concatenate(
            [jnp.where(first, value, got), jnp.where(first, got, value)], axis=0
        )
    return value


def total_over(axes, value):
    for axis in axes:
        for bit in bits_of(axis):
            value = value + swap(value, axis, bit)
    return value


def ring(value, by):
    count = lax.axis_size("ctx")
    return lax.ppermute(value, "ctx", [(i, (i + by) % count) for i in range(count)])


def gather_weight(piece):
    count = lax.axis_size("ctx")
    place = lax.axis_index("ctx")
    ways = lax.axis_size("shard")
    blocks = [piece] + [ring(piece, by) for by in range(1, count)]
    whole = jnp.zeros((ways * count,) + piece.shape, piece.dtype)
    me = lax.axis_index("shard")
    for by, block in enumerate(blocks):
        at = (place - by) % count
        held = [(jnp.int32(0), block)]
        for bit in bits_of("shard"):
            held = held + [(other ^ bit, swap(value, "shard", bit)) for other, value in held]
        for other, value in held:
            whole = lax.dynamic_update_index_in_dim(whole, value, (me ^ other) * count + at, 0)
    return whole.reshape((ways * count * piece.shape[0],) + piece.shape[1:]), blocks[-1]


def scatter_weight(partial, total):
    count = lax.axis_size("ctx")
    place = lax.axis_index("ctx")
    mine = halve("shard", bits_of("shard")[::-1], partial, total).astype(LOW)
    mine = mine.reshape((count, mine.shape[0] // count) + mine.shape[1:])
    value = lax.dynamic_index_in_dim(mine, place, 0, False).astype(FULL)
    for by in range(1, count):
        given = lax.dynamic_index_in_dim(mine, (place + by) % count, 0, False)
        value = value + ring(given, by).astype(FULL)
    return value


def dot(left, right, contract):
    return lax.dot_general(
        left, right, ((contract[0], contract[1]), ((), ())), preferred_element_type=FULL
    )


def turned(value):
    return value.astype(FULL).T.astype(LOW)


def normalize(rows, gain, shift):
    row_mean = jnp.mean(rows, axis=-1, keepdims=True)
    centred = rows - row_mean
    inverse = lax.rsqrt(jnp.mean(centred * centred, axis=-1, keepdims=True) + EPSILON)
    normed = centred * inverse
    return (normed * gain + shift, normed, inverse)


def normalize_back(grad_out, normed, inverse, gain):
    scaled = grad_out * gain
    mean_grad = jnp.mean(scaled, axis=-1, keepdims=True)
    mean_cross = jnp.mean(scaled * normed, axis=-1, keepdims=True)
    return inverse * (scaled - mean_grad - normed * mean_cross)


def gelu_pair(value):
    spread = 0.5 * (1.0 + lax.erf(value * (0.5**0.5)))
    slope = spread + value * jnp.exp(-0.5 * value * value) * (1.0 / math.sqrt(2.0 * math.pi))
    return (value * spread).astype(LOW), slope.astype(LOW)


class Mover:
    def __init__(self, sizes, send, recv, local):
        self.ctx_count, self.shard_count = sizes
        self.send, self.recv, self.local = send, recv, local
        self.copies, self.here = [], []
        self.arrived = set()
        self.landed = set()
        self.ctx = lax.axis_index("ctx")
        self.shard = lax.axis_index("shard")

    def go(self, source, target, **device):
        index = len(self.copies)
        copy = pltpu.make_async_remote_copy(
            src_ref=source,
            dst_ref=target,
            send_sem=self.send.at[index],
            recv_sem=self.recv.at[index],
            device_id=device,
            device_id_type=MESH,
        )
        copy.start()
        self.copies.append(copy)
        return index

    def stay(self, source, target):
        index = len(self.here)
        copy = pltpu.make_async_copy(source, target, self.local.at[index])
        copy.start()
        self.here.append(copy)
        return index

    def near(self, *indices):
        for index in indices:
            if index not in self.landed:
                self.landed.add(index)
                self.here[index].wait()

    def take(self, index):
        if index not in self.arrived:
            self.arrived.add(index)
            self.copies[index].wait_recv()

    def flip(self, bits):
        place = self.ctx
        if bits & 1:
            place = place + 1 - 2 * lax.rem(self.ctx, 2)
        if bits & 2:
            place = place + 2 - 4 * (self.ctx // 2)
        return place

    def on(self, by):
        return lax.rem(self.ctx + by, self.ctx_count)

    def back(self, by):
        return lax.rem(self.ctx + self.ctx_count - by, self.ctx_count)

    def settle(self):
        for index, copy in enumerate(self.copies):
            self.take(index)
            copy.wait_send()
        self.near(*range(len(self.here)))


class Gather:
    def __init__(self, mover, source, target):
        self.mover, self.source, self.target = mover, source, target
        self.over = []

    def start(self):
        mover = self.mover
        mine, there = self.source, self.block(mover.ctx)
        self.far = mover.go(mine, there, ctx=mover.flip(2))
        self.close = mover.go(mine, there, ctx=mover.flip(1))
        self.over.append(mover.go(mine, there, shard=1 - mover.shard))
        self.own = mover.stay(mine, there)

    def block(self, ctx):
        mover = self.mover
        rows = self.source.shape[0]
        start = (mover.shard * mover.ctx_count + ctx) * rows
        return self.target.at[pl.ds(pl.multiple_of(start, rows), rows)]

    def pass_on(self, stage):
        mover = self.mover
        if stage == 1:
            mover.take(self.far)
            rows = self.block(mover.flip(2))
            self.passed = mover.go(rows, rows, ctx=mover.flip(1))
        elif stage == 2:
            mover.take(self.close)
            rows = self.block(mover.flip(1))
        else:
            mover.take(self.passed)
            rows = self.block(mover.flip(3))
        self.over.append(mover.go(rows, rows, shard=1 - mover.shard))

    def have(self):
        for copy in self.over:
            self.mover.take(copy)
        self.mover.near(self.own)


class Reduce:
    def __init__(self, mover, buffers, out, lhs, rhs):
        self.mover, self.out, self.lhs, self.rhs = mover, out, lhs, rhs
        self.give, self.got, self.mid, self.line = buffers
        self.half = self.give.shape[0]
        self.block = self.half // mover.ctx_count

    def compute(self, target, shard):
        chunk = min(256, self.half)

        def step(i, carry):
            at = pl.ds(pl.multiple_of(shard * self.half + i * chunk, chunk), chunk)
            here = pl.ds(pl.multiple_of(i * chunk, chunk), chunk)
            target[here, :] = dot(self.lhs[:, at], self.rhs[...], ((0,), (0,))).astype(LOW)
            return carry

        lax.fori_loop(0, self.half // chunk, step, 0)

    def begin(self):
        mover = self.mover
        self.compute(self.give, 1 - mover.shard)
        self.cross = mover.go(self.give, self.got, shard=1 - mover.shard)
        self.compute(self.mid, mover.shard)

    def fold(self):
        self.mover.take(self.cross)
        self.mid[...] = (self.mid[...].astype(FULL) + self.got[...].astype(FULL)).astype(LOW)

    def rows(self, ctx):
        return self.mid.at[pl.ds(pl.multiple_of(ctx * self.block, self.block), self.block)]

    def spread(self):
        mover = self.mover
        self.first = mover.go(self.rows(mover.flip(3)), self.line.at[1], ctx=mover.flip(1))
        self.second = mover.go(self.rows(mover.flip(1)), self.line.at[0], ctx=mover.flip(1))

    def finish(self):
        mover = self.mover
        mover.take(self.first)
        rows = self.rows(mover.flip(2))
        rows[...] = (rows[...].astype(FULL) + self.line[1].astype(FULL)).astype(LOW)
        self.third = mover.go(rows, self.line.at[2], ctx=mover.flip(2))

    def done(self):
        self.mover.take(self.second)
        self.mover.take(self.third)
        value = self.rows(self.mover.ctx)[...].astype(FULL)
        self.out[...] = value + self.line[0].astype(FULL) + self.line[2].astype(FULL)


def reduce_buffers(half, width, count):
    return [
        VMEM((half, width), LOW),
        VMEM((half, width), LOW),
        VMEM((half, width), LOW),
        VMEM((count - 1, half // count, width), LOW),
    ]


def greet(mover, shard):
    barrier = pltpu.get_barrier_semaphore()
    peers = [dict(ctx=mover.on(by)) for by in range(1, mover.ctx_count)]
    peers += [dict(tp=peer) for peer in tp_peers()]
    if shard:
        peers.append(dict(shard=1 - mover.shard))
    for peer in peers:
        pl.semaphore_signal(barrier, inc=1, device_id=peer, device_id_type=MESH)
    pl.semaphore_wait(barrier, len(peers))


def tp_peers():
    place = lax.axis_index("tp")
    core, far = lax.rem(place, 2), place // 2
    return place + 1 - 2 * core, place + 2 - 4 * far


def run(kernel, name, ident, inputs, outputs, scratch, remote, local, sizes, vmem, flops):
    n_in, n_out, n_scratch = len(inputs), len(outputs), len(scratch)

    def body(*refs):
        ins, outs = refs[:n_in], refs[n_in : n_in + n_out]
        work = refs[n_in + n_out :]
        mover = Mover(sizes, *work[n_scratch:])
        kernel(mover, ins, outs, work[:n_scratch])

    return pl.pallas_call(
        body,
        in_specs=[pl.BlockSpec(memory_space=space) for _, space in inputs],
        out_specs=[pl.BlockSpec(memory_space=space) for _, _, space in outputs],
        out_shape=[jax.ShapeDtypeStruct(shape, dtype) for shape, dtype, _ in outputs],
        scratch_shapes=list(scratch)
        + [
            pltpu.SemaphoreType.DMA((remote,)),
            pltpu.SemaphoreType.DMA((remote,)),
            pltpu.SemaphoreType.DMA((local,)),
        ],
        compiler_params=pltpu.CompilerParams(
            collective_id=ident, has_side_effects=True, vmem_limit_bytes=vmem * 2**20
        ),
        cost_estimate=pl.CostEstimate(flops=flops, bytes_accessed=2**24, transcendentals=0),
        name=name,
    )(*[value for value, _ in inputs])


def order_of(block, count):
    return (block + count - 1) % count


def tiles_of(count, capacity, tile):
    ends = [-(-(p + 1) * capacity // tile) for p in range(count)]
    return list(zip([0] + ends[:-1], ends))


def tile_at(t, tile):
    return pl.ds(pl.multiple_of(t * tile, tile), tile)


def turned_product(left, right, bias, target):
    def step(i, carry):
        at = pl.ds(pl.multiple_of(i * PAD, PAD), PAD)
        value = jnp.dot(left[at, :], right[...], preferred_element_type=FULL)
        if bias is not None:
            value = value + bias[0:1, :]
        target[:, at] = turned(value.astype(LOW))
        return carry

    lax.fori_loop(0, left.shape[0] // PAD, step, 0)


def head_rows(ref, head, width):
    return ref.at[pl.ds(pl.multiple_of(head * width, 16), width)]


def attend_part(size, tile, mover, joint, bias, heads, qkv, o_ref, lse, work, after_send, between):
    k_ref, q_ref, v_ref, low_ref = work
    count, width, capacity = qkv.shape
    slots = count * capacity
    sent = [None] + [
        mover.go(head_rows(joint, mover.on(by), width), qkv.at[by], ctx=mover.on(by))
        for by in range(1, count)
    ]
    after_send()
    qkv[0] = head_rows(joint, mover.ctx, width)[...]
    q_ref[size:PAD, :] = jnp.concatenate(
        [jnp.ones((16, slots), LOW), jnp.zeros((PAD - size - 16, slots), LOW)], axis=0
    )

    def prepare(r):
        here = slice(r * capacity, (r + 1) * capacity)
        p = order_of(r, count)
        q_ref[0:size, p * capacity : (p + 1) * capacity] = (
            qkv[r, 0:size, :] * (size**-0.5)
        ).astype(LOW)
        v_ref[:, here] = qkv[r, 2 * size : 3 * size, :]
        keys = jnp.concatenate(
            [qkv[r, size : 2 * size, :], bias[:, here], jnp.zeros((PAD - size - 16, capacity), LOW)],
            axis=0,
        )
        k_ref[here, :] = turned(keys)

    prepare(0)
    for by in range(1, count):
        mover.take(sent[by])
        prepare(by)

    def step(t, carry):
        at = tile_at(t, tile)
        scores = jnp.dot(k_ref[...], q_ref[:, at], preferred_element_type=FULL)
        top = jnp.max(scores, axis=0, keepdims=True)
        weights = jnp.exp(scores - top)
        total = jnp.sum(weights, axis=0, keepdims=True)
        summed = jnp.dot(v_ref[...], weights.astype(LOW), preferred_element_type=FULL)
        out = summed / total
        o_ref[:, at] = out
        low_ref[:, at] = out.astype(LOW)
        lse[:, at] = jnp.broadcast_to(top + jnp.log(total), (8, tile))
        return carry

    arriving = []
    for p, (low, high) in enumerate(tiles_of(count, capacity, tile)):
        lax.fori_loop(low, high, step, 0)
        done = low_ref.at[:, p * capacity : (p + 1) * capacity]
        if p < count - 1:
            there = head_rows(heads, mover.ctx, size)
            arriving.append(mover.go(done, there, ctx=mover.back(p + 1)))
        else:
            head_rows(heads, mover.ctx, size)[...] = low_ref[:, p * capacity : (p + 1) * capacity]
        between(p + 1)
    for copy in arriving:
        mover.take(copy)


def attend_back_part(size, tile, mover, parts, bias, qkv, o_ref, lse, grads, work, ready, waiting, begun, between):
    k_ref, v_ref, q_ref, do_ref, nat_ref, delta_ref, dq_ref, dk_ref, dv_ref, got, back = work
    count, width, capacity = qkv.shape
    slots = count * capacity
    sent = [None] + [
        mover.go(head_rows(parts, mover.on(by), size), got.at[by], ctx=mover.on(by))
        for by in range(1, count)
    ]
    got[0] = head_rows(parts, mover.ctx, size)[...]
    waiting()
    ready()
    q_ref[size:PAD, :] = jnp.concatenate(
        [jnp.ones((16, slots), LOW), jnp.zeros((PAD - size - 16, slots), LOW)], axis=0
    )
    do_ref[size:PAD, :] = jnp.zeros((PAD - size, slots), LOW)
    dq_ref[...] = jnp.zeros_like(dq_ref)
    for r in range(count):
        here = slice(r * capacity, (r + 1) * capacity)
        pad = jnp.zeros((PAD - size - 16, capacity), LOW)
        k_ref[here, :] = turned(
            jnp.concatenate([qkv[r, size : 2 * size, :], bias[:, here], pad], axis=0)
        )
        v_ref[here, :] = turned(
            jnp.concatenate(
                [qkv[r, 2 * size : 3 * size, :], jnp.zeros((PAD - size, capacity), LOW)], axis=0
            )
        )
    for r in range(count):
        if r:
            mover.take(sent[r])
        p = order_of(r, count)
        at = slice(p * capacity, (p + 1) * capacity)
        scaled = (qkv[r, 0:size, :] * (size**-0.5)).astype(LOW)
        dout = got[r]
        q_ref[0:size, at] = scaled
        do_ref[0:size, at] = dout
        nat_ref[at, :] = turned(jnp.concatenate([scaled, dout], axis=0))
        delta = jnp.sum(dout.astype(FULL) * o_ref[:, at], axis=0, keepdims=True)
        delta_ref[:, at] = jnp.broadcast_to(delta, (8, capacity))

    begun()
    tiles = tiles_of(count, capacity, tile)
    arriving = []
    mine = head_rows(grads, mover.ctx, width)
    for turn, r in enumerate(list(range(1, count)) + [0]):
        here = slice(r * capacity, (r + 1) * capacity)
        dk_ref[...] = jnp.zeros_like(dk_ref)
        dv_ref[...] = jnp.zeros_like(dv_ref)

        def step(t, carry, r=r, here=here):
            at = tile_at(t, tile)
            scores = jnp.dot(k_ref[here, :], q_ref[:, at], preferred_element_type=FULL)
            chance = jnp.exp(scores - lse[0:1, at])
            chance_grad = jnp.dot(v_ref[here, :], do_ref[:, at], preferred_element_type=FULL)
            score_grad = (chance * (chance_grad - delta_ref[0:1, at])).astype(LOW)
            dq_ref[:, at] += jnp.dot(
                qkv[r, size : 2 * size, :], score_grad, preferred_element_type=FULL
            )
            dk_ref[...] += jnp.dot(score_grad, nat_ref[at, :], preferred_element_type=FULL)
            dv_ref[...] += jnp.dot(
                chance.astype(LOW), nat_ref[at, :], preferred_element_type=FULL
            )
            return carry

        if r:
            lax.fori_loop(0, tiles[-1][1], step, 0)
        else:
            for p, (low, high) in enumerate(tiles):
                lax.fori_loop(low, high, step, 0)
                at = slice(p * capacity, (p + 1) * capacity)
                value = (dq_ref[:, at] * (size**-0.5)).astype(LOW)
                if p < count - 1:
                    back[p + 1, 0:size, :] = value
                    arriving.append(
                        mover.go(
                            back.at[p + 1, 0:size], mine.at[0:size], ctx=mover.back(p + 1)
                        )
                    )
                else:
                    mine[0:size, :] = value
        keys = dk_ref[...].T[0:size].astype(LOW)
        values = dv_ref[...].T[size : 2 * size].astype(LOW)
        if r:
            back[r, size : 2 * size, :] = keys
            back[r, 2 * size : 3 * size, :] = values
            arriving.append(
                mover.go(
                    back.at[r, size : 3 * size], mine.at[size : 3 * size], ctx=mover.back(r)
                )
            )
        else:
            mine[size : 2 * size, :] = keys
            mine[2 * size : 3 * size, :] = values
        between(turn)
    for copy in arriving:
        mover.take(copy)


def attend_back_buffers(size, count, capacity):
    slots = count * capacity
    return [
        VMEM((slots, PAD), LOW),
        VMEM((slots, PAD), LOW),
        VMEM((PAD, slots), LOW),
        VMEM((PAD, slots), LOW),
        VMEM((slots, PAD), LOW),
        VMEM((8, slots), FULL),
        VMEM((size, slots), FULL),
        VMEM((capacity, PAD), FULL),
        VMEM((capacity, PAD), FULL),
        VMEM((count, size, capacity), LOW),
        VMEM((count, 3 * size, capacity), LOW),
    ]


class Round:
    def __init__(self, mover, rows, full, buffers):
        place = lax.axis_index("tp")
        core, far = lax.rem(place, 2), place // 2
        self.mover, self.full = mover, full
        self.give, self.ra, self.passing, self.rb, self.keep = buffers
        self.span = rows // 4
        self.half = self.span // 2
        self.mate, self.far = tp_peers()

        def quarter(c, f):
            return (c * 2 + f) * self.span

        self.own, self.other = quarter(core, far), quarter(core, 1 - far)
        self.mate_own, self.mate_other = quarter(1 - core, far), quarter(1 - core, 1 - far)

    def rows(self, start, count=None):
        return pl.ds(pl.multiple_of(start, 16), count or self.span)

    def hand(self, slot, value):
        self.give[slot] = value.astype(LOW)
        return self.mover.go(self.give.at[slot], self.ra.at[slot], tp=self.mate)

    def onward(self, value, index):
        self.mover.take(index)
        self.passing[...] = (value + self.ra[1].astype(FULL)).astype(LOW)
        return [
            self.mover.go(self.passing.at[at], self.rb.at[at], tp=self.far)
            for at in (pl.ds(0, self.half), pl.ds(self.half, self.half))
        ]

    def close(self, far_copies, index, finish):
        self.mover.take(index)
        self.keep[...] += self.ra[0].astype(FULL)
        self.to_far, self.to_mate = [], []
        for c in range(2):
            at = pl.ds(c * self.half, self.half)
            self.mover.take(far_copies[c])
            low = finish(at, self.keep[at] + self.rb[at].astype(FULL))
            mine = self.full.at[self.rows(self.own + c * self.half, self.half)]
            mine[...] = low
            self.to_far.append(self.mover.go(mine, mine, tp=self.far))
            self.to_mate.append(self.mover.go(mine, mine, tp=self.mate))

    def eager(self, make, finish, meanwhile=None):
        first = self.hand(1, make(self.mate_other))
        copies = self.onward(make(self.other), first)
        second = self.hand(0, make(self.mate_own))
        self.keep[...] = make(self.own)
        if meanwhile:
            meanwhile()
        self.close(copies, second, finish)

    def after(self, before, make, finish, meanwhile=None):
        before.have_mate_own()
        second = self.hand(0, make(self.mate_own))
        self.keep[...] = make(self.own)
        before.have_other()
        value = make(self.other)
        before.have_mate_other()
        first = self.hand(1, make(self.mate_other))
        copies = self.onward(value, first)
        if meanwhile:
            meanwhile()
        self.close(copies, second, finish)

    def have_mate_own(self):
        for copy in self.to_mate:
            self.mover.take(copy)

    def have_other(self):
        self.passed = []
        for c in range(2):
            self.mover.take(self.to_far[c])
            rows = self.full.at[self.rows(self.other + c * self.half, self.half)]
            self.passed.append(self.mover.go(rows, rows, tp=self.mate))

    def have_mate_other(self):
        for copy in self.passed:
            self.mover.take(copy)

    def have(self):
        self.have_mate_own()
        self.have_other()
        self.have_mate_other()


ROUND_COPIES = 10


def round_buffers(rows, width):
    span = rows // 4
    return [
        VMEM((2, span, width), LOW),
        VMEM((2, span, width), LOW),
        VMEM((span, width), LOW),
        VMEM((span, width), LOW),
        VMEM((span, width), FULL),
    ]


NAMES = ("qkv", "out", "up", "down")


def layer_kernel(plan, last, size, tile, mover, ins, outs, work):
    ins, outs, work = iter(ins), iter(outs), iter(work)
    source = next(ins)
    x_ref = None if plan.entry else next(ins)
    bias, qkv_bias, vectors, b_up, mask = [next(ins) for _ in range(5)]
    stream, following = next(outs), next(outs)
    far_qkv, far_o, far_lse, far_heads, far_middle, far_second, far_hidden, far_slope = [
        next(outs) for _ in range(8)
    ]
    far_first = next(outs) if plan.entry else None
    joint, nat, heads, qkv, o_ref, lse, middle, second, hidden, slope = [
        next(work) for _ in range(10)
    ]
    first = next(work) if plan.entry else source
    attend_work = [next(work) for _ in range(4)]
    one_work, two_work = [next(work) for _ in range(5)], [next(work) for _ in range(5)]
    rows = source.shape[0]
    whole = {name: next(work) for name in NAMES}
    gathers, loads = {}, {}
    for name in plan.held:
        loads[name] = (next(ins), whole[name])
    for name in plan.own:
        gathers[name, 0] = Gather(mover, next(ins).at[plan.layer], whole[name])
    for name in plan.ahead:
        gathers[name, 1] = Gather(mover, next(ins).at[plan.layer + 1], next(outs))
    kept = {name: next(outs) for name in plan.own}

    greet(mover, bool(gathers))
    loads = {name: mover.stay(*pair) for name, pair in loads.items()}

    def have(name):
        if name in loads:
            mover.near(loads[name])
        else:
            gathers[name, 0].have()
            mover.stay(whole[name], kept[name])
        return whole[name]

    def begin(keys):
        for key in keys:
            if key in gathers:
                gathers[key].start()

    def pass_on(keys, stage):
        for key in keys:
            if key in gathers:
                gathers[key].pass_on(stage)

    def pass_all(keys):
        for stage in (1, 2, 3):
            pass_on(keys, stage)

    b_out, gain2, shift2, b_down, gain1, shift1, gain0, shift0 = [
        vectors[i : i + 1, :] for i in range(8)
    ]
    one = Round(mover, rows, second, one_work)
    two = Round(mover, rows, following, two_work)
    if plan.entry:
        begin([("qkv", 0)])
        chunk = rows // 5 if rows % 80 == 0 else rows

        def norm_step(i, carry):
            at = pl.ds(pl.multiple_of(i * chunk, 16), chunk)
            value = normalize(source[at, :].astype(FULL), gain0, shift0)[0]
            first[at, :] = value.astype(LOW)
            return carry

        lax.fori_loop(0, rows // chunk, norm_step, 0)
        mover.stay(first, far_first)
        pass_all([("qkv", 0)])
        begin([("out", 0), ("up", 0)])
        turned_product(first, have("qkv"), qkv_bias, joint)
    else:
        turned_product(first, have("qkv"), qkv_bias, joint)

    def after_send():
        if plan.entry:
            pass_all([("out", 0), ("up", 0)])
        else:
            begin([("out", 0), ("down", 0)])

    def between(p):
        if plan.entry and p == 1:
            begin([("down", 0)])
        if not plan.entry and p > 1:
            pass_on([("out", 0), ("down", 0)], p - 1)

    attend_part(
        size, tile, mover, joint, bias, heads, qkv, o_ref, lse, attend_work, after_send, between
    )
    nat[...] = turned(heads[...])
    mover.stay(qkv, far_qkv)
    mover.stay(o_ref, far_o)
    mover.stay(lse, far_lse)
    mover.stay(nat, far_heads)
    w_out = have("out")

    def out_part(start):
        return dot(nat[one.rows(start), :], w_out[...], ((1,), (1,)))

    def to_second(at, value):
        if plan.entry:
            before = source[one.rows(one.own + at.start, at.size), :].astype(FULL)
        else:
            before = x_ref[at]
        value = before + value + b_out
        middle[at] = value
        return normalize(value, gain2, shift2)[0].astype(LOW)

    if plan.entry:
        one.eager(out_part, to_second, lambda: pass_all([("down", 0)]))
    else:
        one.eager(out_part, to_second)
    begin([("qkv", 1), ("up", 1)])
    w_up, w_down = have("up"), have("down")

    def mlp_part(start):
        at = two.rows(start)
        pre = jnp.dot(second[at, :], w_up[...], preferred_element_type=FULL) + b_up[0:1, :]
        low, low_slope = gelu_pair(pre)
        hidden[at, :] = low
        slope[at, :] = low_slope
        return dot(low, w_down[...], ((1,), (1,)))

    def to_following(at, value):
        value = middle[at] + value + b_down
        stream[at] = value
        if last:
            live = mask[two.rows(two.own + at.start, at.size), 0:1]
            return (value * live).astype(LOW)
        return normalize(value, gain1, shift1)[0].astype(LOW)

    def meanwhile():
        mover.stay(middle, far_middle)
        mover.stay(second, far_second)
        mover.stay(hidden, far_hidden)
        mover.stay(slope, far_slope)
        pass_all([("qkv", 1), ("up", 1)])

    two.after(one, mlp_part, to_following, meanwhile)
    two.have()
    mover.settle()


class Plan:
    def __init__(self, layer, last, inside):
        self.layer, self.entry = layer, layer == 0
        self.own = (NAMES if layer == 0 else ("out", "down")) if inside else ()
        self.ahead = ("qkv", "up") if inside and not last else ()
        self.held = tuple(name for name in NAMES if name not in self.own)


def forward_layer(source, x, bias, qkv_bias, vectors, b_up, mask, gathered, weights, plan, last, size, sizes, ident):
    rows, width = source.shape
    count = sizes[0]
    joint, hidden = qkv_bias.shape[1], b_up.shape[1]
    heads = joint // (3 * size)
    attn, slots, span = heads * size, count * rows, rows // 4
    tile = 256 if slots % 256 == 0 else PAD
    columns = {"qkv": joint, "out": attn, "up": hidden, "down": hidden}
    inputs = [(source, VMEM)] + ([] if plan.entry else [(x, VMEM)])
    inputs += [(value, VMEM) for value in (bias, qkv_bias, vectors, b_up, mask)]
    inputs += [(gathered[name, plan.layer], HBM) for name in plan.held]
    inputs += [(weights[name], HBM) for name in plan.own + plan.ahead]
    saved = [
        ((count, 3 * size, rows), LOW),
        ((size, slots), FULL),
        ((8, slots), FULL),
        ((rows, attn), LOW),
        ((span, width), FULL),
        ((rows, width), LOW),
        ((rows, hidden), LOW),
        ((rows, hidden), LOW),
    ]
    outputs = [((span, width), FULL, VMEM), ((rows, width), LOW, VMEM)]
    outputs += [(shape, dtype, HBM) for shape, dtype in saved]
    if plan.entry:
        outputs.append(((rows, width), LOW, HBM))
    outputs += [((width, columns[name]), LOW, HBM) for name in plan.ahead + plan.own]
    qkv_shape, o_shape, lse_shape, heads_shape = saved[:4]
    scratch = [VMEM((joint, rows), LOW), VMEM((rows, attn), LOW), VMEM((attn, rows), LOW)]
    scratch += [VMEM(*pair) for pair in saved[:3] + saved[4:]]
    if plan.entry:
        scratch.append(VMEM((rows, width), LOW))
    scratch += [
        VMEM((slots, PAD), LOW),
        VMEM((PAD, slots), LOW),
        VMEM((size, slots), LOW),
        VMEM((size, slots), LOW),
    ]
    scratch += round_buffers(rows, width) + round_buffers(rows, width)
    scratch += [VMEM((width, columns[name]), LOW) for name in NAMES]
    results = run(
        functools.partial(layer_kernel, plan, last, size, tile),
        "forward_layer",
        ident,
        inputs,
        outputs,
        scratch,
        2 * (count - 1) + 2 * ROUND_COPIES + 2 * count * len(plan.own + plan.ahead),
        9 + 2 * len(NAMES) + 2,
        sizes,
        48,
        2 * rows * width * (2 * hidden + attn + joint) + 4 * slots * slots * 256,
    )
    stream, following = results[:2]
    kept = results[2 : 11 if plan.entry else 10]
    for name, value in zip(plan.ahead, results[2 + len(kept) :]):
        gathered[name, plan.layer + 1] = value
    for name, value in zip(plan.own, results[2 + len(kept) + len(plan.ahead) :]):
        gathered[name, plan.layer] = value
    return stream, following, kept


def sums_into(sums, first, at, values):
    for index, value in enumerate(values):
        row = first + index
        added = jnp.sum(value, axis=0, keepdims=True)
        width = added.shape[1]
        sums[row : row + 1, 0:width] = (
            added if at.start == 0 else sums[row : row + 1, 0:width] + added
        )


def back_kernel(plan, size, tile, mover, ins, outs, work):
    ins, outs, work = iter(ins), iter(outs), iter(work)
    source = next(ins)
    x_ref = None if plan.last else next(ins)
    bias, vectors, mask = [next(ins) for _ in range(3)]
    far = [next(ins) for _ in range(14)]
    late_far = next(ins) if plan.late else None
    others = [(next(ins), next(ins)) for _ in range(plan.others)]
    stream, following = next(outs), next(outs)
    grad_outs = {name: next(outs) for name in NAMES if plan.inside and (name != "qkv" or plan.final)}
    mid_out = next(outs) if plan.inside and not plan.final else None
    late_out = next(outs) if plan.late else None
    split = local = totals = None
    if plan.joined:
        totals = next(outs)
    else:
        split, local = next(outs), next(outs)
    wholes = {} if plan.inside else {name: next(outs) for name in NAMES}
    near = [next(work) for _ in range(14)]
    slope, w_down, w_up, middle, hidden, second, w_out, heads, qkv, o_ref, lse, first, w_qkv, before = near
    grad = next(work) if plan.last else source
    pre_grad, attn_grad, parts, grads, nat = [next(work) for _ in range(5)]
    attend_work = [next(work) for _ in range(11)]
    one_work, two_work = [next(work) for _ in range(5)], [next(work) for _ in range(5)]
    rows, width = source.shape
    reduces = {}
    if plan.inside:
        pairs = {
            "down": (grad, hidden),
            "up": (second, pre_grad),
            "out": (attn_grad, heads),
            "qkv": (first, nat),
        }
        for name in ("down", "up", "out", "qkv"):
            buffers = [next(work) for _ in range(4)]
            reduces[name] = Reduce(mover, buffers, grad_outs.get(name), *pairs[name])
    late = None
    if plan.late:
        late_mid, late_line = next(work), next(work)
        late = Reduce(mover, (late_mid, None, late_mid, late_line), late_out, None, None)
    if plan.joined:
        split, local = next(work), next(work)
        got_tp, got_shard, got_ctx, mine = [next(work) for _ in range(4)]

    greet(mover, plan.inside)
    load = [mover.stay(there, here) for there, here in zip(far, near)]
    if late:
        mover.near(mover.stay(late_far, late_mid))
        late.spread()
    if plan.last:
        chunk = rows // 5 if rows % 80 == 0 else rows

        def mask_step(i, carry):
            at = pl.ds(pl.multiple_of(i * chunk, 16), chunk)
            grad[at, :] = (source[at, :].astype(FULL) * mask[at, 0:1]).astype(LOW)
            return carry

        lax.fori_loop(0, rows // chunk, mask_step, 0)
    one = Round(mover, rows, attn_grad, one_work)
    two = Round(mover, rows, following, two_work)
    gain2, gain1 = vectors[0:1, :], vectors[1:2, :]
    split[...] = jnp.zeros_like(split)
    local[...] = jnp.zeros_like(local)
    split[5:6, 0:width] = jnp.sum(
        grad[one.rows(one.own), :].astype(FULL), axis=0, keepdims=True
    )
    mover.near(*load[:3])
    hidden_width = slope.shape[1]

    def mlp_part(start):
        at = one.rows(start)
        pre = jnp.dot(grad[at, :], w_down[...], preferred_element_type=FULL)
        low = (pre * slope[at, :].astype(FULL)).astype(LOW)
        pre_grad[at, :] = low
        local[0:1, 0:hidden_width] += jnp.sum(low.astype(FULL), axis=0, keepdims=True)
        return dot(low, w_up[...], ((1,), (1,)))

    def to_attn(at, value):
        if plan.last:
            above = grad[one.rows(one.own + at.start, at.size), :].astype(FULL)
        else:
            above = x_ref[at]
        _, normed, inverse = normalize(middle[at], 1.0, 0.0)
        result = above + normalize_back(value, normed, inverse, gain2)
        stream[at] = result
        low = result.astype(LOW)
        sums_into(split, 2, at, (value * normed, value, low.astype(FULL)))
        return low

    def reduce(name):
        if name in reduces:
            reduces[name].begin()

    def fold(name):
        if name in reduces:
            reduces[name].fold()
            reduces[name].spread()

    def finish(name):
        if name in reduces:
            reduces[name].finish()

    def start_down():
        mover.near(load[3], load[4])
        reduce("down")

    one.eager(mlp_part, to_attn, start_down)
    mover.near(load[5])
    reduce("up")
    one.have()
    mover.near(load[6])
    turned_product(attn_grad, w_out, None, parts)

    def waiting():
        mover.near(load[7])
        reduce("out")

    def ready():
        mover.near(load[8], load[9], load[10])
        if late:
            late.finish()

    def between(turn):
        if turn == 0:
            finish("down")

    attend_back_part(
        size,
        tile,
        mover,
        parts,
        bias,
        qkv,
        o_ref,
        lse,
        grads,
        attend_work,
        ready,
        waiting,
        lambda: fold("down"),
        between,
    )
    nat[...] = turned(grads[...])
    local[1:2, 0 : nat.shape[1]] = jnp.sum(nat[...].astype(FULL), axis=0, keepdims=True)
    mover.near(*load[11:])

    def qkv_part(start):
        return dot(nat[two.rows(start), :], w_qkv[...], ((1,), (1,)))

    def to_following(at, value):
        if plan.final:
            row = before[two.rows(two.own + at.start, at.size), :].astype(FULL)
        else:
            row = before[at]
        _, normed, inverse = normalize(row, 1.0, 0.0)
        result = stream[at] + normalize_back(value, normed, inverse, gain1)
        stream[at] = result
        low = result.astype(LOW)
        sums_into(split, 0, at, (value * normed, value))
        return low

    def start_qkv():
        fold("up")
        fold("out")
        reduce("qkv")

    two.eager(qkv_part, to_following, start_qkv)
    finish("up")
    finish("out")
    if plan.joined:
        place = lax.axis_index("tp")
        ways = got_tp.shape[0]
        top = split.shape[0]
        for index, (other_split, other_local) in enumerate(others):
            at = slice((index + 1) * top, (index + 2) * top)
            mine[0, at] = other_split[...]
            mine[1, at] = other_local[...]
        mine[0, 0:top] = split[...]
        mine[1, 0:top] = local[...]
        got_tp[place] = mine[0]
        tp_copies = [
            mover.go(mine.at[0], got_tp.at[place], tp=lax.rem(place + by, ways))
            for by in range(1, ways)
        ]
    if plan.final:
        fold("qkv")
    two.have()
    if plan.final:
        finish("qkv")
    if plan.inside:
        if not plan.final:
            reduces["qkv"].fold()
            mover.stay(reduces["qkv"].mid, mid_out)
    if plan.joined:
        for copy in tp_copies:
            mover.take(copy)
        value = got_tp[0]
        for other in range(1, ways):
            value = value + got_tp[other]
        mine[2] = value
        cross = mover.go(mine.at[pl.ds(1, 2)], got_shard, shard=1 - mover.shard)
        mover.take(cross)
        got_ctx[mover.ctx] = mine[1:3] + got_shard[...]
        there = got_ctx.at[mover.ctx]
        lines = [mover.go(there, there, ctx=mover.on(by)) for by in range(1, mover.ctx_count)]
        for copy in lines:
            mover.take(copy)
        value = got_ctx[0]
        for other in range(1, mover.ctx_count):
            value = value + got_ctx[other]
        totals[...] = value
    for name in ("down", "up", "out"):
        if name in reduces:
            reduces[name].done()
    if late:
        late.done()
    if plan.inside and plan.final:
        reduces["qkv"].done()
    if not plan.inside:
        for name, (lhs, rhs) in {
            "down": (grad, hidden),
            "up": (second, pre_grad),
            "out": (attn_grad, heads),
            "qkv": (first, nat),
        }.items():
            full = Reduce(mover, (wholes[name],) * 4, None, lhs, rhs)
            full.compute(wholes[name], 0)
    mover.settle()


class BackPlan:
    def __init__(self, layer, layers, inside):
        self.inside = inside
        self.last, self.final = layer == layers - 1, layer == 0
        self.late = inside and not self.last
        self.joined = inside and self.final
        self.others = layers - 1 if self.joined else 0


def back_layer(source, x, bias, vectors, mask, saved, late, others, plan, size, sizes, ident):
    rows, width = source.shape
    count = sizes[0]
    slope, w_down, w_up = saved[:3]
    hidden, joint, attn = slope.shape[1], saved[12].shape[1], saved[6].shape[1]
    slots, span = count * rows, rows // 4
    tile = 256 if slots % 256 == 0 else PAD
    wide = max(width, hidden, joint)
    half = width // 2
    block = half // count
    columns = {"qkv": joint, "out": attn, "up": hidden, "down": hidden}
    inputs = [(source, VMEM)] + ([] if plan.last else [(x, VMEM)])
    inputs += [(value, VMEM) for value in (bias, vectors, mask)]
    inputs += [(value, HBM) for value in saved]
    if plan.late:
        inputs.append((late, HBM))
    for pair in others[: plan.others]:
        inputs += [(value, VMEM) for value in pair]
    outputs = [((span, width), FULL, VMEM), ((rows, width), LOW, VMEM)]
    names = [name for name in NAMES if plan.inside and (name != "qkv" or plan.final)]
    outputs += [((block, columns[name]), FULL, VMEM) for name in names]
    if plan.inside and not plan.final:
        outputs.append(((half, joint), LOW, HBM))
    if plan.late:
        outputs.append(((block, joint), FULL, VMEM))
    depth = 8 * (plan.others + 1)
    if plan.joined:
        outputs.append(((2, depth, wide), FULL, VMEM))
    else:
        outputs += [((8, wide), FULL, VMEM)] * 2
    if not plan.inside:
        outputs += [((width, columns[name]), LOW, VMEM) for name in NAMES]
    scratch = [VMEM(value.shape, value.dtype) for value in saved]
    if plan.last:
        scratch.append(VMEM((rows, width), LOW))
    scratch += [
        VMEM((rows, hidden), LOW),
        VMEM((rows, width), LOW),
        VMEM((attn, rows), LOW),
        VMEM((joint, rows), LOW),
        VMEM((rows, joint), LOW),
    ]
    scratch += attend_back_buffers(size, count, rows)
    scratch += round_buffers(rows, width) + round_buffers(rows, width)
    if plan.inside:
        for name in ("down", "up", "out", "qkv"):
            scratch += reduce_buffers(half, columns[name], count)
    if plan.late:
        scratch += [VMEM((half, joint), LOW), VMEM((count - 1, block, joint), LOW)]
    ways = lax.axis_size("tp")
    if plan.joined:
        scratch += [VMEM((8, wide), FULL)] * 2
        scratch += [
            VMEM((ways, depth, wide), FULL),
            VMEM((2, depth, wide), FULL),
            VMEM((count, 2, depth, wide), FULL),
            VMEM((3, depth, wide), FULL),
        ]
    results = run(
        functools.partial(back_kernel, plan, size, tile),
        "back_layer",
        ident,
        inputs,
        outputs,
        scratch,
        3 * (count - 1) + 2 * ROUND_COPIES + 5 * count + ways + count,
        len(saved) + 2,
        sizes,
        58,
        6 * rows * width * (2 * hidden + attn + joint) + 10 * slots * slots * 256,
    )
    return results[:2], names, results[2:]


def shards(
    tokens,
    block_tokens,
    ln1_gain,
    ln1_bias,
    w_qkv,
    b_qv,
    w_out,
    b_out,
    ln2_gain,
    ln2_bias,
    w_up,
    b_up,
    w_down,
    b_down,
    cotangent,
):
    images, capacity, width = tokens.shape
    assert images == 1
    layers = w_qkv.shape[0]
    size = HEAD_DIM
    ctx_count = lax.axis_size("ctx")
    ctx_place = lax.axis_index("ctx")
    joint_width = w_qkv.shape[2]
    heads = joint_width // (3 * size)
    assert heads == ctx_count
    attn_width = heads * size
    hidden_width = w_up.shape[2]
    lengths = block_tokens[0]
    order = (ctx_place - jnp.arange(ctx_count, dtype=jnp.int32)) % ctx_count
    ordered = jnp.sum(
        jnp.where(
            order[:, None] == jnp.arange(ctx_count, dtype=jnp.int32)[None, :], lengths[None, :], 0
        ),
        axis=1,
    )
    usable = jnp.arange(capacity, dtype=jnp.int32)[None, :] < ordered[:, None]
    bias_row = jnp.where(usable, 0.0, NEG_LARGE).astype(LOW).reshape(1, ctx_count * capacity)
    bias = jnp.concatenate([bias_row, jnp.zeros((15, ctx_count * capacity), LOW)], axis=0)
    live = (jnp.arange(capacity, dtype=jnp.int32) < ordered[0]).astype(FULL)
    mask = jnp.broadcast_to(live[:, None], (capacity, PAD))

    weights = {"qkv": w_qkv, "out": w_out, "up": w_up, "down": w_down}
    sizes = (ctx_count, lax.axis_size("shard"))
    inside = sizes == (4, 2)
    gathered = {}
    if not inside:
        for name, value in weights.items():
            for layer in range(layers):
                gathered[name, layer] = gather_weight(value[layer])[0]
    source, stream = tokens[0], None
    saved = []
    for layer in range(layers):
        pair = b_qv[layer].astype(FULL).reshape(heads, 2, size)
        joint_bias = jnp.stack(
            [pair[:, 0], jnp.zeros_like(pair[:, 0]), pair[:, 1]], axis=1
        ).reshape(1, joint_width)
        joint_bias = jnp.broadcast_to(joint_bias, (8, joint_width))
        after = min(layer + 1, layers - 1)
        vectors = jnp.stack(
            [
                b_out[layer],
                ln2_gain[layer],
                ln2_bias[layer],
                b_down[layer],
                ln1_gain[after],
                ln1_bias[after],
                ln1_gain[layer],
                ln1_bias[layer],
            ]
        ).astype(FULL)
        b_up_rows = jnp.broadcast_to(b_up[layer].astype(FULL)[None], (8, hidden_width))
        last = layer == layers - 1
        result, following, kept = forward_layer(
            source,
            stream,
            bias,
            joint_bias,
            vectors,
            b_up_rows,
            mask,
            gathered,
            weights,
            Plan(layer, last, inside),
            last,
            size,
            sizes,
            1 + layer,
        )
        before = stream if layer else source
        first = source if layer else kept[8]
        saved.append((before, first) + tuple(kept[:8]))
        source, stream = following, result
    mixed = source[None]

    done, packs = {}, {}
    source, stream, late = cotangent[0], None, None
    for layer in reversed(range(layers)):
        before, first, qkv, head_out, lse, heads_low, middle, second, hidden, slope = saved[layer]
        plan = BackPlan(layer, layers, inside)
        whole = {name: gathered[name, layer] for name in NAMES}
        near = [slope, whole["down"], whole["up"], middle, hidden, second, whole["out"]]
        near += [heads_low, qkv, head_out, lse, first, whole["qkv"], before]
        vectors = jnp.stack([ln2_gain[layer], ln1_gain[layer]] * 4).astype(FULL)
        others = [packs[key] for key in sorted(packs)]
        (stream, source), names, rest = back_layer(
            source, stream, bias, vectors, mask, near, late, others, plan, size, sizes, 1 + layers + layer
        )
        rest = iter(rest)
        for name in names:
            done[name, layer] = next(rest)
        if plan.inside and not plan.final:
            late = next(rest)
        if plan.late:
            done["qkv", layer + 1] = next(rest)
        if plan.joined:
            totals = next(rest)
        else:
            packs[layer] = (next(rest), next(rest))
        if not inside:
            for name in NAMES:
                value = next(rest)
                done[name, layer] = scatter_weight(
                    lambda start, count, value=value: rows_of(value, start, count).astype(FULL),
                    width,
                )
    token_grads = source.astype(FULL)[None]
    if not inside:
        split = total_over(("tp",), jnp.concatenate([packs[l][0] for l in range(layers)]))
        local = jnp.concatenate([packs[l][1] for l in range(layers)])
        totals = total_over(("shard", "ctx"), jnp.stack([local, split]))
    local = totals[0].reshape(layers, 8, -1)
    named = totals[1].reshape(layers, 8, -1)[:, :, :width]
    columns = local[:, 1, :joint_width].reshape(layers, heads, 3, size)
    g_qv = jnp.stack([columns[:, :, 0], columns[:, :, 2]], axis=2).reshape(layers, -1)
    stacked = [
        jnp.stack([done[name, layer] for layer in range(layers)], axis=0) for name in NAMES
    ]
    return (
        mixed,
        token_grads,
        named[:, 0],
        named[:, 1],
        stacked[0],
        g_qv,
        stacked[1],
        named[:, 4],
        named[:, 2],
        named[:, 3],
        stacked[2],
        local[:, 0, :hidden_width],
        stacked[3],
        named[:, 5],
    )


def solution(mesh):
    split_rows = P(None, ("shard", "ctx"), "tp")
    split_tokens = P("shard", "ctx", None)
    return jax.shard_map(
        shards,
        mesh=mesh,
        in_specs=(
            split_tokens,
            P("shard", None),
            P(),
            P(),
            split_rows,
            P(None, "tp"),
            split_rows,
            P(),
            P(),
            P(),
            split_rows,
            P(None, "tp"),
            split_rows,
            P(),
            split_tokens,
        ),
        out_specs=(
            split_tokens,
            split_tokens,
            P(),
            P(),
            split_rows,
            P(None, "tp"),
            split_rows,
            P(),
            P(),
            P(),
            split_rows,
            P(None, "tp"),
            split_rows,
            P(),
        ),
        check_vma=False,
    )
```

```python
import functools
import math

import jax
import jax.numpy as jnp
from jax import lax
from jax.experimental import pallas as pl
from jax.experimental.pallas import tpu as pltpu
from jax.sharding import PartitionSpec as P

HEAD_DIM = 64
EPSILON = 1e-06
NEG_LARGE = -1e30
LOW = jnp.bfloat16
FULL = jnp.float32
PAD = 128
MESH = pl.DeviceIdType.MESH
VMEM = pltpu.VMEM
HBM = pltpu.HBM
SMEM = pltpu.SMEM


def bits_of(axis):
    size = lax.axis_size(axis)
    assert size & (size - 1) == 0
    return [1 << i for i in range(size.bit_length() - 1)]


def swap(value, axis, bit):
    size = lax.axis_size(axis)
    return lax.ppermute(value, axis, [(i, i ^ bit) for i in range(size)])


def side_of(axis, bit):
    return (lax.axis_index(axis) // bit) % 2


def rows_of(value, start, count, axis=0):
    return lax.dynamic_slice_in_dim(value, start, count, axis)


def halve(axis, bits, partial, total):
    offset, span, received = jnp.int32(0), total, []

    def summed(start, count):
        value = partial(start, count)
        for got, base in received:
            value = value + rows_of(got, start - base, count).astype(FULL)
        return value

    for bit in bits:
        half = span // 2
        side = side_of(axis, bit)
        got = swap(summed(offset + (1 - side) * half, half).astype(LOW), axis, bit)
        offset = offset + side * half
        received.append((got, offset))
        span = half
    return summed(offset, span)


def double(axis, bits, value):
    for bit in bits:
        got = swap(value, axis, bit)
        first = side_of(axis, bit) == 0
        value = jnp.concatenate(
            [jnp.where(first, value, got), jnp.where(first, got, value)], axis=0
        )
    return value


def total_over(axes, value):
    for axis in axes:
        for bit in bits_of(axis):
            value = value + swap(value, axis, bit)
    return value


def ring(value, by):
    count = lax.axis_size("ctx")
    return lax.ppermute(value, "ctx", [(i, (i + by) % count) for i in range(count)])


def gather_weight(piece):
    count = lax.axis_size("ctx")
    place = lax.axis_index("ctx")
    ways = lax.axis_size("shard")
    blocks = [piece] + [ring(piece, by) for by in range(1, count)]
    whole = jnp.zeros((ways * count,) + piece.shape, piece.dtype)
    me = lax.axis_index("shard")
    for by, block in enumerate(blocks):
        at = (place - by) % count
        held = [(jnp.int32(0), block)]
        for bit in bits_of("shard"):
            held = held + [(other ^ bit, swap(value, "shard", bit)) for other, value in held]
        for other, value in held:
            whole = lax.dynamic_update_index_in_dim(whole, value, (me ^ other) * count + at, 0)
    return whole.reshape((ways * count * piece.shape[0],) + piece.shape[1:]), blocks[-1]


def scatter_weight(partial, total):
    count = lax.axis_size("ctx")
    place = lax.axis_index("ctx")
    mine = halve("shard", bits_of("shard")[::-1], partial, total).astype(LOW)
    mine = mine.reshape((count, mine.shape[0] // count) + mine.shape[1:])
    value = lax.dynamic_index_in_dim(mine, place, 0, False).astype(FULL)
    for by in range(1, count):
        given = lax.dynamic_index_in_dim(mine, (place + by) % count, 0, False)
        value = value + ring(given, by).astype(FULL)
    return value


def dot(left, right, contract):
    return lax.dot_general(
        left, right, ((contract[0], contract[1]), ((), ())), preferred_element_type=FULL
    )


def turned(value):
    return value.astype(FULL).T.astype(LOW)


def normalize(rows, gain, shift):
    row_mean = jnp.mean(rows, axis=-1, keepdims=True)
    centred = rows - row_mean
    inverse = lax.rsqrt(jnp.mean(centred * centred, axis=-1, keepdims=True) + EPSILON)
    normed = centred * inverse
    return (normed * gain + shift, normed, inverse)


def normalize_back(grad_out, normed, inverse, gain):
    scaled = grad_out * gain
    mean_grad = jnp.mean(scaled, axis=-1, keepdims=True)
    mean_cross = jnp.mean(scaled * normed, axis=-1, keepdims=True)
    return inverse * (scaled - mean_grad - normed * mean_cross)


def gelu_pair(value):
    spread = 0.5 * (1.0 + lax.erf(value * (0.5**0.5)))
    slope = spread + value * jnp.exp(-0.5 * value * value) * (1.0 / math.sqrt(2.0 * math.pi))
    return (value * spread).astype(LOW), slope.astype(LOW)


class Mover:
    def __init__(self, sizes, send, recv, local):
        self.ctx_count, self.shard_count = sizes
        self.send, self.recv, self.local = send, recv, local
        self.copies, self.here = [], []
        self.arrived = set()
        self.landed = set()
        self.ctx = lax.axis_index("ctx")
        self.shard = lax.axis_index("shard")

    def go(self, source, target, **device):
        index = len(self.copies)
        copy = pltpu.make_async_remote_copy(
            src_ref=source,
            dst_ref=target,
            send_sem=self.send.at[index],
            recv_sem=self.recv.at[index],
            device_id=device,
            device_id_type=MESH,
        )
        copy.start()
        self.copies.append(copy)
        return index

    def stay(self, source, target):
        index = len(self.here)
        copy = pltpu.make_async_copy(source, target, self.local.at[index])
        copy.start()
        self.here.append(copy)
        return index

    def near(self, *indices):
        for index in indices:
            if index not in self.landed:
                self.landed.add(index)
                self.here[index].wait()

    def take(self, index):
        if index not in self.arrived:
            self.arrived.add(index)
            self.copies[index].wait_recv()

    def flip(self, bits):
        place = self.ctx
        if bits & 1:
            place = place + 1 - 2 * lax.rem(self.ctx, 2)
        if bits & 2:
            place = place + 2 - 4 * (self.ctx // 2)
        return place

    def on(self, by):
        return lax.rem(self.ctx + by, self.ctx_count)

    def back(self, by):
        return lax.rem(self.ctx + self.ctx_count - by, self.ctx_count)

    def settle(self):
        for index, copy in enumerate(self.copies):
            self.take(index)
            copy.wait_send()
        self.near(*range(len(self.here)))


class Gather:
    def __init__(self, mover, source, target):
        self.mover, self.source, self.target = mover, source, target
        self.over = []

    def start(self):
        mover = self.mover
        mine, there = self.source, self.block(mover.ctx)
        self.far = mover.go(mine, there, ctx=mover.flip(2))
        self.close = mover.go(mine, there, ctx=mover.flip(1))
        self.over.append(mover.go(mine, there, shard=1 - mover.shard))
        self.own = mover.stay(mine, there)

    def block(self, ctx):
        mover = self.mover
        rows = self.source.shape[0]
        start = (mover.shard * mover.ctx_count + ctx) * rows
        return self.target.at[pl.ds(pl.multiple_of(start, rows), rows)]

    def pass_on(self, stage):
        mover = self.mover
        if stage == 1:
            mover.take(self.far)
            rows = self.block(mover.flip(2))
            self.passed = mover.go(rows, rows, ctx=mover.flip(1))
        elif stage == 2:
            mover.take(self.close)
            rows = self.block(mover.flip(1))
        else:
            mover.take(self.passed)
            rows = self.block(mover.flip(3))
        self.over.append(mover.go(rows, rows, shard=1 - mover.shard))

    def have(self):
        for copy in self.over:
            self.mover.take(copy)
        self.mover.near(self.own)


class Reduce:
    def __init__(self, mover, buffers, out, lhs, rhs):
        self.mover, self.out, self.lhs, self.rhs = mover, out, lhs, rhs
        self.give, self.got, self.mid, self.line = buffers
        self.half = self.give.shape[0]
        self.block = self.half // mover.ctx_count

    def compute(self, target, shard):
        chunk = min(256, self.half)

        def step(i, carry):
            at = pl.ds(pl.multiple_of(shard * self.half + i * chunk, chunk), chunk)
            here = pl.ds(pl.multiple_of(i * chunk, chunk), chunk)
            target[here, :] = dot(self.lhs[:, at], self.rhs[...], ((0,), (0,))).astype(LOW)
            return carry

        lax.fori_loop(0, self.half // chunk, step, 0)

    def begin(self):
        mover = self.mover
        self.compute(self.give, 1 - mover.shard)
        self.cross = mover.go(self.give, self.got, shard=1 - mover.shard)
        self.compute(self.mid, mover.shard)

    def fold(self):
        self.mover.take(self.cross)
        self.mid[...] = (self.mid[...].astype(FULL) + self.got[...].astype(FULL)).astype(LOW)

    def begin_blocks(self):
        mover = self.mover
        self.blocks = {}
        for bits in (3, 1, 2, 0):
            ctx = mover.flip(bits)
            at = pl.ds(pl.multiple_of(ctx * self.block, self.block), self.block)
            start = pl.multiple_of((1 - mover.shard) * self.half + ctx * self.block, self.block)
            lhs = self.lhs[:, pl.ds(start, self.block)]
            self.give[at, :] = dot(lhs, self.rhs[...], ((0,), (0,))).astype(LOW)
            self.blocks[bits] = mover.go(
                self.give.at[at], self.got.at[at], shard=1 - mover.shard
            )
        self.compute(self.mid, mover.shard)

    def fold_blocks(self, *which):
        mover = self.mover
        for bits in which:
            mover.take(self.blocks[bits])
            ctx = mover.flip(bits)
            at = pl.ds(pl.multiple_of(ctx * self.block, self.block), self.block)
            self.mid[at, :] = (
                self.mid[at, :].astype(FULL) + self.got[at, :].astype(FULL)
            ).astype(LOW)

    def rows(self, ctx):
        return self.mid.at[pl.ds(pl.multiple_of(ctx * self.block, self.block), self.block)]

    def spread(self):
        mover = self.mover
        self.first = mover.go(self.rows(mover.flip(3)), self.line.at[1], ctx=mover.flip(1))
        self.second = mover.go(self.rows(mover.flip(1)), self.line.at[0], ctx=mover.flip(1))

    def finish(self):
        mover = self.mover
        mover.take(self.first)
        rows = self.rows(mover.flip(2))
        rows[...] = (rows[...].astype(FULL) + self.line[1].astype(FULL)).astype(LOW)
        self.third = mover.go(rows, self.line.at[2], ctx=mover.flip(2))

    def done(self):
        self.mover.take(self.second)
        self.mover.take(self.third)
        value = self.rows(self.mover.ctx)[...].astype(FULL)
        self.out[...] = value + self.line[0].astype(FULL) + self.line[2].astype(FULL)


def reduce_buffers(half, width, count):
    return [
        VMEM((half, width), LOW),
        VMEM((half, width), LOW),
        VMEM((half, width), LOW),
        VMEM((count - 1, half // count, width), LOW),
    ]


def greet(mover, shard):
    barrier = pltpu.get_barrier_semaphore()
    peers = [dict(ctx=mover.on(by)) for by in range(1, mover.ctx_count)]
    peers += [dict(tp=peer) for peer in tp_peers()]
    if shard:
        peers.append(dict(shard=1 - mover.shard))
    for peer in peers:
        pl.semaphore_signal(barrier, inc=1, device_id=peer, device_id_type=MESH)
    pl.semaphore_wait(barrier, len(peers))


def tp_peers():
    place = lax.axis_index("tp")
    core, far = lax.rem(place, 2), place // 2
    return place + 1 - 2 * core, place + 2 - 4 * far


def run(kernel, name, ident, inputs, outputs, scratch, remote, local, sizes, vmem, flops):
    n_in, n_out, n_scratch = len(inputs), len(outputs), len(scratch)

    def body(*refs):
        ins, outs = refs[:n_in], refs[n_in : n_in + n_out]
        work = refs[n_in + n_out :]
        mover = Mover(sizes, *work[n_scratch:])
        kernel(mover, ins, outs, work[:n_scratch])

    return pl.pallas_call(
        body,
        in_specs=[pl.BlockSpec(memory_space=space) for _, space in inputs],
        out_specs=[pl.BlockSpec(memory_space=space) for _, _, space in outputs],
        out_shape=[jax.ShapeDtypeStruct(shape, dtype) for shape, dtype, _ in outputs],
        scratch_shapes=list(scratch)
        + [
            pltpu.SemaphoreType.DMA((remote,)),
            pltpu.SemaphoreType.DMA((remote,)),
            pltpu.SemaphoreType.DMA((local,)),
        ],
        compiler_params=pltpu.CompilerParams(
            collective_id=ident, has_side_effects=True, vmem_limit_bytes=vmem * 2**20
        ),
        cost_estimate=pl.CostEstimate(flops=flops, bytes_accessed=2**24, transcendentals=0),
        name=name,
    )(*[value for value, _ in inputs])


def order_of(block, count):
    return (block + count - 1) % count


def tiles_of(count, capacity, tile):
    ends = [-(-(p + 1) * capacity // tile) for p in range(count)]
    return list(zip([0] + ends[:-1], ends))


def parts_of(capacity):
    middle = capacity // 2 // PAD * PAD
    return [(0, middle), (middle, capacity)] if middle else [(0, capacity)]


def tile_at(t, tile):
    return pl.ds(pl.multiple_of(t * tile, tile), tile)


def turned_product(left, right, bias, target):
    def step(i, carry):
        at = pl.ds(pl.multiple_of(i * PAD, PAD), PAD)
        value = jnp.dot(left[at, :], right[...], preferred_element_type=FULL)
        if bias is not None:
            value = value + bias[0:1, :]
        target[:, at] = turned(value.astype(LOW))
        return carry

    lax.fori_loop(0, left.shape[0] // PAD, step, 0)


def head_rows(ref, head, width):
    return ref.at[pl.ds(pl.multiple_of(head * width, 16), width)]


def attend_part(size, tile, mover, joint, bias, heads, qkv, o_ref, lse, work, after_send, between):
    k_ref, q_ref, v_ref, low_ref, score_ref, top_ref = work
    count, width, capacity = qkv.shape
    slots = count * capacity
    sent = [None] + [
        mover.go(head_rows(joint, mover.on(by), width), qkv.at[by], ctx=mover.on(by))
        for by in range(1, count)
    ]
    after_send()
    qkv[0] = head_rows(joint, mover.ctx, width)[...]
    q_ref[size:PAD, :] = jnp.concatenate(
        [jnp.ones((16, slots), LOW), jnp.zeros((PAD - size - 16, slots), LOW)], axis=0
    )

    def prepare(r):
        here = slice(r * capacity, (r + 1) * capacity)
        p = order_of(r, count)
        q_ref[0:size, p * capacity : (p + 1) * capacity] = (
            qkv[r, 0:size, :] * (size**-0.5)
        ).astype(LOW)
        v_ref[:, here] = qkv[r, 2 * size : 3 * size, :]
        keys = jnp.concatenate(
            [qkv[r, size : 2 * size, :], bias[:, here], jnp.zeros((PAD - size - 16, capacity), LOW)],
            axis=0,
        )
        k_ref[here, :] = turned(keys)

    prepare(0)
    for by in range(1, count):
        mover.take(sent[by])
        prepare(by)

    last = slots // tile - 1
    assert last % 2 == 1

    def phase(t, now, following, then):
        at, ahead = tile_at(t, tile), tile_at(following, tile)
        top = top_ref[now, 0:1, :]
        total = jnp.zeros((1, tile), FULL)
        summed = jnp.zeros((size, tile), FULL)
        new_top = jnp.full((1, tile), NEG_LARGE, FULL)
        for r in range(count):
            here = slice(r * capacity, (r + 1) * capacity)
            scores = jnp.dot(k_ref[here, :], q_ref[:, ahead], preferred_element_type=FULL)
            score_ref[then, here, :] = scores
            new_top = jnp.maximum(new_top, jnp.max(scores, axis=0, keepdims=True))
            weights = jnp.exp(score_ref[now, here, :] - top)
            total = total + jnp.sum(weights, axis=0, keepdims=True)
            summed = summed + jnp.dot(
                v_ref[:, here], weights.astype(LOW), preferred_element_type=FULL
            )
        top_ref[then] = jnp.broadcast_to(new_top, (8, tile))
        out = summed / total
        o_ref[:, at] = out
        low_ref[:, at] = out.astype(LOW)
        lse[:, at] = jnp.broadcast_to(top + jnp.log(total), (8, tile))

    def step(i, carry):
        phase(2 * i, 0, 2 * i + 1, 1)
        phase(2 * i + 1, 1, jnp.minimum(2 * i + 2, last), 0)
        return carry

    scores = jnp.dot(k_ref[...], q_ref[:, 0:tile], preferred_element_type=FULL)
    score_ref[0] = scores
    top_ref[0] = jnp.broadcast_to(jnp.max(scores, axis=0, keepdims=True), (8, tile))
    arriving = []
    for p, (low, high) in enumerate(tiles_of(count, capacity, 2 * tile)):
        lax.fori_loop(low, high, step, 0)
        done = low_ref.at[:, p * capacity : (p + 1) * capacity]
        if p < count - 1:
            there = head_rows(heads, mover.ctx, size)
            arriving.append(mover.go(done, there, ctx=mover.back(p + 1)))
        else:
            head_rows(heads, mover.ctx, size)[...] = low_ref[:, p * capacity : (p + 1) * capacity]
        between(p + 1)
    for copy in arriving:
        mover.take(copy)


def attend_back_part(size, tile, mover, parts, bias, qkv, o_ref, lse, grads, work, ready, waiting, begun, between):
    k_ref, v_ref, q_ref, do_ref, nat_ref, delta_ref, dq_ref, dk_ref, dv_ref, got, back, score_ref, grad_ref = work
    count, width, capacity = qkv.shape
    slots = count * capacity
    sent = [None] + [
        mover.go(head_rows(parts, mover.on(by), size), got.at[by], ctx=mover.on(by))
        for by in range(1, count)
    ]
    got[0] = head_rows(parts, mover.ctx, size)[...]
    waiting()
    ready()
    q_ref[size:PAD, :] = jnp.concatenate(
        [jnp.ones((16, slots), LOW), jnp.zeros((PAD - size - 16, slots), LOW)], axis=0
    )
    do_ref[size:PAD, :] = jnp.zeros((PAD - size, slots), LOW)
    dq_ref[...] = jnp.zeros_like(dq_ref)
    for r in range(count):
        here = slice(r * capacity, (r + 1) * capacity)
        pad = jnp.zeros((PAD - size - 16, capacity), LOW)
        k_ref[here, :] = turned(
            jnp.concatenate([qkv[r, size : 2 * size, :], bias[:, here], pad], axis=0)
        )
        v_ref[here, :] = turned(
            jnp.concatenate(
                [qkv[r, 2 * size : 3 * size, :], jnp.zeros((PAD - size, capacity), LOW)], axis=0
            )
        )
    for r in range(count):
        if r:
            mover.take(sent[r])
        p = order_of(r, count)
        at = slice(p * capacity, (p + 1) * capacity)
        scaled = (qkv[r, 0:size, :] * (size**-0.5)).astype(LOW)
        dout = got[r]
        q_ref[0:size, at] = scaled
        do_ref[0:size, at] = dout
        nat_ref[at, :] = turned(jnp.concatenate([scaled, dout], axis=0))
        delta = jnp.sum(dout.astype(FULL) * o_ref[:, at], axis=0, keepdims=True)
        delta_ref[:, at] = jnp.broadcast_to(delta, (8, capacity))

    begun()
    last = slots // tile - 1
    assert last % 2 == 1
    tiles = tiles_of(count, capacity, 2 * tile)
    arriving = []
    mine = head_rows(grads, mover.ctx, width)
    for turn, r in enumerate(list(range(1, count)) + [0]):
        here = slice(r * capacity, (r + 1) * capacity)
        dk_ref[...] = jnp.zeros_like(dk_ref)
        dv_ref[...] = jnp.zeros_like(dv_ref)

        def ready_scores(t, then, low, high, r=r):
            ahead = tile_at(t, tile)
            rows = slice(r * capacity + low, r * capacity + high)
            score_ref[then, low:high, :] = jnp.dot(
                k_ref[rows, :], q_ref[:, ahead], preferred_element_type=FULL
            )
            grad_ref[then, low:high, :] = jnp.dot(
                v_ref[rows, :], do_ref[:, ahead], preferred_element_type=FULL
            )

        def phase(t, now, following, then, r=r):
            at = tile_at(t, tile)
            query_grad = jnp.zeros((size, tile), FULL)
            for low, high in parts_of(capacity):
                ready_scores(following, then, low, high)
                chance = jnp.exp(score_ref[now, low:high, :] - lse[0:1, at])
                score_grad = (
                    chance * (grad_ref[now, low:high, :] - delta_ref[0:1, at])
                ).astype(LOW)
                query_grad = query_grad + jnp.dot(
                    qkv[r, size : 2 * size, low:high], score_grad, preferred_element_type=FULL
                )
                dk_ref[low:high, :] += jnp.dot(
                    score_grad, nat_ref[at, :], preferred_element_type=FULL
                )
                dv_ref[low:high, :] += jnp.dot(
                    chance.astype(LOW), nat_ref[at, :], preferred_element_type=FULL
                )
            dq_ref[:, at] += query_grad

        def step(i, carry, phase=phase):
            phase(2 * i, 0, 2 * i + 1, 1)
            phase(2 * i + 1, 1, jnp.minimum(2 * i + 2, last), 0)
            return carry

        ready_scores(0, 0, 0, capacity)
        if r:
            lax.fori_loop(0, tiles[-1][1], step, 0)
        else:
            for p, (low, high) in enumerate(tiles):
                lax.fori_loop(low, high, step, 0)
                at = slice(p * capacity, (p + 1) * capacity)
                value = (dq_ref[:, at] * (size**-0.5)).astype(LOW)
                if p < count - 1:
                    back[p + 1, 0:size, :] = value
                    arriving.append(
                        mover.go(
                            back.at[p + 1, 0:size], mine.at[0:size], ctx=mover.back(p + 1)
                        )
                    )
                else:
                    mine[0:size, :] = value
        keys = dk_ref[...].T[0:size].astype(LOW)
        values = dv_ref[...].T[size : 2 * size].astype(LOW)
        if r:
            back[r, size : 2 * size, :] = keys
            back[r, 2 * size : 3 * size, :] = values
            arriving.append(
                mover.go(
                    back.at[r, size : 3 * size], mine.at[size : 3 * size], ctx=mover.back(r)
                )
            )
        else:
            mine[size : 2 * size, :] = keys
            mine[2 * size : 3 * size, :] = values
        between(turn)
    for copy in arriving:
        mover.take(copy)


def attend_back_buffers(size, count, capacity, tile):
    slots = count * capacity
    return [
        VMEM((slots, PAD), LOW),
        VMEM((slots, PAD), LOW),
        VMEM((PAD, slots), LOW),
        VMEM((PAD, slots), LOW),
        VMEM((slots, PAD), LOW),
        VMEM((8, slots), FULL),
        VMEM((size, slots), FULL),
        VMEM((capacity, PAD), FULL),
        VMEM((capacity, PAD), FULL),
        VMEM((count, size, capacity), LOW),
        VMEM((count, 3 * size, capacity), LOW),
        VMEM((2, capacity, tile), FULL),
        VMEM((2, capacity, tile), FULL),
    ]


class Round:
    def __init__(self, mover, rows, full, buffers):
        place = lax.axis_index("tp")
        core, far = lax.rem(place, 2), place // 2
        self.mover, self.full = mover, full
        self.give, self.ra, self.passing, self.rb, self.keep = buffers
        self.span = rows // 4
        self.half = self.span // 2
        self.mate, self.far = tp_peers()

        def quarter(c, f):
            return (c * 2 + f) * self.span

        self.own, self.other = quarter(core, far), quarter(core, 1 - far)
        self.mate_own, self.mate_other = quarter(1 - core, far), quarter(1 - core, 1 - far)

    def rows(self, start, count=None):
        return pl.ds(pl.multiple_of(start, 16), count or self.span)

    def hand(self, slot, value):
        self.give[slot] = value.astype(LOW)
        return self.mover.go(self.give.at[slot], self.ra.at[slot], tp=self.mate)

    def onward(self, value, index):
        self.mover.take(index)
        self.passing[...] = (value + self.ra[1].astype(FULL)).astype(LOW)
        return [
            self.mover.go(self.passing.at[at], self.rb.at[at], tp=self.far)
            for at in (pl.ds(0, self.half), pl.ds(self.half, self.half))
        ]

    def close(self, far_copies, index, finish):
        self.mover.take(index)
        self.keep[...] += self.ra[0].astype(FULL)
        self.to_far, self.to_mate = [], []
        for c in range(2):
            at = pl.ds(c * self.half, self.half)
            self.mover.take(far_copies[c])
            low = finish(at, self.keep[at] + self.rb[at].astype(FULL))
            mine = self.full.at[self.rows(self.own + c * self.half, self.half)]
            mine[...] = low
            self.to_far.append(self.mover.go(mine, mine, tp=self.far))
            self.to_mate.append(self.mover.go(mine, mine, tp=self.mate))

    def eager(self, make, finish, meanwhile=None):
        first = self.hand(1, make(self.mate_other))
        copies = self.onward(make(self.other), first)
        second = self.hand(0, make(self.mate_own))
        self.keep[...] = make(self.own)
        if meanwhile:
            meanwhile()
        self.close(copies, second, finish)

    def after(self, before, make, finish, meanwhile=None):
        before.have_mate_own()
        second = self.hand(0, make(self.mate_own))
        self.keep[...] = make(self.own)
        before.have_other()
        value = make(self.other)
        before.have_mate_other()
        first = self.hand(1, make(self.mate_other))
        copies = self.onward(value, first)
        if meanwhile:
            meanwhile()
        self.close(copies, second, finish)

    def have_mate_own(self):
        for copy in self.to_mate:
            self.mover.take(copy)

    def have_other(self):
        self.passed = []
        for c in range(2):
            self.mover.take(self.to_far[c])
            rows = self.full.at[self.rows(self.other + c * self.half, self.half)]
            self.passed.append(self.mover.go(rows, rows, tp=self.mate))

    def have_mate_other(self):
        for copy in self.passed:
            self.mover.take(copy)

    def have(self):
        self.have_mate_own()
        self.have_other()
        self.have_mate_other()


ROUND_COPIES = 10


def round_buffers(rows, width):
    span = rows // 4
    return [
        VMEM((2, span, width), LOW),
        VMEM((2, span, width), LOW),
        VMEM((span, width), LOW),
        VMEM((span, width), LOW),
        VMEM((span, width), FULL),
    ]


NAMES = ("qkv", "out", "up", "down")


def layer_kernel(plan, last, size, tile, mover, ins, outs, work):
    ins, outs, work = iter(ins), iter(outs), iter(work)
    source = next(ins)
    x_ref = None if plan.entry else next(ins)
    live_ref = next(ins)
    far_params = [next(ins) for _ in range(8)]
    stream, following = next(outs), next(outs)
    far_qkv, far_o, far_lse, far_heads, far_middle, far_second, far_hidden, far_slope = [
        next(outs) for _ in range(8)
    ]
    far_first = next(outs) if plan.entry else None
    joint, nat, heads, qkv, o_ref, lse, middle, second, hidden, slope = [
        next(work) for _ in range(10)
    ]
    first = next(work) if plan.entry else source
    attend_work = [next(work) for _ in range(6)]
    one_work, two_work = [next(work) for _ in range(5)], [next(work) for _ in range(5)]
    rows = source.shape[0]
    bias, qkv_bias = next(work), next(work)
    params = [next(work) for _ in range(8)]
    whole = {name: next(work) for name in NAMES}
    gathers, loads = {}, {}
    for name in plan.held:
        loads[name] = (next(ins), whole[name])
    for name in plan.own:
        gathers[name, 0] = Gather(mover, next(ins).at[plan.layer], whole[name])
    for name in plan.ahead:
        gathers[name, 1] = Gather(mover, next(ins).at[plan.layer + 1], next(outs))
    kept = {name: next(outs) for name in plan.own}

    greet(mover, bool(gathers))
    if plan.entry:
        gathers_first = [key for key in [("qkv", 0)] if key in gathers]
        for key in gathers_first:
            gathers[key].start()
    param_loads = [mover.stay(there, here) for there, here in zip(far_params, params)]
    loads = {name: mover.stay(*pair) for name, pair in loads.items()}

    def have(name):
        if name in loads:
            mover.near(loads[name])
        else:
            gathers[name, 0].have()
            mover.stay(whole[name], kept[name])
        return whole[name]

    def begin(keys):
        for key in keys:
            if key in gathers:
                gathers[key].start()

    def pass_on(keys, stage):
        for key in keys:
            if key in gathers:
                gathers[key].pass_on(stage)

    def pass_all(keys):
        for stage in (1, 2, 3):
            pass_on(keys, stage)

    mover.near(*param_loads)
    layer, after = plan.layer, min(plan.layer + 1, params[0].shape[0] - 1)

    def row(index, layer=layer):
        return params[index][...].astype(FULL)[layer : layer + 1]

    b_out, gain2, shift2, b_down, b_up = row(0), row(1), row(2), row(3), row(6)
    gain1, shift1, gain0, shift0 = row(4, after), row(5, after), row(4), row(5)
    qkv_bias[...] = joint_bias(row(7), size, joint.shape[0])
    key_bias(mover, live_ref, bias)
    one = Round(mover, rows, second, one_work)
    two = Round(mover, rows, following, two_work)
    if plan.entry:
        chunk = rows // 5 if rows % 80 == 0 else rows

        def norm_step(i, carry):
            at = pl.ds(pl.multiple_of(i * chunk, 16), chunk)
            value = normalize(source[at, :].astype(FULL), gain0, shift0)[0]
            first[at, :] = value.astype(LOW)
            return carry

        lax.fori_loop(0, rows // chunk, norm_step, 0)
        mover.stay(first, far_first)
        pass_all([("qkv", 0)])
        begin([("out", 0), ("up", 0)])
        turned_product(first, have("qkv"), qkv_bias, joint)
    else:
        turned_product(first, have("qkv"), qkv_bias, joint)

    def after_send():
        if plan.entry:
            pass_all([("out", 0), ("up", 0)])
        else:
            begin([("out", 0), ("down", 0)])

    def between(p):
        if plan.entry and p == 1:
            begin([("down", 0)])
        if not plan.entry and p > 1:
            pass_on([("out", 0), ("down", 0)], p - 1)

    attend_part(
        size, tile, mover, joint, bias, heads, qkv, o_ref, lse, attend_work, after_send, between
    )
    nat[...] = turned(heads[...])
    mover.stay(qkv, far_qkv)
    mover.stay(o_ref, far_o)
    mover.stay(lse, far_lse)
    mover.stay(nat, far_heads)
    w_out = have("out")

    def out_part(start):
        return dot(nat[one.rows(start), :], w_out[...], ((1,), (1,)))

    def to_second(at, value):
        if plan.entry:
            before = source[one.rows(one.own + at.start, at.size), :].astype(FULL)
        else:
            before = x_ref[at]
        value = before + value + b_out
        middle[at] = value
        return normalize(value, gain2, shift2)[0].astype(LOW)

    if plan.entry:
        one.eager(out_part, to_second, lambda: pass_all([("down", 0)]))
    else:
        one.eager(out_part, to_second)
    begin([("qkv", 1), ("up", 1)])
    w_up, w_down = have("up"), have("down")

    def mlp_part(start):
        at = two.rows(start)
        pre = jnp.dot(second[at, :], w_up[...], preferred_element_type=FULL) + b_up
        low, low_slope = gelu_pair(pre)
        hidden[at, :] = low
        slope[at, :] = low_slope
        return dot(low, w_down[...], ((1,), (1,)))

    def to_following(at, value):
        value = middle[at] + value + b_down
        stream[at] = value
        if last:
            return live_rows(value, two.own + at.start, live_ref[0, mover.ctx]).astype(LOW)
        return normalize(value, gain1, shift1)[0].astype(LOW)

    def meanwhile():
        mover.stay(middle, far_middle)
        mover.stay(second, far_second)
        mover.stay(hidden, far_hidden)
        mover.stay(slope, far_slope)
        pass_all([("qkv", 1), ("up", 1)])

    two.after(one, mlp_part, to_following, meanwhile)
    two.have()
    mover.settle()


class Plan:
    def __init__(self, layer, last, inside):
        self.layer, self.entry = layer, layer == 0
        self.own = (NAMES if layer == 0 else ("out", "down")) if inside else ()
        self.ahead = ("qkv", "up") if inside and not last else ()
        self.held = tuple(name for name in NAMES if name not in self.own)


def forward_layer(source, x, live, params, gathered, weights, plan, last, size, sizes, ident):
    rows, width = source.shape
    count = sizes[0]
    joint, hidden = weights["qkv"].shape[2], weights["up"].shape[2]
    heads = joint // (3 * size)
    attn, slots, span = heads * size, count * rows, rows // 4
    tile = 256 if slots % 256 == 0 else PAD
    columns = {"qkv": joint, "out": attn, "up": hidden, "down": hidden}
    inputs = [(source, VMEM)] + ([] if plan.entry else [(x, VMEM)])
    inputs += [(live, SMEM)] + [(value, HBM) for value in params]
    inputs += [(gathered[name, plan.layer], HBM) for name in plan.held]
    inputs += [(weights[name], HBM) for name in plan.own + plan.ahead]
    saved = [
        ((count, 3 * size, rows), LOW),
        ((size, slots), FULL),
        ((8, slots), FULL),
        ((rows, attn), LOW),
        ((span, width), FULL),
        ((rows, width), LOW),
        ((rows, hidden), LOW),
        ((rows, hidden), LOW),
    ]
    outputs = [((span, width), FULL, VMEM), ((rows, width), LOW, VMEM)]
    outputs += [(shape, dtype, HBM) for shape, dtype in saved]
    if plan.entry:
        outputs.append(((rows, width), LOW, HBM))
    outputs += [((width, columns[name]), LOW, HBM) for name in plan.ahead + plan.own]
    qkv_shape, o_shape, lse_shape, heads_shape = saved[:4]
    scratch = [VMEM((joint, rows), LOW), VMEM((rows, attn), LOW), VMEM((attn, rows), LOW)]
    scratch += [VMEM(*pair) for pair in saved[:3] + saved[4:]]
    if plan.entry:
        scratch.append(VMEM((rows, width), LOW))
    scratch += [
        VMEM((slots, PAD), LOW),
        VMEM((PAD, slots), LOW),
        VMEM((size, slots), LOW),
        VMEM((size, slots), LOW),
        VMEM((2, slots, tile), FULL),
        VMEM((2, 8, tile), FULL),
    ]
    scratch += round_buffers(rows, width) + round_buffers(rows, width)
    scratch += [VMEM((16, slots), LOW), VMEM((16, joint), FULL)]
    scratch += [VMEM(value.shape, value.dtype) for value in params]
    scratch += [VMEM((width, columns[name]), LOW) for name in NAMES]
    results = run(
        functools.partial(layer_kernel, plan, last, size, tile),
        "forward_layer",
        ident,
        inputs,
        outputs,
        scratch,
        2 * (count - 1) + 2 * ROUND_COPIES + 2 * count * len(plan.own + plan.ahead),
        9 + 2 * len(NAMES) + 2 + len(params),
        sizes,
        58,
        2 * rows * width * (2 * hidden + attn + joint) + 4 * slots * slots * 256,
    )
    stream, following = results[:2]
    kept = results[2 : 11 if plan.entry else 10]
    for name, value in zip(plan.ahead, results[2 + len(kept) :]):
        gathered[name, plan.layer + 1] = value
    for name, value in zip(plan.own, results[2 + len(kept) + len(plan.ahead) :]):
        gathered[name, plan.layer] = value
    return stream, following, kept


def key_bias(mover, live_ref, bias):
    capacity = bias.shape[1] // mover.ctx_count
    row = lax.broadcasted_iota(jnp.int32, (16, capacity), 0)
    slot = lax.broadcasted_iota(jnp.int32, (16, capacity), 1)
    for r in range(mover.ctx_count):
        live = live_ref[0, mover.back(r)]
        value = jnp.where((row == 0) & (slot >= live), NEG_LARGE, 0.0)
        bias[:, r * capacity : (r + 1) * capacity] = value.astype(LOW)


def joint_bias(pair, size, width):
    rows = pair.shape[1]
    given = lax.broadcasted_iota(jnp.int32, (rows, width), 0)
    column = lax.broadcasted_iota(jnp.int32, (rows, width), 1)
    head, within = column // (3 * size), column % (3 * size)
    wanted = head * (2 * size) + jnp.where(within < size, within, within - size)
    key = (within >= size) & (within < 2 * size)
    chosen = jnp.where((given == wanted) & ~key, 1.0, 0.0).astype(LOW)
    spread = jnp.broadcast_to(pair, (16, rows)).astype(LOW)
    return jnp.dot(spread, chosen, preferred_element_type=FULL)


def live_rows(value, start, live):
    row = start + lax.broadcasted_iota(jnp.int32, value.shape, 0)
    return jnp.where(row < live, value, 0.0)


def sums_into(sums, first, at, values):
    for index, value in enumerate(values):
        row = first + index
        added = jnp.sum(value, axis=0, keepdims=True)
        width = added.shape[1]
        sums[row : row + 1, 0:width] = (
            added if at.start == 0 else sums[row : row + 1, 0:width] + added
        )


def back_kernel(plan, size, tile, mover, ins, outs, work):
    ins, outs, work = iter(ins), iter(outs), iter(work)
    source = next(ins)
    x_ref = None if plan.last else next(ins)
    live_ref, far_gain2, far_gain1 = [next(ins) for _ in range(3)]
    far = [next(ins) for _ in range(14)]
    late_far = next(ins) if plan.late else None
    others = [(next(ins), next(ins)) for _ in range(plan.others)]
    stream, following = next(outs), next(outs)
    grad_outs = {name: next(outs) for name in NAMES if plan.inside and (name != "qkv" or plan.final)}
    mid_out = next(outs) if plan.inside and not plan.final else None
    late_out = next(outs) if plan.late else None
    split = local = totals = None
    if plan.joined:
        totals = next(outs)
    else:
        split, local = next(outs), next(outs)
    wholes = {} if plan.inside else {name: next(outs) for name in NAMES}
    near = [next(work) for _ in range(14)]
    slope, w_down, w_up, middle, hidden, second, w_out, heads, qkv, o_ref, lse, first, w_qkv, before = near
    grad = next(work) if plan.last else source
    pre_grad, attn_grad, parts, grads, nat = [next(work) for _ in range(5)]
    attend_work = [next(work) for _ in range(13)]
    one_work, two_work = [next(work) for _ in range(5)], [next(work) for _ in range(5)]
    rows, width = source.shape
    reduces = {}
    if plan.inside:
        pairs = {
            "down": (grad, hidden),
            "up": (second, pre_grad),
            "out": (attn_grad, heads),
            "qkv": (first, nat),
        }
        for name in ("down", "up", "out", "qkv"):
            buffers = [next(work) for _ in range(4)]
            reduces[name] = Reduce(mover, buffers, grad_outs.get(name), *pairs[name])
    late = None
    if plan.late:
        late_mid, late_line = next(work), next(work)
        late = Reduce(mover, (late_mid, None, late_mid, late_line), late_out, None, None)
    bias, gain2_ref, gain1_ref = [next(work) for _ in range(3)]
    if plan.joined:
        split, local = next(work), next(work)
        got_tp, got_shard, got_ctx, mine = [next(work) for _ in range(4)]

    greet(mover, plan.inside)
    gain_loads = [mover.stay(far_gain2, gain2_ref), mover.stay(far_gain1, gain1_ref)]
    load = [mover.stay(there, here) for there, here in zip(far, near)]
    if late:
        mover.near(mover.stay(late_far, late_mid))
        late.spread()
    if plan.last:
        chunk = rows // 5 if rows % 80 == 0 else rows

        def mask_step(i, carry):
            at = pl.ds(pl.multiple_of(i * chunk, 16), chunk)
            value = source[at, :].astype(FULL)
            grad[at, :] = live_rows(value, i * chunk, live_ref[0, mover.ctx]).astype(LOW)
            return carry

        lax.fori_loop(0, rows // chunk, mask_step, 0)
    one = Round(mover, rows, attn_grad, one_work)
    two = Round(mover, rows, following, two_work)
    key_bias(mover, live_ref, bias)
    mover.near(*gain_loads)
    gain2, gain1 = [
        ref[...].astype(FULL)[plan.layer : plan.layer + 1] for ref in (gain2_ref, gain1_ref)
    ]
    split[...] = jnp.zeros_like(split)
    local[...] = jnp.zeros_like(local)
    split[5:6, 0:width] = jnp.sum(
        grad[one.rows(one.own), :].astype(FULL), axis=0, keepdims=True
    )
    mover.near(*load[:3])
    hidden_width = slope.shape[1]

    def mlp_part(start):
        at = one.rows(start)
        pre = jnp.dot(grad[at, :], w_down[...], preferred_element_type=FULL)
        low = (pre * slope[at, :].astype(FULL)).astype(LOW)
        pre_grad[at, :] = low
        local[0:1, 0:hidden_width] += jnp.sum(low.astype(FULL), axis=0, keepdims=True)
        return dot(low, w_up[...], ((1,), (1,)))

    def to_attn(at, value):
        if plan.last:
            above = grad[one.rows(one.own + at.start, at.size), :].astype(FULL)
        else:
            above = x_ref[at]
        _, normed, inverse = normalize(middle[at], 1.0, 0.0)
        result = above + normalize_back(value, normed, inverse, gain2)
        stream[at] = result
        low = result.astype(LOW)
        sums_into(split, 2, at, (value * normed, value, low.astype(FULL)))
        return low

    def reduce(name):
        if name in reduces:
            reduces[name].begin()

    def fold(name):
        if name in reduces:
            reduces[name].fold()
            reduces[name].spread()

    def finish(name):
        if name in reduces:
            reduces[name].finish()

    def start_down():
        mover.near(load[3], load[4])
        reduce("down")

    one.eager(mlp_part, to_attn, start_down)
    mover.near(load[5])
    reduce("up")
    one.have()
    mover.near(load[6])
    turned_product(attn_grad, w_out, None, parts)

    def waiting():
        mover.near(load[7])
        reduce("out")

    def ready():
        mover.near(load[8], load[9], load[10])
        if late:
            late.finish()

    def between(turn):
        if turn == 0:
            finish("down")

    attend_back_part(
        size,
        tile,
        mover,
        parts,
        bias,
        qkv,
        o_ref,
        lse,
        grads,
        attend_work,
        ready,
        waiting,
        lambda: fold("down"),
        between,
    )
    nat[...] = turned(grads[...])
    local[1:2, 0 : nat.shape[1]] = jnp.sum(nat[...].astype(FULL), axis=0, keepdims=True)
    mover.near(*load[11:])

    def qkv_part(start):
        return dot(nat[two.rows(start), :], w_qkv[...], ((1,), (1,)))

    def to_following(at, value):
        if plan.final:
            row = before[two.rows(two.own + at.start, at.size), :].astype(FULL)
        else:
            row = before[at]
        _, normed, inverse = normalize(row, 1.0, 0.0)
        result = stream[at] + normalize_back(value, normed, inverse, gain1)
        stream[at] = result
        low = result.astype(LOW)
        sums_into(split, 0, at, (value * normed, value))
        return low

    def start_qkv():
        if plan.inside:
            reduces["qkv"].begin_blocks()
        fold("up")
        fold("out")

    two.eager(qkv_part, to_following, start_qkv)
    finish("up")
    finish("out")
    if plan.joined:
        place = lax.axis_index("tp")
        ways = got_tp.shape[0]
        count = plan.others + 1
        for layer, pair in enumerate([(split, local)] + others):
            for index, value in enumerate(pair):
                for row in range(8):
                    mine[index, row * count + layer : row * count + layer + 1] = value[
                        row : row + 1, :
                    ]
        got_tp[place] = mine[0]
        tp_copies = [
            mover.go(mine.at[0], got_tp.at[place], tp=lax.rem(place + by, ways))
            for by in range(1, ways)
        ]
    if plan.inside:
        reduces["qkv"].fold_blocks(3, 1)
        if plan.final:
            reduces["qkv"].spread()
    two.have()
    if plan.inside:
        reduces["qkv"].fold_blocks(2, 0)
        if plan.final:
            reduces["qkv"].finish()
        else:
            mover.stay(reduces["qkv"].mid, mid_out)
    if plan.joined:
        for copy in tp_copies:
            mover.take(copy)
        value = got_tp[0]
        for other in range(1, ways):
            value = value + got_tp[other]
        mine[2] = value
        cross = mover.go(mine.at[pl.ds(1, 2)], got_shard, shard=1 - mover.shard)
        mover.take(cross)
        got_ctx[mover.ctx] = mine[1:3] + got_shard[...]
        there = got_ctx.at[mover.ctx]
        lines = [mover.go(there, there, ctx=mover.on(by)) for by in range(1, mover.ctx_count)]
        for copy in lines:
            mover.take(copy)
        value = got_ctx[0]
        for other in range(1, mover.ctx_count):
            value = value + got_ctx[other]
        totals[...] = value
    for name in ("down", "up", "out"):
        if name in reduces:
            reduces[name].done()
    if late:
        late.done()
    if plan.inside and plan.final:
        reduces["qkv"].done()
    if not plan.inside:
        for name, (lhs, rhs) in {
            "down": (grad, hidden),
            "up": (second, pre_grad),
            "out": (attn_grad, heads),
            "qkv": (first, nat),
        }.items():
            full = Reduce(mover, (wholes[name],) * 4, None, lhs, rhs)
            full.compute(wholes[name], 0)
    mover.settle()


class BackPlan:
    def __init__(self, layer, layers, inside):
        self.inside, self.layer = inside, layer
        self.last, self.final = layer == layers - 1, layer == 0
        self.late = inside and not self.last
        self.joined = inside and self.final
        self.others = layers - 1 if self.joined else 0


def back_layer(source, x, live, gain2, gain1, saved, late, others, plan, size, sizes, ident):
    rows, width = source.shape
    count = sizes[0]
    slope, w_down, w_up = saved[:3]
    hidden, joint, attn = slope.shape[1], saved[12].shape[1], saved[6].shape[1]
    slots, span = count * rows, rows // 4
    tile = 256 if slots % 256 == 0 else PAD
    wide = max(width, hidden, joint)
    half = width // 2
    block = half // count
    columns = {"qkv": joint, "out": attn, "up": hidden, "down": hidden}
    inputs = [(source, VMEM)] + ([] if plan.last else [(x, VMEM)])
    inputs += [(live, SMEM), (gain2, HBM), (gain1, HBM)]
    inputs += [(value, HBM) for value in saved]
    if plan.late:
        inputs.append((late, HBM))
    for pair in others[: plan.others]:
        inputs += [(value, VMEM) for value in pair]
    outputs = [((span, width), FULL, VMEM), ((rows, width), LOW, VMEM)]
    names = [name for name in NAMES if plan.inside and (name != "qkv" or plan.final)]
    outputs += [((block, columns[name]), FULL, VMEM) for name in names]
    if plan.inside and not plan.final:
        outputs.append(((half, joint), LOW, HBM))
    if plan.late:
        outputs.append(((block, joint), FULL, VMEM))
    depth = 8 * (plan.others + 1)
    if plan.joined:
        outputs.append(((2, depth, wide), FULL, VMEM))
    else:
        outputs += [((8, wide), FULL, VMEM)] * 2
    if not plan.inside:
        outputs += [((width, columns[name]), LOW, VMEM) for name in NAMES]
    scratch = [VMEM(value.shape, value.dtype) for value in saved]
    if plan.last:
        scratch.append(VMEM((rows, width), LOW))
    scratch += [
        VMEM((rows, hidden), LOW),
        VMEM((rows, width), LOW),
        VMEM((attn, rows), LOW),
        VMEM((joint, rows), LOW),
        VMEM((rows, joint), LOW),
    ]
    scratch += attend_back_buffers(size, count, rows, tile)
    scratch += round_buffers(rows, width) + round_buffers(rows, width)
    if plan.inside:
        for name in ("down", "up", "out", "qkv"):
            scratch += reduce_buffers(half, columns[name], count)
    if plan.late:
        scratch += [VMEM((half, joint), LOW), VMEM((count - 1, block, joint), LOW)]
    scratch.append(VMEM((16, slots), LOW))
    scratch += [VMEM(value.shape, value.dtype) for value in (gain2, gain1)]
    ways = lax.axis_size("tp")
    if plan.joined:
        scratch += [VMEM((8, wide), FULL)] * 2
        scratch += [
            VMEM((ways, depth, wide), FULL),
            VMEM((2, depth, wide), FULL),
            VMEM((count, 2, depth, wide), FULL),
            VMEM((3, depth, wide), FULL),
        ]
    results = run(
        functools.partial(back_kernel, plan, size, tile),
        "back_layer",
        ident,
        inputs,
        outputs,
        scratch,
        3 * (count - 1) + 2 * ROUND_COPIES + 6 * count + ways + count,
        len(saved) + 4,
        sizes,
        58,
        6 * rows * width * (2 * hidden + attn + joint) + 10 * slots * slots * 256,
    )
    return results[:2], names, results[2:]


def shards(
    tokens,
    block_tokens,
    ln1_gain,
    ln1_bias,
    w_qkv,
    b_qv,
    w_out,
    b_out,
    ln2_gain,
    ln2_bias,
    w_up,
    b_up,
    w_down,
    b_down,
    cotangent,
):
    images, capacity, width = tokens.shape
    assert images == 1
    layers = w_qkv.shape[0]
    size = HEAD_DIM
    ctx_count = lax.axis_size("ctx")
    ctx_place = lax.axis_index("ctx")
    joint_width = w_qkv.shape[2]
    heads = joint_width // (3 * size)
    assert heads == ctx_count
    attn_width = heads * size
    hidden_width = w_up.shape[2]
    weights = {"qkv": w_qkv, "out": w_out, "up": w_up, "down": w_down}
    sizes = (ctx_count, lax.axis_size("shard"))
    inside = sizes == (4, 2)
    gathered = {}
    if not inside:
        for name, value in weights.items():
            for layer in range(layers):
                gathered[name, layer] = gather_weight(value[layer])[0]
    source, stream = tokens[0], None
    saved = []
    for layer in range(layers):
        last = layer == layers - 1
        result, following, kept = forward_layer(
            source,
            stream,
            block_tokens,
            (b_out, ln2_gain, ln2_bias, b_down, ln1_gain, ln1_bias, b_up, b_qv),
            gathered,
            weights,
            Plan(layer, last, inside),
            last,
            size,
            sizes,
            1 + layer,
        )
        before = stream if layer else source
        first = source if layer else kept[8]
        saved.append((before, first) + tuple(kept[:8]))
        source, stream = following, result
    mixed = source[None]

    done, packs = {}, {}
    source, stream, late = cotangent[0], None, None
    for layer in reversed(range(layers)):
        before, first, qkv, head_out, lse, heads_low, middle, second, hidden, slope = saved[layer]
        plan = BackPlan(layer, layers, inside)
        whole = {name: gathered[name, layer] for name in NAMES}
        near = [slope, whole["down"], whole["up"], middle, hidden, second, whole["out"]]
        near += [heads_low, qkv, head_out, lse, first, whole["qkv"], before]
        others = [packs[key] for key in sorted(packs)]
        (stream, source), names, rest = back_layer(
            source, stream, block_tokens, ln2_gain, ln1_gain, near, late, others, plan, size, sizes, 1 + layers + layer
        )
        rest = iter(rest)
        for name in names:
            done[name, layer] = next(rest)
        if plan.inside and not plan.final:
            late = next(rest)
        if plan.late:
            done["qkv", layer + 1] = next(rest)
        if plan.joined:
            totals = next(rest)
        else:
            packs[layer] = (next(rest), next(rest))
        if not inside:
            for name in NAMES:
                value = next(rest)
                done[name, layer] = scatter_weight(
                    lambda start, count, value=value: rows_of(value, start, count).astype(FULL),
                    width,
                )
    token_grads = source.astype(FULL)[None]
    if not inside:
        split = total_over(("tp",), jnp.stack([packs[l][0] for l in range(layers)], axis=1))
        local = jnp.stack([packs[l][1] for l in range(layers)], axis=1)
        totals = total_over(("shard", "ctx"), jnp.stack([local, split]))
    local = totals[0].reshape(8, layers, -1)
    named = totals[1].reshape(8, layers, -1)[:, :, :width]
    columns = local[1, :, :joint_width].reshape(layers, heads, 3, size)
    g_qv = jnp.stack([columns[:, :, 0], columns[:, :, 2]], axis=2).reshape(layers, -1)
    stacked = [
        jnp.stack([done[name, layer] for layer in range(layers)], axis=0) for name in NAMES
    ]
    return (
        mixed,
        token_grads,
        named[0],
        named[1],
        stacked[0],
        g_qv,
        stacked[1],
        named[4],
        named[2],
        named[3],
        stacked[2],
        local[0, :, :hidden_width],
        stacked[3],
        named[5],
    )


def solution(mesh):
    split_rows = P(None, ("shard", "ctx"), "tp")
    split_tokens = P("shard", "ctx", None)
    return jax.shard_map(
        shards,
        mesh=mesh,
        in_specs=(
            split_tokens,
            P("shard", None),
            P(),
            P(),
            split_rows,
            P(None, "tp"),
            split_rows,
            P(),
            P(),
            P(),
            split_rows,
            P(None, "tp"),
            split_rows,
            P(),
            split_tokens,
        ),
        out_specs=(
            split_tokens,
            split_tokens,
            P(),
            P(),
            split_rows,
            P(None, "tp"),
            split_rows,
            P(),
            P(),
            P(),
            split_rows,
            P(None, "tp"),
            split_rows,
            P(),
        ),
        check_vma=False,
    )
```

```python
import functools
import math

import jax
import jax.numpy as jnp
from jax import lax
from jax.experimental import pallas as pl
from jax.experimental.pallas import tpu as pltpu
from jax.sharding import PartitionSpec as P

HEAD_DIM = 64
EPSILON = 1e-06
NEG_LARGE = -1e30
LOW = jnp.bfloat16
FULL = jnp.float32
PAD = 128
MESH = pl.DeviceIdType.MESH
VMEM = pltpu.VMEM
HBM = pltpu.HBM
SMEM = pltpu.SMEM


def bits_of(axis):
    size = lax.axis_size(axis)
    assert size & (size - 1) == 0
    return [1 << i for i in range(size.bit_length() - 1)]


def swap(value, axis, bit):
    size = lax.axis_size(axis)
    return lax.ppermute(value, axis, [(i, i ^ bit) for i in range(size)])


def side_of(axis, bit):
    return (lax.axis_index(axis) // bit) % 2


def rows_of(value, start, count, axis=0):
    return lax.dynamic_slice_in_dim(value, start, count, axis)


def halve(axis, bits, partial, total):
    offset, span, received = jnp.int32(0), total, []

    def summed(start, count):
        value = partial(start, count)
        for got, base in received:
            value = value + rows_of(got, start - base, count).astype(FULL)
        return value

    for bit in bits:
        half = span // 2
        side = side_of(axis, bit)
        got = swap(summed(offset + (1 - side) * half, half).astype(LOW), axis, bit)
        offset = offset + side * half
        received.append((got, offset))
        span = half
    return summed(offset, span)


def double(axis, bits, value):
    for bit in bits:
        got = swap(value, axis, bit)
        first = side_of(axis, bit) == 0
        value = jnp.concatenate(
            [jnp.where(first, value, got), jnp.where(first, got, value)], axis=0
        )
    return value


def total_over(axes, value):
    for axis in axes:
        for bit in bits_of(axis):
            value = value + swap(value, axis, bit)
    return value


def ring(value, by):
    count = lax.axis_size("ctx")
    return lax.ppermute(value, "ctx", [(i, (i + by) % count) for i in range(count)])


def gather_weight(piece):
    count = lax.axis_size("ctx")
    place = lax.axis_index("ctx")
    ways = lax.axis_size("shard")
    blocks = [piece] + [ring(piece, by) for by in range(1, count)]
    whole = jnp.zeros((ways * count,) + piece.shape, piece.dtype)
    me = lax.axis_index("shard")
    for by, block in enumerate(blocks):
        at = (place - by) % count
        held = [(jnp.int32(0), block)]
        for bit in bits_of("shard"):
            held = held + [(other ^ bit, swap(value, "shard", bit)) for other, value in held]
        for other, value in held:
            whole = lax.dynamic_update_index_in_dim(whole, value, (me ^ other) * count + at, 0)
    return whole.reshape((ways * count * piece.shape[0],) + piece.shape[1:]), blocks[-1]


def scatter_weight(partial, total):
    count = lax.axis_size("ctx")
    place = lax.axis_index("ctx")
    mine = halve("shard", bits_of("shard")[::-1], partial, total).astype(LOW)
    mine = mine.reshape((count, mine.shape[0] // count) + mine.shape[1:])
    value = lax.dynamic_index_in_dim(mine, place, 0, False).astype(FULL)
    for by in range(1, count):
        given = lax.dynamic_index_in_dim(mine, (place + by) % count, 0, False)
        value = value + ring(given, by).astype(FULL)
    return value


def dot(left, right, contract):
    return lax.dot_general(
        left, right, ((contract[0], contract[1]), ((), ())), preferred_element_type=FULL
    )


def turned(value):
    return value.astype(FULL).T.astype(LOW)


def normalize(rows, gain, shift):
    row_mean = jnp.mean(rows, axis=-1, keepdims=True)
    centred = rows - row_mean
    inverse = lax.rsqrt(jnp.mean(centred * centred, axis=-1, keepdims=True) + EPSILON)
    normed = centred * inverse
    return (normed * gain + shift, normed, inverse)


def normalize_back(grad_out, normed, inverse, gain):
    scaled = grad_out * gain
    mean_grad = jnp.mean(scaled, axis=-1, keepdims=True)
    mean_cross = jnp.mean(scaled * normed, axis=-1, keepdims=True)
    return inverse * (scaled - mean_grad - normed * mean_cross)


def gelu_pair(value):
    spread = 0.5 * (1.0 + lax.erf(value * (0.5**0.5)))
    slope = spread + value * jnp.exp(-0.5 * value * value) * (1.0 / math.sqrt(2.0 * math.pi))
    return (value * spread).astype(LOW), slope.astype(LOW)


class Mover:
    def __init__(self, sizes, send, recv, local):
        self.ctx_count, self.shard_count = sizes
        self.send, self.recv, self.local = send, recv, local
        self.copies, self.here = [], []
        self.arrived = set()
        self.landed = set()
        self.ctx = lax.axis_index("ctx")
        self.shard = lax.axis_index("shard")

    def go(self, source, target, **device):
        index = len(self.copies)
        copy = pltpu.make_async_remote_copy(
            src_ref=source,
            dst_ref=target,
            send_sem=self.send.at[index],
            recv_sem=self.recv.at[index],
            device_id=device,
            device_id_type=MESH,
        )
        copy.start()
        self.copies.append(copy)
        return index

    def stay(self, source, target):
        index = len(self.here)
        copy = pltpu.make_async_copy(source, target, self.local.at[index])
        copy.start()
        self.here.append(copy)
        return index

    def near(self, *indices):
        for index in indices:
            if index not in self.landed:
                self.landed.add(index)
                self.here[index].wait()

    def take(self, index):
        if index not in self.arrived:
            self.arrived.add(index)
            self.copies[index].wait_recv()

    def flip(self, bits):
        place = self.ctx
        if bits & 1:
            place = place + 1 - 2 * lax.rem(self.ctx, 2)
        if bits & 2:
            place = place + 2 - 4 * (self.ctx // 2)
        return place

    def on(self, by):
        return lax.rem(self.ctx + by, self.ctx_count)

    def back(self, by):
        return lax.rem(self.ctx + self.ctx_count - by, self.ctx_count)

    def settle(self):
        for index, copy in enumerate(self.copies):
            self.take(index)
            copy.wait_send()
        self.near(*range(len(self.here)))


class Gather:
    def __init__(self, mover, source, target):
        self.mover, self.source, self.target = mover, source, target
        self.over = []

    def start(self):
        self.start_line()
        self.start_over()

    def start_line(self):
        mover = self.mover
        mine, there = self.source, self.block(mover.ctx)
        self.far = mover.go(mine, there, ctx=mover.flip(2))
        self.close = mover.go(mine, there, ctx=mover.flip(1))

    def start_over(self):
        mover = self.mover
        mine, there = self.source, self.block(mover.ctx)
        self.over.append(mover.go(mine, there, shard=1 - mover.shard))
        self.own = mover.stay(mine, there)

    def block(self, ctx):
        mover = self.mover
        rows = self.source.shape[0]
        start = (mover.shard * mover.ctx_count + ctx) * rows
        return self.target.at[pl.ds(pl.multiple_of(start, rows), rows)]

    def pass_on(self, stage):
        mover = self.mover
        if stage == 1:
            mover.take(self.far)
            rows = self.block(mover.flip(2))
            self.passed = mover.go(rows, rows, ctx=mover.flip(1))
        elif stage == 2:
            mover.take(self.close)
            rows = self.block(mover.flip(1))
        else:
            mover.take(self.passed)
            rows = self.block(mover.flip(3))
        self.over.append(mover.go(rows, rows, shard=1 - mover.shard))

    def have(self):
        for copy in self.over:
            self.mover.take(copy)
        self.mover.near(self.own)


class Reduce:
    def __init__(self, mover, buffers, out, lhs, rhs):
        self.mover, self.out, self.lhs, self.rhs = mover, out, lhs, rhs
        self.give, self.got, self.mid, self.line = buffers
        self.half = self.give.shape[0]
        self.block = self.half // mover.ctx_count

    def compute(self, target, shard):
        chunk = min(256, self.half)

        def step(i, carry):
            at = pl.ds(pl.multiple_of(shard * self.half + i * chunk, chunk), chunk)
            here = pl.ds(pl.multiple_of(i * chunk, chunk), chunk)
            target[here, :] = dot(self.lhs[:, at], self.rhs[...], ((0,), (0,))).astype(LOW)
            return carry

        lax.fori_loop(0, self.half // chunk, step, 0)

    def begin(self):
        mover = self.mover
        self.compute(self.give, 1 - mover.shard)
        self.cross = mover.go(self.give, self.got, shard=1 - mover.shard)
        self.compute(self.mid, mover.shard)

    def fold(self):
        self.mover.take(self.cross)
        self.mid[...] = (self.mid[...].astype(FULL) + self.got[...].astype(FULL)).astype(LOW)

    def begin_blocks(self):
        mover = self.mover
        self.blocks = {}
        for bits in (3, 1, 2, 0):
            ctx = mover.flip(bits)
            at = pl.ds(pl.multiple_of(ctx * self.block, self.block), self.block)
            start = pl.multiple_of((1 - mover.shard) * self.half + ctx * self.block, self.block)
            lhs = self.lhs[:, pl.ds(start, self.block)]
            self.give[at, :] = dot(lhs, self.rhs[...], ((0,), (0,))).astype(LOW)
            self.blocks[bits] = mover.go(
                self.give.at[at], self.got.at[at], shard=1 - mover.shard
            )

    def fold_blocks(self, *which):
        mover = self.mover
        for bits in which:
            mover.take(self.blocks[bits])
            ctx = mover.flip(bits)
            at = pl.ds(pl.multiple_of(ctx * self.block, self.block), self.block)
            self.mid[at, :] = (
                self.mid[at, :].astype(FULL) + self.got[at, :].astype(FULL)
            ).astype(LOW)

    def rows(self, ctx):
        return self.mid.at[pl.ds(pl.multiple_of(ctx * self.block, self.block), self.block)]

    def spread(self):
        mover = self.mover
        self.first = mover.go(self.rows(mover.flip(3)), self.line.at[1], ctx=mover.flip(1))
        self.second = mover.go(self.rows(mover.flip(1)), self.line.at[0], ctx=mover.flip(1))

    def finish(self):
        mover = self.mover
        mover.take(self.first)
        rows = self.rows(mover.flip(2))
        rows[...] = (rows[...].astype(FULL) + self.line[1].astype(FULL)).astype(LOW)
        self.third = mover.go(rows, self.line.at[2], ctx=mover.flip(2))

    def done(self):
        self.mover.take(self.second)
        self.mover.take(self.third)
        value = self.rows(self.mover.ctx)[...].astype(FULL)
        self.out[...] = value + self.line[0].astype(FULL) + self.line[2].astype(FULL)


def reduce_buffers(half, width, count):
    return [
        VMEM((half, width), LOW),
        VMEM((half, width), LOW),
        VMEM((half, width), LOW),
        VMEM((count - 1, half // count, width), LOW),
    ]


def greet(mover, shard):
    barrier = pltpu.get_barrier_semaphore()
    peers = [dict(ctx=mover.on(by)) for by in range(1, mover.ctx_count)]
    peers += [dict(tp=peer) for peer in tp_peers()]
    if shard:
        peers.append(dict(shard=1 - mover.shard))
    for peer in peers:
        pl.semaphore_signal(barrier, inc=1, device_id=peer, device_id_type=MESH)
    pl.semaphore_wait(barrier, len(peers))


def tp_peers():
    place = lax.axis_index("tp")
    core, far = lax.rem(place, 2), place // 2
    return place + 1 - 2 * core, place + 2 - 4 * far


def run(kernel, name, ident, inputs, outputs, scratch, remote, local, sizes, vmem, flops):
    n_in, n_out, n_scratch = len(inputs), len(outputs), len(scratch)

    def body(*refs):
        ins, outs = refs[:n_in], refs[n_in : n_in + n_out]
        work = refs[n_in + n_out :]
        mover = Mover(sizes, *work[n_scratch:])
        kernel(mover, ins, outs, work[:n_scratch])

    return pl.pallas_call(
        body,
        in_specs=[pl.BlockSpec(memory_space=space) for _, space in inputs],
        out_specs=[pl.BlockSpec(memory_space=space) for _, _, space in outputs],
        out_shape=[jax.ShapeDtypeStruct(shape, dtype) for shape, dtype, _ in outputs],
        scratch_shapes=list(scratch)
        + [
            pltpu.SemaphoreType.DMA((remote,)),
            pltpu.SemaphoreType.DMA((remote,)),
            pltpu.SemaphoreType.DMA((local,)),
        ],
        compiler_params=pltpu.CompilerParams(
            collective_id=ident, has_side_effects=True, vmem_limit_bytes=vmem * 2**20
        ),
        cost_estimate=pl.CostEstimate(flops=flops, bytes_accessed=2**24, transcendentals=0),
        name=name,
    )(*[value for value, _ in inputs])


def order_of(block, count):
    return (block + count - 1) % count


def tiles_of(count, capacity, tile):
    ends = [-(-(p + 1) * capacity // tile) for p in range(count)]
    return list(zip([0] + ends[:-1], ends))


def parts_of(capacity):
    middle = capacity // 2 // PAD * PAD
    return [(0, middle), (middle, capacity)] if middle else [(0, capacity)]


def tile_at(t, tile):
    return pl.ds(pl.multiple_of(t * tile, tile), tile)


def turned_product(left, right, bias, target):
    def step(i, carry):
        at = pl.ds(pl.multiple_of(i * PAD, PAD), PAD)
        value = jnp.dot(left[at, :], right[...], preferred_element_type=FULL)
        if bias is not None:
            value = value + bias[0:1, :]
        target[:, at] = turned(value.astype(LOW))
        return carry

    lax.fori_loop(0, left.shape[0] // PAD, step, 0)


def head_rows(ref, head, width):
    return ref.at[pl.ds(pl.multiple_of(head * width, 16), width)]


def attend_part(size, tile, mover, joint, bias, heads, qkv, o_ref, lse, work, after_send, begun, between):
    k_ref, q_ref, v_ref, low_ref, score_ref, top_ref = work
    count, width, capacity = qkv.shape
    slots = count * capacity
    sent = [None] + [
        mover.go(head_rows(joint, mover.on(by), width), qkv.at[by], ctx=mover.on(by))
        for by in range(1, count)
    ]
    after_send()
    qkv[0] = head_rows(joint, mover.ctx, width)[...]
    q_ref[size:PAD, :] = jnp.concatenate(
        [jnp.ones((16, slots), LOW), jnp.zeros((PAD - size - 16, slots), LOW)], axis=0
    )

    def prepare(r):
        here = slice(r * capacity, (r + 1) * capacity)
        p = order_of(r, count)
        q_ref[0:size, p * capacity : (p + 1) * capacity] = (
            qkv[r, 0:size, :] * (size**-0.5)
        ).astype(LOW)
        v_ref[:, here] = qkv[r, 2 * size : 3 * size, :]
        keys = jnp.concatenate(
            [qkv[r, size : 2 * size, :], bias[:, here], jnp.zeros((PAD - size - 16, capacity), LOW)],
            axis=0,
        )
        k_ref[here, :] = turned(keys)

    prepare(0)
    for by in range(1, count):
        mover.take(sent[by])
        prepare(by)

    begun()
    last = slots // tile - 1
    assert last % 2 == 1

    def phase(t, now, following, then):
        at, ahead = tile_at(t, tile), tile_at(following, tile)
        top = top_ref[now, 0:1, :]
        total = jnp.zeros((1, tile), FULL)
        summed = jnp.zeros((size, tile), FULL)
        new_top = jnp.full((1, tile), NEG_LARGE, FULL)
        for r in range(count):
            here = slice(r * capacity, (r + 1) * capacity)
            scores = jnp.dot(k_ref[here, :], q_ref[:, ahead], preferred_element_type=FULL)
            score_ref[then, here, :] = scores
            new_top = jnp.maximum(new_top, jnp.max(scores, axis=0, keepdims=True))
            weights = jnp.exp(score_ref[now, here, :] - top)
            total = total + jnp.sum(weights, axis=0, keepdims=True)
            summed = summed + jnp.dot(
                v_ref[:, here], weights.astype(LOW), preferred_element_type=FULL
            )
        top_ref[then] = jnp.broadcast_to(new_top, (8, tile))
        out = summed / total
        o_ref[:, at] = out
        low_ref[:, at] = out.astype(LOW)
        lse[:, at] = jnp.broadcast_to(top + jnp.log(total), (8, tile))

    def step(i, carry):
        phase(2 * i, 0, 2 * i + 1, 1)
        phase(2 * i + 1, 1, jnp.minimum(2 * i + 2, last), 0)
        return carry

    scores = jnp.dot(k_ref[...], q_ref[:, 0:tile], preferred_element_type=FULL)
    score_ref[0] = scores
    top_ref[0] = jnp.broadcast_to(jnp.max(scores, axis=0, keepdims=True), (8, tile))
    arriving = []
    for p, (low, high) in enumerate(tiles_of(count, capacity, 2 * tile)):
        lax.fori_loop(low, high, step, 0)
        done = low_ref.at[:, p * capacity : (p + 1) * capacity]
        if p < count - 1:
            there = head_rows(heads, mover.ctx, size)
            arriving.append(mover.go(done, there, ctx=mover.back(p + 1)))
        else:
            head_rows(heads, mover.ctx, size)[...] = low_ref[:, p * capacity : (p + 1) * capacity]
        between(p + 1)
    for copy in arriving:
        mover.take(copy)


def attend_back_part(size, tile, mover, parts, bias, qkv, o_ref, lse, grads, work, ready, waiting, begun, between):
    k_ref, v_ref, q_ref, do_ref, nat_ref, delta_ref, dq_ref, dk_ref, dv_ref, got, back, score_ref, grad_ref = work
    count, width, capacity = qkv.shape
    slots = count * capacity
    sent = [None] + [
        mover.go(head_rows(parts, mover.on(by), size), got.at[by], ctx=mover.on(by))
        for by in range(1, count)
    ]
    got[0] = head_rows(parts, mover.ctx, size)[...]
    waiting()
    ready()
    q_ref[size:PAD, :] = jnp.concatenate(
        [jnp.ones((16, slots), LOW), jnp.zeros((PAD - size - 16, slots), LOW)], axis=0
    )
    do_ref[size:PAD, :] = jnp.zeros((PAD - size, slots), LOW)
    dq_ref[...] = jnp.zeros_like(dq_ref)
    for r in range(count):
        here = slice(r * capacity, (r + 1) * capacity)
        pad = jnp.zeros((PAD - size - 16, capacity), LOW)
        k_ref[here, :] = turned(
            jnp.concatenate([qkv[r, size : 2 * size, :], bias[:, here], pad], axis=0)
        )
        v_ref[here, :] = turned(
            jnp.concatenate(
                [qkv[r, 2 * size : 3 * size, :], jnp.zeros((PAD - size, capacity), LOW)], axis=0
            )
        )
    for r in range(count):
        if r:
            mover.take(sent[r])
        p = order_of(r, count)
        at = slice(p * capacity, (p + 1) * capacity)
        scaled = (qkv[r, 0:size, :] * (size**-0.5)).astype(LOW)
        dout = got[r]
        q_ref[0:size, at] = scaled
        do_ref[0:size, at] = dout
        nat_ref[at, :] = turned(jnp.concatenate([scaled, dout], axis=0))
        delta = jnp.sum(dout.astype(FULL) * o_ref[:, at], axis=0, keepdims=True)
        delta_ref[:, at] = jnp.broadcast_to(delta, (8, capacity))

    begun()
    last = slots // tile - 1
    assert last % 2 == 1
    tiles = tiles_of(count, capacity, 2 * tile)
    arriving = []
    mine = head_rows(grads, mover.ctx, width)
    for turn, r in enumerate(list(range(1, count)) + [0]):
        here = slice(r * capacity, (r + 1) * capacity)
        dk_ref[...] = jnp.zeros_like(dk_ref)
        dv_ref[...] = jnp.zeros_like(dv_ref)

        def ready_scores(t, then, low, high, r=r):
            ahead = tile_at(t, tile)
            rows = slice(r * capacity + low, r * capacity + high)
            score_ref[then, low:high, :] = jnp.dot(
                k_ref[rows, :], q_ref[:, ahead], preferred_element_type=FULL
            )
            grad_ref[then, low:high, :] = jnp.dot(
                v_ref[rows, :], do_ref[:, ahead], preferred_element_type=FULL
            )

        def phase(t, now, following, then, r=r):
            at = tile_at(t, tile)
            query_grad = jnp.zeros((size, tile), FULL)
            for low, high in parts_of(capacity):
                ready_scores(following, then, low, high)
                chance = jnp.exp(score_ref[now, low:high, :] - lse[0:1, at])
                score_grad = (
                    chance * (grad_ref[now, low:high, :] - delta_ref[0:1, at])
                ).astype(LOW)
                query_grad = query_grad + jnp.dot(
                    qkv[r, size : 2 * size, low:high], score_grad, preferred_element_type=FULL
                )
                dk_ref[low:high, :] += jnp.dot(
                    score_grad, nat_ref[at, :], preferred_element_type=FULL
                )
                dv_ref[low:high, :] += jnp.dot(
                    chance.astype(LOW), nat_ref[at, :], preferred_element_type=FULL
                )
            dq_ref[:, at] += query_grad

        def step(i, carry, phase=phase):
            phase(2 * i, 0, 2 * i + 1, 1)
            phase(2 * i + 1, 1, jnp.minimum(2 * i + 2, last), 0)
            return carry

        ready_scores(0, 0, 0, capacity)
        if r:
            lax.fori_loop(0, tiles[-1][1], step, 0)
        else:
            for p, (low, high) in enumerate(tiles):
                lax.fori_loop(low, high, step, 0)
                at = slice(p * capacity, (p + 1) * capacity)
                value = (dq_ref[:, at] * (size**-0.5)).astype(LOW)
                if p < count - 1:
                    back[p + 1, 0:size, :] = value
                    arriving.append(
                        mover.go(
                            back.at[p + 1, 0:size], mine.at[0:size], ctx=mover.back(p + 1)
                        )
                    )
                else:
                    mine[0:size, :] = value
        keys = dk_ref[...].T[0:size].astype(LOW)
        values = dv_ref[...].T[size : 2 * size].astype(LOW)
        if r:
            back[r, size : 2 * size, :] = keys
            back[r, 2 * size : 3 * size, :] = values
            arriving.append(
                mover.go(
                    back.at[r, size : 3 * size], mine.at[size : 3 * size], ctx=mover.back(r)
                )
            )
        else:
            mine[size : 2 * size, :] = keys
            mine[2 * size : 3 * size, :] = values
        between(turn)
    for copy in arriving:
        mover.take(copy)


def attend_back_buffers(size, count, capacity, tile):
    slots = count * capacity
    return [
        VMEM((slots, PAD), LOW),
        VMEM((slots, PAD), LOW),
        VMEM((PAD, slots), LOW),
        VMEM((PAD, slots), LOW),
        VMEM((slots, PAD), LOW),
        VMEM((8, slots), FULL),
        VMEM((size, slots), FULL),
        VMEM((capacity, PAD), FULL),
        VMEM((capacity, PAD), FULL),
        VMEM((count, size, capacity), LOW),
        VMEM((count, 3 * size, capacity), LOW),
        VMEM((2, capacity, tile), FULL),
        VMEM((2, capacity, tile), FULL),
    ]


class Round:
    def __init__(self, mover, rows, full, buffers):
        place = lax.axis_index("tp")
        core, far = lax.rem(place, 2), place // 2
        self.mover, self.full = mover, full
        self.give, self.ra, self.passing, self.rb, self.keep = buffers
        self.span = rows // 4
        self.half = self.span // 2
        self.mate, self.far = tp_peers()

        def quarter(c, f):
            return (c * 2 + f) * self.span

        self.own, self.other = quarter(core, far), quarter(core, 1 - far)
        self.mate_own, self.mate_other = quarter(1 - core, far), quarter(1 - core, 1 - far)

    def rows(self, start, count=None):
        return pl.ds(pl.multiple_of(start, 16), count or self.span)

    def hand(self, slot, value):
        self.give[slot] = value.astype(LOW)
        return self.mover.go(self.give.at[slot], self.ra.at[slot], tp=self.mate)

    def onward(self, value, index):
        self.mover.take(index)
        self.passing[...] = (value + self.ra[1].astype(FULL)).astype(LOW)
        return [
            self.mover.go(self.passing.at[at], self.rb.at[at], tp=self.far)
            for at in (pl.ds(0, self.half), pl.ds(self.half, self.half))
        ]

    def close(self, far_copies, index, finish, halfway=None):
        self.mover.take(index)
        self.keep[...] += self.ra[0].astype(FULL)
        self.to_far, self.to_mate = [], []
        for c in range(2):
            at = pl.ds(c * self.half, self.half)
            self.mover.take(far_copies[c])
            low = finish(at, self.keep[at] + self.rb[at].astype(FULL))
            mine = self.full.at[self.rows(self.own + c * self.half, self.half)]
            mine[...] = low
            self.to_far.append(self.mover.go(mine, mine, tp=self.far))
            self.to_mate.append(self.mover.go(mine, mine, tp=self.mate))
            if halfway and c == 0:
                halfway()

    def eager(self, make, finish, meanwhile=None, halfway=None):
        first = self.hand(1, make(self.mate_other))
        copies = self.onward(make(self.other), first)
        second = self.hand(0, make(self.mate_own))
        self.keep[...] = make(self.own)
        if meanwhile:
            meanwhile()
        self.close(copies, second, finish, halfway)

    def after(self, before, make, finish, meanwhile=None):
        before.have_mate_own()
        second = self.hand(0, make(self.mate_own))
        self.keep[...] = make(self.own)
        before.have_other()
        value = make(self.other)
        before.have_mate_other()
        first = self.hand(1, make(self.mate_other))
        copies = self.onward(value, first)
        if meanwhile:
            meanwhile()
        self.close(copies, second, finish)

    def have_mate_own(self):
        for copy in self.to_mate:
            self.mover.take(copy)

    def have_other(self):
        self.passed = []
        for c in range(2):
            self.mover.take(self.to_far[c])
            rows = self.full.at[self.rows(self.other + c * self.half, self.half)]
            self.passed.append(self.mover.go(rows, rows, tp=self.mate))

    def have_mate_other(self):
        for copy in self.passed:
            self.mover.take(copy)

    def have(self):
        self.have_mate_own()
        self.have_other()
        self.have_mate_other()


ROUND_COPIES = 10


def round_buffers(rows, width):
    span = rows // 4
    return [
        VMEM((2, span, width), LOW),
        VMEM((2, span, width), LOW),
        VMEM((span, width), LOW),
        VMEM((span, width), LOW),
        VMEM((span, width), FULL),
    ]


NAMES = ("qkv", "out", "up", "down")


def layer_kernel(plan, last, size, tile, mover, ins, outs, work):
    ins, outs, work = iter(ins), iter(outs), iter(work)
    source = next(ins)
    x_ref = None if plan.entry else next(ins)
    live_ref = next(ins)
    far_params = [next(ins) for _ in range(8)]
    stream, following = next(outs), next(outs)
    far_qkv, far_o, far_lse, far_heads, far_middle, far_second, far_hidden, far_slope = [
        next(outs) for _ in range(8)
    ]
    far_first = next(outs) if plan.entry else None
    joint, nat, heads, qkv, o_ref, lse, middle, second, hidden, slope = [
        next(work) for _ in range(10)
    ]
    first = next(work) if plan.entry else source
    attend_work = [next(work) for _ in range(6)]
    one_work, two_work = [next(work) for _ in range(5)], [next(work) for _ in range(5)]
    rows = source.shape[0]
    bias, qkv_bias = next(work), next(work)
    params = [next(work) for _ in range(8)]
    whole = {name: next(work) for name in NAMES}
    gathers, loads = {}, {}
    for name in plan.held:
        loads[name] = (next(ins), whole[name])
    for name in plan.own:
        gathers[name, 0] = Gather(mover, next(ins).at[plan.layer], whole[name])
    for name in plan.ahead:
        gathers[name, 1] = Gather(mover, next(ins).at[plan.layer + 1], next(outs))
    kept = {name: next(outs) for name in plan.own}

    greet(mover, bool(gathers))
    if plan.entry:
        gathers_first = [key for key in [("qkv", 0)] if key in gathers]
        for key in gathers_first:
            gathers[key].start()
    param_loads = [mover.stay(there, here) for there, here in zip(far_params, params)]
    loads = {name: mover.stay(*pair) for name, pair in loads.items()}

    def have(name):
        if name in loads:
            mover.near(loads[name])
        else:
            gathers[name, 0].have()
            mover.stay(whole[name], kept[name])
        return whole[name]

    def begin(keys):
        for key in keys:
            if key in gathers:
                gathers[key].start()

    def pass_on(keys, stage):
        for key in keys:
            if key in gathers:
                gathers[key].pass_on(stage)

    def pass_all(keys):
        for stage in (1, 2, 3):
            pass_on(keys, stage)

    mover.near(*param_loads)
    layer, after = plan.layer, min(plan.layer + 1, params[0].shape[0] - 1)

    def row(index, layer=layer):
        return params[index][...].astype(FULL)[layer : layer + 1]

    b_out, gain2, shift2, b_down, b_up = row(0), row(1), row(2), row(3), row(6)
    gain1, shift1, gain0, shift0 = row(4, after), row(5, after), row(4), row(5)
    qkv_bias[...] = joint_bias(row(7), size, joint.shape[0])
    key_bias(mover, live_ref, bias)
    one = Round(mover, rows, second, one_work)
    two = Round(mover, rows, following, two_work)
    if plan.entry:
        chunk = rows // 5 if rows % 80 == 0 else rows

        def norm_step(i, carry):
            at = pl.ds(pl.multiple_of(i * chunk, 16), chunk)
            value = normalize(source[at, :].astype(FULL), gain0, shift0)[0]
            first[at, :] = value.astype(LOW)
            return carry

        lax.fori_loop(0, rows // chunk, norm_step, 0)
        mover.stay(first, far_first)
        pass_all([("qkv", 0)])
        begin([("out", 0), ("up", 0)])
        turned_product(first, have("qkv"), qkv_bias, joint)
    else:
        turned_product(first, have("qkv"), qkv_bias, joint)

    ahead = [("qkv", 1), ("out", 1)]

    def after_send():
        if plan.entry:
            pass_all([("out", 0), ("up", 0)])
        else:
            for name in plan.own:
                gathers[name, 0].start_over()

    def begun():
        if plan.entry:
            begin([("down", 0)])
        else:
            for name in plan.own:
                gathers[name, 0].start_line()

    def between(p):
        if p > 1:
            pass_on([("down", 0)] + ([] if plan.entry else [("up", 0)]), p - 1)
        if p == 4:
            begin(ahead)

    attend_part(
        size, tile, mover, joint, bias, heads, qkv, o_ref, lse, attend_work, after_send, begun, between
    )
    nat[...] = turned(heads[...])
    w_out = have("out")

    def out_part(start):
        return dot(nat[one.rows(start), :], w_out[...], ((1,), (1,)))

    def to_second(at, value):
        if plan.entry:
            before = source[one.rows(one.own + at.start, at.size), :].astype(FULL)
        else:
            before = x_ref[at]
        value = before + value + b_out
        middle[at] = value
        return normalize(value, gain2, shift2)[0].astype(LOW)

    def meanwhile():
        mover.stay(qkv, far_qkv)
        mover.stay(o_ref, far_o)
        mover.stay(lse, far_lse)
        mover.stay(nat, far_heads)

    one.eager(out_part, to_second, meanwhile, lambda: pass_on(ahead, 1))
    pass_on(ahead, 2)
    pass_on(ahead, 3)
    w_up, w_down = have("up"), have("down")

    def mlp_part(start):
        at = two.rows(start)
        pre = jnp.dot(second[at, :], w_up[...], preferred_element_type=FULL) + b_up
        low, low_slope = gelu_pair(pre)
        hidden[at, :] = low
        slope[at, :] = low_slope
        return dot(low, w_down[...], ((1,), (1,)))

    def to_following(at, value):
        value = middle[at] + value + b_down
        stream[at] = value
        if last:
            return live_rows(value, two.own + at.start, live_ref[0, mover.ctx]).astype(LOW)
        return normalize(value, gain1, shift1)[0].astype(LOW)

    def meanwhile():
        mover.stay(middle, far_middle)
        mover.stay(second, far_second)
        mover.stay(hidden, far_hidden)
        mover.stay(slope, far_slope)

    two.after(one, mlp_part, to_following, meanwhile)
    two.have()
    mover.settle()


class Plan:
    def __init__(self, layer, last, inside):
        self.layer, self.entry = layer, layer == 0
        self.own = (NAMES if layer == 0 else ("up", "down")) if inside else ()
        self.ahead = ("qkv", "out") if inside and not last else ()
        self.held = tuple(name for name in NAMES if name not in self.own)


def forward_layer(source, x, live, params, gathered, weights, plan, last, size, sizes, ident):
    rows, width = source.shape
    count = sizes[0]
    joint, hidden = weights["qkv"].shape[2], weights["up"].shape[2]
    heads = joint // (3 * size)
    attn, slots, span = heads * size, count * rows, rows // 4
    tile = 256 if slots % 256 == 0 else PAD
    columns = {"qkv": joint, "out": attn, "up": hidden, "down": hidden}
    inputs = [(source, VMEM)] + ([] if plan.entry else [(x, VMEM)])
    inputs += [(live, SMEM)] + [(value, HBM) for value in params]
    inputs += [(gathered[name, plan.layer], HBM) for name in plan.held]
    inputs += [(weights[name], HBM) for name in plan.own + plan.ahead]
    saved = [
        ((count, 3 * size, rows), LOW),
        ((size, slots), FULL),
        ((8, slots), FULL),
        ((rows, attn), LOW),
        ((span, width), FULL),
        ((rows, width), LOW),
        ((rows, hidden), LOW),
        ((rows, hidden), LOW),
    ]
    outputs = [((span, width), FULL, VMEM), ((rows, width), LOW, VMEM)]
    outputs += [(shape, dtype, HBM) for shape, dtype in saved]
    if plan.entry:
        outputs.append(((rows, width), LOW, HBM))
    outputs += [((width, columns[name]), LOW, HBM) for name in plan.ahead + plan.own]
    qkv_shape, o_shape, lse_shape, heads_shape = saved[:4]
    scratch = [VMEM((joint, rows), LOW), VMEM((rows, attn), LOW), VMEM((attn, rows), LOW)]
    scratch += [VMEM(*pair) for pair in saved[:3] + saved[4:]]
    if plan.entry:
        scratch.append(VMEM((rows, width), LOW))
    scratch += [
        VMEM((slots, PAD), LOW),
        VMEM((PAD, slots), LOW),
        VMEM((size, slots), LOW),
        VMEM((size, slots), LOW),
        VMEM((2, slots, tile), FULL),
        VMEM((2, 8, tile), FULL),
    ]
    scratch += round_buffers(rows, width) + round_buffers(rows, width)
    scratch += [VMEM((16, slots), LOW), VMEM((16, joint), FULL)]
    scratch += [VMEM(value.shape, value.dtype) for value in params]
    scratch += [VMEM((width, columns[name]), LOW) for name in NAMES]
    results = run(
        functools.partial(layer_kernel, plan, last, size, tile),
        "forward_layer",
        ident,
        inputs,
        outputs,
        scratch,
        2 * (count - 1) + 2 * ROUND_COPIES + 2 * count * len(plan.own + plan.ahead),
        9 + 2 * len(NAMES) + 2 + len(params),
        sizes,
        58,
        2 * rows * width * (2 * hidden + attn + joint) + 4 * slots * slots * 256,
    )
    stream, following = results[:2]
    kept = results[2 : 11 if plan.entry else 10]
    for name, value in zip(plan.ahead, results[2 + len(kept) :]):
        gathered[name, plan.layer + 1] = value
    for name, value in zip(plan.own, results[2 + len(kept) + len(plan.ahead) :]):
        gathered[name, plan.layer] = value
    return stream, following, kept


def key_bias(mover, live_ref, bias):
    capacity = bias.shape[1] // mover.ctx_count
    row = lax.broadcasted_iota(jnp.int32, (16, capacity), 0)
    slot = lax.broadcasted_iota(jnp.int32, (16, capacity), 1)
    for r in range(mover.ctx_count):
        live = live_ref[0, mover.back(r)]
        value = jnp.where((row == 0) & (slot >= live), NEG_LARGE, 0.0)
        bias[:, r * capacity : (r + 1) * capacity] = value.astype(LOW)


def pair_columns(rows, width, size, turn):
    shape = (width, rows) if turn else (rows, width)
    given = lax.broadcasted_iota(jnp.int32, shape, 1 if turn else 0)
    column = lax.broadcasted_iota(jnp.int32, shape, 0 if turn else 1)
    head, within = column // (3 * size), column % (3 * size)
    wanted = head * (2 * size) + jnp.where(within < size, within, within - size)
    key = (within >= size) & (within < 2 * size)
    return jnp.where((given == wanted) & ~key, 1.0, 0.0).astype(LOW)


def joint_bias(pair, size, width):
    rows = pair.shape[1]
    spread = jnp.broadcast_to(pair, (16, rows)).astype(LOW)
    return jnp.dot(spread, pair_columns(rows, width, size, False), preferred_element_type=FULL)


def live_rows(value, start, live):
    row = start + lax.broadcasted_iota(jnp.int32, value.shape, 0)
    return jnp.where(row < live, value, 0.0)


def sums_into(sums, first, at, values):
    for index, value in enumerate(values):
        row = first + index
        added = jnp.sum(value, axis=0, keepdims=True)
        width = added.shape[1]
        sums[row : row + 1, 0:width] = (
            added if at.start == 0 else sums[row : row + 1, 0:width] + added
        )


def back_kernel(plan, size, tile, mover, ins, outs, work):
    ins, outs, work = iter(ins), iter(outs), iter(work)
    source = next(ins)
    x_ref = None if plan.last else next(ins)
    live_ref, far_gain2, far_gain1 = [next(ins) for _ in range(3)]
    far = [next(ins) for _ in range(14)]
    late_far = next(ins) if plan.late else None
    others = [(next(ins), next(ins)) for _ in range(plan.others)]
    stream, following = next(outs), next(outs)
    grad_outs = {name: next(outs) for name in NAMES if plan.inside and (name != "qkv" or plan.final)}
    mid_out = next(outs) if plan.inside and not plan.final else None
    late_out = next(outs) if plan.late else None
    split = local = totals = None
    if plan.joined:
        totals = next(outs)
    else:
        split, local = next(outs), next(outs)
    wholes = {} if plan.inside else {name: next(outs) for name in NAMES}
    near = [next(work) for _ in range(14)]
    slope, w_down, w_up, middle, hidden, second, w_out, heads, qkv, o_ref, lse, first, w_qkv, before = near
    grad = next(work) if plan.last else source
    pre_grad, attn_grad, parts, grads, nat = [next(work) for _ in range(5)]
    attend_work = [next(work) for _ in range(13)]
    one_work, two_work = [next(work) for _ in range(5)], [next(work) for _ in range(5)]
    rows, width = source.shape
    reduces = {}
    if plan.inside:
        pairs = {
            "down": (grad, hidden),
            "up": (second, pre_grad),
            "out": (attn_grad, heads),
            "qkv": (first, nat),
        }
        for name in ("down", "up", "out", "qkv"):
            buffers = [next(work) for _ in range(4)]
            reduces[name] = Reduce(mover, buffers, grad_outs.get(name), *pairs[name])
    late = None
    if plan.late:
        late_mid, late_line = next(work), next(work)
        late = Reduce(mover, (late_mid, None, late_mid, late_line), late_out, None, None)
    bias, gain2_ref, gain1_ref = [next(work) for _ in range(3)]
    if plan.joined:
        split, local = next(work), next(work)
        got_tp, got_shard, got_ctx, mine = [next(work) for _ in range(4)]

    greet(mover, plan.inside)
    gain_loads = [mover.stay(far_gain2, gain2_ref), mover.stay(far_gain1, gain1_ref)]
    one = Round(mover, rows, attn_grad, one_work)
    two = Round(mover, rows, following, two_work)
    if plan.final:
        far[13] = far[13].at[two.rows(two.own)]
    load = [mover.stay(there, here) for there, here in zip(far, near)]
    if late:
        mover.near(mover.stay(late_far, late_mid))
        late.spread()
    if plan.last:
        chunk = rows // 5 if rows % 80 == 0 else rows

        def mask_step(i, carry):
            at = pl.ds(pl.multiple_of(i * chunk, 16), chunk)
            value = source[at, :].astype(FULL)
            grad[at, :] = live_rows(value, i * chunk, live_ref[0, mover.ctx]).astype(LOW)
            return carry

        lax.fori_loop(0, rows // chunk, mask_step, 0)
    key_bias(mover, live_ref, bias)
    mover.near(*gain_loads)
    gain2, gain1 = [
        ref[...].astype(FULL)[plan.layer : plan.layer + 1] for ref in (gain2_ref, gain1_ref)
    ]
    split[...] = jnp.zeros_like(split)
    local[...] = jnp.zeros_like(local)
    split[5:6, 0:width] = jnp.sum(
        grad[one.rows(one.own), :].astype(FULL), axis=0, keepdims=True
    )
    mover.near(*load[:3])
    hidden_width = slope.shape[1]

    def mlp_part(start):
        at = one.rows(start)
        pre = jnp.dot(grad[at, :], w_down[...], preferred_element_type=FULL)
        low = (pre * slope[at, :].astype(FULL)).astype(LOW)
        pre_grad[at, :] = low
        local[0:1, 0:hidden_width] += jnp.sum(low.astype(FULL), axis=0, keepdims=True)
        return dot(low, w_up[...], ((1,), (1,)))

    def to_attn(at, value):
        if plan.last:
            above = grad[one.rows(one.own + at.start, at.size), :].astype(FULL)
        else:
            above = x_ref[at]
        _, normed, inverse = normalize(middle[at], 1.0, 0.0)
        result = above + normalize_back(value, normed, inverse, gain2)
        stream[at] = result
        low = result.astype(LOW)
        sums_into(split, 2, at, (value * normed, value, low.astype(FULL)))
        return low

    def reduce(name):
        if name in reduces:
            reduces[name].begin()

    def fold(name):
        if name in reduces:
            reduces[name].fold()
            reduces[name].spread()

    def finish(name):
        if name in reduces:
            reduces[name].finish()

    def start_down():
        mover.near(load[3], load[4])
        reduce("down")

    one.eager(mlp_part, to_attn, start_down)
    mover.near(load[5])
    reduce("up")
    one.have()
    mover.near(load[6])
    turned_product(attn_grad, w_out, None, parts)

    def waiting():
        mover.near(load[7])
        reduce("out")

    def ready():
        mover.near(load[8], load[9], load[10])
        if late:
            late.finish()

    def between(turn):
        if turn == 0:
            finish("down")
        if turn == 3:
            fold("up")
            fold("out")

    attend_back_part(
        size,
        tile,
        mover,
        parts,
        bias,
        qkv,
        o_ref,
        lse,
        grads,
        attend_work,
        ready,
        waiting,
        lambda: fold("down"),
        between,
    )
    nat[...] = turned(grads[...])
    pairs_width = nat.shape[1] // 3 * 2
    picked = jnp.dot(
        nat[...], pair_columns(pairs_width, nat.shape[1], size, True), preferred_element_type=FULL
    )
    local[1:2, 0:pairs_width] = jnp.sum(picked, axis=0, keepdims=True)
    mover.near(*load[11:])

    def qkv_part(start):
        return dot(nat[two.rows(start), :], w_qkv[...], ((1,), (1,)))

    def to_following(at, value):
        row = before[at, :].astype(FULL)
        _, normed, inverse = normalize(row, 1.0, 0.0)
        result = stream[at] + normalize_back(value, normed, inverse, gain1)
        stream[at] = result
        low = result.astype(LOW)
        sums_into(split, 0, at, (value * normed, value))
        return low

    def meanwhile():
        if plan.inside:
            last = reduces["qkv"]
            last.compute(last.mid, mover.shard)
        finish("up")
        finish("out")

    def halfway():
        if plan.inside:
            reduces["qkv"].fold_blocks(3, 1)
            if plan.final:
                reduces["qkv"].spread()

    if plan.inside:
        reduces["qkv"].begin_blocks()
    two.eager(qkv_part, to_following, meanwhile, halfway)
    if plan.joined:
        place = lax.axis_index("tp")
        ways = got_tp.shape[0]
        count = plan.others + 1
        for layer, pair in enumerate([(split, local)] + others):
            for index, value in enumerate(pair):
                for row in range(8):
                    mine[index, row * count + layer : row * count + layer + 1] = value[
                        row : row + 1, :
                    ]
        got_tp[place] = mine[0]
        tp_copies = [
            mover.go(mine.at[0], got_tp.at[place], tp=lax.rem(place + by, ways))
            for by in range(1, ways)
        ]
    if plan.inside:
        reduces["qkv"].fold_blocks(2, 0)
        if plan.final:
            reduces["qkv"].finish()
        else:
            mover.stay(reduces["qkv"].mid, mid_out)
    two.have()
    if plan.joined:
        for copy in tp_copies:
            mover.take(copy)
        value = got_tp[0]
        for other in range(1, ways):
            value = value + got_tp[other]
        mine[2] = value
        cross = mover.go(mine.at[pl.ds(1, 2)], got_shard, shard=1 - mover.shard)
        mover.take(cross)
        got_ctx[mover.ctx] = mine[1:3] + got_shard[...]
        there = got_ctx.at[mover.ctx]
        lines = [mover.go(there, there, ctx=mover.on(by)) for by in range(1, mover.ctx_count)]
        for copy in lines:
            mover.take(copy)
        value = got_ctx[0]
        for other in range(1, mover.ctx_count):
            value = value + got_ctx[other]
        totals[...] = value
    for name in ("down", "up", "out"):
        if name in reduces:
            reduces[name].done()
    if late:
        late.done()
    if plan.inside and plan.final:
        reduces["qkv"].done()
    if not plan.inside:
        for name, (lhs, rhs) in {
            "down": (grad, hidden),
            "up": (second, pre_grad),
            "out": (attn_grad, heads),
            "qkv": (first, nat),
        }.items():
            full = Reduce(mover, (wholes[name],) * 4, None, lhs, rhs)
            full.compute(wholes[name], 0)
    mover.settle()


def gather_outputs_kernel(layers, *refs):
    count = layers * len(NAMES)
    parts, token_grads, mixed, totals = refs[:count], refs[count], refs[count + 1], refs[count + 2]
    outs = refs[count + 3 : -1]
    sems = refs[-1]
    copies = []
    for index in range(len(NAMES)):
        for layer in range(layers):
            copies.append((parts[index * layers + layer], outs[index].at[layer]))
    copies.append((mixed, outs[4].at[0]))
    copies = [pltpu.make_async_copy(*pair, sems.at[i]) for i, pair in enumerate(copies)]
    for copy in copies:
        copy.start()
    outs[5][0] = token_grads[...].astype(FULL)
    for row, out in enumerate(outs[6:12]):
        out[...] = totals[1, row * layers : (row + 1) * layers, 0 : out.shape[1]]
    for row, out in enumerate(outs[12:14]):
        out[...] = totals[0, row * layers : (row + 1) * layers, 0 : out.shape[1]]
    for copy in copies:
        copy.wait()


def gather_outputs(done, token_grads, mixed, totals, layers, widths):
    rows, width = token_grads.shape
    parts = [done[name, layer] for name in NAMES for layer in range(layers)]
    hbm, whole = pl.BlockSpec(memory_space=HBM), lambda shape: pl.BlockSpec(
        shape, lambda i: (0,) * len(shape)
    )
    shapes = [(layers,) + done[name, 0].shape for name in NAMES] + [(1, rows, width)] * 2
    types = [FULL] * 4 + [LOW, FULL]
    small = [(layers, width)] * 6 + [(layers, count) for count in widths]
    return pl.pallas_call(
        functools.partial(gather_outputs_kernel, layers),
        grid=(1,),
        in_specs=[hbm] * len(parts) + [whole(token_grads.shape), hbm, whole(totals.shape)],
        out_specs=[hbm] * 5 + [whole(shape) for shape in shapes[5:] + small],
        out_shape=[jax.ShapeDtypeStruct(*pair) for pair in zip(shapes, types)]
        + [jax.ShapeDtypeStruct(shape, FULL) for shape in small],
        scratch_shapes=[pltpu.SemaphoreType.DMA((len(parts) + 1,))],
        compiler_params=pltpu.CompilerParams(vmem_limit_bytes=60 * 2**20),
        name="gather_outputs",
    )(*parts, token_grads, mixed, totals)


class BackPlan:
    def __init__(self, layer, layers, inside):
        self.inside, self.layer = inside, layer
        self.last, self.final = layer == layers - 1, layer == 0
        self.late = inside and not self.last
        self.joined = inside and self.final
        self.others = layers - 1 if self.joined else 0


def back_layer(source, x, live, gain2, gain1, saved, late, others, plan, size, sizes, ident):
    rows, width = source.shape
    count = sizes[0]
    slope, w_down, w_up = saved[:3]
    hidden, joint, attn = slope.shape[1], saved[12].shape[1], saved[6].shape[1]
    slots, span = count * rows, rows // 4
    tile = 256 if slots % 256 == 0 else PAD
    wide = max(width, hidden, joint)
    half = width // 2
    block = half // count
    columns = {"qkv": joint, "out": attn, "up": hidden, "down": hidden}
    inputs = [(source, VMEM)] + ([] if plan.last else [(x, VMEM)])
    inputs += [(live, SMEM), (gain2, HBM), (gain1, HBM)]
    inputs += [(value, HBM) for value in saved]
    if plan.late:
        inputs.append((late, HBM))
    for pair in others[: plan.others]:
        inputs += [(value, VMEM) for value in pair]
    outputs = [((span, width), FULL, VMEM), ((rows, width), LOW, VMEM)]
    names = [name for name in NAMES if plan.inside and (name != "qkv" or plan.final)]
    outputs += [((block, columns[name]), FULL, VMEM) for name in names]
    if plan.inside and not plan.final:
        outputs.append(((half, joint), LOW, HBM))
    if plan.late:
        outputs.append(((block, joint), FULL, VMEM))
    depth = 8 * (plan.others + 1)
    if plan.joined:
        outputs.append(((2, depth, wide), FULL, VMEM))
    else:
        outputs += [((8, wide), FULL, VMEM)] * 2
    if not plan.inside:
        outputs += [((width, columns[name]), LOW, VMEM) for name in NAMES]
    scratch = [VMEM(value.shape, value.dtype) for value in saved]
    scratch[13] = VMEM((span, width), saved[13].dtype)
    if plan.last:
        scratch.append(VMEM((rows, width), LOW))
    scratch += [
        VMEM((rows, hidden), LOW),
        VMEM((rows, width), LOW),
        VMEM((attn, rows), LOW),
        VMEM((joint, rows), LOW),
        VMEM((rows, joint), LOW),
    ]
    scratch += attend_back_buffers(size, count, rows, tile)
    scratch += round_buffers(rows, width) + round_buffers(rows, width)
    if plan.inside:
        for name in ("down", "up", "out", "qkv"):
            scratch += reduce_buffers(half, columns[name], count)
    if plan.late:
        scratch += [VMEM((half, joint), LOW), VMEM((count - 1, block, joint), LOW)]
    scratch.append(VMEM((16, slots), LOW))
    scratch += [VMEM(value.shape, value.dtype) for value in (gain2, gain1)]
    ways = lax.axis_size("tp")
    if plan.joined:
        scratch += [VMEM((8, wide), FULL)] * 2
        scratch += [
            VMEM((ways, depth, wide), FULL),
            VMEM((2, depth, wide), FULL),
            VMEM((count, 2, depth, wide), FULL),
            VMEM((3, depth, wide), FULL),
        ]
    results = run(
        functools.partial(back_kernel, plan, size, tile),
        "back_layer",
        ident,
        inputs,
        outputs,
        scratch,
        3 * (count - 1) + 2 * ROUND_COPIES + 6 * count + ways + count,
        len(saved) + 4,
        sizes,
        58,
        6 * rows * width * (2 * hidden + attn + joint) + 10 * slots * slots * 256,
    )
    return results[:2], names, results[2:]


def shards(
    tokens,
    block_tokens,
    ln1_gain,
    ln1_bias,
    w_qkv,
    b_qv,
    w_out,
    b_out,
    ln2_gain,
    ln2_bias,
    w_up,
    b_up,
    w_down,
    b_down,
    cotangent,
):
    images, capacity, width = tokens.shape
    assert images == 1
    layers = w_qkv.shape[0]
    size = HEAD_DIM
    ctx_count = lax.axis_size("ctx")
    ctx_place = lax.axis_index("ctx")
    joint_width = w_qkv.shape[2]
    heads = joint_width // (3 * size)
    assert heads == ctx_count
    attn_width = heads * size
    hidden_width = w_up.shape[2]
    weights = {"qkv": w_qkv, "out": w_out, "up": w_up, "down": w_down}
    sizes = (ctx_count, lax.axis_size("shard"))
    inside = sizes == (4, 2)
    gathered = {}
    if not inside:
        for name, value in weights.items():
            for layer in range(layers):
                gathered[name, layer] = gather_weight(value[layer])[0]
    source, stream = tokens[0], None
    saved = []
    for layer in range(layers):
        last = layer == layers - 1
        result, following, kept = forward_layer(
            source,
            stream,
            block_tokens,
            (b_out, ln2_gain, ln2_bias, b_down, ln1_gain, ln1_bias, b_up, b_qv),
            gathered,
            weights,
            Plan(layer, last, inside),
            last,
            size,
            sizes,
            1 + layer,
        )
        before = stream if layer else source
        first = source if layer else kept[8]
        saved.append((before, first) + tuple(kept[:8]))
        source, stream = following, result
    mixed = source

    done, packs = {}, {}
    source, stream, late = cotangent[0], None, None
    for layer in reversed(range(layers)):
        before, first, qkv, head_out, lse, heads_low, middle, second, hidden, slope = saved[layer]
        plan = BackPlan(layer, layers, inside)
        whole = {name: gathered[name, layer] for name in NAMES}
        near = [slope, whole["down"], whole["up"], middle, hidden, second, whole["out"]]
        near += [heads_low, qkv, head_out, lse, first, whole["qkv"], before]
        others = [packs[key] for key in sorted(packs)]
        (stream, source), names, rest = back_layer(
            source, stream, block_tokens, ln2_gain, ln1_gain, near, late, others, plan, size, sizes, 1 + layers + layer
        )
        rest = iter(rest)
        for name in names:
            done[name, layer] = next(rest)
        if plan.inside and not plan.final:
            late = next(rest)
        if plan.late:
            done["qkv", layer + 1] = next(rest)
        if plan.joined:
            totals = next(rest)
        else:
            packs[layer] = (next(rest), next(rest))
        if not inside:
            for name in NAMES:
                value = next(rest)
                done[name, layer] = scatter_weight(
                    lambda start, count, value=value: rows_of(value, start, count).astype(FULL),
                    width,
                )
    if not inside:
        split = total_over(("tp",), jnp.stack([packs[l][0] for l in range(layers)], axis=1))
        local = jnp.stack([packs[l][1] for l in range(layers)], axis=1)
        totals = total_over(("shard", "ctx"), jnp.stack([local, split]))
        totals = totals.reshape(2, 8 * layers, -1)
    pairs = b_qv.shape[1]
    outs = gather_outputs(done, source, mixed, totals, layers, (hidden_width, pairs))
    g_qkv, g_out, g_up, g_down, mixed, token_grads = outs[:6]
    g_ln1_gain, g_ln1_bias, g_ln2_gain, g_ln2_bias, g_b_out, g_b_down, g_b_up, g_b_qv = outs[6:]
    return (
        mixed,
        token_grads,
        g_ln1_gain,
        g_ln1_bias,
        g_qkv,
        g_b_qv,
        g_out,
        g_b_out,
        g_ln2_gain,
        g_ln2_bias,
        g_up,
        g_b_up,
        g_down,
        g_b_down,
    )


def solution(mesh):
    split_rows = P(None, ("shard", "ctx"), "tp")
    split_tokens = P("shard", "ctx", None)
    return jax.shard_map(
        shards,
        mesh=mesh,
        in_specs=(
            split_tokens,
            P("shard", None),
            P(),
            P(),
            split_rows,
            P(None, "tp"),
            split_rows,
            P(),
            P(),
            P(),
            split_rows,
            P(None, "tp"),
            split_rows,
            P(),
            split_tokens,
        ),
        out_specs=(
            split_tokens,
            split_tokens,
            P(),
            P(),
            split_rows,
            P(None, "tp"),
            split_rows,
            P(),
            P(),
            P(),
            split_rows,
            P(None, "tp"),
            split_rows,
            P(),
        ),
        check_vma=False,
    )
```

```python
import functools
import math

import jax
import jax.numpy as jnp
from jax import lax
from jax.experimental import pallas as pl
from jax.experimental.pallas import tpu as pltpu
from jax.sharding import PartitionSpec as P

HEAD_DIM = 64
EPSILON = 1e-06
NEG_LARGE = -1e30
LOW = jnp.bfloat16
FULL = jnp.float32
PAD = 128
MESH = pl.DeviceIdType.MESH
VMEM = pltpu.VMEM
HBM = pltpu.HBM
SMEM = pltpu.SMEM


def bits_of(axis):
    size = lax.axis_size(axis)
    assert size & (size - 1) == 0
    return [1 << i for i in range(size.bit_length() - 1)]


def swap(value, axis, bit):
    size = lax.axis_size(axis)
    return lax.ppermute(value, axis, [(i, i ^ bit) for i in range(size)])


def side_of(axis, bit):
    return (lax.axis_index(axis) // bit) % 2


def rows_of(value, start, count, axis=0):
    return lax.dynamic_slice_in_dim(value, start, count, axis)


def halve(axis, bits, partial, total):
    offset, span, received = jnp.int32(0), total, []

    def summed(start, count):
        value = partial(start, count)
        for got, base in received:
            value = value + rows_of(got, start - base, count).astype(FULL)
        return value

    for bit in bits:
        half = span // 2
        side = side_of(axis, bit)
        got = swap(summed(offset + (1 - side) * half, half).astype(LOW), axis, bit)
        offset = offset + side * half
        received.append((got, offset))
        span = half
    return summed(offset, span)


def double(axis, bits, value):
    for bit in bits:
        got = swap(value, axis, bit)
        first = side_of(axis, bit) == 0
        value = jnp.concatenate(
            [jnp.where(first, value, got), jnp.where(first, got, value)], axis=0
        )
    return value


def total_over(axes, value):
    for axis in axes:
        for bit in bits_of(axis):
            value = value + swap(value, axis, bit)
    return value


def ring(value, by):
    count = lax.axis_size("ctx")
    return lax.ppermute(value, "ctx", [(i, (i + by) % count) for i in range(count)])


def gather_weight(piece):
    count = lax.axis_size("ctx")
    place = lax.axis_index("ctx")
    ways = lax.axis_size("shard")
    blocks = [piece] + [ring(piece, by) for by in range(1, count)]
    whole = jnp.zeros((ways * count,) + piece.shape, piece.dtype)
    me = lax.axis_index("shard")
    for by, block in enumerate(blocks):
        at = (place - by) % count
        held = [(jnp.int32(0), block)]
        for bit in bits_of("shard"):
            held = held + [(other ^ bit, swap(value, "shard", bit)) for other, value in held]
        for other, value in held:
            whole = lax.dynamic_update_index_in_dim(whole, value, (me ^ other) * count + at, 0)
    return whole.reshape((ways * count * piece.shape[0],) + piece.shape[1:]), blocks[-1]


def scatter_weight(partial, total):
    count = lax.axis_size("ctx")
    place = lax.axis_index("ctx")
    mine = halve("shard", bits_of("shard")[::-1], partial, total).astype(LOW)
    mine = mine.reshape((count, mine.shape[0] // count) + mine.shape[1:])
    value = lax.dynamic_index_in_dim(mine, place, 0, False).astype(FULL)
    for by in range(1, count):
        given = lax.dynamic_index_in_dim(mine, (place + by) % count, 0, False)
        value = value + ring(given, by).astype(FULL)
    return value


def dot(left, right, contract):
    return lax.dot_general(
        left, right, ((contract[0], contract[1]), ((), ())), preferred_element_type=FULL
    )


def turned(value):
    return value.astype(FULL).T.astype(LOW)


def normalize(rows, gain, shift):
    row_mean = jnp.mean(rows, axis=-1, keepdims=True)
    centred = rows - row_mean
    inverse = lax.rsqrt(jnp.mean(centred * centred, axis=-1, keepdims=True) + EPSILON)
    normed = centred * inverse
    return (normed * gain + shift, normed, inverse)


def normalize_back(grad_out, normed, inverse, gain):
    scaled = grad_out * gain
    mean_grad = jnp.mean(scaled, axis=-1, keepdims=True)
    mean_cross = jnp.mean(scaled * normed, axis=-1, keepdims=True)
    return inverse * (scaled - mean_grad - normed * mean_cross)


def gelu_pair(value):
    spread = 0.5 * (1.0 + lax.erf(value * (0.5**0.5)))
    slope = spread + value * jnp.exp(-0.5 * value * value) * (1.0 / math.sqrt(2.0 * math.pi))
    return (value * spread).astype(LOW), slope.astype(LOW)


class Mover:
    def __init__(self, sizes, send, recv, local):
        self.ctx_count, self.shard_count = sizes
        self.send, self.recv, self.local = send, recv, local
        self.copies, self.here = [], []
        self.arrived = set()
        self.landed = set()
        self.ctx = lax.axis_index("ctx")
        self.shard = lax.axis_index("shard")

    def go(self, source, target, **device):
        index = len(self.copies)
        assert index < self.send.shape[0]
        copy = pltpu.make_async_remote_copy(
            src_ref=source,
            dst_ref=target,
            send_sem=self.send.at[index],
            recv_sem=self.recv.at[index],
            device_id=device,
            device_id_type=MESH,
        )
        copy.start()
        self.copies.append(copy)
        return index

    def stay(self, source, target):
        index = len(self.here)
        assert index < self.local.shape[0]
        copy = pltpu.make_async_copy(source, target, self.local.at[index])
        copy.start()
        self.here.append(copy)
        return index

    def near(self, *indices):
        for index in indices:
            if index not in self.landed:
                self.landed.add(index)
                self.here[index].wait()

    def take(self, index):
        if index not in self.arrived:
            self.arrived.add(index)
            self.copies[index].wait_recv()

    def flip(self, bits):
        place = self.ctx
        if bits & 1:
            place = place + 1 - 2 * lax.rem(self.ctx, 2)
        if bits & 2:
            place = place + 2 - 4 * (self.ctx // 2)
        return place

    def on(self, by):
        return lax.rem(self.ctx + by, self.ctx_count)

    def back(self, by):
        return lax.rem(self.ctx + self.ctx_count - by, self.ctx_count)

    def settle(self):
        for index, copy in enumerate(self.copies):
            self.take(index)
            copy.wait_send()
        self.near(*range(len(self.here)))


class Gather:
    def __init__(self, mover, source, target):
        self.mover, self.source, self.target = mover, source, target
        self.over = []

    def start(self):
        self.start_line()
        self.start_over()

    def start_line(self):
        mover = self.mover
        mine, there = self.source, self.block(mover.ctx)
        self.far = mover.go(mine, there, ctx=mover.flip(2))
        self.close = mover.go(mine, there, ctx=mover.flip(1))

    def start_over(self):
        mover = self.mover
        mine, there = self.source, self.block(mover.ctx)
        self.over.append(mover.go(mine, there, shard=1 - mover.shard))
        self.own = mover.stay(mine, there)

    def block(self, ctx):
        mover = self.mover
        rows = self.source.shape[0]
        start = (mover.shard * mover.ctx_count + ctx) * rows
        return self.target.at[pl.ds(pl.multiple_of(start, rows), rows)]

    def pass_on(self, stage):
        mover = self.mover
        if stage == 1:
            mover.take(self.far)
            rows = self.block(mover.flip(2))
            self.passed = mover.go(rows, rows, ctx=mover.flip(1))
        elif stage == 2:
            mover.take(self.close)
            rows = self.block(mover.flip(1))
        else:
            mover.take(self.passed)
            rows = self.block(mover.flip(3))
        self.over.append(mover.go(rows, rows, shard=1 - mover.shard))

    def have(self):
        for copy in self.over:
            self.mover.take(copy)
        self.mover.near(self.own)


class Reduce:
    def __init__(self, mover, buffers, out, lhs, rhs):
        self.mover, self.out, self.lhs, self.rhs = mover, out, lhs, rhs
        self.give, self.got, self.mid, self.line = buffers
        self.half = self.give.shape[0]
        self.block = self.half // mover.ctx_count

    def compute(self, target, shard):
        chunk = min(256, self.half)

        def step(i, carry):
            at = pl.ds(pl.multiple_of(shard * self.half + i * chunk, chunk), chunk)
            here = pl.ds(pl.multiple_of(i * chunk, chunk), chunk)
            target[here, :] = dot(self.lhs[:, at], self.rhs[...], ((0,), (0,))).astype(LOW)
            return carry

        lax.fori_loop(0, self.half // chunk, step, 0)

    def begin(self):
        mover = self.mover
        self.compute(self.give, 1 - mover.shard)
        self.cross = mover.go(self.give, self.got, shard=1 - mover.shard)
        self.compute(self.mid, mover.shard)

    def fold(self):
        self.mover.take(self.cross)
        self.mid[...] = (self.mid[...].astype(FULL) + self.got[...].astype(FULL)).astype(LOW)

    def begin_blocks(self):
        mover = self.mover
        self.blocks = {}
        for bits in (3, 1, 2, 0):
            ctx = mover.flip(bits)
            at = pl.ds(pl.multiple_of(ctx * self.block, self.block), self.block)
            start = pl.multiple_of((1 - mover.shard) * self.half + ctx * self.block, self.block)
            lhs = self.lhs[:, pl.ds(start, self.block)]
            self.give[at, :] = dot(lhs, self.rhs[...], ((0,), (0,))).astype(LOW)
            self.blocks[bits] = mover.go(
                self.give.at[at], self.got.at[at], shard=1 - mover.shard
            )

    def fold_blocks(self, *which):
        mover = self.mover
        for bits in which:
            mover.take(self.blocks[bits])
            ctx = mover.flip(bits)
            at = pl.ds(pl.multiple_of(ctx * self.block, self.block), self.block)
            self.mid[at, :] = (
                self.mid[at, :].astype(FULL) + self.got[at, :].astype(FULL)
            ).astype(LOW)

    def rows(self, ctx):
        return self.mid.at[pl.ds(pl.multiple_of(ctx * self.block, self.block), self.block)]

    def spread(self):
        mover = self.mover
        self.first = mover.go(self.rows(mover.flip(3)), self.line.at[1], ctx=mover.flip(1))
        self.second = mover.go(self.rows(mover.flip(1)), self.line.at[0], ctx=mover.flip(1))

    def finish(self):
        mover = self.mover
        mover.take(self.first)
        rows = self.rows(mover.flip(2))
        rows[...] = (rows[...].astype(FULL) + self.line[1].astype(FULL)).astype(LOW)
        self.third = mover.go(rows, self.line.at[2], ctx=mover.flip(2))

    def done(self):
        self.mover.take(self.second)
        self.mover.take(self.third)
        value = self.rows(self.mover.ctx)[...].astype(FULL)
        self.out[...] = value + self.line[0].astype(FULL) + self.line[2].astype(FULL)


def reduce_buffers(half, width, count):
    return [
        VMEM((half, width), LOW),
        VMEM((half, width), LOW),
        VMEM((half, width), LOW),
        VMEM((count - 1, half // count, width), LOW),
    ]


def greet(mover, shard):
    barrier = pltpu.get_barrier_semaphore()
    peers = [dict(ctx=mover.on(by)) for by in range(1, mover.ctx_count)]
    peers += [dict(tp=peer) for peer in tp_peers()]
    if shard:
        peers.append(dict(shard=1 - mover.shard))
    for peer in peers:
        pl.semaphore_signal(barrier, inc=1, device_id=peer, device_id_type=MESH)
    pl.semaphore_wait(barrier, len(peers))


def tp_peers():
    place = lax.axis_index("tp")
    core, far = lax.rem(place, 2), place // 2
    return place + 1 - 2 * core, place + 2 - 4 * far


def run(kernel, name, ident, inputs, outputs, scratch, remote, local, sizes, vmem, flops):
    n_in, n_out, n_scratch = len(inputs), len(outputs), len(scratch)

    def body(*refs):
        ins, outs = refs[:n_in], refs[n_in : n_in + n_out]
        work = refs[n_in + n_out :]
        mover = Mover(sizes, *work[n_scratch:])
        kernel(mover, ins, outs, work[:n_scratch])

    return pl.pallas_call(
        body,
        in_specs=[pl.BlockSpec(memory_space=space) for _, space in inputs],
        out_specs=[pl.BlockSpec(memory_space=space) for _, _, space in outputs],
        out_shape=[jax.ShapeDtypeStruct(shape, dtype) for shape, dtype, _ in outputs],
        scratch_shapes=list(scratch)
        + [
            pltpu.SemaphoreType.DMA((remote,)),
            pltpu.SemaphoreType.DMA((remote,)),
            pltpu.SemaphoreType.DMA((local,)),
        ],
        compiler_params=pltpu.CompilerParams(
            collective_id=ident, has_side_effects=True, vmem_limit_bytes=vmem * 2**20
        ),
        cost_estimate=pl.CostEstimate(flops=flops, bytes_accessed=2**24, transcendentals=0),
        name=name,
    )(*[value for value, _ in inputs])


def order_of(block, count):
    return (block + count - 1) % count


def tiles_of(count, capacity, tile):
    ends = [-(-(p + 1) * capacity // tile) for p in range(count)]
    return list(zip([0] + ends[:-1], ends))


def parts_of(capacity):
    middle = capacity // 2 // PAD * PAD
    return [(0, middle), (middle, capacity)] if middle else [(0, capacity)]


def tile_at(t, tile):
    return pl.ds(pl.multiple_of(t * tile, tile), tile)


def turned_product(left, right, bias, target):
    def step(i, carry):
        at = pl.ds(pl.multiple_of(i * PAD, PAD), PAD)
        value = jnp.dot(left[at, :], right[...], preferred_element_type=FULL)
        if bias is not None:
            value = value + bias[0:1, :]
        target[:, at] = turned(value.astype(LOW))
        return carry

    lax.fori_loop(0, left.shape[0] // PAD, step, 0)


def head_rows(ref, head, width):
    return ref.at[pl.ds(pl.multiple_of(head * width, 16), width)]


def attend_part(size, tile, mover, joint, bias, heads, qkv, o_ref, lse, work, after_send, begun, between):
    k_ref, q_ref, v_ref, low_ref, score_ref, top_ref = work
    count, width, capacity = qkv.shape
    slots = count * capacity
    sent = [None] + [
        mover.go(head_rows(joint, mover.on(by), width), qkv.at[by], ctx=mover.on(by))
        for by in range(1, count)
    ]
    after_send()
    qkv[0] = head_rows(joint, mover.ctx, width)[...]
    q_ref[size:PAD, :] = jnp.concatenate(
        [jnp.ones((16, slots), LOW), jnp.zeros((PAD - size - 16, slots), LOW)], axis=0
    )

    def prepare(r):
        here = slice(r * capacity, (r + 1) * capacity)
        p = order_of(r, count)
        q_ref[0:size, p * capacity : (p + 1) * capacity] = (
            qkv[r, 0:size, :] * (size**-0.5)
        ).astype(LOW)
        v_ref[:, here] = qkv[r, 2 * size : 3 * size, :]
        keys = jnp.concatenate(
            [qkv[r, size : 2 * size, :], bias[:, here], jnp.zeros((PAD - size - 16, capacity), LOW)],
            axis=0,
        )
        k_ref[here, :] = turned(keys)

    prepare(0)
    for by in range(1, count):
        mover.take(sent[by])
        prepare(by)

    begun()
    last = slots // tile - 1
    assert last % 2 == 1

    def phase(t, now, following, then):
        at, ahead = tile_at(t, tile), tile_at(following, tile)
        top = top_ref[now, 0:1, :]
        total = jnp.zeros((1, tile), FULL)
        summed = jnp.zeros((size, tile), FULL)
        new_top = jnp.full((1, tile), NEG_LARGE, FULL)
        for r in range(count):
            here = slice(r * capacity, (r + 1) * capacity)
            scores = jnp.dot(k_ref[here, :], q_ref[:, ahead], preferred_element_type=FULL)
            score_ref[then, here, :] = scores
            new_top = jnp.maximum(new_top, jnp.max(scores, axis=0, keepdims=True))
            weights = jnp.exp(score_ref[now, here, :] - top)
            total = total + jnp.sum(weights, axis=0, keepdims=True)
            summed = summed + jnp.dot(
                v_ref[:, here], weights.astype(LOW), preferred_element_type=FULL
            )
        top_ref[then] = jnp.broadcast_to(new_top, (8, tile))
        out = summed / total
        o_ref[:, at] = out
        low_ref[:, at] = out.astype(LOW)
        lse[:, at] = jnp.broadcast_to(top + jnp.log(total), (8, tile))

    def step(i, carry):
        phase(2 * i, 0, 2 * i + 1, 1)
        phase(2 * i + 1, 1, jnp.minimum(2 * i + 2, last), 0)
        return carry

    scores = jnp.dot(k_ref[...], q_ref[:, 0:tile], preferred_element_type=FULL)
    score_ref[0] = scores
    top_ref[0] = jnp.broadcast_to(jnp.max(scores, axis=0, keepdims=True), (8, tile))
    arriving = []
    for p, (low, high) in enumerate(tiles_of(count, capacity, 2 * tile)):
        lax.fori_loop(low, high, step, 0)
        done = low_ref.at[:, p * capacity : (p + 1) * capacity]
        if p < count - 1:
            there = head_rows(heads, mover.ctx, size)
            arriving.append(mover.go(done, there, ctx=mover.back(p + 1)))
        else:
            head_rows(heads, mover.ctx, size)[...] = low_ref[:, p * capacity : (p + 1) * capacity]
        between(p + 1)
    for copy in arriving:
        mover.take(copy)


def attend_back_part(size, tile, mover, parts, bias, qkv, o_ref, lse, grads, work, ready, waiting, begun, between):
    k_ref, v_ref, q_ref, do_ref, nat_ref, delta_ref, dq_ref, dk_ref, dv_ref, got, back, score_ref, grad_ref = work
    count, width, capacity = qkv.shape
    slots = count * capacity
    sent = [None] + [
        mover.go(head_rows(parts, mover.on(by), size), got.at[by], ctx=mover.on(by))
        for by in range(1, count)
    ]
    got[0] = head_rows(parts, mover.ctx, size)[...]
    waiting()
    ready()
    q_ref[size:PAD, :] = jnp.concatenate(
        [jnp.ones((16, slots), LOW), jnp.zeros((PAD - size - 16, slots), LOW)], axis=0
    )
    do_ref[size:PAD, :] = jnp.zeros((PAD - size, slots), LOW)
    dq_ref[...] = jnp.zeros_like(dq_ref)
    for r in range(count):
        here = slice(r * capacity, (r + 1) * capacity)
        pad = jnp.zeros((PAD - size - 16, capacity), LOW)
        k_ref[here, :] = turned(
            jnp.concatenate([qkv[r, size : 2 * size, :], bias[:, here], pad], axis=0)
        )
        v_ref[here, :] = turned(
            jnp.concatenate(
                [qkv[r, 2 * size : 3 * size, :], jnp.zeros((PAD - size, capacity), LOW)], axis=0
            )
        )
    for r in range(count):
        if r:
            mover.take(sent[r])
        p = order_of(r, count)
        at = slice(p * capacity, (p + 1) * capacity)
        scaled = (qkv[r, 0:size, :] * (size**-0.5)).astype(LOW)
        dout = got[r]
        q_ref[0:size, at] = scaled
        do_ref[0:size, at] = dout
        nat_ref[at, :] = turned(jnp.concatenate([scaled, dout], axis=0))
        delta = jnp.sum(dout.astype(FULL) * o_ref[:, at], axis=0, keepdims=True)
        delta_ref[:, at] = jnp.broadcast_to(delta, (8, capacity))

    begun()
    last = slots // tile - 1
    assert last % 2 == 1
    tiles = tiles_of(count, capacity, 2 * tile)
    arriving = []
    mine = head_rows(grads, mover.ctx, width)
    for turn, r in enumerate(list(range(1, count)) + [0]):
        here = slice(r * capacity, (r + 1) * capacity)
        dk_ref[...] = jnp.zeros_like(dk_ref)
        dv_ref[...] = jnp.zeros_like(dv_ref)

        def ready_scores(t, then, low, high, r=r):
            ahead = tile_at(t, tile)
            rows = slice(r * capacity + low, r * capacity + high)
            score_ref[then, low:high, :] = jnp.dot(
                k_ref[rows, :], q_ref[:, ahead], preferred_element_type=FULL
            )
            grad_ref[then, low:high, :] = jnp.dot(
                v_ref[rows, :], do_ref[:, ahead], preferred_element_type=FULL
            )

        def phase(t, now, following, then, r=r):
            at = tile_at(t, tile)
            query_grad = jnp.zeros((size, tile), FULL)
            for low, high in parts_of(capacity):
                ready_scores(following, then, low, high)
                chance = jnp.exp(score_ref[now, low:high, :] - lse[0:1, at])
                score_grad = (
                    chance * (grad_ref[now, low:high, :] - delta_ref[0:1, at])
                ).astype(LOW)
                query_grad = query_grad + jnp.dot(
                    qkv[r, size : 2 * size, low:high], score_grad, preferred_element_type=FULL
                )
                dk_ref[low:high, :] += jnp.dot(
                    score_grad, nat_ref[at, :], preferred_element_type=FULL
                )
                dv_ref[low:high, :] += jnp.dot(
                    chance.astype(LOW), nat_ref[at, :], preferred_element_type=FULL
                )
            dq_ref[:, at] += query_grad

        def step(i, carry, phase=phase):
            phase(2 * i, 0, 2 * i + 1, 1)
            phase(2 * i + 1, 1, jnp.minimum(2 * i + 2, last), 0)
            return carry

        ready_scores(0, 0, 0, capacity)
        if r:
            lax.fori_loop(0, tiles[-1][1], step, 0)
        else:
            for p, (low, high) in enumerate(tiles):
                lax.fori_loop(low, high, step, 0)
                at = slice(p * capacity, (p + 1) * capacity)
                value = (dq_ref[:, at] * (size**-0.5)).astype(LOW)
                if p < count - 1:
                    back[p + 1, 0:size, :] = value
                    arriving.append(
                        mover.go(
                            back.at[p + 1, 0:size], mine.at[0:size], ctx=mover.back(p + 1)
                        )
                    )
                else:
                    mine[0:size, :] = value
        keys = dk_ref[...].T[0:size].astype(LOW)
        values = dv_ref[...].T[size : 2 * size].astype(LOW)
        if r:
            back[r, size : 2 * size, :] = keys
            back[r, 2 * size : 3 * size, :] = values
            arriving.append(
                mover.go(
                    back.at[r, size : 3 * size], mine.at[size : 3 * size], ctx=mover.back(r)
                )
            )
        else:
            mine[size : 2 * size, :] = keys
            mine[2 * size : 3 * size, :] = values
        between(turn)
    for copy in arriving:
        mover.take(copy)


def attend_back_buffers(size, count, capacity, tile):
    slots = count * capacity
    return [
        VMEM((slots, PAD), LOW),
        VMEM((slots, PAD), LOW),
        VMEM((PAD, slots), LOW),
        VMEM((PAD, slots), LOW),
        VMEM((slots, PAD), LOW),
        VMEM((8, slots), FULL),
        VMEM((size, slots), FULL),
        VMEM((capacity, PAD), FULL),
        VMEM((capacity, PAD), FULL),
        VMEM((count, size, capacity), LOW),
        VMEM((count, 3 * size, capacity), LOW),
        VMEM((2, capacity, tile), FULL),
        VMEM((2, capacity, tile), FULL),
    ]


class Round:
    def __init__(self, mover, rows, full, buffers):
        place = lax.axis_index("tp")
        core, far = lax.rem(place, 2), place // 2
        self.mover, self.full = mover, full
        self.give, self.ra, self.passing, self.rb, self.keep = buffers
        self.span = rows // 4
        self.half = self.span // 2
        self.mate, self.far = tp_peers()

        def quarter(c, f):
            return (c * 2 + f) * self.span

        self.own, self.other = quarter(core, far), quarter(core, 1 - far)
        self.mate_own, self.mate_other = quarter(1 - core, far), quarter(1 - core, 1 - far)

    def rows(self, start, count=None):
        return pl.ds(pl.multiple_of(start, 16), count or self.span)

    def hand(self, slot, value):
        self.give[slot] = value.astype(LOW)
        return self.mover.go(self.give.at[slot], self.ra.at[slot], tp=self.mate)

    def onward(self, value, index):
        self.mover.take(index)
        self.passing[...] = (value + self.ra[1].astype(FULL)).astype(LOW)
        return [
            self.mover.go(self.passing.at[at], self.rb.at[at], tp=self.far)
            for at in (pl.ds(0, self.half), pl.ds(self.half, self.half))
        ]

    def close(self, far_copies, index, finish, halfway=None):
        self.mover.take(index)
        self.keep[...] += self.ra[0].astype(FULL)
        self.to_far, self.to_mate = [], []
        for c in range(2):
            at = pl.ds(c * self.half, self.half)
            self.mover.take(far_copies[c])
            low = finish(at, self.keep[at] + self.rb[at].astype(FULL))
            mine = self.full.at[self.rows(self.own + c * self.half, self.half)]
            mine[...] = low
            self.to_far.append(self.mover.go(mine, mine, tp=self.far))
            self.to_mate.append(self.mover.go(mine, mine, tp=self.mate))
            if halfway and c == 0:
                halfway()

    def eager(self, make, finish, meanwhile=None, halfway=None):
        first = self.hand(1, make(self.mate_other))
        copies = self.onward(make(self.other), first)
        second = self.hand(0, make(self.mate_own))
        self.keep[...] = make(self.own)
        if meanwhile:
            meanwhile()
        self.close(copies, second, finish, halfway)

    def after(self, before, make, finish, meanwhile=None, halfway=None):
        before.have_mate_own()
        second = self.hand(0, make(self.mate_own))
        self.keep[...] = make(self.own)
        before.have_other()
        value = make(self.other)
        before.have_mate_other()
        first = self.hand(1, make(self.mate_other))
        copies = self.onward(value, first)
        if meanwhile:
            meanwhile()
        self.close(copies, second, finish, halfway)

    def have_mate_own(self):
        for copy in self.to_mate:
            self.mover.take(copy)

    def have_other(self):
        self.passed = []
        for c in range(2):
            self.mover.take(self.to_far[c])
            rows = self.full.at[self.rows(self.other + c * self.half, self.half)]
            self.passed.append(self.mover.go(rows, rows, tp=self.mate))

    def have_mate_other(self):
        for copy in self.passed:
            self.mover.take(copy)

    def have(self):
        self.have_mate_own()
        self.have_other()
        self.have_mate_other()


ROUND_COPIES = 10


def round_buffers(rows, width):
    span = rows // 4
    return [
        VMEM((2, span, width), LOW),
        VMEM((2, span, width), LOW),
        VMEM((span, width), LOW),
        VMEM((span, width), LOW),
        VMEM((span, width), FULL),
    ]


NAMES = ("qkv", "out", "up", "down")


def layer_kernel(plan, last, size, tile, mover, ins, outs, work):
    ins, outs, work = iter(ins), iter(outs), iter(work)
    source = next(ins)
    x_ref = None if plan.entry else next(ins)
    live_ref = next(ins)
    far_params = [next(ins) for _ in range(8)]
    stream, following = next(outs), next(outs)
    far_qkv, far_o, far_lse, far_heads, far_middle, far_second, far_hidden, far_slope = [
        next(outs) for _ in range(8)
    ]
    far_first = next(outs) if plan.entry else None
    joint, nat, heads, qkv, o_ref, lse, middle, second, hidden, slope = [
        next(work) for _ in range(10)
    ]
    first = next(work) if plan.entry else source
    attend_work = [next(work) for _ in range(6)]
    one_work, two_work = [next(work) for _ in range(5)], [next(work) for _ in range(5)]
    rows = source.shape[0]
    bias, qkv_bias = next(work), next(work)
    params = [next(work) for _ in range(8)]
    whole = {name: next(work) for name in NAMES}
    gathers, loads = {}, {}
    for name in plan.held:
        loads[name] = (next(ins), whole[name])
    for name in plan.own:
        gathers[name, 0] = Gather(mover, next(ins).at[plan.layer], whole[name])
    kept_ahead = {name: next(outs) for name in plan.ahead}
    for name in plan.ahead:
        gathers[name, 1] = Gather(mover, next(ins).at[plan.layer + 1], next(work))
    kept = {name: next(outs) for name in plan.own}

    greet(mover, bool(gathers))
    if plan.entry:
        gathers_first = [key for key in [("qkv", 0)] if key in gathers]
        for key in gathers_first:
            gathers[key].start()
    param_loads = [mover.stay(there, here) for there, here in zip(far_params, params)]
    loads = {name: mover.stay(*pair) for name, pair in loads.items()}

    def have(name):
        if name in loads:
            mover.near(loads[name])
        else:
            gathers[name, 0].have()
            mover.stay(whole[name], kept[name])
        return whole[name]

    def begin(keys):
        for key in keys:
            if key in gathers:
                gathers[key].start()

    def pass_on(keys, stage):
        for key in keys:
            if key in gathers:
                gathers[key].pass_on(stage)

    def pass_all(keys):
        for stage in (1, 2, 3):
            pass_on(keys, stage)

    mover.near(*param_loads)
    layer, after = plan.layer, min(plan.layer + 1, params[0].shape[0] - 1)

    def row(index, layer=layer):
        return params[index][...].astype(FULL)[layer : layer + 1]

    b_out, gain2, shift2, b_down, b_up = row(0), row(1), row(2), row(3), row(6)
    gain1, shift1, gain0, shift0 = row(4, after), row(5, after), row(4), row(5)
    qkv_bias[...] = joint_bias(row(7), size, joint.shape[0])
    key_bias(mover, live_ref, bias)
    one = Round(mover, rows, second, one_work)
    two = Round(mover, rows, following, two_work)
    if plan.entry:
        chunk = rows // 5 if rows % 80 == 0 else rows

        def norm_step(i, carry):
            at = pl.ds(pl.multiple_of(i * chunk, 16), chunk)
            value = normalize(source[at, :].astype(FULL), gain0, shift0)[0]
            first[at, :] = value.astype(LOW)
            return carry

        lax.fori_loop(0, rows // chunk, norm_step, 0)
        mover.stay(first, far_first)
        pass_all([("qkv", 0)])
        begin([("out", 0), ("up", 0)])
        turned_product(first, have("qkv"), qkv_bias, joint)
    else:
        turned_product(first, have("qkv"), qkv_bias, joint)

    ahead = [("qkv", 1), ("out", 1)]

    def after_send():
        if plan.entry:
            pass_all([("out", 0), ("up", 0)])
        else:
            for name in plan.own:
                gathers[name, 0].start_over()

    def begun():
        if plan.entry:
            begin([("down", 0)])
        else:
            for name in plan.own:
                gathers[name, 0].start_line()

    def between(p):
        if p > 1:
            pass_on([("down", 0)], p - 1)
        if p == 4:
            begin(ahead)

    attend_part(
        size, tile, mover, joint, bias, heads, qkv, o_ref, lse, attend_work, after_send, begun, between
    )
    nat[...] = turned(heads[...])
    w_out = have("out")

    def out_part(start):
        return dot(nat[one.rows(start), :], w_out[...], ((1,), (1,)))

    def to_second(at, value):
        if plan.entry:
            before = source[one.rows(one.own + at.start, at.size), :].astype(FULL)
        else:
            before = x_ref[at]
        value = before + value + b_out
        middle[at] = value
        return normalize(value, gain2, shift2)[0].astype(LOW)

    def meanwhile():
        mover.stay(qkv, far_qkv)
        mover.stay(o_ref, far_o)
        mover.stay(lse, far_lse)
        mover.stay(nat, far_heads)

    one.eager(out_part, to_second, meanwhile, lambda: pass_on(ahead, 1))
    pass_on(ahead, 2)
    pass_on(ahead, 3)
    begin([("up", 1)])
    w_up, w_down = have("up"), have("down")

    def mlp_part(start):
        at = two.rows(start)
        pre = jnp.dot(second[at, :], w_up[...], preferred_element_type=FULL) + b_up
        low, low_slope = gelu_pair(pre)
        hidden[at, :] = low
        slope[at, :] = low_slope
        return dot(low, w_down[...], ((1,), (1,)))

    def to_following(at, value):
        value = middle[at] + value + b_down
        stream[at] = value
        if last:
            return live_rows(value, two.own + at.start, live_ref[0, mover.ctx]).astype(LOW)
        return normalize(value, gain1, shift1)[0].astype(LOW)

    def meanwhile():
        mover.stay(middle, far_middle)
        mover.stay(second, far_second)
        mover.stay(hidden, far_hidden)
        mover.stay(slope, far_slope)
        pass_on([("up", 1)], 1)
        pass_on([("up", 1)], 2)

    two.after(one, mlp_part, to_following, meanwhile, lambda: pass_on([("up", 1)], 3))
    two.have()
    for name in plan.ahead:
        gathers[name, 1].have()
        mover.stay(gathers[name, 1].target, kept_ahead[name])
    mover.settle()


class Plan:
    def __init__(self, layer, last, inside):
        self.layer, self.entry = layer, layer == 0
        self.own = (NAMES if layer == 0 else ("down",)) if inside else ()
        self.ahead = ("qkv", "out", "up") if inside and not last else ()
        self.held = tuple(name for name in NAMES if name not in self.own)


def forward_layer(source, x, live, params, gathered, weights, plan, last, size, sizes, ident):
    rows, width = source.shape
    count = sizes[0]
    joint, hidden = weights["qkv"].shape[2], weights["up"].shape[2]
    heads = joint // (3 * size)
    attn, slots, span = heads * size, count * rows, rows // 4
    tile = 256 if slots % 256 == 0 else PAD
    columns = {"qkv": joint, "out": attn, "up": hidden, "down": hidden}
    inputs = [(source, VMEM)] + ([] if plan.entry else [(x, VMEM)])
    inputs += [(live, SMEM)] + [(value, HBM) for value in params]
    inputs += [(gathered[name, plan.layer], HBM) for name in plan.held]
    inputs += [(weights[name], HBM) for name in plan.own + plan.ahead]
    saved = [
        ((count, 3 * size, rows), LOW),
        ((size, slots), FULL),
        ((8, slots), FULL),
        ((rows, attn), LOW),
        ((span, width), FULL),
        ((rows, width), LOW),
        ((rows, hidden), LOW),
        ((rows, hidden), LOW),
    ]
    outputs = [((span, width), FULL, VMEM), ((rows, width), LOW, VMEM)]
    outputs += [(shape, dtype, HBM) for shape, dtype in saved]
    if plan.entry:
        outputs.append(((rows, width), LOW, HBM))
    outputs += [((width, columns[name]), LOW, HBM) for name in plan.ahead + plan.own]
    qkv_shape, o_shape, lse_shape, heads_shape = saved[:4]
    scratch = [VMEM((joint, rows), LOW), VMEM((rows, attn), LOW), VMEM((attn, rows), LOW)]
    scratch += [VMEM(*pair) for pair in saved[:3] + saved[4:]]
    if plan.entry:
        scratch.append(VMEM((rows, width), LOW))
    scratch += [
        VMEM((slots, PAD), LOW),
        VMEM((PAD, slots), LOW),
        VMEM((size, slots), LOW),
        VMEM((size, slots), LOW),
        VMEM((2, slots, tile), FULL),
        VMEM((2, 8, tile), FULL),
    ]
    scratch += round_buffers(rows, width) + round_buffers(rows, width)
    scratch += [VMEM((16, slots), LOW), VMEM((16, joint), FULL)]
    scratch += [VMEM(value.shape, value.dtype) for value in params]
    scratch += [VMEM((width, columns[name]), LOW) for name in NAMES + plan.ahead]
    results = run(
        functools.partial(layer_kernel, plan, last, size, tile),
        "forward_layer",
        ident,
        inputs,
        outputs,
        scratch,
        2 * (count - 1) + 2 * ROUND_COPIES + 2 * count * len(plan.own + plan.ahead),
        10 + 2 * len(plan.own + plan.ahead) + len(plan.held) + len(params),
        sizes,
        58,
        2 * rows * width * (2 * hidden + attn + joint) + 4 * slots * slots * 256,
    )
    stream, following = results[:2]
    kept = results[2 : 11 if plan.entry else 10]
    for name, value in zip(plan.ahead, results[2 + len(kept) :]):
        gathered[name, plan.layer + 1] = value
    for name, value in zip(plan.own, results[2 + len(kept) + len(plan.ahead) :]):
        gathered[name, plan.layer] = value
    return stream, following, kept


class SmallSums:
    def __init__(self, mover, rows, held, got):
        self.mover, self.rows, self.held, self.got = mover, rows, held, got
        self.stage = 0
        mate, far = tp_peers()
        self.peers = [
            dict(tp=mate),
            dict(tp=far),
            dict(shard=1 - mover.shard),
            dict(ctx=mover.flip(2)),
            dict(ctx=mover.flip(1)),
        ]

    def part(self, stage):
        return pl.ds(0, self.rows if stage < 2 else self.held.shape[1])

    def step(self):
        stage, mover = self.stage, self.mover
        if stage:
            mover.take(self.copy)
            at = self.part(stage - 1)
            self.held[stage] = self.held[stage - 1]
            self.held[stage, at, :] = self.held[stage - 1, at, :] + self.got[stage - 1, at, :]
        if stage < len(self.peers):
            at = self.part(stage)
            self.copy = mover.go(
                self.held.at[stage, at], self.got.at[stage, at], **self.peers[stage]
            )
        self.stage = stage + 1

    def value(self):
        return self.held[len(self.peers)]


def key_bias(mover, live_ref, bias):
    capacity = bias.shape[1] // mover.ctx_count
    row = lax.broadcasted_iota(jnp.int32, (16, capacity), 0)
    slot = lax.broadcasted_iota(jnp.int32, (16, capacity), 1)
    for r in range(mover.ctx_count):
        live = live_ref[0, mover.back(r)]
        value = jnp.where((row == 0) & (slot >= live), NEG_LARGE, 0.0)
        bias[:, r * capacity : (r + 1) * capacity] = value.astype(LOW)


def pair_columns(rows, width, size, turn):
    shape = (width, rows) if turn else (rows, width)
    given = lax.broadcasted_iota(jnp.int32, shape, 1 if turn else 0)
    column = lax.broadcasted_iota(jnp.int32, shape, 0 if turn else 1)
    head, within = column // (3 * size), column % (3 * size)
    wanted = head * (2 * size) + jnp.where(within < size, within, within - size)
    key = (within >= size) & (within < 2 * size)
    return jnp.where((given == wanted) & ~key, 1.0, 0.0).astype(LOW)


def joint_bias(pair, size, width):
    rows = pair.shape[1]
    spread = jnp.broadcast_to(pair, (16, rows)).astype(LOW)
    return jnp.dot(spread, pair_columns(rows, width, size, False), preferred_element_type=FULL)


def live_rows(value, start, live):
    row = start + lax.broadcasted_iota(jnp.int32, value.shape, 0)
    return jnp.where(row < live, value, 0.0)


def sums_into(sums, first, at, values):
    for index, value in enumerate(values):
        row = first + index
        added = jnp.sum(value, axis=0, keepdims=True)
        width = added.shape[1]
        sums[row : row + 1, 0:width] = (
            added if at.start == 0 else sums[row : row + 1, 0:width] + added
        )


def back_kernel(plan, size, tile, mover, ins, outs, work):
    ins, outs, work = iter(ins), iter(outs), iter(work)
    source = next(ins)
    x_ref = None if plan.last else next(ins)
    live_ref, far_gain2, far_gain1 = [next(ins) for _ in range(3)]
    far = [next(ins) for _ in range(14)]
    late_far = next(ins) if plan.late else None
    others = [(next(ins), next(ins)) for _ in range(plan.others)]
    stream, following = next(outs), next(outs)
    grad_outs = {name: next(outs) for name in NAMES if plan.inside and (name != "qkv" or plan.final)}
    mid_out = next(outs) if plan.inside and not plan.final else None
    late_out = next(outs) if plan.late else None
    split = local = totals = None
    if plan.joined:
        totals = next(outs)
    else:
        split, local = next(outs), next(outs)
    wholes = {} if plan.inside else {name: next(outs) for name in NAMES}
    near = [next(work) for _ in range(14)]
    slope, w_down, w_up, middle, hidden, second, w_out, heads, qkv, o_ref, lse, first, w_qkv, before = near
    grad = next(work) if plan.last else source
    pre_grad, attn_grad, parts, grads, nat = [next(work) for _ in range(5)]
    attend_work = [next(work) for _ in range(13)]
    one_work, two_work = [next(work) for _ in range(5)], [next(work) for _ in range(5)]
    rows, width = source.shape
    reduces = {}
    if plan.inside:
        pairs = {
            "down": (grad, hidden),
            "up": (second, pre_grad),
            "out": (attn_grad, heads),
            "qkv": (first, nat),
        }
        for name in ("down", "up", "out", "qkv"):
            buffers = [next(work) for _ in range(4)]
            reduces[name] = Reduce(mover, buffers, grad_outs.get(name), *pairs[name])
    late = None
    if plan.late:
        late_mid, late_line = next(work), next(work)
        late = Reduce(mover, (late_mid, None, late_mid, late_line), late_out, None, None)
    bias, gain2_ref, gain1_ref = [next(work) for _ in range(3)]
    if plan.joined:
        split, local = next(work), next(work)
        early_held, early_got, late_held, late_got = [next(work) for _ in range(4)]
        tops = 8 * (plan.others + 1)
        early = SmallSums(mover, tops, early_held, early_got)
        final = SmallSums(mover, 8, late_held, late_got)
        everything = [(split, local)] + others

    greet(mover, plan.inside)
    gain_loads = [mover.stay(far_gain2, gain2_ref), mover.stay(far_gain1, gain1_ref)]
    one = Round(mover, rows, attn_grad, one_work)
    two = Round(mover, rows, following, two_work)
    if plan.final:
        far[13] = far[13].at[two.rows(two.own)]
    load = [mover.stay(there, here) for there, here in zip(far, near)]
    if late:
        mover.near(mover.stay(late_far, late_mid))
        late.spread()
    if plan.last:
        chunk = rows // 5 if rows % 80 == 0 else rows

        def mask_step(i, carry):
            at = pl.ds(pl.multiple_of(i * chunk, 16), chunk)
            value = source[at, :].astype(FULL)
            grad[at, :] = live_rows(value, i * chunk, live_ref[0, mover.ctx]).astype(LOW)
            return carry

        lax.fori_loop(0, rows // chunk, mask_step, 0)
    key_bias(mover, live_ref, bias)
    mover.near(*gain_loads)
    gain2, gain1 = [
        ref[...].astype(FULL)[plan.layer : plan.layer + 1] for ref in (gain2_ref, gain1_ref)
    ]
    split[...] = jnp.zeros_like(split)
    local[...] = jnp.zeros_like(local)
    split[5:6, 0:width] = jnp.sum(
        grad[one.rows(one.own), :].astype(FULL), axis=0, keepdims=True
    )
    mover.near(*load[:3])
    hidden_width = slope.shape[1]

    def mlp_part(start):
        at = one.rows(start)
        pre = jnp.dot(grad[at, :], w_down[...], preferred_element_type=FULL)
        low = (pre * slope[at, :].astype(FULL)).astype(LOW)
        pre_grad[at, :] = low
        local[0:1, 0:hidden_width] += jnp.sum(low.astype(FULL), axis=0, keepdims=True)
        return dot(low, w_up[...], ((1,), (1,)))

    def to_attn(at, value):
        if plan.last:
            above = grad[one.rows(one.own + at.start, at.size), :].astype(FULL)
        else:
            above = x_ref[at]
        _, normed, inverse = normalize(middle[at], 1.0, 0.0)
        result = above + normalize_back(value, normed, inverse, gain2)
        stream[at] = result
        low = result.astype(LOW)
        sums_into(split, 2, at, (value * normed, value, low.astype(FULL)))
        return low

    def reduce(name):
        if name in reduces:
            reduces[name].begin()

    def fold(name):
        if name in reduces:
            reduces[name].fold()
            reduces[name].spread()

    def finish(name):
        if name in reduces:
            reduces[name].finish()

    def begin_early():
        if plan.joined:
            early_held[0] = jnp.zeros(early_held.shape[1:], FULL)
            for layer, (some, more) in enumerate(everything):
                first_row = 0 if layer else 2
                for row in range(first_row, 6):
                    at = row * len(everything) + layer
                    early_held[0, at : at + 1, :] = some[row : row + 1, :]
                for row in range(2 if layer else 1):
                    at = tops + row * len(everything) + layer
                    early_held[0, at : at + 1, :] = more[row : row + 1, :]

    def early_step():
        if plan.joined:
            early.step()

    def start_down():
        mover.near(load[3], load[4])
        reduce("down")

    one.eager(mlp_part, to_attn, start_down)
    mover.near(load[5])
    reduce("up")
    one.have()
    mover.near(load[6])
    turned_product(attn_grad, w_out, None, parts)

    def waiting():
        begin_early()
        early_step()
        mover.near(load[7])
        reduce("out")
        early_step()

    def ready():
        mover.near(load[8], load[9], load[10])
        if late:
            late.finish()

    def between(turn):
        early_step()
        if turn == 0:
            finish("down")
        if turn == 3:
            fold("up")
            fold("out")

    attend_back_part(
        size,
        tile,
        mover,
        parts,
        bias,
        qkv,
        o_ref,
        lse,
        grads,
        attend_work,
        ready,
        waiting,
        lambda: fold("down"),
        between,
    )
    nat[...] = turned(grads[...])
    pairs_width = nat.shape[1] // 3 * 2
    picked = jnp.dot(
        nat[...], pair_columns(pairs_width, nat.shape[1], size, True), preferred_element_type=FULL
    )
    local[1:2, 0:pairs_width] = jnp.sum(picked, axis=0, keepdims=True)
    mover.near(*load[11:])

    def qkv_part(start):
        return dot(nat[two.rows(start), :], w_qkv[...], ((1,), (1,)))

    def to_following(at, value):
        row = before[at, :].astype(FULL)
        _, normed, inverse = normalize(row, 1.0, 0.0)
        result = stream[at] + normalize_back(value, normed, inverse, gain1)
        stream[at] = result
        low = result.astype(LOW)
        sums_into(split, 0, at, (value * normed, value))
        return low

    def meanwhile():
        if plan.inside:
            last = reduces["qkv"]
            last.compute(last.mid, mover.shard)
        finish("up")
        finish("out")

    def halfway():
        if plan.inside:
            reduces["qkv"].fold_blocks(3, 1)
            if plan.final:
                reduces["qkv"].spread()

    if plan.inside:
        reduces["qkv"].begin_blocks()
    two.eager(qkv_part, to_following, meanwhile, halfway)
    if plan.joined:
        late_held[0, 0:8, :] = jnp.zeros((8, late_held.shape[2]), FULL)
        late_held[0, 0:2, :] = split[0:2, :]
        late_held[0, 8:16, :] = local[...]
        final.step()
    if plan.inside:
        reduces["qkv"].fold_blocks(2, 0)
        if plan.final:
            reduces["qkv"].finish()
        else:
            mover.stay(reduces["qkv"].mid, mid_out)
    if plan.joined:
        final.step()
    two.have_mate_own()
    two.have_other()
    if plan.joined:
        final.step()
        final.step()
    two.have_mate_other()
    if plan.joined:
        final.step()
    for name in ("down", "up", "out"):
        if name in reduces:
            reduces[name].done()
    if late:
        late.done()
    if plan.inside and plan.final:
        reduces["qkv"].done()
    if plan.joined:
        final.step()
        totals[...] = early.value()
        last_value = final.value()
        for row in range(2):
            at = row * len(everything)
            totals[at : at + 1, :] = last_value[row : row + 1, :]
        at = tops + len(everything)
        totals[at : at + 1, :] = last_value[9:10, :]
    if not plan.inside:
        for name, (lhs, rhs) in {
            "down": (grad, hidden),
            "up": (second, pre_grad),
            "out": (attn_grad, heads),
            "qkv": (first, nat),
        }.items():
            full = Reduce(mover, (wholes[name],) * 4, None, lhs, rhs)
            full.compute(wholes[name], 0)
    mover.settle()


def gather_outputs_kernel(layers, *refs):
    count = layers * len(NAMES)
    parts, token_grads, mixed, totals = refs[:count], refs[count], refs[count + 1], refs[count + 2]
    outs, work = refs[count + 3 : count + 17], refs[count + 17 : -2]
    into, out_of = refs[-2:]
    coming, going = [], []
    pairs = [(mixed, work[4], outs[4].at[0])]
    for index in range(len(NAMES)):
        for layer in range(layers):
            pairs.append(
                (parts[index * layers + layer], work[index].at[layer], outs[index].at[layer])
            )
    for i, (source, stage, _) in enumerate(pairs):
        coming.append(pltpu.make_async_copy(source, stage, into.at[i]))
        coming[-1].start()
    outs[5][0] = token_grads[...].astype(FULL)
    for row, out in enumerate(outs[6:12]):
        out[...] = totals[row * layers : (row + 1) * layers, 0 : out.shape[1]]
    for row, out in enumerate(outs[12:14]):
        row = row + 8
        out[...] = totals[row * layers : (row + 1) * layers, 0 : out.shape[1]]
    for i, (_, stage, target) in enumerate(pairs):
        coming[i].wait()
        going.append(pltpu.make_async_copy(stage, target, out_of.at[i]))
        going[-1].start()
    for copy in going:
        copy.wait()


def gather_outputs(done, token_grads, mixed, totals, layers, widths):
    rows, width = token_grads.shape
    parts = [done[name, layer] for name in NAMES for layer in range(layers)]
    hbm, whole = pl.BlockSpec(memory_space=HBM), lambda shape: pl.BlockSpec(
        shape, lambda i: (0,) * len(shape)
    )
    shapes = [(layers,) + done[name, 0].shape for name in NAMES] + [(1, rows, width)] * 2
    types = [FULL] * 4 + [LOW, FULL]
    small = [(layers, width)] * 6 + [(layers, count) for count in widths]
    copies = len(parts) + 1
    return pl.pallas_call(
        functools.partial(gather_outputs_kernel, layers),
        grid=(1,),
        in_specs=[hbm] * len(parts) + [whole(token_grads.shape), hbm, whole(totals.shape)],
        out_specs=[hbm] * 5 + [whole(shape) for shape in shapes[5:] + small],
        out_shape=[jax.ShapeDtypeStruct(*pair) for pair in zip(shapes, types)]
        + [jax.ShapeDtypeStruct(shape, FULL) for shape in small],
        scratch_shapes=[VMEM(shape, FULL) for shape in shapes[:4]]
        + [VMEM((rows, width), LOW)]
        + [pltpu.SemaphoreType.DMA((copies,)), pltpu.SemaphoreType.DMA((copies,))],
        compiler_params=pltpu.CompilerParams(vmem_limit_bytes=60 * 2**20),
        name="gather_outputs",
    )(*parts, token_grads, mixed, totals)


class BackPlan:
    def __init__(self, layer, layers, inside):
        self.inside, self.layer = inside, layer
        self.last, self.final = layer == layers - 1, layer == 0
        self.late = inside and not self.last
        self.joined = inside and self.final
        self.others = layers - 1 if self.joined else 0


def back_layer(source, x, live, gain2, gain1, saved, late, others, plan, size, sizes, ident):
    rows, width = source.shape
    count = sizes[0]
    slope, w_down, w_up = saved[:3]
    hidden, joint, attn = slope.shape[1], saved[12].shape[1], saved[6].shape[1]
    slots, span = count * rows, rows // 4
    tile = 256 if slots % 256 == 0 else PAD
    wide = max(width, hidden, joint)
    half = width // 2
    block = half // count
    columns = {"qkv": joint, "out": attn, "up": hidden, "down": hidden}
    inputs = [(source, VMEM)] + ([] if plan.last else [(x, VMEM)])
    inputs += [(live, SMEM), (gain2, HBM), (gain1, HBM)]
    inputs += [(value, HBM) for value in saved]
    if plan.late:
        inputs.append((late, HBM))
    for pair in others[: plan.others]:
        inputs += [(value, VMEM) for value in pair]
    outputs = [((span, width), FULL, VMEM), ((rows, width), LOW, VMEM)]
    names = [name for name in NAMES if plan.inside and (name != "qkv" or plan.final)]
    outputs += [((block, columns[name]), FULL, VMEM) for name in names]
    if plan.inside and not plan.final:
        outputs.append(((half, joint), LOW, HBM))
    if plan.late:
        outputs.append(((block, joint), FULL, VMEM))
    depth = 8 * (plan.others + 1)
    if plan.joined:
        outputs.append(((depth + 8, wide), FULL, VMEM))
    else:
        outputs += [((8, wide), FULL, VMEM)] * 2
    if not plan.inside:
        outputs += [((width, columns[name]), LOW, VMEM) for name in NAMES]
    scratch = [VMEM(value.shape, value.dtype) for value in saved]
    scratch[13] = VMEM((span, width), saved[13].dtype)
    if plan.last:
        scratch.append(VMEM((rows, width), LOW))
    scratch += [
        VMEM((rows, hidden), LOW),
        VMEM((rows, width), LOW),
        VMEM((attn, rows), LOW),
        VMEM((joint, rows), LOW),
        VMEM((rows, joint), LOW),
    ]
    scratch += attend_back_buffers(size, count, rows, tile)
    scratch += round_buffers(rows, width) + round_buffers(rows, width)
    if plan.inside:
        for name in ("down", "up", "out", "qkv"):
            scratch += reduce_buffers(half, columns[name], count)
    if plan.late:
        scratch += [VMEM((half, joint), LOW), VMEM((count - 1, block, joint), LOW)]
    scratch.append(VMEM((16, slots), LOW))
    scratch += [VMEM(value.shape, value.dtype) for value in (gain2, gain1)]
    assert 2 * (plan.others + 1) <= 8
    if plan.joined:
        scratch += [VMEM((8, wide), FULL)] * 2
        scratch += [
            VMEM((6, depth + 8, wide), FULL),
            VMEM((5, depth + 8, wide), FULL),
            VMEM((6, 16, wide), FULL),
            VMEM((5, 16, wide), FULL),
        ]
    results = run(
        functools.partial(back_kernel, plan, size, tile),
        "back_layer",
        ident,
        inputs,
        outputs,
        scratch,
        3 * (count - 1) + 2 * ROUND_COPIES + 6 * count + 10 + count,
        len(saved) + 4,
        sizes,
        58,
        6 * rows * width * (2 * hidden + attn + joint) + 10 * slots * slots * 256,
    )
    return results[:2], names, results[2:]


def shards(
    tokens,
    block_tokens,
    ln1_gain,
    ln1_bias,
    w_qkv,
    b_qv,
    w_out,
    b_out,
    ln2_gain,
    ln2_bias,
    w_up,
    b_up,
    w_down,
    b_down,
    cotangent,
):
    images, capacity, width = tokens.shape
    assert images == 1
    layers = w_qkv.shape[0]
    size = HEAD_DIM
    ctx_count = lax.axis_size("ctx")
    ctx_place = lax.axis_index("ctx")
    joint_width = w_qkv.shape[2]
    heads = joint_width // (3 * size)
    assert heads == ctx_count
    attn_width = heads * size
    hidden_width = w_up.shape[2]
    weights = {"qkv": w_qkv, "out": w_out, "up": w_up, "down": w_down}
    sizes = (ctx_count, lax.axis_size("shard"))
    inside = sizes == (4, 2)
    gathered = {}
    if not inside:
        for name, value in weights.items():
            for layer in range(layers):
                gathered[name, layer] = gather_weight(value[layer])[0]
    source, stream = tokens[0], None
    saved = []
    for layer in range(layers):
        last = layer == layers - 1
        result, following, kept = forward_layer(
            source,
            stream,
            block_tokens,
            (b_out, ln2_gain, ln2_bias, b_down, ln1_gain, ln1_bias, b_up, b_qv),
            gathered,
            weights,
            Plan(layer, last, inside),
            last,
            size,
            sizes,
            1 + layer,
        )
        before = stream if layer else source
        first = source if layer else kept[8]
        saved.append((before, first) + tuple(kept[:8]))
        source, stream = following, result
    mixed = source

    done, packs = {}, {}
    source, stream, late = cotangent[0], None, None
    for layer in reversed(range(layers)):
        before, first, qkv, head_out, lse, heads_low, middle, second, hidden, slope = saved[layer]
        plan = BackPlan(layer, layers, inside)
        whole = {name: gathered[name, layer] for name in NAMES}
        near = [slope, whole["down"], whole["up"], middle, hidden, second, whole["out"]]
        near += [heads_low, qkv, head_out, lse, first, whole["qkv"], before]
        others = [packs[key] for key in sorted(packs)]
        (stream, source), names, rest = back_layer(
            source, stream, block_tokens, ln2_gain, ln1_gain, near, late, others, plan, size, sizes, 1 + layers + layer
        )
        rest = iter(rest)
        for name in names:
            done[name, layer] = next(rest)
        if plan.inside and not plan.final:
            late = next(rest)
        if plan.late:
            done["qkv", layer + 1] = next(rest)
        if plan.joined:
            totals = next(rest)
        else:
            packs[layer] = (next(rest), next(rest))
        if not inside:
            for name in NAMES:
                value = next(rest)
                done[name, layer] = scatter_weight(
                    lambda start, count, value=value: rows_of(value, start, count).astype(FULL),
                    width,
                )
    if not inside:
        split = total_over(("tp",), jnp.stack([packs[l][0] for l in range(layers)], axis=1))
        local = jnp.stack([packs[l][1] for l in range(layers)], axis=1)
        totals = total_over(("shard", "ctx"), jnp.concatenate([split, local[:2]]))
        totals = totals.reshape(10 * layers, -1)
    pairs = b_qv.shape[1]
    outs = gather_outputs(done, source, mixed, totals, layers, (hidden_width, pairs))
    g_qkv, g_out, g_up, g_down, mixed, token_grads = outs[:6]
    g_ln1_gain, g_ln1_bias, g_ln2_gain, g_ln2_bias, g_b_out, g_b_down, g_b_up, g_b_qv = outs[6:]
    return (
        mixed,
        token_grads,
        g_ln1_gain,
        g_ln1_bias,
        g_qkv,
        g_b_qv,
        g_out,
        g_b_out,
        g_ln2_gain,
        g_ln2_bias,
        g_up,
        g_b_up,
        g_down,
        g_b_down,
    )


def solution(mesh):
    split_rows = P(None, ("shard", "ctx"), "tp")
    split_tokens = P("shard", "ctx", None)
    return jax.shard_map(
        shards,
        mesh=mesh,
        in_specs=(
            split_tokens,
            P("shard", None),
            P(),
            P(),
            split_rows,
            P(None, "tp"),
            split_rows,
            P(),
            P(),
            P(),
            split_rows,
            P(None, "tp"),
            split_rows,
            P(),
            split_tokens,
        ),
        out_specs=(
            split_tokens,
            split_tokens,
            P(),
            P(),
            split_rows,
            P(None, "tp"),
            split_rows,
            P(),
            P(),
            P(),
            split_rows,
            P(None, "tp"),
            split_rows,
            P(),
        ),
        check_vma=False,
    )
```

```python
import functools
import math

import jax
import jax.numpy as jnp
from jax import lax
from jax.experimental import pallas as pl
from jax.experimental.pallas import tpu as pltpu
from jax.sharding import PartitionSpec as P

HEAD_DIM = 64
EPSILON = 1e-06
NEG_LARGE = -1e30
LOW = jnp.bfloat16
FULL = jnp.float32
PAD = 128
MESH = pl.DeviceIdType.MESH
VMEM = pltpu.VMEM
HBM = pltpu.HBM
SMEM = pltpu.SMEM


def bits_of(axis):
    size = lax.axis_size(axis)
    assert size & (size - 1) == 0
    return [1 << i for i in range(size.bit_length() - 1)]


def swap(value, axis, bit):
    size = lax.axis_size(axis)
    return lax.ppermute(value, axis, [(i, i ^ bit) for i in range(size)])


def side_of(axis, bit):
    return (lax.axis_index(axis) // bit) % 2


def rows_of(value, start, count, axis=0):
    return lax.dynamic_slice_in_dim(value, start, count, axis)


def halve(axis, bits, partial, total):
    offset, span, received = jnp.int32(0), total, []

    def summed(start, count):
        value = partial(start, count)
        for got, base in received:
            value = value + rows_of(got, start - base, count).astype(FULL)
        return value

    for bit in bits:
        half = span // 2
        side = side_of(axis, bit)
        got = swap(summed(offset + (1 - side) * half, half).astype(LOW), axis, bit)
        offset = offset + side * half
        received.append((got, offset))
        span = half
    return summed(offset, span)


def double(axis, bits, value):
    for bit in bits:
        got = swap(value, axis, bit)
        first = side_of(axis, bit) == 0
        value = jnp.concatenate(
            [jnp.where(first, value, got), jnp.where(first, got, value)], axis=0
        )
    return value


def total_over(axes, value):
    for axis in axes:
        for bit in bits_of(axis):
            value = value + swap(value, axis, bit)
    return value


def ring(value, by):
    count = lax.axis_size("ctx")
    return lax.ppermute(value, "ctx", [(i, (i + by) % count) for i in range(count)])


def gather_weight(piece):
    count = lax.axis_size("ctx")
    place = lax.axis_index("ctx")
    ways = lax.axis_size("shard")
    blocks = [piece] + [ring(piece, by) for by in range(1, count)]
    whole = jnp.zeros((ways * count,) + piece.shape, piece.dtype)
    me = lax.axis_index("shard")
    for by, block in enumerate(blocks):
        at = (place - by) % count
        held = [(jnp.int32(0), block)]
        for bit in bits_of("shard"):
            held = held + [(other ^ bit, swap(value, "shard", bit)) for other, value in held]
        for other, value in held:
            whole = lax.dynamic_update_index_in_dim(whole, value, (me ^ other) * count + at, 0)
    return whole.reshape((ways * count * piece.shape[0],) + piece.shape[1:]), blocks[-1]


def scatter_weight(partial, total):
    count = lax.axis_size("ctx")
    place = lax.axis_index("ctx")
    mine = halve("shard", bits_of("shard")[::-1], partial, total).astype(LOW)
    mine = mine.reshape((count, mine.shape[0] // count) + mine.shape[1:])
    value = lax.dynamic_index_in_dim(mine, place, 0, False).astype(FULL)
    for by in range(1, count):
        given = lax.dynamic_index_in_dim(mine, (place + by) % count, 0, False)
        value = value + ring(given, by).astype(FULL)
    return value


def dot(left, right, contract):
    return lax.dot_general(
        left, right, ((contract[0], contract[1]), ((), ())), preferred_element_type=FULL
    )


def turned(value):
    return value.astype(FULL).T.astype(LOW)


def normalize(rows, gain, shift):
    row_mean = jnp.mean(rows, axis=-1, keepdims=True)
    centred = rows - row_mean
    inverse = lax.rsqrt(jnp.mean(centred * centred, axis=-1, keepdims=True) + EPSILON)
    normed = centred * inverse
    return (normed * gain + shift, normed, inverse)


def normalize_back(grad_out, normed, inverse, gain):
    scaled = grad_out * gain
    mean_grad = jnp.mean(scaled, axis=-1, keepdims=True)
    mean_cross = jnp.mean(scaled * normed, axis=-1, keepdims=True)
    return inverse * (scaled - mean_grad - normed * mean_cross)


def gelu_pair(value):
    spread = 0.5 * (1.0 + lax.erf(value * (0.5**0.5)))
    slope = spread + value * jnp.exp(-0.5 * value * value) * (1.0 / math.sqrt(2.0 * math.pi))
    return (value * spread).astype(LOW), slope.astype(LOW)


class Mover:
    def __init__(self, sizes, send, recv, local):
        self.ctx_count, self.shard_count = sizes
        self.send, self.recv, self.local = send, recv, local
        self.copies, self.here = [], []
        self.arrived = set()
        self.landed = set()
        self.ctx = lax.axis_index("ctx")
        self.shard = lax.axis_index("shard")

    def go(self, source, target, **device):
        index = len(self.copies)
        assert index < self.send.shape[0]
        copy = pltpu.make_async_remote_copy(
            src_ref=source,
            dst_ref=target,
            send_sem=self.send.at[index],
            recv_sem=self.recv.at[index],
            device_id=device,
            device_id_type=MESH,
        )
        copy.start()
        self.copies.append(copy)
        return index

    def stay(self, source, target):
        index = len(self.here)
        assert index < self.local.shape[0]
        copy = pltpu.make_async_copy(source, target, self.local.at[index])
        copy.start()
        self.here.append(copy)
        return index

    def near(self, *indices):
        for index in indices:
            if index not in self.landed:
                self.landed.add(index)
                self.here[index].wait()

    def take(self, index):
        if index not in self.arrived:
            self.arrived.add(index)
            self.copies[index].wait_recv()

    def flip(self, bits):
        place = self.ctx
        if bits & 1:
            place = place + 1 - 2 * lax.rem(self.ctx, 2)
        if bits & 2:
            place = place + 2 - 4 * (self.ctx // 2)
        return place

    def on(self, by):
        return lax.rem(self.ctx + by, self.ctx_count)

    def back(self, by):
        return lax.rem(self.ctx + self.ctx_count - by, self.ctx_count)

    def settle(self):
        for index, copy in enumerate(self.copies):
            self.take(index)
            copy.wait_send()
        self.near(*range(len(self.here)))


class Gather:
    def __init__(self, mover, source, target):
        self.mover, self.source, self.target = mover, source, target
        self.over = []

    def start(self):
        self.start_line()
        self.start_over()

    def start_line(self):
        mover = self.mover
        mine, there = self.source, self.block(mover.ctx)
        self.far = mover.go(mine, there, ctx=mover.flip(2))
        self.close = mover.go(mine, there, ctx=mover.flip(1))

    def start_over(self):
        mover = self.mover
        mine, there = self.source, self.block(mover.ctx)
        self.over.append(mover.go(mine, there, shard=1 - mover.shard))
        self.own = mover.stay(mine, there)

    def block(self, ctx):
        mover = self.mover
        rows = self.source.shape[0]
        start = (mover.shard * mover.ctx_count + ctx) * rows
        return self.target.at[pl.ds(pl.multiple_of(start, rows), rows)]

    def pass_on(self, stage):
        mover = self.mover
        if stage == 1:
            mover.take(self.far)
            rows = self.block(mover.flip(2))
            self.passed = mover.go(rows, rows, ctx=mover.flip(1))
        elif stage == 2:
            mover.take(self.close)
            rows = self.block(mover.flip(1))
        else:
            mover.take(self.passed)
            rows = self.block(mover.flip(3))
        self.over.append(mover.go(rows, rows, shard=1 - mover.shard))

    def have(self):
        for copy in self.over:
            self.mover.take(copy)
        self.mover.near(self.own)


class Reduce:
    def __init__(self, mover, buffers, out, lhs, rhs):
        self.mover, self.out, self.lhs, self.rhs = mover, out, lhs, rhs
        self.give, self.got, self.mid, self.line = buffers
        self.half = self.give.shape[0]
        self.block = self.half // mover.ctx_count

    def compute(self, target, shard):
        chunk = min(256, self.half)

        def step(i, carry):
            at = pl.ds(pl.multiple_of(shard * self.half + i * chunk, chunk), chunk)
            here = pl.ds(pl.multiple_of(i * chunk, chunk), chunk)
            target[here, :] = dot(self.lhs[:, at], self.rhs[...], ((0,), (0,))).astype(LOW)
            return carry

        lax.fori_loop(0, self.half // chunk, step, 0)

    def begin(self):
        mover = self.mover
        self.compute(self.give, 1 - mover.shard)
        self.cross = mover.go(self.give, self.got, shard=1 - mover.shard)
        self.compute(self.mid, mover.shard)

    def fold(self):
        self.mover.take(self.cross)
        self.mid[...] = (self.mid[...].astype(FULL) + self.got[...].astype(FULL)).astype(LOW)

    def begin_blocks(self):
        mover = self.mover
        self.blocks = {}
        for bits in (3, 1, 2, 0):
            ctx = mover.flip(bits)
            at = pl.ds(pl.multiple_of(ctx * self.block, self.block), self.block)
            start = pl.multiple_of((1 - mover.shard) * self.half + ctx * self.block, self.block)
            lhs = self.lhs[:, pl.ds(start, self.block)]
            self.give[at, :] = dot(lhs, self.rhs[...], ((0,), (0,))).astype(LOW)
            self.blocks[bits] = mover.go(
                self.give.at[at], self.got.at[at], shard=1 - mover.shard
            )

    def fold_blocks(self, *which):
        mover = self.mover
        for bits in which:
            mover.take(self.blocks[bits])
            ctx = mover.flip(bits)
            at = pl.ds(pl.multiple_of(ctx * self.block, self.block), self.block)
            self.mid[at, :] = (
                self.mid[at, :].astype(FULL) + self.got[at, :].astype(FULL)
            ).astype(LOW)

    def rows(self, ctx):
        return self.mid.at[pl.ds(pl.multiple_of(ctx * self.block, self.block), self.block)]

    def spread(self):
        mover = self.mover
        self.first = mover.go(self.rows(mover.flip(3)), self.line.at[1], ctx=mover.flip(1))
        self.second = mover.go(self.rows(mover.flip(1)), self.line.at[0], ctx=mover.flip(1))

    def finish(self):
        mover = self.mover
        mover.take(self.first)
        rows = self.rows(mover.flip(2))
        rows[...] = (rows[...].astype(FULL) + self.line[1].astype(FULL)).astype(LOW)
        self.third = mover.go(rows, self.line.at[2], ctx=mover.flip(2))

    def done(self):
        self.mover.take(self.second)
        self.mover.take(self.third)
        value = self.rows(self.mover.ctx)[...].astype(FULL)
        self.out[...] = value + self.line[0].astype(FULL) + self.line[2].astype(FULL)


def reduce_buffers(half, width, count):
    return [
        VMEM((half, width), LOW),
        VMEM((half, width), LOW),
        VMEM((half, width), LOW),
        VMEM((count - 1, half // count, width), LOW),
    ]


def greet(mover, shard):
    barrier = pltpu.get_barrier_semaphore()
    peers = [dict(ctx=mover.on(by)) for by in range(1, mover.ctx_count)]
    peers += [dict(tp=peer) for peer in tp_peers()]
    if shard:
        peers.append(dict(shard=1 - mover.shard))
    for peer in peers:
        pl.semaphore_signal(barrier, inc=1, device_id=peer, device_id_type=MESH)
    pl.semaphore_wait(barrier, len(peers))


def tp_peers():
    place = lax.axis_index("tp")
    core, far = lax.rem(place, 2), place // 2
    return place + 1 - 2 * core, place + 2 - 4 * far


def run(kernel, name, ident, inputs, outputs, scratch, remote, local, sizes, vmem, flops):
    n_in, n_out, n_scratch = len(inputs), len(outputs), len(scratch)

    def body(*refs):
        ins, outs = refs[:n_in], refs[n_in : n_in + n_out]
        work = refs[n_in + n_out :]
        mover = Mover(sizes, *work[n_scratch:])
        kernel(mover, ins, outs, work[:n_scratch])

    return pl.pallas_call(
        body,
        in_specs=[pl.BlockSpec(memory_space=space) for _, space in inputs],
        out_specs=[pl.BlockSpec(memory_space=space) for _, _, space in outputs],
        out_shape=[jax.ShapeDtypeStruct(shape, dtype) for shape, dtype, _ in outputs],
        scratch_shapes=list(scratch)
        + [
            pltpu.SemaphoreType.DMA((remote,)),
            pltpu.SemaphoreType.DMA((remote,)),
            pltpu.SemaphoreType.DMA((local,)),
        ],
        compiler_params=pltpu.CompilerParams(
            collective_id=ident, has_side_effects=True, vmem_limit_bytes=vmem * 2**20
        ),
        cost_estimate=pl.CostEstimate(flops=flops, bytes_accessed=2**24, transcendentals=0),
        name=name,
    )(*[value for value, _ in inputs])


def order_of(block, count):
    return (block + count - 1) % count


def tiles_of(count, capacity, tile):
    ends = [-(-(p + 1) * capacity // tile) for p in range(count)]
    return list(zip([0] + ends[:-1], ends))


def parts_of(capacity):
    middle = capacity // 2 // PAD * PAD
    return [(0, middle), (middle, capacity)] if middle else [(0, capacity)]


def tile_at(t, tile):
    return pl.ds(pl.multiple_of(t * tile, tile), tile)


def turned_product(left, right, bias, target):
    def step(i, carry):
        at = pl.ds(pl.multiple_of(i * PAD, PAD), PAD)
        value = jnp.dot(left[at, :], right[...], preferred_element_type=FULL)
        if bias is not None:
            value = value + bias[0:1, :]
        target[:, at] = turned(value.astype(LOW))
        return carry

    lax.fori_loop(0, left.shape[0] // PAD, step, 0)


def head_rows(ref, head, width):
    return ref.at[pl.ds(pl.multiple_of(head * width, 16), width)]


def attend_part(size, tile, mover, joint, bias, heads, qkv, o_ref, lse, work, after_send, begun, between):
    k_ref, q_ref, v_ref, low_ref, score_ref, top_ref = work
    count, width, capacity = qkv.shape
    slots = count * capacity
    sent = [None] + [
        mover.go(head_rows(joint, mover.on(by), width), qkv.at[by], ctx=mover.on(by))
        for by in range(1, count)
    ]
    after_send()
    qkv[0] = head_rows(joint, mover.ctx, width)[...]
    q_ref[size:PAD, :] = jnp.concatenate(
        [jnp.ones((16, slots), LOW), jnp.zeros((PAD - size - 16, slots), LOW)], axis=0
    )

    def prepare(r):
        here = slice(r * capacity, (r + 1) * capacity)
        p = order_of(r, count)
        q_ref[0:size, p * capacity : (p + 1) * capacity] = (
            qkv[r, 0:size, :] * (size**-0.5)
        ).astype(LOW)
        v_ref[:, here] = qkv[r, 2 * size : 3 * size, :]
        keys = jnp.concatenate(
            [qkv[r, size : 2 * size, :], bias[:, here], jnp.zeros((PAD - size - 16, capacity), LOW)],
            axis=0,
        )
        k_ref[here, :] = turned(keys)

    prepare(0)
    for by in range(1, count):
        mover.take(sent[by])
        prepare(by)

    begun()
    last = slots // tile - 1
    assert last % 2 == 1

    def phase(t, now, following, then):
        at, ahead = tile_at(t, tile), tile_at(following, tile)
        top = top_ref[now, 0:1, :]
        total = jnp.zeros((1, tile), FULL)
        summed = jnp.zeros((size, tile), FULL)
        new_top = jnp.full((1, tile), NEG_LARGE, FULL)
        for r in range(count):
            here = slice(r * capacity, (r + 1) * capacity)
            scores = jnp.dot(k_ref[here, :], q_ref[:, ahead], preferred_element_type=FULL)
            score_ref[then, here, :] = scores
            new_top = jnp.maximum(new_top, jnp.max(scores, axis=0, keepdims=True))
            weights = jnp.exp(score_ref[now, here, :] - top)
            total = total + jnp.sum(weights, axis=0, keepdims=True)
            summed = summed + jnp.dot(
                v_ref[:, here], weights.astype(LOW), preferred_element_type=FULL
            )
        top_ref[then] = jnp.broadcast_to(new_top, (8, tile))
        out = summed / total
        o_ref[:, at] = out
        low_ref[:, at] = out.astype(LOW)
        lse[:, at] = jnp.broadcast_to(top + jnp.log(total), (8, tile))

    def step(i, carry):
        phase(2 * i, 0, 2 * i + 1, 1)
        phase(2 * i + 1, 1, jnp.minimum(2 * i + 2, last), 0)
        return carry

    scores = jnp.dot(k_ref[...], q_ref[:, 0:tile], preferred_element_type=FULL)
    score_ref[0] = scores
    top_ref[0] = jnp.broadcast_to(jnp.max(scores, axis=0, keepdims=True), (8, tile))
    arriving = []
    for p, (low, high) in enumerate(tiles_of(count, capacity, 2 * tile)):
        lax.fori_loop(low, high, step, 0)
        done = low_ref.at[:, p * capacity : (p + 1) * capacity]
        if p < count - 1:
            there = head_rows(heads, mover.ctx, size)
            arriving.append(mover.go(done, there, ctx=mover.back(p + 1)))
        else:
            head_rows(heads, mover.ctx, size)[...] = low_ref[:, p * capacity : (p + 1) * capacity]
        between(p + 1)
    for copy in arriving:
        mover.take(copy)


def attend_back_part(size, tile, mover, parts, bias, qkv, o_ref, lse, grads, work, ready, waiting, begun, between):
    k_ref, v_ref, q_ref, do_ref, nat_ref, delta_ref, dq_ref, dk_ref, dv_ref, got, back, score_ref, grad_ref = work
    count, width, capacity = qkv.shape
    slots = count * capacity
    sent = [None] + [
        mover.go(head_rows(parts, mover.on(by), size), got.at[by], ctx=mover.on(by))
        for by in range(1, count)
    ]
    got[0] = head_rows(parts, mover.ctx, size)[...]
    waiting()
    ready()
    q_ref[size:PAD, :] = jnp.concatenate(
        [jnp.ones((16, slots), LOW), jnp.zeros((PAD - size - 16, slots), LOW)], axis=0
    )
    do_ref[size:PAD, :] = jnp.zeros((PAD - size, slots), LOW)
    dq_ref[...] = jnp.zeros_like(dq_ref)
    for r in range(count):
        here = slice(r * capacity, (r + 1) * capacity)
        pad = jnp.zeros((PAD - size - 16, capacity), LOW)
        k_ref[here, :] = turned(
            jnp.concatenate([qkv[r, size : 2 * size, :], bias[:, here], pad], axis=0)
        )
        v_ref[here, :] = turned(
            jnp.concatenate(
                [qkv[r, 2 * size : 3 * size, :], jnp.zeros((PAD - size, capacity), LOW)], axis=0
            )
        )
    for r in range(count):
        if r:
            mover.take(sent[r])
        p = order_of(r, count)
        at = slice(p * capacity, (p + 1) * capacity)
        scaled = (qkv[r, 0:size, :] * (size**-0.5)).astype(LOW)
        dout = got[r]
        q_ref[0:size, at] = scaled
        do_ref[0:size, at] = dout
        nat_ref[at, :] = turned(jnp.concatenate([scaled, dout], axis=0))
        delta = jnp.sum(dout.astype(FULL) * o_ref[:, at], axis=0, keepdims=True)
        delta_ref[:, at] = jnp.broadcast_to(delta, (8, capacity))

    begun()
    last = slots // tile - 1
    assert last % 2 == 1
    tiles = tiles_of(count, capacity, 2 * tile)
    arriving = []
    mine = head_rows(grads, mover.ctx, width)
    for turn, r in enumerate(list(range(1, count)) + [0]):
        here = slice(r * capacity, (r + 1) * capacity)
        dk_ref[...] = jnp.zeros_like(dk_ref)
        dv_ref[...] = jnp.zeros_like(dv_ref)

        def ready_scores(t, then, low, high, r=r):
            ahead = tile_at(t, tile)
            rows = slice(r * capacity + low, r * capacity + high)
            score_ref[then, low:high, :] = jnp.dot(
                k_ref[rows, :], q_ref[:, ahead], preferred_element_type=FULL
            )
            grad_ref[then, low:high, :] = jnp.dot(
                v_ref[rows, :], do_ref[:, ahead], preferred_element_type=FULL
            )

        def phase(t, now, following, then, r=r):
            at = tile_at(t, tile)
            query_grad = jnp.zeros((size, tile), FULL)
            for low, high in parts_of(capacity):
                ready_scores(following, then, low, high)
                chance = jnp.exp(score_ref[now, low:high, :] - lse[0:1, at])
                score_grad = (
                    chance * (grad_ref[now, low:high, :] - delta_ref[0:1, at])
                ).astype(LOW)
                query_grad = query_grad + jnp.dot(
                    qkv[r, size : 2 * size, low:high], score_grad, preferred_element_type=FULL
                )
                dk_ref[low:high, :] += jnp.dot(
                    score_grad, nat_ref[at, :], preferred_element_type=FULL
                )
                dv_ref[low:high, :] += jnp.dot(
                    chance.astype(LOW), nat_ref[at, :], preferred_element_type=FULL
                )
            dq_ref[:, at] += query_grad

        def step(i, carry, phase=phase):
            phase(2 * i, 0, 2 * i + 1, 1)
            phase(2 * i + 1, 1, jnp.minimum(2 * i + 2, last), 0)
            return carry

        ready_scores(0, 0, 0, capacity)
        if r:
            lax.fori_loop(0, tiles[-1][1], step, 0)
        else:
            for p, (low, high) in enumerate(tiles):
                lax.fori_loop(low, high, step, 0)
                at = slice(p * capacity, (p + 1) * capacity)
                value = (dq_ref[:, at] * (size**-0.5)).astype(LOW)
                if p < count - 1:
                    back[p + 1, 0:size, :] = value
                    arriving.append(
                        mover.go(
                            back.at[p + 1, 0:size], mine.at[0:size], ctx=mover.back(p + 1)
                        )
                    )
                else:
                    mine[0:size, :] = value
        keys = dk_ref[...].T[0:size].astype(LOW)
        values = dv_ref[...].T[size : 2 * size].astype(LOW)
        if r:
            back[r, size : 2 * size, :] = keys
            back[r, 2 * size : 3 * size, :] = values
            arriving.append(
                mover.go(
                    back.at[r, size : 3 * size], mine.at[size : 3 * size], ctx=mover.back(r)
                )
            )
        else:
            mine[size : 2 * size, :] = keys
            mine[2 * size : 3 * size, :] = values
        between(turn)
    for copy in arriving:
        mover.take(copy)


def attend_back_buffers(size, count, capacity, tile):
    slots = count * capacity
    return [
        VMEM((slots, PAD), LOW),
        VMEM((slots, PAD), LOW),
        VMEM((PAD, slots), LOW),
        VMEM((PAD, slots), LOW),
        VMEM((slots, PAD), LOW),
        VMEM((8, slots), FULL),
        VMEM((size, slots), FULL),
        VMEM((capacity, PAD), FULL),
        VMEM((capacity, PAD), FULL),
        VMEM((count, size, capacity), LOW),
        VMEM((count, 3 * size, capacity), LOW),
        VMEM((2, capacity, tile), FULL),
        VMEM((2, capacity, tile), FULL),
    ]


class Round:
    def __init__(self, mover, rows, full, buffers):
        place = lax.axis_index("tp")
        core, far = lax.rem(place, 2), place // 2
        self.mover, self.full = mover, full
        self.give, self.ra, self.passing, self.rb, self.keep = buffers
        self.span = rows // 4
        self.half = self.span // 2
        self.mate, self.far = tp_peers()

        def quarter(c, f):
            return (c * 2 + f) * self.span

        self.own, self.other = quarter(core, far), quarter(core, 1 - far)
        self.mate_own, self.mate_other = quarter(1 - core, far), quarter(1 - core, 1 - far)

    def rows(self, start, count=None):
        return pl.ds(pl.multiple_of(start, 16), count or self.span)

    def hand(self, slot, value):
        self.give[slot] = value.astype(LOW)
        return self.mover.go(self.give.at[slot], self.ra.at[slot], tp=self.mate)

    def onward(self, value, index):
        self.mover.take(index)
        self.passing[...] = (value + self.ra[1].astype(FULL)).astype(LOW)
        return [
            self.mover.go(self.passing.at[at], self.rb.at[at], tp=self.far)
            for at in (pl.ds(0, self.half), pl.ds(self.half, self.half))
        ]

    def close(self, far_copies, index, finish, halfway=None):
        self.mover.take(index)
        self.keep[...] += self.ra[0].astype(FULL)
        self.to_far, self.to_mate = [], []
        for c in range(2):
            at = pl.ds(c * self.half, self.half)
            self.mover.take(far_copies[c])
            low = finish(at, self.keep[at] + self.rb[at].astype(FULL))
            mine = self.full.at[self.rows(self.own + c * self.half, self.half)]
            mine[...] = low
            self.to_far.append(self.mover.go(mine, mine, tp=self.far))
            self.to_mate.append(self.mover.go(mine, mine, tp=self.mate))
            if halfway and c == 0:
                halfway()

    def eager(self, make, finish, meanwhile=None, halfway=None):
        first = self.hand(1, make(self.mate_other))
        copies = self.onward(make(self.other), first)
        second = self.hand(0, make(self.mate_own))
        self.keep[...] = make(self.own)
        if meanwhile:
            meanwhile()
        self.close(copies, second, finish, halfway)

    def after(self, before, make, finish, meanwhile=None, halfway=None):
        before.have_mate_own()
        second = self.hand(0, make(self.mate_own))
        self.keep[...] = make(self.own)
        before.have_other()
        value = make(self.other)
        before.have_mate_other()
        first = self.hand(1, make(self.mate_other))
        copies = self.onward(value, first)
        if meanwhile:
            meanwhile()
        self.close(copies, second, finish, halfway)

    def have_mate_own(self):
        for copy in self.to_mate:
            self.mover.take(copy)

    def have_other(self):
        self.passed = []
        for c in range(2):
            self.mover.take(self.to_far[c])
            rows = self.full.at[self.rows(self.other + c * self.half, self.half)]
            self.passed.append(self.mover.go(rows, rows, tp=self.mate))

    def have_mate_other(self):
        for copy in self.passed:
            self.mover.take(copy)

    def have(self):
        self.have_mate_own()
        self.have_other()
        self.have_mate_other()


ROUND_COPIES = 10


def round_buffers(rows, width):
    span = rows // 4
    return [
        VMEM((2, span, width), LOW),
        VMEM((2, span, width), LOW),
        VMEM((span, width), LOW),
        VMEM((span, width), LOW),
        VMEM((span, width), FULL),
    ]


NAMES = ("qkv", "out", "up", "down")


def layer_kernel(plan, last, size, tile, mover, ins, outs, work):
    ins, outs, work = iter(ins), iter(outs), iter(work)
    source = next(ins)
    x_ref = None if plan.entry else next(ins)
    live_ref = next(ins)
    far_params = [next(ins) for _ in range(8)]
    stream, following = next(outs), next(outs)
    far_qkv, far_o, far_lse, far_heads, far_middle, far_second, far_hidden, far_slope = [
        next(outs) for _ in range(8)
    ]
    far_first = next(outs) if plan.entry else None
    joint, nat, heads, qkv, o_ref, lse, middle, second, hidden, slope = [
        next(work) for _ in range(10)
    ]
    first = next(work) if plan.entry else source
    attend_work = [next(work) for _ in range(6)]
    one_work, two_work = [next(work) for _ in range(5)], [next(work) for _ in range(5)]
    rows = source.shape[0]
    bias, qkv_bias = next(work), next(work)
    params = [next(work) for _ in range(8)]
    whole = {name: next(work) for name in NAMES}
    gathers, loads = {}, {}
    for name in plan.held:
        loads[name] = (next(ins), whole[name])
    for name in plan.own:
        gathers[name, 0] = Gather(mover, next(ins).at[plan.layer], whole[name])
    kept_ahead = {name: next(outs) for name in plan.ahead}
    for name in plan.ahead:
        gathers[name, 1] = Gather(mover, next(ins).at[plan.layer + 1], next(work))
    kept = {name: next(outs) for name in plan.own}

    greet(mover, bool(gathers))
    if plan.entry:
        gathers_first = [key for key in [("qkv", 0)] if key in gathers]
        for key in gathers_first:
            gathers[key].start()
    param_loads = [mover.stay(there, here) for there, here in zip(far_params, params)]
    loads = {name: mover.stay(*pair) for name, pair in loads.items()}

    def have(name):
        if name in loads:
            mover.near(loads[name])
        else:
            gathers[name, 0].have()
            mover.stay(whole[name], kept[name])
        return whole[name]

    def begin(keys):
        for key in keys:
            if key in gathers:
                gathers[key].start()

    def pass_on(keys, stage):
        for key in keys:
            if key in gathers:
                gathers[key].pass_on(stage)

    def pass_all(keys):
        for stage in (1, 2, 3):
            pass_on(keys, stage)

    mover.near(*param_loads)
    layer, after = plan.layer, min(plan.layer + 1, params[0].shape[0] - 1)

    def row(index, layer=layer):
        return params[index][...].astype(FULL)[layer : layer + 1]

    b_out, gain2, shift2, b_down, b_up = row(0), row(1), row(2), row(3), row(6)
    gain1, shift1, gain0, shift0 = row(4, after), row(5, after), row(4), row(5)
    qkv_bias[...] = joint_bias(row(7), size, joint.shape[0])
    key_bias(mover, live_ref, bias)
    one = Round(mover, rows, second, one_work)
    two = Round(mover, rows, following, two_work)
    if plan.entry:
        chunk = rows // 5 if rows % 80 == 0 else rows

        def norm_step(i, carry):
            at = pl.ds(pl.multiple_of(i * chunk, 16), chunk)
            value = normalize(source[at, :].astype(FULL), gain0, shift0)[0]
            first[at, :] = value.astype(LOW)
            return carry

        lax.fori_loop(0, rows // chunk, norm_step, 0)
        mover.stay(first, far_first)
        pass_all([("qkv", 0)])
        begin([("out", 0), ("up", 0)])
        turned_product(first, have("qkv"), qkv_bias, joint)
    else:
        turned_product(first, have("qkv"), qkv_bias, joint)

    ahead = [("qkv", 1), ("out", 1), ("up", 1)]

    def after_send():
        if plan.entry:
            pass_all([("out", 0), ("up", 0)])
        else:
            for name in plan.own:
                gathers[name, 0].start_over()

    def begun():
        if plan.entry:
            begin([("down", 0)])
        else:
            for name in plan.own:
                gathers[name, 0].start_line()

    def between(p):
        if p > 1:
            pass_on([("down", 0)], p - 1)
        if p == 4:
            begin(ahead)

    attend_part(
        size, tile, mover, joint, bias, heads, qkv, o_ref, lse, attend_work, after_send, begun, between
    )
    nat[...] = turned(heads[...])
    w_out = have("out")

    def out_part(start):
        return dot(nat[one.rows(start), :], w_out[...], ((1,), (1,)))

    def to_second(at, value):
        if plan.entry:
            before = source[one.rows(one.own + at.start, at.size), :].astype(FULL)
        else:
            before = x_ref[at]
        value = before + value + b_out
        middle[at] = value
        return normalize(value, gain2, shift2)[0].astype(LOW)

    def meanwhile():
        mover.stay(qkv, far_qkv)
        mover.stay(o_ref, far_o)
        mover.stay(lse, far_lse)
        mover.stay(nat, far_heads)

    one.eager(out_part, to_second, meanwhile, lambda: pass_on(ahead[:2], 1))
    pass_on(ahead[:2], 2)
    w_up, w_down = have("up"), have("down")

    def mlp_part(start):
        at = two.rows(start)
        pre = jnp.dot(second[at, :], w_up[...], preferred_element_type=FULL) + b_up
        low, low_slope = gelu_pair(pre)
        hidden[at, :] = low
        slope[at, :] = low_slope
        return dot(low, w_down[...], ((1,), (1,)))

    def to_following(at, value):
        value = middle[at] + value + b_down
        stream[at] = value
        if last:
            return live_rows(value, two.own + at.start, live_ref[0, mover.ctx]).astype(LOW)
        return normalize(value, gain1, shift1)[0].astype(LOW)

    def meanwhile():
        mover.stay(middle, far_middle)
        mover.stay(second, far_second)
        mover.stay(hidden, far_hidden)
        mover.stay(slope, far_slope)
        pass_on(ahead[:2], 3)
        pass_on(ahead[2:], 1)
        pass_on(ahead[2:], 2)

    two.after(one, mlp_part, to_following, meanwhile, lambda: pass_on(ahead[2:], 3))
    two.have()
    for name in plan.ahead:
        gathers[name, 1].have()
        mover.stay(gathers[name, 1].target, kept_ahead[name])
    mover.settle()


class Plan:
    def __init__(self, layer, last, inside):
        self.layer, self.entry = layer, layer == 0
        self.own = (NAMES if layer == 0 else ("down",)) if inside else ()
        self.ahead = ("qkv", "out", "up") if inside and not last else ()
        self.held = tuple(name for name in NAMES if name not in self.own)


def forward_layer(source, x, live, params, gathered, weights, plan, last, size, sizes, ident):
    rows, width = source.shape
    count = sizes[0]
    joint, hidden = weights["qkv"].shape[2], weights["up"].shape[2]
    heads = joint // (3 * size)
    attn, slots, span = heads * size, count * rows, rows // 4
    tile = 256 if slots % 256 == 0 else PAD
    columns = {"qkv": joint, "out": attn, "up": hidden, "down": hidden}
    inputs = [(source, VMEM)] + ([] if plan.entry else [(x, VMEM)])
    inputs += [(live, SMEM)] + [(value, HBM) for value in params]
    inputs += [(gathered[name, plan.layer], HBM) for name in plan.held]
    inputs += [(weights[name], HBM) for name in plan.own + plan.ahead]
    saved = [
        ((count, 3 * size, rows), LOW),
        ((size, slots), FULL),
        ((8, slots), FULL),
        ((rows, attn), LOW),
        ((span, width), FULL),
        ((rows, width), LOW),
        ((rows, hidden), LOW),
        ((rows, hidden), LOW),
    ]
    outputs = [((span, width), FULL, VMEM), ((rows, width), LOW, VMEM)]
    outputs += [(shape, dtype, HBM) for shape, dtype in saved]
    if plan.entry:
        outputs.append(((rows, width), LOW, HBM))
    outputs += [((width, columns[name]), LOW, HBM) for name in plan.ahead + plan.own]
    qkv_shape, o_shape, lse_shape, heads_shape = saved[:4]
    scratch = [VMEM((joint, rows), LOW), VMEM((rows, attn), LOW), VMEM((attn, rows), LOW)]
    scratch += [VMEM(*pair) for pair in saved[:3] + saved[4:]]
    if plan.entry:
        scratch.append(VMEM((rows, width), LOW))
    scratch += [
        VMEM((slots, PAD), LOW),
        VMEM((PAD, slots), LOW),
        VMEM((size, slots), LOW),
        VMEM((size, slots), LOW),
        VMEM((2, slots, tile), FULL),
        VMEM((2, 8, tile), FULL),
    ]
    scratch += round_buffers(rows, width) + round_buffers(rows, width)
    scratch += [VMEM((16, slots), LOW), VMEM((16, joint), FULL)]
    scratch += [VMEM(value.shape, value.dtype) for value in params]
    scratch += [VMEM((width, columns[name]), LOW) for name in NAMES + plan.ahead]
    results = run(
        functools.partial(layer_kernel, plan, last, size, tile),
        "forward_layer",
        ident,
        inputs,
        outputs,
        scratch,
        2 * (count - 1) + 2 * ROUND_COPIES + 2 * count * len(plan.own + plan.ahead),
        10 + 2 * len(plan.own + plan.ahead) + len(plan.held) + len(params),
        sizes,
        58,
        2 * rows * width * (2 * hidden + attn + joint) + 4 * slots * slots * 256,
    )
    stream, following = results[:2]
    kept = results[2 : 11 if plan.entry else 10]
    for name, value in zip(plan.ahead, results[2 + len(kept) :]):
        gathered[name, plan.layer + 1] = value
    for name, value in zip(plan.own, results[2 + len(kept) + len(plan.ahead) :]):
        gathered[name, plan.layer] = value
    return stream, following, kept


class SmallSums:
    def __init__(self, mover, rows, held, got):
        self.mover, self.rows, self.held, self.got = mover, rows, held, got
        self.stage = 0
        mate, far = tp_peers()
        self.peers = [
            dict(tp=mate),
            dict(tp=far),
            dict(shard=1 - mover.shard),
            dict(ctx=mover.flip(2)),
            dict(ctx=mover.flip(1)),
        ]

    def part(self, stage):
        return pl.ds(0, self.rows if stage < 2 else self.held.shape[1])

    def step(self):
        stage, mover = self.stage, self.mover
        if stage:
            mover.take(self.copy)
            at = self.part(stage - 1)
            self.held[stage] = self.held[stage - 1]
            self.held[stage, at, :] = self.held[stage - 1, at, :] + self.got[stage - 1, at, :]
        if stage < len(self.peers):
            at = self.part(stage)
            self.copy = mover.go(
                self.held.at[stage, at], self.got.at[stage, at], **self.peers[stage]
            )
        self.stage = stage + 1

    def value(self):
        return self.held[len(self.peers)]


def key_bias(mover, live_ref, bias):
    capacity = bias.shape[1] // mover.ctx_count
    row = lax.broadcasted_iota(jnp.int32, (16, capacity), 0)
    slot = lax.broadcasted_iota(jnp.int32, (16, capacity), 1)
    for r in range(mover.ctx_count):
        live = live_ref[0, mover.back(r)]
        value = jnp.where((row == 0) & (slot >= live), NEG_LARGE, 0.0)
        bias[:, r * capacity : (r + 1) * capacity] = value.astype(LOW)


def pair_columns(rows, width, size, turn):
    shape = (width, rows) if turn else (rows, width)
    given = lax.broadcasted_iota(jnp.int32, shape, 1 if turn else 0)
    column = lax.broadcasted_iota(jnp.int32, shape, 0 if turn else 1)
    head, within = column // (3 * size), column % (3 * size)
    wanted = head * (2 * size) + jnp.where(within < size, within, within - size)
    key = (within >= size) & (within < 2 * size)
    return jnp.where((given == wanted) & ~key, 1.0, 0.0).astype(LOW)


def joint_bias(pair, size, width):
    rows = pair.shape[1]
    spread = jnp.broadcast_to(pair, (16, rows)).astype(LOW)
    return jnp.dot(spread, pair_columns(rows, width, size, False), preferred_element_type=FULL)


def live_rows(value, start, live):
    row = start + lax.broadcasted_iota(jnp.int32, value.shape, 0)
    return jnp.where(row < live, value, 0.0)


def sums_into(sums, first, at, values):
    for index, value in enumerate(values):
        row = first + index
        added = jnp.sum(value, axis=0, keepdims=True)
        width = added.shape[1]
        sums[row : row + 1, 0:width] = (
            added if at.start == 0 else sums[row : row + 1, 0:width] + added
        )


def back_kernel(plan, size, tile, mover, ins, outs, work):
    ins, outs, work = iter(ins), iter(outs), iter(work)
    source = next(ins)
    x_ref = None if plan.last else next(ins)
    live_ref, far_gain2, far_gain1 = [next(ins) for _ in range(3)]
    far = [next(ins) for _ in range(14)]
    late_far = next(ins) if plan.late else None
    others = [(next(ins), next(ins)) for _ in range(plan.others)]
    stream, following = next(outs), next(outs)
    grad_outs = {name: next(outs) for name in NAMES if plan.inside and (name != "qkv" or plan.final)}
    mid_out = next(outs) if plan.inside and not plan.final else None
    late_out = next(outs) if plan.late else None
    split = local = totals = None
    if plan.joined:
        totals = next(outs)
    else:
        split, local = next(outs), next(outs)
    wholes = {} if plan.inside else {name: next(outs) for name in NAMES}
    near = [next(work) for _ in range(14)]
    slope, w_down, w_up, middle, hidden, second, w_out, heads, qkv, o_ref, lse, first, w_qkv, before = near
    grad = next(work) if plan.last else source
    pre_grad, attn_grad, parts, grads, nat = [next(work) for _ in range(5)]
    attend_work = [next(work) for _ in range(13)]
    one_work, two_work = [next(work) for _ in range(5)], [next(work) for _ in range(5)]
    rows, width = source.shape
    reduces = {}
    if plan.inside:
        pairs = {
            "down": (grad, hidden),
            "up": (second, pre_grad),
            "out": (attn_grad, heads),
            "qkv": (first, nat),
        }
        for name in ("down", "up", "out", "qkv"):
            buffers = [next(work) for _ in range(4)]
            reduces[name] = Reduce(mover, buffers, grad_outs.get(name), *pairs[name])
    late = None
    if plan.late:
        late_mid, late_line = next(work), next(work)
        late = Reduce(mover, (late_mid, None, late_mid, late_line), late_out, None, None)
    bias, gain2_ref, gain1_ref = [next(work) for _ in range(3)]
    if plan.joined:
        split, local = next(work), next(work)
        early_held, early_got, late_held, late_got = [next(work) for _ in range(4)]
        tops = 8 * (plan.others + 1)
        early = SmallSums(mover, tops, early_held, early_got)
        final = SmallSums(mover, 8, late_held, late_got)
        everything = [(split, local)] + others

    greet(mover, plan.inside)
    gain_loads = [mover.stay(far_gain2, gain2_ref), mover.stay(far_gain1, gain1_ref)]
    one = Round(mover, rows, attn_grad, one_work)
    two = Round(mover, rows, following, two_work)
    if plan.final:
        far[13] = far[13].at[two.rows(two.own)]
    load = [mover.stay(there, here) for there, here in zip(far, near)]
    if late:
        mover.near(mover.stay(late_far, late_mid))
        late.spread()
    if plan.last:
        chunk = rows // 5 if rows % 80 == 0 else rows

        def mask_step(i, carry):
            at = pl.ds(pl.multiple_of(i * chunk, 16), chunk)
            value = source[at, :].astype(FULL)
            grad[at, :] = live_rows(value, i * chunk, live_ref[0, mover.ctx]).astype(LOW)
            return carry

        lax.fori_loop(0, rows // chunk, mask_step, 0)
    key_bias(mover, live_ref, bias)
    mover.near(*gain_loads)
    gain2, gain1 = [
        ref[...].astype(FULL)[plan.layer : plan.layer + 1] for ref in (gain2_ref, gain1_ref)
    ]
    split[...] = jnp.zeros_like(split)
    local[...] = jnp.zeros_like(local)
    split[5:6, 0:width] = jnp.sum(
        grad[one.rows(one.own), :].astype(FULL), axis=0, keepdims=True
    )
    mover.near(*load[:3])
    hidden_width = slope.shape[1]

    def mlp_part(start):
        at = one.rows(start)
        pre = jnp.dot(grad[at, :], w_down[...], preferred_element_type=FULL)
        low = (pre * slope[at, :].astype(FULL)).astype(LOW)
        pre_grad[at, :] = low
        local[0:1, 0:hidden_width] += jnp.sum(low.astype(FULL), axis=0, keepdims=True)
        return dot(low, w_up[...], ((1,), (1,)))

    def to_attn(at, value):
        if plan.last:
            above = grad[one.rows(one.own + at.start, at.size), :].astype(FULL)
        else:
            above = x_ref[at]
        _, normed, inverse = normalize(middle[at], 1.0, 0.0)
        result = above + normalize_back(value, normed, inverse, gain2)
        stream[at] = result
        low = result.astype(LOW)
        sums_into(split, 2, at, (value * normed, value, low.astype(FULL)))
        return low

    def reduce(name):
        if name in reduces:
            reduces[name].begin()

    def fold(name):
        if name in reduces:
            reduces[name].fold()
            reduces[name].spread()

    def finish(name):
        if name in reduces:
            reduces[name].finish()

    def begin_early():
        if plan.joined:
            early_held[0] = jnp.zeros(early_held.shape[1:], FULL)
            for layer, (some, more) in enumerate(everything):
                first_row = 0 if layer else 2
                for row in range(first_row, 6):
                    at = row * len(everything) + layer
                    early_held[0, at : at + 1, :] = some[row : row + 1, :]
                for row in range(2 if layer else 1):
                    at = tops + row * len(everything) + layer
                    early_held[0, at : at + 1, :] = more[row : row + 1, :]

    def early_step():
        if plan.joined:
            early.step()

    def start_down():
        mover.near(load[3], load[4])
        reduce("down")

    one.eager(mlp_part, to_attn, start_down)
    mover.near(load[5])
    reduce("up")
    one.have()
    mover.near(load[6])
    turned_product(attn_grad, w_out, None, parts)

    def waiting():
        begin_early()
        early_step()
        mover.near(load[7])
        reduce("out")

    def ready():
        mover.near(load[8], load[9], load[10])
        if late:
            late.finish()

    def between(turn):
        if turn == 0:
            early_step()
        if turn == 2:
            finish("down")
        if turn == 3:
            fold("up")
            fold("out")
            early_step()

    attend_back_part(
        size,
        tile,
        mover,
        parts,
        bias,
        qkv,
        o_ref,
        lse,
        grads,
        attend_work,
        ready,
        waiting,
        lambda: fold("down"),
        between,
    )
    nat[...] = turned(grads[...])
    pairs_width = nat.shape[1] // 3 * 2
    picked = jnp.dot(
        nat[...], pair_columns(pairs_width, nat.shape[1], size, True), preferred_element_type=FULL
    )
    local[1:2, 0:pairs_width] = jnp.sum(picked, axis=0, keepdims=True)
    mover.near(*load[11:])

    def qkv_part(start):
        return dot(nat[two.rows(start), :], w_qkv[...], ((1,), (1,)))

    def to_following(at, value):
        row = before[at, :].astype(FULL)
        _, normed, inverse = normalize(row, 1.0, 0.0)
        result = stream[at] + normalize_back(value, normed, inverse, gain1)
        stream[at] = result
        low = result.astype(LOW)
        sums_into(split, 0, at, (value * normed, value))
        return low

    def meanwhile():
        if plan.inside:
            last = reduces["qkv"]
            last.compute(last.mid, mover.shard)
        early_step()

    def halfway():
        if plan.inside:
            reduces["qkv"].fold_blocks(3, 1)
            if plan.final:
                reduces["qkv"].spread()

    if plan.inside:
        reduces["qkv"].begin_blocks()
    two.eager(qkv_part, to_following, meanwhile, halfway)
    early_step()
    finish("up")
    finish("out")
    if plan.joined:
        late_held[0, 0:8, :] = jnp.zeros((8, late_held.shape[2]), FULL)
        late_held[0, 0:2, :] = split[0:2, :]
        late_held[0, 8:16, :] = local[...]
        final.step()
    if plan.inside:
        reduces["qkv"].fold_blocks(2, 0)
        if plan.final:
            reduces["qkv"].finish()
        else:
            mover.stay(reduces["qkv"].mid, mid_out)
    if plan.joined:
        final.step()
    two.have_mate_own()
    two.have_other()
    if plan.joined:
        final.step()
        final.step()
    two.have_mate_other()
    if plan.joined:
        final.step()
    for name in ("down", "up", "out"):
        if name in reduces:
            reduces[name].done()
    if late:
        late.done()
    if plan.inside and plan.final:
        reduces["qkv"].done()
    if plan.joined:
        final.step()
        early.step()
        totals[...] = early.value()
        last_value = final.value()
        for row in range(2):
            at = row * len(everything)
            totals[at : at + 1, :] = last_value[row : row + 1, :]
        at = tops + len(everything)
        totals[at : at + 1, :] = last_value[9:10, :]
    if not plan.inside:
        for name, (lhs, rhs) in {
            "down": (grad, hidden),
            "up": (second, pre_grad),
            "out": (attn_grad, heads),
            "qkv": (first, nat),
        }.items():
            full = Reduce(mover, (wholes[name],) * 4, None, lhs, rhs)
            full.compute(wholes[name], 0)
    mover.settle()


def gather_outputs_kernel(layers, *refs):
    count = layers * len(NAMES)
    parts, token_grads, mixed, totals = refs[:count], refs[count], refs[count + 1], refs[count + 2]
    outs, work = refs[count + 3 : count + 17], refs[count + 17 : -2]
    into, out_of = refs[-2:]
    coming, going = [], []
    pairs = [(mixed, work[4], outs[4].at[0])]
    for index in range(len(NAMES)):
        for layer in range(layers):
            pairs.append(
                (parts[index * layers + layer], work[index].at[layer], outs[index].at[layer])
            )
    for i, (source, stage, _) in enumerate(pairs):
        coming.append(pltpu.make_async_copy(source, stage, into.at[i]))
        coming[-1].start()
    outs[5][0] = token_grads[...].astype(FULL)
    for row, out in enumerate(outs[6:12]):
        out[...] = totals[row * layers : (row + 1) * layers, 0 : out.shape[1]]
    for row, out in enumerate(outs[12:14]):
        row = row + 8
        out[...] = totals[row * layers : (row + 1) * layers, 0 : out.shape[1]]
    for i, (_, stage, target) in enumerate(pairs):
        coming[i].wait()
        going.append(pltpu.make_async_copy(stage, target, out_of.at[i]))
        going[-1].start()
    for copy in going:
        copy.wait()


def gather_outputs(done, token_grads, mixed, totals, layers, widths):
    rows, width = token_grads.shape
    parts = [done[name, layer] for name in NAMES for layer in range(layers)]
    hbm, whole = pl.BlockSpec(memory_space=HBM), lambda shape: pl.BlockSpec(
        shape, lambda i: (0,) * len(shape)
    )
    shapes = [(layers,) + done[name, 0].shape for name in NAMES] + [(1, rows, width)] * 2
    types = [FULL] * 4 + [LOW, FULL]
    small = [(layers, width)] * 6 + [(layers, count) for count in widths]
    copies = len(parts) + 1
    return pl.pallas_call(
        functools.partial(gather_outputs_kernel, layers),
        grid=(1,),
        in_specs=[hbm] * len(parts) + [whole(token_grads.shape), hbm, whole(totals.shape)],
        out_specs=[hbm] * 5 + [whole(shape) for shape in shapes[5:] + small],
        out_shape=[jax.ShapeDtypeStruct(*pair) for pair in zip(shapes, types)]
        + [jax.ShapeDtypeStruct(shape, FULL) for shape in small],
        scratch_shapes=[VMEM(shape, FULL) for shape in shapes[:4]]
        + [VMEM((rows, width), LOW)]
        + [pltpu.SemaphoreType.DMA((copies,)), pltpu.SemaphoreType.DMA((copies,))],
        compiler_params=pltpu.CompilerParams(vmem_limit_bytes=60 * 2**20),
        name="gather_outputs",
    )(*parts, token_grads, mixed, totals)


class BackPlan:
    def __init__(self, layer, layers, inside):
        self.inside, self.layer = inside, layer
        self.last, self.final = layer == layers - 1, layer == 0
        self.late = inside and not self.last
        self.joined = inside and self.final
        self.others = layers - 1 if self.joined else 0


def back_layer(source, x, live, gain2, gain1, saved, late, others, plan, size, sizes, ident):
    rows, width = source.shape
    count = sizes[0]
    slope, w_down, w_up = saved[:3]
    hidden, joint, attn = slope.shape[1], saved[12].shape[1], saved[6].shape[1]
    slots, span = count * rows, rows // 4
    tile = 256 if slots % 256 == 0 else PAD
    wide = max(width, hidden, joint)
    half = width // 2
    block = half // count
    columns = {"qkv": joint, "out": attn, "up": hidden, "down": hidden}
    inputs = [(source, VMEM)] + ([] if plan.last else [(x, VMEM)])
    inputs += [(live, SMEM), (gain2, HBM), (gain1, HBM)]
    inputs += [(value, HBM) for value in saved]
    if plan.late:
        inputs.append((late, HBM))
    for pair in others[: plan.others]:
        inputs += [(value, VMEM) for value in pair]
    outputs = [((span, width), FULL, VMEM), ((rows, width), LOW, VMEM)]
    names = [name for name in NAMES if plan.inside and (name != "qkv" or plan.final)]
    outputs += [((block, columns[name]), FULL, VMEM) for name in names]
    if plan.inside and not plan.final:
        outputs.append(((half, joint), LOW, HBM))
    if plan.late:
        outputs.append(((block, joint), FULL, VMEM))
    depth = 8 * (plan.others + 1)
    if plan.joined:
        outputs.append(((depth + 8, wide), FULL, VMEM))
    else:
        outputs += [((8, wide), FULL, VMEM)] * 2
    if not plan.inside:
        outputs += [((width, columns[name]), LOW, VMEM) for name in NAMES]
    scratch = [VMEM(value.shape, value.dtype) for value in saved]
    scratch[13] = VMEM((span, width), saved[13].dtype)
    if plan.last:
        scratch.append(VMEM((rows, width), LOW))
    scratch += [
        VMEM((rows, hidden), LOW),
        VMEM((rows, width), LOW),
        VMEM((attn, rows), LOW),
        VMEM((joint, rows), LOW),
        VMEM((rows, joint), LOW),
    ]
    scratch += attend_back_buffers(size, count, rows, tile)
    scratch += round_buffers(rows, width) + round_buffers(rows, width)
    if plan.inside:
        for name in ("down", "up", "out", "qkv"):
            scratch += reduce_buffers(half, columns[name], count)
    if plan.late:
        scratch += [VMEM((half, joint), LOW), VMEM((count - 1, block, joint), LOW)]
    scratch.append(VMEM((16, slots), LOW))
    scratch += [VMEM(value.shape, value.dtype) for value in (gain2, gain1)]
    assert 2 * (plan.others + 1) <= 8
    if plan.joined:
        scratch += [VMEM((8, wide), FULL)] * 2
        scratch += [
            VMEM((6, depth + 8, wide), FULL),
            VMEM((5, depth + 8, wide), FULL),
            VMEM((6, 16, wide), FULL),
            VMEM((5, 16, wide), FULL),
        ]
    results = run(
        functools.partial(back_kernel, plan, size, tile),
        "back_layer",
        ident,
        inputs,
        outputs,
        scratch,
        3 * (count - 1) + 2 * ROUND_COPIES + 6 * count + 10 + count,
        len(saved) + 4,
        sizes,
        58,
        6 * rows * width * (2 * hidden + attn + joint) + 10 * slots * slots * 256,
    )
    return results[:2], names, results[2:]


def shards(
    tokens,
    block_tokens,
    ln1_gain,
    ln1_bias,
    w_qkv,
    b_qv,
    w_out,
    b_out,
    ln2_gain,
    ln2_bias,
    w_up,
    b_up,
    w_down,
    b_down,
    cotangent,
):
    images, capacity, width = tokens.shape
    assert images == 1
    layers = w_qkv.shape[0]
    size = HEAD_DIM
    ctx_count = lax.axis_size("ctx")
    ctx_place = lax.axis_index("ctx")
    joint_width = w_qkv.shape[2]
    heads = joint_width // (3 * size)
    assert heads == ctx_count
    attn_width = heads * size
    hidden_width = w_up.shape[2]
    weights = {"qkv": w_qkv, "out": w_out, "up": w_up, "down": w_down}
    sizes = (ctx_count, lax.axis_size("shard"))
    inside = sizes == (4, 2)
    gathered = {}
    if not inside:
        for name, value in weights.items():
            for layer in range(layers):
                gathered[name, layer] = gather_weight(value[layer])[0]
    source, stream = tokens[0], None
    saved = []
    for layer in range(layers):
        last = layer == layers - 1
        result, following, kept = forward_layer(
            source,
            stream,
            block_tokens,
            (b_out, ln2_gain, ln2_bias, b_down, ln1_gain, ln1_bias, b_up, b_qv),
            gathered,
            weights,
            Plan(layer, last, inside),
            last,
            size,
            sizes,
            1 + layer,
        )
        before = stream if layer else source
        first = source if layer else kept[8]
        saved.append((before, first) + tuple(kept[:8]))
        source, stream = following, result
    mixed = source

    done, packs = {}, {}
    source, stream, late = cotangent[0], None, None
    for layer in reversed(range(layers)):
        before, first, qkv, head_out, lse, heads_low, middle, second, hidden, slope = saved[layer]
        plan = BackPlan(layer, layers, inside)
        whole = {name: gathered[name, layer] for name in NAMES}
        near = [slope, whole["down"], whole["up"], middle, hidden, second, whole["out"]]
        near += [heads_low, qkv, head_out, lse, first, whole["qkv"], before]
        others = [packs[key] for key in sorted(packs)]
        (stream, source), names, rest = back_layer(
            source, stream, block_tokens, ln2_gain, ln1_gain, near, late, others, plan, size, sizes, 1 + layers + layer
        )
        rest = iter(rest)
        for name in names:
            done[name, layer] = next(rest)
        if plan.inside and not plan.final:
            late = next(rest)
        if plan.late:
            done["qkv", layer + 1] = next(rest)
        if plan.joined:
            totals = next(rest)
        else:
            packs[layer] = (next(rest), next(rest))
        if not inside:
            for name in NAMES:
                value = next(rest)
                done[name, layer] = scatter_weight(
                    lambda start, count, value=value: rows_of(value, start, count).astype(FULL),
                    width,
                )
    if not inside:
        split = total_over(("tp",), jnp.stack([packs[l][0] for l in range(layers)], axis=1))
        local = jnp.stack([packs[l][1] for l in range(layers)], axis=1)
        totals = total_over(("shard", "ctx"), jnp.concatenate([split, local[:2]]))
        totals = totals.reshape(10 * layers, -1)
    pairs = b_qv.shape[1]
    outs = gather_outputs(done, source, mixed, totals, layers, (hidden_width, pairs))
    g_qkv, g_out, g_up, g_down, mixed, token_grads = outs[:6]
    g_ln1_gain, g_ln1_bias, g_ln2_gain, g_ln2_bias, g_b_out, g_b_down, g_b_up, g_b_qv = outs[6:]
    return (
        mixed,
        token_grads,
        g_ln1_gain,
        g_ln1_bias,
        g_qkv,
        g_b_qv,
        g_out,
        g_b_out,
        g_ln2_gain,
        g_ln2_bias,
        g_up,
        g_b_up,
        g_down,
        g_b_down,
    )


def solution(mesh):
    split_rows = P(None, ("shard", "ctx"), "tp")
    split_tokens = P("shard", "ctx", None)
    return jax.shard_map(
        shards,
        mesh=mesh,
        in_specs=(
            split_tokens,
            P("shard", None),
            P(),
            P(),
            split_rows,
            P(None, "tp"),
            split_rows,
            P(),
            P(),
            P(),
            split_rows,
            P(None, "tp"),
            split_rows,
            P(),
            split_tokens,
        ),
        out_specs=(
            split_tokens,
            split_tokens,
            P(),
            P(),
            split_rows,
            P(None, "tp"),
            split_rows,
            P(),
            P(),
            P(),
            split_rows,
            P(None, "tp"),
            split_rows,
            P(),
        ),
        check_vma=False,
    )
```

```python
import functools
import math

import jax
import jax.numpy as jnp
from jax import lax
from jax.experimental import pallas as pl
from jax.experimental.pallas import tpu as pltpu
from jax.sharding import PartitionSpec as P

HEAD_DIM = 64
EPSILON = 1e-06
NEG_LARGE = -1e30
LOW = jnp.bfloat16
FULL = jnp.float32
PAD = 128
MESH = pl.DeviceIdType.MESH
VMEM = pltpu.VMEM
HBM = pltpu.HBM
SMEM = pltpu.SMEM


def bits_of(axis):
    size = lax.axis_size(axis)
    assert size & (size - 1) == 0
    return [1 << i for i in range(size.bit_length() - 1)]


def swap(value, axis, bit):
    size = lax.axis_size(axis)
    return lax.ppermute(value, axis, [(i, i ^ bit) for i in range(size)])


def side_of(axis, bit):
    return (lax.axis_index(axis) // bit) % 2


def rows_of(value, start, count, axis=0):
    return lax.dynamic_slice_in_dim(value, start, count, axis)


def halve(axis, bits, partial, total):
    offset, span, received = jnp.int32(0), total, []

    def summed(start, count):
        value = partial(start, count)
        for got, base in received:
            value = value + rows_of(got, start - base, count).astype(FULL)
        return value

    for bit in bits:
        half = span // 2
        side = side_of(axis, bit)
        got = swap(summed(offset + (1 - side) * half, half).astype(LOW), axis, bit)
        offset = offset + side * half
        received.append((got, offset))
        span = half
    return summed(offset, span)


def double(axis, bits, value):
    for bit in bits:
        got = swap(value, axis, bit)
        first = side_of(axis, bit) == 0
        value = jnp.concatenate(
            [jnp.where(first, value, got), jnp.where(first, got, value)], axis=0
        )
    return value


def total_over(axes, value):
    for axis in axes:
        for bit in bits_of(axis):
            value = value + swap(value, axis, bit)
    return value


def ring(value, by):
    count = lax.axis_size("ctx")
    return lax.ppermute(value, "ctx", [(i, (i + by) % count) for i in range(count)])


def gather_weight(piece):
    count = lax.axis_size("ctx")
    place = lax.axis_index("ctx")
    ways = lax.axis_size("shard")
    blocks = [piece] + [ring(piece, by) for by in range(1, count)]
    whole = jnp.zeros((ways * count,) + piece.shape, piece.dtype)
    me = lax.axis_index("shard")
    for by, block in enumerate(blocks):
        at = (place - by) % count
        held = [(jnp.int32(0), block)]
        for bit in bits_of("shard"):
            held = held + [(other ^ bit, swap(value, "shard", bit)) for other, value in held]
        for other, value in held:
            whole = lax.dynamic_update_index_in_dim(whole, value, (me ^ other) * count + at, 0)
    return whole.reshape((ways * count * piece.shape[0],) + piece.shape[1:]), blocks[-1]


def scatter_weight(partial, total):
    count = lax.axis_size("ctx")
    place = lax.axis_index("ctx")
    mine = halve("shard", bits_of("shard")[::-1], partial, total).astype(LOW)
    mine = mine.reshape((count, mine.shape[0] // count) + mine.shape[1:])
    value = lax.dynamic_index_in_dim(mine, place, 0, False).astype(FULL)
    for by in range(1, count):
        given = lax.dynamic_index_in_dim(mine, (place + by) % count, 0, False)
        value = value + ring(given, by).astype(FULL)
    return value


def dot(left, right, contract):
    return lax.dot_general(
        left, right, ((contract[0], contract[1]), ((), ())), preferred_element_type=FULL
    )


def turned(value):
    return value.astype(FULL).T.astype(LOW)


def normalize(rows, gain, shift):
    row_mean = jnp.mean(rows, axis=-1, keepdims=True)
    centred = rows - row_mean
    inverse = lax.rsqrt(jnp.mean(centred * centred, axis=-1, keepdims=True) + EPSILON)
    normed = centred * inverse
    return (normed * gain + shift, normed, inverse)


def normalize_back(grad_out, normed, inverse, gain):
    scaled = grad_out * gain
    mean_grad = jnp.mean(scaled, axis=-1, keepdims=True)
    mean_cross = jnp.mean(scaled * normed, axis=-1, keepdims=True)
    return inverse * (scaled - mean_grad - normed * mean_cross)


def gelu_pair(value):
    spread = 0.5 * (1.0 + lax.erf(value * (0.5**0.5)))
    slope = spread + value * jnp.exp(-0.5 * value * value) * (1.0 / math.sqrt(2.0 * math.pi))
    return (value * spread).astype(LOW), slope.astype(LOW)


class Mover:
    def __init__(self, sizes, send, recv, local):
        self.ctx_count, self.shard_count = sizes
        self.send, self.recv, self.local = send, recv, local
        self.copies, self.here = [], []
        self.arrived = set()
        self.landed = set()
        self.ctx = lax.axis_index("ctx")
        self.shard = lax.axis_index("shard")

    def go(self, source, target, **device):
        index = len(self.copies)
        assert index < self.send.shape[0]
        copy = pltpu.make_async_remote_copy(
            src_ref=source,
            dst_ref=target,
            send_sem=self.send.at[index],
            recv_sem=self.recv.at[index],
            device_id=device,
            device_id_type=MESH,
        )
        copy.start()
        self.copies.append(copy)
        return index

    def stay(self, source, target):
        index = len(self.here)
        assert index < self.local.shape[0]
        copy = pltpu.make_async_copy(source, target, self.local.at[index])
        copy.start()
        self.here.append(copy)
        return index

    def near(self, *indices):
        for index in indices:
            if index not in self.landed:
                self.landed.add(index)
                self.here[index].wait()

    def take(self, index):
        if index not in self.arrived:
            self.arrived.add(index)
            self.copies[index].wait_recv()

    def flip(self, bits):
        place = self.ctx
        if bits & 1:
            place = place + 1 - 2 * lax.rem(self.ctx, 2)
        if bits & 2:
            place = place + 2 - 4 * (self.ctx // 2)
        return place

    def on(self, by):
        return lax.rem(self.ctx + by, self.ctx_count)

    def back(self, by):
        return lax.rem(self.ctx + self.ctx_count - by, self.ctx_count)

    def settle(self):
        for index, copy in enumerate(self.copies):
            self.take(index)
            copy.wait_send()
        self.near(*range(len(self.here)))


class Gather:
    def __init__(self, mover, source, target):
        self.mover, self.source, self.target = mover, source, target
        self.over = []

    def start(self):
        self.start_line()
        self.start_over()

    def start_line(self):
        mover = self.mover
        mine, there = self.source, self.block(mover.ctx)
        self.far = mover.go(mine, there, ctx=mover.flip(2))
        self.close = mover.go(mine, there, ctx=mover.flip(1))

    def start_over(self):
        mover = self.mover
        mine, there = self.source, self.block(mover.ctx)
        self.over.append(mover.go(mine, there, shard=1 - mover.shard))
        self.own = mover.stay(mine, there)

    def block(self, ctx):
        mover = self.mover
        rows = self.source.shape[0]
        start = (mover.shard * mover.ctx_count + ctx) * rows
        return self.target.at[pl.ds(pl.multiple_of(start, rows), rows)]

    def pass_on(self, stage):
        mover = self.mover
        if stage == 1:
            mover.take(self.far)
            rows = self.block(mover.flip(2))
            self.passed = mover.go(rows, rows, ctx=mover.flip(1))
        elif stage == 2:
            mover.take(self.close)
            rows = self.block(mover.flip(1))
        else:
            mover.take(self.passed)
            rows = self.block(mover.flip(3))
        self.over.append(mover.go(rows, rows, shard=1 - mover.shard))

    def have(self):
        for copy in self.over:
            self.mover.take(copy)
        self.mover.near(self.own)


class Reduce:
    def __init__(self, mover, buffers, out, lhs, rhs):
        self.mover, self.out, self.lhs, self.rhs = mover, out, lhs, rhs
        self.give, self.got, self.mid, self.line = buffers
        self.half = self.give.shape[0]
        self.block = self.half // mover.ctx_count

    def compute(self, target, shard):
        chunk = min(256, self.half)

        def step(i, carry):
            at = pl.ds(pl.multiple_of(shard * self.half + i * chunk, chunk), chunk)
            here = pl.ds(pl.multiple_of(i * chunk, chunk), chunk)
            target[here, :] = dot(self.lhs[:, at], self.rhs[...], ((0,), (0,))).astype(LOW)
            return carry

        lax.fori_loop(0, self.half // chunk, step, 0)

    def begin(self):
        mover = self.mover
        self.compute(self.give, 1 - mover.shard)
        self.cross = mover.go(self.give, self.got, shard=1 - mover.shard)
        self.compute(self.mid, mover.shard)

    def fold(self):
        self.mover.take(self.cross)
        self.mid[...] = (self.mid[...].astype(FULL) + self.got[...].astype(FULL)).astype(LOW)

    def begin_blocks(self):
        mover = self.mover
        self.blocks = {}
        for bits in (3, 1, 2, 0):
            ctx = mover.flip(bits)
            at = pl.ds(pl.multiple_of(ctx * self.block, self.block), self.block)
            start = pl.multiple_of((1 - mover.shard) * self.half + ctx * self.block, self.block)
            lhs = self.lhs[:, pl.ds(start, self.block)]
            self.give[at, :] = dot(lhs, self.rhs[...], ((0,), (0,))).astype(LOW)
            self.blocks[bits] = mover.go(
                self.give.at[at], self.got.at[at], shard=1 - mover.shard
            )

    def fold_blocks(self, *which):
        mover = self.mover
        for bits in which:
            mover.take(self.blocks[bits])
            ctx = mover.flip(bits)
            at = pl.ds(pl.multiple_of(ctx * self.block, self.block), self.block)
            self.mid[at, :] = (
                self.mid[at, :].astype(FULL) + self.got[at, :].astype(FULL)
            ).astype(LOW)

    def rows(self, ctx):
        return self.mid.at[pl.ds(pl.multiple_of(ctx * self.block, self.block), self.block)]

    def spread(self):
        mover = self.mover
        self.first = mover.go(self.rows(mover.flip(3)), self.line.at[1], ctx=mover.flip(1))
        self.second = mover.go(self.rows(mover.flip(1)), self.line.at[0], ctx=mover.flip(1))

    def finish(self):
        mover = self.mover
        mover.take(self.first)
        rows = self.rows(mover.flip(2))
        rows[...] = (rows[...].astype(FULL) + self.line[1].astype(FULL)).astype(LOW)
        self.third = mover.go(rows, self.line.at[2], ctx=mover.flip(2))

    def done(self):
        self.mover.take(self.second)
        self.mover.take(self.third)
        value = self.rows(self.mover.ctx)[...].astype(FULL)
        self.out[...] = value + self.line[0].astype(FULL) + self.line[2].astype(FULL)


def reduce_buffers(half, width, count):
    return [
        VMEM((half, width), LOW),
        VMEM((half, width), LOW),
        VMEM((half, width), LOW),
        VMEM((count - 1, half // count, width), LOW),
    ]


def greet(mover, shard):
    barrier = pltpu.get_barrier_semaphore()
    peers = [dict(ctx=mover.on(by)) for by in range(1, mover.ctx_count)]
    peers += [dict(tp=peer) for peer in tp_peers()]
    if shard:
        peers.append(dict(shard=1 - mover.shard))
    for peer in peers:
        pl.semaphore_signal(barrier, inc=1, device_id=peer, device_id_type=MESH)
    pl.semaphore_wait(barrier, len(peers))


def tp_peers():
    place = lax.axis_index("tp")
    core, far = lax.rem(place, 2), place // 2
    return place + 1 - 2 * core, place + 2 - 4 * far


def run(kernel, name, ident, inputs, outputs, scratch, remote, local, sizes, vmem, flops):
    n_in, n_out, n_scratch = len(inputs), len(outputs), len(scratch)

    def body(*refs):
        ins, outs = refs[:n_in], refs[n_in : n_in + n_out]
        work = refs[n_in + n_out :]
        mover = Mover(sizes, *work[n_scratch:])
        kernel(mover, ins, outs, work[:n_scratch])

    return pl.pallas_call(
        body,
        in_specs=[pl.BlockSpec(memory_space=space) for _, space in inputs],
        out_specs=[pl.BlockSpec(memory_space=space) for _, _, space in outputs],
        out_shape=[jax.ShapeDtypeStruct(shape, dtype) for shape, dtype, _ in outputs],
        scratch_shapes=list(scratch)
        + [
            pltpu.SemaphoreType.DMA((remote,)),
            pltpu.SemaphoreType.DMA((remote,)),
            pltpu.SemaphoreType.DMA((local,)),
        ],
        compiler_params=pltpu.CompilerParams(
            collective_id=ident, has_side_effects=True, vmem_limit_bytes=vmem * 2**20
        ),
        cost_estimate=pl.CostEstimate(flops=flops, bytes_accessed=2**24, transcendentals=0),
        name=name,
    )(*[value for value, _ in inputs])


def order_of(block, count):
    return (block + count - 1) % count


def tiles_of(count, capacity, tile):
    ends = [-(-(p + 1) * capacity // tile) for p in range(count)]
    return list(zip([0] + ends[:-1], ends))


def parts_of(capacity):
    middle = capacity // 2 // PAD * PAD
    return [(0, middle), (middle, capacity)] if middle else [(0, capacity)]


def tile_at(t, tile):
    return pl.ds(pl.multiple_of(t * tile, tile), tile)


def turned_product(left, right, bias, target):
    def step(i, carry):
        at = pl.ds(pl.multiple_of(i * PAD, PAD), PAD)
        value = jnp.dot(left[at, :], right[...], preferred_element_type=FULL)
        if bias is not None:
            value = value + bias[0:1, :]
        target[:, at] = turned(value.astype(LOW))
        return carry

    lax.fori_loop(0, left.shape[0] // PAD, step, 0)


def head_rows(ref, head, width):
    return ref.at[pl.ds(pl.multiple_of(head * width, 16), width)]


def attend_part(size, tile, mover, joint, bias, heads, qkv, o_ref, lse, work, after_send, begun, between):
    k_ref, q_ref, v_ref, low_ref, score_ref, top_ref = work
    count, width, capacity = qkv.shape
    slots = count * capacity
    sent = [None] + [
        mover.go(head_rows(joint, mover.on(by), width), qkv.at[by], ctx=mover.on(by))
        for by in range(1, count)
    ]
    after_send()
    qkv[0] = head_rows(joint, mover.ctx, width)[...]
    q_ref[size:PAD, :] = jnp.concatenate(
        [jnp.ones((16, slots), LOW), jnp.zeros((PAD - size - 16, slots), LOW)], axis=0
    )

    def prepare(r):
        here = slice(r * capacity, (r + 1) * capacity)
        p = order_of(r, count)
        q_ref[0:size, p * capacity : (p + 1) * capacity] = (
            qkv[r, 0:size, :] * (size**-0.5)
        ).astype(LOW)
        v_ref[:, here] = qkv[r, 2 * size : 3 * size, :]
        keys = jnp.concatenate(
            [qkv[r, size : 2 * size, :], bias[:, here], jnp.zeros((PAD - size - 16, capacity), LOW)],
            axis=0,
        )
        k_ref[here, :] = turned(keys)

    prepare(0)
    for by in range(1, count):
        mover.take(sent[by])
        prepare(by)

    begun()
    last = slots // tile - 1
    assert last % 2 == 1

    def phase(t, now, following, then):
        at, ahead = tile_at(t, tile), tile_at(following, tile)
        top = top_ref[now, 0:1, :]
        total = jnp.zeros((1, tile), FULL)
        summed = jnp.zeros((size, tile), FULL)
        new_top = jnp.full((1, tile), NEG_LARGE, FULL)
        for r in range(count):
            here = slice(r * capacity, (r + 1) * capacity)
            scores = jnp.dot(k_ref[here, :], q_ref[:, ahead], preferred_element_type=FULL)
            score_ref[then, here, :] = scores
            new_top = jnp.maximum(new_top, jnp.max(scores, axis=0, keepdims=True))
            weights = jnp.exp(score_ref[now, here, :] - top)
            total = total + jnp.sum(weights, axis=0, keepdims=True)
            summed = summed + jnp.dot(
                v_ref[:, here], weights.astype(LOW), preferred_element_type=FULL
            )
        top_ref[then] = jnp.broadcast_to(new_top, (8, tile))
        out = summed / total
        o_ref[:, at] = out
        low_ref[:, at] = out.astype(LOW)
        lse[:, at] = jnp.broadcast_to(top + jnp.log(total), (8, tile))

    def step(i, carry):
        phase(2 * i, 0, 2 * i + 1, 1)
        phase(2 * i + 1, 1, jnp.minimum(2 * i + 2, last), 0)
        return carry

    scores = jnp.dot(k_ref[...], q_ref[:, 0:tile], preferred_element_type=FULL)
    score_ref[0] = scores
    top_ref[0] = jnp.broadcast_to(jnp.max(scores, axis=0, keepdims=True), (8, tile))
    arriving = []
    for p, (low, high) in enumerate(tiles_of(count, capacity, 2 * tile)):
        lax.fori_loop(low, high, step, 0)
        done = low_ref.at[:, p * capacity : (p + 1) * capacity]
        if p < count - 1:
            there = head_rows(heads, mover.ctx, size)
            arriving.append(mover.go(done, there, ctx=mover.back(p + 1)))
        else:
            head_rows(heads, mover.ctx, size)[...] = low_ref[:, p * capacity : (p + 1) * capacity]
        between(p + 1)
    for copy in arriving:
        mover.take(copy)


def attend_back_part(size, tile, mover, parts, bias, qkv, o_ref, lse, grads, work, ready, waiting, begun, between):
    k_ref, v_ref, q_ref, do_ref, nat_ref, delta_ref, dq_ref, dk_ref, dv_ref, got, back, score_ref, grad_ref = work
    count, width, capacity = qkv.shape
    slots = count * capacity
    sent = [None] + [
        mover.go(head_rows(parts, mover.on(by), size), got.at[by], ctx=mover.on(by))
        for by in range(1, count)
    ]
    got[0] = head_rows(parts, mover.ctx, size)[...]
    waiting()
    ready()
    q_ref[size:PAD, :] = jnp.concatenate(
        [jnp.ones((16, slots), LOW), jnp.zeros((PAD - size - 16, slots), LOW)], axis=0
    )
    do_ref[size:PAD, :] = jnp.zeros((PAD - size, slots), LOW)
    dq_ref[...] = jnp.zeros_like(dq_ref)
    for r in range(count):
        here = slice(r * capacity, (r + 1) * capacity)
        pad = jnp.zeros((PAD - size - 16, capacity), LOW)
        k_ref[here, :] = turned(
            jnp.concatenate([qkv[r, size : 2 * size, :], bias[:, here], pad], axis=0)
        )
        v_ref[here, :] = turned(
            jnp.concatenate(
                [qkv[r, 2 * size : 3 * size, :], jnp.zeros((PAD - size, capacity), LOW)], axis=0
            )
        )
    for r in range(count):
        if r:
            mover.take(sent[r])
        p = order_of(r, count)
        at = slice(p * capacity, (p + 1) * capacity)
        scaled = (qkv[r, 0:size, :] * (size**-0.5)).astype(LOW)
        dout = got[r]
        q_ref[0:size, at] = scaled
        do_ref[0:size, at] = dout
        nat_ref[at, :] = turned(jnp.concatenate([scaled, dout], axis=0))
        delta = jnp.sum(dout.astype(FULL) * o_ref[:, at], axis=0, keepdims=True)
        delta_ref[:, at] = jnp.broadcast_to(delta, (8, capacity))

    begun()
    last = slots // tile - 1
    assert last % 2 == 1
    tiles = tiles_of(count, capacity, 2 * tile)
    arriving = []
    mine = head_rows(grads, mover.ctx, width)
    for turn, r in enumerate(list(range(1, count)) + [0]):
        here = slice(r * capacity, (r + 1) * capacity)
        dk_ref[...] = jnp.zeros_like(dk_ref)
        dv_ref[...] = jnp.zeros_like(dv_ref)

        def ready_scores(t, then, low, high, r=r):
            ahead = tile_at(t, tile)
            rows = slice(r * capacity + low, r * capacity + high)
            score_ref[then, low:high, :] = jnp.dot(
                k_ref[rows, :], q_ref[:, ahead], preferred_element_type=FULL
            )
            grad_ref[then, low:high, :] = jnp.dot(
                v_ref[rows, :], do_ref[:, ahead], preferred_element_type=FULL
            )

        def phase(t, now, following, then, r=r):
            at = tile_at(t, tile)
            query_grad = jnp.zeros((size, tile), FULL)
            for low, high in parts_of(capacity):
                ready_scores(following, then, low, high)
                chance = jnp.exp(score_ref[now, low:high, :] - lse[0:1, at])
                score_grad = (
                    chance * (grad_ref[now, low:high, :] - delta_ref[0:1, at])
                ).astype(LOW)
                query_grad = query_grad + jnp.dot(
                    qkv[r, size : 2 * size, low:high], score_grad, preferred_element_type=FULL
                )
                dk_ref[low:high, :] += jnp.dot(
                    score_grad, nat_ref[at, :], preferred_element_type=FULL
                )
                dv_ref[low:high, :] += jnp.dot(
                    chance.astype(LOW), nat_ref[at, :], preferred_element_type=FULL
                )
            dq_ref[:, at] += query_grad

        def step(i, carry, phase=phase):
            phase(2 * i, 0, 2 * i + 1, 1)
            phase(2 * i + 1, 1, jnp.minimum(2 * i + 2, last), 0)
            return carry

        ready_scores(0, 0, 0, capacity)
        if r:
            lax.fori_loop(0, tiles[-1][1], step, 0)
        else:
            for p, (low, high) in enumerate(tiles):
                lax.fori_loop(low, high, step, 0)
                at = slice(p * capacity, (p + 1) * capacity)
                value = (dq_ref[:, at] * (size**-0.5)).astype(LOW)
                if p < count - 1:
                    back[p + 1, 0:size, :] = value
                    arriving.append(
                        mover.go(
                            back.at[p + 1, 0:size], mine.at[0:size], ctx=mover.back(p + 1)
                        )
                    )
                else:
                    mine[0:size, :] = value
        keys = dk_ref[...].T[0:size].astype(LOW)
        values = dv_ref[...].T[size : 2 * size].astype(LOW)
        if r:
            back[r, size : 2 * size, :] = keys
            back[r, 2 * size : 3 * size, :] = values
            arriving.append(
                mover.go(
                    back.at[r, size : 3 * size], mine.at[size : 3 * size], ctx=mover.back(r)
                )
            )
        else:
            mine[size : 2 * size, :] = keys
            mine[2 * size : 3 * size, :] = values
        between(turn)
    for copy in arriving:
        mover.take(copy)


def attend_back_buffers(size, count, capacity, tile):
    slots = count * capacity
    return [
        VMEM((slots, PAD), LOW),
        VMEM((slots, PAD), LOW),
        VMEM((PAD, slots), LOW),
        VMEM((PAD, slots), LOW),
        VMEM((slots, PAD), LOW),
        VMEM((8, slots), FULL),
        VMEM((size, slots), FULL),
        VMEM((capacity, PAD), FULL),
        VMEM((capacity, PAD), FULL),
        VMEM((count, size, capacity), LOW),
        VMEM((count, 3 * size, capacity), LOW),
        VMEM((2, capacity, tile), FULL),
        VMEM((2, capacity, tile), FULL),
    ]


class Round:
    def __init__(self, mover, rows, full, buffers):
        place = lax.axis_index("tp")
        core, far = lax.rem(place, 2), place // 2
        self.mover, self.full = mover, full
        self.give, self.ra, self.passing, self.rb, self.keep = buffers
        self.span = rows // 4
        self.half = self.span // 2
        self.mate, self.far = tp_peers()

        def quarter(c, f):
            return (c * 2 + f) * self.span

        self.own, self.other = quarter(core, far), quarter(core, 1 - far)
        self.mate_own, self.mate_other = quarter(1 - core, far), quarter(1 - core, 1 - far)

    def rows(self, start, count=None):
        return pl.ds(pl.multiple_of(start, 16), count or self.span)

    def hand(self, slot, value):
        self.give[slot] = value.astype(LOW)
        return self.mover.go(self.give.at[slot], self.ra.at[slot], tp=self.mate)

    def onward(self, value, index):
        self.mover.take(index)
        self.passing[...] = (value + self.ra[1].astype(FULL)).astype(LOW)
        return [
            self.mover.go(self.passing.at[at], self.rb.at[at], tp=self.far)
            for at in (pl.ds(0, self.half), pl.ds(self.half, self.half))
        ]

    def close(self, far_copies, index, finish, halfway=None):
        self.mover.take(index)
        self.keep[...] += self.ra[0].astype(FULL)
        self.to_far, self.to_mate = [], []
        for c in range(2):
            at = pl.ds(c * self.half, self.half)
            self.mover.take(far_copies[c])
            low = finish(at, self.keep[at] + self.rb[at].astype(FULL))
            mine = self.full.at[self.rows(self.own + c * self.half, self.half)]
            mine[...] = low
            self.to_far.append(self.mover.go(mine, mine, tp=self.far))
            self.to_mate.append(self.mover.go(mine, mine, tp=self.mate))
            if halfway and c == 0:
                halfway()

    def eager(self, make, finish, meanwhile=None, halfway=None):
        first = self.hand(1, make(self.mate_other))
        copies = self.onward(make(self.other), first)
        second = self.hand(0, make(self.mate_own))
        self.keep[...] = make(self.own)
        if meanwhile:
            meanwhile()
        self.close(copies, second, finish, halfway)

    def after(self, before, make, finish, meanwhile=None, halfway=None):
        before.have_mate_own()
        second = self.hand(0, make(self.mate_own))
        self.keep[...] = make(self.own)
        before.have_other()
        value = make(self.other)
        before.have_mate_other()
        first = self.hand(1, make(self.mate_other))
        copies = self.onward(value, first)
        if meanwhile:
            meanwhile()
        self.close(copies, second, finish, halfway)

    def have_mate_own(self):
        for copy in self.to_mate:
            self.mover.take(copy)

    def have_other(self):
        self.passed = []
        for c in range(2):
            self.mover.take(self.to_far[c])
            rows = self.full.at[self.rows(self.other + c * self.half, self.half)]
            self.passed.append(self.mover.go(rows, rows, tp=self.mate))

    def have_mate_other(self):
        for copy in self.passed:
            self.mover.take(copy)

    def have(self):
        self.have_mate_own()
        self.have_other()
        self.have_mate_other()


ROUND_COPIES = 10


def round_buffers(rows, width):
    span = rows // 4
    return [
        VMEM((2, span, width), LOW),
        VMEM((2, span, width), LOW),
        VMEM((span, width), LOW),
        VMEM((span, width), LOW),
        VMEM((span, width), FULL),
    ]


NAMES = ("qkv", "out", "up", "down")


def layer_kernel(plan, last, size, tile, mover, ins, outs, work):
    ins, outs, work = iter(ins), iter(outs), iter(work)
    source = next(ins)
    x_ref = None if plan.entry else next(ins)
    live_ref = next(ins)
    far_params = [next(ins) for _ in range(8)]
    stream, following = next(outs), next(outs)
    far_qkv, far_o, far_lse, far_heads, far_middle, far_second, far_hidden, far_slope = [
        next(outs) for _ in range(8)
    ]
    far_first = next(outs) if plan.entry else None
    joint, nat, heads, qkv, o_ref, lse, middle, second, hidden, slope = [
        next(work) for _ in range(10)
    ]
    first = next(work) if plan.entry else source
    attend_work = [next(work) for _ in range(6)]
    one_work, two_work = [next(work) for _ in range(5)], [next(work) for _ in range(5)]
    rows = source.shape[0]
    bias, qkv_bias = next(work), next(work)
    params = [next(work) for _ in range(8)]
    whole = {name: next(work) for name in NAMES}
    gathers, loads = {}, {}
    for name in plan.held:
        loads[name] = (next(ins), whole[name])
    for name in plan.own:
        gathers[name, 0] = Gather(mover, next(ins).at[plan.layer], whole[name])
    kept_ahead = {name: next(outs) for name in plan.ahead}
    for name in plan.ahead:
        gathers[name, 1] = Gather(mover, next(ins).at[plan.layer + 1], next(work))
    kept = {name: next(outs) for name in plan.own}

    greet(mover, bool(gathers))
    if plan.entry:
        gathers_first = [key for key in [("qkv", 0)] if key in gathers]
        for key in gathers_first:
            gathers[key].start()
    param_loads = [mover.stay(there, here) for there, here in zip(far_params, params)]
    loads = {name: mover.stay(*pair) for name, pair in loads.items()}

    def have(name):
        if name in loads:
            mover.near(loads[name])
        else:
            gathers[name, 0].have()
            mover.stay(whole[name], kept[name])
        return whole[name]

    def begin(keys):
        for key in keys:
            if key in gathers:
                gathers[key].start_line()

    def begin_over(keys):
        for key in keys:
            if key in gathers:
                gathers[key].start_over()

    def pass_on(keys, stage):
        for key in keys:
            if key in gathers:
                gathers[key].pass_on(stage)

    def pass_all(keys):
        for stage in (1, 2, 3):
            pass_on(keys, stage)

    mover.near(*param_loads)
    layer, after = plan.layer, min(plan.layer + 1, params[0].shape[0] - 1)

    def row(index, layer=layer):
        return params[index][...].astype(FULL)[layer : layer + 1]

    b_out, gain2, shift2, b_down, b_up = row(0), row(1), row(2), row(3), row(6)
    gain1, shift1, gain0, shift0 = row(4, after), row(5, after), row(4), row(5)
    qkv_bias[...] = joint_bias(row(7), size, joint.shape[0])
    key_bias(mover, live_ref, bias)
    ahead = [("qkv", 1), ("out", 1), ("up", 1)]
    one = Round(mover, rows, second, one_work)
    two = Round(mover, rows, following, two_work)
    if plan.entry:
        chunk = rows // 5 if rows % 80 == 0 else rows

        def norm_step(i, carry):
            at = pl.ds(pl.multiple_of(i * chunk, 16), chunk)
            value = normalize(source[at, :].astype(FULL), gain0, shift0)[0]
            first[at, :] = value.astype(LOW)
            return carry

        lax.fori_loop(0, rows // chunk, norm_step, 0)
        mover.stay(first, far_first)
        pass_all([("qkv", 0)])
        begin([("out", 0), ("up", 0)])
        begin_over([("out", 0), ("up", 0), ("down", 0)] + ahead)
        turned_product(first, have("qkv"), qkv_bias, joint)
    else:
        turned_product(first, have("qkv"), qkv_bias, joint)

    def after_send():
        if plan.entry:
            pass_all([("out", 0), ("up", 0)])
        else:
            for name in plan.own:
                gathers[name, 0].start_over()

    def begun():
        if plan.entry:
            begin([("down", 0)])
        else:
            for name in plan.own:
                gathers[name, 0].start_line()

    def between(p):
        if p > 1:
            pass_on([("down", 0)], p - 1)
        if p == 4:
            if not plan.entry:
                begin_over(ahead)
            begin(ahead)

    attend_part(
        size, tile, mover, joint, bias, heads, qkv, o_ref, lse, attend_work, after_send, begun, between
    )
    nat[...] = turned(heads[...])
    w_out = have("out")

    def out_part(start):
        return dot(nat[one.rows(start), :], w_out[...], ((1,), (1,)))

    def to_second(at, value):
        if plan.entry:
            before = source[one.rows(one.own + at.start, at.size), :].astype(FULL)
        else:
            before = x_ref[at]
        value = before + value + b_out
        middle[at] = value
        return normalize(value, gain2, shift2)[0].astype(LOW)

    def meanwhile():
        mover.stay(qkv, far_qkv)
        mover.stay(o_ref, far_o)
        mover.stay(lse, far_lse)
        mover.stay(nat, far_heads)

    one.eager(out_part, to_second, meanwhile, lambda: pass_on(ahead[:2], 1))
    pass_on(ahead[:2], 2)
    w_up, w_down = have("up"), have("down")

    def mlp_part(start):
        at = two.rows(start)
        pre = jnp.dot(second[at, :], w_up[...], preferred_element_type=FULL) + b_up
        low, low_slope = gelu_pair(pre)
        hidden[at, :] = low
        slope[at, :] = low_slope
        return dot(low, w_down[...], ((1,), (1,)))

    def to_following(at, value):
        value = middle[at] + value + b_down
        stream[at] = value
        if last:
            return live_rows(value, two.own + at.start, live_ref[0, mover.ctx]).astype(LOW)
        return normalize(value, gain1, shift1)[0].astype(LOW)

    def meanwhile():
        mover.stay(middle, far_middle)
        mover.stay(second, far_second)
        mover.stay(hidden, far_hidden)
        mover.stay(slope, far_slope)
        pass_on(ahead[:2], 3)
        pass_on(ahead[2:], 1)
        pass_on(ahead[2:], 2)

    two.after(one, mlp_part, to_following, meanwhile, lambda: pass_on(ahead[2:], 3))
    two.have()
    for name in plan.ahead:
        gathers[name, 1].have()
        mover.stay(gathers[name, 1].target, kept_ahead[name])
    mover.settle()


class Plan:
    def __init__(self, layer, last, inside):
        self.layer, self.entry = layer, layer == 0
        self.own = (NAMES if layer == 0 else ("down",)) if inside else ()
        self.ahead = ("qkv", "out", "up") if inside and not last else ()
        self.held = tuple(name for name in NAMES if name not in self.own)


def forward_layer(source, x, live, params, gathered, weights, plan, last, size, sizes, ident):
    rows, width = source.shape
    count = sizes[0]
    joint, hidden = weights["qkv"].shape[2], weights["up"].shape[2]
    heads = joint // (3 * size)
    attn, slots, span = heads * size, count * rows, rows // 4
    tile = 256 if slots % 256 == 0 else PAD
    columns = {"qkv": joint, "out": attn, "up": hidden, "down": hidden}
    inputs = [(source, VMEM)] + ([] if plan.entry else [(x, VMEM)])
    inputs += [(live, SMEM)] + [(value, HBM) for value in params]
    inputs += [(gathered[name, plan.layer], HBM) for name in plan.held]
    inputs += [(weights[name], HBM) for name in plan.own + plan.ahead]
    saved = [
        ((count, 3 * size, rows), LOW),
        ((size, slots), FULL),
        ((8, slots), FULL),
        ((rows, attn), LOW),
        ((span, width), FULL),
        ((rows, width), LOW),
        ((rows, hidden), LOW),
        ((rows, hidden), LOW),
    ]
    outputs = [((span, width), FULL, VMEM), ((rows, width), LOW, VMEM)]
    outputs += [(shape, dtype, HBM) for shape, dtype in saved]
    if plan.entry:
        outputs.append(((rows, width), LOW, HBM))
    outputs += [((width, columns[name]), LOW, HBM) for name in plan.ahead + plan.own]
    qkv_shape, o_shape, lse_shape, heads_shape = saved[:4]
    scratch = [VMEM((joint, rows), LOW), VMEM((rows, attn), LOW), VMEM((attn, rows), LOW)]
    scratch += [VMEM(*pair) for pair in saved[:3] + saved[4:]]
    if plan.entry:
        scratch.append(VMEM((rows, width), LOW))
    scratch += [
        VMEM((slots, PAD), LOW),
        VMEM((PAD, slots), LOW),
        VMEM((size, slots), LOW),
        VMEM((size, slots), LOW),
        VMEM((2, slots, tile), FULL),
        VMEM((2, 8, tile), FULL),
    ]
    scratch += round_buffers(rows, width) + round_buffers(rows, width)
    scratch += [VMEM((16, slots), LOW), VMEM((16, joint), FULL)]
    scratch += [VMEM(value.shape, value.dtype) for value in params]
    scratch += [VMEM((width, columns[name]), LOW) for name in NAMES + plan.ahead]
    results = run(
        functools.partial(layer_kernel, plan, last, size, tile),
        "forward_layer",
        ident,
        inputs,
        outputs,
        scratch,
        2 * (count - 1) + 2 * ROUND_COPIES + 2 * count * len(plan.own + plan.ahead),
        10 + 2 * len(plan.own + plan.ahead) + len(plan.held) + len(params),
        sizes,
        58,
        2 * rows * width * (2 * hidden + attn + joint) + 4 * slots * slots * 256,
    )
    stream, following = results[:2]
    kept = results[2 : 11 if plan.entry else 10]
    for name, value in zip(plan.ahead, results[2 + len(kept) :]):
        gathered[name, plan.layer + 1] = value
    for name, value in zip(plan.own, results[2 + len(kept) + len(plan.ahead) :]):
        gathered[name, plan.layer] = value
    return stream, following, kept


class SmallSums:
    def __init__(self, mover, rows, held, got):
        self.mover, self.rows, self.held, self.got = mover, rows, held, got
        self.stage = 0
        mate, far = tp_peers()
        self.peers = [
            dict(tp=mate),
            dict(tp=far),
            dict(shard=1 - mover.shard),
            dict(ctx=mover.flip(2)),
            dict(ctx=mover.flip(1)),
        ]

    def part(self, stage):
        return pl.ds(0, self.rows if stage < 2 else self.held.shape[1])

    def step(self):
        stage, mover = self.stage, self.mover
        if stage:
            mover.take(self.copy)
            at = self.part(stage - 1)
            self.held[stage] = self.held[stage - 1]
            self.held[stage, at, :] = self.held[stage - 1, at, :] + self.got[stage - 1, at, :]
        if stage < len(self.peers):
            at = self.part(stage)
            self.copy = mover.go(
                self.held.at[stage, at], self.got.at[stage, at], **self.peers[stage]
            )
        self.stage = stage + 1

    def value(self):
        return self.held[len(self.peers)]


def key_bias(mover, live_ref, bias):
    capacity = bias.shape[1] // mover.ctx_count
    row = lax.broadcasted_iota(jnp.int32, (16, capacity), 0)
    slot = lax.broadcasted_iota(jnp.int32, (16, capacity), 1)
    for r in range(mover.ctx_count):
        live = live_ref[0, mover.back(r)]
        value = jnp.where((row == 0) & (slot >= live), NEG_LARGE, 0.0)
        bias[:, r * capacity : (r + 1) * capacity] = value.astype(LOW)


def pair_columns(rows, width, size, turn):
    shape = (width, rows) if turn else (rows, width)
    given = lax.broadcasted_iota(jnp.int32, shape, 1 if turn else 0)
    column = lax.broadcasted_iota(jnp.int32, shape, 0 if turn else 1)
    head, within = column // (3 * size), column % (3 * size)
    wanted = head * (2 * size) + jnp.where(within < size, within, within - size)
    key = (within >= size) & (within < 2 * size)
    return jnp.where((given == wanted) & ~key, 1.0, 0.0).astype(LOW)


def joint_bias(pair, size, width):
    rows = pair.shape[1]
    spread = jnp.broadcast_to(pair, (16, rows)).astype(LOW)
    return jnp.dot(spread, pair_columns(rows, width, size, False), preferred_element_type=FULL)


def live_rows(value, start, live):
    row = start + lax.broadcasted_iota(jnp.int32, value.shape, 0)
    return jnp.where(row < live, value, 0.0)


def sums_into(sums, first, at, values):
    for index, value in enumerate(values):
        row = first + index
        added = jnp.sum(value, axis=0, keepdims=True)
        width = added.shape[1]
        sums[row : row + 1, 0:width] = (
            added if at.start == 0 else sums[row : row + 1, 0:width] + added
        )


def back_kernel(plan, size, tile, mover, ins, outs, work):
    ins, outs, work = iter(ins), iter(outs), iter(work)
    source = next(ins)
    x_ref = None if plan.last else next(ins)
    live_ref, far_gain2, far_gain1 = [next(ins) for _ in range(3)]
    far = [next(ins) for _ in range(14)]
    late_far = next(ins) if plan.late else None
    others = [(next(ins), next(ins)) for _ in range(plan.others)]
    stream, following = next(outs), next(outs)
    grad_outs = {name: next(outs) for name in NAMES if plan.inside and (name != "qkv" or plan.final)}
    mid_out = next(outs) if plan.inside and not plan.final else None
    late_out = next(outs) if plan.late else None
    split = local = totals = None
    if plan.joined:
        totals = next(outs)
    else:
        split, local = next(outs), next(outs)
    wholes = {} if plan.inside else {name: next(outs) for name in NAMES}
    near = [next(work) for _ in range(14)]
    slope, w_down, w_up, middle, hidden, second, w_out, heads, qkv, o_ref, lse, first, w_qkv, before = near
    grad = next(work) if plan.last else source
    pre_grad, attn_grad, parts, grads, nat = [next(work) for _ in range(5)]
    attend_work = [next(work) for _ in range(13)]
    one_work, two_work = [next(work) for _ in range(5)], [next(work) for _ in range(5)]
    rows, width = source.shape
    reduces = {}
    if plan.inside:
        pairs = {
            "down": (grad, hidden),
            "up": (second, pre_grad),
            "out": (attn_grad, heads),
            "qkv": (first, nat),
        }
        for name in ("down", "up", "out", "qkv"):
            buffers = [next(work) for _ in range(4)]
            reduces[name] = Reduce(mover, buffers, grad_outs.get(name), *pairs[name])
    late = None
    if plan.late:
        late_mid, late_line = next(work), next(work)
        late = Reduce(mover, (late_mid, None, late_mid, late_line), late_out, None, None)
    bias, gain2_ref, gain1_ref = [next(work) for _ in range(3)]
    if plan.joined:
        split, local = next(work), next(work)
        early_held, early_got, late_held, late_got = [next(work) for _ in range(4)]
        tops = 8 * (plan.others + 1)
        early = SmallSums(mover, tops, early_held, early_got)
        final = SmallSums(mover, 8, late_held, late_got)
        everything = [(split, local)] + others

    greet(mover, plan.inside)
    gain_loads = [mover.stay(far_gain2, gain2_ref), mover.stay(far_gain1, gain1_ref)]
    one = Round(mover, rows, attn_grad, one_work)
    two = Round(mover, rows, following, two_work)
    if plan.final:
        far[13] = far[13].at[two.rows(two.own)]
    load = [mover.stay(there, here) for there, here in zip(far, near)]
    if late:
        mover.near(mover.stay(late_far, late_mid))
        late.spread()
    if plan.last:
        chunk = rows // 5 if rows % 80 == 0 else rows

        def mask_step(i, carry):
            at = pl.ds(pl.multiple_of(i * chunk, 16), chunk)
            value = source[at, :].astype(FULL)
            grad[at, :] = live_rows(value, i * chunk, live_ref[0, mover.ctx]).astype(LOW)
            return carry

        lax.fori_loop(0, rows // chunk, mask_step, 0)
    key_bias(mover, live_ref, bias)
    mover.near(*gain_loads)
    gain2, gain1 = [
        ref[...].astype(FULL)[plan.layer : plan.layer + 1] for ref in (gain2_ref, gain1_ref)
    ]
    split[...] = jnp.zeros_like(split)
    local[...] = jnp.zeros_like(local)
    split[5:6, 0:width] = jnp.sum(
        grad[one.rows(one.own), :].astype(FULL), axis=0, keepdims=True
    )
    mover.near(*load[:3])
    hidden_width = slope.shape[1]

    def mlp_part(start):
        at = one.rows(start)
        pre = jnp.dot(grad[at, :], w_down[...], preferred_element_type=FULL)
        low = (pre * slope[at, :].astype(FULL)).astype(LOW)
        pre_grad[at, :] = low
        local[0:1, 0:hidden_width] += jnp.sum(low.astype(FULL), axis=0, keepdims=True)
        return dot(low, w_up[...], ((1,), (1,)))

    def to_attn(at, value):
        if plan.last:
            above = grad[one.rows(one.own + at.start, at.size), :].astype(FULL)
        else:
            above = x_ref[at]
        _, normed, inverse = normalize(middle[at], 1.0, 0.0)
        result = above + normalize_back(value, normed, inverse, gain2)
        stream[at] = result
        low = result.astype(LOW)
        sums_into(split, 2, at, (value * normed, value, low.astype(FULL)))
        return low

    def reduce(name):
        if name in reduces:
            reduces[name].begin()

    def fold(name):
        if name in reduces:
            reduces[name].fold()
            reduces[name].spread()

    def finish(name):
        if name in reduces:
            reduces[name].finish()

    def begin_early():
        if plan.joined:
            early_held[0] = jnp.zeros(early_held.shape[1:], FULL)
            for layer, (some, more) in enumerate(everything):
                first_row = 0 if layer else 2
                for row in range(first_row, 6):
                    at = row * len(everything) + layer
                    early_held[0, at : at + 1, :] = some[row : row + 1, :]
                for row in range(2 if layer else 1):
                    at = tops + row * len(everything) + layer
                    early_held[0, at : at + 1, :] = more[row : row + 1, :]

    def early_step():
        if plan.joined:
            early.step()

    def start_down():
        mover.near(load[3], load[4])
        reduce("down")

    one.eager(mlp_part, to_attn, start_down)
    if late:
        late.finish()
    mover.near(load[5])
    reduce("up")
    one.have()
    mover.near(load[6])
    turned_product(attn_grad, w_out, None, parts)

    def waiting():
        begin_early()
        early_step()
        mover.near(load[7])
        reduce("out")

    def ready():
        mover.near(load[8], load[9], load[10])

    def between(turn):
        if turn == 0:
            early_step()
        if turn == 1:
            finish("down")

    attend_back_part(
        size,
        tile,
        mover,
        parts,
        bias,
        qkv,
        o_ref,
        lse,
        grads,
        attend_work,
        ready,
        waiting,
        lambda: fold("down"),
        between,
    )
    fold("up")
    fold("out")
    early_step()
    nat[...] = turned(grads[...])
    pairs_width = nat.shape[1] // 3 * 2
    picked = jnp.dot(
        nat[...], pair_columns(pairs_width, nat.shape[1], size, True), preferred_element_type=FULL
    )
    local[1:2, 0:pairs_width] = jnp.sum(picked, axis=0, keepdims=True)
    mover.near(*load[11:])

    def qkv_part(start):
        return dot(nat[two.rows(start), :], w_qkv[...], ((1,), (1,)))

    def to_following(at, value):
        row = before[at, :].astype(FULL)
        _, normed, inverse = normalize(row, 1.0, 0.0)
        result = stream[at] + normalize_back(value, normed, inverse, gain1)
        stream[at] = result
        low = result.astype(LOW)
        sums_into(split, 0, at, (value * normed, value))
        return low

    def meanwhile():
        if plan.inside:
            last = reduces["qkv"]
            last.compute(last.mid, mover.shard)
        early_step()
        finish("up")
        finish("out")

    def halfway():
        if plan.inside:
            reduces["qkv"].fold_blocks(3, 1)
            if plan.final:
                reduces["qkv"].spread()

    if plan.inside:
        reduces["qkv"].begin_blocks()
    two.eager(qkv_part, to_following, meanwhile, halfway)
    early_step()
    if plan.joined:
        late_held[0, 0:8, :] = jnp.zeros((8, late_held.shape[2]), FULL)
        late_held[0, 0:2, :] = split[0:2, :]
        late_held[0, 8:16, :] = local[...]
        final.step()
    if plan.inside:
        reduces["qkv"].fold_blocks(2, 0)
        if plan.final:
            reduces["qkv"].finish()
        else:
            mover.stay(reduces["qkv"].mid, mid_out)
    if plan.joined:
        final.step()
    two.have_mate_own()
    two.have_other()
    if plan.joined:
        final.step()
        final.step()
    two.have_mate_other()
    if plan.joined:
        final.step()
    for name in ("down", "up", "out"):
        if name in reduces:
            reduces[name].done()
    if late:
        late.done()
    if plan.inside and plan.final:
        reduces["qkv"].done()
    if plan.joined:
        final.step()
        early.step()
        totals[...] = early.value()
        last_value = final.value()
        for row in range(2):
            at = row * len(everything)
            totals[at : at + 1, :] = last_value[row : row + 1, :]
        at = tops + len(everything)
        totals[at : at + 1, :] = last_value[9:10, :]
    if not plan.inside:
        for name, (lhs, rhs) in {
            "down": (grad, hidden),
            "up": (second, pre_grad),
            "out": (attn_grad, heads),
            "qkv": (first, nat),
        }.items():
            full = Reduce(mover, (wholes[name],) * 4, None, lhs, rhs)
            full.compute(wholes[name], 0)
    mover.settle()


def gather_outputs_kernel(layers, *refs):
    count = layers * len(NAMES)
    parts, token_grads, mixed, totals = refs[:count], refs[count], refs[count + 1], refs[count + 2]
    outs, work = refs[count + 3 : count + 17], refs[count + 17 : -2]
    into, out_of = refs[-2:]
    coming, going = [], []
    pairs = [(mixed, work[4], outs[4].at[0])]
    for index in range(len(NAMES)):
        for layer in range(layers):
            pairs.append(
                (parts[index * layers + layer], work[index].at[layer], outs[index].at[layer])
            )
    for i, (source, stage, _) in enumerate(pairs):
        coming.append(pltpu.make_async_copy(source, stage, into.at[i]))
        coming[-1].start()
    outs[5][0] = token_grads[...].astype(FULL)
    for row, out in enumerate(outs[6:12]):
        out[...] = totals[row * layers : (row + 1) * layers, 0 : out.shape[1]]
    for row, out in enumerate(outs[12:14]):
        row = row + 8
        out[...] = totals[row * layers : (row + 1) * layers, 0 : out.shape[1]]
    for i, (_, stage, target) in enumerate(pairs):
        coming[i].wait()
        going.append(pltpu.make_async_copy(stage, target, out_of.at[i]))
        going[-1].start()
    for copy in going:
        copy.wait()


def gather_outputs(done, token_grads, mixed, totals, layers, widths):
    rows, width = token_grads.shape
    parts = [done[name, layer] for name in NAMES for layer in range(layers)]
    hbm, whole = pl.BlockSpec(memory_space=HBM), lambda shape: pl.BlockSpec(
        shape, lambda i: (0,) * len(shape)
    )
    shapes = [(layers,) + done[name, 0].shape for name in NAMES] + [(1, rows, width)] * 2
    types = [FULL] * 4 + [LOW, FULL]
    small = [(layers, width)] * 6 + [(layers, count) for count in widths]
    copies = len(parts) + 1
    return pl.pallas_call(
        functools.partial(gather_outputs_kernel, layers),
        grid=(1,),
        in_specs=[hbm] * len(parts) + [whole(token_grads.shape), hbm, whole(totals.shape)],
        out_specs=[hbm] * 5 + [whole(shape) for shape in shapes[5:] + small],
        out_shape=[jax.ShapeDtypeStruct(*pair) for pair in zip(shapes, types)]
        + [jax.ShapeDtypeStruct(shape, FULL) for shape in small],
        scratch_shapes=[VMEM(shape, FULL) for shape in shapes[:4]]
        + [VMEM((rows, width), LOW)]
        + [pltpu.SemaphoreType.DMA((copies,)), pltpu.SemaphoreType.DMA((copies,))],
        compiler_params=pltpu.CompilerParams(vmem_limit_bytes=60 * 2**20),
        name="gather_outputs",
    )(*parts, token_grads, mixed, totals)


class BackPlan:
    def __init__(self, layer, layers, inside):
        self.inside, self.layer = inside, layer
        self.last, self.final = layer == layers - 1, layer == 0
        self.late = inside and not self.last
        self.joined = inside and self.final
        self.others = layers - 1 if self.joined else 0


def back_layer(source, x, live, gain2, gain1, saved, late, others, plan, size, sizes, ident):
    rows, width = source.shape
    count = sizes[0]
    slope, w_down, w_up = saved[:3]
    hidden, joint, attn = slope.shape[1], saved[12].shape[1], saved[6].shape[1]
    slots, span = count * rows, rows // 4
    tile = 256 if slots % 256 == 0 else PAD
    wide = max(width, hidden, joint)
    half = width // 2
    block = half // count
    columns = {"qkv": joint, "out": attn, "up": hidden, "down": hidden}
    inputs = [(source, VMEM)] + ([] if plan.last else [(x, VMEM)])
    inputs += [(live, SMEM), (gain2, HBM), (gain1, HBM)]
    inputs += [(value, HBM) for value in saved]
    if plan.late:
        inputs.append((late, HBM))
    for pair in others[: plan.others]:
        inputs += [(value, VMEM) for value in pair]
    outputs = [((span, width), FULL, VMEM), ((rows, width), LOW, VMEM)]
    names = [name for name in NAMES if plan.inside and (name != "qkv" or plan.final)]
    outputs += [((block, columns[name]), FULL, VMEM) for name in names]
    if plan.inside and not plan.final:
        outputs.append(((half, joint), LOW, HBM))
    if plan.late:
        outputs.append(((block, joint), FULL, VMEM))
    depth = 8 * (plan.others + 1)
    if plan.joined:
        outputs.append(((depth + 8, wide), FULL, VMEM))
    else:
        outputs += [((8, wide), FULL, VMEM)] * 2
    if not plan.inside:
        outputs += [((width, columns[name]), LOW, VMEM) for name in NAMES]
    scratch = [VMEM(value.shape, value.dtype) for value in saved]
    scratch[13] = VMEM((span, width), saved[13].dtype)
    if plan.last:
        scratch.append(VMEM((rows, width), LOW))
    scratch += [
        VMEM((rows, hidden), LOW),
        VMEM((rows, width), LOW),
        VMEM((attn, rows), LOW),
        VMEM((joint, rows), LOW),
        VMEM((rows, joint), LOW),
    ]
    scratch += attend_back_buffers(size, count, rows, tile)
    scratch += round_buffers(rows, width) + round_buffers(rows, width)
    if plan.inside:
        for name in ("down", "up", "out", "qkv"):
            scratch += reduce_buffers(half, columns[name], count)
    if plan.late:
        scratch += [VMEM((half, joint), LOW), VMEM((count - 1, block, joint), LOW)]
    scratch.append(VMEM((16, slots), LOW))
    scratch += [VMEM(value.shape, value.dtype) for value in (gain2, gain1)]
    assert 2 * (plan.others + 1) <= 8
    if plan.joined:
        scratch += [VMEM((8, wide), FULL)] * 2
        scratch += [
            VMEM((6, depth + 8, wide), FULL),
            VMEM((5, depth + 8, wide), FULL),
            VMEM((6, 16, wide), FULL),
            VMEM((5, 16, wide), FULL),
        ]
    results = run(
        functools.partial(back_kernel, plan, size, tile),
        "back_layer",
        ident,
        inputs,
        outputs,
        scratch,
        3 * (count - 1) + 2 * ROUND_COPIES + 6 * count + 10 + count,
        len(saved) + 4,
        sizes,
        58,
        6 * rows * width * (2 * hidden + attn + joint) + 10 * slots * slots * 256,
    )
    return results[:2], names, results[2:]


def shards(
    tokens,
    block_tokens,
    ln1_gain,
    ln1_bias,
    w_qkv,
    b_qv,
    w_out,
    b_out,
    ln2_gain,
    ln2_bias,
    w_up,
    b_up,
    w_down,
    b_down,
    cotangent,
):
    images, capacity, width = tokens.shape
    assert images == 1
    layers = w_qkv.shape[0]
    size = HEAD_DIM
    ctx_count = lax.axis_size("ctx")
    ctx_place = lax.axis_index("ctx")
    joint_width = w_qkv.shape[2]
    heads = joint_width // (3 * size)
    assert heads == ctx_count
    attn_width = heads * size
    hidden_width = w_up.shape[2]
    weights = {"qkv": w_qkv, "out": w_out, "up": w_up, "down": w_down}
    sizes = (ctx_count, lax.axis_size("shard"))
    inside = sizes == (4, 2)
    gathered = {}
    if not inside:
        for name, value in weights.items():
            for layer in range(layers):
                gathered[name, layer] = gather_weight(value[layer])[0]
    source, stream = tokens[0], None
    saved = []
    for layer in range(layers):
        last = layer == layers - 1
        result, following, kept = forward_layer(
            source,
            stream,
            block_tokens,
            (b_out, ln2_gain, ln2_bias, b_down, ln1_gain, ln1_bias, b_up, b_qv),
            gathered,
            weights,
            Plan(layer, last, inside),
            last,
            size,
            sizes,
            1 + layer,
        )
        before = stream if layer else source
        first = source if layer else kept[8]
        saved.append((before, first) + tuple(kept[:8]))
        source, stream = following, result
    mixed = source

    done, packs = {}, {}
    source, stream, late = cotangent[0], None, None
    for layer in reversed(range(layers)):
        before, first, qkv, head_out, lse, heads_low, middle, second, hidden, slope = saved[layer]
        plan = BackPlan(layer, layers, inside)
        whole = {name: gathered[name, layer] for name in NAMES}
        near = [slope, whole["down"], whole["up"], middle, hidden, second, whole["out"]]
        near += [heads_low, qkv, head_out, lse, first, whole["qkv"], before]
        others = [packs[key] for key in sorted(packs)]
        (stream, source), names, rest = back_layer(
            source, stream, block_tokens, ln2_gain, ln1_gain, near, late, others, plan, size, sizes, 1 + layers + layer
        )
        rest = iter(rest)
        for name in names:
            done[name, layer] = next(rest)
        if plan.inside and not plan.final:
            late = next(rest)
        if plan.late:
            done["qkv", layer + 1] = next(rest)
        if plan.joined:
            totals = next(rest)
        else:
            packs[layer] = (next(rest), next(rest))
        if not inside:
            for name in NAMES:
                value = next(rest)
                done[name, layer] = scatter_weight(
                    lambda start, count, value=value: rows_of(value, start, count).astype(FULL),
                    width,
                )
    if not inside:
        split = total_over(("tp",), jnp.stack([packs[l][0] for l in range(layers)], axis=1))
        local = jnp.stack([packs[l][1] for l in range(layers)], axis=1)
        totals = total_over(("shard", "ctx"), jnp.concatenate([split, local[:2]]))
        totals = totals.reshape(10 * layers, -1)
    pairs = b_qv.shape[1]
    outs = gather_outputs(done, source, mixed, totals, layers, (hidden_width, pairs))
    g_qkv, g_out, g_up, g_down, mixed, token_grads = outs[:6]
    g_ln1_gain, g_ln1_bias, g_ln2_gain, g_ln2_bias, g_b_out, g_b_down, g_b_up, g_b_qv = outs[6:]
    return (
        mixed,
        token_grads,
        g_ln1_gain,
        g_ln1_bias,
        g_qkv,
        g_b_qv,
        g_out,
        g_b_out,
        g_ln2_gain,
        g_ln2_bias,
        g_up,
        g_b_up,
        g_down,
        g_b_down,
    )


def solution(mesh):
    split_rows = P(None, ("shard", "ctx"), "tp")
    split_tokens = P("shard", "ctx", None)
    return jax.shard_map(
        shards,
        mesh=mesh,
        in_specs=(
            split_tokens,
            P("shard", None),
            P(),
            P(),
            split_rows,
            P(None, "tp"),
            split_rows,
            P(),
            P(),
            P(),
            split_rows,
            P(None, "tp"),
            split_rows,
            P(),
            split_tokens,
        ),
        out_specs=(
            split_tokens,
            split_tokens,
            P(),
            P(),
            split_rows,
            P(None, "tp"),
            split_rows,
            P(),
            P(),
            P(),
            split_rows,
            P(None, "tp"),
            split_rows,
            P(),
        ),
        check_vma=False,
    )
```

```python
import functools
import math

import jax
import jax.numpy as jnp
from jax import lax
from jax.experimental import pallas as pl
from jax.experimental.pallas import tpu as pltpu
from jax.sharding import PartitionSpec as P

HEAD_DIM = 64
EPSILON = 1e-06
NEG_LARGE = -1e30
LOW = jnp.bfloat16
FULL = jnp.float32
PAD = 128
MESH = pl.DeviceIdType.MESH
VMEM = pltpu.VMEM
HBM = pltpu.HBM
SMEM = pltpu.SMEM


def bits_of(axis):
    size = lax.axis_size(axis)
    assert size & (size - 1) == 0
    return [1 << i for i in range(size.bit_length() - 1)]


def swap(value, axis, bit):
    size = lax.axis_size(axis)
    return lax.ppermute(value, axis, [(i, i ^ bit) for i in range(size)])


def side_of(axis, bit):
    return (lax.axis_index(axis) // bit) % 2


def rows_of(value, start, count, axis=0):
    return lax.dynamic_slice_in_dim(value, start, count, axis)


def halve(axis, bits, partial, total):
    offset, span, received = jnp.int32(0), total, []

    def summed(start, count):
        value = partial(start, count)
        for got, base in received:
            value = value + rows_of(got, start - base, count).astype(FULL)
        return value

    for bit in bits:
        half = span // 2
        side = side_of(axis, bit)
        got = swap(summed(offset + (1 - side) * half, half).astype(LOW), axis, bit)
        offset = offset + side * half
        received.append((got, offset))
        span = half
    return summed(offset, span)


def double(axis, bits, value):
    for bit in bits:
        got = swap(value, axis, bit)
        first = side_of(axis, bit) == 0
        value = jnp.concatenate(
            [jnp.where(first, value, got), jnp.where(first, got, value)], axis=0
        )
    return value


def total_over(axes, value):
    for axis in axes:
        for bit in bits_of(axis):
            value = value + swap(value, axis, bit)
    return value


def ring(value, by):
    count = lax.axis_size("ctx")
    return lax.ppermute(value, "ctx", [(i, (i + by) % count) for i in range(count)])


def gather_weight(piece):
    count = lax.axis_size("ctx")
    place = lax.axis_index("ctx")
    ways = lax.axis_size("shard")
    blocks = [piece] + [ring(piece, by) for by in range(1, count)]
    whole = jnp.zeros((ways * count,) + piece.shape, piece.dtype)
    me = lax.axis_index("shard")
    for by, block in enumerate(blocks):
        at = (place - by) % count
        held = [(jnp.int32(0), block)]
        for bit in bits_of("shard"):
            held = held + [(other ^ bit, swap(value, "shard", bit)) for other, value in held]
        for other, value in held:
            whole = lax.dynamic_update_index_in_dim(whole, value, (me ^ other) * count + at, 0)
    return whole.reshape((ways * count * piece.shape[0],) + piece.shape[1:]), blocks[-1]


def scatter_weight(partial, total):
    count = lax.axis_size("ctx")
    place = lax.axis_index("ctx")
    mine = halve("shard", bits_of("shard")[::-1], partial, total).astype(LOW)
    mine = mine.reshape((count, mine.shape[0] // count) + mine.shape[1:])
    value = lax.dynamic_index_in_dim(mine, place, 0, False).astype(FULL)
    for by in range(1, count):
        given = lax.dynamic_index_in_dim(mine, (place + by) % count, 0, False)
        value = value + ring(given, by).astype(FULL)
    return value


def dot(left, right, contract):
    return lax.dot_general(
        left, right, ((contract[0], contract[1]), ((), ())), preferred_element_type=FULL
    )


def turned(value):
    return value.astype(FULL).T.astype(LOW)


def normalize(rows, gain, shift):
    row_mean = jnp.mean(rows, axis=-1, keepdims=True)
    centred = rows - row_mean
    inverse = lax.rsqrt(jnp.mean(centred * centred, axis=-1, keepdims=True) + EPSILON)
    normed = centred * inverse
    return (normed * gain + shift, normed, inverse)


def normalize_back(grad_out, normed, inverse, gain):
    scaled = grad_out * gain
    mean_grad = jnp.mean(scaled, axis=-1, keepdims=True)
    mean_cross = jnp.mean(scaled * normed, axis=-1, keepdims=True)
    return inverse * (scaled - mean_grad - normed * mean_cross)


def gelu_pair(value):
    spread = 0.5 * (1.0 + lax.erf(value * (0.5**0.5)))
    slope = spread + value * jnp.exp(-0.5 * value * value) * (1.0 / math.sqrt(2.0 * math.pi))
    return (value * spread).astype(LOW), slope.astype(LOW)


class Mover:
    def __init__(self, sizes, send, recv, local):
        self.ctx_count, self.shard_count = sizes
        self.send, self.recv, self.local = send, recv, local
        self.copies, self.here = [], []
        self.arrived = set()
        self.landed = set()
        self.ctx = lax.axis_index("ctx")
        self.shard = lax.axis_index("shard")

    def go(self, source, target, **device):
        index = len(self.copies)
        assert index < self.send.shape[0]
        copy = pltpu.make_async_remote_copy(
            src_ref=source,
            dst_ref=target,
            send_sem=self.send.at[index],
            recv_sem=self.recv.at[index],
            device_id=device,
            device_id_type=MESH,
        )
        copy.start()
        self.copies.append(copy)
        return index

    def stay(self, source, target):
        index = len(self.here)
        assert index < self.local.shape[0]
        copy = pltpu.make_async_copy(source, target, self.local.at[index])
        copy.start()
        self.here.append(copy)
        return index

    def near(self, *indices):
        for index in indices:
            if index not in self.landed:
                self.landed.add(index)
                self.here[index].wait()

    def take(self, index):
        if index not in self.arrived:
            self.arrived.add(index)
            self.copies[index].wait_recv()

    def flip(self, bits):
        place = self.ctx
        if bits & 1:
            place = place + 1 - 2 * lax.rem(self.ctx, 2)
        if bits & 2:
            place = place + 2 - 4 * (self.ctx // 2)
        return place

    def on(self, by):
        return lax.rem(self.ctx + by, self.ctx_count)

    def back(self, by):
        return lax.rem(self.ctx + self.ctx_count - by, self.ctx_count)

    def settle(self):
        for index, copy in enumerate(self.copies):
            self.take(index)
            copy.wait_send()
        self.near(*range(len(self.here)))


class Gather:
    def __init__(self, mover, source, target):
        self.mover, self.source, self.target = mover, source, target
        self.over = []

    def start(self):
        self.start_line()
        self.start_over()

    def start_line(self):
        mover = self.mover
        mine, there = self.source, self.block(mover.ctx)
        self.far = mover.go(mine, there, ctx=mover.flip(2))
        self.close = mover.go(mine, there, ctx=mover.flip(1))

    def start_over(self):
        mover = self.mover
        mine, there = self.source, self.block(mover.ctx)
        self.over.append(mover.go(mine, there, shard=1 - mover.shard))
        self.own = mover.stay(mine, there)

    def block(self, ctx):
        mover = self.mover
        rows = self.source.shape[0]
        start = (mover.shard * mover.ctx_count + ctx) * rows
        return self.target.at[pl.ds(pl.multiple_of(start, rows), rows)]

    def pass_on(self, stage):
        mover = self.mover
        if stage == 1:
            mover.take(self.far)
            rows = self.block(mover.flip(2))
            self.passed = mover.go(rows, rows, ctx=mover.flip(1))
        elif stage == 2:
            mover.take(self.close)
            rows = self.block(mover.flip(1))
        else:
            mover.take(self.passed)
            rows = self.block(mover.flip(3))
        self.over.append(mover.go(rows, rows, shard=1 - mover.shard))

    def have(self):
        for copy in self.over:
            self.mover.take(copy)
        self.mover.near(self.own)


class Reduce:
    def __init__(self, mover, buffers, out, lhs, rhs):
        self.mover, self.out, self.lhs, self.rhs = mover, out, lhs, rhs
        self.give, self.got, self.mid, self.line = buffers
        self.half = self.give.shape[0]
        self.block = self.half // mover.ctx_count

    def compute(self, target, shard):
        chunk = min(256, self.half)

        def step(i, carry):
            at = pl.ds(pl.multiple_of(shard * self.half + i * chunk, chunk), chunk)
            here = pl.ds(pl.multiple_of(i * chunk, chunk), chunk)
            target[here, :] = dot(self.lhs[:, at], self.rhs[...], ((0,), (0,))).astype(LOW)
            return carry

        lax.fori_loop(0, self.half // chunk, step, 0)

    def begin_blocks(self):
        mover = self.mover
        self.blocks = {}
        for bits in (3, 1, 2, 0):
            ctx = mover.flip(bits)
            at = pl.ds(pl.multiple_of(ctx * self.block, self.block), self.block)
            start = pl.multiple_of((1 - mover.shard) * self.half + ctx * self.block, self.block)
            lhs = self.lhs[:, pl.ds(start, self.block)]
            self.give[at, :] = dot(lhs, self.rhs[...], ((0,), (0,))).astype(LOW)
            self.blocks[bits] = mover.go(
                self.give.at[at], self.got.at[at], shard=1 - mover.shard
            )

    def own(self):
        self.compute(self.mid, self.mover.shard)

    def fold_blocks(self, *which):
        mover = self.mover
        for bits in which:
            mover.take(self.blocks[bits])
            ctx = mover.flip(bits)
            at = pl.ds(pl.multiple_of(ctx * self.block, self.block), self.block)
            self.mid[at, :] = (
                self.mid[at, :].astype(FULL) + self.got[at, :].astype(FULL)
            ).astype(LOW)

    def rows(self, ctx):
        return self.mid.at[pl.ds(pl.multiple_of(ctx * self.block, self.block), self.block)]

    def spread(self):
        mover = self.mover
        self.first = mover.go(self.rows(mover.flip(3)), self.line.at[1], ctx=mover.flip(1))
        self.second = mover.go(self.rows(mover.flip(1)), self.line.at[0], ctx=mover.flip(1))

    def finish(self):
        mover = self.mover
        mover.take(self.first)
        rows = self.rows(mover.flip(2))
        rows[...] = (rows[...].astype(FULL) + self.line[1].astype(FULL)).astype(LOW)
        self.third = mover.go(rows, self.line.at[2], ctx=mover.flip(2))

    def done(self):
        self.mover.take(self.second)
        self.mover.take(self.third)
        value = self.rows(self.mover.ctx)[...].astype(FULL)
        self.out[...] = value + self.line[0].astype(FULL) + self.line[2].astype(FULL)


def reduce_buffers(half, width, count):
    return [
        VMEM((half, width), LOW),
        VMEM((half, width), LOW),
        VMEM((half, width), LOW),
        VMEM((count - 1, half // count, width), LOW),
    ]


def greet(mover, shard):
    barrier = pltpu.get_barrier_semaphore()
    peers = [dict(ctx=mover.on(by)) for by in range(1, mover.ctx_count)]
    peers += [dict(tp=peer) for peer in tp_peers()]
    if shard:
        peers.append(dict(shard=1 - mover.shard))
    for peer in peers:
        pl.semaphore_signal(barrier, inc=1, device_id=peer, device_id_type=MESH)
    pl.semaphore_wait(barrier, len(peers))


def tp_peers():
    place = lax.axis_index("tp")
    core, far = lax.rem(place, 2), place // 2
    return place + 1 - 2 * core, place + 2 - 4 * far


def run(kernel, name, ident, inputs, outputs, scratch, remote, local, sizes, vmem, flops):
    n_in, n_out, n_scratch = len(inputs), len(outputs), len(scratch)

    def body(*refs):
        ins, outs = refs[:n_in], refs[n_in : n_in + n_out]
        work = refs[n_in + n_out :]
        mover = Mover(sizes, *work[n_scratch:])
        kernel(mover, ins, outs, work[:n_scratch])

    return pl.pallas_call(
        body,
        in_specs=[pl.BlockSpec(memory_space=space) for _, space in inputs],
        out_specs=[pl.BlockSpec(memory_space=space) for _, _, space in outputs],
        out_shape=[jax.ShapeDtypeStruct(shape, dtype) for shape, dtype, _ in outputs],
        scratch_shapes=list(scratch)
        + [
            pltpu.SemaphoreType.DMA((remote,)),
            pltpu.SemaphoreType.DMA((remote,)),
            pltpu.SemaphoreType.DMA((local,)),
        ],
        compiler_params=pltpu.CompilerParams(
            collective_id=ident, has_side_effects=True, vmem_limit_bytes=vmem * 2**20
        ),
        cost_estimate=pl.CostEstimate(flops=flops, bytes_accessed=2**24, transcendentals=0),
        name=name,
    )(*[value for value, _ in inputs])


def order_of(block, count):
    return (block + count - 1) % count


def tiles_of(count, capacity, tile):
    ends = [-(-(p + 1) * capacity // tile) for p in range(count)]
    return list(zip([0] + ends[:-1], ends))


def parts_of(capacity):
    middle = capacity // 2 // PAD * PAD
    return [(0, middle), (middle, capacity)] if middle else [(0, capacity)]


def tile_at(t, tile):
    return pl.ds(pl.multiple_of(t * tile, tile), tile)


def turned_product(left, right, bias, target):
    def step(i, carry):
        at = pl.ds(pl.multiple_of(i * PAD, PAD), PAD)
        value = jnp.dot(left[at, :], right[...], preferred_element_type=FULL)
        if bias is not None:
            value = value + bias[0:1, :]
        target[:, at] = turned(value.astype(LOW))
        return carry

    lax.fori_loop(0, left.shape[0] // PAD, step, 0)


def head_rows(ref, head, width):
    return ref.at[pl.ds(pl.multiple_of(head * width, 16), width)]


def attend_part(size, tile, mover, joint, bias, heads, qkv, o_ref, lse, work, after_send, begun, between):
    k_ref, q_ref, v_ref, low_ref, score_ref, top_ref = work
    count, width, capacity = qkv.shape
    slots = count * capacity
    sent = [None] + [
        mover.go(head_rows(joint, mover.on(by), width), qkv.at[by], ctx=mover.on(by))
        for by in range(1, count)
    ]
    after_send()
    qkv[0] = head_rows(joint, mover.ctx, width)[...]
    q_ref[size:PAD, :] = jnp.concatenate(
        [jnp.ones((16, slots), LOW), jnp.zeros((PAD - size - 16, slots), LOW)], axis=0
    )

    def prepare(r):
        here = slice(r * capacity, (r + 1) * capacity)
        p = order_of(r, count)
        q_ref[0:size, p * capacity : (p + 1) * capacity] = (
            qkv[r, 0:size, :] * (size**-0.5)
        ).astype(LOW)
        v_ref[:, here] = qkv[r, 2 * size : 3 * size, :]
        keys = jnp.concatenate(
            [qkv[r, size : 2 * size, :], bias[:, here], jnp.zeros((PAD - size - 16, capacity), LOW)],
            axis=0,
        )
        k_ref[here, :] = turned(keys)

    prepare(0)
    for by in range(1, count):
        mover.take(sent[by])
        prepare(by)

    begun()
    last = slots // tile - 1
    assert last % 2 == 1

    def phase(t, now, following, then):
        at, ahead = tile_at(t, tile), tile_at(following, tile)
        top = top_ref[now, 0:1, :]
        total = jnp.zeros((1, tile), FULL)
        summed = jnp.zeros((size, tile), FULL)
        new_top = jnp.full((1, tile), NEG_LARGE, FULL)
        for r in range(count):
            here = slice(r * capacity, (r + 1) * capacity)
            scores = jnp.dot(k_ref[here, :], q_ref[:, ahead], preferred_element_type=FULL)
            score_ref[then, here, :] = scores
            new_top = jnp.maximum(new_top, jnp.max(scores, axis=0, keepdims=True))
            weights = jnp.exp(score_ref[now, here, :] - top)
            total = total + jnp.sum(weights, axis=0, keepdims=True)
            summed = summed + jnp.dot(
                v_ref[:, here], weights.astype(LOW), preferred_element_type=FULL
            )
        top_ref[then] = jnp.broadcast_to(new_top, (8, tile))
        out = summed / total
        o_ref[:, at] = out
        low_ref[:, at] = out.astype(LOW)
        lse[:, at] = jnp.broadcast_to(top + jnp.log(total), (8, tile))

    def step(i, carry):
        phase(2 * i, 0, 2 * i + 1, 1)
        phase(2 * i + 1, 1, jnp.minimum(2 * i + 2, last), 0)
        return carry

    scores = jnp.dot(k_ref[...], q_ref[:, 0:tile], preferred_element_type=FULL)
    score_ref[0] = scores
    top_ref[0] = jnp.broadcast_to(jnp.max(scores, axis=0, keepdims=True), (8, tile))
    arriving = []
    for p, (low, high) in enumerate(tiles_of(count, capacity, 2 * tile)):
        lax.fori_loop(low, high, step, 0)
        done = low_ref.at[:, p * capacity : (p + 1) * capacity]
        if p < count - 1:
            there = head_rows(heads, mover.ctx, size)
            arriving.append(mover.go(done, there, ctx=mover.back(p + 1)))
        else:
            head_rows(heads, mover.ctx, size)[...] = low_ref[:, p * capacity : (p + 1) * capacity]
        between(p + 1)
    for copy in arriving:
        mover.take(copy)


def attend_back_part(size, tile, mover, parts, bias, qkv, o_ref, lse, grads, work, ready, waiting, begun, between):
    k_ref, v_ref, q_ref, do_ref, nat_ref, delta_ref, dq_ref, dk_ref, dv_ref, got, back, score_ref, grad_ref = work
    count, width, capacity = qkv.shape
    slots = count * capacity
    sent = [None] + [
        mover.go(head_rows(parts, mover.on(by), size), got.at[by], ctx=mover.on(by))
        for by in range(1, count)
    ]
    got[0] = head_rows(parts, mover.ctx, size)[...]
    waiting()
    ready()
    q_ref[size:PAD, :] = jnp.concatenate(
        [jnp.ones((16, slots), LOW), jnp.zeros((PAD - size - 16, slots), LOW)], axis=0
    )
    do_ref[size:PAD, :] = jnp.zeros((PAD - size, slots), LOW)
    dq_ref[...] = jnp.zeros_like(dq_ref)
    for r in range(count):
        here = slice(r * capacity, (r + 1) * capacity)
        pad = jnp.zeros((PAD - size - 16, capacity), LOW)
        k_ref[here, :] = turned(
            jnp.concatenate([qkv[r, size : 2 * size, :], bias[:, here], pad], axis=0)
        )
        v_ref[here, :] = turned(
            jnp.concatenate(
                [qkv[r, 2 * size : 3 * size, :], jnp.zeros((PAD - size, capacity), LOW)], axis=0
            )
        )
    for r in range(count):
        if r:
            mover.take(sent[r])
        p = order_of(r, count)
        at = slice(p * capacity, (p + 1) * capacity)
        scaled = (qkv[r, 0:size, :] * (size**-0.5)).astype(LOW)
        dout = got[r]
        q_ref[0:size, at] = scaled
        do_ref[0:size, at] = dout
        nat_ref[at, :] = turned(jnp.concatenate([scaled, dout], axis=0))
        delta = jnp.sum(dout.astype(FULL) * o_ref[:, at], axis=0, keepdims=True)
        delta_ref[:, at] = jnp.broadcast_to(delta, (8, capacity))

    begun()
    last = slots // tile - 1
    assert last % 2 == 1
    tiles = tiles_of(count, capacity, 2 * tile)
    arriving = []
    mine = head_rows(grads, mover.ctx, width)
    for turn, r in enumerate(list(range(1, count)) + [0]):
        here = slice(r * capacity, (r + 1) * capacity)
        dk_ref[...] = jnp.zeros_like(dk_ref)
        dv_ref[...] = jnp.zeros_like(dv_ref)

        def ready_scores(t, then, low, high, r=r):
            ahead = tile_at(t, tile)
            rows = slice(r * capacity + low, r * capacity + high)
            score_ref[then, low:high, :] = jnp.dot(
                k_ref[rows, :], q_ref[:, ahead], preferred_element_type=FULL
            )
            grad_ref[then, low:high, :] = jnp.dot(
                v_ref[rows, :], do_ref[:, ahead], preferred_element_type=FULL
            )

        def phase(t, now, following, then, r=r):
            at = tile_at(t, tile)
            query_grad = jnp.zeros((size, tile), FULL)
            for low, high in parts_of(capacity):
                ready_scores(following, then, low, high)
                chance = jnp.exp(score_ref[now, low:high, :] - lse[0:1, at])
                score_grad = (
                    chance * (grad_ref[now, low:high, :] - delta_ref[0:1, at])
                ).astype(LOW)
                query_grad = query_grad + jnp.dot(
                    qkv[r, size : 2 * size, low:high], score_grad, preferred_element_type=FULL
                )
                dk_ref[low:high, :] += jnp.dot(
                    score_grad, nat_ref[at, :], preferred_element_type=FULL
                )
                dv_ref[low:high, :] += jnp.dot(
                    chance.astype(LOW), nat_ref[at, :], preferred_element_type=FULL
                )
            dq_ref[:, at] += query_grad

        def step(i, carry, phase=phase):
            phase(2 * i, 0, 2 * i + 1, 1)
            phase(2 * i + 1, 1, jnp.minimum(2 * i + 2, last), 0)
            return carry

        ready_scores(0, 0, 0, capacity)
        if r:
            lax.fori_loop(0, tiles[-1][1], step, 0)
        else:
            for p, (low, high) in enumerate(tiles):
                lax.fori_loop(low, high, step, 0)
                at = slice(p * capacity, (p + 1) * capacity)
                value = (dq_ref[:, at] * (size**-0.5)).astype(LOW)
                if p < count - 1:
                    back[p + 1, 0:size, :] = value
                    arriving.append(
                        mover.go(
                            back.at[p + 1, 0:size], mine.at[0:size], ctx=mover.back(p + 1)
                        )
                    )
                else:
                    mine[0:size, :] = value
        keys = dk_ref[...].T[0:size].astype(LOW)
        values = dv_ref[...].T[size : 2 * size].astype(LOW)
        if r:
            back[r, size : 2 * size, :] = keys
            back[r, 2 * size : 3 * size, :] = values
            arriving.append(
                mover.go(
                    back.at[r, size : 3 * size], mine.at[size : 3 * size], ctx=mover.back(r)
                )
            )
        else:
            mine[size : 2 * size, :] = keys
            mine[2 * size : 3 * size, :] = values
        between(turn)
    for copy in arriving:
        mover.take(copy)


def attend_back_buffers(size, count, capacity, tile):
    slots = count * capacity
    return [
        VMEM((slots, PAD), LOW),
        VMEM((slots, PAD), LOW),
        VMEM((PAD, slots), LOW),
        VMEM((PAD, slots), LOW),
        VMEM((slots, PAD), LOW),
        VMEM((8, slots), FULL),
        VMEM((size, slots), FULL),
        VMEM((capacity, PAD), FULL),
        VMEM((capacity, PAD), FULL),
        VMEM((count, size, capacity), LOW),
        VMEM((count, 3 * size, capacity), LOW),
        VMEM((2, capacity, tile), FULL),
        VMEM((2, capacity, tile), FULL),
    ]


class Round:
    def __init__(self, mover, rows, full, buffers):
        place = lax.axis_index("tp")
        core, far = lax.rem(place, 2), place // 2
        self.mover, self.full = mover, full
        self.give, self.ra, self.passing, self.rb, self.keep = buffers
        self.span = rows // 4
        self.half = self.span // 2
        self.mate, self.far = tp_peers()

        def quarter(c, f):
            return (c * 2 + f) * self.span

        self.own, self.other = quarter(core, far), quarter(core, 1 - far)
        self.mate_own, self.mate_other = quarter(1 - core, far), quarter(1 - core, 1 - far)

    def rows(self, start, count=None):
        return pl.ds(pl.multiple_of(start, 16), count or self.span)

    def hand(self, slot, value):
        self.give[slot] = value.astype(LOW)
        return self.mover.go(self.give.at[slot], self.ra.at[slot], tp=self.mate)

    def onward(self, value, index):
        self.mover.take(index)
        self.passing[...] = (value + self.ra[1].astype(FULL)).astype(LOW)
        return [
            self.mover.go(self.passing.at[at], self.rb.at[at], tp=self.far)
            for at in (pl.ds(0, self.half), pl.ds(self.half, self.half))
        ]

    def close(self, far_copies, index, finish, halfway=None):
        self.mover.take(index)
        self.keep[...] += self.ra[0].astype(FULL)
        self.to_far, self.to_mate = [], []
        for c in range(2):
            at = pl.ds(c * self.half, self.half)
            self.mover.take(far_copies[c])
            low = finish(at, self.keep[at] + self.rb[at].astype(FULL))
            mine = self.full.at[self.rows(self.own + c * self.half, self.half)]
            mine[...] = low
            self.to_far.append(self.mover.go(mine, mine, tp=self.far))
            self.to_mate.append(self.mover.go(mine, mine, tp=self.mate))
            if halfway and c == 0:
                halfway()

    def eager(self, make, finish, meanwhile=None, halfway=None):
        first = self.hand(1, make(self.mate_other))
        copies = self.onward(make(self.other), first)
        second = self.hand(0, make(self.mate_own))
        self.keep[...] = make(self.own)
        if meanwhile:
            meanwhile()
        self.close(copies, second, finish, halfway)

    def after(self, before, make, finish, meanwhile=None, halfway=None):
        before.have_mate_own()
        second = self.hand(0, make(self.mate_own))
        self.keep[...] = make(self.own)
        before.have_other()
        value = make(self.other)
        before.have_mate_other()
        first = self.hand(1, make(self.mate_other))
        copies = self.onward(value, first)
        if meanwhile:
            meanwhile()
        self.close(copies, second, finish, halfway)

    def have_mate_own(self):
        for copy in self.to_mate:
            self.mover.take(copy)

    def have_other(self):
        self.passed = []
        for c in range(2):
            self.mover.take(self.to_far[c])
            rows = self.full.at[self.rows(self.other + c * self.half, self.half)]
            self.passed.append(self.mover.go(rows, rows, tp=self.mate))

    def have_mate_other(self):
        for copy in self.passed:
            self.mover.take(copy)

    def have(self):
        self.have_mate_own()
        self.have_other()
        self.have_mate_other()


ROUND_COPIES = 10


def round_buffers(rows, width):
    span = rows // 4
    return [
        VMEM((2, span, width), LOW),
        VMEM((2, span, width), LOW),
        VMEM((span, width), LOW),
        VMEM((span, width), LOW),
        VMEM((span, width), FULL),
    ]


NAMES = ("qkv", "out", "up", "down")


def layer_kernel(plan, last, size, tile, mover, ins, outs, work):
    ins, outs, work = iter(ins), iter(outs), iter(work)
    source = next(ins)
    x_ref = None if plan.entry else next(ins)
    live_ref = next(ins)
    far_params = [next(ins) for _ in range(8)]
    stream, following = next(outs), next(outs)
    far_qkv, far_o, far_lse, far_heads, far_middle, far_second, far_hidden, far_slope = [
        next(outs) for _ in range(8)
    ]
    far_first = next(outs) if plan.entry else None
    joint, nat, heads, qkv, o_ref, lse, middle, second, hidden, slope = [
        next(work) for _ in range(10)
    ]
    first = next(work) if plan.entry else source
    attend_work = [next(work) for _ in range(6)]
    one_work, two_work = [next(work) for _ in range(5)], [next(work) for _ in range(5)]
    rows = source.shape[0]
    bias, qkv_bias = next(work), next(work)
    params = [next(work) for _ in range(8)]
    whole = {name: next(work) for name in NAMES}
    gathers, loads = {}, {}
    for name in plan.held:
        loads[name] = (next(ins), whole[name])
    for name in plan.own:
        gathers[name, 0] = Gather(mover, next(ins).at[plan.layer], whole[name])
    kept_ahead = {name: next(outs) for name in plan.ahead}
    for name in plan.ahead:
        gathers[name, 1] = Gather(mover, next(ins).at[plan.layer + 1], next(work))
    kept = {name: next(outs) for name in plan.own}

    greet(mover, bool(gathers))
    if plan.entry:
        gathers_first = [key for key in [("qkv", 0)] if key in gathers]
        for key in gathers_first:
            gathers[key].start()
    param_loads = [mover.stay(there, here) for there, here in zip(far_params, params)]
    loads = {name: mover.stay(*pair) for name, pair in loads.items()}

    def have(name):
        if name in loads:
            mover.near(loads[name])
        else:
            gathers[name, 0].have()
            mover.stay(whole[name], kept[name])
        return whole[name]

    def begin(keys):
        for key in keys:
            if key in gathers:
                gathers[key].start_line()

    def begin_over(keys):
        for key in keys:
            if key in gathers:
                gathers[key].start_over()

    def pass_on(keys, stage):
        for key in keys:
            if key in gathers:
                gathers[key].pass_on(stage)

    def pass_all(keys):
        for stage in (1, 2, 3):
            pass_on(keys, stage)

    mover.near(*param_loads)
    layer, after = plan.layer, min(plan.layer + 1, params[0].shape[0] - 1)

    def row(index, layer=layer):
        return params[index][...].astype(FULL)[layer : layer + 1]

    b_out, gain2, shift2, b_down, b_up = row(0), row(1), row(2), row(3), row(6)
    gain1, shift1, gain0, shift0 = row(4, after), row(5, after), row(4), row(5)
    qkv_bias[...] = joint_bias(row(7), size, joint.shape[0])
    key_bias(mover, live_ref, bias)
    ahead = [("qkv", 1), ("out", 1), ("up", 1)]
    one = Round(mover, rows, second, one_work)
    two = Round(mover, rows, following, two_work)
    if plan.entry:
        chunk = rows // 5 if rows % 80 == 0 else rows

        def norm_step(i, carry):
            at = pl.ds(pl.multiple_of(i * chunk, 16), chunk)
            value = normalize(source[at, :].astype(FULL), gain0, shift0)[0]
            first[at, :] = value.astype(LOW)
            return carry

        lax.fori_loop(0, rows // chunk, norm_step, 0)
        mover.stay(first, far_first)
        pass_all([("qkv", 0)])
        begin([("out", 0), ("up", 0)])
        begin_over([("out", 0), ("up", 0), ("down", 0)] + ahead)
        turned_product(first, have("qkv"), qkv_bias, joint)
    else:
        turned_product(first, have("qkv"), qkv_bias, joint)

    def after_send():
        if plan.entry:
            pass_all([("out", 0), ("up", 0)])
        else:
            for name in plan.own:
                gathers[name, 0].start_over()

    def begun():
        if plan.entry:
            begin([("down", 0)])
        else:
            for name in plan.own:
                gathers[name, 0].start_line()

    def between(p):
        if p > 1:
            pass_on([("down", 0)], p - 1)
        if p == 4:
            if not plan.entry:
                begin_over(ahead)
            begin(ahead)

    attend_part(
        size, tile, mover, joint, bias, heads, qkv, o_ref, lse, attend_work, after_send, begun, between
    )
    nat[...] = turned(heads[...])
    w_out = have("out")

    def out_part(start):
        return dot(nat[one.rows(start), :], w_out[...], ((1,), (1,)))

    def to_second(at, value):
        if plan.entry:
            before = source[one.rows(one.own + at.start, at.size), :].astype(FULL)
        else:
            before = x_ref[at]
        value = before + value + b_out
        middle[at] = value
        return normalize(value, gain2, shift2)[0].astype(LOW)

    def meanwhile():
        mover.stay(qkv, far_qkv)
        mover.stay(o_ref, far_o)
        mover.stay(lse, far_lse)
        mover.stay(nat, far_heads)

    one.eager(out_part, to_second, meanwhile, lambda: pass_on(ahead[:2], 1))
    pass_on(ahead[:2], 2)
    w_up, w_down = have("up"), have("down")

    def mlp_part(start):
        at = two.rows(start)
        pre = jnp.dot(second[at, :], w_up[...], preferred_element_type=FULL) + b_up
        low, low_slope = gelu_pair(pre)
        hidden[at, :] = low
        slope[at, :] = low_slope
        return dot(low, w_down[...], ((1,), (1,)))

    def to_following(at, value):
        value = middle[at] + value + b_down
        stream[at] = value
        if last:
            return live_rows(value, two.own + at.start, live_ref[0, mover.ctx]).astype(LOW)
        return normalize(value, gain1, shift1)[0].astype(LOW)

    def meanwhile():
        mover.stay(middle, far_middle)
        mover.stay(second, far_second)
        mover.stay(hidden, far_hidden)
        mover.stay(slope, far_slope)
        pass_on(ahead[:2], 3)
        pass_on(ahead[2:], 1)
        pass_on(ahead[2:], 2)

    two.after(one, mlp_part, to_following, meanwhile, lambda: pass_on(ahead[2:], 3))
    two.have()
    for name in plan.ahead:
        gathers[name, 1].have()
        mover.stay(gathers[name, 1].target, kept_ahead[name])
    mover.settle()


class Plan:
    def __init__(self, layer, last, inside):
        self.layer, self.entry = layer, layer == 0
        self.own = (NAMES if layer == 0 else ("down",)) if inside else ()
        self.ahead = ("qkv", "out", "up") if inside and not last else ()
        self.held = tuple(name for name in NAMES if name not in self.own)


def forward_layer(source, x, live, params, gathered, weights, plan, last, size, sizes, ident):
    rows, width = source.shape
    count = sizes[0]
    joint, hidden = weights["qkv"].shape[2], weights["up"].shape[2]
    heads = joint // (3 * size)
    attn, slots, span = heads * size, count * rows, rows // 4
    tile = 256 if slots % 256 == 0 else PAD
    columns = {"qkv": joint, "out": attn, "up": hidden, "down": hidden}
    inputs = [(source, VMEM)] + ([] if plan.entry else [(x, VMEM)])
    inputs += [(live, SMEM)] + [(value, HBM) for value in params]
    inputs += [(gathered[name, plan.layer], HBM) for name in plan.held]
    inputs += [(weights[name], HBM) for name in plan.own + plan.ahead]
    saved = [
        ((count, 3 * size, rows), LOW),
        ((size, slots), FULL),
        ((8, slots), FULL),
        ((rows, attn), LOW),
        ((span, width), FULL),
        ((rows, width), LOW),
        ((rows, hidden), LOW),
        ((rows, hidden), LOW),
    ]
    outputs = [((span, width), FULL, VMEM), ((rows, width), LOW, VMEM)]
    outputs += [(shape, dtype, HBM) for shape, dtype in saved]
    if plan.entry:
        outputs.append(((rows, width), LOW, HBM))
    outputs += [((width, columns[name]), LOW, HBM) for name in plan.ahead + plan.own]
    qkv_shape, o_shape, lse_shape, heads_shape = saved[:4]
    scratch = [VMEM((joint, rows), LOW), VMEM((rows, attn), LOW), VMEM((attn, rows), LOW)]
    scratch += [VMEM(*pair) for pair in saved[:3] + saved[4:]]
    if plan.entry:
        scratch.append(VMEM((rows, width), LOW))
    scratch += [
        VMEM((slots, PAD), LOW),
        VMEM((PAD, slots), LOW),
        VMEM((size, slots), LOW),
        VMEM((size, slots), LOW),
        VMEM((2, slots, tile), FULL),
        VMEM((2, 8, tile), FULL),
    ]
    scratch += round_buffers(rows, width) + round_buffers(rows, width)
    scratch += [VMEM((16, slots), LOW), VMEM((16, joint), FULL)]
    scratch += [VMEM(value.shape, value.dtype) for value in params]
    scratch += [VMEM((width, columns[name]), LOW) for name in NAMES + plan.ahead]
    results = run(
        functools.partial(layer_kernel, plan, last, size, tile),
        "forward_layer",
        ident,
        inputs,
        outputs,
        scratch,
        2 * (count - 1) + 2 * ROUND_COPIES + 2 * count * len(plan.own + plan.ahead),
        10 + 2 * len(plan.own + plan.ahead) + len(plan.held) + len(params),
        sizes,
        58,
        2 * rows * width * (2 * hidden + attn + joint) + 4 * slots * slots * 256,
    )
    stream, following = results[:2]
    kept = results[2 : 11 if plan.entry else 10]
    for name, value in zip(plan.ahead, results[2 + len(kept) :]):
        gathered[name, plan.layer + 1] = value
    for name, value in zip(plan.own, results[2 + len(kept) + len(plan.ahead) :]):
        gathered[name, plan.layer] = value
    return stream, following, kept


class SmallSums:
    def __init__(self, mover, rows, held, got):
        self.mover, self.rows, self.held, self.got = mover, rows, held, got
        self.stage = 0
        mate, far = tp_peers()
        self.peers = [
            dict(tp=mate),
            dict(tp=far),
            dict(shard=1 - mover.shard),
            dict(ctx=mover.flip(2)),
            dict(ctx=mover.flip(1)),
        ]

    def part(self, stage):
        return pl.ds(0, self.rows if stage < 2 else self.held.shape[1])

    def step(self):
        stage, mover = self.stage, self.mover
        if stage:
            mover.take(self.copy)
            at = self.part(stage - 1)
            self.held[stage] = self.held[stage - 1]
            self.held[stage, at, :] = self.held[stage - 1, at, :] + self.got[stage - 1, at, :]
        if stage < len(self.peers):
            at = self.part(stage)
            self.copy = mover.go(
                self.held.at[stage, at], self.got.at[stage, at], **self.peers[stage]
            )
        self.stage = stage + 1

    def value(self):
        return self.held[len(self.peers)]


def key_bias(mover, live_ref, bias):
    capacity = bias.shape[1] // mover.ctx_count
    row = lax.broadcasted_iota(jnp.int32, (16, capacity), 0)
    slot = lax.broadcasted_iota(jnp.int32, (16, capacity), 1)
    for r in range(mover.ctx_count):
        live = live_ref[0, mover.back(r)]
        value = jnp.where((row == 0) & (slot >= live), NEG_LARGE, 0.0)
        bias[:, r * capacity : (r + 1) * capacity] = value.astype(LOW)


def pair_columns(rows, width, size, turn):
    shape = (width, rows) if turn else (rows, width)
    given = lax.broadcasted_iota(jnp.int32, shape, 1 if turn else 0)
    column = lax.broadcasted_iota(jnp.int32, shape, 0 if turn else 1)
    head, within = column // (3 * size), column % (3 * size)
    wanted = head * (2 * size) + jnp.where(within < size, within, within - size)
    key = (within >= size) & (within < 2 * size)
    return jnp.where((given == wanted) & ~key, 1.0, 0.0).astype(LOW)


def joint_bias(pair, size, width):
    rows = pair.shape[1]
    spread = jnp.broadcast_to(pair, (16, rows)).astype(LOW)
    return jnp.dot(spread, pair_columns(rows, width, size, False), preferred_element_type=FULL)


def live_rows(value, start, live):
    row = start + lax.broadcasted_iota(jnp.int32, value.shape, 0)
    return jnp.where(row < live, value, 0.0)


def sums_into(sums, first, at, values):
    for index, value in enumerate(values):
        row = first + index
        added = jnp.sum(value, axis=0, keepdims=True)
        width = added.shape[1]
        sums[row : row + 1, 0:width] = (
            added if at.start == 0 else sums[row : row + 1, 0:width] + added
        )


def back_kernel(plan, size, tile, mover, ins, outs, work):
    ins, outs, work = iter(ins), iter(outs), iter(work)
    source = next(ins)
    x_ref = None if plan.last else next(ins)
    live_ref, far_gain2, far_gain1 = [next(ins) for _ in range(3)]
    far = [next(ins) for _ in range(14)]
    late_far = next(ins) if plan.late else None
    others = [(next(ins), next(ins)) for _ in range(plan.others)]
    stream, following = next(outs), next(outs)
    grad_outs = {name: next(outs) for name in NAMES if plan.inside and (name != "qkv" or plan.final)}
    mid_out = next(outs) if plan.inside and not plan.final else None
    late_out = next(outs) if plan.late else None
    split = local = totals = None
    if plan.joined:
        totals = next(outs)
    else:
        split, local = next(outs), next(outs)
    wholes = {} if plan.inside else {name: next(outs) for name in NAMES}
    near = [next(work) for _ in range(14)]
    slope, w_down, w_up, middle, hidden, second, w_out, heads, qkv, o_ref, lse, first, w_qkv, before = near
    grad = next(work) if plan.last else source
    pre_grad, attn_grad, parts, grads, nat = [next(work) for _ in range(5)]
    attend_work = [next(work) for _ in range(13)]
    one_work, two_work = [next(work) for _ in range(5)], [next(work) for _ in range(5)]
    rows, width = source.shape
    reduces = {}
    if plan.inside:
        pairs = {
            "down": (grad, hidden),
            "up": (second, pre_grad),
            "out": (attn_grad, heads),
            "qkv": (first, nat),
        }
        for name in ("down", "up", "out", "qkv"):
            buffers = [next(work) for _ in range(4)]
            reduces[name] = Reduce(mover, buffers, grad_outs.get(name), *pairs[name])
    late = None
    if plan.late:
        late_mid, late_line = next(work), next(work)
        late = Reduce(mover, (late_mid, None, late_mid, late_line), late_out, None, None)
    bias, gain2_ref, gain1_ref = [next(work) for _ in range(3)]
    if plan.joined:
        split, local = next(work), next(work)
        early_held, early_got, late_held, late_got = [next(work) for _ in range(4)]
        tops = 8 * (plan.others + 1)
        early = SmallSums(mover, tops, early_held, early_got)
        final = SmallSums(mover, 8, late_held, late_got)
        everything = [(split, local)] + others

    greet(mover, plan.inside)
    gain_loads = [mover.stay(far_gain2, gain2_ref), mover.stay(far_gain1, gain1_ref)]
    one = Round(mover, rows, attn_grad, one_work)
    two = Round(mover, rows, following, two_work)
    if plan.final:
        far[13] = far[13].at[two.rows(two.own)]
    load = [mover.stay(there, here) for there, here in zip(far, near)]
    if late:
        mover.near(mover.stay(late_far, late_mid))
        late.spread()
    if plan.last:
        chunk = rows // 5 if rows % 80 == 0 else rows

        def mask_step(i, carry):
            at = pl.ds(pl.multiple_of(i * chunk, 16), chunk)
            value = source[at, :].astype(FULL)
            grad[at, :] = live_rows(value, i * chunk, live_ref[0, mover.ctx]).astype(LOW)
            return carry

        lax.fori_loop(0, rows // chunk, mask_step, 0)
    key_bias(mover, live_ref, bias)
    mover.near(*gain_loads)
    gain2, gain1 = [
        ref[...].astype(FULL)[plan.layer : plan.layer + 1] for ref in (gain2_ref, gain1_ref)
    ]
    split[...] = jnp.zeros_like(split)
    local[...] = jnp.zeros_like(local)
    split[5:6, 0:width] = jnp.sum(
        grad[one.rows(one.own), :].astype(FULL), axis=0, keepdims=True
    )
    mover.near(*load[:3])
    hidden_width = slope.shape[1]

    def mlp_part(start):
        at = one.rows(start)
        pre = jnp.dot(grad[at, :], w_down[...], preferred_element_type=FULL)
        low = (pre * slope[at, :].astype(FULL)).astype(LOW)
        pre_grad[at, :] = low
        local[0:1, 0:hidden_width] += jnp.sum(low.astype(FULL), axis=0, keepdims=True)
        return dot(low, w_up[...], ((1,), (1,)))

    def to_attn(at, value):
        if plan.last:
            above = grad[one.rows(one.own + at.start, at.size), :].astype(FULL)
        else:
            above = x_ref[at]
        _, normed, inverse = normalize(middle[at], 1.0, 0.0)
        result = above + normalize_back(value, normed, inverse, gain2)
        stream[at] = result
        low = result.astype(LOW)
        sums_into(split, 2, at, (value * normed, value, low.astype(FULL)))
        return low

    def reduce(name):
        if name in reduces:
            reduces[name].begin_blocks()

    def own(name):
        if name in reduces:
            reduces[name].own()

    def spread(name):
        if name in reduces:
            reduces[name].fold_blocks(3, 1)
            reduces[name].spread()

    def finish(name):
        if name in reduces:
            reduces[name].fold_blocks(2, 0)
            reduces[name].finish()

    def begin_early():
        if plan.joined:
            early_held[0] = jnp.zeros(early_held.shape[1:], FULL)
            for layer, (some, more) in enumerate(everything):
                first_row = 0 if layer else 2
                for row in range(first_row, 6):
                    at = row * len(everything) + layer
                    early_held[0, at : at + 1, :] = some[row : row + 1, :]
                for row in range(2 if layer else 1):
                    at = tops + row * len(everything) + layer
                    early_held[0, at : at + 1, :] = more[row : row + 1, :]

    def early_step():
        if plan.joined:
            early.step()

    def start_mlp():
        mover.near(*load[3:6])
        reduce("down")
        reduce("up")

    one.eager(mlp_part, to_attn, start_mlp)
    if late:
        late.finish()
    own("down")
    spread("down")
    own("up")
    one.have()
    mover.near(load[6])
    turned_product(attn_grad, w_out, None, parts)

    def waiting():
        begin_early()
        early_step()
        mover.near(load[7])
        reduce("out")
        own("out")

    def ready():
        mover.near(load[8], load[9], load[10])

    def between(turn):
        if turn == 0:
            early_step()
        if turn == 1:
            spread("up")

    attend_back_part(
        size,
        tile,
        mover,
        parts,
        bias,
        qkv,
        o_ref,
        lse,
        grads,
        attend_work,
        ready,
        waiting,
        lambda: finish("down"),
        between,
    )
    finish("up")
    spread("out")
    early_step()
    nat[...] = turned(grads[...])
    pairs_width = nat.shape[1] // 3 * 2
    picked = jnp.dot(
        nat[...], pair_columns(pairs_width, nat.shape[1], size, True), preferred_element_type=FULL
    )
    local[1:2, 0:pairs_width] = jnp.sum(picked, axis=0, keepdims=True)
    mover.near(*load[11:])

    def qkv_part(start):
        return dot(nat[two.rows(start), :], w_qkv[...], ((1,), (1,)))

    def to_following(at, value):
        row = before[at, :].astype(FULL)
        _, normed, inverse = normalize(row, 1.0, 0.0)
        result = stream[at] + normalize_back(value, normed, inverse, gain1)
        stream[at] = result
        low = result.astype(LOW)
        sums_into(split, 0, at, (value * normed, value))
        return low

    def meanwhile():
        own("qkv")
        finish("out")
        early_step()

    def halfway():
        if plan.inside:
            reduces["qkv"].fold_blocks(3, 1)
            if plan.final:
                reduces["qkv"].spread()

    reduce("qkv")
    two.eager(qkv_part, to_following, meanwhile, halfway)
    early_step()
    if plan.joined:
        late_held[0, 0:8, :] = jnp.zeros((8, late_held.shape[2]), FULL)
        late_held[0, 0:2, :] = split[0:2, :]
        late_held[0, 8:16, :] = local[...]
        final.step()
    if plan.inside:
        reduces["qkv"].fold_blocks(2, 0)
        if plan.final:
            reduces["qkv"].finish()
        else:
            mover.stay(reduces["qkv"].mid, mid_out)
    if plan.joined:
        final.step()
    two.have_mate_own()
    two.have_other()
    if plan.joined:
        final.step()
        final.step()
    two.have_mate_other()
    if plan.joined:
        final.step()
    for name in ("down", "up", "out"):
        if name in reduces:
            reduces[name].done()
    if late:
        late.done()
    if plan.inside and plan.final:
        reduces["qkv"].done()
    if plan.joined:
        final.step()
        early.step()
        totals[...] = early.value()
        last_value = final.value()
        for row in range(2):
            at = row * len(everything)
            totals[at : at + 1, :] = last_value[row : row + 1, :]
        at = tops + len(everything)
        totals[at : at + 1, :] = last_value[9:10, :]
    if not plan.inside:
        for name, (lhs, rhs) in {
            "down": (grad, hidden),
            "up": (second, pre_grad),
            "out": (attn_grad, heads),
            "qkv": (first, nat),
        }.items():
            full = Reduce(mover, (wholes[name],) * 4, None, lhs, rhs)
            full.compute(wholes[name], 0)
    mover.settle()


def gather_outputs_kernel(layers, *refs):
    count = layers * len(NAMES)
    parts, token_grads, mixed, totals = refs[:count], refs[count], refs[count + 1], refs[count + 2]
    outs, work = refs[count + 3 : count + 17], refs[count + 17 : -2]
    into, out_of = refs[-2:]
    coming, going = [], []
    pairs = [(mixed, work[4], outs[4].at[0])]
    for index in range(len(NAMES)):
        for layer in range(layers):
            pairs.append(
                (parts[index * layers + layer], work[index].at[layer], outs[index].at[layer])
            )
    for i, (source, stage, _) in enumerate(pairs):
        coming.append(pltpu.make_async_copy(source, stage, into.at[i]))
        coming[-1].start()
    outs[5][0] = token_grads[...].astype(FULL)
    for row, out in enumerate(outs[6:12]):
        out[...] = totals[row * layers : (row + 1) * layers, 0 : out.shape[1]]
    for row, out in enumerate(outs[12:14]):
        row = row + 8
        out[...] = totals[row * layers : (row + 1) * layers, 0 : out.shape[1]]
    for i, (_, stage, target) in enumerate(pairs):
        coming[i].wait()
        going.append(pltpu.make_async_copy(stage, target, out_of.at[i]))
        going[-1].start()
    for copy in going:
        copy.wait()


def gather_outputs(done, token_grads, mixed, totals, layers, widths):
    rows, width = token_grads.shape
    parts = [done[name, layer] for name in NAMES for layer in range(layers)]
    hbm, whole = pl.BlockSpec(memory_space=HBM), lambda shape: pl.BlockSpec(
        shape, lambda i: (0,) * len(shape)
    )
    shapes = [(layers,) + done[name, 0].shape for name in NAMES] + [(1, rows, width)] * 2
    types = [FULL] * 4 + [LOW, FULL]
    small = [(layers, width)] * 6 + [(layers, count) for count in widths]
    copies = len(parts) + 1
    return pl.pallas_call(
        functools.partial(gather_outputs_kernel, layers),
        grid=(1,),
        in_specs=[hbm] * len(parts) + [whole(token_grads.shape), hbm, whole(totals.shape)],
        out_specs=[hbm] * 5 + [whole(shape) for shape in shapes[5:] + small],
        out_shape=[jax.ShapeDtypeStruct(*pair) for pair in zip(shapes, types)]
        + [jax.ShapeDtypeStruct(shape, FULL) for shape in small],
        scratch_shapes=[VMEM(shape, FULL) for shape in shapes[:4]]
        + [VMEM((rows, width), LOW)]
        + [pltpu.SemaphoreType.DMA((copies,)), pltpu.SemaphoreType.DMA((copies,))],
        compiler_params=pltpu.CompilerParams(vmem_limit_bytes=60 * 2**20),
        name="gather_outputs",
    )(*parts, token_grads, mixed, totals)


class BackPlan:
    def __init__(self, layer, layers, inside):
        self.inside, self.layer = inside, layer
        self.last, self.final = layer == layers - 1, layer == 0
        self.late = inside and not self.last
        self.joined = inside and self.final
        self.others = layers - 1 if self.joined else 0


def back_layer(source, x, live, gain2, gain1, saved, late, others, plan, size, sizes, ident):
    rows, width = source.shape
    count = sizes[0]
    slope, w_down, w_up = saved[:3]
    hidden, joint, attn = slope.shape[1], saved[12].shape[1], saved[6].shape[1]
    slots, span = count * rows, rows // 4
    tile = 256 if slots % 256 == 0 else PAD
    wide = max(width, hidden, joint)
    half = width // 2
    block = half // count
    columns = {"qkv": joint, "out": attn, "up": hidden, "down": hidden}
    inputs = [(source, VMEM)] + ([] if plan.last else [(x, VMEM)])
    inputs += [(live, SMEM), (gain2, HBM), (gain1, HBM)]
    inputs += [(value, HBM) for value in saved]
    if plan.late:
        inputs.append((late, HBM))
    for pair in others[: plan.others]:
        inputs += [(value, VMEM) for value in pair]
    outputs = [((span, width), FULL, VMEM), ((rows, width), LOW, VMEM)]
    names = [name for name in NAMES if plan.inside and (name != "qkv" or plan.final)]
    outputs += [((block, columns[name]), FULL, VMEM) for name in names]
    if plan.inside and not plan.final:
        outputs.append(((half, joint), LOW, HBM))
    if plan.late:
        outputs.append(((block, joint), FULL, VMEM))
    depth = 8 * (plan.others + 1)
    if plan.joined:
        outputs.append(((depth + 8, wide), FULL, VMEM))
    else:
        outputs += [((8, wide), FULL, VMEM)] * 2
    if not plan.inside:
        outputs += [((width, columns[name]), LOW, VMEM) for name in NAMES]
    scratch = [VMEM(value.shape, value.dtype) for value in saved]
    scratch[13] = VMEM((span, width), saved[13].dtype)
    if plan.last:
        scratch.append(VMEM((rows, width), LOW))
    scratch += [
        VMEM((rows, hidden), LOW),
        VMEM((rows, width), LOW),
        VMEM((attn, rows), LOW),
        VMEM((joint, rows), LOW),
        VMEM((rows, joint), LOW),
    ]
    scratch += attend_back_buffers(size, count, rows, tile)
    scratch += round_buffers(rows, width) + round_buffers(rows, width)
    if plan.inside:
        for name in ("down", "up", "out", "qkv"):
            scratch += reduce_buffers(half, columns[name], count)
    if plan.late:
        scratch += [VMEM((half, joint), LOW), VMEM((count - 1, block, joint), LOW)]
    scratch.append(VMEM((16, slots), LOW))
    scratch += [VMEM(value.shape, value.dtype) for value in (gain2, gain1)]
    assert 2 * (plan.others + 1) <= 8
    if plan.joined:
        scratch += [VMEM((8, wide), FULL)] * 2
        scratch += [
            VMEM((6, depth + 8, wide), FULL),
            VMEM((5, depth + 8, wide), FULL),
            VMEM((6, 16, wide), FULL),
            VMEM((5, 16, wide), FULL),
        ]
    results = run(
        functools.partial(back_kernel, plan, size, tile),
        "back_layer",
        ident,
        inputs,
        outputs,
        scratch,
        3 * (count - 1) + 2 * ROUND_COPIES + 8 * count + 10 + count,
        len(saved) + 4,
        sizes,
        58,
        6 * rows * width * (2 * hidden + attn + joint) + 10 * slots * slots * 256,
    )
    return results[:2], names, results[2:]


def shards(
    tokens,
    block_tokens,
    ln1_gain,
    ln1_bias,
    w_qkv,
    b_qv,
    w_out,
    b_out,
    ln2_gain,
    ln2_bias,
    w_up,
    b_up,
    w_down,
    b_down,
    cotangent,
):
    images, capacity, width = tokens.shape
    assert images == 1
    layers = w_qkv.shape[0]
    size = HEAD_DIM
    ctx_count = lax.axis_size("ctx")
    ctx_place = lax.axis_index("ctx")
    joint_width = w_qkv.shape[2]
    heads = joint_width // (3 * size)
    assert heads == ctx_count
    attn_width = heads * size
    hidden_width = w_up.shape[2]
    weights = {"qkv": w_qkv, "out": w_out, "up": w_up, "down": w_down}
    sizes = (ctx_count, lax.axis_size("shard"))
    inside = sizes == (4, 2)
    gathered = {}
    if not inside:
        for name, value in weights.items():
            for layer in range(layers):
                gathered[name, layer] = gather_weight(value[layer])[0]
    source, stream = tokens[0], None
    saved = []
    for layer in range(layers):
        last = layer == layers - 1
        result, following, kept = forward_layer(
            source,
            stream,
            block_tokens,
            (b_out, ln2_gain, ln2_bias, b_down, ln1_gain, ln1_bias, b_up, b_qv),
            gathered,
            weights,
            Plan(layer, last, inside),
            last,
            size,
            sizes,
            1 + layer,
        )
        before = stream if layer else source
        first = source if layer else kept[8]
        saved.append((before, first) + tuple(kept[:8]))
        source, stream = following, result
    mixed = source

    done, packs = {}, {}
    source, stream, late = cotangent[0], None, None
    for layer in reversed(range(layers)):
        before, first, qkv, head_out, lse, heads_low, middle, second, hidden, slope = saved[layer]
        plan = BackPlan(layer, layers, inside)
        whole = {name: gathered[name, layer] for name in NAMES}
        near = [slope, whole["down"], whole["up"], middle, hidden, second, whole["out"]]
        near += [heads_low, qkv, head_out, lse, first, whole["qkv"], before]
        others = [packs[key] for key in sorted(packs)]
        (stream, source), names, rest = back_layer(
            source, stream, block_tokens, ln2_gain, ln1_gain, near, late, others, plan, size, sizes, 1 + layers + layer
        )
        rest = iter(rest)
        for name in names:
            done[name, layer] = next(rest)
        if plan.inside and not plan.final:
            late = next(rest)
        if plan.late:
            done["qkv", layer + 1] = next(rest)
        if plan.joined:
            totals = next(rest)
        else:
            packs[layer] = (next(rest), next(rest))
        if not inside:
            for name in NAMES:
                value = next(rest)
                done[name, layer] = scatter_weight(
                    lambda start, count, value=value: rows_of(value, start, count).astype(FULL),
                    width,
                )
    if not inside:
        split = total_over(("tp",), jnp.stack([packs[l][0] for l in range(layers)], axis=1))
        local = jnp.stack([packs[l][1] for l in range(layers)], axis=1)
        totals = total_over(("shard", "ctx"), jnp.concatenate([split, local[:2]]))
        totals = totals.reshape(10 * layers, -1)
    pairs = b_qv.shape[1]
    outs = gather_outputs(done, source, mixed, totals, layers, (hidden_width, pairs))
    g_qkv, g_out, g_up, g_down, mixed, token_grads = outs[:6]
    g_ln1_gain, g_ln1_bias, g_ln2_gain, g_ln2_bias, g_b_out, g_b_down, g_b_up, g_b_qv = outs[6:]
    return (
        mixed,
        token_grads,
        g_ln1_gain,
        g_ln1_bias,
        g_qkv,
        g_b_qv,
        g_out,
        g_b_out,
        g_ln2_gain,
        g_ln2_bias,
        g_up,
        g_b_up,
        g_down,
        g_b_down,
    )


def solution(mesh):
    split_rows = P(None, ("shard", "ctx"), "tp")
    split_tokens = P("shard", "ctx", None)
    return jax.shard_map(
        shards,
        mesh=mesh,
        in_specs=(
            split_tokens,
            P("shard", None),
            P(),
            P(),
            split_rows,
            P(None, "tp"),
            split_rows,
            P(),
            P(),
            P(),
            split_rows,
            P(None, "tp"),
            split_rows,
            P(),
            split_tokens,
        ),
        out_specs=(
            split_tokens,
            split_tokens,
            P(),
            P(),
            split_rows,
            P(None, "tp"),
            split_rows,
            P(),
            P(),
            P(),
            split_rows,
            P(None, "tp"),
            split_rows,
            P(),
        ),
        check_vma=False,
    )
```

```python
import functools
import math

import jax
import jax.numpy as jnp
from jax import lax
from jax.experimental import pallas as pl
from jax.experimental.pallas import tpu as pltpu
from jax.sharding import PartitionSpec as P

HEAD_DIM = 64
EPSILON = 1e-06
NEG_LARGE = -1e30
LOW = jnp.bfloat16
FULL = jnp.float32
PAD = 128
MESH = pl.DeviceIdType.MESH
VMEM = pltpu.VMEM
HBM = pltpu.HBM
SMEM = pltpu.SMEM


def bits_of(axis):
    size = lax.axis_size(axis)
    assert size & (size - 1) == 0
    return [1 << i for i in range(size.bit_length() - 1)]


def swap(value, axis, bit):
    size = lax.axis_size(axis)
    return lax.ppermute(value, axis, [(i, i ^ bit) for i in range(size)])


def side_of(axis, bit):
    return (lax.axis_index(axis) // bit) % 2


def rows_of(value, start, count, axis=0):
    return lax.dynamic_slice_in_dim(value, start, count, axis)


def halve(axis, bits, partial, total):
    offset, span, received = jnp.int32(0), total, []

    def summed(start, count):
        value = partial(start, count)
        for got, base in received:
            value = value + rows_of(got, start - base, count).astype(FULL)
        return value

    for bit in bits:
        half = span // 2
        side = side_of(axis, bit)
        got = swap(summed(offset + (1 - side) * half, half).astype(LOW), axis, bit)
        offset = offset + side * half
        received.append((got, offset))
        span = half
    return summed(offset, span)


def double(axis, bits, value):
    for bit in bits:
        got = swap(value, axis, bit)
        first = side_of(axis, bit) == 0
        value = jnp.concatenate(
            [jnp.where(first, value, got), jnp.where(first, got, value)], axis=0
        )
    return value


def total_over(axes, value):
    for axis in axes:
        for bit in bits_of(axis):
            value = value + swap(value, axis, bit)
    return value


def ring(value, by):
    count = lax.axis_size("ctx")
    return lax.ppermute(value, "ctx", [(i, (i + by) % count) for i in range(count)])


def gather_weight(piece):
    count = lax.axis_size("ctx")
    place = lax.axis_index("ctx")
    ways = lax.axis_size("shard")
    blocks = [piece] + [ring(piece, by) for by in range(1, count)]
    whole = jnp.zeros((ways * count,) + piece.shape, piece.dtype)
    me = lax.axis_index("shard")
    for by, block in enumerate(blocks):
        at = (place - by) % count
        held = [(jnp.int32(0), block)]
        for bit in bits_of("shard"):
            held = held + [(other ^ bit, swap(value, "shard", bit)) for other, value in held]
        for other, value in held:
            whole = lax.dynamic_update_index_in_dim(whole, value, (me ^ other) * count + at, 0)
    return whole.reshape((ways * count * piece.shape[0],) + piece.shape[1:]), blocks[-1]


def scatter_weight(partial, total):
    count = lax.axis_size("ctx")
    place = lax.axis_index("ctx")
    mine = halve("shard", bits_of("shard")[::-1], partial, total).astype(LOW)
    mine = mine.reshape((count, mine.shape[0] // count) + mine.shape[1:])
    value = lax.dynamic_index_in_dim(mine, place, 0, False).astype(FULL)
    for by in range(1, count):
        given = lax.dynamic_index_in_dim(mine, (place + by) % count, 0, False)
        value = value + ring(given, by).astype(FULL)
    return value


def dot(left, right, contract):
    return lax.dot_general(
        left, right, ((contract[0], contract[1]), ((), ())), preferred_element_type=FULL
    )


def turned(value):
    return value.astype(FULL).T.astype(LOW)


def normalize(rows, gain, shift):
    row_mean = jnp.mean(rows, axis=-1, keepdims=True)
    centred = rows - row_mean
    inverse = lax.rsqrt(jnp.mean(centred * centred, axis=-1, keepdims=True) + EPSILON)
    normed = centred * inverse
    return (normed * gain + shift, normed, inverse)


def normalize_back(grad_out, normed, inverse, gain):
    scaled = grad_out * gain
    mean_grad = jnp.mean(scaled, axis=-1, keepdims=True)
    mean_cross = jnp.mean(scaled * normed, axis=-1, keepdims=True)
    return inverse * (scaled - mean_grad - normed * mean_cross)


def gelu_pair(value):
    spread = 0.5 * (1.0 + lax.erf(value * (0.5**0.5)))
    slope = spread + value * jnp.exp(-0.5 * value * value) * (1.0 / math.sqrt(2.0 * math.pi))
    return (value * spread).astype(LOW), slope.astype(LOW)


class Mover:
    def __init__(self, sizes, send, recv, local):
        self.ctx_count, self.shard_count = sizes
        self.send, self.recv, self.local = send, recv, local
        self.copies, self.here = [], []
        self.arrived = set()
        self.landed = set()
        self.ctx = lax.axis_index("ctx")
        self.shard = lax.axis_index("shard")

    def go(self, source, target, **device):
        index = len(self.copies)
        assert index < self.send.shape[0]
        copy = pltpu.make_async_remote_copy(
            src_ref=source,
            dst_ref=target,
            send_sem=self.send.at[index],
            recv_sem=self.recv.at[index],
            device_id=device,
            device_id_type=MESH,
        )
        copy.start()
        self.copies.append(copy)
        return index

    def stay(self, source, target):
        index = len(self.here)
        assert index < self.local.shape[0]
        copy = pltpu.make_async_copy(source, target, self.local.at[index])
        copy.start()
        self.here.append(copy)
        return index

    def near(self, *indices):
        for index in indices:
            if index not in self.landed:
                self.landed.add(index)
                self.here[index].wait()

    def take(self, index):
        if index not in self.arrived:
            self.arrived.add(index)
            self.copies[index].wait_recv()

    def flip(self, bits):
        place = self.ctx
        if bits & 1:
            place = place + 1 - 2 * lax.rem(self.ctx, 2)
        if bits & 2:
            place = place + 2 - 4 * (self.ctx // 2)
        return place

    def on(self, by):
        return lax.rem(self.ctx + by, self.ctx_count)

    def back(self, by):
        return lax.rem(self.ctx + self.ctx_count - by, self.ctx_count)

    def settle(self):
        for index, copy in enumerate(self.copies):
            self.take(index)
            copy.wait_send()
        self.near(*range(len(self.here)))


class Gather:
    def __init__(self, mover, source, target):
        self.mover, self.source, self.target = mover, source, target
        self.over = []

    def start(self):
        self.start_line()
        self.start_over()

    def start_line(self):
        mover = self.mover
        mine, there = self.source, self.block(mover.ctx)
        self.far = mover.go(mine, there, ctx=mover.flip(2))
        self.close = mover.go(mine, there, ctx=mover.flip(1))

    def start_over(self):
        mover = self.mover
        mine, there = self.source, self.block(mover.ctx)
        self.over.append(mover.go(mine, there, shard=1 - mover.shard))
        self.own = mover.stay(mine, there)

    def block(self, ctx):
        mover = self.mover
        rows = self.source.shape[0]
        start = (mover.shard * mover.ctx_count + ctx) * rows
        return self.target.at[pl.ds(pl.multiple_of(start, rows), rows)]

    def pass_on(self, stage):
        mover = self.mover
        if stage == 1:
            mover.take(self.far)
            rows = self.block(mover.flip(2))
            self.passed = mover.go(rows, rows, ctx=mover.flip(1))
        elif stage == 2:
            mover.take(self.close)
            rows = self.block(mover.flip(1))
        else:
            mover.take(self.passed)
            rows = self.block(mover.flip(3))
        self.over.append(mover.go(rows, rows, shard=1 - mover.shard))

    def have(self):
        for copy in self.over:
            self.mover.take(copy)
        self.mover.near(self.own)


class Reduce:
    def __init__(self, mover, buffers, out, lhs, rhs):
        self.mover, self.out, self.lhs, self.rhs = mover, out, lhs, rhs
        self.give, self.got, self.mid, self.line = buffers
        self.half = self.give.shape[0]
        self.block = self.half // mover.ctx_count

    def compute(self, target, shard):
        chunk = min(256, self.half)

        def step(i, carry):
            at = pl.ds(pl.multiple_of(shard * self.half + i * chunk, chunk), chunk)
            here = pl.ds(pl.multiple_of(i * chunk, chunk), chunk)
            target[here, :] = dot(self.lhs[:, at], self.rhs[...], ((0,), (0,))).astype(LOW)
            return carry

        lax.fori_loop(0, self.half // chunk, step, 0)

    def begin_blocks(self):
        mover = self.mover
        self.blocks = {}
        for bits in (3, 1, 2, 0):
            ctx = mover.flip(bits)
            at = pl.ds(pl.multiple_of(ctx * self.block, self.block), self.block)
            start = pl.multiple_of((1 - mover.shard) * self.half + ctx * self.block, self.block)
            lhs = self.lhs[:, pl.ds(start, self.block)]
            self.give[at, :] = dot(lhs, self.rhs[...], ((0,), (0,))).astype(LOW)
            self.blocks[bits] = mover.go(
                self.give.at[at], self.got.at[at], shard=1 - mover.shard
            )

    def own(self):
        self.compute(self.mid, self.mover.shard)

    def fold_blocks(self, *which):
        mover = self.mover
        for bits in which:
            mover.take(self.blocks[bits])
            ctx = mover.flip(bits)
            at = pl.ds(pl.multiple_of(ctx * self.block, self.block), self.block)
            self.mid[at, :] = (
                self.mid[at, :].astype(FULL) + self.got[at, :].astype(FULL)
            ).astype(LOW)

    def rows(self, ctx):
        return self.mid.at[pl.ds(pl.multiple_of(ctx * self.block, self.block), self.block)]

    def spread(self):
        mover = self.mover
        self.first = mover.go(self.rows(mover.flip(3)), self.line.at[1], ctx=mover.flip(1))
        self.second = mover.go(self.rows(mover.flip(1)), self.line.at[0], ctx=mover.flip(1))

    def finish(self):
        mover = self.mover
        mover.take(self.first)
        rows = self.rows(mover.flip(2))
        rows[...] = (rows[...].astype(FULL) + self.line[1].astype(FULL)).astype(LOW)
        self.third = mover.go(rows, self.line.at[2], ctx=mover.flip(2))

    def done(self):
        self.mover.take(self.second)
        self.mover.take(self.third)
        value = self.rows(self.mover.ctx)[...].astype(FULL)
        self.out[...] = value + self.line[0].astype(FULL) + self.line[2].astype(FULL)


def reduce_buffers(half, width, count):
    return [
        VMEM((half, width), LOW),
        VMEM((half, width), LOW),
        VMEM((half, width), LOW),
        VMEM((count - 1, half // count, width), LOW),
    ]


def greet(mover, shard):
    barrier = pltpu.get_barrier_semaphore()
    peers = [dict(ctx=mover.on(by)) for by in range(1, mover.ctx_count)]
    peers += [dict(tp=peer) for peer in tp_peers()]
    if shard:
        peers.append(dict(shard=1 - mover.shard))
    for peer in peers:
        pl.semaphore_signal(barrier, inc=1, device_id=peer, device_id_type=MESH)
    pl.semaphore_wait(barrier, len(peers))


def tp_peers():
    place = lax.axis_index("tp")
    core, far = lax.rem(place, 2), place // 2
    return place + 1 - 2 * core, place + 2 - 4 * far


def run(kernel, name, ident, inputs, outputs, scratch, remote, local, sizes, vmem, flops):
    n_in, n_out, n_scratch = len(inputs), len(outputs), len(scratch)

    def body(*refs):
        ins, outs = refs[:n_in], refs[n_in : n_in + n_out]
        work = refs[n_in + n_out :]
        mover = Mover(sizes, *work[n_scratch:])
        kernel(mover, ins, outs, work[:n_scratch])

    return pl.pallas_call(
        body,
        in_specs=[pl.BlockSpec(memory_space=space) for _, space in inputs],
        out_specs=[pl.BlockSpec(memory_space=space) for _, _, space in outputs],
        out_shape=[jax.ShapeDtypeStruct(shape, dtype) for shape, dtype, _ in outputs],
        scratch_shapes=list(scratch)
        + [
            pltpu.SemaphoreType.DMA((remote,)),
            pltpu.SemaphoreType.DMA((remote,)),
            pltpu.SemaphoreType.DMA((local,)),
        ],
        compiler_params=pltpu.CompilerParams(
            collective_id=ident, has_side_effects=True, vmem_limit_bytes=vmem * 2**20
        ),
        cost_estimate=pl.CostEstimate(flops=flops, bytes_accessed=2**24, transcendentals=0),
        name=name,
    )(*[value for value, _ in inputs])


def order_of(block, count):
    return (block + count - 1) % count


def tiles_of(count, capacity, tile):
    ends = [-(-(p + 1) * capacity // tile) for p in range(count)]
    return list(zip([0] + ends[:-1], ends))


def parts_of(capacity):
    middle = capacity // 2 // PAD * PAD
    return [(0, middle), (middle, capacity)] if middle else [(0, capacity)]


def tile_at(t, tile):
    return pl.ds(pl.multiple_of(t * tile, tile), tile)


def turned_product(left, right, bias, target):
    def step(i, carry):
        at = pl.ds(pl.multiple_of(i * PAD, PAD), PAD)
        value = jnp.dot(left[at, :], right[...], preferred_element_type=FULL)
        if bias is not None:
            value = value + bias[0:1, :]
        target[:, at] = turned(value.astype(LOW))
        return carry

    lax.fori_loop(0, left.shape[0] // PAD, step, 0)


def head_rows(ref, head, width):
    return ref.at[pl.ds(pl.multiple_of(head * width, 16), width)]


def attend_part(size, tile, mover, joint, bias, heads, qkv, o_ref, lse, work, after_send, begun, between):
    k_ref, q_ref, v_ref, low_ref, score_ref, top_ref = work
    count, width, capacity = qkv.shape
    slots = count * capacity
    sent = [None] + [
        mover.go(head_rows(joint, mover.on(by), width), qkv.at[by], ctx=mover.on(by))
        for by in range(1, count)
    ]
    after_send()
    qkv[0] = head_rows(joint, mover.ctx, width)[...]
    q_ref[size:PAD, :] = jnp.concatenate(
        [jnp.ones((16, slots), LOW), jnp.zeros((PAD - size - 16, slots), LOW)], axis=0
    )

    def prepare(r):
        here = slice(r * capacity, (r + 1) * capacity)
        p = order_of(r, count)
        q_ref[0:size, p * capacity : (p + 1) * capacity] = (
            qkv[r, 0:size, :] * (size**-0.5)
        ).astype(LOW)
        v_ref[:, here] = qkv[r, 2 * size : 3 * size, :]
        keys = jnp.concatenate(
            [qkv[r, size : 2 * size, :], bias[:, here], jnp.zeros((PAD - size - 16, capacity), LOW)],
            axis=0,
        )
        k_ref[here, :] = turned(keys)

    prepare(0)
    for by in range(1, count):
        mover.take(sent[by])
        prepare(by)

    begun()
    last = slots // tile - 1
    assert last % 2 == 1

    def phase(t, now, following, then):
        at, ahead = tile_at(t, tile), tile_at(following, tile)
        top = top_ref[now, 0:1, :]
        total = jnp.zeros((1, tile), FULL)
        summed = jnp.zeros((size, tile), FULL)
        new_top = jnp.full((1, tile), NEG_LARGE, FULL)
        for r in range(count):
            here = slice(r * capacity, (r + 1) * capacity)
            scores = jnp.dot(k_ref[here, :], q_ref[:, ahead], preferred_element_type=FULL)
            score_ref[then, here, :] = scores
            new_top = jnp.maximum(new_top, jnp.max(scores, axis=0, keepdims=True))
            weights = jnp.exp(score_ref[now, here, :] - top)
            total = total + jnp.sum(weights, axis=0, keepdims=True)
            summed = summed + jnp.dot(
                v_ref[:, here], weights.astype(LOW), preferred_element_type=FULL
            )
        top_ref[then] = jnp.broadcast_to(new_top, (8, tile))
        out = summed / total
        o_ref[:, at] = out
        low_ref[:, at] = out.astype(LOW)
        lse[:, at] = jnp.broadcast_to(top + jnp.log(total), (8, tile))

    def step(i, carry):
        phase(2 * i, 0, 2 * i + 1, 1)
        phase(2 * i + 1, 1, jnp.minimum(2 * i + 2, last), 0)
        return carry

    scores = jnp.dot(k_ref[...], q_ref[:, 0:tile], preferred_element_type=FULL)
    score_ref[0] = scores
    top_ref[0] = jnp.broadcast_to(jnp.max(scores, axis=0, keepdims=True), (8, tile))
    arriving = []
    for p, (low, high) in enumerate(tiles_of(count, capacity, 2 * tile)):
        lax.fori_loop(low, high, step, 0)
        done = low_ref.at[:, p * capacity : (p + 1) * capacity]
        if p < count - 1:
            there = head_rows(heads, mover.ctx, size)
            arriving.append(mover.go(done, there, ctx=mover.back(p + 1)))
        else:
            head_rows(heads, mover.ctx, size)[...] = low_ref[:, p * capacity : (p + 1) * capacity]
        between(p + 1)
    for copy in arriving:
        mover.take(copy)


def attend_back_part(size, tile, mover, parts, bias, qkv, o_ref, lse, grads, work, ready, waiting, begun, between):
    k_ref, v_ref, q_ref, do_ref, nat_ref, delta_ref, dq_ref, dk_ref, dv_ref, got, back, score_ref, grad_ref = work
    count, width, capacity = qkv.shape
    slots = count * capacity
    sent = [None] + [
        mover.go(head_rows(parts, mover.on(by), size), got.at[by], ctx=mover.on(by))
        for by in range(1, count)
    ]
    got[0] = head_rows(parts, mover.ctx, size)[...]
    waiting()
    ready()
    q_ref[size:PAD, :] = jnp.concatenate(
        [jnp.ones((16, slots), LOW), jnp.zeros((PAD - size - 16, slots), LOW)], axis=0
    )
    do_ref[size:PAD, :] = jnp.zeros((PAD - size, slots), LOW)
    dq_ref[...] = jnp.zeros_like(dq_ref)
    for r in range(count):
        here = slice(r * capacity, (r + 1) * capacity)
        pad = jnp.zeros((PAD - size - 16, capacity), LOW)
        k_ref[here, :] = turned(
            jnp.concatenate([qkv[r, size : 2 * size, :], bias[:, here], pad], axis=0)
        )
        v_ref[here, :] = turned(
            jnp.concatenate(
                [qkv[r, 2 * size : 3 * size, :], jnp.zeros((PAD - size, capacity), LOW)], axis=0
            )
        )
    for r in range(count):
        if r:
            mover.take(sent[r])
        p = order_of(r, count)
        at = slice(p * capacity, (p + 1) * capacity)
        scaled = (qkv[r, 0:size, :] * (size**-0.5)).astype(LOW)
        dout = got[r]
        q_ref[0:size, at] = scaled
        do_ref[0:size, at] = dout
        nat_ref[at, :] = turned(jnp.concatenate([scaled, dout], axis=0))
        delta = jnp.sum(dout.astype(FULL) * o_ref[:, at], axis=0, keepdims=True)
        delta_ref[:, at] = jnp.broadcast_to(delta, (8, capacity))

    begun()
    last = slots // tile - 1
    assert last % 2 == 1
    tiles = tiles_of(count, capacity, 2 * tile)
    arriving = []
    mine = head_rows(grads, mover.ctx, width)
    for turn, r in enumerate(list(range(1, count)) + [0]):
        here = slice(r * capacity, (r + 1) * capacity)
        dk_ref[...] = jnp.zeros_like(dk_ref)
        dv_ref[...] = jnp.zeros_like(dv_ref)

        def ready_scores(t, then, low, high, r=r):
            ahead = tile_at(t, tile)
            rows = slice(r * capacity + low, r * capacity + high)
            score_ref[then, low:high, :] = jnp.dot(
                k_ref[rows, :], q_ref[:, ahead], preferred_element_type=FULL
            )
            grad_ref[then, low:high, :] = jnp.dot(
                v_ref[rows, :], do_ref[:, ahead], preferred_element_type=FULL
            )

        def phase(t, now, following, then, r=r):
            at = tile_at(t, tile)
            query_grad = jnp.zeros((size, tile), FULL)
            for low, high in parts_of(capacity):
                ready_scores(following, then, low, high)
                chance = jnp.exp(score_ref[now, low:high, :] - lse[0:1, at])
                score_grad = (
                    chance * (grad_ref[now, low:high, :] - delta_ref[0:1, at])
                ).astype(LOW)
                query_grad = query_grad + jnp.dot(
                    qkv[r, size : 2 * size, low:high], score_grad, preferred_element_type=FULL
                )
                dk_ref[low:high, :] += jnp.dot(
                    score_grad, nat_ref[at, :], preferred_element_type=FULL
                )
                dv_ref[low:high, :] += jnp.dot(
                    chance.astype(LOW), nat_ref[at, :], preferred_element_type=FULL
                )
            dq_ref[:, at] += query_grad

        def step(i, carry, phase=phase):
            phase(2 * i, 0, 2 * i + 1, 1)
            phase(2 * i + 1, 1, jnp.minimum(2 * i + 2, last), 0)
            return carry

        ready_scores(0, 0, 0, capacity)
        if r:
            lax.fori_loop(0, tiles[-1][1], step, 0)
        else:
            for p, (low, high) in enumerate(tiles):
                lax.fori_loop(low, high, step, 0)
                at = slice(p * capacity, (p + 1) * capacity)
                value = (dq_ref[:, at] * (size**-0.5)).astype(LOW)
                if p < count - 1:
                    back[p + 1, 0:size, :] = value
                    arriving.append(
                        mover.go(
                            back.at[p + 1, 0:size], mine.at[0:size], ctx=mover.back(p + 1)
                        )
                    )
                else:
                    mine[0:size, :] = value
        keys = dk_ref[...].T[0:size].astype(LOW)
        values = dv_ref[...].T[size : 2 * size].astype(LOW)
        if r:
            back[r, size : 2 * size, :] = keys
            back[r, 2 * size : 3 * size, :] = values
            arriving.append(
                mover.go(
                    back.at[r, size : 3 * size], mine.at[size : 3 * size], ctx=mover.back(r)
                )
            )
        else:
            mine[size : 2 * size, :] = keys
            mine[2 * size : 3 * size, :] = values
        between(turn)
    for copy in arriving:
        mover.take(copy)


def attend_back_buffers(size, count, capacity, tile):
    slots = count * capacity
    return [
        VMEM((slots, PAD), LOW),
        VMEM((slots, PAD), LOW),
        VMEM((PAD, slots), LOW),
        VMEM((PAD, slots), LOW),
        VMEM((slots, PAD), LOW),
        VMEM((8, slots), FULL),
        VMEM((size, slots), FULL),
        VMEM((capacity, PAD), FULL),
        VMEM((capacity, PAD), FULL),
        VMEM((count, size, capacity), LOW),
        VMEM((count, 3 * size, capacity), LOW),
        VMEM((2, capacity, tile), FULL),
        VMEM((2, capacity, tile), FULL),
    ]


class Round:
    def __init__(self, mover, rows, full, buffers):
        place = lax.axis_index("tp")
        core, far = lax.rem(place, 2), place // 2
        self.mover, self.full = mover, full
        self.give, self.ra, self.passing, self.rb, self.keep = buffers
        self.span = rows // 4
        self.half = self.span // 2
        self.mate, self.far = tp_peers()

        def quarter(c, f):
            return (c * 2 + f) * self.span

        self.own, self.other = quarter(core, far), quarter(core, 1 - far)
        self.mate_own, self.mate_other = quarter(1 - core, far), quarter(1 - core, 1 - far)

    def rows(self, start, count=None):
        return pl.ds(pl.multiple_of(start, 16), count or self.span)

    def hand(self, slot, value):
        self.give[slot] = value.astype(LOW)
        return self.mover.go(self.give.at[slot], self.ra.at[slot], tp=self.mate)

    def onward(self, value, index):
        self.mover.take(index)
        self.passing[...] = (value + self.ra[1].astype(FULL)).astype(LOW)
        return [
            self.mover.go(self.passing.at[at], self.rb.at[at], tp=self.far)
            for at in (pl.ds(0, self.half), pl.ds(self.half, self.half))
        ]

    def close(self, far_copies, index, finish, halfway=None):
        self.mover.take(index)
        self.keep[...] += self.ra[0].astype(FULL)
        self.to_far, self.to_mate = [], []
        for c in range(2):
            at = pl.ds(c * self.half, self.half)
            self.mover.take(far_copies[c])
            low = finish(at, self.keep[at] + self.rb[at].astype(FULL))
            mine = self.full.at[self.rows(self.own + c * self.half, self.half)]
            mine[...] = low
            self.to_far.append(self.mover.go(mine, mine, tp=self.far))
            self.to_mate.append(self.mover.go(mine, mine, tp=self.mate))
            if halfway and c == 0:
                halfway()

    def eager(self, make, finish, meanwhile=None, halfway=None):
        first = self.hand(1, make(self.mate_other))
        copies = self.onward(make(self.other), first)
        second = self.hand(0, make(self.mate_own))
        self.keep[...] = make(self.own)
        if meanwhile:
            meanwhile()
        self.close(copies, second, finish, halfway)

    def after(self, before, make, finish, meanwhile, between):
        before.have_mate_own()
        second = self.hand(0, make(self.mate_own))
        self.keep[...] = make(self.own)
        before.have_other()
        between()
        value = make(self.other)
        before.have_mate_other()
        first = self.hand(1, make(self.mate_other))
        copies = self.onward(value, first)
        meanwhile()
        self.close(copies, second, finish)

    def have_mate_own(self):
        for copy in self.to_mate:
            self.mover.take(copy)

    def have_other(self):
        self.passed = []
        for c in range(2):
            self.mover.take(self.to_far[c])
            rows = self.full.at[self.rows(self.other + c * self.half, self.half)]
            self.passed.append(self.mover.go(rows, rows, tp=self.mate))

    def have_mate_other(self):
        for copy in self.passed:
            self.mover.take(copy)

    def have(self):
        self.have_mate_own()
        self.have_other()
        self.have_mate_other()


ROUND_COPIES = 10


def round_buffers(rows, width):
    span = rows // 4
    return [
        VMEM((2, span, width), LOW),
        VMEM((2, span, width), LOW),
        VMEM((span, width), LOW),
        VMEM((span, width), LOW),
        VMEM((span, width), FULL),
    ]


NAMES = ("qkv", "out", "up", "down")


def layer_kernel(plan, last, size, tile, mover, ins, outs, work):
    ins, outs, work = iter(ins), iter(outs), iter(work)
    source = next(ins)
    x_ref = None if plan.entry else next(ins)
    live_ref = next(ins)
    far_params = [next(ins) for _ in range(8)]
    stream, following = next(outs), next(outs)
    far_qkv, far_o, far_lse, far_heads, far_middle, far_second, far_hidden, far_slope = [
        next(outs) for _ in range(8)
    ]
    far_first = next(outs) if plan.entry else None
    joint, nat, heads, qkv, o_ref, lse, middle, second, hidden, slope = [
        next(work) for _ in range(10)
    ]
    first = next(work) if plan.entry else source
    attend_work = [next(work) for _ in range(6)]
    one_work, two_work = [next(work) for _ in range(5)], [next(work) for _ in range(5)]
    rows = source.shape[0]
    bias, qkv_bias = next(work), next(work)
    params = [next(work) for _ in range(8)]
    whole = {name: next(work) for name in NAMES}
    gathers, loads = {}, {}
    for name in plan.held:
        loads[name] = (next(ins), whole[name])
    for name in plan.own:
        gathers[name, 0] = Gather(mover, next(ins).at[plan.layer], whole[name])
    kept_ahead = {name: next(outs) for name in plan.ahead}
    for name in plan.ahead:
        gathers[name, 1] = Gather(mover, next(ins).at[plan.layer + 1], next(work))
    kept = {name: next(outs) for name in plan.own}

    greet(mover, bool(gathers))
    if plan.entry:
        gathers_first = [key for key in [("qkv", 0)] if key in gathers]
        for key in gathers_first:
            gathers[key].start()
    param_loads = [mover.stay(there, here) for there, here in zip(far_params, params)]
    waiting_loads = dict(loads)
    loads = {}

    def load(names):
        for name in names:
            if name in waiting_loads and name not in loads:
                loads[name] = mover.stay(*waiting_loads[name])

    load(["qkv"])

    def have(name):
        if name in waiting_loads:
            mover.near(loads[name])
            load(NAMES)
        else:
            gathers[name, 0].have()
            mover.stay(whole[name], kept[name])
        return whole[name]

    def begin(keys):
        for key in keys:
            if key in gathers:
                gathers[key].start_line()

    def begin_over(keys):
        for key in keys:
            if key in gathers:
                gathers[key].start_over()

    def pass_on(keys, stage):
        for key in keys:
            if key in gathers:
                gathers[key].pass_on(stage)

    def pass_all(keys):
        for stage in (1, 2, 3):
            pass_on(keys, stage)

    mover.near(*param_loads)
    layer, after = plan.layer, min(plan.layer + 1, params[0].shape[0] - 1)

    def row(index, layer=layer):
        return params[index][...].astype(FULL)[layer : layer + 1]

    b_out, gain2, shift2, b_down, b_up = row(0), row(1), row(2), row(3), row(6)
    gain1, shift1, gain0, shift0 = row(4, after), row(5, after), row(4), row(5)
    qkv_bias[...] = joint_bias(row(7), size, joint.shape[0])
    key_bias(mover, live_ref, bias)
    ahead = [("qkv", 1), ("out", 1), ("up", 1)]
    one = Round(mover, rows, second, one_work)
    two = Round(mover, rows, following, two_work)
    if plan.entry:
        chunk = rows // 5 if rows % 80 == 0 else rows

        def norm_step(i, carry):
            at = pl.ds(pl.multiple_of(i * chunk, 16), chunk)
            value = normalize(source[at, :].astype(FULL), gain0, shift0)[0]
            first[at, :] = value.astype(LOW)
            return carry

        lax.fori_loop(0, rows // chunk, norm_step, 0)
        mover.stay(first, far_first)
        pass_all([("qkv", 0)])
        begin([("out", 0), ("up", 0)])
        begin_over([("out", 0), ("up", 0), ("down", 0)] + ahead)
        turned_product(first, have("qkv"), qkv_bias, joint)
    else:
        turned_product(first, have("qkv"), qkv_bias, joint)

    def after_send():
        if plan.entry:
            pass_all([("out", 0), ("up", 0)])
        else:
            for name in plan.own:
                gathers[name, 0].start_over()

    def begun():
        if plan.entry:
            begin([("down", 0)])
        else:
            for name in plan.own:
                gathers[name, 0].start_line()

    def between(p):
        if p > 2:
            pass_on([("down", 0)], p - 2)
        if p == 4:
            if not plan.entry:
                begin_over(ahead)
            begin(ahead)

    attend_part(
        size, tile, mover, joint, bias, heads, qkv, o_ref, lse, attend_work, after_send, begun, between
    )
    nat[...] = turned(heads[...])
    w_out = have("out")

    def out_part(start):
        return dot(nat[one.rows(start), :], w_out[...], ((1,), (1,)))

    def to_second(at, value):
        if plan.entry:
            before = source[one.rows(one.own + at.start, at.size), :].astype(FULL)
        else:
            before = x_ref[at]
        value = before + value + b_out
        middle[at] = value
        return normalize(value, gain2, shift2)[0].astype(LOW)

    def meanwhile():
        mover.stay(qkv, far_qkv)
        mover.stay(o_ref, far_o)
        mover.stay(lse, far_lse)
        mover.stay(nat, far_heads)
        pass_on([("down", 0)], 3)

    one.eager(out_part, to_second, meanwhile, lambda: pass_on(ahead[:2], 1))
    pass_on(ahead[:2], 2)
    w_up, w_down = have("up"), have("down")

    def mlp_part(start):
        at = two.rows(start)
        pre = jnp.dot(second[at, :], w_up[...], preferred_element_type=FULL) + b_up
        low, low_slope = gelu_pair(pre)
        hidden[at, :] = low
        slope[at, :] = low_slope
        return dot(low, w_down[...], ((1,), (1,)))

    def to_following(at, value):
        value = middle[at] + value + b_down
        stream[at] = value
        if last:
            return live_rows(value, two.own + at.start, live_ref[0, mover.ctx]).astype(LOW)
        return normalize(value, gain1, shift1)[0].astype(LOW)

    def meanwhile():
        mover.stay(middle, far_middle)
        mover.stay(second, far_second)
        mover.stay(hidden, far_hidden)
        mover.stay(slope, far_slope)
        pass_on(ahead[2:], 3)

    def between_parts():
        pass_on(ahead[:2], 3)
        pass_on(ahead[2:], 1)
        pass_on(ahead[2:], 2)

    two.after(one, mlp_part, to_following, meanwhile, between_parts)
    two.have()
    for name in plan.ahead:
        gathers[name, 1].have()
        mover.stay(gathers[name, 1].target, kept_ahead[name])
    mover.settle()


class Plan:
    def __init__(self, layer, last, inside):
        self.layer, self.entry = layer, layer == 0
        self.own = (NAMES if layer == 0 else ("down",)) if inside else ()
        self.ahead = ("qkv", "out", "up") if inside and not last else ()
        self.held = tuple(name for name in NAMES if name not in self.own)


def forward_layer(source, x, live, params, gathered, weights, plan, last, size, sizes, ident):
    rows, width = source.shape
    count = sizes[0]
    joint, hidden = weights["qkv"].shape[2], weights["up"].shape[2]
    heads = joint // (3 * size)
    attn, slots, span = heads * size, count * rows, rows // 4
    tile = 256 if slots % 256 == 0 else PAD
    columns = {"qkv": joint, "out": attn, "up": hidden, "down": hidden}
    inputs = [(source, VMEM)] + ([] if plan.entry else [(x, VMEM)])
    inputs += [(live, SMEM)] + [(value, HBM) for value in params]
    inputs += [(gathered[name, plan.layer], HBM) for name in plan.held]
    inputs += [(weights[name], HBM) for name in plan.own + plan.ahead]
    saved = [
        ((count, 3 * size, rows), LOW),
        ((size, slots), FULL),
        ((8, slots), FULL),
        ((rows, attn), LOW),
        ((span, width), FULL),
        ((rows, width), LOW),
        ((rows, hidden), LOW),
        ((rows, hidden), LOW),
    ]
    outputs = [((span, width), FULL, VMEM), ((rows, width), LOW, VMEM)]
    outputs += [(shape, dtype, HBM) for shape, dtype in saved]
    if plan.entry:
        outputs.append(((rows, width), LOW, HBM))
    outputs += [((width, columns[name]), LOW, HBM) for name in plan.ahead + plan.own]
    qkv_shape, o_shape, lse_shape, heads_shape = saved[:4]
    scratch = [VMEM((joint, rows), LOW), VMEM((rows, attn), LOW), VMEM((attn, rows), LOW)]
    scratch += [VMEM(*pair) for pair in saved[:3] + saved[4:]]
    if plan.entry:
        scratch.append(VMEM((rows, width), LOW))
    scratch += [
        VMEM((slots, PAD), LOW),
        VMEM((PAD, slots), LOW),
        VMEM((size, slots), LOW),
        VMEM((size, slots), LOW),
        VMEM((2, slots, tile), FULL),
        VMEM((2, 8, tile), FULL),
    ]
    scratch += round_buffers(rows, width) + round_buffers(rows, width)
    scratch += [VMEM((16, slots), LOW), VMEM((16, joint), FULL)]
    scratch += [VMEM(value.shape, value.dtype) for value in params]
    scratch += [VMEM((width, columns[name]), LOW) for name in NAMES + plan.ahead]
    results = run(
        functools.partial(layer_kernel, plan, last, size, tile),
        "forward_layer",
        ident,
        inputs,
        outputs,
        scratch,
        2 * (count - 1) + 2 * ROUND_COPIES + 2 * count * len(plan.own + plan.ahead),
        10 + 2 * len(plan.own + plan.ahead) + len(plan.held) + len(params),
        sizes,
        58,
        2 * rows * width * (2 * hidden + attn + joint) + 4 * slots * slots * 256,
    )
    stream, following = results[:2]
    kept = results[2 : 11 if plan.entry else 10]
    for name, value in zip(plan.ahead, results[2 + len(kept) :]):
        gathered[name, plan.layer + 1] = value
    for name, value in zip(plan.own, results[2 + len(kept) + len(plan.ahead) :]):
        gathered[name, plan.layer] = value
    return stream, following, kept


class SmallSums:
    def __init__(self, mover, rows, held, got):
        self.mover, self.rows, self.held, self.got = mover, rows, held, got
        self.stage = 0
        mate, far = tp_peers()
        self.peers = [
            dict(tp=mate),
            dict(tp=far),
            dict(shard=1 - mover.shard),
            dict(ctx=mover.flip(2)),
            dict(ctx=mover.flip(1)),
        ]

    def part(self, stage):
        return pl.ds(0, self.rows if stage < 2 else self.held.shape[1])

    def step(self):
        stage, mover = self.stage, self.mover
        if stage:
            mover.take(self.copy)
            at = self.part(stage - 1)
            self.held[stage] = self.held[stage - 1]
            self.held[stage, at, :] = self.held[stage - 1, at, :] + self.got[stage - 1, at, :]
        if stage < len(self.peers):
            at = self.part(stage)
            self.copy = mover.go(
                self.held.at[stage, at], self.got.at[stage, at], **self.peers[stage]
            )
        self.stage = stage + 1

    def value(self):
        return self.held[len(self.peers)]


def key_bias(mover, live_ref, bias):
    capacity = bias.shape[1] // mover.ctx_count
    row = lax.broadcasted_iota(jnp.int32, (16, capacity), 0)
    slot = lax.broadcasted_iota(jnp.int32, (16, capacity), 1)
    for r in range(mover.ctx_count):
        live = live_ref[0, mover.back(r)]
        value = jnp.where((row == 0) & (slot >= live), NEG_LARGE, 0.0)
        bias[:, r * capacity : (r + 1) * capacity] = value.astype(LOW)


def pair_columns(rows, width, size, turn):
    shape = (width, rows) if turn else (rows, width)
    given = lax.broadcasted_iota(jnp.int32, shape, 1 if turn else 0)
    column = lax.broadcasted_iota(jnp.int32, shape, 0 if turn else 1)
    head, within = column // (3 * size), column % (3 * size)
    wanted = head * (2 * size) + jnp.where(within < size, within, within - size)
    key = (within >= size) & (within < 2 * size)
    return jnp.where((given == wanted) & ~key, 1.0, 0.0).astype(LOW)


def joint_bias(pair, size, width):
    rows = pair.shape[1]
    spread = jnp.broadcast_to(pair, (16, rows)).astype(LOW)
    return jnp.dot(spread, pair_columns(rows, width, size, False), preferred_element_type=FULL)


def live_rows(value, start, live):
    row = start + lax.broadcasted_iota(jnp.int32, value.shape, 0)
    return jnp.where(row < live, value, 0.0)


def sums_into(sums, first, at, values):
    for index, value in enumerate(values):
        row = first + index
        added = jnp.sum(value, axis=0, keepdims=True)
        width = added.shape[1]
        sums[row : row + 1, 0:width] = (
            added if at.start == 0 else sums[row : row + 1, 0:width] + added
        )


def back_kernel(plan, size, tile, mover, ins, outs, work):
    ins, outs, work = iter(ins), iter(outs), iter(work)
    source = next(ins)
    x_ref = None if plan.last else next(ins)
    live_ref, far_gain2, far_gain1 = [next(ins) for _ in range(3)]
    far = [next(ins) for _ in range(14)]
    late_far = next(ins) if plan.late else None
    others = [(next(ins), next(ins)) for _ in range(plan.others)]
    stream, following = next(outs), next(outs)
    grad_outs = {name: next(outs) for name in NAMES if plan.inside and (name != "qkv" or plan.final)}
    mid_out = next(outs) if plan.inside and not plan.final else None
    late_out = next(outs) if plan.late else None
    split = local = totals = None
    if plan.joined:
        totals = next(outs)
    else:
        split, local = next(outs), next(outs)
    wholes = {} if plan.inside else {name: next(outs) for name in NAMES}
    near = [next(work) for _ in range(14)]
    slope, w_down, w_up, middle, hidden, second, w_out, heads, qkv, o_ref, lse, first, w_qkv, before = near
    grad = next(work) if plan.last else source
    pre_grad, attn_grad, parts, grads, nat = [next(work) for _ in range(5)]
    attend_work = [next(work) for _ in range(13)]
    one_work, two_work = [next(work) for _ in range(5)], [next(work) for _ in range(5)]
    rows, width = source.shape
    reduces = {}
    if plan.inside:
        pairs = {
            "down": (grad, hidden),
            "up": (second, pre_grad),
            "out": (attn_grad, heads),
            "qkv": (first, nat),
        }
        for name in ("down", "up", "out", "qkv"):
            buffers = [next(work) for _ in range(4)]
            reduces[name] = Reduce(mover, buffers, grad_outs.get(name), *pairs[name])
    late = None
    if plan.late:
        late_mid, late_line = next(work), next(work)
        late = Reduce(mover, (late_mid, None, late_mid, late_line), late_out, None, None)
    bias, gain2_ref, gain1_ref = [next(work) for _ in range(3)]
    if plan.joined:
        split, local = next(work), next(work)
        early_held, early_got, late_held, late_got = [next(work) for _ in range(4)]
        tops = 8 * (plan.others + 1)
        early = SmallSums(mover, tops, early_held, early_got)
        final = SmallSums(mover, 8, late_held, late_got)
        everything = [(split, local)] + others

    greet(mover, plan.inside)
    gain_loads = [mover.stay(far_gain2, gain2_ref), mover.stay(far_gain1, gain1_ref)]
    one = Round(mover, rows, attn_grad, one_work)
    two = Round(mover, rows, following, two_work)
    if plan.final:
        far[13] = far[13].at[two.rows(two.own)]
    load = [mover.stay(there, here) for there, here in zip(far[:3], near[:3])]
    if late:
        mover.near(mover.stay(late_far, late_mid))
        late.spread()
    if plan.last:
        chunk = rows // 5 if rows % 80 == 0 else rows

        def mask_step(i, carry):
            at = pl.ds(pl.multiple_of(i * chunk, 16), chunk)
            value = source[at, :].astype(FULL)
            grad[at, :] = live_rows(value, i * chunk, live_ref[0, mover.ctx]).astype(LOW)
            return carry

        lax.fori_loop(0, rows // chunk, mask_step, 0)
    key_bias(mover, live_ref, bias)
    mover.near(*gain_loads)
    gain2, gain1 = [
        ref[...].astype(FULL)[plan.layer : plan.layer + 1] for ref in (gain2_ref, gain1_ref)
    ]
    split[...] = jnp.zeros_like(split)
    local[...] = jnp.zeros_like(local)
    split[5:6, 0:width] = jnp.sum(
        grad[one.rows(one.own), :].astype(FULL), axis=0, keepdims=True
    )
    mover.near(*load[:3])
    load += [mover.stay(there, here) for there, here in zip(far[3:], near[3:])]
    hidden_width = slope.shape[1]

    def mlp_part(start):
        at = one.rows(start)
        pre = jnp.dot(grad[at, :], w_down[...], preferred_element_type=FULL)
        low = (pre * slope[at, :].astype(FULL)).astype(LOW)
        pre_grad[at, :] = low
        local[0:1, 0:hidden_width] += jnp.sum(low.astype(FULL), axis=0, keepdims=True)
        return dot(low, w_up[...], ((1,), (1,)))

    def to_attn(at, value):
        if plan.last:
            above = grad[one.rows(one.own + at.start, at.size), :].astype(FULL)
        else:
            above = x_ref[at]
        _, normed, inverse = normalize(middle[at], 1.0, 0.0)
        result = above + normalize_back(value, normed, inverse, gain2)
        stream[at] = result
        low = result.astype(LOW)
        sums_into(split, 2, at, (value * normed, value, low.astype(FULL)))
        return low

    def reduce(name):
        if name in reduces:
            reduces[name].begin_blocks()

    def own(name):
        if name in reduces:
            reduces[name].own()

    def spread(name):
        if name in reduces:
            reduces[name].fold_blocks(3, 1)
            reduces[name].spread()

    def finish(name):
        if name in reduces:
            reduces[name].fold_blocks(2, 0)
            reduces[name].finish()

    def begin_early():
        if plan.joined:
            early_held[0] = jnp.zeros(early_held.shape[1:], FULL)
            for layer, (some, more) in enumerate(everything):
                first_row = 0 if layer else 2
                for row in range(first_row, 6):
                    at = row * len(everything) + layer
                    early_held[0, at : at + 1, :] = some[row : row + 1, :]
                for row in range(2 if layer else 1):
                    at = tops + row * len(everything) + layer
                    early_held[0, at : at + 1, :] = more[row : row + 1, :]

    def early_step():
        if plan.joined:
            early.step()

    def start_down():
        mover.near(*load[3:5])
        reduce("down")

    one.eager(mlp_part, to_attn, start_down)
    if late:
        late.finish()
    mover.near(load[5])
    reduce("up")
    one.have()
    mover.near(load[6])
    turned_product(attn_grad, w_out, None, parts)

    def waiting():
        begin_early()
        early_step()
        own("down")
        spread("down")
        mover.near(load[7])
        reduce("out")
        own("out")

    def ready():
        own("up")
        mover.near(load[8], load[9], load[10])

    def between(turn):
        if turn == 0:
            early_step()
        if turn == 3:
            finish("down")
            spread("up")

    attend_back_part(
        size,
        tile,
        mover,
        parts,
        bias,
        qkv,
        o_ref,
        lse,
        grads,
        attend_work,
        ready,
        waiting,
        lambda: None,
        between,
    )
    early_step()
    nat[...] = turned(grads[...])
    pairs_width = nat.shape[1] // 3 * 2
    picked = jnp.dot(
        nat[...], pair_columns(pairs_width, nat.shape[1], size, True), preferred_element_type=FULL
    )
    local[1:2, 0:pairs_width] = jnp.sum(picked, axis=0, keepdims=True)
    mover.near(*load[11:])

    def qkv_part(start):
        return dot(nat[two.rows(start), :], w_qkv[...], ((1,), (1,)))

    def to_following(at, value):
        row = before[at, :].astype(FULL)
        _, normed, inverse = normalize(row, 1.0, 0.0)
        result = stream[at] + normalize_back(value, normed, inverse, gain1)
        stream[at] = result
        low = result.astype(LOW)
        sums_into(split, 0, at, (value * normed, value))
        return low

    def meanwhile():
        own("qkv")
        finish("up")
        spread("out")
        early_step()

    def halfway():
        if plan.inside:
            reduces["qkv"].fold_blocks(3, 1)
            if plan.final:
                reduces["qkv"].spread()

    reduce("qkv")
    two.eager(qkv_part, to_following, meanwhile, halfway)
    if plan.joined:
        late_held[0, 0:8, :] = jnp.zeros((8, late_held.shape[2]), FULL)
        late_held[0, 0:2, :] = split[0:2, :]
        late_held[0, 8:16, :] = local[...]
        final.step()
        early_step()
        final.step()
    finish("out")
    two.have_mate_own()
    two.have_other()
    if plan.joined:
        final.step()
    if plan.inside:
        reduces["qkv"].fold_blocks(2, 0)
        if plan.final:
            reduces["qkv"].finish()
        else:
            mover.stay(reduces["qkv"].mid, mid_out)
    if plan.joined:
        final.step()
    two.have_mate_other()
    if plan.joined:
        final.step()
    for name in ("down", "up", "out"):
        if name in reduces:
            reduces[name].done()
    if late:
        late.done()
    if plan.inside and plan.final:
        reduces["qkv"].done()
    if plan.joined:
        final.step()
        early.step()
        totals[...] = early.value()
        last_value = final.value()
        for row in range(2):
            at = row * len(everything)
            totals[at : at + 1, :] = last_value[row : row + 1, :]
        at = tops + len(everything)
        totals[at : at + 1, :] = last_value[9:10, :]
    if not plan.inside:
        for name, (lhs, rhs) in {
            "down": (grad, hidden),
            "up": (second, pre_grad),
            "out": (attn_grad, heads),
            "qkv": (first, nat),
        }.items():
            full = Reduce(mover, (wholes[name],) * 4, None, lhs, rhs)
            full.compute(wholes[name], 0)
    mover.settle()


def gather_outputs_kernel(layers, *refs):
    count = layers * len(NAMES)
    parts, token_grads, mixed, totals = refs[:count], refs[count], refs[count + 1], refs[count + 2]
    outs, work = refs[count + 3 : count + 17], refs[count + 17 : -2]
    into, out_of = refs[-2:]
    coming, going = [], []
    pairs = [(mixed, work[4], outs[4].at[0])]
    for index in range(len(NAMES)):
        for layer in range(layers):
            pairs.append(
                (parts[index * layers + layer], work[index].at[layer], outs[index].at[layer])
            )
    for i, (source, stage, _) in enumerate(pairs):
        coming.append(pltpu.make_async_copy(source, stage, into.at[i]))
        coming[-1].start()
    outs[5][0] = token_grads[...].astype(FULL)
    for row, out in enumerate(outs[6:12]):
        out[...] = totals[row * layers : (row + 1) * layers, 0 : out.shape[1]]
    for row, out in enumerate(outs[12:14]):
        row = row + 8
        out[...] = totals[row * layers : (row + 1) * layers, 0 : out.shape[1]]
    for i, (_, stage, target) in enumerate(pairs):
        coming[i].wait()
        going.append(pltpu.make_async_copy(stage, target, out_of.at[i]))
        going[-1].start()
    for copy in going:
        copy.wait()


def gather_outputs(done, token_grads, mixed, totals, layers, widths):
    rows, width = token_grads.shape
    parts = [done[name, layer] for name in NAMES for layer in range(layers)]
    hbm, whole = pl.BlockSpec(memory_space=HBM), lambda shape: pl.BlockSpec(
        shape, lambda i: (0,) * len(shape)
    )
    shapes = [(layers,) + done[name, 0].shape for name in NAMES] + [(1, rows, width)] * 2
    types = [FULL] * 4 + [LOW, FULL]
    small = [(layers, width)] * 6 + [(layers, count) for count in widths]
    copies = len(parts) + 1
    return pl.pallas_call(
        functools.partial(gather_outputs_kernel, layers),
        grid=(1,),
        in_specs=[hbm] * len(parts) + [whole(token_grads.shape), hbm, whole(totals.shape)],
        out_specs=[hbm] * 5 + [whole(shape) for shape in shapes[5:] + small],
        out_shape=[jax.ShapeDtypeStruct(*pair) for pair in zip(shapes, types)]
        + [jax.ShapeDtypeStruct(shape, FULL) for shape in small],
        scratch_shapes=[VMEM(shape, FULL) for shape in shapes[:4]]
        + [VMEM((rows, width), LOW)]
        + [pltpu.SemaphoreType.DMA((copies,)), pltpu.SemaphoreType.DMA((copies,))],
        compiler_params=pltpu.CompilerParams(vmem_limit_bytes=60 * 2**20),
        name="gather_outputs",
    )(*parts, token_grads, mixed, totals)


class BackPlan:
    def __init__(self, layer, layers, inside):
        self.inside, self.layer = inside, layer
        self.last, self.final = layer == layers - 1, layer == 0
        self.late = inside and not self.last
        self.joined = inside and self.final
        self.others = layers - 1 if self.joined else 0


def back_layer(source, x, live, gain2, gain1, saved, late, others, plan, size, sizes, ident):
    rows, width = source.shape
    count = sizes[0]
    slope, w_down, w_up = saved[:3]
    hidden, joint, attn = slope.shape[1], saved[12].shape[1], saved[6].shape[1]
    slots, span = count * rows, rows // 4
    tile = 256 if slots % 256 == 0 else PAD
    wide = max(width, hidden, joint)
    half = width // 2
    block = half // count
    columns = {"qkv": joint, "out": attn, "up": hidden, "down": hidden}
    inputs = [(source, VMEM)] + ([] if plan.last else [(x, VMEM)])
    inputs += [(live, SMEM), (gain2, HBM), (gain1, HBM)]
    inputs += [(value, HBM) for value in saved]
    if plan.late:
        inputs.append((late, HBM))
    for pair in others[: plan.others]:
        inputs += [(value, VMEM) for value in pair]
    outputs = [((span, width), FULL, VMEM), ((rows, width), LOW, VMEM)]
    names = [name for name in NAMES if plan.inside and (name != "qkv" or plan.final)]
    outputs += [((block, columns[name]), FULL, VMEM) for name in names]
    if plan.inside and not plan.final:
        outputs.append(((half, joint), LOW, HBM))
    if plan.late:
        outputs.append(((block, joint), FULL, VMEM))
    depth = 8 * (plan.others + 1)
    if plan.joined:
        outputs.append(((depth + 8, wide), FULL, VMEM))
    else:
        outputs += [((8, wide), FULL, VMEM)] * 2
    if not plan.inside:
        outputs += [((width, columns[name]), LOW, VMEM) for name in NAMES]
    scratch = [VMEM(value.shape, value.dtype) for value in saved]
    scratch[13] = VMEM((span, width), saved[13].dtype)
    if plan.last:
        scratch.append(VMEM((rows, width), LOW))
    scratch += [
        VMEM((rows, hidden), LOW),
        VMEM((rows, width), LOW),
        VMEM((attn, rows), LOW),
        VMEM((joint, rows), LOW),
        VMEM((rows, joint), LOW),
    ]
    scratch += attend_back_buffers(size, count, rows, tile)
    scratch += round_buffers(rows, width) + round_buffers(rows, width)
    if plan.inside:
        for name in ("down", "up", "out", "qkv"):
            scratch += reduce_buffers(half, columns[name], count)
    if plan.late:
        scratch += [VMEM((half, joint), LOW), VMEM((count - 1, block, joint), LOW)]
    scratch.append(VMEM((16, slots), LOW))
    scratch += [VMEM(value.shape, value.dtype) for value in (gain2, gain1)]
    assert 2 * (plan.others + 1) <= 8
    if plan.joined:
        scratch += [VMEM((8, wide), FULL)] * 2
        scratch += [
            VMEM((6, depth + 8, wide), FULL),
            VMEM((5, depth + 8, wide), FULL),
            VMEM((6, 16, wide), FULL),
            VMEM((5, 16, wide), FULL),
        ]
    results = run(
        functools.partial(back_kernel, plan, size, tile),
        "back_layer",
        ident,
        inputs,
        outputs,
        scratch,
        3 * (count - 1) + 2 * ROUND_COPIES + 8 * count + 10 + count,
        len(saved) + 4,
        sizes,
        58,
        6 * rows * width * (2 * hidden + attn + joint) + 10 * slots * slots * 256,
    )
    return results[:2], names, results[2:]


def shards(
    tokens,
    block_tokens,
    ln1_gain,
    ln1_bias,
    w_qkv,
    b_qv,
    w_out,
    b_out,
    ln2_gain,
    ln2_bias,
    w_up,
    b_up,
    w_down,
    b_down,
    cotangent,
):
    images, capacity, width = tokens.shape
    assert images == 1
    layers = w_qkv.shape[0]
    size = HEAD_DIM
    ctx_count = lax.axis_size("ctx")
    ctx_place = lax.axis_index("ctx")
    joint_width = w_qkv.shape[2]
    heads = joint_width // (3 * size)
    assert heads == ctx_count
    attn_width = heads * size
    hidden_width = w_up.shape[2]
    weights = {"qkv": w_qkv, "out": w_out, "up": w_up, "down": w_down}
    sizes = (ctx_count, lax.axis_size("shard"))
    inside = sizes == (4, 2)
    gathered = {}
    if not inside:
        for name, value in weights.items():
            for layer in range(layers):
                gathered[name, layer] = gather_weight(value[layer])[0]
    source, stream = tokens[0], None
    saved = []
    for layer in range(layers):
        last = layer == layers - 1
        result, following, kept = forward_layer(
            source,
            stream,
            block_tokens,
            (b_out, ln2_gain, ln2_bias, b_down, ln1_gain, ln1_bias, b_up, b_qv),
            gathered,
            weights,
            Plan(layer, last, inside),
            last,
            size,
            sizes,
            1 + layer,
        )
        before = stream if layer else source
        first = source if layer else kept[8]
        saved.append((before, first) + tuple(kept[:8]))
        source, stream = following, result
    mixed = source

    done, packs = {}, {}
    source, stream, late = cotangent[0], None, None
    for layer in reversed(range(layers)):
        before, first, qkv, head_out, lse, heads_low, middle, second, hidden, slope = saved[layer]
        plan = BackPlan(layer, layers, inside)
        whole = {name: gathered[name, layer] for name in NAMES}
        near = [slope, whole["down"], whole["up"], middle, hidden, second, whole["out"]]
        near += [heads_low, qkv, head_out, lse, first, whole["qkv"], before]
        others = [packs[key] for key in sorted(packs)]
        (stream, source), names, rest = back_layer(
            source, stream, block_tokens, ln2_gain, ln1_gain, near, late, others, plan, size, sizes, 1 + layers + layer
        )
        rest = iter(rest)
        for name in names:
            done[name, layer] = next(rest)
        if plan.inside and not plan.final:
            late = next(rest)
        if plan.late:
            done["qkv", layer + 1] = next(rest)
        if plan.joined:
            totals = next(rest)
        else:
            packs[layer] = (next(rest), next(rest))
        if not inside:
            for name in NAMES:
                value = next(rest)
                done[name, layer] = scatter_weight(
                    lambda start, count, value=value: rows_of(value, start, count).astype(FULL),
                    width,
                )
    if not inside:
        split = total_over(("tp",), jnp.stack([packs[l][0] for l in range(layers)], axis=1))
        local = jnp.stack([packs[l][1] for l in range(layers)], axis=1)
        totals = total_over(("shard", "ctx"), jnp.concatenate([split, local[:2]]))
        totals = totals.reshape(10 * layers, -1)
    pairs = b_qv.shape[1]
    outs = gather_outputs(done, source, mixed, totals, layers, (hidden_width, pairs))
    g_qkv, g_out, g_up, g_down, mixed, token_grads = outs[:6]
    g_ln1_gain, g_ln1_bias, g_ln2_gain, g_ln2_bias, g_b_out, g_b_down, g_b_up, g_b_qv = outs[6:]
    return (
        mixed,
        token_grads,
        g_ln1_gain,
        g_ln1_bias,
        g_qkv,
        g_b_qv,
        g_out,
        g_b_out,
        g_ln2_gain,
        g_ln2_bias,
        g_up,
        g_b_up,
        g_down,
        g_b_down,
    )


def solution(mesh):
    split_rows = P(None, ("shard", "ctx"), "tp")
    split_tokens = P("shard", "ctx", None)
    return jax.shard_map(
        shards,
        mesh=mesh,
        in_specs=(
            split_tokens,
            P("shard", None),
            P(),
            P(),
            split_rows,
            P(None, "tp"),
            split_rows,
            P(),
            P(),
            P(),
            split_rows,
            P(None, "tp"),
            split_rows,
            P(),
            split_tokens,
        ),
        out_specs=(
            split_tokens,
            split_tokens,
            P(),
            P(),
            split_rows,
            P(None, "tp"),
            split_rows,
            P(),
            P(),
            P(),
            split_rows,
            P(None, "tp"),
            split_rows,
            P(),
        ),
        check_vma=False,
    )
```

```python
import functools
import math

import jax
import jax.numpy as jnp
from jax import lax
from jax.experimental import pallas as pl
from jax.experimental.pallas import tpu as pltpu
from jax.sharding import PartitionSpec as P

HEAD_DIM = 64
EPSILON = 1e-06
NEG_LARGE = -1e30
LOW = jnp.bfloat16
FULL = jnp.float32
PAD = 128
MESH = pl.DeviceIdType.MESH
VMEM = pltpu.VMEM
HBM = pltpu.HBM
SMEM = pltpu.SMEM


def bits_of(axis):
    size = lax.axis_size(axis)
    assert size & (size - 1) == 0
    return [1 << i for i in range(size.bit_length() - 1)]


def swap(value, axis, bit):
    size = lax.axis_size(axis)
    return lax.ppermute(value, axis, [(i, i ^ bit) for i in range(size)])


def side_of(axis, bit):
    return (lax.axis_index(axis) // bit) % 2


def rows_of(value, start, count, axis=0):
    return lax.dynamic_slice_in_dim(value, start, count, axis)


def halve(axis, bits, partial, total):
    offset, span, received = jnp.int32(0), total, []

    def summed(start, count):
        value = partial(start, count)
        for got, base in received:
            value = value + rows_of(got, start - base, count).astype(FULL)
        return value

    for bit in bits:
        half = span // 2
        side = side_of(axis, bit)
        got = swap(summed(offset + (1 - side) * half, half).astype(LOW), axis, bit)
        offset = offset + side * half
        received.append((got, offset))
        span = half
    return summed(offset, span)


def double(axis, bits, value):
    for bit in bits:
        got = swap(value, axis, bit)
        first = side_of(axis, bit) == 0
        value = jnp.concatenate(
            [jnp.where(first, value, got), jnp.where(first, got, value)], axis=0
        )
    return value


def total_over(axes, value):
    for axis in axes:
        for bit in bits_of(axis):
            value = value + swap(value, axis, bit)
    return value


def ring(value, by):
    count = lax.axis_size("ctx")
    return lax.ppermute(value, "ctx", [(i, (i + by) % count) for i in range(count)])


def gather_weight(piece):
    count = lax.axis_size("ctx")
    place = lax.axis_index("ctx")
    ways = lax.axis_size("shard")
    blocks = [piece] + [ring(piece, by) for by in range(1, count)]
    whole = jnp.zeros((ways * count,) + piece.shape, piece.dtype)
    me = lax.axis_index("shard")
    for by, block in enumerate(blocks):
        at = (place - by) % count
        held = [(jnp.int32(0), block)]
        for bit in bits_of("shard"):
            held = held + [(other ^ bit, swap(value, "shard", bit)) for other, value in held]
        for other, value in held:
            whole = lax.dynamic_update_index_in_dim(whole, value, (me ^ other) * count + at, 0)
    return whole.reshape((ways * count * piece.shape[0],) + piece.shape[1:]), blocks[-1]


def scatter_weight(partial, total):
    count = lax.axis_size("ctx")
    place = lax.axis_index("ctx")
    mine = halve("shard", bits_of("shard")[::-1], partial, total).astype(LOW)
    mine = mine.reshape((count, mine.shape[0] // count) + mine.shape[1:])
    value = lax.dynamic_index_in_dim(mine, place, 0, False).astype(FULL)
    for by in range(1, count):
        given = lax.dynamic_index_in_dim(mine, (place + by) % count, 0, False)
        value = value + ring(given, by).astype(FULL)
    return value


def dot(left, right, contract):
    return lax.dot_general(
        left, right, ((contract[0], contract[1]), ((), ())), preferred_element_type=FULL
    )


def turned(value):
    return value.astype(FULL).T.astype(LOW)


def normalize(rows, gain, shift):
    row_mean = jnp.mean(rows, axis=-1, keepdims=True)
    centred = rows - row_mean
    inverse = lax.rsqrt(jnp.mean(centred * centred, axis=-1, keepdims=True) + EPSILON)
    normed = centred * inverse
    return (normed * gain + shift, normed, inverse)


def normalize_back(grad_out, normed, inverse, gain):
    scaled = grad_out * gain
    mean_grad = jnp.mean(scaled, axis=-1, keepdims=True)
    mean_cross = jnp.mean(scaled * normed, axis=-1, keepdims=True)
    return inverse * (scaled - mean_grad - normed * mean_cross)


def gelu_pair(value):
    spread = 0.5 * (1.0 + lax.erf(value * (0.5**0.5)))
    slope = spread + value * jnp.exp(-0.5 * value * value) * (1.0 / math.sqrt(2.0 * math.pi))
    return (value * spread).astype(LOW), slope.astype(LOW)


class Mover:
    def __init__(self, sizes, send, recv, local):
        self.ctx_count, self.shard_count = sizes
        self.send, self.recv, self.local = send, recv, local
        self.copies, self.here = [], []
        self.arrived = set()
        self.landed = set()
        self.ctx = lax.axis_index("ctx")
        self.shard = lax.axis_index("shard")

    def go(self, source, target, **device):
        index = len(self.copies)
        assert index < self.send.shape[0]
        copy = pltpu.make_async_remote_copy(
            src_ref=source,
            dst_ref=target,
            send_sem=self.send.at[index],
            recv_sem=self.recv.at[index],
            device_id=device,
            device_id_type=MESH,
        )
        copy.start()
        self.copies.append(copy)
        return index

    def stay(self, source, target):
        index = len(self.here)
        assert index < self.local.shape[0]
        copy = pltpu.make_async_copy(source, target, self.local.at[index])
        copy.start()
        self.here.append(copy)
        return index

    def near(self, *indices):
        for index in indices:
            if index not in self.landed:
                self.landed.add(index)
                self.here[index].wait()

    def take(self, index):
        if index not in self.arrived:
            self.arrived.add(index)
            self.copies[index].wait_recv()

    def flip(self, bits):
        place = self.ctx
        if bits & 1:
            place = place + 1 - 2 * lax.rem(self.ctx, 2)
        if bits & 2:
            place = place + 2 - 4 * (self.ctx // 2)
        return place

    def on(self, by):
        return lax.rem(self.ctx + by, self.ctx_count)

    def back(self, by):
        return lax.rem(self.ctx + self.ctx_count - by, self.ctx_count)

    def settle(self):
        for index, copy in enumerate(self.copies):
            self.take(index)
            copy.wait_send()
        self.near(*range(len(self.here)))


class Gather:
    def __init__(self, mover, source, target):
        self.mover, self.source, self.target = mover, source, target
        self.over = []

    def start(self):
        self.start_line()
        self.start_over()

    def start_line(self):
        mover = self.mover
        mine, there = self.source, self.block(mover.ctx)
        self.far = mover.go(mine, there, ctx=mover.flip(2))
        self.close = mover.go(mine, there, ctx=mover.flip(1))

    def start_over(self):
        mover = self.mover
        mine, there = self.source, self.block(mover.ctx)
        self.over.append(mover.go(mine, there, shard=1 - mover.shard))
        self.own = mover.stay(mine, there)

    def block(self, ctx):
        mover = self.mover
        rows = self.source.shape[0]
        start = (mover.shard * mover.ctx_count + ctx) * rows
        return self.target.at[pl.ds(pl.multiple_of(start, rows), rows)]

    def pass_on(self, stage):
        mover = self.mover
        if stage == 1:
            mover.take(self.far)
            rows = self.block(mover.flip(2))
            self.passed = mover.go(rows, rows, ctx=mover.flip(1))
        elif stage == 2:
            mover.take(self.close)
            rows = self.block(mover.flip(1))
        else:
            mover.take(self.passed)
            rows = self.block(mover.flip(3))
        self.over.append(mover.go(rows, rows, shard=1 - mover.shard))

    def have(self):
        for copy in self.over:
            self.mover.take(copy)
        self.mover.near(self.own)


class Reduce:
    def __init__(self, mover, buffers, out, lhs, rhs):
        self.mover, self.out, self.lhs, self.rhs = mover, out, lhs, rhs
        self.give, self.got, self.mid, self.line = buffers
        self.half = self.give.shape[0]
        self.block = self.half // mover.ctx_count

    def compute(self, target, shard):
        chunk = min(256, self.half)

        def step(i, carry):
            at = pl.ds(pl.multiple_of(shard * self.half + i * chunk, chunk), chunk)
            here = pl.ds(pl.multiple_of(i * chunk, chunk), chunk)
            target[here, :] = dot(self.lhs[:, at], self.rhs[...], ((0,), (0,))).astype(LOW)
            return carry

        lax.fori_loop(0, self.half // chunk, step, 0)

    def begin_blocks(self):
        mover = self.mover
        self.blocks = {}
        for bits in (3, 2, 1, 0):
            ctx = mover.flip(bits)
            at = pl.ds(pl.multiple_of(ctx * self.block, self.block), self.block)
            start = pl.multiple_of((1 - mover.shard) * self.half + ctx * self.block, self.block)
            lhs = self.lhs[:, pl.ds(start, self.block)]
            self.give[at, :] = dot(lhs, self.rhs[...], ((0,), (0,))).astype(LOW)
            self.blocks[bits] = mover.go(
                self.give.at[at], self.got.at[at], shard=1 - mover.shard
            )

    def own(self):
        self.compute(self.mid, self.mover.shard)

    def fold_blocks(self, *which):
        mover = self.mover
        for bits in which:
            mover.take(self.blocks[bits])
            ctx = mover.flip(bits)
            at = pl.ds(pl.multiple_of(ctx * self.block, self.block), self.block)
            self.mid[at, :] = (
                self.mid[at, :].astype(FULL) + self.got[at, :].astype(FULL)
            ).astype(LOW)

    def rows(self, ctx):
        return self.mid.at[pl.ds(pl.multiple_of(ctx * self.block, self.block), self.block)]

    def send_first(self):
        mover = self.mover
        self.first = mover.go(self.rows(mover.flip(3)), self.line.at[1], ctx=mover.flip(1))

    def send_second(self):
        mover = self.mover
        self.second = mover.go(self.rows(mover.flip(1)), self.line.at[0], ctx=mover.flip(1))

    def send_third(self):
        mover = self.mover
        mover.take(self.first)
        rows = self.rows(mover.flip(2))
        rows[...] = (rows[...].astype(FULL) + self.line[1].astype(FULL)).astype(LOW)
        self.third = mover.go(rows, self.line.at[2], ctx=mover.flip(2))

    def done(self):
        self.mover.take(self.second)
        self.mover.take(self.third)
        value = self.rows(self.mover.ctx)[...].astype(FULL)
        self.out[...] = value + self.line[0].astype(FULL) + self.line[2].astype(FULL)


def reduce_buffers(half, width, count):
    return [
        VMEM((half, width), LOW),
        VMEM((half, width), LOW),
        VMEM((half, width), LOW),
        VMEM((count - 1, half // count, width), LOW),
    ]


def greet(mover, shard):
    barrier = pltpu.get_barrier_semaphore()
    peers = [dict(ctx=mover.on(by)) for by in range(1, mover.ctx_count)]
    peers += [dict(tp=peer) for peer in tp_peers()]
    if shard:
        peers.append(dict(shard=1 - mover.shard))
    for peer in peers:
        pl.semaphore_signal(barrier, inc=1, device_id=peer, device_id_type=MESH)
    pl.semaphore_wait(barrier, len(peers))


def tp_peers():
    place = lax.axis_index("tp")
    core, far = lax.rem(place, 2), place // 2
    return place + 1 - 2 * core, place + 2 - 4 * far


def run(kernel, name, ident, inputs, outputs, scratch, remote, local, sizes, vmem, flops):
    n_in, n_out, n_scratch = len(inputs), len(outputs), len(scratch)

    def body(*refs):
        ins, outs = refs[:n_in], refs[n_in : n_in + n_out]
        work = refs[n_in + n_out :]
        mover = Mover(sizes, *work[n_scratch:])
        kernel(mover, ins, outs, work[:n_scratch])

    return pl.pallas_call(
        body,
        in_specs=[pl.BlockSpec(memory_space=space) for _, space in inputs],
        out_specs=[pl.BlockSpec(memory_space=space) for _, _, space in outputs],
        out_shape=[jax.ShapeDtypeStruct(shape, dtype) for shape, dtype, _ in outputs],
        scratch_shapes=list(scratch)
        + [
            pltpu.SemaphoreType.DMA((remote,)),
            pltpu.SemaphoreType.DMA((remote,)),
            pltpu.SemaphoreType.DMA((local,)),
        ],
        compiler_params=pltpu.CompilerParams(
            collective_id=ident, has_side_effects=True, vmem_limit_bytes=vmem * 2**20
        ),
        cost_estimate=pl.CostEstimate(flops=flops, bytes_accessed=2**24, transcendentals=0),
        name=name,
    )(*[value for value, _ in inputs])


def order_of(block, count):
    return (block + count - 1) % count


def tiles_of(count, capacity, tile):
    ends = [-(-(p + 1) * capacity // tile) for p in range(count)]
    return list(zip([0] + ends[:-1], ends))


def parts_of(capacity):
    middle = capacity // 2 // PAD * PAD
    return [(0, middle), (middle, capacity)] if middle else [(0, capacity)]


def tile_at(t, tile):
    return pl.ds(pl.multiple_of(t * tile, tile), tile)


def turned_product(left, right, bias, target):
    def step(i, carry):
        at = pl.ds(pl.multiple_of(i * PAD, PAD), PAD)
        value = jnp.dot(left[at, :], right[...], preferred_element_type=FULL)
        if bias is not None:
            value = value + bias[0:1, :]
        target[:, at] = turned(value.astype(LOW))
        return carry

    lax.fori_loop(0, left.shape[0] // PAD, step, 0)


def head_rows(ref, head, width):
    return ref.at[pl.ds(pl.multiple_of(head * width, 16), width)]


def attend_part(size, tile, mover, joint, bias, heads, qkv, o_ref, lse, work, after_send, begun, between):
    k_ref, q_ref, v_ref, low_ref, score_ref, top_ref = work
    count, width, capacity = qkv.shape
    slots = count * capacity
    sent = [None] + [
        mover.go(head_rows(joint, mover.on(by), width), qkv.at[by], ctx=mover.on(by))
        for by in range(1, count)
    ]
    after_send()
    qkv[0] = head_rows(joint, mover.ctx, width)[...]
    q_ref[size:PAD, :] = jnp.concatenate(
        [jnp.ones((16, slots), LOW), jnp.zeros((PAD - size - 16, slots), LOW)], axis=0
    )

    v_ref[size : size + 16, :] = jnp.ones((16, slots), LOW)

    def prepare(r):
        here = slice(r * capacity, (r + 1) * capacity)
        p = order_of(r, count)
        q_ref[0:size, p * capacity : (p + 1) * capacity] = (
            qkv[r, 0:size, :] * (size**-0.5)
        ).astype(LOW)
        v_ref[0:size, here] = qkv[r, 2 * size : 3 * size, :]
        keys = jnp.concatenate(
            [qkv[r, size : 2 * size, :], bias[:, here], jnp.zeros((PAD - size - 16, capacity), LOW)],
            axis=0,
        )
        k_ref[here, :] = turned(keys)

    prepare(0)
    for by in range(1, count):
        mover.take(sent[by])
        prepare(by)

    begun()
    last = slots // tile - 1
    assert last % 2 == 1

    def phase(t, now, following, then):
        at, ahead = tile_at(t, tile), tile_at(following, tile)
        top = top_ref[now, 0:1, :]
        summed = jnp.zeros((size + 16, tile), FULL)
        new_top = jnp.full((1, tile), NEG_LARGE, FULL)
        for r in range(count):
            here = slice(r * capacity, (r + 1) * capacity)
            scores = jnp.dot(k_ref[here, :], q_ref[:, ahead], preferred_element_type=FULL)
            score_ref[then, here, :] = scores
            new_top = jnp.maximum(new_top, jnp.max(scores, axis=0, keepdims=True))
            weights = jnp.exp(score_ref[now, here, :] - top)
            summed = summed + jnp.dot(
                v_ref[:, here], weights.astype(LOW), preferred_element_type=FULL
            )
        top_ref[then] = jnp.broadcast_to(new_top, (8, tile))
        total = summed[size : size + 1]
        out = summed[0:size] / total
        o_ref[:, at] = out
        low_ref[:, at] = out.astype(LOW)
        lse[:, at] = jnp.broadcast_to(top + jnp.log(total), (8, tile))

    def step(i, carry):
        phase(2 * i, 0, 2 * i + 1, 1)
        phase(2 * i + 1, 1, jnp.minimum(2 * i + 2, last), 0)
        return carry

    scores = jnp.dot(k_ref[...], q_ref[:, 0:tile], preferred_element_type=FULL)
    score_ref[0] = scores
    top_ref[0] = jnp.broadcast_to(jnp.max(scores, axis=0, keepdims=True), (8, tile))
    arriving = []
    for p, (low, high) in enumerate(tiles_of(count, capacity, 2 * tile)):
        lax.fori_loop(low, high, step, 0)
        done = low_ref.at[:, p * capacity : (p + 1) * capacity]
        if p < count - 1:
            there = head_rows(heads, mover.ctx, size)
            arriving.append(mover.go(done, there, ctx=mover.back(p + 1)))
        else:
            head_rows(heads, mover.ctx, size)[...] = low_ref[:, p * capacity : (p + 1) * capacity]
        between(p + 1)
    for copy in arriving:
        mover.take(copy)


def below(row, ones):
    width = row.shape[1]
    high = row.astype(LOW).astype(FULL)
    middle = (row - high).astype(LOW).astype(FULL)
    low = row - high - middle
    lead = jnp.full((1, width), 1.0 if ones else 0.0, FULL)
    rest = jnp.zeros((PAD // 2 - 4, width), FULL)
    return jnp.concatenate([lead, high, middle, low, rest], axis=0).astype(LOW)


def attend_back_part(size, tile, mover, parts, bias, qkv, o_ref, lse, grads, work, ready, waiting, begun, between):
    k_ref, v_ref, q_ref, do_ref, nat_ref, dq_ref, dk_ref, dv_ref, got, back, score_ref, grad_ref = work
    count, width, capacity = qkv.shape
    slots = count * capacity
    sent = [None] + [
        mover.go(head_rows(parts, mover.on(by), size), got.at[by], ctx=mover.on(by))
        for by in range(1, count)
    ]
    got[0] = head_rows(parts, mover.ctx, size)[...]
    waiting()
    ready()
    q_ref[size:PAD, :] = below(lse[0:1, :], True)
    dq_ref[...] = jnp.zeros_like(dq_ref)
    off = (lax.broadcasted_iota(jnp.int32, (16, capacity), 0) + 2) // 3
    taken = jnp.where(off == 1, -1.0, 0.0).astype(LOW)
    pad = jnp.zeros((PAD - size - 16, capacity), LOW)
    for r in range(count):
        here = slice(r * capacity, (r + 1) * capacity)
        k_ref[here, :] = turned(
            jnp.concatenate([qkv[r, size : 2 * size, :], bias[:, here] + taken, pad], axis=0)
        )
        v_ref[here, :] = turned(
            jnp.concatenate([qkv[r, 2 * size : 3 * size, :], taken, pad], axis=0)
        )
    for r in range(count):
        if r:
            mover.take(sent[r])
        p = order_of(r, count)
        at = slice(p * capacity, (p + 1) * capacity)
        scaled = (qkv[r, 0:size, :] * (size**-0.5)).astype(LOW)
        dout = got[r]
        q_ref[0:size, at] = scaled
        do_ref[0:size, at] = dout
        nat_ref[at, :] = turned(jnp.concatenate([scaled, dout], axis=0))
        delta = jnp.sum(dout.astype(FULL) * o_ref[:, at], axis=0, keepdims=True)
        do_ref[size:PAD, at] = below(delta, False)

    begun()
    last = slots // tile - 1
    assert last % 2 == 1
    tiles = tiles_of(count, capacity, 2 * tile)
    arriving = []
    mine = head_rows(grads, mover.ctx, width)
    for turn, r in enumerate(list(range(1, count)) + [0]):
        here = slice(r * capacity, (r + 1) * capacity)
        dk_ref[...] = jnp.zeros_like(dk_ref)
        dv_ref[...] = jnp.zeros_like(dv_ref)

        def ready_scores(t, then, low, high, r=r):
            ahead = tile_at(t, tile)
            rows = slice(r * capacity + low, r * capacity + high)
            score_ref[then, low:high, :] = jnp.dot(
                k_ref[rows, :], q_ref[:, ahead], preferred_element_type=FULL
            )
            grad_ref[then, low:high, :] = jnp.dot(
                v_ref[rows, :], do_ref[:, ahead], preferred_element_type=FULL
            )

        def phase(t, now, following, then, r=r):
            at = tile_at(t, tile)
            query_grad = jnp.zeros((size, tile), FULL)
            for low, high in parts_of(capacity):
                ready_scores(following, then, low, high)
                chance = jnp.exp(score_ref[now, low:high, :])
                score_grad = (chance * grad_ref[now, low:high, :]).astype(LOW)
                query_grad = query_grad + jnp.dot(
                    qkv[r, size : 2 * size, low:high], score_grad, preferred_element_type=FULL
                )
                dk_ref[low:high, :] += jnp.dot(
                    score_grad, nat_ref[at, :], preferred_element_type=FULL
                )
                dv_ref[low:high, :] += jnp.dot(
                    chance.astype(LOW), nat_ref[at, :], preferred_element_type=FULL
                )
            dq_ref[:, at] += query_grad

        def step(i, carry, phase=phase):
            phase(2 * i, 0, 2 * i + 1, 1)
            phase(2 * i + 1, 1, jnp.minimum(2 * i + 2, last), 0)
            return carry

        ready_scores(0, 0, 0, capacity)
        if r:
            lax.fori_loop(0, tiles[-1][1], step, 0)
        else:
            for p, (low, high) in enumerate(tiles):
                lax.fori_loop(low, high, step, 0)
                at = slice(p * capacity, (p + 1) * capacity)
                value = (dq_ref[:, at] * (size**-0.5)).astype(LOW)
                if p < count - 1:
                    back[p + 1, 0:size, :] = value
                    arriving.append(
                        mover.go(
                            back.at[p + 1, 0:size], mine.at[0:size], ctx=mover.back(p + 1)
                        )
                    )
                else:
                    mine[0:size, :] = value
        keys = dk_ref[...].T[0:size].astype(LOW)
        values = dv_ref[...].T[size : 2 * size].astype(LOW)
        if r:
            back[r, size : 2 * size, :] = keys
            back[r, 2 * size : 3 * size, :] = values
            arriving.append(
                mover.go(
                    back.at[r, size : 3 * size], mine.at[size : 3 * size], ctx=mover.back(r)
                )
            )
        else:
            mine[size : 2 * size, :] = keys
            mine[2 * size : 3 * size, :] = values
        between(turn)
    for copy in arriving:
        mover.take(copy)


def attend_back_buffers(size, count, capacity, tile):
    slots = count * capacity
    return [
        VMEM((slots, PAD), LOW),
        VMEM((slots, PAD), LOW),
        VMEM((PAD, slots), LOW),
        VMEM((PAD, slots), LOW),
        VMEM((slots, PAD), LOW),
        VMEM((size, slots), FULL),
        VMEM((capacity, PAD), FULL),
        VMEM((capacity, PAD), FULL),
        VMEM((count, size, capacity), LOW),
        VMEM((count, 3 * size, capacity), LOW),
        VMEM((2, capacity, tile), FULL),
        VMEM((2, capacity, tile), FULL),
    ]


class Round:
    def __init__(self, mover, rows, full, buffers):
        place = lax.axis_index("tp")
        core, far = lax.rem(place, 2), place // 2
        self.mover, self.full = mover, full
        self.give, self.ra, self.passing, self.rb, self.keep = buffers
        self.span = rows // 4
        self.half = self.span // 2
        self.mate, self.far = tp_peers()

        def quarter(c, f):
            return (c * 2 + f) * self.span

        self.own, self.other = quarter(core, far), quarter(core, 1 - far)
        self.mate_own, self.mate_other = quarter(1 - core, far), quarter(1 - core, 1 - far)

    def rows(self, start, count=None):
        return pl.ds(pl.multiple_of(start, 16), count or self.span)

    def hand(self, slot, value):
        self.give[slot] = value.astype(LOW)
        return self.mover.go(self.give.at[slot], self.ra.at[slot], tp=self.mate)

    def onward(self, value, index):
        self.mover.take(index)
        self.passing[...] = (value + self.ra[1].astype(FULL)).astype(LOW)
        return [
            self.mover.go(self.passing.at[at], self.rb.at[at], tp=self.far)
            for at in (pl.ds(0, self.half), pl.ds(self.half, self.half))
        ]

    def close(self, far_copies, index, finish, halfway=None):
        self.mover.take(index)
        self.keep[...] += self.ra[0].astype(FULL)
        self.to_far, self.to_mate = [], []
        for c in range(2):
            at = pl.ds(c * self.half, self.half)
            self.mover.take(far_copies[c])
            low = finish(at, self.keep[at] + self.rb[at].astype(FULL))
            mine = self.full.at[self.rows(self.own + c * self.half, self.half)]
            mine[...] = low
            self.to_far.append(self.mover.go(mine, mine, tp=self.far))
            self.to_mate.append(self.mover.go(mine, mine, tp=self.mate))
            if halfway and c == 0:
                halfway()

    def eager(self, make, finish, meanwhile=None, halfway=None):
        first = self.hand(1, make(self.mate_other))
        copies = self.onward(make(self.other), first)
        second = self.hand(0, make(self.mate_own))
        self.keep[...] = make(self.own)
        if meanwhile:
            meanwhile()
        self.close(copies, second, finish, halfway)

    def after(self, before, make, finish, meanwhile, between):
        before.have_mate_own()
        second = self.hand(0, make(self.mate_own))
        self.keep[...] = make(self.own)
        before.have_other()
        between()
        value = make(self.other)
        before.have_mate_other()
        first = self.hand(1, make(self.mate_other))
        copies = self.onward(value, first)
        meanwhile()
        self.close(copies, second, finish)

    def have_mate_own(self):
        for copy in self.to_mate:
            self.mover.take(copy)

    def have_other(self):
        self.passed = []
        for c in range(2):
            self.mover.take(self.to_far[c])
            rows = self.full.at[self.rows(self.other + c * self.half, self.half)]
            self.passed.append(self.mover.go(rows, rows, tp=self.mate))

    def have_mate_other(self):
        for copy in self.passed:
            self.mover.take(copy)

    def have(self):
        self.have_mate_own()
        self.have_other()
        self.have_mate_other()


ROUND_COPIES = 10


def round_buffers(rows, width):
    span = rows // 4
    return [
        VMEM((2, span, width), LOW),
        VMEM((2, span, width), LOW),
        VMEM((span, width), LOW),
        VMEM((span, width), LOW),
        VMEM((span, width), FULL),
    ]


NAMES = ("qkv", "out", "up", "down")


def layer_kernel(plan, last, size, tile, mover, ins, outs, work):
    ins, outs, work = iter(ins), iter(outs), iter(work)
    source = next(ins)
    x_ref = None if plan.entry else next(ins)
    live_ref = next(ins)
    far_params = [next(ins) for _ in range(8)]
    stream, following = next(outs), next(outs)
    far_qkv, far_o, far_lse, far_heads, far_middle, far_second, far_hidden, far_slope = [
        next(outs) for _ in range(8)
    ]
    far_first = next(outs) if plan.entry else None
    joint, nat, heads, qkv, o_ref, lse, middle, second, hidden, slope = [
        next(work) for _ in range(10)
    ]
    first = next(work) if plan.entry else source
    attend_work = [next(work) for _ in range(6)]
    one_work, two_work = [next(work) for _ in range(5)], [next(work) for _ in range(5)]
    rows = source.shape[0]
    bias, qkv_bias = next(work), next(work)
    params = [next(work) for _ in range(8)]
    whole = {name: next(work) for name in NAMES}
    gathers, loads = {}, {}
    for name in plan.held:
        loads[name] = (next(ins), whole[name])
    for name in plan.own:
        gathers[name, 0] = Gather(mover, next(ins).at[plan.layer], whole[name])
    kept_ahead = {name: next(outs) for name in plan.ahead}
    for name in plan.ahead:
        gathers[name, 1] = Gather(mover, next(ins).at[plan.layer + 1], next(work))
    kept = {name: next(outs) for name in plan.own}

    greet(mover, bool(gathers))
    if plan.entry:
        gathers_first = [key for key in [("qkv", 0)] if key in gathers]
        for key in gathers_first:
            gathers[key].start()
    param_loads = [mover.stay(there, here) for there, here in zip(far_params, params)]
    waiting_loads = dict(loads)
    loads = {}

    def load(names):
        for name in names:
            if name in waiting_loads and name not in loads:
                loads[name] = mover.stay(*waiting_loads[name])

    load(["qkv"])

    def have(name):
        if name in waiting_loads:
            mover.near(loads[name])
            load(NAMES)
        else:
            gathers[name, 0].have()
            mover.stay(whole[name], kept[name])
        return whole[name]

    def begin(keys):
        for key in keys:
            if key in gathers:
                gathers[key].start_line()

    def begin_over(keys):
        for key in keys:
            if key in gathers:
                gathers[key].start_over()

    def pass_on(keys, stage):
        for key in keys:
            if key in gathers:
                gathers[key].pass_on(stage)

    def pass_all(keys):
        for stage in (1, 2, 3):
            pass_on(keys, stage)

    mover.near(*param_loads)
    layer, after = plan.layer, min(plan.layer + 1, params[0].shape[0] - 1)

    def row(index, layer=layer):
        return params[index][...].astype(FULL)[layer : layer + 1]

    b_out, gain2, shift2, b_down, b_up = row(0), row(1), row(2), row(3), row(6)
    gain1, shift1, gain0, shift0 = row(4, after), row(5, after), row(4), row(5)
    qkv_bias[...] = joint_bias(row(7), size, joint.shape[0])
    key_bias(mover, live_ref, bias)
    ahead = [("qkv", 1), ("out", 1), ("up", 1)]
    one = Round(mover, rows, second, one_work)
    two = Round(mover, rows, following, two_work)
    if plan.entry:
        chunk = rows // 5 if rows % 80 == 0 else rows

        def norm_step(i, carry):
            at = pl.ds(pl.multiple_of(i * chunk, 16), chunk)
            value = normalize(source[at, :].astype(FULL), gain0, shift0)[0]
            first[at, :] = value.astype(LOW)
            return carry

        lax.fori_loop(0, rows // chunk, norm_step, 0)
        mover.stay(first, far_first)
        pass_all([("qkv", 0)])
        begin([("out", 0)])
        begin_over([("out", 0), ("up", 0), ("down", 0)] + ahead)
        turned_product(first, have("qkv"), qkv_bias, joint)
    else:
        turned_product(first, have("qkv"), qkv_bias, joint)

    def after_send():
        if plan.entry:
            begin([("up", 0)])
            pass_all([("out", 0)])
        else:
            for name in plan.own:
                gathers[name, 0].start_over()

    def begun():
        begin([("down", 0)])

    def between(p):
        if plan.entry and p < 4:
            pass_on([("up", 0)], p)
        if p > 2:
            pass_on([("down", 0)], p - 2)
        if p == 4:
            if not plan.entry:
                begin_over(ahead)
            begin(ahead)

    attend_part(
        size, tile, mover, joint, bias, heads, qkv, o_ref, lse, attend_work, after_send, begun, between
    )
    nat[...] = turned(heads[...])
    w_out = have("out")

    def out_part(start):
        return dot(nat[one.rows(start), :], w_out[...], ((1,), (1,)))

    def to_second(at, value):
        if plan.entry:
            before = source[one.rows(one.own + at.start, at.size), :].astype(FULL)
        else:
            before = x_ref[at]
        value = before + value + b_out
        middle[at] = value
        return normalize(value, gain2, shift2)[0].astype(LOW)

    def meanwhile():
        mover.stay(qkv, far_qkv)
        mover.stay(o_ref, far_o)
        mover.stay(lse, far_lse)
        mover.stay(nat, far_heads)
        pass_on([("down", 0)], 3)

    one.eager(out_part, to_second, meanwhile, lambda: pass_on(ahead[:2], 1))
    pass_on(ahead[:2], 2)
    w_up, w_down = have("up"), have("down")

    def mlp_part(start):
        at = two.rows(start)
        pre = jnp.dot(second[at, :], w_up[...], preferred_element_type=FULL) + b_up
        low, low_slope = gelu_pair(pre)
        hidden[at, :] = low
        slope[at, :] = low_slope
        return dot(low, w_down[...], ((1,), (1,)))

    def to_following(at, value):
        value = middle[at] + value + b_down
        stream[at] = value
        if last:
            return live_rows(value, two.own + at.start, live_ref[0, mover.ctx]).astype(LOW)
        return normalize(value, gain1, shift1)[0].astype(LOW)

    def meanwhile():
        mover.stay(middle, far_middle)
        mover.stay(second, far_second)
        mover.stay(hidden, far_hidden)
        mover.stay(slope, far_slope)
        pass_on(ahead[2:], 3)

    def between_parts():
        pass_on(ahead[:2], 3)
        pass_on(ahead[2:], 1)
        pass_on(ahead[2:], 2)

    two.after(one, mlp_part, to_following, meanwhile, between_parts)
    two.have()
    for name in plan.ahead:
        gathers[name, 1].have()
        mover.stay(gathers[name, 1].target, kept_ahead[name])
    mover.settle()


class Plan:
    def __init__(self, layer, last, inside):
        self.layer, self.entry = layer, layer == 0
        self.own = (NAMES if layer == 0 else ("down",)) if inside else ()
        self.ahead = ("qkv", "out", "up") if inside and not last else ()
        self.held = tuple(name for name in NAMES if name not in self.own)


def forward_layer(source, x, live, params, gathered, weights, plan, last, size, sizes, ident):
    rows, width = source.shape
    count = sizes[0]
    joint, hidden = weights["qkv"].shape[2], weights["up"].shape[2]
    heads = joint // (3 * size)
    attn, slots, span = heads * size, count * rows, rows // 4
    tile = 256 if slots % 256 == 0 else PAD
    columns = {"qkv": joint, "out": attn, "up": hidden, "down": hidden}
    inputs = [(source, VMEM)] + ([] if plan.entry else [(x, VMEM)])
    inputs += [(live, SMEM)] + [(value, HBM) for value in params]
    inputs += [(gathered[name, plan.layer], HBM) for name in plan.held]
    inputs += [(weights[name], HBM) for name in plan.own + plan.ahead]
    saved = [
        ((count, 3 * size, rows), LOW),
        ((size, slots), FULL),
        ((8, slots), FULL),
        ((rows, attn), LOW),
        ((span, width), FULL),
        ((rows, width), LOW),
        ((rows, hidden), LOW),
        ((rows, hidden), LOW),
    ]
    outputs = [((span, width), FULL, VMEM), ((rows, width), LOW, VMEM)]
    outputs += [(shape, dtype, HBM) for shape, dtype in saved]
    if plan.entry:
        outputs.append(((rows, width), LOW, HBM))
    outputs += [((width, columns[name]), LOW, HBM) for name in plan.ahead + plan.own]
    qkv_shape, o_shape, lse_shape, heads_shape = saved[:4]
    scratch = [VMEM((joint, rows), LOW), VMEM((rows, attn), LOW), VMEM((attn, rows), LOW)]
    scratch += [VMEM(*pair) for pair in saved[:3] + saved[4:]]
    if plan.entry:
        scratch.append(VMEM((rows, width), LOW))
    scratch += [
        VMEM((slots, PAD), LOW),
        VMEM((PAD, slots), LOW),
        VMEM((size + 16, slots), LOW),
        VMEM((size, slots), LOW),
        VMEM((2, slots, tile), FULL),
        VMEM((2, 8, tile), FULL),
    ]
    scratch += round_buffers(rows, width) + round_buffers(rows, width)
    scratch += [VMEM((16, slots), LOW), VMEM((16, joint), FULL)]
    scratch += [VMEM(value.shape, value.dtype) for value in params]
    scratch += [VMEM((width, columns[name]), LOW) for name in NAMES + plan.ahead]
    results = run(
        functools.partial(layer_kernel, plan, last, size, tile),
        "forward_layer",
        ident,
        inputs,
        outputs,
        scratch,
        2 * (count - 1) + 2 * ROUND_COPIES + 2 * count * len(plan.own + plan.ahead),
        10 + 2 * len(plan.own + plan.ahead) + len(plan.held) + len(params),
        sizes,
        58,
        2 * rows * width * (2 * hidden + attn + joint) + 4 * slots * slots * 256,
    )
    stream, following = results[:2]
    kept = results[2 : 11 if plan.entry else 10]
    for name, value in zip(plan.ahead, results[2 + len(kept) :]):
        gathered[name, plan.layer + 1] = value
    for name, value in zip(plan.own, results[2 + len(kept) + len(plan.ahead) :]):
        gathered[name, plan.layer] = value
    return stream, following, kept


class SmallSums:
    def __init__(self, mover, rows, held, got):
        self.mover, self.rows, self.held, self.got = mover, rows, held, got
        self.stage = 0
        mate, far = tp_peers()
        self.peers = [
            dict(tp=mate),
            dict(tp=far),
            dict(shard=1 - mover.shard),
            dict(ctx=mover.flip(2)),
            dict(ctx=mover.flip(1)),
        ]

    def part(self, stage):
        return pl.ds(0, self.rows if stage < 2 else self.held.shape[1])

    def step(self):
        stage, mover = self.stage, self.mover
        if stage:
            mover.take(self.copy)
            at = self.part(stage - 1)
            self.held[stage] = self.held[stage - 1]
            self.held[stage, at, :] = self.held[stage - 1, at, :] + self.got[stage - 1, at, :]
        if stage < len(self.peers):
            at = self.part(stage)
            self.copy = mover.go(
                self.held.at[stage, at], self.got.at[stage, at], **self.peers[stage]
            )
        self.stage = stage + 1

    def value(self):
        return self.held[len(self.peers)]


def key_bias(mover, live_ref, bias):
    capacity = bias.shape[1] // mover.ctx_count
    row = lax.broadcasted_iota(jnp.int32, (16, capacity), 0)
    slot = lax.broadcasted_iota(jnp.int32, (16, capacity), 1)
    for r in range(mover.ctx_count):
        live = live_ref[0, mover.back(r)]
        value = jnp.where((row == 0) & (slot >= live), NEG_LARGE, 0.0)
        bias[:, r * capacity : (r + 1) * capacity] = value.astype(LOW)


def pair_columns(rows, width, size, turn):
    shape = (width, rows) if turn else (rows, width)
    given = lax.broadcasted_iota(jnp.int32, shape, 1 if turn else 0)
    column = lax.broadcasted_iota(jnp.int32, shape, 0 if turn else 1)
    head, within = column // (3 * size), column % (3 * size)
    wanted = head * (2 * size) + jnp.where(within < size, within, within - size)
    key = (within >= size) & (within < 2 * size)
    return jnp.where((given == wanted) & ~key, 1.0, 0.0).astype(LOW)


def joint_bias(pair, size, width):
    rows = pair.shape[1]
    spread = jnp.broadcast_to(pair, (16, rows)).astype(LOW)
    return jnp.dot(spread, pair_columns(rows, width, size, False), preferred_element_type=FULL)


def live_rows(value, start, live):
    row = start + lax.broadcasted_iota(jnp.int32, value.shape, 0)
    return jnp.where(row < live, value, 0.0)


def sums_into(sums, first, at, values):
    for index, value in enumerate(values):
        row = first + index
        added = jnp.sum(value, axis=0, keepdims=True)
        width = added.shape[1]
        sums[row : row + 1, 0:width] = (
            added if at.start == 0 else sums[row : row + 1, 0:width] + added
        )


def back_kernel(plan, size, tile, mover, ins, outs, work):
    ins, outs, work = iter(ins), iter(outs), iter(work)
    source = next(ins)
    x_ref = None if plan.last else next(ins)
    live_ref, far_gain2, far_gain1 = [next(ins) for _ in range(3)]
    far = [next(ins) for _ in range(14)]
    late_far = next(ins) if plan.late else None
    others = [(next(ins), next(ins)) for _ in range(plan.others)]
    stream, following = next(outs), next(outs)
    grad_outs = {name: next(outs) for name in NAMES if plan.inside and (name != "qkv" or plan.final)}
    mid_out = next(outs) if plan.inside and not plan.final else None
    late_out = next(outs) if plan.late else None
    split = local = totals = None
    if plan.joined:
        totals = next(outs)
    else:
        split, local = next(outs), next(outs)
    wholes = {} if plan.inside else {name: next(outs) for name in NAMES}
    near = [next(work) for _ in range(14)]
    slope, w_down, w_up, middle, hidden, second, w_out, heads, qkv, o_ref, lse, first, w_qkv, before = near
    grad = next(work) if plan.last else source
    pre_grad, attn_grad, parts, grads, nat = [next(work) for _ in range(5)]
    attend_work = [next(work) for _ in range(12)]
    one_work, two_work = [next(work) for _ in range(5)], [next(work) for _ in range(5)]
    rows, width = source.shape
    reduces = {}
    if plan.inside:
        pairs = {
            "down": (grad, hidden),
            "up": (second, pre_grad),
            "out": (attn_grad, heads),
            "qkv": (first, nat),
        }
        for name in ("down", "up", "out", "qkv"):
            buffers = [next(work) for _ in range(4)]
            reduces[name] = Reduce(mover, buffers, grad_outs.get(name), *pairs[name])
    late = None
    if plan.late:
        late_mid, late_line = next(work), next(work)
        late = Reduce(mover, (late_mid, None, late_mid, late_line), late_out, None, None)
    bias, gain2_ref, gain1_ref = [next(work) for _ in range(3)]
    if plan.joined:
        split, local = next(work), next(work)
        early_held, early_got, late_held, late_got = [next(work) for _ in range(4)]
        tops = 8 * (plan.others + 1)
        early = SmallSums(mover, tops, early_held, early_got)
        final = SmallSums(mover, 8, late_held, late_got)
        everything = [(split, local)] + others

    greet(mover, plan.inside)
    gain_loads = [mover.stay(far_gain2, gain2_ref), mover.stay(far_gain1, gain1_ref)]
    one = Round(mover, rows, attn_grad, one_work)
    two = Round(mover, rows, following, two_work)
    if plan.final:
        far[13] = far[13].at[two.rows(two.own)]
    load = [mover.stay(there, here) for there, here in zip(far[:3], near[:3])]
    if late:
        mover.near(mover.stay(late_far, late_mid))
        late.send_first()
        late.send_second()
    if plan.last:
        chunk = rows // 5 if rows % 80 == 0 else rows

        def mask_step(i, carry):
            at = pl.ds(pl.multiple_of(i * chunk, 16), chunk)
            value = source[at, :].astype(FULL)
            grad[at, :] = live_rows(value, i * chunk, live_ref[0, mover.ctx]).astype(LOW)
            return carry

        lax.fori_loop(0, rows // chunk, mask_step, 0)
    key_bias(mover, live_ref, bias)
    mover.near(*gain_loads)
    gain2, gain1 = [
        ref[...].astype(FULL)[plan.layer : plan.layer + 1] for ref in (gain2_ref, gain1_ref)
    ]
    split[...] = jnp.zeros_like(split)
    local[...] = jnp.zeros_like(local)
    split[5:6, 0:width] = jnp.sum(
        grad[one.rows(one.own), :].astype(FULL), axis=0, keepdims=True
    )
    mover.near(*load[:3])
    load += [mover.stay(there, here) for there, here in zip(far[3:], near[3:])]
    hidden_width = slope.shape[1]

    def mlp_part(start):
        at = one.rows(start)
        pre = jnp.dot(grad[at, :], w_down[...], preferred_element_type=FULL)
        low = (pre * slope[at, :].astype(FULL)).astype(LOW)
        pre_grad[at, :] = low
        local[0:1, 0:hidden_width] += jnp.sum(low.astype(FULL), axis=0, keepdims=True)
        return dot(low, w_up[...], ((1,), (1,)))

    def to_attn(at, value):
        if plan.last:
            above = grad[one.rows(one.own + at.start, at.size), :].astype(FULL)
        else:
            above = x_ref[at]
        _, normed, inverse = normalize(middle[at], 1.0, 0.0)
        result = above + normalize_back(value, normed, inverse, gain2)
        stream[at] = result
        low = result.astype(LOW)
        sums_into(split, 2, at, (value * normed, value, low.astype(FULL)))
        return low

    def reduce(name):
        if name in reduces:
            reduces[name].begin_blocks()

    def own(name):
        if name in reduces:
            reduces[name].own()

    def first_step(name):
        if name in reduces:
            reduces[name].fold_blocks(3)
            reduces[name].send_first()

    def second_step(name):
        if name in reduces:
            reduces[name].fold_blocks(2)
            reduces[name].send_third()

    def rest(name):
        if name in reduces:
            reduces[name].fold_blocks(1)
            reduces[name].send_second()
            reduces[name].fold_blocks(0)

    def begin_early():
        if plan.joined:
            early_held[0] = jnp.zeros(early_held.shape[1:], FULL)
            for layer, (some, more) in enumerate(everything):
                first_row = 0 if layer else 2
                for row in range(first_row, 6):
                    at = row * len(everything) + layer
                    early_held[0, at : at + 1, :] = some[row : row + 1, :]
                for row in range(2 if layer else 1):
                    at = tops + row * len(everything) + layer
                    early_held[0, at : at + 1, :] = more[row : row + 1, :]

    def early_step():
        if plan.joined:
            early.step()

    def start_down():
        mover.near(*load[3:5])
        reduce("down")

    one.eager(mlp_part, to_attn, start_down)
    if late:
        late.send_third()
    own("down")
    first_step("down")
    mover.near(load[5])
    reduce("up")
    one.have()
    mover.near(load[6])
    turned_product(attn_grad, w_out, None, parts)

    def waiting():
        begin_early()
        early_step()
        second_step("down")
        mover.near(load[7])
        reduce("out")
        own("out")

    def ready():
        own("up")
        mover.near(load[8], load[9], load[10])

    def between(turn):
        if turn == 0:
            early_step()
            first_step("up")
        if turn == 3:
            second_step("up")
            rest("down")

    attend_back_part(
        size,
        tile,
        mover,
        parts,
        bias,
        qkv,
        o_ref,
        lse,
        grads,
        attend_work,
        ready,
        waiting,
        lambda: None,
        between,
    )
    early_step()
    nat[...] = turned(grads[...])
    pairs_width = nat.shape[1] // 3 * 2
    picked = jnp.dot(
        nat[...], pair_columns(pairs_width, nat.shape[1], size, True), preferred_element_type=FULL
    )
    local[1:2, 0:pairs_width] = jnp.sum(picked, axis=0, keepdims=True)
    mover.near(*load[11:])

    def qkv_part(start):
        return dot(nat[two.rows(start), :], w_qkv[...], ((1,), (1,)))

    def to_following(at, value):
        row = before[at, :].astype(FULL)
        _, normed, inverse = normalize(row, 1.0, 0.0)
        result = stream[at] + normalize_back(value, normed, inverse, gain1)
        stream[at] = result
        low = result.astype(LOW)
        sums_into(split, 0, at, (value * normed, value))
        return low

    def meanwhile():
        own("qkv")
        early_step()
        first_step("out")
        rest("up")

    def halfway():
        if plan.inside:
            reduces["qkv"].fold_blocks(3)
            if plan.final:
                reduces["qkv"].send_first()

    reduce("qkv")
    two.eager(qkv_part, to_following, meanwhile, halfway)
    if plan.joined:
        late_held[0, 0:8, :] = jnp.zeros((8, late_held.shape[2]), FULL)
        late_held[0, 0:2, :] = split[0:2, :]
        late_held[0, 8:16, :] = local[...]
        final.step()
        early_step()
        final.step()
    second_step("out")
    rest("out")
    two.have_mate_own()
    two.have_other()
    if plan.joined:
        final.step()
        final.step()
    if plan.inside:
        last = reduces["qkv"]
        if plan.final:
            second_step("qkv")
            rest("qkv")
        else:
            last.fold_blocks(2, 1, 0)
            mover.stay(last.mid, mid_out)
    two.have_mate_other()
    if plan.joined:
        final.step()
    for name in ("down", "up", "out"):
        if name in reduces:
            reduces[name].done()
    if late:
        late.done()
    if plan.inside and plan.final:
        reduces["qkv"].done()
    if plan.joined:
        final.step()
        early.step()
        totals[...] = early.value()
        last_value = final.value()
        for row in range(2):
            at = row * len(everything)
            totals[at : at + 1, :] = last_value[row : row + 1, :]
        at = tops + len(everything)
        totals[at : at + 1, :] = last_value[9:10, :]
    if not plan.inside:
        for name, (lhs, rhs) in {
            "down": (grad, hidden),
            "up": (second, pre_grad),
            "out": (attn_grad, heads),
            "qkv": (first, nat),
        }.items():
            full = Reduce(mover, (wholes[name],) * 4, None, lhs, rhs)
            full.compute(wholes[name], 0)
    mover.settle()


def gather_outputs_kernel(layers, *refs):
    count = layers * len(NAMES)
    parts, token_grads, mixed, totals = refs[:count], refs[count], refs[count + 1], refs[count + 2]
    outs, work = refs[count + 3 : count + 17], refs[count + 17 : -2]
    into, out_of = refs[-2:]
    coming, going = [], []
    pairs = [(mixed, work[4], outs[4].at[0])]
    for index in range(len(NAMES)):
        for layer in range(layers):
            pairs.append(
                (parts[index * layers + layer], work[index].at[layer], outs[index].at[layer])
            )
    for i, (source, stage, _) in enumerate(pairs):
        coming.append(pltpu.make_async_copy(source, stage, into.at[i]))
        coming[-1].start()
    outs[5][0] = token_grads[...].astype(FULL)
    for row, out in enumerate(outs[6:12]):
        out[...] = totals[row * layers : (row + 1) * layers, 0 : out.shape[1]]
    for row, out in enumerate(outs[12:14]):
        row = row + 8
        out[...] = totals[row * layers : (row + 1) * layers, 0 : out.shape[1]]
    for i, (_, stage, target) in enumerate(pairs):
        coming[i].wait()
        going.append(pltpu.make_async_copy(stage, target, out_of.at[i]))
        going[-1].start()
    for copy in going:
        copy.wait()


def gather_outputs(done, token_grads, mixed, totals, layers, widths):
    rows, width = token_grads.shape
    parts = [done[name, layer] for name in NAMES for layer in range(layers)]
    hbm, whole = pl.BlockSpec(memory_space=HBM), lambda shape: pl.BlockSpec(
        shape, lambda i: (0,) * len(shape)
    )
    shapes = [(layers,) + done[name, 0].shape for name in NAMES] + [(1, rows, width)] * 2
    types = [FULL] * 4 + [LOW, FULL]
    small = [(layers, width)] * 6 + [(layers, count) for count in widths]
    copies = len(parts) + 1
    return pl.pallas_call(
        functools.partial(gather_outputs_kernel, layers),
        grid=(1,),
        in_specs=[hbm] * len(parts) + [whole(token_grads.shape), hbm, whole(totals.shape)],
        out_specs=[hbm] * 5 + [whole(shape) for shape in shapes[5:] + small],
        out_shape=[jax.ShapeDtypeStruct(*pair) for pair in zip(shapes, types)]
        + [jax.ShapeDtypeStruct(shape, FULL) for shape in small],
        scratch_shapes=[VMEM(shape, FULL) for shape in shapes[:4]]
        + [VMEM((rows, width), LOW)]
        + [pltpu.SemaphoreType.DMA((copies,)), pltpu.SemaphoreType.DMA((copies,))],
        compiler_params=pltpu.CompilerParams(vmem_limit_bytes=60 * 2**20),
        name="gather_outputs",
    )(*parts, token_grads, mixed, totals)


class BackPlan:
    def __init__(self, layer, layers, inside):
        self.inside, self.layer = inside, layer
        self.last, self.final = layer == layers - 1, layer == 0
        self.late = inside and not self.last
        self.joined = inside and self.final
        self.others = layers - 1 if self.joined else 0


def back_layer(source, x, live, gain2, gain1, saved, late, others, plan, size, sizes, ident):
    rows, width = source.shape
    count = sizes[0]
    slope, w_down, w_up = saved[:3]
    hidden, joint, attn = slope.shape[1], saved[12].shape[1], saved[6].shape[1]
    slots, span = count * rows, rows // 4
    tile = 256 if slots % 256 == 0 else PAD
    wide = max(width, hidden, joint)
    half = width // 2
    block = half // count
    columns = {"qkv": joint, "out": attn, "up": hidden, "down": hidden}
    inputs = [(source, VMEM)] + ([] if plan.last else [(x, VMEM)])
    inputs += [(live, SMEM), (gain2, HBM), (gain1, HBM)]
    inputs += [(value, HBM) for value in saved]
    if plan.late:
        inputs.append((late, HBM))
    for pair in others[: plan.others]:
        inputs += [(value, VMEM) for value in pair]
    outputs = [((span, width), FULL, VMEM), ((rows, width), LOW, VMEM)]
    names = [name for name in NAMES if plan.inside and (name != "qkv" or plan.final)]
    outputs += [((block, columns[name]), FULL, VMEM) for name in names]
    if plan.inside and not plan.final:
        outputs.append(((half, joint), LOW, HBM))
    if plan.late:
        outputs.append(((block, joint), FULL, VMEM))
    depth = 8 * (plan.others + 1)
    if plan.joined:
        outputs.append(((depth + 8, wide), FULL, VMEM))
    else:
        outputs += [((8, wide), FULL, VMEM)] * 2
    if not plan.inside:
        outputs += [((width, columns[name]), LOW, VMEM) for name in NAMES]
    scratch = [VMEM(value.shape, value.dtype) for value in saved]
    scratch[13] = VMEM((span, width), saved[13].dtype)
    if plan.last:
        scratch.append(VMEM((rows, width), LOW))
    scratch += [
        VMEM((rows, hidden), LOW),
        VMEM((rows, width), LOW),
        VMEM((attn, rows), LOW),
        VMEM((joint, rows), LOW),
        VMEM((rows, joint), LOW),
    ]
    scratch += attend_back_buffers(size, count, rows, tile)
    scratch += round_buffers(rows, width) + round_buffers(rows, width)
    if plan.inside:
        for name in ("down", "up", "out", "qkv"):
            scratch += reduce_buffers(half, columns[name], count)
    if plan.late:
        scratch += [VMEM((half, joint), LOW), VMEM((count - 1, block, joint), LOW)]
    scratch.append(VMEM((16, slots), LOW))
    scratch += [VMEM(value.shape, value.dtype) for value in (gain2, gain1)]
    assert 2 * (plan.others + 1) <= 8
    if plan.joined:
        scratch += [VMEM((8, wide), FULL)] * 2
        scratch += [
            VMEM((6, depth + 8, wide), FULL),
            VMEM((5, depth + 8, wide), FULL),
            VMEM((6, 16, wide), FULL),
            VMEM((5, 16, wide), FULL),
        ]
    results = run(
        functools.partial(back_kernel, plan, size, tile),
        "back_layer",
        ident,
        inputs,
        outputs,
        scratch,
        3 * (count - 1) + 2 * ROUND_COPIES + 8 * count + 10 + count,
        len(saved) + 4,
        sizes,
        58,
        6 * rows * width * (2 * hidden + attn + joint) + 10 * slots * slots * 256,
    )
    return results[:2], names, results[2:]


def shards(
    tokens,
    block_tokens,
    ln1_gain,
    ln1_bias,
    w_qkv,
    b_qv,
    w_out,
    b_out,
    ln2_gain,
    ln2_bias,
    w_up,
    b_up,
    w_down,
    b_down,
    cotangent,
):
    images, capacity, width = tokens.shape
    assert images == 1
    layers = w_qkv.shape[0]
    size = HEAD_DIM
    ctx_count = lax.axis_size("ctx")
    ctx_place = lax.axis_index("ctx")
    joint_width = w_qkv.shape[2]
    heads = joint_width // (3 * size)
    assert heads == ctx_count
    attn_width = heads * size
    hidden_width = w_up.shape[2]
    weights = {"qkv": w_qkv, "out": w_out, "up": w_up, "down": w_down}
    sizes = (ctx_count, lax.axis_size("shard"))
    inside = sizes == (4, 2)
    gathered = {}
    if not inside:
        for name, value in weights.items():
            for layer in range(layers):
                gathered[name, layer] = gather_weight(value[layer])[0]
    source, stream = tokens[0], None
    saved = []
    for layer in range(layers):
        last = layer == layers - 1
        result, following, kept = forward_layer(
            source,
            stream,
            block_tokens,
            (b_out, ln2_gain, ln2_bias, b_down, ln1_gain, ln1_bias, b_up, b_qv),
            gathered,
            weights,
            Plan(layer, last, inside),
            last,
            size,
            sizes,
            1 + layer,
        )
        before = stream if layer else source
        first = source if layer else kept[8]
        saved.append((before, first) + tuple(kept[:8]))
        source, stream = following, result
    mixed = source

    done, packs = {}, {}
    source, stream, late = cotangent[0], None, None
    for layer in reversed(range(layers)):
        before, first, qkv, head_out, lse, heads_low, middle, second, hidden, slope = saved[layer]
        plan = BackPlan(layer, layers, inside)
        whole = {name: gathered[name, layer] for name in NAMES}
        near = [slope, whole["down"], whole["up"], middle, hidden, second, whole["out"]]
        near += [heads_low, qkv, head_out, lse, first, whole["qkv"], before]
        others = [packs[key] for key in sorted(packs)]
        (stream, source), names, rest = back_layer(
            source, stream, block_tokens, ln2_gain, ln1_gain, near, late, others, plan, size, sizes, 1 + layers + layer
        )
        rest = iter(rest)
        for name in names:
            done[name, layer] = next(rest)
        if plan.inside and not plan.final:
            late = next(rest)
        if plan.late:
            done["qkv", layer + 1] = next(rest)
        if plan.joined:
            totals = next(rest)
        else:
            packs[layer] = (next(rest), next(rest))
        if not inside:
            for name in NAMES:
                value = next(rest)
                done[name, layer] = scatter_weight(
                    lambda start, count, value=value: rows_of(value, start, count).astype(FULL),
                    width,
                )
    if not inside:
        split = total_over(("tp",), jnp.stack([packs[l][0] for l in range(layers)], axis=1))
        local = jnp.stack([packs[l][1] for l in range(layers)], axis=1)
        totals = total_over(("shard", "ctx"), jnp.concatenate([split, local[:2]]))
        totals = totals.reshape(10 * layers, -1)
    pairs = b_qv.shape[1]
    outs = gather_outputs(done, source, mixed, totals, layers, (hidden_width, pairs))
    g_qkv, g_out, g_up, g_down, mixed, token_grads = outs[:6]
    g_ln1_gain, g_ln1_bias, g_ln2_gain, g_ln2_bias, g_b_out, g_b_down, g_b_up, g_b_qv = outs[6:]
    return (
        mixed,
        token_grads,
        g_ln1_gain,
        g_ln1_bias,
        g_qkv,
        g_b_qv,
        g_out,
        g_b_out,
        g_ln2_gain,
        g_ln2_bias,
        g_up,
        g_b_up,
        g_down,
        g_b_down,
    )


def solution(mesh):
    split_rows = P(None, ("shard", "ctx"), "tp")
    split_tokens = P("shard", "ctx", None)
    return jax.shard_map(
        shards,
        mesh=mesh,
        in_specs=(
            split_tokens,
            P("shard", None),
            P(),
            P(),
            split_rows,
            P(None, "tp"),
            split_rows,
            P(),
            P(),
            P(),
            split_rows,
            P(None, "tp"),
            split_rows,
            P(),
            split_tokens,
        ),
        out_specs=(
            split_tokens,
            split_tokens,
            P(),
            P(),
            split_rows,
            P(None, "tp"),
            split_rows,
            P(),
            P(),
            P(),
            split_rows,
            P(None, "tp"),
            split_rows,
            P(),
        ),
        check_vma=False,
    )
```

```python
import functools
import math

import jax
import jax.numpy as jnp
from jax import lax
from jax.experimental import pallas as pl
from jax.experimental.pallas import tpu as pltpu
from jax.sharding import PartitionSpec as P

HEAD_DIM = 64
EPSILON = 1e-06
NEG_LARGE = -1e30
LOW = jnp.bfloat16
FULL = jnp.float32
PAD = 128
MESH = pl.DeviceIdType.MESH
VMEM = pltpu.VMEM
HBM = pltpu.HBM
SMEM = pltpu.SMEM


def bits_of(axis):
    size = lax.axis_size(axis)
    assert size & (size - 1) == 0
    return [1 << i for i in range(size.bit_length() - 1)]


def swap(value, axis, bit):
    size = lax.axis_size(axis)
    return lax.ppermute(value, axis, [(i, i ^ bit) for i in range(size)])


def side_of(axis, bit):
    return (lax.axis_index(axis) // bit) % 2


def rows_of(value, start, count, axis=0):
    return lax.dynamic_slice_in_dim(value, start, count, axis)


def halve(axis, bits, partial, total):
    offset, span, received = jnp.int32(0), total, []

    def summed(start, count):
        value = partial(start, count)
        for got, base in received:
            value = value + rows_of(got, start - base, count).astype(FULL)
        return value

    for bit in bits:
        half = span // 2
        side = side_of(axis, bit)
        got = swap(summed(offset + (1 - side) * half, half).astype(LOW), axis, bit)
        offset = offset + side * half
        received.append((got, offset))
        span = half
    return summed(offset, span)


def double(axis, bits, value):
    for bit in bits:
        got = swap(value, axis, bit)
        first = side_of(axis, bit) == 0
        value = jnp.concatenate(
            [jnp.where(first, value, got), jnp.where(first, got, value)], axis=0
        )
    return value


def total_over(axes, value):
    for axis in axes:
        for bit in bits_of(axis):
            value = value + swap(value, axis, bit)
    return value


def ring(value, by):
    count = lax.axis_size("ctx")
    return lax.ppermute(value, "ctx", [(i, (i + by) % count) for i in range(count)])


def gather_weight(piece):
    count = lax.axis_size("ctx")
    place = lax.axis_index("ctx")
    ways = lax.axis_size("shard")
    blocks = [piece] + [ring(piece, by) for by in range(1, count)]
    whole = jnp.zeros((ways * count,) + piece.shape, piece.dtype)
    me = lax.axis_index("shard")
    for by, block in enumerate(blocks):
        at = (place - by) % count
        held = [(jnp.int32(0), block)]
        for bit in bits_of("shard"):
            held = held + [(other ^ bit, swap(value, "shard", bit)) for other, value in held]
        for other, value in held:
            whole = lax.dynamic_update_index_in_dim(whole, value, (me ^ other) * count + at, 0)
    return whole.reshape((ways * count * piece.shape[0],) + piece.shape[1:]), blocks[-1]


def scatter_weight(partial, total):
    count = lax.axis_size("ctx")
    place = lax.axis_index("ctx")
    mine = halve("shard", bits_of("shard")[::-1], partial, total).astype(LOW)
    mine = mine.reshape((count, mine.shape[0] // count) + mine.shape[1:])
    value = lax.dynamic_index_in_dim(mine, place, 0, False).astype(FULL)
    for by in range(1, count):
        given = lax.dynamic_index_in_dim(mine, (place + by) % count, 0, False)
        value = value + ring(given, by).astype(FULL)
    return value


def dot(left, right, contract):
    return lax.dot_general(
        left, right, ((contract[0], contract[1]), ((), ())), preferred_element_type=FULL
    )


def turned(value):
    return value.astype(FULL).T.astype(LOW)


def normalize(rows, gain, shift):
    row_mean = jnp.mean(rows, axis=-1, keepdims=True)
    centred = rows - row_mean
    inverse = lax.rsqrt(jnp.mean(centred * centred, axis=-1, keepdims=True) + EPSILON)
    normed = centred * inverse
    return (normed * gain + shift, normed, inverse)


def normalize_back(grad_out, normed, inverse, gain):
    scaled = grad_out * gain
    mean_grad = jnp.mean(scaled, axis=-1, keepdims=True)
    mean_cross = jnp.mean(scaled * normed, axis=-1, keepdims=True)
    return inverse * (scaled - mean_grad - normed * mean_cross)


def gelu_pair(value):
    spread = 0.5 * (1.0 + lax.erf(value * (0.5**0.5)))
    slope = spread + value * jnp.exp(-0.5 * value * value) * (1.0 / math.sqrt(2.0 * math.pi))
    return (value * spread).astype(LOW), slope.astype(LOW)


class Mover:
    def __init__(self, sizes, send, recv, local):
        self.ctx_count, self.shard_count = sizes
        self.send, self.recv, self.local = send, recv, local
        self.copies, self.here = [], []
        self.arrived = set()
        self.landed = set()
        self.ctx = lax.axis_index("ctx")
        self.shard = lax.axis_index("shard")

    def go(self, source, target, **device):
        index = len(self.copies)
        assert index < self.send.shape[0]
        copy = pltpu.make_async_remote_copy(
            src_ref=source,
            dst_ref=target,
            send_sem=self.send.at[index],
            recv_sem=self.recv.at[index],
            device_id=device,
            device_id_type=MESH,
        )
        copy.start()
        self.copies.append(copy)
        return index

    def stay(self, source, target):
        index = len(self.here)
        assert index < self.local.shape[0]
        copy = pltpu.make_async_copy(source, target, self.local.at[index])
        copy.start()
        self.here.append(copy)
        return index

    def near(self, *indices):
        for index in indices:
            if index not in self.landed:
                self.landed.add(index)
                self.here[index].wait()

    def take(self, index):
        if index not in self.arrived:
            self.arrived.add(index)
            self.copies[index].wait_recv()

    def flip(self, bits):
        place = self.ctx
        if bits & 1:
            place = place + 1 - 2 * lax.rem(self.ctx, 2)
        if bits & 2:
            place = place + 2 - 4 * (self.ctx // 2)
        return place

    def on(self, by):
        return lax.rem(self.ctx + by, self.ctx_count)

    def back(self, by):
        return lax.rem(self.ctx + self.ctx_count - by, self.ctx_count)

    def settle(self):
        for index, copy in enumerate(self.copies):
            self.take(index)
            copy.wait_send()
        self.near(*range(len(self.here)))


class Gather:
    def __init__(self, mover, source, target):
        self.mover, self.source, self.target = mover, source, target
        self.over = []

    def start(self):
        self.start_line()
        self.start_over()

    def start_line(self):
        mover = self.mover
        mine, there = self.source, self.block(mover.ctx)
        self.far = mover.go(mine, there, ctx=mover.flip(2))
        self.close = mover.go(mine, there, ctx=mover.flip(1))

    def start_over(self):
        mover = self.mover
        mine, there = self.source, self.block(mover.ctx)
        self.over.append(mover.go(mine, there, shard=1 - mover.shard))
        self.own = mover.stay(mine, there)

    def block(self, ctx):
        mover = self.mover
        rows = self.source.shape[0]
        start = (mover.shard * mover.ctx_count + ctx) * rows
        return self.target.at[pl.ds(pl.multiple_of(start, rows), rows)]

    def pass_on(self, stage):
        mover = self.mover
        if stage == 1:
            mover.take(self.far)
            rows = self.block(mover.flip(2))
            self.passed = mover.go(rows, rows, ctx=mover.flip(1))
        elif stage == 2:
            mover.take(self.close)
            rows = self.block(mover.flip(1))
        else:
            mover.take(self.passed)
            rows = self.block(mover.flip(3))
        self.over.append(mover.go(rows, rows, shard=1 - mover.shard))

    def have(self):
        for copy in self.over:
            self.mover.take(copy)
        self.mover.near(self.own)


class Reduce:
    def __init__(self, mover, buffers, out, lhs, rhs):
        self.mover, self.out, self.lhs, self.rhs = mover, out, lhs, rhs
        self.give, self.got, self.mid, self.line = buffers
        self.half = self.give.shape[0]
        self.block = self.half // mover.ctx_count

    def compute(self, target, shard):
        chunk = min(256, self.half)

        def step(i, carry):
            at = pl.ds(pl.multiple_of(shard * self.half + i * chunk, chunk), chunk)
            here = pl.ds(pl.multiple_of(i * chunk, chunk), chunk)
            target[here, :] = dot(self.lhs[:, at], self.rhs[...], ((0,), (0,))).astype(LOW)
            return carry

        lax.fori_loop(0, self.half // chunk, step, 0)

    def begin_blocks(self):
        mover = self.mover
        self.blocks = {}
        for bits in (3, 2, 1, 0):
            ctx = mover.flip(bits)
            at = pl.ds(pl.multiple_of(ctx * self.block, self.block), self.block)
            start = pl.multiple_of((1 - mover.shard) * self.half + ctx * self.block, self.block)
            lhs = self.lhs[:, pl.ds(start, self.block)]
            self.give[at, :] = dot(lhs, self.rhs[...], ((0,), (0,))).astype(LOW)
            self.blocks[bits] = mover.go(
                self.give.at[at], self.got.at[at], shard=1 - mover.shard
            )

    def own(self):
        self.compute(self.mid, self.mover.shard)

    def fold_blocks(self, *which):
        mover = self.mover
        for bits in which:
            mover.take(self.blocks[bits])
            ctx = mover.flip(bits)
            at = pl.ds(pl.multiple_of(ctx * self.block, self.block), self.block)
            self.mid[at, :] = (
                self.mid[at, :].astype(FULL) + self.got[at, :].astype(FULL)
            ).astype(LOW)

    def rows(self, ctx):
        return self.mid.at[pl.ds(pl.multiple_of(ctx * self.block, self.block), self.block)]

    def send_first(self):
        mover = self.mover
        self.first = mover.go(self.rows(mover.flip(3)), self.line.at[1], ctx=mover.flip(1))

    def send_second(self):
        mover = self.mover
        self.second = mover.go(self.rows(mover.flip(1)), self.line.at[0], ctx=mover.flip(1))

    def send_third(self):
        mover = self.mover
        mover.take(self.first)
        rows = self.rows(mover.flip(2))
        rows[...] = (rows[...].astype(FULL) + self.line[1].astype(FULL)).astype(LOW)
        self.third = mover.go(rows, self.line.at[2], ctx=mover.flip(2))

    def done(self):
        self.mover.take(self.second)
        self.mover.take(self.third)
        value = self.rows(self.mover.ctx)[...].astype(FULL)
        self.out[...] = value + self.line[0].astype(FULL) + self.line[2].astype(FULL)


def reduce_buffers(half, width, count):
    return [
        VMEM((half, width), LOW),
        VMEM((half, width), LOW),
        VMEM((half, width), LOW),
        VMEM((count - 1, half // count, width), LOW),
    ]


def greet(mover, shard):
    barrier = pltpu.get_barrier_semaphore()
    peers = [dict(ctx=mover.on(by)) for by in range(1, mover.ctx_count)]
    peers += [dict(tp=peer) for peer in tp_peers()]
    if shard:
        peers.append(dict(shard=1 - mover.shard))
    for peer in peers:
        pl.semaphore_signal(barrier, inc=1, device_id=peer, device_id_type=MESH)
    pl.semaphore_wait(barrier, len(peers))


def tp_peers():
    place = lax.axis_index("tp")
    core, far = lax.rem(place, 2), place // 2
    return place + 1 - 2 * core, place + 2 - 4 * far


def run(kernel, name, ident, inputs, outputs, scratch, remote, local, sizes, vmem, flops):
    n_in, n_out, n_scratch = len(inputs), len(outputs), len(scratch)

    def body(*refs):
        ins, outs = refs[:n_in], refs[n_in : n_in + n_out]
        work = refs[n_in + n_out :]
        mover = Mover(sizes, *work[n_scratch:])
        kernel(mover, ins, outs, work[:n_scratch])

    return pl.pallas_call(
        body,
        in_specs=[pl.BlockSpec(memory_space=space) for _, space in inputs],
        out_specs=[pl.BlockSpec(memory_space=space) for _, _, space in outputs],
        out_shape=[jax.ShapeDtypeStruct(shape, dtype) for shape, dtype, _ in outputs],
        scratch_shapes=list(scratch)
        + [
            pltpu.SemaphoreType.DMA((remote,)),
            pltpu.SemaphoreType.DMA((remote,)),
            pltpu.SemaphoreType.DMA((local,)),
        ],
        compiler_params=pltpu.CompilerParams(
            collective_id=ident, has_side_effects=True, vmem_limit_bytes=vmem * 2**20
        ),
        cost_estimate=pl.CostEstimate(flops=flops, bytes_accessed=2**24, transcendentals=0),
        name=name,
    )(*[value for value, _ in inputs])


def order_of(block, count):
    return (block + count - 1) % count


def tiles_of(count, capacity, tile):
    ends = [-(-(p + 1) * capacity // tile) for p in range(count)]
    return list(zip([0] + ends[:-1], ends))


def tile_at(t, tile):
    return pl.ds(pl.multiple_of(t * tile, tile), tile)


def turned_product(left, right, bias, target):
    value = jnp.dot(left[...], right[...], preferred_element_type=FULL)
    if bias is not None:
        value = value + bias[0:1, :]
    target[...] = turned(value.astype(LOW))


def head_rows(ref, head, width):
    return ref.at[pl.ds(pl.multiple_of(head * width, 16), width)]


def attend_part(size, tile, mover, joint, bias, heads, qkv, o_ref, lse, work, after_send, begun, between):
    k_ref, q_ref, v_ref, low_ref, score_ref, top_ref = work
    count, width, capacity = qkv.shape
    slots = count * capacity
    sent = [None] + [
        mover.go(head_rows(joint, mover.on(by), width), qkv.at[by], ctx=mover.on(by))
        for by in range(1, count)
    ]
    after_send()
    qkv[0] = head_rows(joint, mover.ctx, width)[...]
    q_ref[size:PAD, :] = jnp.concatenate(
        [jnp.ones((16, slots), LOW), jnp.zeros((PAD - size - 16, slots), LOW)], axis=0
    )

    v_ref[size : size + 16, :] = jnp.ones((16, slots), LOW)

    def prepare(r):
        here = slice(r * capacity, (r + 1) * capacity)
        p = order_of(r, count)
        q_ref[0:size, p * capacity : (p + 1) * capacity] = (
            qkv[r, 0:size, :] * (size**-0.5)
        ).astype(LOW)
        v_ref[0:size, here] = qkv[r, 2 * size : 3 * size, :]
        keys = jnp.concatenate(
            [qkv[r, size : 2 * size, :], bias[:, here], jnp.zeros((PAD - size - 16, capacity), LOW)],
            axis=0,
        )
        k_ref[here, :] = turned(keys)

    prepare(0)
    for by in range(1, count):
        mover.take(sent[by])
        prepare(by)

    begun()
    last = slots // tile - 1
    assert last % 2 == 1

    def phase(t, now, following, then):
        at, ahead = tile_at(t, tile), tile_at(following, tile)
        top = top_ref[now, 0:1, :]
        summed = jnp.zeros((size + 16, tile), FULL)
        new_top = jnp.full((1, tile), NEG_LARGE, FULL)
        for r in range(count):
            here = slice(r * capacity, (r + 1) * capacity)
            scores = jnp.dot(k_ref[here, :], q_ref[:, ahead], preferred_element_type=FULL)
            score_ref[then, here, :] = scores
            new_top = jnp.maximum(new_top, jnp.max(scores, axis=0, keepdims=True))
            weights = jnp.exp(score_ref[now, here, :] - top)
            summed = summed + jnp.dot(
                v_ref[:, here], weights.astype(LOW), preferred_element_type=FULL
            )
        top_ref[then] = jnp.broadcast_to(new_top, (8, tile))
        total = summed[size : size + 1]
        out = summed[0:size] / total
        o_ref[:, at] = out
        low_ref[:, at] = out.astype(LOW)
        lse[:, at] = jnp.broadcast_to(top + jnp.log(total), (8, tile))

    def step(i, carry):
        phase(2 * i, 0, 2 * i + 1, 1)
        phase(2 * i + 1, 1, jnp.minimum(2 * i + 2, last), 0)
        return carry

    scores = jnp.dot(k_ref[...], q_ref[:, 0:tile], preferred_element_type=FULL)
    score_ref[0] = scores
    top_ref[0] = jnp.broadcast_to(jnp.max(scores, axis=0, keepdims=True), (8, tile))
    arriving = []
    for p, (low, high) in enumerate(tiles_of(count, capacity, 2 * tile)):
        lax.fori_loop(low, high, step, 0)
        done = low_ref.at[:, p * capacity : (p + 1) * capacity]
        if p < count - 1:
            there = head_rows(heads, mover.ctx, size)
            arriving.append(mover.go(done, there, ctx=mover.back(p + 1)))
        else:
            head_rows(heads, mover.ctx, size)[...] = low_ref[:, p * capacity : (p + 1) * capacity]
        between(p + 1)
    for copy in arriving:
        mover.take(copy)


def below(row, ones):
    width = row.shape[1]
    high = row.astype(LOW).astype(FULL)
    middle = (row - high).astype(LOW).astype(FULL)
    low = row - high - middle
    lead = jnp.full((1, width), 1.0 if ones else 0.0, FULL)
    rest = jnp.zeros((PAD // 2 - 4, width), FULL)
    return jnp.concatenate([lead, high, middle, low, rest], axis=0).astype(LOW)


def attend_back_part(size, tile, mover, parts, bias, qkv, o_ref, lse, grads, work, ready, waiting, begun, between):
    k_ref, v_ref, q_ref, do_ref, nat_ref, dq_ref, dk_ref, dv_ref, got, back = work
    count, width, capacity = qkv.shape
    slots = count * capacity
    sent = [None] + [
        mover.go(head_rows(parts, mover.on(by), size), got.at[by], ctx=mover.on(by))
        for by in range(1, count)
    ]
    got[0] = head_rows(parts, mover.ctx, size)[...]
    waiting()
    ready()
    q_ref[size:PAD, :] = below(lse[0:1, :], True)
    dq_ref[...] = jnp.zeros_like(dq_ref)
    off = (lax.broadcasted_iota(jnp.int32, (16, capacity), 0) + 2) // 3
    taken = jnp.where(off == 1, -1.0, 0.0).astype(LOW)
    pad = jnp.zeros((PAD - size - 16, capacity), LOW)
    for r in range(count):
        here = slice(r * capacity, (r + 1) * capacity)
        k_ref[here, :] = turned(
            jnp.concatenate([qkv[r, size : 2 * size, :], bias[:, here] + taken, pad], axis=0)
        )
        v_ref[here, :] = turned(
            jnp.concatenate([qkv[r, 2 * size : 3 * size, :], taken, pad], axis=0)
        )
    for r in range(count):
        if r:
            mover.take(sent[r])
        p = order_of(r, count)
        at = slice(p * capacity, (p + 1) * capacity)
        scaled = (qkv[r, 0:size, :] * (size**-0.5)).astype(LOW)
        dout = got[r]
        q_ref[0:size, at] = scaled
        do_ref[0:size, at] = dout
        nat_ref[at, :] = turned(jnp.concatenate([scaled, dout], axis=0))
        delta = jnp.sum(dout.astype(FULL) * o_ref[:, at], axis=0, keepdims=True)
        do_ref[size:PAD, at] = below(delta, False)

    begun()
    tiles = tiles_of(count, capacity, tile)
    arriving = []
    mine = head_rows(grads, mover.ctx, width)
    for turn, r in enumerate(list(range(1, count)) + [0]):
        here = slice(r * capacity, (r + 1) * capacity)
        dk_ref[...] = jnp.zeros_like(dk_ref)
        dv_ref[...] = jnp.zeros_like(dv_ref)

        def step(t, carry, r=r, here=here):
            at = tile_at(t, tile)
            scores = jnp.dot(k_ref[here, :], q_ref[:, at], preferred_element_type=FULL)
            chance = jnp.exp(scores)
            chance_grad = jnp.dot(v_ref[here, :], do_ref[:, at], preferred_element_type=FULL)
            score_grad = (chance * chance_grad).astype(LOW)
            dq_ref[:, at] += jnp.dot(
                qkv[r, size : 2 * size, :], score_grad, preferred_element_type=FULL
            )
            dk_ref[...] += jnp.dot(score_grad, nat_ref[at, :], preferred_element_type=FULL)
            dv_ref[...] += jnp.dot(
                chance.astype(LOW), nat_ref[at, :], preferred_element_type=FULL
            )
            return carry

        if r:
            lax.fori_loop(0, tiles[-1][1], step, 0)
        else:
            for p, (low, high) in enumerate(tiles):
                lax.fori_loop(low, high, step, 0)
                at = slice(p * capacity, (p + 1) * capacity)
                value = (dq_ref[:, at] * (size**-0.5)).astype(LOW)
                if p < count - 1:
                    back[p + 1, 0:size, :] = value
                    arriving.append(
                        mover.go(
                            back.at[p + 1, 0:size], mine.at[0:size], ctx=mover.back(p + 1)
                        )
                    )
                else:
                    mine[0:size, :] = value
        keys = dk_ref[...].T[0:size].astype(LOW)
        values = dv_ref[...].T[size : 2 * size].astype(LOW)
        if r:
            back[r, size : 2 * size, :] = keys
            back[r, 2 * size : 3 * size, :] = values
            arriving.append(
                mover.go(
                    back.at[r, size : 3 * size], mine.at[size : 3 * size], ctx=mover.back(r)
                )
            )
        else:
            mine[size : 2 * size, :] = keys
            mine[2 * size : 3 * size, :] = values
        between(turn)
    for copy in arriving:
        mover.take(copy)


def attend_back_buffers(size, count, capacity):
    slots = count * capacity
    return [
        VMEM((slots, PAD), LOW),
        VMEM((slots, PAD), LOW),
        VMEM((PAD, slots), LOW),
        VMEM((PAD, slots), LOW),
        VMEM((slots, PAD), LOW),
        VMEM((size, slots), FULL),
        VMEM((capacity, PAD), FULL),
        VMEM((capacity, PAD), FULL),
        VMEM((count, size, capacity), LOW),
        VMEM((count, 3 * size, capacity), LOW),
    ]


class Round:
    def __init__(self, mover, rows, full, buffers):
        place = lax.axis_index("tp")
        core, far = lax.rem(place, 2), place // 2
        self.mover, self.full = mover, full
        self.give, self.ra, self.passing, self.rb, self.keep = buffers
        self.span = rows // 4
        self.half = self.span // 2
        self.mate, self.far = tp_peers()

        def quarter(c, f):
            return (c * 2 + f) * self.span

        self.own, self.other = quarter(core, far), quarter(core, 1 - far)
        self.mate_own, self.mate_other = quarter(1 - core, far), quarter(1 - core, 1 - far)

    def rows(self, start, count=None):
        return pl.ds(pl.multiple_of(start, 16), count or self.span)

    def hand(self, slot, value):
        self.give[slot] = value.astype(LOW)
        return self.mover.go(self.give.at[slot], self.ra.at[slot], tp=self.mate)

    def onward(self, value, index):
        self.mover.take(index)
        self.passing[...] = (value + self.ra[1].astype(FULL)).astype(LOW)
        return [
            self.mover.go(self.passing.at[at], self.rb.at[at], tp=self.far)
            for at in (pl.ds(0, self.half), pl.ds(self.half, self.half))
        ]

    def close(self, far_copies, index, finish, halfway=None):
        self.mover.take(index)
        self.keep[...] += self.ra[0].astype(FULL)
        self.to_far, self.to_mate = [], []
        for c in range(2):
            at = pl.ds(c * self.half, self.half)
            self.mover.take(far_copies[c])
            low = finish(at, self.keep[at] + self.rb[at].astype(FULL))
            mine = self.full.at[self.rows(self.own + c * self.half, self.half)]
            mine[...] = low
            self.to_far.append(self.mover.go(mine, mine, tp=self.far))
            self.to_mate.append(self.mover.go(mine, mine, tp=self.mate))
            if halfway and c == 0:
                halfway()

    def eager(self, make, finish, meanwhile=None, halfway=None):
        first = self.hand(1, make(self.mate_other))
        copies = self.onward(make(self.other), first)
        second = self.hand(0, make(self.mate_own))
        self.keep[...] = make(self.own)
        if meanwhile:
            meanwhile()
        self.close(copies, second, finish, halfway)

    def after(self, before, make, finish, meanwhile, between):
        before.have_mate_own()
        second = self.hand(0, make(self.mate_own))
        self.keep[...] = make(self.own)
        before.have_other()
        between()
        value = make(self.other)
        before.have_mate_other()
        first = self.hand(1, make(self.mate_other))
        copies = self.onward(value, first)
        meanwhile()
        self.close(copies, second, finish)

    def have_mate_own(self):
        for copy in self.to_mate:
            self.mover.take(copy)

    def have_other(self):
        self.passed = []
        for c in range(2):
            self.mover.take(self.to_far[c])
            rows = self.full.at[self.rows(self.other + c * self.half, self.half)]
            self.passed.append(self.mover.go(rows, rows, tp=self.mate))

    def have_mate_other(self):
        for copy in self.passed:
            self.mover.take(copy)

    def have(self):
        self.have_mate_own()
        self.have_other()
        self.have_mate_other()


ROUND_COPIES = 10


def round_buffers(rows, width):
    span = rows // 4
    return [
        VMEM((2, span, width), LOW),
        VMEM((2, span, width), LOW),
        VMEM((span, width), LOW),
        VMEM((span, width), LOW),
        VMEM((span, width), FULL),
    ]


NAMES = ("qkv", "out", "up", "down")


def layer_kernel(plan, last, size, tile, mover, ins, outs, work):
    ins, outs, work = iter(ins), iter(outs), iter(work)
    source = next(ins)
    x_ref = None if plan.entry else next(ins)
    live_ref = next(ins)
    far_params = [next(ins) for _ in range(8)]
    stream, following = next(outs), next(outs)
    far_qkv, far_o, far_lse, far_heads, far_middle, far_second, far_hidden, far_slope = [
        next(outs) for _ in range(8)
    ]
    far_first = next(outs) if plan.entry else None
    joint, nat, heads, qkv, o_ref, lse, middle, second, hidden, slope = [
        next(work) for _ in range(10)
    ]
    first = next(work) if plan.entry else source
    attend_work = [next(work) for _ in range(6)]
    one_work, two_work = [next(work) for _ in range(5)], [next(work) for _ in range(5)]
    rows = source.shape[0]
    bias, qkv_bias = next(work), next(work)
    params = [next(work) for _ in range(8)]
    whole = {name: next(work) for name in NAMES}
    gathers, loads = {}, {}
    for name in plan.held:
        loads[name] = (next(ins), whole[name])
    for name in plan.own:
        gathers[name, 0] = Gather(mover, next(ins).at[plan.layer], whole[name])
    kept_ahead = {name: next(outs) for name in plan.ahead}
    for name in plan.ahead:
        gathers[name, 1] = Gather(mover, next(ins).at[plan.layer + 1], next(work))
    kept = {name: next(outs) for name in plan.own}

    greet(mover, bool(gathers))
    if plan.entry:
        gathers_first = [key for key in [("qkv", 0)] if key in gathers]
        for key in gathers_first:
            gathers[key].start()
    param_loads = [mover.stay(there, here) for there, here in zip(far_params, params)]
    waiting_loads = dict(loads)
    loads = {}

    def load(names):
        for name in names:
            if name in waiting_loads and name not in loads:
                loads[name] = mover.stay(*waiting_loads[name])

    load(["qkv"])

    def have(name):
        if name in waiting_loads:
            mover.near(loads[name])
            load(NAMES)
        else:
            gathers[name, 0].have()
            mover.stay(whole[name], kept[name])
        return whole[name]

    def begin(keys):
        for key in keys:
            if key in gathers:
                gathers[key].start_line()

    def begin_over(keys):
        for key in keys:
            if key in gathers:
                gathers[key].start_over()

    def pass_on(keys, stage):
        for key in keys:
            if key in gathers:
                gathers[key].pass_on(stage)

    def pass_all(keys):
        for stage in (1, 2, 3):
            pass_on(keys, stage)

    mover.near(*param_loads)
    layer, after = plan.layer, min(plan.layer + 1, params[0].shape[0] - 1)

    def row(index, layer=layer):
        return params[index][...].astype(FULL)[layer : layer + 1]

    b_out, gain2, shift2, b_down, b_up = row(0), row(1), row(2), row(3), row(6)
    gain1, shift1, gain0, shift0 = row(4, after), row(5, after), row(4), row(5)
    qkv_bias[...] = joint_bias(row(7), size, joint.shape[0])
    key_bias(mover, live_ref, bias)
    ahead = [("qkv", 1), ("out", 1), ("up", 1)]
    one = Round(mover, rows, second, one_work)
    two = Round(mover, rows, following, two_work)
    if plan.entry:
        chunk = rows // 5 if rows % 80 == 0 else rows

        def norm_step(i, carry):
            at = pl.ds(pl.multiple_of(i * chunk, 16), chunk)
            value = normalize(source[at, :].astype(FULL), gain0, shift0)[0]
            first[at, :] = value.astype(LOW)
            return carry

        lax.fori_loop(0, rows // chunk, norm_step, 0)
        mover.stay(first, far_first)
        pass_all([("qkv", 0)])
        begin([("out", 0), ("up", 0)])
        begin_over([("out", 0), ("up", 0), ("down", 0)] + ahead)
        turned_product(first, have("qkv"), qkv_bias, joint)
    else:
        turned_product(first, have("qkv"), qkv_bias, joint)

    def after_send():
        if plan.entry:
            pass_all([("out", 0), ("up", 0)])
        else:
            for name in plan.own:
                gathers[name, 0].start_over()

    def begun():
        begin([("down", 0)])

    def between(p):
        if p > 2:
            pass_on([("down", 0)], p - 2)
        if p == 4:
            if not plan.entry:
                begin_over(ahead)
            begin(ahead)

    attend_part(
        size, tile, mover, joint, bias, heads, qkv, o_ref, lse, attend_work, after_send, begun, between
    )
    nat[...] = turned(heads[...])
    w_out = have("out")

    def out_part(start):
        return dot(nat[one.rows(start), :], w_out[...], ((1,), (1,)))

    def to_second(at, value):
        if plan.entry:
            before = source[one.rows(one.own + at.start, at.size), :].astype(FULL)
        else:
            before = x_ref[at]
        value = before + value + b_out
        middle[at] = value
        return normalize(value, gain2, shift2)[0].astype(LOW)

    def meanwhile():
        mover.stay(qkv, far_qkv)
        mover.stay(o_ref, far_o)
        mover.stay(lse, far_lse)
        mover.stay(nat, far_heads)
        pass_on([("down", 0)], 3)

    one.eager(out_part, to_second, meanwhile, lambda: pass_on(ahead[:2], 1))
    pass_on(ahead[:2], 2)
    w_up, w_down = have("up"), have("down")

    def mlp_part(start):
        at = two.rows(start)
        pre = jnp.dot(second[at, :], w_up[...], preferred_element_type=FULL) + b_up
        low, low_slope = gelu_pair(pre)
        hidden[at, :] = low
        slope[at, :] = low_slope
        return dot(low, w_down[...], ((1,), (1,)))

    def to_following(at, value):
        value = middle[at] + value + b_down
        stream[at] = value
        if last:
            return live_rows(value, two.own + at.start, live_ref[0, mover.ctx]).astype(LOW)
        return normalize(value, gain1, shift1)[0].astype(LOW)

    def meanwhile():
        mover.stay(middle, far_middle)
        mover.stay(second, far_second)
        mover.stay(hidden, far_hidden)
        mover.stay(slope, far_slope)
        pass_on(ahead[2:], 3)

    def between_parts():
        pass_on(ahead[:2], 3)
        pass_on(ahead[2:], 1)
        pass_on(ahead[2:], 2)

    two.after(one, mlp_part, to_following, meanwhile, between_parts)
    two.have()
    for name in plan.ahead:
        gathers[name, 1].have()
        mover.stay(gathers[name, 1].target, kept_ahead[name])
    mover.settle()


class Plan:
    def __init__(self, layer, last, inside):
        self.layer, self.entry = layer, layer == 0
        self.own = (NAMES if layer == 0 else ("down",)) if inside else ()
        self.ahead = ("qkv", "out", "up") if inside and not last else ()
        self.held = tuple(name for name in NAMES if name not in self.own)


def forward_layer(source, x, live, params, gathered, weights, plan, last, size, sizes, ident):
    rows, width = source.shape
    count = sizes[0]
    joint, hidden = weights["qkv"].shape[2], weights["up"].shape[2]
    heads = joint // (3 * size)
    attn, slots, span = heads * size, count * rows, rows // 4
    tile = 256 if slots % 256 == 0 else PAD
    columns = {"qkv": joint, "out": attn, "up": hidden, "down": hidden}
    inputs = [(source, VMEM)] + ([] if plan.entry else [(x, VMEM)])
    inputs += [(live, SMEM)] + [(value, HBM) for value in params]
    inputs += [(gathered[name, plan.layer], HBM) for name in plan.held]
    inputs += [(weights[name], HBM) for name in plan.own + plan.ahead]
    saved = [
        ((count, 3 * size, rows), LOW),
        ((size, slots), FULL),
        ((8, slots), FULL),
        ((rows, attn), LOW),
        ((span, width), FULL),
        ((rows, width), LOW),
        ((rows, hidden), LOW),
        ((rows, hidden), LOW),
    ]
    outputs = [((span, width), FULL, VMEM), ((rows, width), LOW, VMEM)]
    outputs += [(shape, dtype, HBM) for shape, dtype in saved]
    if plan.entry:
        outputs.append(((rows, width), LOW, HBM))
    outputs += [((width, columns[name]), LOW, HBM) for name in plan.ahead + plan.own]
    qkv_shape, o_shape, lse_shape, heads_shape = saved[:4]
    scratch = [VMEM((joint, rows), LOW), VMEM((rows, attn), LOW), VMEM((attn, rows), LOW)]
    scratch += [VMEM(*pair) for pair in saved[:3] + saved[4:]]
    if plan.entry:
        scratch.append(VMEM((rows, width), LOW))
    scratch += [
        VMEM((slots, PAD), LOW),
        VMEM((PAD, slots), LOW),
        VMEM((size + 16, slots), LOW),
        VMEM((size, slots), LOW),
        VMEM((2, slots, tile), FULL),
        VMEM((2, 8, tile), FULL),
    ]
    scratch += round_buffers(rows, width) + round_buffers(rows, width)
    scratch += [VMEM((16, slots), LOW), VMEM((16, joint), FULL)]
    scratch += [VMEM(value.shape, value.dtype) for value in params]
    scratch += [VMEM((width, columns[name]), LOW) for name in NAMES + plan.ahead]
    results = run(
        functools.partial(layer_kernel, plan, last, size, tile),
        "forward_layer",
        ident,
        inputs,
        outputs,
        scratch,
        2 * (count - 1) + 2 * ROUND_COPIES + 2 * count * len(plan.own + plan.ahead),
        10 + 2 * len(plan.own + plan.ahead) + len(plan.held) + len(params),
        sizes,
        58,
        2 * rows * width * (2 * hidden + attn + joint) + 4 * slots * slots * 256,
    )
    stream, following = results[:2]
    kept = results[2 : 11 if plan.entry else 10]
    for name, value in zip(plan.ahead, results[2 + len(kept) :]):
        gathered[name, plan.layer + 1] = value
    for name, value in zip(plan.own, results[2 + len(kept) + len(plan.ahead) :]):
        gathered[name, plan.layer] = value
    return stream, following, kept


class SmallSums:
    def __init__(self, mover, rows, held, got):
        self.mover, self.rows, self.held, self.got = mover, rows, held, got
        self.stage = 0
        mate, far = tp_peers()
        self.peers = [
            dict(tp=mate),
            dict(tp=far),
            dict(shard=1 - mover.shard),
            dict(ctx=mover.flip(2)),
            dict(ctx=mover.flip(1)),
        ]

    def part(self, stage):
        return pl.ds(0, self.rows if stage < 2 else self.held.shape[1])

    def step(self):
        stage, mover = self.stage, self.mover
        if stage:
            mover.take(self.copy)
            at = self.part(stage - 1)
            self.held[stage] = self.held[stage - 1]
            self.held[stage, at, :] = self.held[stage - 1, at, :] + self.got[stage - 1, at, :]
        if stage < len(self.peers):
            at = self.part(stage)
            self.copy = mover.go(
                self.held.at[stage, at], self.got.at[stage, at], **self.peers[stage]
            )
        self.stage = stage + 1

    def value(self):
        return self.held[len(self.peers)]


def key_bias(mover, live_ref, bias):
    capacity = bias.shape[1] // mover.ctx_count
    row = lax.broadcasted_iota(jnp.int32, (16, capacity), 0)
    slot = lax.broadcasted_iota(jnp.int32, (16, capacity), 1)
    for r in range(mover.ctx_count):
        live = live_ref[0, mover.back(r)]
        value = jnp.where((row == 0) & (slot >= live), NEG_LARGE, 0.0)
        bias[:, r * capacity : (r + 1) * capacity] = value.astype(LOW)


def pair_columns(rows, width, size, turn):
    shape = (width, rows) if turn else (rows, width)
    given = lax.broadcasted_iota(jnp.int32, shape, 1 if turn else 0)
    column = lax.broadcasted_iota(jnp.int32, shape, 0 if turn else 1)
    head, within = column // (3 * size), column % (3 * size)
    wanted = head * (2 * size) + jnp.where(within < size, within, within - size)
    key = (within >= size) & (within < 2 * size)
    return jnp.where((given == wanted) & ~key, 1.0, 0.0).astype(LOW)


def joint_bias(pair, size, width):
    rows = pair.shape[1]
    spread = jnp.broadcast_to(pair, (16, rows)).astype(LOW)
    return jnp.dot(spread, pair_columns(rows, width, size, False), preferred_element_type=FULL)


def live_rows(value, start, live):
    row = start + lax.broadcasted_iota(jnp.int32, value.shape, 0)
    return jnp.where(row < live, value, 0.0)


def sums_into(sums, first, at, values):
    for index, value in enumerate(values):
        row = first + index
        added = jnp.sum(value, axis=0, keepdims=True)
        width = added.shape[1]
        sums[row : row + 1, 0:width] = (
            added if at.start == 0 else sums[row : row + 1, 0:width] + added
        )


def back_kernel(plan, size, tile, mover, ins, outs, work):
    ins, outs, work = iter(ins), iter(outs), iter(work)
    source = next(ins)
    x_ref = None if plan.last else next(ins)
    live_ref, far_gain2, far_gain1 = [next(ins) for _ in range(3)]
    far = [next(ins) for _ in range(14)]
    late_far = next(ins) if plan.late else None
    others = [(next(ins), next(ins)) for _ in range(plan.others)]
    stream, following = next(outs), next(outs)
    grad_outs = {name: next(outs) for name in NAMES if plan.inside and (name != "qkv" or plan.final)}
    mid_out = next(outs) if plan.inside and not plan.final else None
    late_out = next(outs) if plan.late else None
    split = local = totals = None
    if plan.joined:
        totals = next(outs)
    else:
        split, local = next(outs), next(outs)
    wholes = {} if plan.inside else {name: next(outs) for name in NAMES}
    near = [next(work) for _ in range(14)]
    slope, w_down, w_up, middle, hidden, second, w_out, heads, qkv, o_ref, lse, first, w_qkv, before = near
    grad = next(work) if plan.last else source
    pre_grad, attn_grad, parts, grads, nat = [next(work) for _ in range(5)]
    attend_work = [next(work) for _ in range(10)]
    one_work, two_work = [next(work) for _ in range(5)], [next(work) for _ in range(5)]
    rows, width = source.shape
    reduces = {}
    if plan.inside:
        pairs = {
            "down": (grad, hidden),
            "up": (second, pre_grad),
            "out": (attn_grad, heads),
            "qkv": (first, nat),
        }
        for name in ("down", "up", "out", "qkv"):
            buffers = [next(work) for _ in range(4)]
            reduces[name] = Reduce(mover, buffers, grad_outs.get(name), *pairs[name])
    late = None
    if plan.late:
        late_mid, late_line = next(work), next(work)
        late = Reduce(mover, (late_mid, None, late_mid, late_line), late_out, None, None)
    bias, gain2_ref, gain1_ref = [next(work) for _ in range(3)]
    if plan.joined:
        split, local = next(work), next(work)
        early_held, early_got, late_held, late_got = [next(work) for _ in range(4)]
        tops = 8 * (plan.others + 1)
        early = SmallSums(mover, tops, early_held, early_got)
        final = SmallSums(mover, 8, late_held, late_got)
        everything = [(split, local)] + others

    greet(mover, plan.inside)
    gain_loads = [mover.stay(far_gain2, gain2_ref), mover.stay(far_gain1, gain1_ref)]
    one = Round(mover, rows, attn_grad, one_work)
    two = Round(mover, rows, following, two_work)
    if plan.final:
        far[13] = far[13].at[two.rows(two.own)]
    load = [mover.stay(there, here) for there, here in zip(far[:3], near[:3])]
    if late:
        mover.near(mover.stay(late_far, late_mid))
        late.send_first()
        late.send_second()
    if plan.last:
        chunk = rows // 5 if rows % 80 == 0 else rows

        def mask_step(i, carry):
            at = pl.ds(pl.multiple_of(i * chunk, 16), chunk)
            value = source[at, :].astype(FULL)
            grad[at, :] = live_rows(value, i * chunk, live_ref[0, mover.ctx]).astype(LOW)
            return carry

        lax.fori_loop(0, rows // chunk, mask_step, 0)
    key_bias(mover, live_ref, bias)
    mover.near(*gain_loads)
    gain2, gain1 = [
        ref[...].astype(FULL)[plan.layer : plan.layer + 1] for ref in (gain2_ref, gain1_ref)
    ]
    split[...] = jnp.zeros_like(split)
    local[...] = jnp.zeros_like(local)
    split[5:6, 0:width] = jnp.sum(
        grad[one.rows(one.own), :].astype(FULL), axis=0, keepdims=True
    )
    mover.near(*load[:3])
    load += [mover.stay(there, here) for there, here in zip(far[3:], near[3:])]
    hidden_width = slope.shape[1]

    def mlp_part(start):
        at = one.rows(start)
        pre = jnp.dot(grad[at, :], w_down[...], preferred_element_type=FULL)
        low = (pre * slope[at, :].astype(FULL)).astype(LOW)
        pre_grad[at, :] = low
        local[0:1, 0:hidden_width] += jnp.sum(low.astype(FULL), axis=0, keepdims=True)
        return dot(low, w_up[...], ((1,), (1,)))

    def to_attn(at, value):
        if plan.last:
            above = grad[one.rows(one.own + at.start, at.size), :].astype(FULL)
        else:
            above = x_ref[at]
        _, normed, inverse = normalize(middle[at], 1.0, 0.0)
        result = above + normalize_back(value, normed, inverse, gain2)
        stream[at] = result
        low = result.astype(LOW)
        sums_into(split, 2, at, (value * normed, value, low.astype(FULL)))
        return low

    def reduce(name):
        if name in reduces:
            reduces[name].begin_blocks()

    def own(name):
        if name in reduces:
            reduces[name].own()

    def first_step(name):
        if name in reduces:
            reduces[name].fold_blocks(3)
            reduces[name].send_first()

    def second_step(name):
        if name in reduces:
            reduces[name].fold_blocks(2)
            reduces[name].send_third()

    def rest(name):
        if name in reduces:
            reduces[name].fold_blocks(1)
            reduces[name].send_second()
            reduces[name].fold_blocks(0)

    def begin_early():
        if plan.joined:
            early_held[0] = jnp.zeros(early_held.shape[1:], FULL)
            for layer, (some, more) in enumerate(everything):
                first_row = 0 if layer else 2
                for row in range(first_row, 6):
                    at = row * len(everything) + layer
                    early_held[0, at : at + 1, :] = some[row : row + 1, :]
                for row in range(2 if layer else 1):
                    at = tops + row * len(everything) + layer
                    early_held[0, at : at + 1, :] = more[row : row + 1, :]

    def early_step():
        if plan.joined:
            early.step()

    def start_down():
        mover.near(*load[3:5])
        reduce("down")

    one.eager(mlp_part, to_attn, start_down)
    if late:
        late.send_third()
    mover.near(load[5])
    reduce("up")
    one.have()
    mover.near(load[6])
    turned_product(attn_grad, w_out, None, parts)

    def waiting():
        begin_early()
        early_step()
        own("down")
        first_step("down")
        mover.near(load[7])
        reduce("out")
        own("out")

    def ready():
        own("up")
        mover.near(load[8], load[9], load[10])

    def between(turn):
        if turn == 0:
            early_step()
        if turn == 3:
            second_step("down")
            first_step("up")
            rest("down")

    attend_back_part(
        size,
        tile,
        mover,
        parts,
        bias,
        qkv,
        o_ref,
        lse,
        grads,
        attend_work,
        ready,
        waiting,
        lambda: None,
        between,
    )
    early_step()
    nat[...] = turned(grads[...])
    pairs_width = nat.shape[1] // 3 * 2
    picked = jnp.dot(
        nat[...], pair_columns(pairs_width, nat.shape[1], size, True), preferred_element_type=FULL
    )
    local[1:2, 0:pairs_width] = jnp.sum(picked, axis=0, keepdims=True)
    mover.near(*load[11:])

    def qkv_part(start):
        return dot(nat[two.rows(start), :], w_qkv[...], ((1,), (1,)))

    def to_following(at, value):
        row = before[at, :].astype(FULL)
        _, normed, inverse = normalize(row, 1.0, 0.0)
        result = stream[at] + normalize_back(value, normed, inverse, gain1)
        stream[at] = result
        low = result.astype(LOW)
        sums_into(split, 0, at, (value * normed, value))
        return low

    def meanwhile():
        own("qkv")
        second_step("up")
        first_step("out")
        rest("up")
        early_step()

    def halfway():
        if plan.inside:
            reduces["qkv"].fold_blocks(3)
            if plan.final:
                reduces["qkv"].send_first()

    reduce("qkv")
    two.eager(qkv_part, to_following, meanwhile, halfway)
    if plan.joined:
        late_held[0, 0:8, :] = jnp.zeros((8, late_held.shape[2]), FULL)
        late_held[0, 0:2, :] = split[0:2, :]
        late_held[0, 8:16, :] = local[...]
        final.step()
        early_step()
        final.step()
    second_step("out")
    rest("out")
    two.have_mate_own()
    two.have_other()
    if plan.joined:
        final.step()
        final.step()
    if plan.inside:
        last = reduces["qkv"]
        if plan.final:
            second_step("qkv")
            rest("qkv")
        else:
            last.fold_blocks(2, 1, 0)
            mover.stay(last.mid, mid_out)
    two.have_mate_other()
    if plan.joined:
        final.step()
    for name in ("down", "up", "out"):
        if name in reduces:
            reduces[name].done()
    if late:
        late.done()
    if plan.inside and plan.final:
        reduces["qkv"].done()
    if plan.joined:
        final.step()
        early.step()
        totals[...] = early.value()
        last_value = final.value()
        for row in range(2):
            at = row * len(everything)
            totals[at : at + 1, :] = last_value[row : row + 1, :]
        at = tops + len(everything)
        totals[at : at + 1, :] = last_value[9:10, :]
    if not plan.inside:
        for name, (lhs, rhs) in {
            "down": (grad, hidden),
            "up": (second, pre_grad),
            "out": (attn_grad, heads),
            "qkv": (first, nat),
        }.items():
            full = Reduce(mover, (wholes[name],) * 4, None, lhs, rhs)
            full.compute(wholes[name], 0)
    mover.settle()


def gather_outputs_kernel(layers, *refs):
    count = layers * len(NAMES)
    parts, token_grads, mixed, totals = refs[:count], refs[count], refs[count + 1], refs[count + 2]
    outs, work = refs[count + 3 : count + 17], refs[count + 17 : -2]
    into, out_of = refs[-2:]
    coming, going = [], []
    pairs = [(mixed, work[4], outs[4].at[0])]
    for index in range(len(NAMES)):
        for layer in range(layers):
            pairs.append(
                (parts[index * layers + layer], work[index].at[layer], outs[index].at[layer])
            )
    for i, (source, stage, _) in enumerate(pairs):
        coming.append(pltpu.make_async_copy(source, stage, into.at[i]))
        coming[-1].start()
    outs[5][0] = token_grads[...].astype(FULL)
    for row, out in enumerate(outs[6:12]):
        out[...] = totals[row * layers : (row + 1) * layers, 0 : out.shape[1]]
    for row, out in enumerate(outs[12:14]):
        row = row + 8
        out[...] = totals[row * layers : (row + 1) * layers, 0 : out.shape[1]]
    for i, (_, stage, target) in enumerate(pairs):
        coming[i].wait()
        going.append(pltpu.make_async_copy(stage, target, out_of.at[i]))
        going[-1].start()
    for copy in going:
        copy.wait()


def gather_outputs(done, token_grads, mixed, totals, layers, widths):
    rows, width = token_grads.shape
    parts = [done[name, layer] for name in NAMES for layer in range(layers)]
    hbm, whole = pl.BlockSpec(memory_space=HBM), lambda shape: pl.BlockSpec(
        shape, lambda i: (0,) * len(shape)
    )
    shapes = [(layers,) + done[name, 0].shape for name in NAMES] + [(1, rows, width)] * 2
    types = [FULL] * 4 + [LOW, FULL]
    small = [(layers, width)] * 6 + [(layers, count) for count in widths]
    copies = len(parts) + 1
    return pl.pallas_call(
        functools.partial(gather_outputs_kernel, layers),
        grid=(1,),
        in_specs=[hbm] * len(parts) + [whole(token_grads.shape), hbm, whole(totals.shape)],
        out_specs=[hbm] * 5 + [whole(shape) for shape in shapes[5:] + small],
        out_shape=[jax.ShapeDtypeStruct(*pair) for pair in zip(shapes, types)]
        + [jax.ShapeDtypeStruct(shape, FULL) for shape in small],
        scratch_shapes=[VMEM(shape, FULL) for shape in shapes[:4]]
        + [VMEM((rows, width), LOW)]
        + [pltpu.SemaphoreType.DMA((copies,)), pltpu.SemaphoreType.DMA((copies,))],
        compiler_params=pltpu.CompilerParams(vmem_limit_bytes=60 * 2**20),
        name="gather_outputs",
    )(*parts, token_grads, mixed, totals)


class BackPlan:
    def __init__(self, layer, layers, inside):
        self.inside, self.layer = inside, layer
        self.last, self.final = layer == layers - 1, layer == 0
        self.late = inside and not self.last
        self.joined = inside and self.final
        self.others = layers - 1 if self.joined else 0


def back_layer(source, x, live, gain2, gain1, saved, late, others, plan, size, sizes, ident):
    rows, width = source.shape
    count = sizes[0]
    slope, w_down, w_up = saved[:3]
    hidden, joint, attn = slope.shape[1], saved[12].shape[1], saved[6].shape[1]
    slots, span = count * rows, rows // 4
    tile = 512 if slots % 512 == 0 else PAD
    wide = max(width, hidden, joint)
    half = width // 2
    block = half // count
    columns = {"qkv": joint, "out": attn, "up": hidden, "down": hidden}
    inputs = [(source, VMEM)] + ([] if plan.last else [(x, VMEM)])
    inputs += [(live, SMEM), (gain2, HBM), (gain1, HBM)]
    inputs += [(value, HBM) for value in saved]
    if plan.late:
        inputs.append((late, HBM))
    for pair in others[: plan.others]:
        inputs += [(value, VMEM) for value in pair]
    outputs = [((span, width), FULL, VMEM), ((rows, width), LOW, VMEM)]
    names = [name for name in NAMES if plan.inside and (name != "qkv" or plan.final)]
    outputs += [((block, columns[name]), FULL, VMEM) for name in names]
    if plan.inside and not plan.final:
        outputs.append(((half, joint), LOW, HBM))
    if plan.late:
        outputs.append(((block, joint), FULL, VMEM))
    depth = 8 * (plan.others + 1)
    if plan.joined:
        outputs.append(((depth + 8, wide), FULL, VMEM))
    else:
        outputs += [((8, wide), FULL, VMEM)] * 2
    if not plan.inside:
        outputs += [((width, columns[name]), LOW, VMEM) for name in NAMES]
    scratch = [VMEM(value.shape, value.dtype) for value in saved]
    scratch[13] = VMEM((span, width), saved[13].dtype)
    if plan.last:
        scratch.append(VMEM((rows, width), LOW))
    scratch += [
        VMEM((rows, hidden), LOW),
        VMEM((rows, width), LOW),
        VMEM((attn, rows), LOW),
        VMEM((joint, rows), LOW),
        VMEM((rows, joint), LOW),
    ]
    scratch += attend_back_buffers(size, count, rows)
    scratch += round_buffers(rows, width) + round_buffers(rows, width)
    if plan.inside:
        for name in ("down", "up", "out", "qkv"):
            scratch += reduce_buffers(half, columns[name], count)
    if plan.late:
        scratch += [VMEM((half, joint), LOW), VMEM((count - 1, block, joint), LOW)]
    scratch.append(VMEM((16, slots), LOW))
    scratch += [VMEM(value.shape, value.dtype) for value in (gain2, gain1)]
    assert 2 * (plan.others + 1) <= 8
    if plan.joined:
        scratch += [VMEM((8, wide), FULL)] * 2
        scratch += [
            VMEM((6, depth + 8, wide), FULL),
            VMEM((5, depth + 8, wide), FULL),
            VMEM((6, 16, wide), FULL),
            VMEM((5, 16, wide), FULL),
        ]
    results = run(
        functools.partial(back_kernel, plan, size, tile),
        "back_layer",
        ident,
        inputs,
        outputs,
        scratch,
        3 * (count - 1) + 2 * ROUND_COPIES + 8 * count + 10 + count,
        len(saved) + 4,
        sizes,
        58,
        6 * rows * width * (2 * hidden + attn + joint) + 10 * slots * slots * 256,
    )
    return results[:2], names, results[2:]


def shards(
    tokens,
    block_tokens,
    ln1_gain,
    ln1_bias,
    w_qkv,
    b_qv,
    w_out,
    b_out,
    ln2_gain,
    ln2_bias,
    w_up,
    b_up,
    w_down,
    b_down,
    cotangent,
):
    images, capacity, width = tokens.shape
    assert images == 1
    layers = w_qkv.shape[0]
    size = HEAD_DIM
    ctx_count = lax.axis_size("ctx")
    ctx_place = lax.axis_index("ctx")
    joint_width = w_qkv.shape[2]
    heads = joint_width // (3 * size)
    assert heads == ctx_count
    attn_width = heads * size
    hidden_width = w_up.shape[2]
    weights = {"qkv": w_qkv, "out": w_out, "up": w_up, "down": w_down}
    sizes = (ctx_count, lax.axis_size("shard"))
    inside = sizes == (4, 2)
    gathered = {}
    if not inside:
        for name, value in weights.items():
            for layer in range(layers):
                gathered[name, layer] = gather_weight(value[layer])[0]
    source, stream = tokens[0], None
    saved = []
    for layer in range(layers):
        last = layer == layers - 1
        result, following, kept = forward_layer(
            source,
            stream,
            block_tokens,
            (b_out, ln2_gain, ln2_bias, b_down, ln1_gain, ln1_bias, b_up, b_qv),
            gathered,
            weights,
            Plan(layer, last, inside),
            last,
            size,
            sizes,
            1 + layer,
        )
        before = stream if layer else source
        first = source if layer else kept[8]
        saved.append((before, first) + tuple(kept[:8]))
        source, stream = following, result
    mixed = source

    done, packs = {}, {}
    source, stream, late = cotangent[0], None, None
    for layer in reversed(range(layers)):
        before, first, qkv, head_out, lse, heads_low, middle, second, hidden, slope = saved[layer]
        plan = BackPlan(layer, layers, inside)
        whole = {name: gathered[name, layer] for name in NAMES}
        near = [slope, whole["down"], whole["up"], middle, hidden, second, whole["out"]]
        near += [heads_low, qkv, head_out, lse, first, whole["qkv"], before]
        others = [packs[key] for key in sorted(packs)]
        (stream, source), names, rest = back_layer(
            source, stream, block_tokens, ln2_gain, ln1_gain, near, late, others, plan, size, sizes, 1 + layers + layer
        )
        rest = iter(rest)
        for name in names:
            done[name, layer] = next(rest)
        if plan.inside and not plan.final:
            late = next(rest)
        if plan.late:
            done["qkv", layer + 1] = next(rest)
        if plan.joined:
            totals = next(rest)
        else:
            packs[layer] = (next(rest), next(rest))
        if not inside:
            for name in NAMES:
                value = next(rest)
                done[name, layer] = scatter_weight(
                    lambda start, count, value=value: rows_of(value, start, count).astype(FULL),
                    width,
                )
    if not inside:
        split = total_over(("tp",), jnp.stack([packs[l][0] for l in range(layers)], axis=1))
        local = jnp.stack([packs[l][1] for l in range(layers)], axis=1)
        totals = total_over(("shard", "ctx"), jnp.concatenate([split, local[:2]]))
        totals = totals.reshape(10 * layers, -1)
    pairs = b_qv.shape[1]
    outs = gather_outputs(done, source, mixed, totals, layers, (hidden_width, pairs))
    g_qkv, g_out, g_up, g_down, mixed, token_grads = outs[:6]
    g_ln1_gain, g_ln1_bias, g_ln2_gain, g_ln2_bias, g_b_out, g_b_down, g_b_up, g_b_qv = outs[6:]
    return (
        mixed,
        token_grads,
        g_ln1_gain,
        g_ln1_bias,
        g_qkv,
        g_b_qv,
        g_out,
        g_b_out,
        g_ln2_gain,
        g_ln2_bias,
        g_up,
        g_b_up,
        g_down,
        g_b_down,
    )


def solution(mesh):
    split_rows = P(None, ("shard", "ctx"), "tp")
    split_tokens = P("shard", "ctx", None)
    return jax.shard_map(
        shards,
        mesh=mesh,
        in_specs=(
            split_tokens,
            P("shard", None),
            P(),
            P(),
            split_rows,
            P(None, "tp"),
            split_rows,
            P(),
            P(),
            P(),
            split_rows,
            P(None, "tp"),
            split_rows,
            P(),
            split_tokens,
        ),
        out_specs=(
            split_tokens,
            split_tokens,
            P(),
            P(),
            split_rows,
            P(None, "tp"),
            split_rows,
            P(),
            P(),
            P(),
            split_rows,
            P(None, "tp"),
            split_rows,
            P(),
        ),
        check_vma=False,
    )
```

```python
import functools
import math

import jax
import jax.numpy as jnp
from jax import lax
from jax.experimental import pallas as pl
from jax.experimental.pallas import tpu as pltpu
from jax.sharding import PartitionSpec as P

HEAD_DIM = 64
EPSILON = 1e-06
NEG_LARGE = -1e30
LOW = jnp.bfloat16
FULL = jnp.float32
PAD = 128
MESH = pl.DeviceIdType.MESH
VMEM = pltpu.VMEM
HBM = pltpu.HBM
SMEM = pltpu.SMEM


def bits_of(axis):
    size = lax.axis_size(axis)
    assert size & (size - 1) == 0
    return [1 << i for i in range(size.bit_length() - 1)]


def swap(value, axis, bit):
    size = lax.axis_size(axis)
    return lax.ppermute(value, axis, [(i, i ^ bit) for i in range(size)])


def side_of(axis, bit):
    return (lax.axis_index(axis) // bit) % 2


def rows_of(value, start, count, axis=0):
    return lax.dynamic_slice_in_dim(value, start, count, axis)


def halve(axis, bits, partial, total):
    offset, span, received = jnp.int32(0), total, []

    def summed(start, count):
        value = partial(start, count)
        for got, base in received:
            value = value + rows_of(got, start - base, count).astype(FULL)
        return value

    for bit in bits:
        half = span // 2
        side = side_of(axis, bit)
        got = swap(summed(offset + (1 - side) * half, half).astype(LOW), axis, bit)
        offset = offset + side * half
        received.append((got, offset))
        span = half
    return summed(offset, span)


def double(axis, bits, value):
    for bit in bits:
        got = swap(value, axis, bit)
        first = side_of(axis, bit) == 0
        value = jnp.concatenate(
            [jnp.where(first, value, got), jnp.where(first, got, value)], axis=0
        )
    return value


def total_over(axes, value):
    for axis in axes:
        for bit in bits_of(axis):
            value = value + swap(value, axis, bit)
    return value


def ring(value, by):
    count = lax.axis_size("ctx")
    return lax.ppermute(value, "ctx", [(i, (i + by) % count) for i in range(count)])


def gather_weight(piece):
    count = lax.axis_size("ctx")
    place = lax.axis_index("ctx")
    ways = lax.axis_size("shard")
    blocks = [piece] + [ring(piece, by) for by in range(1, count)]
    whole = jnp.zeros((ways * count,) + piece.shape, piece.dtype)
    me = lax.axis_index("shard")
    for by, block in enumerate(blocks):
        at = (place - by) % count
        held = [(jnp.int32(0), block)]
        for bit in bits_of("shard"):
            held = held + [(other ^ bit, swap(value, "shard", bit)) for other, value in held]
        for other, value in held:
            whole = lax.dynamic_update_index_in_dim(whole, value, (me ^ other) * count + at, 0)
    return whole.reshape((ways * count * piece.shape[0],) + piece.shape[1:]), blocks[-1]


def scatter_weight(partial, total):
    count = lax.axis_size("ctx")
    place = lax.axis_index("ctx")
    mine = halve("shard", bits_of("shard")[::-1], partial, total).astype(LOW)
    mine = mine.reshape((count, mine.shape[0] // count) + mine.shape[1:])
    value = lax.dynamic_index_in_dim(mine, place, 0, False).astype(FULL)
    for by in range(1, count):
        given = lax.dynamic_index_in_dim(mine, (place + by) % count, 0, False)
        value = value + ring(given, by).astype(FULL)
    return value


def dot(left, right, contract):
    return lax.dot_general(
        left, right, ((contract[0], contract[1]), ((), ())), preferred_element_type=FULL
    )


def turned(value):
    return value.astype(FULL).T.astype(LOW)


def normalize(rows, gain, shift):
    row_mean = jnp.mean(rows, axis=-1, keepdims=True)
    centred = rows - row_mean
    inverse = lax.rsqrt(jnp.mean(centred * centred, axis=-1, keepdims=True) + EPSILON)
    normed = centred * inverse
    return (normed * gain + shift, normed, inverse)


def normalize_back(grad_out, normed, inverse, gain):
    scaled = grad_out * gain
    mean_grad = jnp.mean(scaled, axis=-1, keepdims=True)
    mean_cross = jnp.mean(scaled * normed, axis=-1, keepdims=True)
    return inverse * (scaled - mean_grad - normed * mean_cross)


def gelu_pair(value):
    spread = 0.5 * (1.0 + lax.erf(value * (0.5**0.5)))
    slope = spread + value * jnp.exp(-0.5 * value * value) * (1.0 / math.sqrt(2.0 * math.pi))
    return (value * spread).astype(LOW), slope.astype(LOW)


class Mover:
    def __init__(self, sizes, send, recv, local):
        self.ctx_count, self.shard_count = sizes
        self.send, self.recv, self.local = send, recv, local
        self.copies, self.here = [], []
        self.arrived = set()
        self.landed = set()
        self.ctx = lax.axis_index("ctx")
        self.shard = lax.axis_index("shard")

    def go(self, source, target, **device):
        index = len(self.copies)
        assert index < self.send.shape[0]
        copy = pltpu.make_async_remote_copy(
            src_ref=source,
            dst_ref=target,
            send_sem=self.send.at[index],
            recv_sem=self.recv.at[index],
            device_id=device,
            device_id_type=MESH,
        )
        copy.start()
        self.copies.append(copy)
        return index

    def stay(self, source, target):
        index = len(self.here)
        assert index < self.local.shape[0]
        copy = pltpu.make_async_copy(source, target, self.local.at[index])
        copy.start()
        self.here.append(copy)
        return index

    def near(self, *indices):
        for index in indices:
            if index not in self.landed:
                self.landed.add(index)
                self.here[index].wait()

    def take(self, index):
        if index not in self.arrived:
            self.arrived.add(index)
            self.copies[index].wait_recv()

    def flip(self, bits):
        place = self.ctx
        if bits & 1:
            place = place + 1 - 2 * lax.rem(self.ctx, 2)
        if bits & 2:
            place = place + 2 - 4 * (self.ctx // 2)
        return place

    def on(self, by):
        return lax.rem(self.ctx + by, self.ctx_count)

    def back(self, by):
        return lax.rem(self.ctx + self.ctx_count - by, self.ctx_count)

    def settle(self):
        for index, copy in enumerate(self.copies):
            self.take(index)
            copy.wait_send()
        self.near(*range(len(self.here)))


class Gather:
    def __init__(self, mover, source, target, across=True):
        self.mover, self.source, self.target, self.across = mover, source, target, across
        self.over = []

    def start_line(self):
        mover = self.mover
        mine, there = self.source, self.block(mover.ctx)
        self.far = mover.go(mine, there, ctx=mover.flip(2))
        self.close = mover.go(mine, there, ctx=mover.flip(1))

    def start_over(self):
        mover = self.mover
        mine, there = self.source, self.block(mover.ctx)
        if self.across:
            self.over.append(mover.go(mine, there, shard=1 - mover.shard))
        self.own = mover.stay(mine, there)

    def block(self, ctx):
        mover = self.mover
        rows = self.source.shape[0]
        start = ctx * rows
        if self.across:
            start = start + mover.shard * mover.ctx_count * rows
        return self.target.at[pl.ds(pl.multiple_of(start, rows), rows)]

    def pass_on(self, stage):
        mover = self.mover
        if stage == 1:
            mover.take(self.far)
            rows = self.block(mover.flip(2))
            self.passed = mover.go(rows, rows, ctx=mover.flip(1))
        elif stage == 2:
            mover.take(self.close)
            rows = self.block(mover.flip(1))
        else:
            mover.take(self.passed)
            rows = self.block(mover.flip(3))
        if self.across:
            self.over.append(mover.go(rows, rows, shard=1 - mover.shard))

    def have(self):
        for copy in self.over:
            self.mover.take(copy)
        self.mover.near(self.own)


class Across:
    def __init__(self, mover, source, target):
        rows = source.shape[0]
        there = target.at[pl.ds(pl.multiple_of(mover.shard * rows, rows), rows)]
        self.mover = mover
        self.copy = mover.go(source, there, shard=1 - mover.shard)
        self.own = mover.stay(source, there)

    def have(self):
        self.mover.take(self.copy)
        self.mover.near(self.own)


class Reduce:
    def __init__(self, mover, buffers, out, lhs, rhs):
        self.mover, self.out, self.lhs, self.rhs = mover, out, lhs, rhs
        self.give, self.got, self.mid, self.line = buffers
        self.half = self.give.shape[0]
        self.block = self.half // mover.ctx_count

    def compute(self, target, shard):
        chunk = min(256, self.half)

        def step(i, carry):
            at = pl.ds(pl.multiple_of(shard * self.half + i * chunk, chunk), chunk)
            here = pl.ds(pl.multiple_of(i * chunk, chunk), chunk)
            target[here, :] = dot(self.lhs[:, at], self.rhs[...], ((0,), (0,))).astype(LOW)
            return carry

        lax.fori_loop(0, self.half // chunk, step, 0)

    def begin_blocks(self):
        mover = self.mover
        self.blocks = {}
        for bits in (3, 2, 1, 0):
            ctx = mover.flip(bits)
            at = pl.ds(pl.multiple_of(ctx * self.block, self.block), self.block)
            start = pl.multiple_of((1 - mover.shard) * self.half + ctx * self.block, self.block)
            lhs = self.lhs[:, pl.ds(start, self.block)]
            self.give[at, :] = dot(lhs, self.rhs[...], ((0,), (0,))).astype(LOW)
            self.blocks[bits] = mover.go(
                self.give.at[at], self.got.at[at], shard=1 - mover.shard
            )

    def own(self):
        self.compute(self.mid, self.mover.shard)

    def fold_blocks(self, *which):
        mover = self.mover
        for bits in which:
            mover.take(self.blocks[bits])
            ctx = mover.flip(bits)
            at = pl.ds(pl.multiple_of(ctx * self.block, self.block), self.block)
            self.mid[at, :] = (
                self.mid[at, :].astype(FULL) + self.got[at, :].astype(FULL)
            ).astype(LOW)

    def rows(self, ctx):
        return self.mid.at[pl.ds(pl.multiple_of(ctx * self.block, self.block), self.block)]

    def send_first(self):
        mover = self.mover
        self.first = mover.go(self.rows(mover.flip(3)), self.line.at[1], ctx=mover.flip(1))

    def send_second(self):
        mover = self.mover
        self.second = mover.go(self.rows(mover.flip(1)), self.line.at[0], ctx=mover.flip(1))

    def send_third(self):
        mover = self.mover
        mover.take(self.first)
        rows = self.rows(mover.flip(2))
        rows[...] = (rows[...].astype(FULL) + self.line[1].astype(FULL)).astype(LOW)
        self.third = mover.go(rows, self.line.at[2], ctx=mover.flip(2))

    def done(self):
        self.mover.take(self.second)
        self.mover.take(self.third)
        value = self.rows(self.mover.ctx)[...].astype(FULL)
        self.out[...] = value + self.line[0].astype(FULL) + self.line[2].astype(FULL)


def reduce_buffers(half, width, count):
    return [
        VMEM((half, width), LOW),
        VMEM((half, width), LOW),
        VMEM((half, width), LOW),
        VMEM((count - 1, half // count, width), LOW),
    ]


def greet(mover, shard):
    barrier = pltpu.get_barrier_semaphore()
    peers = [dict(ctx=mover.on(by)) for by in range(1, mover.ctx_count)]
    peers += [dict(tp=peer) for peer in tp_peers()]
    if shard:
        peers.append(dict(shard=1 - mover.shard))
    for peer in peers:
        pl.semaphore_signal(barrier, inc=1, device_id=peer, device_id_type=MESH)
    pl.semaphore_wait(barrier, len(peers))


def tp_peers():
    place = lax.axis_index("tp")
    core, far = lax.rem(place, 2), place // 2
    return place + 1 - 2 * core, place + 2 - 4 * far


def run(kernel, name, ident, inputs, outputs, scratch, remote, local, sizes, vmem, flops):
    n_in, n_out, n_scratch = len(inputs), len(outputs), len(scratch)

    def body(*refs):
        ins, outs = refs[:n_in], refs[n_in : n_in + n_out]
        work = refs[n_in + n_out :]
        mover = Mover(sizes, *work[n_scratch:])
        kernel(mover, ins, outs, work[:n_scratch])

    return pl.pallas_call(
        body,
        in_specs=[pl.BlockSpec(memory_space=space) for _, space in inputs],
        out_specs=[pl.BlockSpec(memory_space=space) for _, _, space in outputs],
        out_shape=[jax.ShapeDtypeStruct(shape, dtype) for shape, dtype, _ in outputs],
        scratch_shapes=list(scratch)
        + [
            pltpu.SemaphoreType.DMA((remote,)),
            pltpu.SemaphoreType.DMA((remote,)),
            pltpu.SemaphoreType.DMA((local,)),
        ],
        compiler_params=pltpu.CompilerParams(
            collective_id=ident, has_side_effects=True, vmem_limit_bytes=vmem * 2**20
        ),
        cost_estimate=pl.CostEstimate(flops=flops, bytes_accessed=2**24, transcendentals=0),
        name=name,
    )(*[value for value, _ in inputs])


def order_of(block, count):
    return (block + count - 1) % count


def tiles_of(count, capacity, tile):
    ends = [-(-(p + 1) * capacity // tile) for p in range(count)]
    return list(zip([0] + ends[:-1], ends))


def tile_at(t, tile):
    return pl.ds(pl.multiple_of(t * tile, tile), tile)


def turned_product(left, right, bias, target):
    value = jnp.dot(left[...], right[...], preferred_element_type=FULL)
    if bias is not None:
        value = value + bias[0:1, :]
    target[...] = turned(value.astype(LOW))


def head_rows(ref, head, width):
    return ref.at[pl.ds(pl.multiple_of(head * width, 16), width)]


def attend_part(size, tile, mover, joint, bias, heads, qkv, o_ref, lse, work, after_send, begun, between):
    k_ref, q_ref, v_ref, low_ref, score_ref, top_ref = work
    count, width, capacity = qkv.shape
    slots = count * capacity
    sent = [None] + [
        mover.go(head_rows(joint, mover.on(by), width), qkv.at[by], ctx=mover.on(by))
        for by in range(1, count)
    ]
    after_send()
    qkv[0] = head_rows(joint, mover.ctx, width)[...]
    q_ref[size:PAD, :] = jnp.concatenate(
        [jnp.ones((16, slots), LOW), jnp.zeros((PAD - size - 16, slots), LOW)], axis=0
    )

    v_ref[size : size + 16, :] = jnp.ones((16, slots), LOW)

    def prepare(r):
        here = slice(r * capacity, (r + 1) * capacity)
        p = order_of(r, count)
        q_ref[0:size, p * capacity : (p + 1) * capacity] = (
            qkv[r, 0:size, :] * (size**-0.5)
        ).astype(LOW)
        v_ref[0:size, here] = qkv[r, 2 * size : 3 * size, :]
        keys = jnp.concatenate(
            [qkv[r, size : 2 * size, :], bias[:, here], jnp.zeros((PAD - size - 16, capacity), LOW)],
            axis=0,
        )
        k_ref[here, :] = turned(keys)

    prepare(0)
    for by in range(1, count):
        mover.take(sent[by])
        prepare(by)

    begun()
    last = slots // tile - 1
    assert last % 2 == 1

    def phase(t, now, following, then):
        at, ahead = tile_at(t, tile), tile_at(following, tile)
        top = top_ref[now, 0:1, :]
        summed = jnp.zeros((size + 16, tile), FULL)
        new_top = jnp.full((1, tile), NEG_LARGE, FULL)
        for r in range(count):
            here = slice(r * capacity, (r + 1) * capacity)
            scores = jnp.dot(k_ref[here, :], q_ref[:, ahead], preferred_element_type=FULL)
            score_ref[then, here, :] = scores
            new_top = jnp.maximum(new_top, jnp.max(scores, axis=0, keepdims=True))
            weights = jnp.exp(score_ref[now, here, :] - top)
            summed = summed + jnp.dot(
                v_ref[:, here], weights.astype(LOW), preferred_element_type=FULL
            )
        top_ref[then] = jnp.broadcast_to(new_top, (8, tile))
        total = summed[size : size + 1]
        out = summed[0:size] / total
        o_ref[:, at] = out
        low_ref[:, at] = out.astype(LOW)
        lse[:, at] = jnp.broadcast_to(top + jnp.log(total), (8, tile))

    def step(i, carry):
        phase(2 * i, 0, 2 * i + 1, 1)
        phase(2 * i + 1, 1, jnp.minimum(2 * i + 2, last), 0)
        return carry

    scores = jnp.dot(k_ref[...], q_ref[:, 0:tile], preferred_element_type=FULL)
    score_ref[0] = scores
    top_ref[0] = jnp.broadcast_to(jnp.max(scores, axis=0, keepdims=True), (8, tile))
    arriving = []
    for p, (low, high) in enumerate(tiles_of(count, capacity, 2 * tile)):
        lax.fori_loop(low, high, step, 0)
        done = low_ref.at[:, p * capacity : (p + 1) * capacity]
        if p < count - 1:
            there = head_rows(heads, mover.ctx, size)
            arriving.append(mover.go(done, there, ctx=mover.back(p + 1)))
        else:
            head_rows(heads, mover.ctx, size)[...] = low_ref[:, p * capacity : (p + 1) * capacity]
        between(p + 1)
    for copy in arriving:
        mover.take(copy)


def below(row, ones):
    width = row.shape[1]
    high = row.astype(LOW).astype(FULL)
    middle = (row - high).astype(LOW).astype(FULL)
    low = row - high - middle
    lead = jnp.full((1, width), 1.0 if ones else 0.0, FULL)
    rest = jnp.zeros((PAD // 2 - 4, width), FULL)
    return jnp.concatenate([lead, high, middle, low, rest], axis=0).astype(LOW)


def attend_back_part(size, tile, mover, parts, bias, qkv, o_ref, lse, grads, work, ready, waiting, begun, between):
    k_ref, v_ref, q_ref, do_ref, nat_ref, dq_ref, dk_ref, dv_ref, got, back = work
    count, width, capacity = qkv.shape
    slots = count * capacity
    sent = [None] + [
        mover.go(head_rows(parts, mover.on(by), size), got.at[by], ctx=mover.on(by))
        for by in range(1, count)
    ]
    got[0] = head_rows(parts, mover.ctx, size)[...]
    waiting()
    ready()
    q_ref[size:PAD, :] = below(lse[0:1, :], True)
    dq_ref[...] = jnp.zeros_like(dq_ref)
    off = (lax.broadcasted_iota(jnp.int32, (16, capacity), 0) + 2) // 3
    taken = jnp.where(off == 1, -1.0, 0.0).astype(LOW)
    pad = jnp.zeros((PAD - size - 16, capacity), LOW)
    for r in range(count):
        here = slice(r * capacity, (r + 1) * capacity)
        k_ref[here, :] = turned(
            jnp.concatenate([qkv[r, size : 2 * size, :], bias[:, here] + taken, pad], axis=0)
        )
        v_ref[here, :] = turned(
            jnp.concatenate([qkv[r, 2 * size : 3 * size, :], taken, pad], axis=0)
        )
    for r in range(count):
        if r:
            mover.take(sent[r])
        p = order_of(r, count)
        at = slice(p * capacity, (p + 1) * capacity)
        scaled = (qkv[r, 0:size, :] * (size**-0.5)).astype(LOW)
        dout = got[r]
        q_ref[0:size, at] = scaled
        do_ref[0:size, at] = dout
        nat_ref[at, :] = turned(jnp.concatenate([scaled, dout], axis=0))
        delta = jnp.sum(dout.astype(FULL) * o_ref[:, at], axis=0, keepdims=True)
        do_ref[size:PAD, at] = below(delta, False)

    begun()
    tiles = tiles_of(count, capacity, tile)
    arriving = []
    mine = head_rows(grads, mover.ctx, width)
    for turn, r in enumerate(list(range(1, count)) + [0]):
        here = slice(r * capacity, (r + 1) * capacity)
        dk_ref[...] = jnp.zeros_like(dk_ref)
        dv_ref[...] = jnp.zeros_like(dv_ref)

        def step(t, carry, r=r, here=here):
            at = tile_at(t, tile)
            scores = jnp.dot(k_ref[here, :], q_ref[:, at], preferred_element_type=FULL)
            chance = jnp.exp(scores)
            chance_grad = jnp.dot(v_ref[here, :], do_ref[:, at], preferred_element_type=FULL)
            score_grad = (chance * chance_grad).astype(LOW)
            dq_ref[:, at] += jnp.dot(
                qkv[r, size : 2 * size, :], score_grad, preferred_element_type=FULL
            )
            dk_ref[...] += jnp.dot(score_grad, nat_ref[at, :], preferred_element_type=FULL)
            dv_ref[...] += jnp.dot(
                chance.astype(LOW), nat_ref[at, :], preferred_element_type=FULL
            )
            return carry

        if r:
            lax.fori_loop(0, tiles[-1][1], step, 0)
        else:
            for p, (low, high) in enumerate(tiles):
                lax.fori_loop(low, high, step, 0)
                at = slice(p * capacity, (p + 1) * capacity)
                value = (dq_ref[:, at] * (size**-0.5)).astype(LOW)
                if p < count - 1:
                    back[p + 1, 0:size, :] = value
                    arriving.append(
                        mover.go(
                            back.at[p + 1, 0:size], mine.at[0:size], ctx=mover.back(p + 1)
                        )
                    )
                else:
                    mine[0:size, :] = value
        keys = dk_ref[...].T[0:size].astype(LOW)
        values = dv_ref[...].T[size : 2 * size].astype(LOW)
        if r:
            back[r, size : 2 * size, :] = keys
            back[r, 2 * size : 3 * size, :] = values
            arriving.append(
                mover.go(
                    back.at[r, size : 3 * size], mine.at[size : 3 * size], ctx=mover.back(r)
                )
            )
        else:
            mine[size : 2 * size, :] = keys
            mine[2 * size : 3 * size, :] = values
        between(turn)
    for copy in arriving:
        mover.take(copy)


def attend_back_buffers(size, count, capacity):
    slots = count * capacity
    return [
        VMEM((slots, PAD), LOW),
        VMEM((slots, PAD), LOW),
        VMEM((PAD, slots), LOW),
        VMEM((PAD, slots), LOW),
        VMEM((slots, PAD), LOW),
        VMEM((size, slots), FULL),
        VMEM((capacity, PAD), FULL),
        VMEM((capacity, PAD), FULL),
        VMEM((count, size, capacity), LOW),
        VMEM((count, 3 * size, capacity), LOW),
    ]


class Round:
    def __init__(self, mover, rows, full, buffers):
        place = lax.axis_index("tp")
        core, far = lax.rem(place, 2), place // 2
        self.mover, self.full = mover, full
        self.give, self.ra, self.passing, self.rb, self.keep = buffers
        self.span = rows // 4
        self.half = self.span // 2
        self.mate, self.far = tp_peers()

        def quarter(c, f):
            return (c * 2 + f) * self.span

        self.own, self.other = quarter(core, far), quarter(core, 1 - far)
        self.mate_own, self.mate_other = quarter(1 - core, far), quarter(1 - core, 1 - far)

    def rows(self, start, count=None):
        return pl.ds(pl.multiple_of(start, 16), count or self.span)

    def hand(self, slot, value):
        self.give[slot] = value.astype(LOW)
        return self.mover.go(self.give.at[slot], self.ra.at[slot], tp=self.mate)

    def onward(self, value, index):
        self.mover.take(index)
        self.passing[...] = (value + self.ra[1].astype(FULL)).astype(LOW)
        return [
            self.mover.go(self.passing.at[at], self.rb.at[at], tp=self.far)
            for at in (pl.ds(0, self.half), pl.ds(self.half, self.half))
        ]

    def close(self, far_copies, index, finish, halfway=None):
        self.mover.take(index)
        self.keep[...] += self.ra[0].astype(FULL)
        self.to_far, self.to_mate = [], []
        for c in range(2):
            at = pl.ds(c * self.half, self.half)
            self.mover.take(far_copies[c])
            low = finish(at, self.keep[at] + self.rb[at].astype(FULL))
            mine = self.full.at[self.rows(self.own + c * self.half, self.half)]
            mine[...] = low
            self.to_far.append(self.mover.go(mine, mine, tp=self.far))
            self.to_mate.append(self.mover.go(mine, mine, tp=self.mate))
            if halfway and c == 0:
                halfway()

    def eager(self, make, finish, meanwhile=None, halfway=None):
        first = self.hand(1, make(self.mate_other))
        copies = self.onward(make(self.other), first)
        second = self.hand(0, make(self.mate_own))
        self.keep[...] = make(self.own)
        if meanwhile:
            meanwhile()
        self.close(copies, second, finish, halfway)

    def after(self, before, make, finish, meanwhile, between):
        before.have_mate_own()
        second = self.hand(0, make(self.mate_own))
        self.keep[...] = make(self.own)
        before.have_other()
        between()
        value = make(self.other)
        before.have_mate_other()
        first = self.hand(1, make(self.mate_other))
        copies = self.onward(value, first)
        meanwhile()
        self.close(copies, second, finish)

    def have_mate_own(self):
        for copy in self.to_mate:
            self.mover.take(copy)

    def have_other(self):
        self.passed = []
        for c in range(2):
            self.mover.take(self.to_far[c])
            rows = self.full.at[self.rows(self.other + c * self.half, self.half)]
            self.passed.append(self.mover.go(rows, rows, tp=self.mate))

    def have_mate_other(self):
        for copy in self.passed:
            self.mover.take(copy)

    def have(self):
        self.have_mate_own()
        self.have_other()
        self.have_mate_other()


ROUND_COPIES = 10


def round_buffers(rows, width):
    span = rows // 4
    return [
        VMEM((2, span, width), LOW),
        VMEM((2, span, width), LOW),
        VMEM((span, width), LOW),
        VMEM((span, width), LOW),
        VMEM((span, width), FULL),
    ]


NAMES = ("qkv", "out", "up", "down")


def layer_kernel(plan, last, size, tile, mover, ins, outs, work):
    ins, outs, work = iter(ins), iter(outs), iter(work)
    source = next(ins)
    x_ref = None if plan.entry else next(ins)
    live_ref = next(ins)
    far_params = [next(ins) for _ in range(8)]
    stream, following = next(outs), next(outs)
    far_qkv, far_o, far_lse, far_heads, far_middle, far_second, far_hidden, far_slope = [
        next(outs) for _ in range(8)
    ]
    far_first = next(outs) if plan.entry else None
    joint, nat, heads, qkv, o_ref, lse, middle, second, hidden, slope = [
        next(work) for _ in range(10)
    ]
    first = next(work) if plan.entry else source
    attend_work = [next(work) for _ in range(6)]
    one_work, two_work = [next(work) for _ in range(5)], [next(work) for _ in range(5)]
    rows = source.shape[0]
    bias, qkv_bias = next(work), next(work)
    params = [next(work) for _ in range(8)]
    whole = {name: next(work) for name in NAMES}
    gathers, loads = {}, {}
    for name in plan.held:
        loads[name] = (next(ins), whole[name])
    half_refs = {name: next(ins) for name in plan.halves}
    for name in plan.own:
        gathers[name, 0] = Gather(mover, next(ins).at[plan.layer], whole[name])
    kept_ahead = {name: next(outs) for name in plan.ahead + plan.lines}
    for name in plan.ahead + plan.lines:
        gathers[name, 1] = Gather(
            mover, next(ins).at[plan.layer + 1], next(work), name in plan.ahead
        )
    kept = {name: next(outs) for name in plan.kept}

    greet(mover, bool(gathers))
    halves = {name: Across(mover, half_refs[name], whole[name]) for name in plan.halves}
    if plan.entry:
        gathers_first = [key for key in [("qkv", 0)] if key in gathers]
        for key in gathers_first:
            gathers[key].start_line()
            gathers[key].start_over()
    param_loads = [mover.stay(there, here) for there, here in zip(far_params, params)]
    waiting_loads = dict(loads)
    loads = {}

    def load(names):
        for name in names:
            if name in waiting_loads and name not in loads:
                loads[name] = mover.stay(*waiting_loads[name])

    load(["qkv"])

    def have(name):
        if name in waiting_loads:
            mover.near(loads[name])
            load(NAMES)
        else:
            (halves[name] if name in halves else gathers[name, 0]).have()
            mover.stay(whole[name], kept[name])
        return whole[name]

    def begin(keys):
        for key in keys:
            if key in gathers:
                gathers[key].start_line()

    def begin_over(keys):
        for key in keys:
            if key in gathers:
                gathers[key].start_over()

    def pass_on(keys, stage):
        for key in keys:
            if key in gathers:
                gathers[key].pass_on(stage)

    def pass_all(keys):
        for stage in (1, 2, 3):
            pass_on(keys, stage)

    mover.near(*param_loads)
    layer, after = plan.layer, min(plan.layer + 1, params[0].shape[0] - 1)

    def row(index, layer=layer):
        return params[index][...].astype(FULL)[layer : layer + 1]

    b_out, gain2, shift2, b_down, b_up = row(0), row(1), row(2), row(3), row(6)
    gain1, shift1, gain0, shift0 = row(4, after), row(5, after), row(4), row(5)
    qkv_bias[...] = joint_bias(row(7), size, joint.shape[0])
    key_bias(mover, live_ref, bias)
    ahead = [("qkv", 1), ("out", 1), ("up", 1)]
    one = Round(mover, rows, second, one_work)
    two = Round(mover, rows, following, two_work)
    if plan.entry:
        chunk = rows // 5 if rows % 80 == 0 else rows

        def norm_step(i, carry):
            at = pl.ds(pl.multiple_of(i * chunk, 16), chunk)
            value = normalize(source[at, :].astype(FULL), gain0, shift0)[0]
            first[at, :] = value.astype(LOW)
            return carry

        lax.fori_loop(0, rows // chunk, norm_step, 0)
        mover.stay(first, far_first)
        pass_all([("qkv", 0)])
        begin([("out", 0), ("up", 0)])
        begin_over([("out", 0), ("up", 0), ("down", 0)] + ahead)
        turned_product(first, have("qkv"), qkv_bias, joint)
    else:
        turned_product(first, have("qkv"), qkv_bias, joint)

    def after_send():
        if plan.entry:
            pass_all([("out", 0), ("up", 0)])
        else:
            for name in plan.own:
                gathers[name, 0].start_over()

    def begun():
        begin([("down", 0)])

    def between(p):
        if p > 2:
            pass_on([("down", 0)], p - 2)
        if p == 4:
            if not plan.entry:
                begin_over(ahead)
            begin(ahead)

    attend_part(
        size, tile, mover, joint, bias, heads, qkv, o_ref, lse, attend_work, after_send, begun, between
    )
    nat[...] = turned(heads[...])
    w_out = have("out")

    def out_part(start):
        return dot(nat[one.rows(start), :], w_out[...], ((1,), (1,)))

    def to_second(at, value):
        if plan.entry:
            before = source[one.rows(one.own + at.start, at.size), :].astype(FULL)
        else:
            before = x_ref[at]
        value = before + value + b_out
        middle[at] = value
        return normalize(value, gain2, shift2)[0].astype(LOW)

    def meanwhile():
        mover.stay(qkv, far_qkv)
        mover.stay(o_ref, far_o)
        mover.stay(lse, far_lse)
        mover.stay(nat, far_heads)
        pass_on([("down", 0)], 3)

    one.eager(out_part, to_second, meanwhile, lambda: pass_on(ahead[:2], 1))
    pass_on(ahead[:2], 2)
    w_up, w_down = have("up"), have("down")

    def mlp_part(start):
        at = two.rows(start)
        pre = jnp.dot(second[at, :], w_up[...], preferred_element_type=FULL) + b_up
        low, low_slope = gelu_pair(pre)
        hidden[at, :] = low
        slope[at, :] = low_slope
        return dot(low, w_down[...], ((1,), (1,)))

    def to_following(at, value):
        value = middle[at] + value + b_down
        stream[at] = value
        if last:
            return live_rows(value, two.own + at.start, live_ref[0, mover.ctx]).astype(LOW)
        return normalize(value, gain1, shift1)[0].astype(LOW)

    def meanwhile():
        mover.stay(middle, far_middle)
        mover.stay(second, far_second)
        mover.stay(hidden, far_hidden)
        mover.stay(slope, far_slope)
        pass_on(ahead[2:], 3)

    def between_parts():
        pass_on(ahead[:2], 3)
        pass_on(ahead[2:], 1)
        pass_on(ahead[2:], 2)

    two.after(one, mlp_part, to_following, meanwhile, between_parts)
    two.have()
    for name in plan.ahead + plan.lines:
        gathers[name, 1].have()
        mover.stay(gathers[name, 1].target, kept_ahead[name])
    mover.settle()


class Plan:
    def __init__(self, layer, last, inside):
        self.layer, self.entry = layer, layer == 0
        self.own = (NAMES if layer == 0 else ("down",)) if inside else ()
        self.halves = ("out", "up") if inside and layer else ()
        self.ahead = ("qkv",) if inside and not last else ()
        self.lines = ("out", "up") if inside and not last else ()
        self.kept = self.own + self.halves
        self.held = tuple(name for name in NAMES if name not in self.kept)


def forward_layer(source, x, live, params, gathered, weights, plan, last, size, sizes, ident):
    rows, width = source.shape
    count = sizes[0]
    joint, hidden = weights["qkv"].shape[2], weights["up"].shape[2]
    heads = joint // (3 * size)
    attn, slots, span = heads * size, count * rows, rows // 4
    tile = 256 if slots % 256 == 0 else PAD
    columns = {"qkv": joint, "out": attn, "up": hidden, "down": hidden}
    inputs = [(source, VMEM)] + ([] if plan.entry else [(x, VMEM)])
    inputs += [(live, SMEM)] + [(value, HBM) for value in params]
    inputs += [(gathered[name, plan.layer], HBM) for name in plan.held]
    inputs += [(gathered[name, plan.layer, 0], HBM) for name in plan.halves]
    inputs += [(weights[name], HBM) for name in plan.own + plan.ahead + plan.lines]
    saved = [
        ((count, 3 * size, rows), LOW),
        ((size, slots), FULL),
        ((8, slots), FULL),
        ((rows, attn), LOW),
        ((span, width), FULL),
        ((rows, width), LOW),
        ((rows, hidden), LOW),
        ((rows, hidden), LOW),
    ]
    outputs = [((span, width), FULL, VMEM), ((rows, width), LOW, VMEM)]
    outputs += [(shape, dtype, HBM) for shape, dtype in saved]
    if plan.entry:
        outputs.append(((rows, width), LOW, HBM))
    ahead = [(width, columns[name]) for name in plan.ahead]
    ahead += [(width // 2, columns[name]) for name in plan.lines]
    outputs += [(shape, LOW, HBM) for shape in ahead]
    outputs += [((width, columns[name]), LOW, HBM) for name in plan.kept]
    qkv_shape, o_shape, lse_shape, heads_shape = saved[:4]
    scratch = [VMEM((joint, rows), LOW), VMEM((rows, attn), LOW), VMEM((attn, rows), LOW)]
    scratch += [VMEM(*pair) for pair in saved[:3] + saved[4:]]
    if plan.entry:
        scratch.append(VMEM((rows, width), LOW))
    scratch += [
        VMEM((slots, PAD), LOW),
        VMEM((PAD, slots), LOW),
        VMEM((size + 16, slots), LOW),
        VMEM((size, slots), LOW),
        VMEM((2, slots, tile), FULL),
        VMEM((2, 8, tile), FULL),
    ]
    scratch += round_buffers(rows, width) + round_buffers(rows, width)
    scratch += [VMEM((16, slots), LOW), VMEM((16, joint), FULL)]
    scratch += [VMEM(value.shape, value.dtype) for value in params]
    scratch += [VMEM((width, columns[name]), LOW) for name in NAMES]
    scratch += [VMEM(shape, LOW) for shape in ahead]
    results = run(
        functools.partial(layer_kernel, plan, last, size, tile),
        "forward_layer",
        ident,
        inputs,
        outputs,
        scratch,
        2 * (count - 1) + 2 * ROUND_COPIES + 2 * count * len(plan.kept + plan.ahead + plan.lines),
        10 + 2 * len(plan.kept + plan.ahead + plan.lines) + len(plan.held) + len(params),
        sizes,
        58,
        2 * rows * width * (2 * hidden + attn + joint) + 4 * slots * slots * 256,
    )
    stream, following = results[:2]
    kept = results[2 : 11 if plan.entry else 10]
    rest = iter(results[2 + len(kept) :])
    for name in plan.ahead:
        gathered[name, plan.layer + 1] = next(rest)
    for name in plan.lines:
        gathered[name, plan.layer + 1, 0] = next(rest)
    for name in plan.kept:
        gathered[name, plan.layer] = next(rest)
    return stream, following, kept


class SmallSums:
    def __init__(self, mover, rows, held, got):
        self.mover, self.rows, self.held, self.got = mover, rows, held, got
        self.stage = 0
        mate, far = tp_peers()
        self.peers = [
            dict(tp=mate),
            dict(tp=far),
            dict(shard=1 - mover.shard),
            dict(ctx=mover.flip(2)),
            dict(ctx=mover.flip(1)),
        ]

    def part(self, stage):
        return pl.ds(0, self.rows if stage < 2 else self.held.shape[1])

    def step(self):
        stage, mover = self.stage, self.mover
        if stage:
            mover.take(self.copy)
            at = self.part(stage - 1)
            self.held[stage] = self.held[stage - 1]
            self.held[stage, at, :] = self.held[stage - 1, at, :] + self.got[stage - 1, at, :]
        if stage < len(self.peers):
            at = self.part(stage)
            self.copy = mover.go(
                self.held.at[stage, at], self.got.at[stage, at], **self.peers[stage]
            )
        self.stage = stage + 1

    def value(self):
        return self.held[len(self.peers)]


def key_bias(mover, live_ref, bias):
    capacity = bias.shape[1] // mover.ctx_count
    row = lax.broadcasted_iota(jnp.int32, (16, capacity), 0)
    slot = lax.broadcasted_iota(jnp.int32, (16, capacity), 1)
    for r in range(mover.ctx_count):
        live = live_ref[0, mover.back(r)]
        value = jnp.where((row == 0) & (slot >= live), NEG_LARGE, 0.0)
        bias[:, r * capacity : (r + 1) * capacity] = value.astype(LOW)


def pair_columns(rows, width, size, turn):
    shape = (width, rows) if turn else (rows, width)
    given = lax.broadcasted_iota(jnp.int32, shape, 1 if turn else 0)
    column = lax.broadcasted_iota(jnp.int32, shape, 0 if turn else 1)
    head, within = column // (3 * size), column % (3 * size)
    wanted = head * (2 * size) + jnp.where(within < size, within, within - size)
    key = (within >= size) & (within < 2 * size)
    return jnp.where((given == wanted) & ~key, 1.0, 0.0).astype(LOW)


def joint_bias(pair, size, width):
    rows = pair.shape[1]
    spread = jnp.broadcast_to(pair, (16, rows)).astype(LOW)
    return jnp.dot(spread, pair_columns(rows, width, size, False), preferred_element_type=FULL)


def live_rows(value, start, live):
    row = start + lax.broadcasted_iota(jnp.int32, value.shape, 0)
    return jnp.where(row < live, value, 0.0)


def sums_into(sums, first, at, values):
    for index, value in enumerate(values):
        row = first + index
        added = jnp.sum(value, axis=0, keepdims=True)
        width = added.shape[1]
        sums[row : row + 1, 0:width] = (
            added if at.start == 0 else sums[row : row + 1, 0:width] + added
        )


def back_kernel(plan, size, tile, mover, ins, outs, work):
    ins, outs, work = iter(ins), iter(outs), iter(work)
    source = next(ins)
    x_ref = None if plan.last else next(ins)
    live_ref, far_gain2, far_gain1 = [next(ins) for _ in range(3)]
    far = [next(ins) for _ in range(14)]
    late_far = next(ins) if plan.late else None
    others = [(next(ins), next(ins)) for _ in range(plan.others)]
    stream, following = next(outs), next(outs)
    grad_outs = {name: next(outs) for name in NAMES if plan.inside and (name != "qkv" or plan.final)}
    mid_out = next(outs) if plan.inside and not plan.final else None
    late_out = next(outs) if plan.late else None
    split = local = totals = None
    if plan.joined:
        totals = next(outs)
    else:
        split, local = next(outs), next(outs)
    wholes = {} if plan.inside else {name: next(outs) for name in NAMES}
    near = [next(work) for _ in range(14)]
    slope, w_down, w_up, middle, hidden, second, w_out, heads, qkv, o_ref, lse, first, w_qkv, before = near
    grad = next(work) if plan.last else source
    pre_grad, attn_grad, parts, grads, nat = [next(work) for _ in range(5)]
    attend_work = [next(work) for _ in range(10)]
    one_work, two_work = [next(work) for _ in range(5)], [next(work) for _ in range(5)]
    rows, width = source.shape
    reduces = {}
    if plan.inside:
        pairs = {
            "down": (grad, hidden),
            "up": (second, pre_grad),
            "out": (attn_grad, heads),
            "qkv": (first, nat),
        }
        for name in ("down", "up", "out", "qkv"):
            buffers = [next(work) for _ in range(4)]
            reduces[name] = Reduce(mover, buffers, grad_outs.get(name), *pairs[name])
    late = None
    if plan.late:
        late_mid, late_line = next(work), next(work)
        late = Reduce(mover, (late_mid, None, late_mid, late_line), late_out, None, None)
    bias, gain2_ref, gain1_ref = [next(work) for _ in range(3)]
    if plan.joined:
        split, local = next(work), next(work)
        early_held, early_got, late_held, late_got = [next(work) for _ in range(4)]
        tops = 8 * (plan.others + 1)
        early = SmallSums(mover, tops, early_held, early_got)
        final = SmallSums(mover, 8, late_held, late_got)
        everything = [(split, local)] + others

    greet(mover, plan.inside)
    gain_loads = [mover.stay(far_gain2, gain2_ref), mover.stay(far_gain1, gain1_ref)]
    one = Round(mover, rows, attn_grad, one_work)
    two = Round(mover, rows, following, two_work)
    if plan.final:
        far[13] = far[13].at[two.rows(two.own)]
    load = {index: mover.stay(far[index], near[index]) for index in (4, 0, 1, 2)}
    if late:
        mover.near(mover.stay(late_far, late_mid))
        late.send_first()
        late.send_second()
    if plan.last:
        chunk = rows // 5 if rows % 80 == 0 else rows

        def mask_step(i, carry):
            at = pl.ds(pl.multiple_of(i * chunk, 16), chunk)
            value = source[at, :].astype(FULL)
            grad[at, :] = live_rows(value, i * chunk, live_ref[0, mover.ctx]).astype(LOW)
            return carry

        lax.fori_loop(0, rows // chunk, mask_step, 0)
    key_bias(mover, live_ref, bias)
    mover.near(*gain_loads)
    gain2, gain1 = [
        ref[...].astype(FULL)[plan.layer : plan.layer + 1] for ref in (gain2_ref, gain1_ref)
    ]
    split[...] = jnp.zeros_like(split)
    local[...] = jnp.zeros_like(local)
    split[5:6, 0:width] = jnp.sum(
        grad[one.rows(one.own), :].astype(FULL), axis=0, keepdims=True
    )
    hidden_width = slope.shape[1]

    def mlp_part(start):
        at = one.rows(start)
        pre = jnp.dot(grad[at, :], w_down[...], preferred_element_type=FULL)
        low = (pre * slope[at, :].astype(FULL)).astype(LOW)
        pre_grad[at, :] = low
        local[0:1, 0:hidden_width] += jnp.sum(low.astype(FULL), axis=0, keepdims=True)
        return dot(low, w_up[...], ((1,), (1,)))

    def to_attn(at, value):
        if plan.last:
            above = grad[one.rows(one.own + at.start, at.size), :].astype(FULL)
        else:
            above = x_ref[at]
        _, normed, inverse = normalize(middle[at], 1.0, 0.0)
        result = above + normalize_back(value, normed, inverse, gain2)
        stream[at] = result
        low = result.astype(LOW)
        sums_into(split, 2, at, (value * normed, value, low.astype(FULL)))
        return low

    def reduce(name):
        if name in reduces:
            reduces[name].begin_blocks()

    def own(name):
        if name in reduces:
            reduces[name].own()

    def first_step(name):
        if name in reduces:
            reduces[name].fold_blocks(3)
            reduces[name].send_first()

    def second_step(name):
        if name in reduces:
            reduces[name].fold_blocks(2)
            reduces[name].send_third()

    def rest(name):
        if name in reduces:
            reduces[name].fold_blocks(1)
            reduces[name].send_second()
            reduces[name].fold_blocks(0)

    def begin_early():
        if plan.joined:
            early_held[0] = jnp.zeros(early_held.shape[1:], FULL)
            for layer, (some, more) in enumerate(everything):
                first_row = 0 if layer else 2
                for row in range(first_row, 6):
                    at = row * len(everything) + layer
                    early_held[0, at : at + 1, :] = some[row : row + 1, :]
                for row in range(2 if layer else 1):
                    at = tops + row * len(everything) + layer
                    early_held[0, at : at + 1, :] = more[row : row + 1, :]

    def early_step():
        if plan.joined:
            early.step()

    def start_down():
        mover.near(load[3])
        own("down")
        first_step("down")

    mover.near(load[4])
    reduce("down")
    mover.near(load[0], load[1], load[2])
    for index in (3,) + tuple(range(5, len(far))):
        load[index] = mover.stay(far[index], near[index])
    one.eager(mlp_part, to_attn, start_down)
    if late:
        late.send_third()
    second_step("down")
    mover.near(load[5])
    reduce("up")
    one.have()
    mover.near(load[6])
    turned_product(attn_grad, w_out, None, parts)

    def waiting():
        begin_early()
        early_step()
        rest("down")
        mover.near(load[7])
        reduce("out")
        own("out")

    def ready():
        own("up")
        mover.near(load[8], load[9], load[10])

    def between(turn):
        if turn == 0:
            early_step()
        if turn == 3:
            first_step("up")

    attend_back_part(
        size,
        tile,
        mover,
        parts,
        bias,
        qkv,
        o_ref,
        lse,
        grads,
        attend_work,
        ready,
        waiting,
        lambda: None,
        between,
    )
    second_step("up")
    early_step()
    nat[...] = turned(grads[...])
    pairs_width = nat.shape[1] // 3 * 2
    picked = jnp.dot(
        nat[...], pair_columns(pairs_width, nat.shape[1], size, True), preferred_element_type=FULL
    )
    local[1:2, 0:pairs_width] = jnp.sum(picked, axis=0, keepdims=True)
    mover.near(*[load[index] for index in range(11, len(far))])

    def qkv_part(start):
        return dot(nat[two.rows(start), :], w_qkv[...], ((1,), (1,)))

    def to_following(at, value):
        row = before[at, :].astype(FULL)
        _, normed, inverse = normalize(row, 1.0, 0.0)
        result = stream[at] + normalize_back(value, normed, inverse, gain1)
        stream[at] = result
        low = result.astype(LOW)
        sums_into(split, 0, at, (value * normed, value))
        return low

    def meanwhile():
        own("qkv")
        first_step("out")
        rest("up")
        early_step()

    def halfway():
        if plan.inside:
            reduces["qkv"].fold_blocks(3)
            if plan.final:
                reduces["qkv"].send_first()

    reduce("qkv")
    two.eager(qkv_part, to_following, meanwhile, halfway)
    if plan.joined:
        late_held[0, 0:8, :] = jnp.zeros((8, late_held.shape[2]), FULL)
        late_held[0, 0:2, :] = split[0:2, :]
        late_held[0, 8:16, :] = local[...]
        final.step()
        early_step()
        final.step()
    second_step("out")
    rest("out")
    two.have_mate_own()
    two.have_other()
    if plan.joined:
        final.step()
        final.step()
    if plan.inside:
        last = reduces["qkv"]
        if plan.final:
            second_step("qkv")
            rest("qkv")
        else:
            last.fold_blocks(2, 1, 0)
            mover.stay(last.mid, mid_out)
    two.have_mate_other()
    if plan.joined:
        final.step()
    for name in ("down", "up", "out"):
        if name in reduces:
            reduces[name].done()
    if late:
        late.done()
    if plan.inside and plan.final:
        reduces["qkv"].done()
    if plan.joined:
        final.step()
        early.step()
        totals[...] = early.value()
        last_value = final.value()
        for row in range(2):
            at = row * len(everything)
            totals[at : at + 1, :] = last_value[row : row + 1, :]
        at = tops + len(everything)
        totals[at : at + 1, :] = last_value[9:10, :]
    if not plan.inside:
        for name, (lhs, rhs) in {
            "down": (grad, hidden),
            "up": (second, pre_grad),
            "out": (attn_grad, heads),
            "qkv": (first, nat),
        }.items():
            full = Reduce(mover, (wholes[name],) * 4, None, lhs, rhs)
            full.compute(wholes[name], 0)
    mover.settle()


def gather_outputs_kernel(layers, *refs):
    count = layers * len(NAMES)
    parts, token_grads, mixed, totals = refs[:count], refs[count], refs[count + 1], refs[count + 2]
    outs, work = refs[count + 3 : count + 17], refs[count + 17 : -2]
    into, out_of = refs[-2:]
    coming, going = [], []
    pairs = [(mixed, work[4], outs[4].at[0])]
    for index in range(len(NAMES)):
        for layer in range(layers):
            pairs.append(
                (parts[index * layers + layer], work[index].at[layer], outs[index].at[layer])
            )
    for i, (source, stage, _) in enumerate(pairs):
        coming.append(pltpu.make_async_copy(source, stage, into.at[i]))
        coming[-1].start()
    outs[5][0] = token_grads[...].astype(FULL)
    for row, out in enumerate(outs[6:12]):
        out[...] = totals[row * layers : (row + 1) * layers, 0 : out.shape[1]]
    for row, out in enumerate(outs[12:14]):
        row = row + 8
        out[...] = totals[row * layers : (row + 1) * layers, 0 : out.shape[1]]
    for i, (_, stage, target) in enumerate(pairs):
        coming[i].wait()
        going.append(pltpu.make_async_copy(stage, target, out_of.at[i]))
        going[-1].start()
    for copy in going:
        copy.wait()


def gather_outputs(done, token_grads, mixed, totals, layers, widths):
    rows, width = token_grads.shape
    parts = [done[name, layer] for name in NAMES for layer in range(layers)]
    hbm, whole = pl.BlockSpec(memory_space=HBM), lambda shape: pl.BlockSpec(
        shape, lambda i: (0,) * len(shape)
    )
    shapes = [(layers,) + done[name, 0].shape for name in NAMES] + [(1, rows, width)] * 2
    types = [FULL] * 4 + [LOW, FULL]
    small = [(layers, width)] * 6 + [(layers, count) for count in widths]
    copies = len(parts) + 1
    return pl.pallas_call(
        functools.partial(gather_outputs_kernel, layers),
        grid=(1,),
        in_specs=[hbm] * len(parts) + [whole(token_grads.shape), hbm, whole(totals.shape)],
        out_specs=[hbm] * 5 + [whole(shape) for shape in shapes[5:] + small],
        out_shape=[jax.ShapeDtypeStruct(*pair) for pair in zip(shapes, types)]
        + [jax.ShapeDtypeStruct(shape, FULL) for shape in small],
        scratch_shapes=[VMEM(shape, FULL) for shape in shapes[:4]]
        + [VMEM((rows, width), LOW)]
        + [pltpu.SemaphoreType.DMA((copies,)), pltpu.SemaphoreType.DMA((copies,))],
        compiler_params=pltpu.CompilerParams(vmem_limit_bytes=60 * 2**20),
        name="gather_outputs",
    )(*parts, token_grads, mixed, totals)


class BackPlan:
    def __init__(self, layer, layers, inside):
        self.inside, self.layer = inside, layer
        self.last, self.final = layer == layers - 1, layer == 0
        self.late = inside and not self.last
        self.joined = inside and self.final
        self.others = layers - 1 if self.joined else 0


def back_layer(source, x, live, gain2, gain1, saved, late, others, plan, size, sizes, ident):
    rows, width = source.shape
    count = sizes[0]
    slope, w_down, w_up = saved[:3]
    hidden, joint, attn = slope.shape[1], saved[12].shape[1], saved[6].shape[1]
    slots, span = count * rows, rows // 4
    tile = 512 if slots % 512 == 0 else PAD
    wide = max(width, hidden, joint)
    half = width // 2
    block = half // count
    columns = {"qkv": joint, "out": attn, "up": hidden, "down": hidden}
    inputs = [(source, VMEM)] + ([] if plan.last else [(x, VMEM)])
    inputs += [(live, SMEM), (gain2, HBM), (gain1, HBM)]
    inputs += [(value, HBM) for value in saved]
    if plan.late:
        inputs.append((late, HBM))
    for pair in others[: plan.others]:
        inputs += [(value, VMEM) for value in pair]
    outputs = [((span, width), FULL, VMEM), ((rows, width), LOW, VMEM)]
    names = [name for name in NAMES if plan.inside and (name != "qkv" or plan.final)]
    outputs += [((block, columns[name]), FULL, VMEM) for name in names]
    if plan.inside and not plan.final:
        outputs.append(((half, joint), LOW, HBM))
    if plan.late:
        outputs.append(((block, joint), FULL, VMEM))
    depth = 8 * (plan.others + 1)
    if plan.joined:
        outputs.append(((depth + 8, wide), FULL, VMEM))
    else:
        outputs += [((8, wide), FULL, VMEM)] * 2
    if not plan.inside:
        outputs += [((width, columns[name]), LOW, VMEM) for name in NAMES]
    scratch = [VMEM(value.shape, value.dtype) for value in saved]
    scratch[13] = VMEM((span, width), saved[13].dtype)
    if plan.last:
        scratch.append(VMEM((rows, width), LOW))
    scratch += [
        VMEM((rows, hidden), LOW),
        VMEM((rows, width), LOW),
        VMEM((attn, rows), LOW),
        VMEM((joint, rows), LOW),
        VMEM((rows, joint), LOW),
    ]
    scratch += attend_back_buffers(size, count, rows)
    scratch += round_buffers(rows, width) + round_buffers(rows, width)
    if plan.inside:
        for name in ("down", "up", "out", "qkv"):
            scratch += reduce_buffers(half, columns[name], count)
    if plan.late:
        scratch += [VMEM((half, joint), LOW), VMEM((count - 1, block, joint), LOW)]
    scratch.append(VMEM((16, slots), LOW))
    scratch += [VMEM(value.shape, value.dtype) for value in (gain2, gain1)]
    assert 2 * (plan.others + 1) <= 8
    if plan.joined:
        scratch += [VMEM((8, wide), FULL)] * 2
        scratch += [
            VMEM((6, depth + 8, wide), FULL),
            VMEM((5, depth + 8, wide), FULL),
            VMEM((6, 16, wide), FULL),
            VMEM((5, 16, wide), FULL),
        ]
    results = run(
        functools.partial(back_kernel, plan, size, tile),
        "back_layer",
        ident,
        inputs,
        outputs,
        scratch,
        3 * (count - 1) + 2 * ROUND_COPIES + 8 * count + 10 + count,
        len(saved) + 4,
        sizes,
        58,
        6 * rows * width * (2 * hidden + attn + joint) + 10 * slots * slots * 256,
    )
    return results[:2], names, results[2:]


def shards(
    tokens,
    block_tokens,
    ln1_gain,
    ln1_bias,
    w_qkv,
    b_qv,
    w_out,
    b_out,
    ln2_gain,
    ln2_bias,
    w_up,
    b_up,
    w_down,
    b_down,
    cotangent,
):
    images, capacity, width = tokens.shape
    assert images == 1
    layers = w_qkv.shape[0]
    size = HEAD_DIM
    ctx_count = lax.axis_size("ctx")
    ctx_place = lax.axis_index("ctx")
    joint_width = w_qkv.shape[2]
    heads = joint_width // (3 * size)
    assert heads == ctx_count
    attn_width = heads * size
    hidden_width = w_up.shape[2]
    weights = {"qkv": w_qkv, "out": w_out, "up": w_up, "down": w_down}
    sizes = (ctx_count, lax.axis_size("shard"))
    inside = sizes == (4, 2)
    gathered = {}
    if not inside:
        for name, value in weights.items():
            for layer in range(layers):
                gathered[name, layer] = gather_weight(value[layer])[0]
    source, stream = tokens[0], None
    saved = []
    for layer in range(layers):
        last = layer == layers - 1
        result, following, kept = forward_layer(
            source,
            stream,
            block_tokens,
            (b_out, ln2_gain, ln2_bias, b_down, ln1_gain, ln1_bias, b_up, b_qv),
            gathered,
            weights,
            Plan(layer, last, inside),
            last,
            size,
            sizes,
            1 + layer,
        )
        before = stream if layer else source
        first = source if layer else kept[8]
        saved.append((before, first) + tuple(kept[:8]))
        source, stream = following, result
    mixed = source

    done, packs = {}, {}
    source, stream, late = cotangent[0], None, None
    for layer in reversed(range(layers)):
        before, first, qkv, head_out, lse, heads_low, middle, second, hidden, slope = saved[layer]
        plan = BackPlan(layer, layers, inside)
        whole = {name: gathered[name, layer] for name in NAMES}
        near = [slope, whole["down"], whole["up"], middle, hidden, second, whole["out"]]
        near += [heads_low, qkv, head_out, lse, first, whole["qkv"], before]
        others = [packs[key] for key in sorted(packs)]
        (stream, source), names, rest = back_layer(
            source, stream, block_tokens, ln2_gain, ln1_gain, near, late, others, plan, size, sizes, 1 + layers + layer
        )
        rest = iter(rest)
        for name in names:
            done[name, layer] = next(rest)
        if plan.inside and not plan.final:
            late = next(rest)
        if plan.late:
            done["qkv", layer + 1] = next(rest)
        if plan.joined:
            totals = next(rest)
        else:
            packs[layer] = (next(rest), next(rest))
        if not inside:
            for name in NAMES:
                value = next(rest)
                done[name, layer] = scatter_weight(
                    lambda start, count, value=value: rows_of(value, start, count).astype(FULL),
                    width,
                )
    if not inside:
        split = total_over(("tp",), jnp.stack([packs[l][0] for l in range(layers)], axis=1))
        local = jnp.stack([packs[l][1] for l in range(layers)], axis=1)
        totals = total_over(("shard", "ctx"), jnp.concatenate([split, local[:2]]))
        totals = totals.reshape(10 * layers, -1)
    pairs = b_qv.shape[1]
    outs = gather_outputs(done, source, mixed, totals, layers, (hidden_width, pairs))
    g_qkv, g_out, g_up, g_down, mixed, token_grads = outs[:6]
    g_ln1_gain, g_ln1_bias, g_ln2_gain, g_ln2_bias, g_b_out, g_b_down, g_b_up, g_b_qv = outs[6:]
    return (
        mixed,
        token_grads,
        g_ln1_gain,
        g_ln1_bias,
        g_qkv,
        g_b_qv,
        g_out,
        g_b_out,
        g_ln2_gain,
        g_ln2_bias,
        g_up,
        g_b_up,
        g_down,
        g_b_down,
    )


def solution(mesh):
    split_rows = P(None, ("shard", "ctx"), "tp")
    split_tokens = P("shard", "ctx", None)
    return jax.shard_map(
        shards,
        mesh=mesh,
        in_specs=(
            split_tokens,
            P("shard", None),
            P(),
            P(),
            split_rows,
            P(None, "tp"),
            split_rows,
            P(),
            P(),
            P(),
            split_rows,
            P(None, "tp"),
            split_rows,
            P(),
            split_tokens,
        ),
        out_specs=(
            split_tokens,
            split_tokens,
            P(),
            P(),
            split_rows,
            P(None, "tp"),
            split_rows,
            P(),
            P(),
            P(),
            split_rows,
            P(None, "tp"),
            split_rows,
            P(),
        ),
        check_vma=False,
    )
```

```python
import functools
import math

import jax
import jax.numpy as jnp
from jax import lax
from jax.experimental import pallas as pl
from jax.experimental.pallas import tpu as pltpu
from jax.sharding import PartitionSpec as P

HEAD_DIM = 64
EPSILON = 1e-06
NEG_LARGE = -1e30
LOW = jnp.bfloat16
FULL = jnp.float32
PAD = 128
MESH = pl.DeviceIdType.MESH
VMEM = pltpu.VMEM
HBM = pltpu.HBM
SMEM = pltpu.SMEM


def bits_of(axis):
    size = lax.axis_size(axis)
    assert size & (size - 1) == 0
    return [1 << i for i in range(size.bit_length() - 1)]


def swap(value, axis, bit):
    size = lax.axis_size(axis)
    return lax.ppermute(value, axis, [(i, i ^ bit) for i in range(size)])


def side_of(axis, bit):
    return (lax.axis_index(axis) // bit) % 2


def rows_of(value, start, count, axis=0):
    return lax.dynamic_slice_in_dim(value, start, count, axis)


def halve(axis, bits, partial, total):
    offset, span, received = jnp.int32(0), total, []

    def summed(start, count):
        value = partial(start, count)
        for got, base in received:
            value = value + rows_of(got, start - base, count).astype(FULL)
        return value

    for bit in bits:
        half = span // 2
        side = side_of(axis, bit)
        got = swap(summed(offset + (1 - side) * half, half).astype(LOW), axis, bit)
        offset = offset + side * half
        received.append((got, offset))
        span = half
    return summed(offset, span)


def double(axis, bits, value):
    for bit in bits:
        got = swap(value, axis, bit)
        first = side_of(axis, bit) == 0
        value = jnp.concatenate(
            [jnp.where(first, value, got), jnp.where(first, got, value)], axis=0
        )
    return value


def total_over(axes, value):
    for axis in axes:
        for bit in bits_of(axis):
            value = value + swap(value, axis, bit)
    return value


def ring(value, by):
    count = lax.axis_size("ctx")
    return lax.ppermute(value, "ctx", [(i, (i + by) % count) for i in range(count)])


def gather_weight(piece):
    count = lax.axis_size("ctx")
    place = lax.axis_index("ctx")
    ways = lax.axis_size("shard")
    blocks = [piece] + [ring(piece, by) for by in range(1, count)]
    whole = jnp.zeros((ways * count,) + piece.shape, piece.dtype)
    me = lax.axis_index("shard")
    for by, block in enumerate(blocks):
        at = (place - by) % count
        held = [(jnp.int32(0), block)]
        for bit in bits_of("shard"):
            held = held + [(other ^ bit, swap(value, "shard", bit)) for other, value in held]
        for other, value in held:
            whole = lax.dynamic_update_index_in_dim(whole, value, (me ^ other) * count + at, 0)
    return whole.reshape((ways * count * piece.shape[0],) + piece.shape[1:]), blocks[-1]


def scatter_weight(partial, total):
    count = lax.axis_size("ctx")
    place = lax.axis_index("ctx")
    mine = halve("shard", bits_of("shard")[::-1], partial, total).astype(LOW)
    mine = mine.reshape((count, mine.shape[0] // count) + mine.shape[1:])
    value = lax.dynamic_index_in_dim(mine, place, 0, False).astype(FULL)
    for by in range(1, count):
        given = lax.dynamic_index_in_dim(mine, (place + by) % count, 0, False)
        value = value + ring(given, by).astype(FULL)
    return value


def dot(left, right, contract):
    return lax.dot_general(
        left, right, ((contract[0], contract[1]), ((), ())), preferred_element_type=FULL
    )


def turned(value):
    return value.astype(FULL).T.astype(LOW)


def normalize(rows, gain, shift):
    row_mean = jnp.mean(rows, axis=-1, keepdims=True)
    centred = rows - row_mean
    inverse = lax.rsqrt(jnp.mean(centred * centred, axis=-1, keepdims=True) + EPSILON)
    normed = centred * inverse
    return (normed * gain + shift, normed, inverse)


def normalize_back(grad_out, normed, inverse, gain):
    scaled = grad_out * gain
    mean_grad = jnp.mean(scaled, axis=-1, keepdims=True)
    mean_cross = jnp.mean(scaled * normed, axis=-1, keepdims=True)
    return inverse * (scaled - mean_grad - normed * mean_cross)


def gelu_pair(value):
    spread = 0.5 * (1.0 + lax.erf(value * (0.5**0.5)))
    slope = spread + value * jnp.exp(-0.5 * value * value) * (1.0 / math.sqrt(2.0 * math.pi))
    return (value * spread).astype(LOW), slope.astype(LOW)


class Mover:
    def __init__(self, sizes, send, recv, local):
        self.ctx_count, self.shard_count = sizes
        self.send, self.recv, self.local = send, recv, local
        self.copies, self.here = [], []
        self.arrived = set()
        self.landed = set()
        self.ctx = lax.axis_index("ctx")
        self.shard = lax.axis_index("shard")

    def go(self, source, target, **device):
        index = len(self.copies)
        assert index < self.send.shape[0]
        copy = pltpu.make_async_remote_copy(
            src_ref=source,
            dst_ref=target,
            send_sem=self.send.at[index],
            recv_sem=self.recv.at[index],
            device_id=device,
            device_id_type=MESH,
        )
        copy.start()
        self.copies.append(copy)
        return index

    def stay(self, source, target):
        index = len(self.here)
        assert index < self.local.shape[0]
        copy = pltpu.make_async_copy(source, target, self.local.at[index])
        copy.start()
        self.here.append(copy)
        return index

    def near(self, *indices):
        for index in indices:
            if index not in self.landed:
                self.landed.add(index)
                self.here[index].wait()

    def take(self, index):
        if index not in self.arrived:
            self.arrived.add(index)
            self.copies[index].wait_recv()

    def flip(self, bits):
        place = self.ctx
        if bits & 1:
            place = place + 1 - 2 * lax.rem(self.ctx, 2)
        if bits & 2:
            place = place + 2 - 4 * (self.ctx // 2)
        return place

    def on(self, by):
        return lax.rem(self.ctx + by, self.ctx_count)

    def back(self, by):
        return lax.rem(self.ctx + self.ctx_count - by, self.ctx_count)

    def settle(self):
        for index, copy in enumerate(self.copies):
            self.take(index)
            copy.wait_send()
        self.near(*range(len(self.here)))


class Gather:
    def __init__(self, mover, source, target, across=True):
        self.mover, self.source, self.target, self.across = mover, source, target, across
        self.over = []

    def start_line(self):
        mover = self.mover
        mine, there = self.source, self.block(mover.ctx)
        self.far = mover.go(mine, there, ctx=mover.flip(2))
        self.close = mover.go(mine, there, ctx=mover.flip(1))

    def start_over(self):
        mover = self.mover
        mine, there = self.source, self.block(mover.ctx)
        if self.across:
            self.over.append(mover.go(mine, there, shard=1 - mover.shard))
        self.own = mover.stay(mine, there)

    def block(self, ctx):
        mover = self.mover
        rows = self.source.shape[0]
        start = ctx * rows
        if self.across:
            start = start + mover.shard * mover.ctx_count * rows
        return self.target.at[pl.ds(pl.multiple_of(start, rows), rows)]

    def pass_on(self, stage):
        mover = self.mover
        if stage == 1:
            mover.take(self.far)
            rows = self.block(mover.flip(2))
            self.passed = mover.go(rows, rows, ctx=mover.flip(1))
        elif stage == 2:
            mover.take(self.close)
            rows = self.block(mover.flip(1))
        else:
            mover.take(self.passed)
            rows = self.block(mover.flip(3))
        if self.across:
            self.over.append(mover.go(rows, rows, shard=1 - mover.shard))

    def have(self):
        for copy in self.over:
            self.mover.take(copy)
        self.mover.near(self.own)


class Across:
    def __init__(self, mover, source, target):
        rows = source.shape[0]
        there = target.at[pl.ds(pl.multiple_of(mover.shard * rows, rows), rows)]
        self.mover = mover
        self.copy = mover.go(source, there, shard=1 - mover.shard)
        self.own = mover.stay(source, there)

    def have(self):
        self.mover.take(self.copy)
        self.mover.near(self.own)


class Reduce:
    def __init__(self, mover, buffers, out, lhs, rhs):
        self.mover, self.out, self.lhs, self.rhs = mover, out, lhs, rhs
        self.give, self.got, self.mid, self.line = buffers
        self.half = self.give.shape[0]
        self.block = self.half // mover.ctx_count

    def compute(self, target, shard):
        chunk = min(256, self.half)

        def step(i, carry):
            at = pl.ds(pl.multiple_of(shard * self.half + i * chunk, chunk), chunk)
            here = pl.ds(pl.multiple_of(i * chunk, chunk), chunk)
            target[here, :] = dot(self.lhs[:, at], self.rhs[...], ((0,), (0,))).astype(LOW)
            return carry

        lax.fori_loop(0, self.half // chunk, step, 0)

    def begin_blocks(self):
        mover = self.mover
        self.blocks = {}
        for bits in (3, 2, 1, 0):
            ctx = mover.flip(bits)
            at = pl.ds(pl.multiple_of(ctx * self.block, self.block), self.block)
            start = pl.multiple_of((1 - mover.shard) * self.half + ctx * self.block, self.block)
            lhs = self.lhs[:, pl.ds(start, self.block)]
            self.give[at, :] = dot(lhs, self.rhs[...], ((0,), (0,))).astype(LOW)
            self.blocks[bits] = mover.go(
                self.give.at[at], self.got.at[at], shard=1 - mover.shard
            )

    def own(self):
        self.compute(self.mid, self.mover.shard)

    def fold_blocks(self, *which):
        mover = self.mover
        for bits in which:
            mover.take(self.blocks[bits])
            ctx = mover.flip(bits)
            at = pl.ds(pl.multiple_of(ctx * self.block, self.block), self.block)
            self.mid[at, :] = (
                self.mid[at, :].astype(FULL) + self.got[at, :].astype(FULL)
            ).astype(LOW)

    def rows(self, ctx):
        return self.mid.at[pl.ds(pl.multiple_of(ctx * self.block, self.block), self.block)]

    def send_first(self):
        mover = self.mover
        self.first = mover.go(self.rows(mover.flip(3)), self.line.at[1], ctx=mover.flip(1))

    def send_second(self):
        mover = self.mover
        self.second = mover.go(self.rows(mover.flip(1)), self.line.at[0], ctx=mover.flip(1))

    def send_third(self):
        mover = self.mover
        mover.take(self.first)
        rows = self.rows(mover.flip(2))
        rows[...] = (rows[...].astype(FULL) + self.line[1].astype(FULL)).astype(LOW)
        self.third = mover.go(rows, self.line.at[2], ctx=mover.flip(2))

    def done(self):
        self.mover.take(self.second)
        self.mover.take(self.third)
        value = self.rows(self.mover.ctx)[...].astype(FULL)
        self.out[...] = value + self.line[0].astype(FULL) + self.line[2].astype(FULL)


def reduce_buffers(half, width, count):
    return [
        VMEM((half, width), LOW),
        VMEM((half, width), LOW),
        VMEM((half, width), LOW),
        VMEM((count - 1, half // count, width), LOW),
    ]


def greet(mover, shard):
    barrier = pltpu.get_barrier_semaphore()
    peers = [dict(ctx=mover.on(by)) for by in range(1, mover.ctx_count)]
    peers += [dict(tp=peer) for peer in tp_peers()]
    if shard:
        peers.append(dict(shard=1 - mover.shard))
    for peer in peers:
        pl.semaphore_signal(barrier, inc=1, device_id=peer, device_id_type=MESH)
    pl.semaphore_wait(barrier, len(peers))


def tp_peers():
    place = lax.axis_index("tp")
    core, far = lax.rem(place, 2), place // 2
    return place + 1 - 2 * core, place + 2 - 4 * far


def run(kernel, name, ident, inputs, outputs, scratch, remote, local, sizes, vmem, flops):
    n_in, n_out, n_scratch = len(inputs), len(outputs), len(scratch)

    def body(*refs):
        ins, outs = refs[:n_in], refs[n_in : n_in + n_out]
        work = refs[n_in + n_out :]
        mover = Mover(sizes, *work[n_scratch:])
        kernel(mover, ins, outs, work[:n_scratch])

    return pl.pallas_call(
        body,
        in_specs=[pl.BlockSpec(memory_space=space) for _, space in inputs],
        out_specs=[pl.BlockSpec(memory_space=space) for _, _, space in outputs],
        out_shape=[jax.ShapeDtypeStruct(shape, dtype) for shape, dtype, _ in outputs],
        scratch_shapes=list(scratch)
        + [
            pltpu.SemaphoreType.DMA((remote,)),
            pltpu.SemaphoreType.DMA((remote,)),
            pltpu.SemaphoreType.DMA((local,)),
        ],
        compiler_params=pltpu.CompilerParams(
            collective_id=ident, has_side_effects=True, vmem_limit_bytes=vmem * 2**20
        ),
        cost_estimate=pl.CostEstimate(flops=flops, bytes_accessed=2**24, transcendentals=0),
        name=name,
    )(*[value for value, _ in inputs])


def order_of(block, count):
    return (block + count - 1) % count


def tiles_of(count, capacity, tile):
    ends = [-(-(p + 1) * capacity // tile) for p in range(count)]
    return list(zip([0] + ends[:-1], ends))


def tile_at(t, tile):
    return pl.ds(pl.multiple_of(t * tile, tile), tile)


def turned_product(left, right, bias, target):
    value = jnp.dot(left[...], right[...], preferred_element_type=FULL)
    if bias is not None:
        value = value + bias[0:1, :]
    target[...] = turned(value.astype(LOW))


def head_rows(ref, head, width):
    return ref.at[pl.ds(pl.multiple_of(head * width, 16), width)]


def attend_part(size, tile, mover, joint, bias, heads, qkv, o_ref, lse, work, after_send, begun, between):
    k_ref, q_ref, v_ref, low_ref, score_ref, top_ref = work
    count, width, capacity = qkv.shape
    slots = count * capacity
    sent = [None] + [
        mover.go(head_rows(joint, mover.on(by), width), qkv.at[by], ctx=mover.on(by))
        for by in range(1, count)
    ]
    after_send()
    qkv[0] = head_rows(joint, mover.ctx, width)[...]
    q_ref[size:PAD, :] = jnp.concatenate(
        [jnp.ones((16, slots), LOW), jnp.zeros((PAD - size - 16, slots), LOW)], axis=0
    )

    v_ref[size : size + 16, :] = jnp.ones((16, slots), LOW)

    def prepare(r):
        here = slice(r * capacity, (r + 1) * capacity)
        p = order_of(r, count)
        q_ref[0:size, p * capacity : (p + 1) * capacity] = (
            qkv[r, 0:size, :] * (size**-0.5)
        ).astype(LOW)
        v_ref[0:size, here] = qkv[r, 2 * size : 3 * size, :]
        keys = jnp.concatenate(
            [qkv[r, size : 2 * size, :], bias[:, here], jnp.zeros((PAD - size - 16, capacity), LOW)],
            axis=0,
        )
        k_ref[here, :] = turned(keys)

    prepare(0)
    for by in range(1, count):
        mover.take(sent[by])
        prepare(by)

    begun()
    last = slots // tile - 1
    assert last % 2 == 1

    def phase(t, now, following, then):
        at, ahead = tile_at(t, tile), tile_at(following, tile)
        top = top_ref[now, 0:1, :]
        summed = jnp.zeros((size + 16, tile), FULL)
        new_top = jnp.full((1, tile), NEG_LARGE, FULL)
        for r in range(count):
            here = slice(r * capacity, (r + 1) * capacity)
            scores = jnp.dot(k_ref[here, :], q_ref[:, ahead], preferred_element_type=FULL)
            score_ref[then, here, :] = scores
            new_top = jnp.maximum(new_top, jnp.max(scores, axis=0, keepdims=True))
            weights = jnp.exp(score_ref[now, here, :] - top)
            summed = summed + jnp.dot(
                v_ref[:, here], weights.astype(LOW), preferred_element_type=FULL
            )
        top_ref[then] = jnp.broadcast_to(new_top, (8, tile))
        total = summed[size : size + 1]
        out = summed[0:size] / total
        o_ref[:, at] = out
        low_ref[:, at] = out.astype(LOW)
        lse[:, at] = jnp.broadcast_to(top + jnp.log(total), (8, tile))

    def step(i, carry):
        phase(2 * i, 0, 2 * i + 1, 1)
        phase(2 * i + 1, 1, jnp.minimum(2 * i + 2, last), 0)
        return carry

    scores = jnp.dot(k_ref[...], q_ref[:, 0:tile], preferred_element_type=FULL)
    score_ref[0] = scores
    top_ref[0] = jnp.broadcast_to(jnp.max(scores, axis=0, keepdims=True), (8, tile))
    arriving = []
    for p, (low, high) in enumerate(tiles_of(count, capacity, 2 * tile)):
        lax.fori_loop(low, high, step, 0)
        done = low_ref.at[:, p * capacity : (p + 1) * capacity]
        if p < count - 1:
            there = head_rows(heads, mover.ctx, size)
            arriving.append(mover.go(done, there, ctx=mover.back(p + 1)))
        else:
            head_rows(heads, mover.ctx, size)[...] = low_ref[:, p * capacity : (p + 1) * capacity]
        between(p + 1)
    for copy in arriving:
        mover.take(copy)


def below(row, ones):
    width = row.shape[1]
    high = row.astype(LOW).astype(FULL)
    middle = (row - high).astype(LOW).astype(FULL)
    low = row - high - middle
    lead = jnp.full((1, width), 1.0 if ones else 0.0, FULL)
    rest = jnp.zeros((PAD // 2 - 4, width), FULL)
    return jnp.concatenate([lead, high, middle, low, rest], axis=0).astype(LOW)


def attend_back_part(size, tile, mover, parts, bias, qkv, o_ref, lse, grads, work, ready, waiting, begun, between):
    k_ref, v_ref, q_ref, do_ref, nat_ref, dq_ref, dk_ref, dv_ref, got, back = work
    count, width, capacity = qkv.shape
    slots = count * capacity
    sent = [None] + [
        mover.go(head_rows(parts, mover.on(by), size), got.at[by], ctx=mover.on(by))
        for by in range(1, count)
    ]
    got[0] = head_rows(parts, mover.ctx, size)[...]
    waiting()
    ready()
    q_ref[size:PAD, :] = below(lse[0:1, :], True)
    dq_ref[...] = jnp.zeros_like(dq_ref)
    off = (lax.broadcasted_iota(jnp.int32, (16, capacity), 0) + 2) // 3
    taken = jnp.where(off == 1, -1.0, 0.0).astype(LOW)
    pad = jnp.zeros((PAD - size - 16, capacity), LOW)
    for r in range(count):
        here = slice(r * capacity, (r + 1) * capacity)
        k_ref[here, :] = turned(
            jnp.concatenate([qkv[r, size : 2 * size, :], bias[:, here] + taken, pad], axis=0)
        )
        v_ref[here, :] = turned(
            jnp.concatenate([qkv[r, 2 * size : 3 * size, :], taken, pad], axis=0)
        )
    for r in range(count):
        if r:
            mover.take(sent[r])
        p = order_of(r, count)
        at = slice(p * capacity, (p + 1) * capacity)
        scaled = (qkv[r, 0:size, :] * (size**-0.5)).astype(LOW)
        dout = got[r]
        q_ref[0:size, at] = scaled
        do_ref[0:size, at] = dout
        nat_ref[at, :] = turned(jnp.concatenate([scaled, dout], axis=0))
        delta = jnp.sum(dout.astype(FULL) * o_ref[:, at], axis=0, keepdims=True)
        do_ref[size:PAD, at] = below(delta, False)

    begun()
    tiles = tiles_of(count, capacity, tile)
    arriving = []
    mine = head_rows(grads, mover.ctx, width)
    for turn, r in enumerate(list(range(1, count)) + [0]):
        here = slice(r * capacity, (r + 1) * capacity)
        dk_ref[...] = jnp.zeros_like(dk_ref)
        dv_ref[...] = jnp.zeros_like(dv_ref)

        def step(t, carry, r=r, here=here):
            at = tile_at(t, tile)
            scores = jnp.dot(k_ref[here, :], q_ref[:, at], preferred_element_type=FULL)
            chance = jnp.exp(scores)
            chance_grad = jnp.dot(v_ref[here, :], do_ref[:, at], preferred_element_type=FULL)
            score_grad = (chance * chance_grad).astype(LOW)
            dq_ref[:, at] += jnp.dot(
                qkv[r, size : 2 * size, :], score_grad, preferred_element_type=FULL
            )
            dk_ref[...] += jnp.dot(score_grad, nat_ref[at, :], preferred_element_type=FULL)
            dv_ref[...] += jnp.dot(
                chance.astype(LOW), nat_ref[at, :], preferred_element_type=FULL
            )
            return carry

        if r:
            lax.fori_loop(0, tiles[-1][1], step, 0)
        else:
            for p, (low, high) in enumerate(tiles):
                lax.fori_loop(low, high, step, 0)
                at = slice(p * capacity, (p + 1) * capacity)
                value = (dq_ref[:, at] * (size**-0.5)).astype(LOW)
                if p < count - 1:
                    back[p + 1, 0:size, :] = value
                    arriving.append(
                        mover.go(
                            back.at[p + 1, 0:size], mine.at[0:size], ctx=mover.back(p + 1)
                        )
                    )
                else:
                    mine[0:size, :] = value
        keys = dk_ref[...].T[0:size].astype(LOW)
        values = dv_ref[...].T[size : 2 * size].astype(LOW)
        if r:
            back[r, size : 2 * size, :] = keys
            back[r, 2 * size : 3 * size, :] = values
            arriving.append(
                mover.go(
                    back.at[r, size : 3 * size], mine.at[size : 3 * size], ctx=mover.back(r)
                )
            )
        else:
            mine[size : 2 * size, :] = keys
            mine[2 * size : 3 * size, :] = values
        between(turn)
    for copy in arriving:
        mover.take(copy)


def attend_back_buffers(size, count, capacity):
    slots = count * capacity
    return [
        VMEM((slots, PAD), LOW),
        VMEM((slots, PAD), LOW),
        VMEM((PAD, slots), LOW),
        VMEM((PAD, slots), LOW),
        VMEM((slots, PAD), LOW),
        VMEM((size, slots), FULL),
        VMEM((capacity, PAD), FULL),
        VMEM((capacity, PAD), FULL),
        VMEM((count, size, capacity), LOW),
        VMEM((count, 3 * size, capacity), LOW),
    ]


class Round:
    def __init__(self, mover, rows, full, buffers):
        place = lax.axis_index("tp")
        core, far = lax.rem(place, 2), place // 2
        self.mover, self.full = mover, full
        self.give, self.ra, self.passing, self.rb, self.keep = buffers
        self.span = rows // 4
        self.half = self.span // 2
        self.mate, self.far = tp_peers()

        def quarter(c, f):
            return (c * 2 + f) * self.span

        self.own, self.other = quarter(core, far), quarter(core, 1 - far)
        self.mate_own, self.mate_other = quarter(1 - core, far), quarter(1 - core, 1 - far)

    def rows(self, start, count=None):
        return pl.ds(pl.multiple_of(start, 16), count or self.span)

    def hand(self, slot, value):
        self.give[slot] = value.astype(LOW)
        return self.mover.go(self.give.at[slot], self.ra.at[slot], tp=self.mate)

    def onward(self, value, index):
        self.mover.take(index)
        self.passing[...] = (value + self.ra[1].astype(FULL)).astype(LOW)
        return [
            self.mover.go(self.passing.at[at], self.rb.at[at], tp=self.far)
            for at in (pl.ds(0, self.half), pl.ds(self.half, self.half))
        ]

    def close(self, far_copies, index, finish, halfway=None):
        self.mover.take(index)
        self.keep[...] += self.ra[0].astype(FULL)
        self.to_far, self.to_mate = [], []
        for c in range(2):
            at = pl.ds(c * self.half, self.half)
            self.mover.take(far_copies[c])
            low = finish(at, self.keep[at] + self.rb[at].astype(FULL))
            mine = self.full.at[self.rows(self.own + c * self.half, self.half)]
            mine[...] = low
            self.to_far.append(self.mover.go(mine, mine, tp=self.far))
            self.to_mate.append(self.mover.go(mine, mine, tp=self.mate))
            if halfway and c == 0:
                halfway()

    def eager(self, make, finish, meanwhile=None, halfway=None):
        first = self.hand(1, make(self.mate_other))
        copies = self.onward(make(self.other), first)
        second = self.hand(0, make(self.mate_own))
        self.keep[...] = make(self.own)
        if meanwhile:
            meanwhile()
        self.close(copies, second, finish, halfway)

    def after(self, before, make, finish, meanwhile, between):
        before.have_mate_own()
        second = self.hand(0, make(self.mate_own))
        self.keep[...] = make(self.own)
        before.have_other()
        between()
        value = make(self.other)
        before.have_mate_other()
        first = self.hand(1, make(self.mate_other))
        copies = self.onward(value, first)
        meanwhile()
        self.close(copies, second, finish)

    def have_mate_own(self):
        for copy in self.to_mate:
            self.mover.take(copy)

    def have_other(self):
        self.passed = []
        for c in range(2):
            self.mover.take(self.to_far[c])
            rows = self.full.at[self.rows(self.other + c * self.half, self.half)]
            self.passed.append(self.mover.go(rows, rows, tp=self.mate))

    def have_mate_other(self):
        for copy in self.passed:
            self.mover.take(copy)

    def have(self):
        self.have_mate_own()
        self.have_other()
        self.have_mate_other()


ROUND_COPIES = 10


def round_buffers(rows, width):
    span = rows // 4
    return [
        VMEM((2, span, width), LOW),
        VMEM((2, span, width), LOW),
        VMEM((span, width), LOW),
        VMEM((span, width), LOW),
        VMEM((span, width), FULL),
    ]


NAMES = ("qkv", "out", "up", "down")


def layer_kernel(plan, last, size, tile, mover, ins, outs, work):
    ins, outs, work = iter(ins), iter(outs), iter(work)
    source = next(ins)
    x_ref = None if plan.entry else next(ins)
    live_ref = next(ins)
    far_params = [next(ins) for _ in range(8)]
    stream, following = next(outs), next(outs)
    far_qkv, far_o, far_lse, far_heads, far_middle, far_second, far_hidden, far_slope = [
        next(outs) for _ in range(8)
    ]
    far_first = next(outs) if plan.entry else None
    joint, nat, heads, qkv, o_ref, lse, middle, second, hidden, slope = [
        next(work) for _ in range(10)
    ]
    first = next(work) if plan.entry else source
    attend_work = [next(work) for _ in range(6)]
    one_work, two_work = [next(work) for _ in range(5)], [next(work) for _ in range(5)]
    rows = source.shape[0]
    bias, qkv_bias = next(work), next(work)
    params = [next(work) for _ in range(8)]
    whole = {name: next(work) for name in NAMES}
    gathers, loads = {}, {}
    for name in plan.held:
        loads[name] = (next(ins), whole[name])
    half_refs = {name: next(ins) for name in plan.halves}
    for name in plan.own:
        gathers[name, 0] = Gather(mover, next(ins).at[plan.layer], whole[name])
    kept_ahead = {name: next(outs) for name in plan.ahead + plan.lines}
    for name in plan.ahead + plan.lines:
        gathers[name, 1] = Gather(
            mover, next(ins).at[plan.layer + 1], next(work), name in plan.ahead
        )
    kept = {name: next(outs) for name in plan.kept}

    greet(mover, bool(gathers))
    halves = {name: Across(mover, half_refs[name], whole[name]) for name in plan.halves}
    if plan.entry:
        gathers_first = [key for key in [("qkv", 0)] if key in gathers]
        for key in gathers_first:
            gathers[key].start_line()
            gathers[key].start_over()
    param_loads = [mover.stay(there, here) for there, here in zip(far_params, params)]
    waiting_loads = dict(loads)
    loads = {}

    def load(names):
        for name in names:
            if name in waiting_loads and name not in loads:
                loads[name] = mover.stay(*waiting_loads[name])

    load(["qkv"])

    def have(name):
        if name in waiting_loads:
            mover.near(loads[name])
            load(NAMES)
        else:
            (halves[name] if name in halves else gathers[name, 0]).have()
            mover.stay(whole[name], kept[name])
        return whole[name]

    def begin(keys):
        for key in keys:
            if key in gathers:
                gathers[key].start_line()

    def begin_over(keys):
        for key in keys:
            if key in gathers:
                gathers[key].start_over()

    def pass_on(keys, stage):
        for key in keys:
            if key in gathers:
                gathers[key].pass_on(stage)

    def pass_all(keys):
        for stage in (1, 2, 3):
            pass_on(keys, stage)

    mover.near(*param_loads)
    layer, after = plan.layer, min(plan.layer + 1, params[0].shape[0] - 1)

    def row(index, layer=layer):
        return params[index][...].astype(FULL)[layer : layer + 1]

    b_out, gain2, shift2, b_down, b_up = row(0), row(1), row(2), row(3), row(6)
    gain1, shift1, gain0, shift0 = row(4, after), row(5, after), row(4), row(5)
    qkv_bias[...] = joint_bias(row(7), size, joint.shape[0])
    key_bias(mover, live_ref, bias)
    ahead, lines = [("qkv", 1)], [("out", 1), ("up", 1)]
    one = Round(mover, rows, second, one_work)
    two = Round(mover, rows, following, two_work)
    if plan.entry:
        chunk = rows // 5 if rows % 80 == 0 else rows

        def norm_step(i, carry):
            at = pl.ds(pl.multiple_of(i * chunk, 16), chunk)
            value = normalize(source[at, :].astype(FULL), gain0, shift0)[0]
            first[at, :] = value.astype(LOW)
            return carry

        lax.fori_loop(0, rows // chunk, norm_step, 0)
        mover.stay(first, far_first)
        pass_all([("qkv", 0)])
        begin([("out", 0), ("up", 0)])
        begin_over([("out", 0), ("up", 0), ("down", 0)] + ahead + lines)
        turned_product(first, have("qkv"), qkv_bias, joint)
    else:
        turned_product(first, have("qkv"), qkv_bias, joint)

    def after_send():
        if plan.entry:
            pass_all([("out", 0), ("up", 0)])
        else:
            for name in plan.own:
                gathers[name, 0].start_over()

    def begun():
        begin([("down", 0)])

    def between(p):
        if p > 2:
            pass_on([("down", 0)], p - 2)
        if p == 4:
            if not plan.entry:
                begin_over(ahead + lines)
            begin(ahead)

    attend_part(
        size, tile, mover, joint, bias, heads, qkv, o_ref, lse, attend_work, after_send, begun, between
    )
    nat[...] = turned(heads[...])
    w_out = have("out")

    def out_part(start):
        return dot(nat[one.rows(start), :], w_out[...], ((1,), (1,)))

    def to_second(at, value):
        if plan.entry:
            before = source[one.rows(one.own + at.start, at.size), :].astype(FULL)
        else:
            before = x_ref[at]
        value = before + value + b_out
        middle[at] = value
        return normalize(value, gain2, shift2)[0].astype(LOW)

    def meanwhile():
        mover.stay(qkv, far_qkv)
        mover.stay(o_ref, far_o)
        mover.stay(lse, far_lse)
        mover.stay(nat, far_heads)
        pass_on([("down", 0)], 3)

    one.eager(out_part, to_second, meanwhile, lambda: pass_on(ahead, 1))
    pass_on(ahead, 2)
    begin(lines)
    w_up, w_down = have("up"), have("down")

    def mlp_part(start):
        at = two.rows(start)
        pre = jnp.dot(second[at, :], w_up[...], preferred_element_type=FULL) + b_up
        low, low_slope = gelu_pair(pre)
        hidden[at, :] = low
        slope[at, :] = low_slope
        return dot(low, w_down[...], ((1,), (1,)))

    def to_following(at, value):
        value = middle[at] + value + b_down
        stream[at] = value
        if last:
            return live_rows(value, two.own + at.start, live_ref[0, mover.ctx]).astype(LOW)
        return normalize(value, gain1, shift1)[0].astype(LOW)

    def meanwhile():
        mover.stay(middle, far_middle)
        mover.stay(second, far_second)
        mover.stay(hidden, far_hidden)
        mover.stay(slope, far_slope)
        pass_on(lines, 1)

    two.after(one, mlp_part, to_following, meanwhile, lambda: pass_on(ahead, 3))
    two.have()
    pass_on(lines, 2)
    pass_on(lines, 3)
    for name in plan.ahead + plan.lines:
        gathers[name, 1].have()
        mover.stay(gathers[name, 1].target, kept_ahead[name])
    mover.settle()


class Plan:
    def __init__(self, layer, last, inside):
        self.layer, self.entry = layer, layer == 0
        self.own = (NAMES if layer == 0 else ("down",)) if inside else ()
        self.halves = ("out", "up") if inside and layer else ()
        self.ahead = ("qkv",) if inside and not last else ()
        self.lines = ("out", "up") if inside and not last else ()
        self.kept = self.own + self.halves
        self.held = tuple(name for name in NAMES if name not in self.kept)


def forward_layer(source, x, live, params, gathered, weights, plan, last, size, sizes, ident):
    rows, width = source.shape
    count = sizes[0]
    joint, hidden = weights["qkv"].shape[2], weights["up"].shape[2]
    heads = joint // (3 * size)
    attn, slots, span = heads * size, count * rows, rows // 4
    tile = 256 if slots % 256 == 0 else PAD
    columns = {"qkv": joint, "out": attn, "up": hidden, "down": hidden}
    inputs = [(source, VMEM)] + ([] if plan.entry else [(x, VMEM)])
    inputs += [(live, SMEM)] + [(value, HBM) for value in params]
    inputs += [(gathered[name, plan.layer], HBM) for name in plan.held]
    inputs += [(gathered[name, plan.layer, 0], HBM) for name in plan.halves]
    inputs += [(weights[name], HBM) for name in plan.own + plan.ahead + plan.lines]
    saved = [
        ((count, 3 * size, rows), LOW),
        ((size, slots), FULL),
        ((8, slots), FULL),
        ((rows, attn), LOW),
        ((span, width), FULL),
        ((rows, width), LOW),
        ((rows, hidden), LOW),
        ((rows, hidden), LOW),
    ]
    outputs = [((span, width), FULL, VMEM), ((rows, width), LOW, VMEM)]
    outputs += [(shape, dtype, HBM) for shape, dtype in saved]
    if plan.entry:
        outputs.append(((rows, width), LOW, HBM))
    ahead = [(width, columns[name]) for name in plan.ahead]
    ahead += [(width // 2, columns[name]) for name in plan.lines]
    outputs += [(shape, LOW, HBM) for shape in ahead]
    outputs += [((width, columns[name]), LOW, HBM) for name in plan.kept]
    qkv_shape, o_shape, lse_shape, heads_shape = saved[:4]
    scratch = [VMEM((joint, rows), LOW), VMEM((rows, attn), LOW), VMEM((attn, rows), LOW)]
    scratch += [VMEM(*pair) for pair in saved[:3] + saved[4:]]
    if plan.entry:
        scratch.append(VMEM((rows, width), LOW))
    scratch += [
        VMEM((slots, PAD), LOW),
        VMEM((PAD, slots), LOW),
        VMEM((size + 16, slots), LOW),
        VMEM((size, slots), LOW),
        VMEM((2, slots, tile), FULL),
        VMEM((2, 8, tile), FULL),
    ]
    scratch += round_buffers(rows, width) + round_buffers(rows, width)
    scratch += [VMEM((16, slots), LOW), VMEM((16, joint), FULL)]
    scratch += [VMEM(value.shape, value.dtype) for value in params]
    scratch += [VMEM((width, columns[name]), LOW) for name in NAMES]
    scratch += [VMEM(shape, LOW) for shape in ahead]
    results = run(
        functools.partial(layer_kernel, plan, last, size, tile),
        "forward_layer",
        ident,
        inputs,
        outputs,
        scratch,
        2 * (count - 1) + 2 * ROUND_COPIES + 2 * count * len(plan.kept + plan.ahead + plan.lines),
        10 + 2 * len(plan.kept + plan.ahead + plan.lines) + len(plan.held) + len(params),
        sizes,
        58,
        2 * rows * width * (2 * hidden + attn + joint) + 4 * slots * slots * 256,
    )
    stream, following = results[:2]
    kept = results[2 : 11 if plan.entry else 10]
    rest = iter(results[2 + len(kept) :])
    for name in plan.ahead:
        gathered[name, plan.layer + 1] = next(rest)
    for name in plan.lines:
        gathered[name, plan.layer + 1, 0] = next(rest)
    for name in plan.kept:
        gathered[name, plan.layer] = next(rest)
    return stream, following, kept


class SmallSums:
    def __init__(self, mover, rows, held, got):
        self.mover, self.rows, self.held, self.got = mover, rows, held, got
        self.stage = 0
        mate, far = tp_peers()
        self.peers = [
            dict(tp=mate),
            dict(tp=far),
            dict(shard=1 - mover.shard),
            dict(ctx=mover.flip(2)),
            dict(ctx=mover.flip(1)),
        ]

    def part(self, stage):
        return pl.ds(0, self.rows if stage < 2 else self.held.shape[1])

    def step(self):
        stage, mover = self.stage, self.mover
        if stage:
            mover.take(self.copy)
            at = self.part(stage - 1)
            self.held[stage] = self.held[stage - 1]
            self.held[stage, at, :] = self.held[stage - 1, at, :] + self.got[stage - 1, at, :]
        if stage < len(self.peers):
            at = self.part(stage)
            self.copy = mover.go(
                self.held.at[stage, at], self.got.at[stage, at], **self.peers[stage]
            )
        self.stage = stage + 1

    def value(self):
        return self.held[len(self.peers)]


def key_bias(mover, live_ref, bias):
    capacity = bias.shape[1] // mover.ctx_count
    row = lax.broadcasted_iota(jnp.int32, (16, capacity), 0)
    slot = lax.broadcasted_iota(jnp.int32, (16, capacity), 1)
    for r in range(mover.ctx_count):
        live = live_ref[0, mover.back(r)]
        value = jnp.where((row == 0) & (slot >= live), NEG_LARGE, 0.0)
        bias[:, r * capacity : (r + 1) * capacity] = value.astype(LOW)


def pair_columns(rows, width, size, turn):
    shape = (width, rows) if turn else (rows, width)
    given = lax.broadcasted_iota(jnp.int32, shape, 1 if turn else 0)
    column = lax.broadcasted_iota(jnp.int32, shape, 0 if turn else 1)
    head, within = column // (3 * size), column % (3 * size)
    wanted = head * (2 * size) + jnp.where(within < size, within, within - size)
    key = (within >= size) & (within < 2 * size)
    return jnp.where((given == wanted) & ~key, 1.0, 0.0).astype(LOW)


def joint_bias(pair, size, width):
    rows = pair.shape[1]
    spread = jnp.broadcast_to(pair, (16, rows)).astype(LOW)
    return jnp.dot(spread, pair_columns(rows, width, size, False), preferred_element_type=FULL)


def live_rows(value, start, live):
    row = start + lax.broadcasted_iota(jnp.int32, value.shape, 0)
    return jnp.where(row < live, value, 0.0)


def sums_into(sums, first, at, values):
    for index, value in enumerate(values):
        row = first + index
        added = jnp.sum(value, axis=0, keepdims=True)
        width = added.shape[1]
        sums[row : row + 1, 0:width] = (
            added if at.start == 0 else sums[row : row + 1, 0:width] + added
        )


def back_kernel(plan, size, tile, mover, ins, outs, work):
    ins, outs, work = iter(ins), iter(outs), iter(work)
    source = next(ins)
    x_ref = None if plan.last else next(ins)
    live_ref, far_gain2, far_gain1 = [next(ins) for _ in range(3)]
    far = [next(ins) for _ in range(14)]
    late_far = next(ins) if plan.late else None
    others = [(next(ins), next(ins)) for _ in range(plan.others)]
    stream, following = next(outs), next(outs)
    grad_outs = {name: next(outs) for name in NAMES if plan.inside and (name != "qkv" or plan.final)}
    mid_out = next(outs) if plan.inside and not plan.final else None
    late_out = next(outs) if plan.late else None
    split = local = totals = None
    if plan.joined:
        totals = next(outs)
    else:
        split, local = next(outs), next(outs)
    wholes = {} if plan.inside else {name: next(outs) for name in NAMES}
    near = [next(work) for _ in range(14)]
    slope, w_down, w_up, middle, hidden, second, w_out, heads, qkv, o_ref, lse, first, w_qkv, before = near
    grad = next(work) if plan.last else source
    pre_grad, attn_grad, parts, grads, nat = [next(work) for _ in range(5)]
    attend_work = [next(work) for _ in range(10)]
    one_work, two_work = [next(work) for _ in range(5)], [next(work) for _ in range(5)]
    rows, width = source.shape
    reduces = {}
    if plan.inside:
        pairs = {
            "down": (grad, hidden),
            "up": (second, pre_grad),
            "out": (attn_grad, heads),
            "qkv": (first, nat),
        }
        for name in ("down", "up", "out", "qkv"):
            buffers = [next(work) for _ in range(4)]
            reduces[name] = Reduce(mover, buffers, grad_outs.get(name), *pairs[name])
    late = None
    if plan.late:
        late_mid, late_line = next(work), next(work)
        late = Reduce(mover, (late_mid, None, late_mid, late_line), late_out, None, None)
    bias, gain2_ref, gain1_ref = [next(work) for _ in range(3)]
    if plan.joined:
        split, local = next(work), next(work)
        early_held, early_got, late_held, late_got = [next(work) for _ in range(4)]
        tops = 8 * (plan.others + 1)
        early = SmallSums(mover, tops, early_held, early_got)
        final = SmallSums(mover, 8, late_held, late_got)
        everything = [(split, local)] + others

    greet(mover, plan.inside)
    gain_loads = [mover.stay(far_gain2, gain2_ref), mover.stay(far_gain1, gain1_ref)]
    one = Round(mover, rows, attn_grad, one_work)
    two = Round(mover, rows, following, two_work)
    if plan.final:
        far[13] = far[13].at[two.rows(two.own)]
    load = {index: mover.stay(far[index], near[index]) for index in (0, 1, 2)}
    if late:
        mover.near(mover.stay(late_far, late_mid))
        late.send_first()
        late.send_second()
    if plan.last:
        chunk = rows // 5 if rows % 80 == 0 else rows

        def mask_step(i, carry):
            at = pl.ds(pl.multiple_of(i * chunk, 16), chunk)
            value = source[at, :].astype(FULL)
            grad[at, :] = live_rows(value, i * chunk, live_ref[0, mover.ctx]).astype(LOW)
            return carry

        lax.fori_loop(0, rows // chunk, mask_step, 0)
    key_bias(mover, live_ref, bias)
    mover.near(*gain_loads)
    gain2, gain1 = [
        ref[...].astype(FULL)[plan.layer : plan.layer + 1] for ref in (gain2_ref, gain1_ref)
    ]
    split[...] = jnp.zeros_like(split)
    local[...] = jnp.zeros_like(local)
    split[5:6, 0:width] = jnp.sum(
        grad[one.rows(one.own), :].astype(FULL), axis=0, keepdims=True
    )
    hidden_width = slope.shape[1]

    def mlp_part(start):
        at = one.rows(start)
        pre = jnp.dot(grad[at, :], w_down[...], preferred_element_type=FULL)
        low = (pre * slope[at, :].astype(FULL)).astype(LOW)
        pre_grad[at, :] = low
        local[0:1, 0:hidden_width] += jnp.sum(low.astype(FULL), axis=0, keepdims=True)
        return dot(low, w_up[...], ((1,), (1,)))

    def to_attn(at, value):
        if plan.last:
            above = grad[one.rows(one.own + at.start, at.size), :].astype(FULL)
        else:
            above = x_ref[at]
        _, normed, inverse = normalize(middle[at], 1.0, 0.0)
        result = above + normalize_back(value, normed, inverse, gain2)
        stream[at] = result
        low = result.astype(LOW)
        sums_into(split, 2, at, (value * normed, value, low.astype(FULL)))
        return low

    def reduce(name):
        if name in reduces:
            reduces[name].begin_blocks()

    def own(name):
        if name in reduces:
            reduces[name].own()

    def first_step(name):
        if name in reduces:
            reduces[name].fold_blocks(3)
            reduces[name].send_first()

    def second_step(name):
        if name in reduces:
            reduces[name].fold_blocks(2)
            reduces[name].send_third()

    def rest(name):
        if name in reduces:
            reduces[name].fold_blocks(1)
            reduces[name].send_second()
            reduces[name].fold_blocks(0)

    def begin_early():
        if plan.joined:
            early_held[0] = jnp.zeros(early_held.shape[1:], FULL)
            for layer, (some, more) in enumerate(everything):
                first_row = 0 if layer else 2
                for row in range(first_row, 6):
                    at = row * len(everything) + layer
                    early_held[0, at : at + 1, :] = some[row : row + 1, :]
                for row in range(2 if layer else 1):
                    at = tops + row * len(everything) + layer
                    early_held[0, at : at + 1, :] = more[row : row + 1, :]

    def early_step():
        if plan.joined:
            early.step()

    def start_down():
        mover.near(load[3], load[4])
        reduce("down")
        if late:
            late.send_third()

    mover.near(load[0], load[1], load[2])
    for index in range(3, len(far)):
        load[index] = mover.stay(far[index], near[index])
    one.eager(mlp_part, to_attn, start_down)
    mover.near(load[5])
    reduce("up")
    one.have()
    mover.near(load[6])
    turned_product(attn_grad, w_out, None, parts)

    def waiting():
        begin_early()
        early_step()
        own("down")
        first_step("down")
        mover.near(load[7])
        reduce("out")
        own("out")

    def ready():
        own("up")
        mover.near(load[8], load[9], load[10])

    def between(turn):
        if turn == 0:
            early_step()
        if turn == 3:
            second_step("down")
            first_step("up")
            rest("down")

    attend_back_part(
        size,
        tile,
        mover,
        parts,
        bias,
        qkv,
        o_ref,
        lse,
        grads,
        attend_work,
        ready,
        waiting,
        lambda: None,
        between,
    )
    early_step()
    nat[...] = turned(grads[...])
    pairs_width = nat.shape[1] // 3 * 2
    picked = jnp.dot(
        nat[...], pair_columns(pairs_width, nat.shape[1], size, True), preferred_element_type=FULL
    )
    local[1:2, 0:pairs_width] = jnp.sum(picked, axis=0, keepdims=True)
    mover.near(*[load[index] for index in range(11, len(far))])

    def qkv_part(start):
        return dot(nat[two.rows(start), :], w_qkv[...], ((1,), (1,)))

    def to_following(at, value):
        row = before[at, :].astype(FULL)
        _, normed, inverse = normalize(row, 1.0, 0.0)
        result = stream[at] + normalize_back(value, normed, inverse, gain1)
        stream[at] = result
        low = result.astype(LOW)
        sums_into(split, 0, at, (value * normed, value))
        return low

    def meanwhile():
        own("qkv")
        second_step("up")
        first_step("out")
        rest("up")
        early_step()

    def halfway():
        if plan.inside:
            reduces["qkv"].fold_blocks(3)
            if plan.final:
                reduces["qkv"].send_first()

    reduce("qkv")
    two.eager(qkv_part, to_following, meanwhile, halfway)
    if plan.joined:
        late_held[0, 0:8, :] = jnp.zeros((8, late_held.shape[2]), FULL)
        late_held[0, 0:2, :] = split[0:2, :]
        late_held[0, 8:16, :] = local[...]
        final.step()
        final.step()
    two.have_mate_own()
    two.have_other()
    if plan.joined:
        final.step()
        early_step()
    second_step("out")
    rest("out")
    if plan.joined:
        final.step()
    if plan.inside:
        last = reduces["qkv"]
        if plan.final:
            second_step("qkv")
            rest("qkv")
        else:
            last.fold_blocks(2, 1, 0)
            mover.stay(last.mid, mid_out)
    two.have_mate_other()
    if plan.joined:
        final.step()
    for name in ("down", "up", "out"):
        if name in reduces:
            reduces[name].done()
    if late:
        late.done()
    if plan.inside and plan.final:
        reduces["qkv"].done()
    if plan.joined:
        final.step()
        early.step()
        totals[...] = early.value()
        last_value = final.value()
        for row in range(2):
            at = row * len(everything)
            totals[at : at + 1, :] = last_value[row : row + 1, :]
        at = tops + len(everything)
        totals[at : at + 1, :] = last_value[9:10, :]
    if not plan.inside:
        for name, (lhs, rhs) in {
            "down": (grad, hidden),
            "up": (second, pre_grad),
            "out": (attn_grad, heads),
            "qkv": (first, nat),
        }.items():
            full = Reduce(mover, (wholes[name],) * 4, None, lhs, rhs)
            full.compute(wholes[name], 0)
    mover.settle()


def gather_outputs_kernel(layers, *refs):
    count = layers * len(NAMES)
    parts, token_grads, mixed, totals = refs[:count], refs[count], refs[count + 1], refs[count + 2]
    outs, work = refs[count + 3 : count + 17], refs[count + 17 : -2]
    into, out_of = refs[-2:]
    coming, going = [], []
    pairs = [(mixed, work[4], outs[4].at[0])]
    for index in range(len(NAMES)):
        for layer in range(layers):
            pairs.append(
                (parts[index * layers + layer], work[index].at[layer], outs[index].at[layer])
            )
    for i, (source, stage, _) in enumerate(pairs):
        coming.append(pltpu.make_async_copy(source, stage, into.at[i]))
        coming[-1].start()
    outs[5][0] = token_grads[...].astype(FULL)
    for row, out in enumerate(outs[6:12]):
        out[...] = totals[row * layers : (row + 1) * layers, 0 : out.shape[1]]
    for row, out in enumerate(outs[12:14]):
        row = row + 8
        out[...] = totals[row * layers : (row + 1) * layers, 0 : out.shape[1]]
    for i, (_, stage, target) in enumerate(pairs):
        coming[i].wait()
        going.append(pltpu.make_async_copy(stage, target, out_of.at[i]))
        going[-1].start()
    for copy in going:
        copy.wait()


def gather_outputs(done, token_grads, mixed, totals, layers, widths):
    rows, width = token_grads.shape
    parts = [done[name, layer] for name in NAMES for layer in range(layers)]
    hbm, whole = pl.BlockSpec(memory_space=HBM), lambda shape: pl.BlockSpec(
        shape, lambda i: (0,) * len(shape)
    )
    shapes = [(layers,) + done[name, 0].shape for name in NAMES] + [(1, rows, width)] * 2
    types = [FULL] * 4 + [LOW, FULL]
    small = [(layers, width)] * 6 + [(layers, count) for count in widths]
    copies = len(parts) + 1
    return pl.pallas_call(
        functools.partial(gather_outputs_kernel, layers),
        grid=(1,),
        in_specs=[hbm] * len(parts) + [whole(token_grads.shape), hbm, whole(totals.shape)],
        out_specs=[hbm] * 5 + [whole(shape) for shape in shapes[5:] + small],
        out_shape=[jax.ShapeDtypeStruct(*pair) for pair in zip(shapes, types)]
        + [jax.ShapeDtypeStruct(shape, FULL) for shape in small],
        scratch_shapes=[VMEM(shape, FULL) for shape in shapes[:4]]
        + [VMEM((rows, width), LOW)]
        + [pltpu.SemaphoreType.DMA((copies,)), pltpu.SemaphoreType.DMA((copies,))],
        compiler_params=pltpu.CompilerParams(vmem_limit_bytes=60 * 2**20),
        name="gather_outputs",
    )(*parts, token_grads, mixed, totals)


class BackPlan:
    def __init__(self, layer, layers, inside):
        self.inside, self.layer = inside, layer
        self.last, self.final = layer == layers - 1, layer == 0
        self.late = inside and not self.last
        self.joined = inside and self.final
        self.others = layers - 1 if self.joined else 0


def back_layer(source, x, live, gain2, gain1, saved, late, others, plan, size, sizes, ident):
    rows, width = source.shape
    count = sizes[0]
    slope, w_down, w_up = saved[:3]
    hidden, joint, attn = slope.shape[1], saved[12].shape[1], saved[6].shape[1]
    slots, span = count * rows, rows // 4
    tile = 512 if slots % 512 == 0 else PAD
    wide = max(width, hidden, joint)
    half = width // 2
    block = half // count
    columns = {"qkv": joint, "out": attn, "up": hidden, "down": hidden}
    inputs = [(source, VMEM)] + ([] if plan.last else [(x, VMEM)])
    inputs += [(live, SMEM), (gain2, HBM), (gain1, HBM)]
    inputs += [(value, HBM) for value in saved]
    if plan.late:
        inputs.append((late, HBM))
    for pair in others[: plan.others]:
        inputs += [(value, VMEM) for value in pair]
    outputs = [((span, width), FULL, VMEM), ((rows, width), LOW, VMEM)]
    names = [name for name in NAMES if plan.inside and (name != "qkv" or plan.final)]
    outputs += [((block, columns[name]), FULL, VMEM) for name in names]
    if plan.inside and not plan.final:
        outputs.append(((half, joint), LOW, HBM))
    if plan.late:
        outputs.append(((block, joint), FULL, VMEM))
    depth = 8 * (plan.others + 1)
    if plan.joined:
        outputs.append(((depth + 8, wide), FULL, VMEM))
    else:
        outputs += [((8, wide), FULL, VMEM)] * 2
    if not plan.inside:
        outputs += [((width, columns[name]), LOW, VMEM) for name in NAMES]
    scratch = [VMEM(value.shape, value.dtype) for value in saved]
    scratch[13] = VMEM((span, width), saved[13].dtype)
    if plan.last:
        scratch.append(VMEM((rows, width), LOW))
    scratch += [
        VMEM((rows, hidden), LOW),
        VMEM((rows, width), LOW),
        VMEM((attn, rows), LOW),
        VMEM((joint, rows), LOW),
        VMEM((rows, joint), LOW),
    ]
    scratch += attend_back_buffers(size, count, rows)
    scratch += round_buffers(rows, width) + round_buffers(rows, width)
    if plan.inside:
        for name in ("down", "up", "out", "qkv"):
            scratch += reduce_buffers(half, columns[name], count)
    if plan.late:
        scratch += [VMEM((half, joint), LOW), VMEM((count - 1, block, joint), LOW)]
    scratch.append(VMEM((16, slots), LOW))
    scratch += [VMEM(value.shape, value.dtype) for value in (gain2, gain1)]
    assert 2 * (plan.others + 1) <= 8
    if plan.joined:
        scratch += [VMEM((8, wide), FULL)] * 2
        scratch += [
            VMEM((6, depth + 8, wide), FULL),
            VMEM((5, depth + 8, wide), FULL),
            VMEM((6, 16, wide), FULL),
            VMEM((5, 16, wide), FULL),
        ]
    results = run(
        functools.partial(back_kernel, plan, size, tile),
        "back_layer",
        ident,
        inputs,
        outputs,
        scratch,
        3 * (count - 1) + 2 * ROUND_COPIES + 8 * count + 10 + count,
        len(saved) + 4,
        sizes,
        58,
        6 * rows * width * (2 * hidden + attn + joint) + 10 * slots * slots * 256,
    )
    return results[:2], names, results[2:]


def shards(
    tokens,
    block_tokens,
    ln1_gain,
    ln1_bias,
    w_qkv,
    b_qv,
    w_out,
    b_out,
    ln2_gain,
    ln2_bias,
    w_up,
    b_up,
    w_down,
    b_down,
    cotangent,
):
    images, capacity, width = tokens.shape
    assert images == 1
    layers = w_qkv.shape[0]
    size = HEAD_DIM
    ctx_count = lax.axis_size("ctx")
    ctx_place = lax.axis_index("ctx")
    joint_width = w_qkv.shape[2]
    heads = joint_width // (3 * size)
    assert heads == ctx_count
    attn_width = heads * size
    hidden_width = w_up.shape[2]
    weights = {"qkv": w_qkv, "out": w_out, "up": w_up, "down": w_down}
    sizes = (ctx_count, lax.axis_size("shard"))
    inside = sizes == (4, 2)
    gathered = {}
    if not inside:
        for name, value in weights.items():
            for layer in range(layers):
                gathered[name, layer] = gather_weight(value[layer])[0]
    source, stream = tokens[0], None
    saved = []
    for layer in range(layers):
        last = layer == layers - 1
        result, following, kept = forward_layer(
            source,
            stream,
            block_tokens,
            (b_out, ln2_gain, ln2_bias, b_down, ln1_gain, ln1_bias, b_up, b_qv),
            gathered,
            weights,
            Plan(layer, last, inside),
            last,
            size,
            sizes,
            1 + layer,
        )
        before = stream if layer else source
        first = source if layer else kept[8]
        saved.append((before, first) + tuple(kept[:8]))
        source, stream = following, result
    mixed = source

    done, packs = {}, {}
    source, stream, late = cotangent[0], None, None
    for layer in reversed(range(layers)):
        before, first, qkv, head_out, lse, heads_low, middle, second, hidden, slope = saved[layer]
        plan = BackPlan(layer, layers, inside)
        whole = {name: gathered[name, layer] for name in NAMES}
        near = [slope, whole["down"], whole["up"], middle, hidden, second, whole["out"]]
        near += [heads_low, qkv, head_out, lse, first, whole["qkv"], before]
        others = [packs[key] for key in sorted(packs)]
        (stream, source), names, rest = back_layer(
            source, stream, block_tokens, ln2_gain, ln1_gain, near, late, others, plan, size, sizes, 1 + layers + layer
        )
        rest = iter(rest)
        for name in names:
            done[name, layer] = next(rest)
        if plan.inside and not plan.final:
            late = next(rest)
        if plan.late:
            done["qkv", layer + 1] = next(rest)
        if plan.joined:
            totals = next(rest)
        else:
            packs[layer] = (next(rest), next(rest))
        if not inside:
            for name in NAMES:
                value = next(rest)
                done[name, layer] = scatter_weight(
                    lambda start, count, value=value: rows_of(value, start, count).astype(FULL),
                    width,
                )
    if not inside:
        split = total_over(("tp",), jnp.stack([packs[l][0] for l in range(layers)], axis=1))
        local = jnp.stack([packs[l][1] for l in range(layers)], axis=1)
        totals = total_over(("shard", "ctx"), jnp.concatenate([split, local[:2]]))
        totals = totals.reshape(10 * layers, -1)
    pairs = b_qv.shape[1]
    outs = gather_outputs(done, source, mixed, totals, layers, (hidden_width, pairs))
    g_qkv, g_out, g_up, g_down, mixed, token_grads = outs[:6]
    g_ln1_gain, g_ln1_bias, g_ln2_gain, g_ln2_bias, g_b_out, g_b_down, g_b_up, g_b_qv = outs[6:]
    return (
        mixed,
        token_grads,
        g_ln1_gain,
        g_ln1_bias,
        g_qkv,
        g_b_qv,
        g_out,
        g_b_out,
        g_ln2_gain,
        g_ln2_bias,
        g_up,
        g_b_up,
        g_down,
        g_b_down,
    )


def solution(mesh):
    split_rows = P(None, ("shard", "ctx"), "tp")
    split_tokens = P("shard", "ctx", None)
    return jax.shard_map(
        shards,
        mesh=mesh,
        in_specs=(
            split_tokens,
            P("shard", None),
            P(),
            P(),
            split_rows,
            P(None, "tp"),
            split_rows,
            P(),
            P(),
            P(),
            split_rows,
            P(None, "tp"),
            split_rows,
            P(),
            split_tokens,
        ),
        out_specs=(
            split_tokens,
            split_tokens,
            P(),
            P(),
            split_rows,
            P(None, "tp"),
            split_rows,
            P(),
            P(),
            P(),
            split_rows,
            P(None, "tp"),
            split_rows,
            P(),
        ),
        check_vma=False,
    )
```

```python
import functools
import math

import jax
import jax.numpy as jnp
from jax import lax
from jax.experimental import pallas as pl
from jax.experimental.pallas import tpu as pltpu
from jax.sharding import PartitionSpec as P

HEAD_DIM = 64
EPSILON = 1e-06
NEG_LARGE = -1e30
LOW = jnp.bfloat16
FULL = jnp.float32
PAD = 128
MESH = pl.DeviceIdType.MESH
VMEM = pltpu.VMEM
HBM = pltpu.HBM
SMEM = pltpu.SMEM


def bits_of(axis):
    size = lax.axis_size(axis)
    assert size & (size - 1) == 0
    return [1 << i for i in range(size.bit_length() - 1)]


def swap(value, axis, bit):
    size = lax.axis_size(axis)
    return lax.ppermute(value, axis, [(i, i ^ bit) for i in range(size)])


def side_of(axis, bit):
    return (lax.axis_index(axis) // bit) % 2


def rows_of(value, start, count, axis=0):
    return lax.dynamic_slice_in_dim(value, start, count, axis)


def halve(axis, bits, partial, total):
    offset, span, received = jnp.int32(0), total, []

    def summed(start, count):
        value = partial(start, count)
        for got, base in received:
            value = value + rows_of(got, start - base, count).astype(FULL)
        return value

    for bit in bits:
        half = span // 2
        side = side_of(axis, bit)
        got = swap(summed(offset + (1 - side) * half, half).astype(LOW), axis, bit)
        offset = offset + side * half
        received.append((got, offset))
        span = half
    return summed(offset, span)


def double(axis, bits, value):
    for bit in bits:
        got = swap(value, axis, bit)
        first = side_of(axis, bit) == 0
        value = jnp.concatenate(
            [jnp.where(first, value, got), jnp.where(first, got, value)], axis=0
        )
    return value


def total_over(axes, value):
    for axis in axes:
        for bit in bits_of(axis):
            value = value + swap(value, axis, bit)
    return value


def ring(value, by):
    count = lax.axis_size("ctx")
    return lax.ppermute(value, "ctx", [(i, (i + by) % count) for i in range(count)])


def gather_weight(piece):
    count = lax.axis_size("ctx")
    place = lax.axis_index("ctx")
    ways = lax.axis_size("shard")
    blocks = [piece] + [ring(piece, by) for by in range(1, count)]
    whole = jnp.zeros((ways * count,) + piece.shape, piece.dtype)
    me = lax.axis_index("shard")
    for by, block in enumerate(blocks):
        at = (place - by) % count
        held = [(jnp.int32(0), block)]
        for bit in bits_of("shard"):
            held = held + [(other ^ bit, swap(value, "shard", bit)) for other, value in held]
        for other, value in held:
            whole = lax.dynamic_update_index_in_dim(whole, value, (me ^ other) * count + at, 0)
    return whole.reshape((ways * count * piece.shape[0],) + piece.shape[1:]), blocks[-1]


def scatter_weight(partial, total):
    count = lax.axis_size("ctx")
    place = lax.axis_index("ctx")
    mine = halve("shard", bits_of("shard")[::-1], partial, total).astype(LOW)
    mine = mine.reshape((count, mine.shape[0] // count) + mine.shape[1:])
    value = lax.dynamic_index_in_dim(mine, place, 0, False).astype(FULL)
    for by in range(1, count):
        given = lax.dynamic_index_in_dim(mine, (place + by) % count, 0, False)
        value = value + ring(given, by).astype(FULL)
    return value


def dot(left, right, contract):
    return lax.dot_general(
        left, right, ((contract[0], contract[1]), ((), ())), preferred_element_type=FULL
    )


def turned(value):
    return value.astype(FULL).T.astype(LOW)


def normalize(rows, gain, shift):
    row_mean = jnp.mean(rows, axis=-1, keepdims=True)
    centred = rows - row_mean
    inverse = lax.rsqrt(jnp.mean(centred * centred, axis=-1, keepdims=True) + EPSILON)
    normed = centred * inverse
    return (normed * gain + shift, normed, inverse)


def normalize_back(grad_out, normed, inverse, gain):
    scaled = grad_out * gain
    mean_grad = jnp.mean(scaled, axis=-1, keepdims=True)
    mean_cross = jnp.mean(scaled * normed, axis=-1, keepdims=True)
    return inverse * (scaled - mean_grad - normed * mean_cross)


def gelu_pair(value):
    spread = 0.5 * (1.0 + lax.erf(value * (0.5**0.5)))
    slope = spread + value * jnp.exp(-0.5 * value * value) * (1.0 / math.sqrt(2.0 * math.pi))
    return (value * spread).astype(LOW), slope.astype(LOW)


class Mover:
    def __init__(self, sizes, send, recv, local):
        self.ctx_count, self.shard_count = sizes
        self.send, self.recv, self.local = send, recv, local
        self.copies, self.here = [], []
        self.arrived = set()
        self.landed = set()
        self.ctx = lax.axis_index("ctx")
        self.shard = lax.axis_index("shard")

    def go(self, source, target, **device):
        index = len(self.copies)
        assert index < self.send.shape[0]
        copy = pltpu.make_async_remote_copy(
            src_ref=source,
            dst_ref=target,
            send_sem=self.send.at[index],
            recv_sem=self.recv.at[index],
            device_id=device,
            device_id_type=MESH,
        )
        copy.start()
        self.copies.append(copy)
        return index

    def stay(self, source, target):
        index = len(self.here)
        assert index < self.local.shape[0]
        copy = pltpu.make_async_copy(source, target, self.local.at[index])
        copy.start()
        self.here.append(copy)
        return index

    def near(self, *indices):
        for index in indices:
            if index not in self.landed:
                self.landed.add(index)
                self.here[index].wait()

    def take(self, index):
        if index not in self.arrived:
            self.arrived.add(index)
            self.copies[index].wait_recv()

    def flip(self, bits):
        place = self.ctx
        if bits & 1:
            place = place + 1 - 2 * lax.rem(self.ctx, 2)
        if bits & 2:
            place = place + 2 - 4 * (self.ctx // 2)
        return place

    def on(self, by):
        return lax.rem(self.ctx + by, self.ctx_count)

    def back(self, by):
        return lax.rem(self.ctx + self.ctx_count - by, self.ctx_count)

    def settle(self):
        for index, copy in enumerate(self.copies):
            self.take(index)
            copy.wait_send()
        self.near(*range(len(self.here)))


class Gather:
    def __init__(self, mover, source, target, across=True):
        self.mover, self.source, self.target, self.across = mover, source, target, across
        self.over = []

    def start_line(self):
        mover = self.mover
        mine, there = self.source, self.block(mover.ctx)
        self.far = mover.go(mine, there, ctx=mover.flip(2))
        self.close = mover.go(mine, there, ctx=mover.flip(1))

    def start_over(self):
        mover = self.mover
        mine, there = self.source, self.block(mover.ctx)
        if self.across:
            self.over.append(mover.go(mine, there, shard=1 - mover.shard))
        self.own = mover.stay(mine, there)

    def block(self, ctx):
        mover = self.mover
        rows = self.source.shape[0]
        start = ctx * rows
        if self.across:
            start = start + mover.shard * mover.ctx_count * rows
        return self.target.at[pl.ds(pl.multiple_of(start, rows), rows)]

    def pass_on(self, stage):
        mover = self.mover
        if stage == 1:
            mover.take(self.far)
            rows = self.block(mover.flip(2))
            self.passed = mover.go(rows, rows, ctx=mover.flip(1))
        elif stage == 2:
            mover.take(self.close)
            rows = self.block(mover.flip(1))
        else:
            mover.take(self.passed)
            rows = self.block(mover.flip(3))
        if self.across:
            self.over.append(mover.go(rows, rows, shard=1 - mover.shard))

    def have(self):
        for copy in self.over:
            self.mover.take(copy)
        self.mover.near(self.own)


class Across:
    def __init__(self, mover, source, target):
        rows = source.shape[0]
        there = target.at[pl.ds(pl.multiple_of(mover.shard * rows, rows), rows)]
        self.mover = mover
        self.copy = mover.go(source, there, shard=1 - mover.shard)
        self.own = mover.stay(source, there)

    def have(self):
        self.mover.take(self.copy)
        self.mover.near(self.own)


class Reduce:
    def __init__(self, mover, buffers, out, lhs, rhs):
        self.mover, self.out, self.lhs, self.rhs = mover, out, lhs, rhs
        self.give, self.got, self.mid, self.line = buffers
        self.half = self.give.shape[0]
        self.block = self.half // mover.ctx_count

    def compute(self, target, shard):
        chunk = min(256, self.half)

        def step(i, carry):
            at = pl.ds(pl.multiple_of(shard * self.half + i * chunk, chunk), chunk)
            here = pl.ds(pl.multiple_of(i * chunk, chunk), chunk)
            target[here, :] = dot(self.lhs[:, at], self.rhs[...], ((0,), (0,))).astype(LOW)
            return carry

        lax.fori_loop(0, self.half // chunk, step, 0)

    def begin_blocks(self):
        mover = self.mover
        self.blocks = {}
        for bits in (3, 2, 1, 0):
            ctx = mover.flip(bits)
            at = pl.ds(pl.multiple_of(ctx * self.block, self.block), self.block)
            start = pl.multiple_of((1 - mover.shard) * self.half + ctx * self.block, self.block)
            lhs = self.lhs[:, pl.ds(start, self.block)]
            self.give[at, :] = dot(lhs, self.rhs[...], ((0,), (0,))).astype(LOW)
            self.blocks[bits] = mover.go(
                self.give.at[at], self.got.at[at], shard=1 - mover.shard
            )

    def own(self):
        self.compute(self.mid, self.mover.shard)

    def fold_blocks(self, *which):
        mover = self.mover
        for bits in which:
            mover.take(self.blocks[bits])
            ctx = mover.flip(bits)
            at = pl.ds(pl.multiple_of(ctx * self.block, self.block), self.block)
            self.mid[at, :] = (
                self.mid[at, :].astype(FULL) + self.got[at, :].astype(FULL)
            ).astype(LOW)

    def rows(self, ctx):
        return self.mid.at[pl.ds(pl.multiple_of(ctx * self.block, self.block), self.block)]

    def send_first(self):
        mover = self.mover
        self.first = mover.go(self.rows(mover.flip(3)), self.line.at[1], ctx=mover.flip(1))

    def send_second(self):
        mover = self.mover
        self.second = mover.go(self.rows(mover.flip(1)), self.line.at[0], ctx=mover.flip(1))

    def send_third(self):
        mover = self.mover
        mover.take(self.first)
        rows = self.rows(mover.flip(2))
        rows[...] = (rows[...].astype(FULL) + self.line[1].astype(FULL)).astype(LOW)
        self.third = mover.go(rows, self.line.at[2], ctx=mover.flip(2))

    def done(self):
        self.mover.take(self.second)
        self.mover.take(self.third)
        value = self.rows(self.mover.ctx)[...].astype(FULL)
        self.out[...] = value + self.line[0].astype(FULL) + self.line[2].astype(FULL)


def reduce_buffers(half, width, count):
    return [
        VMEM((half, width), LOW),
        VMEM((half, width), LOW),
        VMEM((half, width), LOW),
        VMEM((count - 1, half // count, width), LOW),
    ]


def greet(mover, shard):
    barrier = pltpu.get_barrier_semaphore()
    peers = [dict(ctx=mover.on(by)) for by in range(1, mover.ctx_count)]
    peers += [dict(tp=peer) for peer in tp_peers()]
    if shard:
        peers.append(dict(shard=1 - mover.shard))
    for peer in peers:
        pl.semaphore_signal(barrier, inc=1, device_id=peer, device_id_type=MESH)
    pl.semaphore_wait(barrier, len(peers))


def tp_peers():
    place = lax.axis_index("tp")
    core, far = lax.rem(place, 2), place // 2
    return place + 1 - 2 * core, place + 2 - 4 * far


def run(kernel, name, ident, inputs, outputs, scratch, remote, local, sizes, vmem, flops):
    n_in, n_out, n_scratch = len(inputs), len(outputs), len(scratch)

    def body(*refs):
        ins, outs = refs[:n_in], refs[n_in : n_in + n_out]
        work = refs[n_in + n_out :]
        mover = Mover(sizes, *work[n_scratch:])
        kernel(mover, ins, outs, work[:n_scratch])

    return pl.pallas_call(
        body,
        in_specs=[pl.BlockSpec(memory_space=space) for _, space in inputs],
        out_specs=[pl.BlockSpec(memory_space=space) for _, _, space in outputs],
        out_shape=[jax.ShapeDtypeStruct(shape, dtype) for shape, dtype, _ in outputs],
        scratch_shapes=list(scratch)
        + [
            pltpu.SemaphoreType.DMA((remote,)),
            pltpu.SemaphoreType.DMA((remote,)),
            pltpu.SemaphoreType.DMA((local,)),
        ],
        compiler_params=pltpu.CompilerParams(
            collective_id=ident, has_side_effects=True, vmem_limit_bytes=vmem * 2**20
        ),
        cost_estimate=pl.CostEstimate(flops=flops, bytes_accessed=2**24, transcendentals=0),
        name=name,
    )(*[value for value, _ in inputs])


def order_of(block, count):
    return (block + count - 1) % count


def tiles_of(count, capacity, tile):
    ends = [-(-(p + 1) * capacity // tile) for p in range(count)]
    return list(zip([0] + ends[:-1], ends))


def tile_at(t, tile):
    return pl.ds(pl.multiple_of(t * tile, tile), tile)


def turned_product(left, right, bias, target):
    value = jnp.dot(left[...], right[...], preferred_element_type=FULL)
    if bias is not None:
        value = value + bias[0:1, :]
    target[...] = turned(value.astype(LOW))


def head_rows(ref, head, width):
    return ref.at[pl.ds(pl.multiple_of(head * width, 16), width)]


def attend_part(size, tile, mover, joint, bias, heads, qkv, o_ref, lse, work, after_send, begun, between):
    k_ref, q_ref, v_ref, low_ref, score_ref, top_ref = work
    count, width, capacity = qkv.shape
    slots = count * capacity
    sent = [None] + [
        mover.go(head_rows(joint, mover.on(by), width), qkv.at[by], ctx=mover.on(by))
        for by in range(1, count)
    ]
    after_send()
    qkv[0] = head_rows(joint, mover.ctx, width)[...]
    q_ref[size:PAD, :] = jnp.concatenate(
        [jnp.ones((16, slots), LOW), jnp.zeros((PAD - size - 16, slots), LOW)], axis=0
    )

    v_ref[size : size + 16, :] = jnp.ones((16, slots), LOW)

    def prepare(r):
        here = slice(r * capacity, (r + 1) * capacity)
        p = order_of(r, count)
        q_ref[0:size, p * capacity : (p + 1) * capacity] = (
            qkv[r, 0:size, :] * (size**-0.5)
        ).astype(LOW)
        v_ref[0:size, here] = qkv[r, 2 * size : 3 * size, :]
        keys = jnp.concatenate(
            [qkv[r, size : 2 * size, :], bias[:, here], jnp.zeros((PAD - size - 16, capacity), LOW)],
            axis=0,
        )
        k_ref[here, :] = turned(keys)

    prepare(0)
    for by in range(1, count):
        mover.take(sent[by])
        prepare(by)

    begun()
    last = slots // tile - 1
    assert last % 2 == 1

    def phase(t, now, following, then):
        at, ahead = tile_at(t, tile), tile_at(following, tile)
        top = top_ref[now, 0:1, :]
        summed = jnp.zeros((size + 16, tile), FULL)
        new_top = jnp.full((1, tile), NEG_LARGE, FULL)
        for r in range(count):
            here = slice(r * capacity, (r + 1) * capacity)
            scores = jnp.dot(k_ref[here, :], q_ref[:, ahead], preferred_element_type=FULL)
            score_ref[then, here, :] = scores
            new_top = jnp.maximum(new_top, jnp.max(scores, axis=0, keepdims=True))
            weights = jnp.exp(score_ref[now, here, :] - top)
            summed = summed + jnp.dot(
                v_ref[:, here], weights.astype(LOW), preferred_element_type=FULL
            )
        top_ref[then] = jnp.broadcast_to(new_top, (8, tile))
        total = summed[size : size + 1]
        out = summed[0:size] / total
        o_ref[:, at] = out
        low_ref[:, at] = out.astype(LOW)
        lse[:, at] = jnp.broadcast_to(top + jnp.log(total), (8, tile))

    def step(i, carry):
        phase(2 * i, 0, 2 * i + 1, 1)
        phase(2 * i + 1, 1, jnp.minimum(2 * i + 2, last), 0)
        return carry

    scores = jnp.dot(k_ref[...], q_ref[:, 0:tile], preferred_element_type=FULL)
    score_ref[0] = scores
    top_ref[0] = jnp.broadcast_to(jnp.max(scores, axis=0, keepdims=True), (8, tile))
    arriving = []
    for p, (low, high) in enumerate(tiles_of(count, capacity, 2 * tile)):
        lax.fori_loop(low, high, step, 0)
        done = low_ref.at[:, p * capacity : (p + 1) * capacity]
        if p < count - 1:
            there = head_rows(heads, mover.ctx, size)
            arriving.append(mover.go(done, there, ctx=mover.back(p + 1)))
        else:
            head_rows(heads, mover.ctx, size)[...] = low_ref[:, p * capacity : (p + 1) * capacity]
        between(p + 1)
    for copy in arriving:
        mover.take(copy)


def below(row, ones):
    width = row.shape[1]
    high = row.astype(LOW).astype(FULL)
    middle = (row - high).astype(LOW).astype(FULL)
    low = row - high - middle
    lead = jnp.full((1, width), 1.0 if ones else 0.0, FULL)
    rest = jnp.zeros((PAD // 2 - 4, width), FULL)
    return jnp.concatenate([lead, high, middle, low, rest], axis=0).astype(LOW)


def attend_back_part(size, tile, mover, parts, bias, qkv, o_ref, lse, grads, work, ready, waiting, begun, between):
    k_ref, v_ref, q_ref, do_ref, nat_ref, dq_ref, dk_ref, dv_ref, got, back = work
    count, width, capacity = qkv.shape
    slots = count * capacity
    sent = [None] + [
        mover.go(head_rows(parts, mover.on(by), size), got.at[by], ctx=mover.on(by))
        for by in range(1, count)
    ]
    got[0] = head_rows(parts, mover.ctx, size)[...]
    waiting()
    ready()
    q_ref[size:PAD, :] = below(lse[0:1, :], True)
    dq_ref[...] = jnp.zeros_like(dq_ref)
    off = (lax.broadcasted_iota(jnp.int32, (16, capacity), 0) + 2) // 3
    taken = jnp.where(off == 1, -1.0, 0.0).astype(LOW)
    pad = jnp.zeros((PAD - size - 16, capacity), LOW)
    for r in range(count):
        here = slice(r * capacity, (r + 1) * capacity)
        k_ref[here, :] = turned(
            jnp.concatenate([qkv[r, size : 2 * size, :], bias[:, here] + taken, pad], axis=0)
        )
        v_ref[here, :] = turned(
            jnp.concatenate([qkv[r, 2 * size : 3 * size, :], taken, pad], axis=0)
        )
    for r in range(count):
        if r:
            mover.take(sent[r])
        p = order_of(r, count)
        at = slice(p * capacity, (p + 1) * capacity)
        scaled = (qkv[r, 0:size, :] * (size**-0.5)).astype(LOW)
        dout = got[r]
        q_ref[0:size, at] = scaled
        do_ref[0:size, at] = dout
        nat_ref[at, :] = turned(jnp.concatenate([scaled, dout], axis=0))
        delta = jnp.sum(dout.astype(FULL) * o_ref[:, at], axis=0, keepdims=True)
        do_ref[size:PAD, at] = below(delta, False)

    begun()
    tiles = tiles_of(count, capacity, tile)
    arriving = []
    mine = head_rows(grads, mover.ctx, width)
    for turn, r in enumerate(list(range(1, count)) + [0]):
        here = slice(r * capacity, (r + 1) * capacity)
        dk_ref[...] = jnp.zeros_like(dk_ref)
        dv_ref[...] = jnp.zeros_like(dv_ref)

        def step(t, carry, r=r, here=here):
            at = tile_at(t, tile)
            scores = jnp.dot(k_ref[here, :], q_ref[:, at], preferred_element_type=FULL)
            chance = jnp.exp(scores)
            chance_grad = jnp.dot(v_ref[here, :], do_ref[:, at], preferred_element_type=FULL)
            score_grad = (chance * chance_grad).astype(LOW)
            dq_ref[:, at] += jnp.dot(
                qkv[r, size : 2 * size, :], score_grad, preferred_element_type=FULL
            )
            dk_ref[...] += jnp.dot(score_grad, nat_ref[at, :], preferred_element_type=FULL)
            dv_ref[...] += jnp.dot(
                chance.astype(LOW), nat_ref[at, :], preferred_element_type=FULL
            )
            return carry

        if r:
            lax.fori_loop(0, tiles[-1][1], step, 0)
        else:
            for p, (low, high) in enumerate(tiles):
                lax.fori_loop(low, high, step, 0)
                at = slice(p * capacity, (p + 1) * capacity)
                value = (dq_ref[:, at] * (size**-0.5)).astype(LOW)
                if p < count - 1:
                    back[p + 1, 0:size, :] = value
                    arriving.append(
                        mover.go(
                            back.at[p + 1, 0:size], mine.at[0:size], ctx=mover.back(p + 1)
                        )
                    )
                else:
                    mine[0:size, :] = value
        keys = dk_ref[...].T[0:size].astype(LOW)
        values = dv_ref[...].T[size : 2 * size].astype(LOW)
        if r:
            back[r, size : 2 * size, :] = keys
            back[r, 2 * size : 3 * size, :] = values
            arriving.append(
                mover.go(
                    back.at[r, size : 3 * size], mine.at[size : 3 * size], ctx=mover.back(r)
                )
            )
        else:
            mine[size : 2 * size, :] = keys
            mine[2 * size : 3 * size, :] = values
        between(turn)
    for copy in arriving:
        mover.take(copy)


def attend_back_buffers(size, count, capacity):
    slots = count * capacity
    return [
        VMEM((slots, PAD), LOW),
        VMEM((slots, PAD), LOW),
        VMEM((PAD, slots), LOW),
        VMEM((PAD, slots), LOW),
        VMEM((slots, PAD), LOW),
        VMEM((size, slots), FULL),
        VMEM((capacity, PAD), FULL),
        VMEM((capacity, PAD), FULL),
        VMEM((count, size, capacity), LOW),
        VMEM((count, 3 * size, capacity), LOW),
    ]


class Round:
    def __init__(self, mover, rows, full, buffers):
        place = lax.axis_index("tp")
        core, far = lax.rem(place, 2), place // 2
        self.mover, self.full = mover, full
        self.give, self.ra, self.passing, self.rb, self.keep = buffers
        self.span = rows // 4
        self.half = self.span // 2
        self.mate, self.far = tp_peers()

        def quarter(c, f):
            return (c * 2 + f) * self.span

        self.own, self.other = quarter(core, far), quarter(core, 1 - far)
        self.mate_own, self.mate_other = quarter(1 - core, far), quarter(1 - core, 1 - far)

    def rows(self, start, count=None):
        return pl.ds(pl.multiple_of(start, 16), count or self.span)

    def hand(self, slot, value):
        self.give[slot] = value.astype(LOW)
        return self.mover.go(self.give.at[slot], self.ra.at[slot], tp=self.mate)

    def onward(self, value, index):
        self.mover.take(index)
        self.passing[...] = (value + self.ra[1].astype(FULL)).astype(LOW)
        return [
            self.mover.go(self.passing.at[at], self.rb.at[at], tp=self.far)
            for at in (pl.ds(0, self.half), pl.ds(self.half, self.half))
        ]

    def close(self, far_copies, index, finish, halfway=None):
        self.mover.take(index)
        self.keep[...] += self.ra[0].astype(FULL)
        self.to_far, self.to_mate = [], []
        for c in range(2):
            at = pl.ds(c * self.half, self.half)
            self.mover.take(far_copies[c])
            low = finish(at, self.keep[at] + self.rb[at].astype(FULL))
            mine = self.full.at[self.rows(self.own + c * self.half, self.half)]
            mine[...] = low
            self.to_far.append(self.mover.go(mine, mine, tp=self.far))
            self.to_mate.append(self.mover.go(mine, mine, tp=self.mate))
            if halfway and c == 0:
                halfway()

    def eager(self, make, finish, meanwhile=None, halfway=None):
        first = self.hand(1, make(self.mate_other))
        copies = self.onward(make(self.other), first)
        second = self.hand(0, make(self.mate_own))
        self.keep[...] = make(self.own)
        if meanwhile:
            meanwhile()
        self.close(copies, second, finish, halfway)

    def after(self, before, make, finish, meanwhile, between):
        before.have_mate_own()
        second = self.hand(0, make(self.mate_own))
        self.keep[...] = make(self.own)
        before.have_other()
        between()
        value = make(self.other)
        before.have_mate_other()
        first = self.hand(1, make(self.mate_other))
        copies = self.onward(value, first)
        meanwhile()
        self.close(copies, second, finish)

    def have_mate_own(self):
        for copy in self.to_mate:
            self.mover.take(copy)

    def have_other(self):
        self.passed = []
        for c in range(2):
            self.mover.take(self.to_far[c])
            rows = self.full.at[self.rows(self.other + c * self.half, self.half)]
            self.passed.append(self.mover.go(rows, rows, tp=self.mate))

    def have_mate_other(self):
        for copy in self.passed:
            self.mover.take(copy)

    def have(self):
        self.have_mate_own()
        self.have_other()
        self.have_mate_other()


ROUND_COPIES = 10


def round_buffers(rows, width):
    span = rows // 4
    return [
        VMEM((2, span, width), LOW),
        VMEM((2, span, width), LOW),
        VMEM((span, width), LOW),
        VMEM((span, width), LOW),
        VMEM((span, width), FULL),
    ]


NAMES = ("qkv", "out", "up", "down")


def layer_kernel(plan, last, size, tile, mover, ins, outs, work):
    ins, outs, work = iter(ins), iter(outs), iter(work)
    source = next(ins)
    x_ref = None if plan.entry else next(ins)
    live_ref = next(ins)
    far_params = [next(ins) for _ in range(8)]
    stream, following = next(outs), next(outs)
    far_qkv, far_o, far_lse, far_heads, far_middle, far_second, far_hidden, far_slope = [
        next(outs) for _ in range(8)
    ]
    far_first = next(outs) if plan.entry else None
    joint, nat, heads, qkv, o_ref, lse, middle, second, hidden, slope = [
        next(work) for _ in range(10)
    ]
    first = next(work) if plan.entry else source
    attend_work = [next(work) for _ in range(6)]
    one_work, two_work = [next(work) for _ in range(5)], [next(work) for _ in range(5)]
    rows = source.shape[0]
    bias, qkv_bias = next(work), next(work)
    params = [next(work) for _ in range(8)]
    whole = {name: next(work) for name in NAMES}
    gathers, loads = {}, {}
    for name in plan.held:
        loads[name] = (next(ins), whole[name])
    half_refs = {name: next(ins) for name in plan.halves}
    for name in plan.own:
        gathers[name, 0] = Gather(mover, next(ins).at[plan.layer], whole[name])
    kept_ahead = {name: next(outs) for name in plan.ahead + plan.lines}
    for name in plan.ahead + plan.lines:
        gathers[name, 1] = Gather(
            mover, next(ins).at[plan.layer + 1], next(work), name in plan.ahead
        )
    kept = {name: next(outs) for name in plan.kept}

    greet(mover, bool(gathers))
    halves = {name: Across(mover, half_refs[name], whole[name]) for name in plan.halves}
    if plan.entry:
        gathers_first = [key for key in [("qkv", 0)] if key in gathers]
        for key in gathers_first:
            gathers[key].start_line()
            gathers[key].start_over()
    param_loads = [mover.stay(there, here) for there, here in zip(far_params, params)]
    waiting_loads = dict(loads)
    loads = {}

    def load(names):
        for name in names:
            if name in waiting_loads and name not in loads:
                loads[name] = mover.stay(*waiting_loads[name])

    load(["qkv"])

    def have(name):
        if name in waiting_loads:
            mover.near(loads[name])
            load(NAMES)
        else:
            (halves[name] if name in halves else gathers[name, 0]).have()
            mover.stay(whole[name], kept[name])
        return whole[name]

    def begin(keys):
        for key in keys:
            if key in gathers:
                gathers[key].start_line()

    def begin_over(keys):
        for key in keys:
            if key in gathers:
                gathers[key].start_over()

    def pass_on(keys, stage):
        for key in keys:
            if key in gathers:
                gathers[key].pass_on(stage)

    def pass_all(keys):
        for stage in (1, 2, 3):
            pass_on(keys, stage)

    mover.near(*param_loads)
    layer, after = plan.layer, min(plan.layer + 1, params[0].shape[0] - 1)

    def row(index, layer=layer):
        return params[index][...].astype(FULL)[layer : layer + 1]

    b_out, gain2, shift2, b_down, b_up = row(0), row(1), row(2), row(3), row(6)
    gain1, shift1, gain0, shift0 = row(4, after), row(5, after), row(4), row(5)
    qkv_bias[...] = joint_bias(row(7), size, joint.shape[0])
    key_bias(mover, live_ref, bias)
    ahead, lines = [("qkv", 1)], [("out", 1), ("up", 1)]
    one = Round(mover, rows, second, one_work)
    two = Round(mover, rows, following, two_work)
    if plan.entry:
        chunk = rows // 5 if rows % 80 == 0 else rows

        def norm_step(i, carry):
            at = pl.ds(pl.multiple_of(i * chunk, 16), chunk)
            value = normalize(source[at, :].astype(FULL), gain0, shift0)[0]
            first[at, :] = value.astype(LOW)
            return carry

        lax.fori_loop(0, rows // chunk, norm_step, 0)
        mover.stay(first, far_first)
        pass_all([("qkv", 0)])
        begin([("out", 0), ("up", 0)])
        begin_over([("out", 0), ("up", 0), ("down", 0)] + ahead + lines)
        turned_product(first, have("qkv"), qkv_bias, joint)
    else:
        turned_product(first, have("qkv"), qkv_bias, joint)

    def after_send():
        if plan.entry:
            pass_all([("out", 0), ("up", 0)])
        else:
            for name in plan.own:
                gathers[name, 0].start_over()

    def begun():
        begin([("down", 0)])

    def between(p):
        if p > 2:
            pass_on([("down", 0)], p - 2)
        if p == 4:
            if not plan.entry:
                begin_over(ahead + lines)
            begin(ahead)

    attend_part(
        size, tile, mover, joint, bias, heads, qkv, o_ref, lse, attend_work, after_send, begun, between
    )
    nat[...] = turned(heads[...])
    w_out = have("out")

    def out_part(start):
        return dot(nat[one.rows(start), :], w_out[...], ((1,), (1,)))

    def to_second(at, value):
        if plan.entry:
            before = source[one.rows(one.own + at.start, at.size), :].astype(FULL)
        else:
            before = x_ref[at]
        value = before + value + b_out
        middle[at] = value
        return normalize(value, gain2, shift2)[0].astype(LOW)

    def meanwhile():
        mover.stay(qkv, far_qkv)
        mover.stay(o_ref, far_o)
        mover.stay(lse, far_lse)
        mover.stay(nat, far_heads)
        pass_on([("down", 0)], 3)

    one.eager(out_part, to_second, meanwhile, lambda: pass_on(ahead, 1))
    pass_on(ahead, 2)
    begin(lines)
    w_up, w_down = have("up"), have("down")

    def mlp_part(start):
        at = two.rows(start)
        pre = jnp.dot(second[at, :], w_up[...], preferred_element_type=FULL) + b_up
        low, low_slope = gelu_pair(pre)
        hidden[at, :] = low
        slope[at, :] = low_slope
        return dot(low, w_down[...], ((1,), (1,)))

    def to_following(at, value):
        value = middle[at] + value + b_down
        stream[at] = value
        if last:
            return live_rows(value, two.own + at.start, live_ref[0, mover.ctx]).astype(LOW)
        return normalize(value, gain1, shift1)[0].astype(LOW)

    def meanwhile():
        mover.stay(middle, far_middle)
        mover.stay(second, far_second)
        mover.stay(hidden, far_hidden)
        mover.stay(slope, far_slope)
        pass_on(lines, 1)

    two.after(one, mlp_part, to_following, meanwhile, lambda: pass_on(ahead, 3))
    two.have()
    pass_on(lines, 2)
    pass_on(lines, 3)
    for name in plan.ahead + plan.lines:
        gathers[name, 1].have()
        mover.stay(gathers[name, 1].target, kept_ahead[name])
    mover.settle()


class Plan:
    def __init__(self, layer, last, inside):
        self.layer, self.entry = layer, layer == 0
        self.own = (NAMES if layer == 0 else ("down",)) if inside else ()
        self.halves = ("out", "up") if inside and layer else ()
        self.ahead = ("qkv",) if inside and not last else ()
        self.lines = ("out", "up") if inside and not last else ()
        self.kept = self.own + self.halves
        self.held = tuple(name for name in NAMES if name not in self.kept)


def forward_layer(source, x, live, params, gathered, weights, plan, last, size, sizes, ident):
    rows, width = source.shape
    count = sizes[0]
    joint, hidden = weights["qkv"].shape[2], weights["up"].shape[2]
    heads = joint // (3 * size)
    attn, slots, span = heads * size, count * rows, rows // 4
    tile = 256 if slots % 256 == 0 else PAD
    columns = {"qkv": joint, "out": attn, "up": hidden, "down": hidden}
    inputs = [(source, VMEM)] + ([] if plan.entry else [(x, VMEM)])
    inputs += [(live, SMEM)] + [(value, HBM) for value in params]
    inputs += [(gathered[name, plan.layer], HBM) for name in plan.held]
    inputs += [(gathered[name, plan.layer, 0], HBM) for name in plan.halves]
    inputs += [(weights[name], HBM) for name in plan.own + plan.ahead + plan.lines]
    saved = [
        ((count, 3 * size, rows), LOW),
        ((size, slots), FULL),
        ((8, slots), FULL),
        ((rows, attn), LOW),
        ((span, width), FULL),
        ((rows, width), LOW),
        ((rows, hidden), LOW),
        ((rows, hidden), LOW),
    ]
    outputs = [((span, width), FULL, VMEM), ((rows, width), LOW, VMEM)]
    outputs += [(shape, dtype, HBM) for shape, dtype in saved]
    if plan.entry:
        outputs.append(((rows, width), LOW, HBM))
    ahead = [(width, columns[name]) for name in plan.ahead]
    ahead += [(width // 2, columns[name]) for name in plan.lines]
    outputs += [(shape, LOW, HBM) for shape in ahead]
    outputs += [((width, columns[name]), LOW, HBM) for name in plan.kept]
    qkv_shape, o_shape, lse_shape, heads_shape = saved[:4]
    scratch = [VMEM((joint, rows), LOW), VMEM((rows, attn), LOW), VMEM((attn, rows), LOW)]
    scratch += [VMEM(*pair) for pair in saved[:3] + saved[4:]]
    if plan.entry:
        scratch.append(VMEM((rows, width), LOW))
    scratch += [
        VMEM((slots, PAD), LOW),
        VMEM((PAD, slots), LOW),
        VMEM((size + 16, slots), LOW),
        VMEM((size, slots), LOW),
        VMEM((2, slots, tile), FULL),
        VMEM((2, 8, tile), FULL),
    ]
    scratch += round_buffers(rows, width) + round_buffers(rows, width)
    scratch += [VMEM((16, slots), LOW), VMEM((16, joint), FULL)]
    scratch += [VMEM(value.shape, value.dtype) for value in params]
    scratch += [VMEM((width, columns[name]), LOW) for name in NAMES]
    scratch += [VMEM(shape, LOW) for shape in ahead]
    results = run(
        functools.partial(layer_kernel, plan, last, size, tile),
        "forward_layer",
        ident,
        inputs,
        outputs,
        scratch,
        2 * (count - 1) + 2 * ROUND_COPIES + 2 * count * len(plan.kept + plan.ahead + plan.lines),
        10 + 2 * len(plan.kept + plan.ahead + plan.lines) + len(plan.held) + len(params),
        sizes,
        58,
        2 * rows * width * (2 * hidden + attn + joint) + 4 * slots * slots * 256,
    )
    stream, following = results[:2]
    kept = results[2 : 11 if plan.entry else 10]
    rest = iter(results[2 + len(kept) :])
    for name in plan.ahead:
        gathered[name, plan.layer + 1] = next(rest)
    for name in plan.lines:
        gathered[name, plan.layer + 1, 0] = next(rest)
    for name in plan.kept:
        gathered[name, plan.layer] = next(rest)
    return stream, following, kept


class SmallSums:
    def __init__(self, mover, rows, held, got):
        self.mover, self.rows, self.held, self.got = mover, rows, held, got
        self.stage = 0
        mate, far = tp_peers()
        self.peers = [
            dict(tp=mate),
            dict(tp=far),
            dict(shard=1 - mover.shard),
            dict(ctx=mover.flip(2)),
            dict(ctx=mover.flip(1)),
        ]

    def part(self, stage):
        return pl.ds(0, self.rows if stage < 2 else self.held.shape[1])

    def step(self):
        stage, mover = self.stage, self.mover
        if stage:
            mover.take(self.copy)
            at = self.part(stage - 1)
            self.held[stage] = self.held[stage - 1]
            self.held[stage, at, :] = self.held[stage - 1, at, :] + self.got[stage - 1, at, :]
        if stage < len(self.peers):
            at = self.part(stage)
            self.copy = mover.go(
                self.held.at[stage, at], self.got.at[stage, at], **self.peers[stage]
            )
        self.stage = stage + 1

    def value(self):
        return self.held[len(self.peers)]


def key_bias(mover, live_ref, bias):
    capacity = bias.shape[1] // mover.ctx_count
    row = lax.broadcasted_iota(jnp.int32, (16, capacity), 0)
    slot = lax.broadcasted_iota(jnp.int32, (16, capacity), 1)
    for r in range(mover.ctx_count):
        live = live_ref[0, mover.back(r)]
        value = jnp.where((row == 0) & (slot >= live), NEG_LARGE, 0.0)
        bias[:, r * capacity : (r + 1) * capacity] = value.astype(LOW)


def pair_columns(rows, width, size, turn):
    shape = (width, rows) if turn else (rows, width)
    given = lax.broadcasted_iota(jnp.int32, shape, 1 if turn else 0)
    column = lax.broadcasted_iota(jnp.int32, shape, 0 if turn else 1)
    head, within = column // (3 * size), column % (3 * size)
    wanted = head * (2 * size) + jnp.where(within < size, within, within - size)
    key = (within >= size) & (within < 2 * size)
    return jnp.where((given == wanted) & ~key, 1.0, 0.0).astype(LOW)


def joint_bias(pair, size, width):
    rows = pair.shape[1]
    spread = jnp.broadcast_to(pair, (16, rows)).astype(LOW)
    return jnp.dot(spread, pair_columns(rows, width, size, False), preferred_element_type=FULL)


def live_rows(value, start, live):
    row = start + lax.broadcasted_iota(jnp.int32, value.shape, 0)
    return jnp.where(row < live, value, 0.0)


def sums_into(sums, first, at, values):
    for index, value in enumerate(values):
        row = first + index
        added = jnp.sum(value, axis=0, keepdims=True)
        width = added.shape[1]
        sums[row : row + 1, 0:width] = (
            added if at.start == 0 else sums[row : row + 1, 0:width] + added
        )


def back_kernel(plan, size, tile, mover, ins, outs, work):
    ins, outs, work = iter(ins), iter(outs), iter(work)
    source = next(ins)
    x_ref = None if plan.last else next(ins)
    live_ref, far_gain2, far_gain1 = [next(ins) for _ in range(3)]
    far = [next(ins) for _ in range(14)]
    late_far = next(ins) if plan.late else None
    others = [(next(ins), next(ins)) for _ in range(plan.others)]
    stream, following = next(outs), next(outs)
    grad_outs = {name: next(outs) for name in NAMES if plan.inside and (name != "qkv" or plan.final)}
    mid_out = next(outs) if plan.inside and not plan.final else None
    late_out = next(outs) if plan.late else None
    split = local = totals = None
    if plan.joined:
        totals = next(outs)
    else:
        split, local = next(outs), next(outs)
    wholes = {} if plan.inside else {name: next(outs) for name in NAMES}
    near = [next(work) for _ in range(14)]
    slope, w_down, w_up, middle, hidden, second, w_out, heads, qkv, o_ref, lse, first, w_qkv, before = near
    grad = next(work) if plan.last else source
    pre_grad, attn_grad, parts, grads, nat = [next(work) for _ in range(5)]
    attend_work = [next(work) for _ in range(10)]
    one_work, two_work = [next(work) for _ in range(5)], [next(work) for _ in range(5)]
    rows, width = source.shape
    reduces = {}
    if plan.inside:
        pairs = {
            "down": (grad, hidden),
            "up": (second, pre_grad),
            "out": (attn_grad, heads),
            "qkv": (first, nat),
        }
        for name in ("down", "up", "out", "qkv"):
            buffers = [next(work) for _ in range(4)]
            reduces[name] = Reduce(mover, buffers, grad_outs.get(name), *pairs[name])
    late = None
    if plan.late:
        late_mid, late_line = next(work), next(work)
        late = Reduce(mover, (late_mid, None, late_mid, late_line), late_out, None, None)
    bias, gain2_ref, gain1_ref = [next(work) for _ in range(3)]
    if plan.joined:
        split, local = next(work), next(work)
        early_held, early_got, late_held, late_got = [next(work) for _ in range(4)]
        tops = 8 * (plan.others + 1)
        early = SmallSums(mover, tops, early_held, early_got)
        final = SmallSums(mover, 8, late_held, late_got)
        everything = [(split, local)] + others

    greet(mover, plan.inside)
    gain_loads = [mover.stay(far_gain2, gain2_ref), mover.stay(far_gain1, gain1_ref)]
    one = Round(mover, rows, attn_grad, one_work)
    two = Round(mover, rows, following, two_work)
    if plan.final:
        far[13] = far[13].at[two.rows(two.own)]
    load = {index: mover.stay(far[index], near[index]) for index in (0, 1, 2)}
    late_load = mover.stay(late_far, late_mid) if late else None
    if plan.last:
        chunk = rows // 5 if rows % 80 == 0 else rows

        def mask_step(i, carry):
            at = pl.ds(pl.multiple_of(i * chunk, 16), chunk)
            value = source[at, :].astype(FULL)
            grad[at, :] = live_rows(value, i * chunk, live_ref[0, mover.ctx]).astype(LOW)
            return carry

        lax.fori_loop(0, rows // chunk, mask_step, 0)
    key_bias(mover, live_ref, bias)
    mover.near(*gain_loads)
    gain2, gain1 = [
        ref[...].astype(FULL)[plan.layer : plan.layer + 1] for ref in (gain2_ref, gain1_ref)
    ]
    split[...] = jnp.zeros_like(split)
    local[...] = jnp.zeros_like(local)
    split[5:6, 0:width] = jnp.sum(
        grad[one.rows(one.own), :].astype(FULL), axis=0, keepdims=True
    )
    hidden_width = slope.shape[1]

    def mlp_part(start):
        at = one.rows(start)
        pre = jnp.dot(grad[at, :], w_down[...], preferred_element_type=FULL)
        low = (pre * slope[at, :].astype(FULL)).astype(LOW)
        pre_grad[at, :] = low
        local[0:1, 0:hidden_width] += jnp.sum(low.astype(FULL), axis=0, keepdims=True)
        return dot(low, w_up[...], ((1,), (1,)))

    def to_attn(at, value):
        if plan.last:
            above = grad[one.rows(one.own + at.start, at.size), :].astype(FULL)
        else:
            above = x_ref[at]
        _, normed, inverse = normalize(middle[at], 1.0, 0.0)
        result = above + normalize_back(value, normed, inverse, gain2)
        stream[at] = result
        low = result.astype(LOW)
        sums_into(split, 2, at, (value * normed, value, low.astype(FULL)))
        return low

    def reduce(name):
        if name in reduces:
            reduces[name].begin_blocks()

    def own(name):
        if name in reduces:
            reduces[name].own()

    def first_step(name):
        if name in reduces:
            reduces[name].fold_blocks(3)
            reduces[name].send_first()

    def second_step(name):
        if name in reduces:
            reduces[name].fold_blocks(2)
            reduces[name].send_third()

    def rest(name):
        if name in reduces:
            reduces[name].fold_blocks(1)
            reduces[name].send_second()
            reduces[name].fold_blocks(0)

    def begin_early():
        if plan.joined:
            early_held[0] = jnp.zeros(early_held.shape[1:], FULL)
            for layer, (some, more) in enumerate(everything):
                first_row = 0 if layer else 2
                for row in range(first_row, 6):
                    at = row * len(everything) + layer
                    early_held[0, at : at + 1, :] = some[row : row + 1, :]
                for row in range(2 if layer else 1):
                    at = tops + row * len(everything) + layer
                    early_held[0, at : at + 1, :] = more[row : row + 1, :]

    def early_step():
        if plan.joined:
            early.step()

    def start_down():
        mover.near(load[3], load[4])
        reduce("down")
        if late:
            late.send_third()

    if late:
        mover.near(late_load)
        late.send_first()
        late.send_second()
    mover.near(load[0], load[1], load[2])
    for index in range(3, len(far)):
        load[index] = mover.stay(far[index], near[index])
    one.eager(mlp_part, to_attn, start_down)
    mover.near(load[5])
    reduce("up")
    one.have()
    mover.near(load[6])
    turned_product(attn_grad, w_out, None, parts)

    def waiting():
        begin_early()
        early_step()
        own("down")
        first_step("down")
        mover.near(load[7])
        reduce("out")
        own("out")

    def ready():
        own("up")
        mover.near(load[8], load[9], load[10])

    def between(turn):
        if turn == 0:
            early_step()
        if turn == 3:
            second_step("down")
            first_step("up")
            rest("down")

    attend_back_part(
        size,
        tile,
        mover,
        parts,
        bias,
        qkv,
        o_ref,
        lse,
        grads,
        attend_work,
        ready,
        waiting,
        lambda: None,
        between,
    )
    early_step()
    nat[...] = turned(grads[...])
    pairs_width = nat.shape[1] // 3 * 2
    picked = jnp.dot(
        nat[...], pair_columns(pairs_width, nat.shape[1], size, True), preferred_element_type=FULL
    )
    local[1:2, 0:pairs_width] = jnp.sum(picked, axis=0, keepdims=True)
    mover.near(*[load[index] for index in range(11, len(far))])

    def qkv_part(start):
        return dot(nat[two.rows(start), :], w_qkv[...], ((1,), (1,)))

    def to_following(at, value):
        row = before[at, :].astype(FULL)
        _, normed, inverse = normalize(row, 1.0, 0.0)
        result = stream[at] + normalize_back(value, normed, inverse, gain1)
        stream[at] = result
        low = result.astype(LOW)
        sums_into(split, 0, at, (value * normed, value))
        return low

    def meanwhile():
        if not plan.final:
            reduce("qkv")
        own("qkv")
        second_step("up")
        first_step("out")
        rest("up")
        early_step()

    def halfway():
        if plan.final:
            first_step("qkv")

    if plan.final:
        reduce("qkv")
    two.eager(qkv_part, to_following, meanwhile, halfway)
    if plan.joined:
        late_held[0, 0:8, :] = jnp.zeros((8, late_held.shape[2]), FULL)
        late_held[0, 0:2, :] = split[0:2, :]
        late_held[0, 8:16, :] = local[...]
        final.step()
        final.step()
    second_step("out")
    if plan.final:
        second_step("qkv")
    rest("out")
    two.have_mate_own()
    two.have_other()
    if plan.joined:
        final.step()
        early_step()
    if plan.final:
        rest("qkv")
    if plan.joined:
        final.step()
    if plan.inside and not plan.final:
        reduces["qkv"].fold_blocks(3, 2, 1, 0)
        mover.stay(reduces["qkv"].mid, mid_out)
    two.have_mate_other()
    if plan.joined:
        final.step()
    for name in ("down", "up", "out"):
        if name in reduces:
            reduces[name].done()
    if late:
        late.done()
    if plan.inside and plan.final:
        reduces["qkv"].done()
    if plan.joined:
        final.step()
        early.step()
        totals[...] = early.value()
        last_value = final.value()
        for row in range(2):
            at = row * len(everything)
            totals[at : at + 1, :] = last_value[row : row + 1, :]
        at = tops + len(everything)
        totals[at : at + 1, :] = last_value[9:10, :]
    if not plan.inside:
        for name, (lhs, rhs) in {
            "down": (grad, hidden),
            "up": (second, pre_grad),
            "out": (attn_grad, heads),
            "qkv": (first, nat),
        }.items():
            full = Reduce(mover, (wholes[name],) * 4, None, lhs, rhs)
            full.compute(wholes[name], 0)
    mover.settle()


def gather_outputs_kernel(layers, *refs):
    count = layers * len(NAMES)
    parts, token_grads, mixed, totals = refs[:count], refs[count], refs[count + 1], refs[count + 2]
    outs, work = refs[count + 3 : count + 17], refs[count + 17 : -2]
    into, out_of = refs[-2:]
    coming, going = [], []
    pairs = [(mixed, work[4], outs[4].at[0])]
    for index in range(len(NAMES)):
        for layer in range(layers):
            pairs.append(
                (parts[index * layers + layer], work[index].at[layer], outs[index].at[layer])
            )
    for i, (source, stage, _) in enumerate(pairs):
        coming.append(pltpu.make_async_copy(source, stage, into.at[i]))
        coming[-1].start()
    work[5][...] = token_grads[...].astype(FULL)
    going.append(pltpu.make_async_copy(work[5], outs[5].at[0], out_of.at[len(pairs)]))
    going[-1].start()
    for row, out in enumerate(outs[6:12]):
        out[...] = totals[row * layers : (row + 1) * layers, 0 : out.shape[1]]
    for row, out in enumerate(outs[12:14]):
        row = row + 8
        out[...] = totals[row * layers : (row + 1) * layers, 0 : out.shape[1]]
    for i, (_, stage, target) in enumerate(pairs):
        coming[i].wait()
        going.append(pltpu.make_async_copy(stage, target, out_of.at[i]))
        going[-1].start()
    for copy in going:
        copy.wait()


def gather_outputs(done, token_grads, mixed, totals, layers, widths):
    rows, width = token_grads.shape
    parts = [done[name, layer] for name in NAMES for layer in range(layers)]
    hbm, whole = pl.BlockSpec(memory_space=HBM), lambda shape: pl.BlockSpec(
        shape, lambda i: (0,) * len(shape)
    )
    shapes = [(layers,) + done[name, 0].shape for name in NAMES] + [(1, rows, width)] * 2
    types = [FULL] * 4 + [LOW, FULL]
    small = [(layers, width)] * 6 + [(layers, count) for count in widths]
    copies = len(parts) + 1
    return pl.pallas_call(
        functools.partial(gather_outputs_kernel, layers),
        grid=(1,),
        in_specs=[hbm] * len(parts) + [whole(token_grads.shape), hbm, whole(totals.shape)],
        out_specs=[hbm] * 6 + [whole(shape) for shape in small],
        out_shape=[jax.ShapeDtypeStruct(*pair) for pair in zip(shapes, types)]
        + [jax.ShapeDtypeStruct(shape, FULL) for shape in small],
        scratch_shapes=[VMEM(shape, FULL) for shape in shapes[:4]]
        + [VMEM((rows, width), LOW), VMEM((rows, width), FULL)]
        + [pltpu.SemaphoreType.DMA((copies,)), pltpu.SemaphoreType.DMA((copies + 1,))],
        compiler_params=pltpu.CompilerParams(vmem_limit_bytes=60 * 2**20),
        name="gather_outputs",
    )(*parts, token_grads, mixed, totals)


class BackPlan:
    def __init__(self, layer, layers, inside):
        self.inside, self.layer = inside, layer
        self.last, self.final = layer == layers - 1, layer == 0
        self.late = inside and not self.last
        self.joined = inside and self.final
        self.others = layers - 1 if self.joined else 0


def back_layer(source, x, live, gain2, gain1, saved, late, others, plan, size, sizes, ident):
    rows, width = source.shape
    count = sizes[0]
    slope, w_down, w_up = saved[:3]
    hidden, joint, attn = slope.shape[1], saved[12].shape[1], saved[6].shape[1]
    slots, span = count * rows, rows // 4
    tile = 512 if slots % 512 == 0 else PAD
    wide = max(width, hidden, joint)
    half = width // 2
    block = half // count
    columns = {"qkv": joint, "out": attn, "up": hidden, "down": hidden}
    inputs = [(source, VMEM)] + ([] if plan.last else [(x, VMEM)])
    inputs += [(live, SMEM), (gain2, HBM), (gain1, HBM)]
    inputs += [(value, HBM) for value in saved]
    if plan.late:
        inputs.append((late, HBM))
    for pair in others[: plan.others]:
        inputs += [(value, VMEM) for value in pair]
    outputs = [((span, width), FULL, VMEM), ((rows, width), LOW, VMEM)]
    names = [name for name in NAMES if plan.inside and (name != "qkv" or plan.final)]
    outputs += [((block, columns[name]), FULL, VMEM) for name in names]
    if plan.inside and not plan.final:
        outputs.append(((half, joint), LOW, HBM))
    if plan.late:
        outputs.append(((block, joint), FULL, VMEM))
    depth = 8 * (plan.others + 1)
    if plan.joined:
        outputs.append(((depth + 8, wide), FULL, VMEM))
    else:
        outputs += [((8, wide), FULL, VMEM)] * 2
    if not plan.inside:
        outputs += [((width, columns[name]), LOW, VMEM) for name in NAMES]
    scratch = [VMEM(value.shape, value.dtype) for value in saved]
    scratch[13] = VMEM((span, width), saved[13].dtype)
    if plan.last:
        scratch.append(VMEM((rows, width), LOW))
    scratch += [
        VMEM((rows, hidden), LOW),
        VMEM((rows, width), LOW),
        VMEM((attn, rows), LOW),
        VMEM((joint, rows), LOW),
        VMEM((rows, joint), LOW),
    ]
    scratch += attend_back_buffers(size, count, rows)
    scratch += round_buffers(rows, width) + round_buffers(rows, width)
    if plan.inside:
        for name in ("down", "up", "out", "qkv"):
            scratch += reduce_buffers(half, columns[name], count)
    if plan.late:
        scratch += [VMEM((half, joint), LOW), VMEM((count - 1, block, joint), LOW)]
    scratch.append(VMEM((16, slots), LOW))
    scratch += [VMEM(value.shape, value.dtype) for value in (gain2, gain1)]
    assert 2 * (plan.others + 1) <= 8
    if plan.joined:
        scratch += [VMEM((8, wide), FULL)] * 2
        scratch += [
            VMEM((6, depth + 8, wide), FULL),
            VMEM((5, depth + 8, wide), FULL),
            VMEM((6, 16, wide), FULL),
            VMEM((5, 16, wide), FULL),
        ]
    results = run(
        functools.partial(back_kernel, plan, size, tile),
        "back_layer",
        ident,
        inputs,
        outputs,
        scratch,
        3 * (count - 1) + 2 * ROUND_COPIES + 8 * count + 10 + count,
        len(saved) + 4,
        sizes,
        58,
        6 * rows * width * (2 * hidden + attn + joint) + 10 * slots * slots * 256,
    )
    return results[:2], names, results[2:]


def shards(
    tokens,
    block_tokens,
    ln1_gain,
    ln1_bias,
    w_qkv,
    b_qv,
    w_out,
    b_out,
    ln2_gain,
    ln2_bias,
    w_up,
    b_up,
    w_down,
    b_down,
    cotangent,
):
    images, capacity, width = tokens.shape
    assert images == 1
    layers = w_qkv.shape[0]
    size = HEAD_DIM
    ctx_count = lax.axis_size("ctx")
    ctx_place = lax.axis_index("ctx")
    joint_width = w_qkv.shape[2]
    heads = joint_width // (3 * size)
    assert heads == ctx_count
    attn_width = heads * size
    hidden_width = w_up.shape[2]
    weights = {"qkv": w_qkv, "out": w_out, "up": w_up, "down": w_down}
    sizes = (ctx_count, lax.axis_size("shard"))
    inside = sizes == (4, 2)
    gathered = {}
    if not inside:
        for name, value in weights.items():
            for layer in range(layers):
                gathered[name, layer] = gather_weight(value[layer])[0]
    source, stream = tokens[0], None
    saved = []
    for layer in range(layers):
        last = layer == layers - 1
        result, following, kept = forward_layer(
            source,
            stream,
            block_tokens,
            (b_out, ln2_gain, ln2_bias, b_down, ln1_gain, ln1_bias, b_up, b_qv),
            gathered,
            weights,
            Plan(layer, last, inside),
            last,
            size,
            sizes,
            1 + layer,
        )
        before = stream if layer else source
        first = source if layer else kept[8]
        saved.append((before, first) + tuple(kept[:8]))
        source, stream = following, result
    mixed = source

    done, packs = {}, {}
    source, stream, late = cotangent[0], None, None
    for layer in reversed(range(layers)):
        before, first, qkv, head_out, lse, heads_low, middle, second, hidden, slope = saved[layer]
        plan = BackPlan(layer, layers, inside)
        whole = {name: gathered[name, layer] for name in NAMES}
        near = [slope, whole["down"], whole["up"], middle, hidden, second, whole["out"]]
        near += [heads_low, qkv, head_out, lse, first, whole["qkv"], before]
        others = [packs[key] for key in sorted(packs)]
        (stream, source), names, rest = back_layer(
            source, stream, block_tokens, ln2_gain, ln1_gain, near, late, others, plan, size, sizes, 1 + layers + layer
        )
        rest = iter(rest)
        for name in names:
            done[name, layer] = next(rest)
        if plan.inside and not plan.final:
            late = next(rest)
        if plan.late:
            done["qkv", layer + 1] = next(rest)
        if plan.joined:
            totals = next(rest)
        else:
            packs[layer] = (next(rest), next(rest))
        if not inside:
            for name in NAMES:
                value = next(rest)
                done[name, layer] = scatter_weight(
                    lambda start, count, value=value: rows_of(value, start, count).astype(FULL),
                    width,
                )
    if not inside:
        split = total_over(("tp",), jnp.stack([packs[l][0] for l in range(layers)], axis=1))
        local = jnp.stack([packs[l][1] for l in range(layers)], axis=1)
        totals = total_over(("shard", "ctx"), jnp.concatenate([split, local[:2]]))
        totals = totals.reshape(10 * layers, -1)
    pairs = b_qv.shape[1]
    outs = gather_outputs(done, source, mixed, totals, layers, (hidden_width, pairs))
    g_qkv, g_out, g_up, g_down, mixed, token_grads = outs[:6]
    g_ln1_gain, g_ln1_bias, g_ln2_gain, g_ln2_bias, g_b_out, g_b_down, g_b_up, g_b_qv = outs[6:]
    return (
        mixed,
        token_grads,
        g_ln1_gain,
        g_ln1_bias,
        g_qkv,
        g_b_qv,
        g_out,
        g_b_out,
        g_ln2_gain,
        g_ln2_bias,
        g_up,
        g_b_up,
        g_down,
        g_b_down,
    )


def solution(mesh):
    split_rows = P(None, ("shard", "ctx"), "tp")
    split_tokens = P("shard", "ctx", None)
    return jax.shard_map(
        shards,
        mesh=mesh,
        in_specs=(
            split_tokens,
            P("shard", None),
            P(),
            P(),
            split_rows,
            P(None, "tp"),
            split_rows,
            P(),
            P(),
            P(),
            split_rows,
            P(None, "tp"),
            split_rows,
            P(),
            split_tokens,
        ),
        out_specs=(
            split_tokens,
            split_tokens,
            P(),
            P(),
            split_rows,
            P(None, "tp"),
            split_rows,
            P(),
            P(),
            P(),
            split_rows,
            P(None, "tp"),
            split_rows,
            P(),
        ),
        check_vma=False,
    )
```

```python
import functools
import math

import jax
import jax.numpy as jnp
from jax import lax
from jax.experimental import pallas as pl
from jax.experimental.pallas import tpu as pltpu
from jax.sharding import PartitionSpec as P

HEAD_DIM = 64
EPSILON = 1e-06
NEG_LARGE = -1e30
LOW = jnp.bfloat16
FULL = jnp.float32
PAD = 128
MESH = pl.DeviceIdType.MESH
VMEM = pltpu.VMEM
HBM = pltpu.HBM
SMEM = pltpu.SMEM


def bits_of(axis):
    size = lax.axis_size(axis)
    assert size & (size - 1) == 0
    return [1 << i for i in range(size.bit_length() - 1)]


def swap(value, axis, bit):
    size = lax.axis_size(axis)
    return lax.ppermute(value, axis, [(i, i ^ bit) for i in range(size)])


def side_of(axis, bit):
    return (lax.axis_index(axis) // bit) % 2


def rows_of(value, start, count, axis=0):
    return lax.dynamic_slice_in_dim(value, start, count, axis)


def halve(axis, bits, partial, total):
    offset, span, received = jnp.int32(0), total, []

    def summed(start, count):
        value = partial(start, count)
        for got, base in received:
            value = value + rows_of(got, start - base, count).astype(FULL)
        return value

    for bit in bits:
        half = span // 2
        side = side_of(axis, bit)
        got = swap(summed(offset + (1 - side) * half, half).astype(LOW), axis, bit)
        offset = offset + side * half
        received.append((got, offset))
        span = half
    return summed(offset, span)


def double(axis, bits, value):
    for bit in bits:
        got = swap(value, axis, bit)
        first = side_of(axis, bit) == 0
        value = jnp.concatenate(
            [jnp.where(first, value, got), jnp.where(first, got, value)], axis=0
        )
    return value


def total_over(axes, value):
    for axis in axes:
        for bit in bits_of(axis):
            value = value + swap(value, axis, bit)
    return value


def ring(value, by):
    count = lax.axis_size("ctx")
    return lax.ppermute(value, "ctx", [(i, (i + by) % count) for i in range(count)])


def gather_weight(piece):
    count = lax.axis_size("ctx")
    place = lax.axis_index("ctx")
    ways = lax.axis_size("shard")
    blocks = [piece] + [ring(piece, by) for by in range(1, count)]
    whole = jnp.zeros((ways * count,) + piece.shape, piece.dtype)
    me = lax.axis_index("shard")
    for by, block in enumerate(blocks):
        at = (place - by) % count
        held = [(jnp.int32(0), block)]
        for bit in bits_of("shard"):
            held = held + [(other ^ bit, swap(value, "shard", bit)) for other, value in held]
        for other, value in held:
            whole = lax.dynamic_update_index_in_dim(whole, value, (me ^ other) * count + at, 0)
    return whole.reshape((ways * count * piece.shape[0],) + piece.shape[1:]), blocks[-1]


def scatter_weight(partial, total):
    count = lax.axis_size("ctx")
    place = lax.axis_index("ctx")
    mine = halve("shard", bits_of("shard")[::-1], partial, total).astype(LOW)
    mine = mine.reshape((count, mine.shape[0] // count) + mine.shape[1:])
    value = lax.dynamic_index_in_dim(mine, place, 0, False).astype(FULL)
    for by in range(1, count):
        given = lax.dynamic_index_in_dim(mine, (place + by) % count, 0, False)
        value = value + ring(given, by).astype(FULL)
    return value


def dot(left, right, contract):
    return lax.dot_general(
        left, right, ((contract[0], contract[1]), ((), ())), preferred_element_type=FULL
    )


def turned(value):
    return value.astype(FULL).T.astype(LOW)


def normalize(rows, gain, shift):
    row_mean = jnp.mean(rows, axis=-1, keepdims=True)
    centred = rows - row_mean
    inverse = lax.rsqrt(jnp.mean(centred * centred, axis=-1, keepdims=True) + EPSILON)
    normed = centred * inverse
    return (normed * gain + shift, normed, inverse)


def normalize_back(grad_out, normed, inverse, gain):
    scaled = grad_out * gain
    mean_grad = jnp.mean(scaled, axis=-1, keepdims=True)
    mean_cross = jnp.mean(scaled * normed, axis=-1, keepdims=True)
    return inverse * (scaled - mean_grad - normed * mean_cross)


def gelu_pair(value):
    spread = 0.5 * (1.0 + lax.erf(value * (0.5**0.5)))
    slope = spread + value * jnp.exp(-0.5 * value * value) * (1.0 / math.sqrt(2.0 * math.pi))
    return (value * spread).astype(LOW), slope.astype(LOW)


class Mover:
    def __init__(self, sizes, send, recv, local):
        self.ctx_count, self.shard_count = sizes
        self.send, self.recv, self.local = send, recv, local
        self.copies, self.here = [], []
        self.arrived = set()
        self.landed = set()
        self.ctx = lax.axis_index("ctx")
        self.shard = lax.axis_index("shard")

    def go(self, source, target, **device):
        index = len(self.copies)
        assert index < self.send.shape[0]
        copy = pltpu.make_async_remote_copy(
            src_ref=source,
            dst_ref=target,
            send_sem=self.send.at[index],
            recv_sem=self.recv.at[index],
            device_id=device,
            device_id_type=MESH,
        )
        copy.start()
        self.copies.append(copy)
        return index

    def stay(self, source, target):
        index = len(self.here)
        assert index < self.local.shape[0]
        copy = pltpu.make_async_copy(source, target, self.local.at[index])
        copy.start()
        self.here.append(copy)
        return index

    def near(self, *indices):
        for index in indices:
            if index not in self.landed:
                self.landed.add(index)
                self.here[index].wait()

    def take(self, index):
        if index not in self.arrived:
            self.arrived.add(index)
            self.copies[index].wait_recv()

    def flip(self, bits):
        place = self.ctx
        if bits & 1:
            place = place + 1 - 2 * lax.rem(self.ctx, 2)
        if bits & 2:
            place = place + 2 - 4 * (self.ctx // 2)
        return place

    def on(self, by):
        return lax.rem(self.ctx + by, self.ctx_count)

    def back(self, by):
        return lax.rem(self.ctx + self.ctx_count - by, self.ctx_count)

    def settle(self):
        for index, copy in enumerate(self.copies):
            self.take(index)
            copy.wait_send()
        self.near(*range(len(self.here)))


class Gather:
    def __init__(self, mover, source, target, across=True):
        self.mover, self.source, self.target, self.across = mover, source, target, across
        self.over = []

    def start_line(self):
        mover = self.mover
        mine, there = self.source, self.block(mover.ctx)
        self.far = mover.go(mine, there, ctx=mover.flip(2))
        self.close = mover.go(mine, there, ctx=mover.flip(1))

    def start_over(self):
        mover = self.mover
        mine, there = self.source, self.block(mover.ctx)
        if self.across:
            self.over.append(mover.go(mine, there, shard=1 - mover.shard))
        self.own = mover.stay(mine, there)

    def block(self, ctx):
        mover = self.mover
        rows = self.source.shape[0]
        start = ctx * rows
        if self.across:
            start = start + mover.shard * mover.ctx_count * rows
        return self.target.at[pl.ds(pl.multiple_of(start, rows), rows)]

    def pass_on(self, stage):
        mover = self.mover
        if stage == 1:
            mover.take(self.far)
            rows = self.block(mover.flip(2))
            self.passed = mover.go(rows, rows, ctx=mover.flip(1))
        elif stage == 2:
            mover.take(self.close)
            rows = self.block(mover.flip(1))
        else:
            mover.take(self.passed)
            rows = self.block(mover.flip(3))
        if self.across:
            self.over.append(mover.go(rows, rows, shard=1 - mover.shard))

    def have(self):
        for copy in self.over:
            self.mover.take(copy)
        self.mover.near(self.own)


class Across:
    def __init__(self, mover, source, target):
        rows = source.shape[0]
        there = target.at[pl.ds(pl.multiple_of(mover.shard * rows, rows), rows)]
        self.mover = mover
        self.copy = mover.go(source, there, shard=1 - mover.shard)
        self.own = mover.stay(source, there)

    def have(self):
        self.mover.take(self.copy)
        self.mover.near(self.own)


class Reduce:
    def __init__(self, mover, buffers, out, lhs, rhs):
        self.mover, self.out, self.lhs, self.rhs = mover, out, lhs, rhs
        self.give, self.got, self.mid, self.line = buffers
        self.half = self.give.shape[0]
        self.block = self.half // mover.ctx_count

    def compute(self, target, shard):
        chunk = min(256, self.half)

        def step(i, carry):
            at = pl.ds(pl.multiple_of(shard * self.half + i * chunk, chunk), chunk)
            here = pl.ds(pl.multiple_of(i * chunk, chunk), chunk)
            target[here, :] = dot(self.lhs[:, at], self.rhs[...], ((0,), (0,))).astype(LOW)
            return carry

        lax.fori_loop(0, self.half // chunk, step, 0)

    def begin_blocks(self):
        mover = self.mover
        self.blocks = {}
        for bits in (3, 2, 1, 0):
            ctx = mover.flip(bits)
            at = pl.ds(pl.multiple_of(ctx * self.block, self.block), self.block)
            start = pl.multiple_of((1 - mover.shard) * self.half + ctx * self.block, self.block)
            lhs = self.lhs[:, pl.ds(start, self.block)]
            self.give[at, :] = dot(lhs, self.rhs[...], ((0,), (0,))).astype(LOW)
            self.blocks[bits] = mover.go(
                self.give.at[at], self.got.at[at], shard=1 - mover.shard
            )

    def own(self):
        self.compute(self.mid, self.mover.shard)

    def fold_blocks(self, *which):
        mover = self.mover
        for bits in which:
            mover.take(self.blocks[bits])
            ctx = mover.flip(bits)
            at = pl.ds(pl.multiple_of(ctx * self.block, self.block), self.block)
            self.mid[at, :] = (
                self.mid[at, :].astype(FULL) + self.got[at, :].astype(FULL)
            ).astype(LOW)

    def rows(self, ctx):
        return self.mid.at[pl.ds(pl.multiple_of(ctx * self.block, self.block), self.block)]

    def send_first(self):
        mover = self.mover
        self.first = mover.go(self.rows(mover.flip(3)), self.line.at[1], ctx=mover.flip(1))

    def send_second(self):
        mover = self.mover
        self.second = mover.go(self.rows(mover.flip(1)), self.line.at[0], ctx=mover.flip(1))

    def send_third(self):
        mover = self.mover
        mover.take(self.first)
        rows = self.rows(mover.flip(2))
        rows[...] = (rows[...].astype(FULL) + self.line[1].astype(FULL)).astype(LOW)
        self.third = mover.go(rows, self.line.at[2], ctx=mover.flip(2))

    def done(self):
        self.mover.take(self.second)
        self.mover.take(self.third)
        value = self.rows(self.mover.ctx)[...].astype(FULL)
        self.out[...] = value + self.line[0].astype(FULL) + self.line[2].astype(FULL)


def reduce_buffers(half, width, count):
    return [
        VMEM((half, width), LOW),
        VMEM((half, width), LOW),
        VMEM((half, width), LOW),
        VMEM((count - 1, half // count, width), LOW),
    ]


def greet(mover, shard):
    barrier = pltpu.get_barrier_semaphore()
    peers = [dict(ctx=mover.on(by)) for by in range(1, mover.ctx_count)]
    peers += [dict(tp=peer) for peer in tp_peers()]
    if shard:
        peers.append(dict(shard=1 - mover.shard))
    for peer in peers:
        pl.semaphore_signal(barrier, inc=1, device_id=peer, device_id_type=MESH)
    pl.semaphore_wait(barrier, len(peers))


def tp_peers():
    place = lax.axis_index("tp")
    core, far = lax.rem(place, 2), place // 2
    return place + 1 - 2 * core, place + 2 - 4 * far


def run(kernel, name, ident, inputs, outputs, scratch, remote, local, sizes, vmem, flops):
    n_in, n_out, n_scratch = len(inputs), len(outputs), len(scratch)

    def body(*refs):
        ins, outs = refs[:n_in], refs[n_in : n_in + n_out]
        work = refs[n_in + n_out :]
        mover = Mover(sizes, *work[n_scratch:])
        kernel(mover, ins, outs, work[:n_scratch])

    return pl.pallas_call(
        body,
        in_specs=[pl.BlockSpec(memory_space=space) for _, space in inputs],
        out_specs=[pl.BlockSpec(memory_space=space) for _, _, space in outputs],
        out_shape=[jax.ShapeDtypeStruct(shape, dtype) for shape, dtype, _ in outputs],
        scratch_shapes=list(scratch)
        + [
            pltpu.SemaphoreType.DMA((remote,)),
            pltpu.SemaphoreType.DMA((remote,)),
            pltpu.SemaphoreType.DMA((local,)),
        ],
        compiler_params=pltpu.CompilerParams(
            collective_id=ident, has_side_effects=True, vmem_limit_bytes=vmem * 2**20
        ),
        cost_estimate=pl.CostEstimate(flops=flops, bytes_accessed=2**24, transcendentals=0),
        name=name,
    )(*[value for value, _ in inputs])


def order_of(block, count):
    return (block + count - 1) % count


def tiles_of(count, capacity, tile):
    ends = [-(-(p + 1) * capacity // tile) for p in range(count)]
    return list(zip([0] + ends[:-1], ends))


def tile_at(t, tile):
    return pl.ds(pl.multiple_of(t * tile, tile), tile)


def turned_product(left, right, bias, target):
    value = jnp.dot(left[...], right[...], preferred_element_type=FULL)
    if bias is not None:
        value = value + bias[0:1, :]
    target[...] = turned(value.astype(LOW))


def head_rows(ref, head, width):
    return ref.at[pl.ds(pl.multiple_of(head * width, 16), width)]


def attend_part(size, tile, mover, joint, bias, heads, qkv, o_ref, lse, work, after_send, begun, between):
    k_ref, q_ref, v_ref, low_ref, score_ref, top_ref = work
    count, width, capacity = qkv.shape
    slots = count * capacity
    sent = [None] + [
        mover.go(head_rows(joint, mover.on(by), width), qkv.at[by], ctx=mover.on(by))
        for by in range(1, count)
    ]
    after_send()
    qkv[0] = head_rows(joint, mover.ctx, width)[...]
    q_ref[size:PAD, :] = jnp.concatenate(
        [jnp.ones((16, slots), LOW), jnp.zeros((PAD - size - 16, slots), LOW)], axis=0
    )

    v_ref[size : size + 16, :] = jnp.ones((16, slots), LOW)

    def prepare(r):
        here = slice(r * capacity, (r + 1) * capacity)
        p = order_of(r, count)
        q_ref[0:size, p * capacity : (p + 1) * capacity] = (
            qkv[r, 0:size, :] * (size**-0.5)
        ).astype(LOW)
        v_ref[0:size, here] = qkv[r, 2 * size : 3 * size, :]
        keys = jnp.concatenate(
            [qkv[r, size : 2 * size, :], bias[:, here], jnp.zeros((PAD - size - 16, capacity), LOW)],
            axis=0,
        )
        k_ref[here, :] = turned(keys)

    prepare(0)
    for by in range(1, count):
        mover.take(sent[by])
        prepare(by)

    begun()
    last = slots // tile - 1
    assert last % 2 == 1

    def phase(t, now, following, then):
        at, ahead = tile_at(t, tile), tile_at(following, tile)
        top = top_ref[now, 0:1, :]
        summed = jnp.zeros((size + 16, tile), FULL)
        new_top = jnp.full((1, tile), NEG_LARGE, FULL)
        for r in range(count):
            here = slice(r * capacity, (r + 1) * capacity)
            scores = jnp.dot(k_ref[here, :], q_ref[:, ahead], preferred_element_type=FULL)
            score_ref[then, here, :] = scores
            new_top = jnp.maximum(new_top, jnp.max(scores, axis=0, keepdims=True))
            weights = jnp.exp(score_ref[now, here, :] - top)
            summed = summed + jnp.dot(
                v_ref[:, here], weights.astype(LOW), preferred_element_type=FULL
            )
        top_ref[then] = jnp.broadcast_to(new_top, (8, tile))
        total = summed[size : size + 1]
        out = summed[0:size] / total
        o_ref[:, at] = out
        low_ref[:, at] = out.astype(LOW)
        lse[:, at] = jnp.broadcast_to(top + jnp.log(total), (8, tile))

    def step(i, carry):
        phase(2 * i, 0, 2 * i + 1, 1)
        phase(2 * i + 1, 1, jnp.minimum(2 * i + 2, last), 0)
        return carry

    scores = jnp.dot(k_ref[...], q_ref[:, 0:tile], preferred_element_type=FULL)
    score_ref[0] = scores
    top_ref[0] = jnp.broadcast_to(jnp.max(scores, axis=0, keepdims=True), (8, tile))
    arriving = []
    for p, (low, high) in enumerate(tiles_of(count, capacity, 2 * tile)):
        lax.fori_loop(low, high, step, 0)
        done = low_ref.at[:, p * capacity : (p + 1) * capacity]
        if p < count - 1:
            there = head_rows(heads, mover.ctx, size)
            arriving.append(mover.go(done, there, ctx=mover.back(p + 1)))
        else:
            head_rows(heads, mover.ctx, size)[...] = low_ref[:, p * capacity : (p + 1) * capacity]
        between(p + 1)
    for copy in arriving:
        mover.take(copy)


def below(row, ones):
    width = row.shape[1]
    high = row.astype(LOW).astype(FULL)
    middle = (row - high).astype(LOW).astype(FULL)
    low = row - high - middle
    lead = jnp.full((1, width), 1.0 if ones else 0.0, FULL)
    rest = jnp.zeros((PAD // 2 - 4, width), FULL)
    return jnp.concatenate([lead, high, middle, low, rest], axis=0).astype(LOW)


def attend_back_part(size, tile, mover, parts, bias, qkv, o_ref, lse, grads, work, ready, waiting, begun, between):
    k_ref, v_ref, q_ref, do_ref, nat_ref, dq_ref, dk_ref, dv_ref, got, back = work
    count, width, capacity = qkv.shape
    slots = count * capacity
    sent = [None] + [
        mover.go(head_rows(parts, mover.on(by), size), got.at[by], ctx=mover.on(by))
        for by in range(1, count)
    ]
    got[0] = head_rows(parts, mover.ctx, size)[...]
    waiting()
    ready()
    q_ref[size:PAD, :] = below(lse[0:1, :], True)
    dq_ref[...] = jnp.zeros_like(dq_ref)
    off = (lax.broadcasted_iota(jnp.int32, (16, capacity), 0) + 2) // 3
    taken = jnp.where(off == 1, -1.0, 0.0).astype(LOW)
    pad = jnp.zeros((PAD - size - 16, capacity), LOW)
    for r in range(count):
        here = slice(r * capacity, (r + 1) * capacity)
        k_ref[here, :] = turned(
            jnp.concatenate([qkv[r, size : 2 * size, :], bias[:, here] + taken, pad], axis=0)
        )
        v_ref[here, :] = turned(
            jnp.concatenate([qkv[r, 2 * size : 3 * size, :], taken, pad], axis=0)
        )
    for r in range(count):
        if r:
            mover.take(sent[r])
        p = order_of(r, count)
        at = slice(p * capacity, (p + 1) * capacity)
        scaled = (qkv[r, 0:size, :] * (size**-0.5)).astype(LOW)
        dout = got[r]
        q_ref[0:size, at] = scaled
        do_ref[0:size, at] = dout
        nat_ref[at, :] = turned(jnp.concatenate([scaled, dout], axis=0))
        delta = jnp.sum(dout.astype(FULL) * o_ref[:, at], axis=0, keepdims=True)
        do_ref[size:PAD, at] = below(delta, False)

    begun()
    tiles = tiles_of(count, capacity, tile)
    arriving = []
    mine = head_rows(grads, mover.ctx, width)
    for turn, r in enumerate(list(range(1, count)) + [0]):
        here = slice(r * capacity, (r + 1) * capacity)
        dk_ref[...] = jnp.zeros_like(dk_ref)
        dv_ref[...] = jnp.zeros_like(dv_ref)

        def step(t, carry, r=r, here=here):
            at = tile_at(t, tile)
            scores = jnp.dot(k_ref[here, :], q_ref[:, at], preferred_element_type=FULL)
            chance = jnp.exp(scores)
            chance_grad = jnp.dot(v_ref[here, :], do_ref[:, at], preferred_element_type=FULL)
            score_grad = (chance * chance_grad).astype(LOW)
            dq_ref[:, at] += jnp.dot(
                qkv[r, size : 2 * size, :], score_grad, preferred_element_type=FULL
            )
            dk_ref[...] += jnp.dot(score_grad, nat_ref[at, :], preferred_element_type=FULL)
            dv_ref[...] += jnp.dot(
                chance.astype(LOW), nat_ref[at, :], preferred_element_type=FULL
            )
            return carry

        if r:
            lax.fori_loop(0, tiles[-1][1], step, 0)
        else:
            for p, (low, high) in enumerate(tiles):
                lax.fori_loop(low, high, step, 0)
                at = slice(p * capacity, (p + 1) * capacity)
                value = (dq_ref[:, at] * (size**-0.5)).astype(LOW)
                if p < count - 1:
                    back[p + 1, 0:size, :] = value
                    arriving.append(
                        mover.go(
                            back.at[p + 1, 0:size], mine.at[0:size], ctx=mover.back(p + 1)
                        )
                    )
                else:
                    mine[0:size, :] = value
        keys = dk_ref[...].T[0:size].astype(LOW)
        values = dv_ref[...].T[size : 2 * size].astype(LOW)
        if r:
            back[r, size : 2 * size, :] = keys
            back[r, 2 * size : 3 * size, :] = values
            arriving.append(
                mover.go(
                    back.at[r, size : 3 * size], mine.at[size : 3 * size], ctx=mover.back(r)
                )
            )
        else:
            mine[size : 2 * size, :] = keys
            mine[2 * size : 3 * size, :] = values
        between(turn)
    for copy in arriving:
        mover.take(copy)


def attend_back_buffers(size, count, capacity):
    slots = count * capacity
    return [
        VMEM((slots, PAD), LOW),
        VMEM((slots, PAD), LOW),
        VMEM((PAD, slots), LOW),
        VMEM((PAD, slots), LOW),
        VMEM((slots, PAD), LOW),
        VMEM((size, slots), FULL),
        VMEM((capacity, PAD), FULL),
        VMEM((capacity, PAD), FULL),
        VMEM((count, size, capacity), LOW),
        VMEM((count, 3 * size, capacity), LOW),
    ]


class Round:
    def __init__(self, mover, rows, full, buffers):
        place = lax.axis_index("tp")
        core, far = lax.rem(place, 2), place // 2
        self.mover, self.full = mover, full
        self.give, self.ra, self.passing, self.rb, self.keep = buffers
        self.span = rows // 4
        self.half = self.span // 2
        self.mate, self.far = tp_peers()

        def quarter(c, f):
            return (c * 2 + f) * self.span

        self.own, self.other = quarter(core, far), quarter(core, 1 - far)
        self.mate_own, self.mate_other = quarter(1 - core, far), quarter(1 - core, 1 - far)

    def rows(self, start, count=None):
        return pl.ds(pl.multiple_of(start, 16), count or self.span)

    def hand(self, slot, value):
        self.give[slot] = value.astype(LOW)
        return self.mover.go(self.give.at[slot], self.ra.at[slot], tp=self.mate)

    def onward(self, value, index):
        self.mover.take(index)
        self.passing[...] = (value + self.ra[1].astype(FULL)).astype(LOW)
        return [
            self.mover.go(self.passing.at[at], self.rb.at[at], tp=self.far)
            for at in (pl.ds(0, self.half), pl.ds(self.half, self.half))
        ]

    def close(self, far_copies, index, finish, halfway=None):
        self.mover.take(index)
        self.keep[...] += self.ra[0].astype(FULL)
        self.to_far, self.to_mate = [], []
        for c in range(2):
            at = pl.ds(c * self.half, self.half)
            self.mover.take(far_copies[c])
            low = finish(at, self.keep[at] + self.rb[at].astype(FULL))
            mine = self.full.at[self.rows(self.own + c * self.half, self.half)]
            mine[...] = low
            self.to_far.append(self.mover.go(mine, mine, tp=self.far))
            self.to_mate.append(self.mover.go(mine, mine, tp=self.mate))
            if halfway and c == 0:
                halfway()

    def eager(self, make, finish, meanwhile=None, halfway=None):
        first = self.hand(1, make(self.mate_other))
        copies = self.onward(make(self.other), first)
        second = self.hand(0, make(self.mate_own))
        self.keep[...] = make(self.own)
        if meanwhile:
            meanwhile()
        self.close(copies, second, finish, halfway)

    def after(self, before, make, finish, meanwhile, between):
        before.have_mate_own()
        second = self.hand(0, make(self.mate_own))
        self.keep[...] = make(self.own)
        before.have_other()
        between()
        value = make(self.other)
        before.have_mate_other()
        first = self.hand(1, make(self.mate_other))
        copies = self.onward(value, first)
        meanwhile()
        self.close(copies, second, finish)

    def have_mate_own(self):
        for copy in self.to_mate:
            self.mover.take(copy)

    def have_other(self):
        self.passed = []
        for c in range(2):
            self.mover.take(self.to_far[c])
            rows = self.full.at[self.rows(self.other + c * self.half, self.half)]
            self.passed.append(self.mover.go(rows, rows, tp=self.mate))

    def have_mate_other(self):
        for copy in self.passed:
            self.mover.take(copy)

    def have(self):
        self.have_mate_own()
        self.have_other()
        self.have_mate_other()


ROUND_COPIES = 10


def round_buffers(rows, width):
    span = rows // 4
    return [
        VMEM((2, span, width), LOW),
        VMEM((2, span, width), LOW),
        VMEM((span, width), LOW),
        VMEM((span, width), LOW),
        VMEM((span, width), FULL),
    ]


NAMES = ("qkv", "out", "up", "down")


def layer_kernel(plan, last, size, tile, mover, ins, outs, work):
    ins, outs, work = iter(ins), iter(outs), iter(work)
    source = next(ins)
    x_ref = None if plan.entry else next(ins)
    live_ref = next(ins)
    far_params = [next(ins) for _ in range(8)]
    stream, following = next(outs), next(outs)
    far_qkv, far_o, far_lse, far_heads, far_middle, far_second, far_hidden, far_slope = [
        next(outs) for _ in range(8)
    ]
    far_first = next(outs) if plan.entry else None
    joint, nat, heads, qkv, o_ref, lse, middle, second, hidden, slope = [
        next(work) for _ in range(10)
    ]
    first = next(work) if plan.entry else source
    attend_work = [next(work) for _ in range(6)]
    one_work, two_work = [next(work) for _ in range(5)], [next(work) for _ in range(5)]
    rows = source.shape[0]
    bias, qkv_bias = next(work), next(work)
    params = [next(work) for _ in range(8)]
    whole = {name: next(work) for name in NAMES}
    gathers, loads = {}, {}
    for name in plan.held:
        loads[name] = (next(ins), whole[name])
    half_refs = {name: next(ins) for name in plan.halves}
    for name in plan.own:
        gathers[name, 0] = Gather(mover, next(ins).at[plan.layer], whole[name])
    kept_ahead = {name: next(outs) for name in plan.ahead + plan.lines}
    for name in plan.ahead + plan.lines:
        gathers[name, 1] = Gather(
            mover, next(ins).at[plan.layer + 1], next(work), name in plan.ahead
        )
    kept = {name: next(outs) for name in plan.kept}

    greet(mover, bool(gathers))
    halves = {name: Across(mover, half_refs[name], whole[name]) for name in plan.halves}
    if plan.entry:
        gathers_first = [key for key in [("qkv", 0)] if key in gathers]
        for key in gathers_first:
            gathers[key].start_line()
            gathers[key].start_over()
    param_loads = [mover.stay(there, here) for there, here in zip(far_params, params)]
    waiting_loads = dict(loads)
    loads = {}

    def load(names):
        for name in names:
            if name in waiting_loads and name not in loads:
                loads[name] = mover.stay(*waiting_loads[name])

    load(["qkv"])

    def have(name):
        if name in waiting_loads:
            mover.near(loads[name])
            load(NAMES)
        else:
            (halves[name] if name in halves else gathers[name, 0]).have()
            mover.stay(whole[name], kept[name])
        return whole[name]

    def begin(keys):
        for key in keys:
            if key in gathers:
                gathers[key].start_line()

    def begin_over(keys):
        for key in keys:
            if key in gathers:
                gathers[key].start_over()

    def pass_on(keys, stage):
        for key in keys:
            if key in gathers:
                gathers[key].pass_on(stage)

    def pass_all(keys):
        for stage in (1, 2, 3):
            pass_on(keys, stage)

    mover.near(*param_loads)
    layer, after = plan.layer, min(plan.layer + 1, params[0].shape[0] - 1)

    def row(index, layer=layer):
        return params[index][...].astype(FULL)[layer : layer + 1]

    b_out, gain2, shift2, b_down, b_up = row(0), row(1), row(2), row(3), row(6)
    gain1, shift1, gain0, shift0 = row(4, after), row(5, after), row(4), row(5)
    qkv_bias[...] = joint_bias(row(7), size, joint.shape[0])
    key_bias(mover, live_ref, bias)
    ahead, lines = [("qkv", 1)], [("out", 1), ("up", 1)]
    one = Round(mover, rows, second, one_work)
    two = Round(mover, rows, following, two_work)
    if plan.entry:
        chunk = rows // 5 if rows % 80 == 0 else rows

        def norm_step(i, carry):
            at = pl.ds(pl.multiple_of(i * chunk, 16), chunk)
            value = normalize(source[at, :].astype(FULL), gain0, shift0)[0]
            first[at, :] = value.astype(LOW)
            return carry

        lax.fori_loop(0, rows // chunk, norm_step, 0)
        mover.stay(first, far_first)
        pass_all([("qkv", 0)])
        begin([("out", 0), ("up", 0)])
        begin_over([("out", 0), ("up", 0), ("down", 0)] + ahead + lines)
        turned_product(first, have("qkv"), qkv_bias, joint)
    else:
        turned_product(first, have("qkv"), qkv_bias, joint)

    def after_send():
        if plan.entry:
            pass_all([("out", 0), ("up", 0)])
        else:
            for name in plan.own:
                gathers[name, 0].start_over()

    def begun():
        begin([("down", 0)])

    def between(p):
        if p > 2:
            pass_on([("down", 0)], p - 2)
        if p == 4:
            if not plan.entry:
                begin_over(ahead + lines)
            begin(ahead)

    attend_part(
        size, tile, mover, joint, bias, heads, qkv, o_ref, lse, attend_work, after_send, begun, between
    )
    nat[...] = turned(heads[...])
    w_out = have("out")

    def out_part(start):
        return dot(nat[one.rows(start), :], w_out[...], ((1,), (1,)))

    def to_second(at, value):
        if plan.entry:
            before = source[one.rows(one.own + at.start, at.size), :].astype(FULL)
        else:
            before = x_ref[at]
        value = before + value + b_out
        middle[at] = value
        return normalize(value, gain2, shift2)[0].astype(LOW)

    def meanwhile():
        mover.stay(qkv, far_qkv)
        mover.stay(o_ref, far_o)
        mover.stay(lse, far_lse)
        mover.stay(nat, far_heads)
        pass_on([("down", 0)], 3)

    one.eager(out_part, to_second, meanwhile, lambda: pass_on(ahead, 1))
    pass_on(ahead, 2)
    begin(lines)
    w_up, w_down = have("up"), have("down")

    def mlp_part(start):
        at = two.rows(start)
        pre = jnp.dot(second[at, :], w_up[...], preferred_element_type=FULL) + b_up
        low, low_slope = gelu_pair(pre)
        hidden[at, :] = low
        slope[at, :] = low_slope
        return dot(low, w_down[...], ((1,), (1,)))

    def to_following(at, value):
        value = middle[at] + value + b_down
        stream[at] = value
        if last:
            return live_rows(value, two.own + at.start, live_ref[0, mover.ctx]).astype(LOW)
        return normalize(value, gain1, shift1)[0].astype(LOW)

    def meanwhile():
        mover.stay(middle, far_middle)
        mover.stay(second, far_second)
        mover.stay(hidden, far_hidden)
        mover.stay(slope, far_slope)
        pass_on(lines, 1)

    two.after(one, mlp_part, to_following, meanwhile, lambda: pass_on(ahead, 3))
    two.have()
    pass_on(lines, 2)
    pass_on(lines, 3)
    for name in plan.ahead + plan.lines:
        gathers[name, 1].have()
        mover.stay(gathers[name, 1].target, kept_ahead[name])
    mover.settle()


class Plan:
    def __init__(self, layer, last, inside):
        self.layer, self.entry = layer, layer == 0
        self.own = (NAMES if layer == 0 else ("down",)) if inside else ()
        self.halves = ("out", "up") if inside and layer else ()
        self.ahead = ("qkv",) if inside and not last else ()
        self.lines = ("out", "up") if inside and not last else ()
        self.kept = self.own + self.halves
        self.held = tuple(name for name in NAMES if name not in self.kept)


def forward_layer(source, x, live, params, gathered, weights, plan, last, size, sizes, ident):
    rows, width = source.shape
    count = sizes[0]
    joint, hidden = weights["qkv"].shape[2], weights["up"].shape[2]
    heads = joint // (3 * size)
    attn, slots, span = heads * size, count * rows, rows // 4
    tile = 256 if slots % 256 == 0 else PAD
    columns = {"qkv": joint, "out": attn, "up": hidden, "down": hidden}
    inputs = [(source, VMEM)] + ([] if plan.entry else [(x, VMEM)])
    inputs += [(live, SMEM)] + [(value, HBM) for value in params]
    inputs += [(gathered[name, plan.layer], HBM) for name in plan.held]
    inputs += [(gathered[name, plan.layer, 0], HBM) for name in plan.halves]
    inputs += [(weights[name], HBM) for name in plan.own + plan.ahead + plan.lines]
    saved = [
        ((count, 3 * size, rows), LOW),
        ((size, slots), FULL),
        ((8, slots), FULL),
        ((rows, attn), LOW),
        ((span, width), FULL),
        ((rows, width), LOW),
        ((rows, hidden), LOW),
        ((rows, hidden), LOW),
    ]
    outputs = [((span, width), FULL, VMEM), ((rows, width), LOW, VMEM)]
    outputs += [(shape, dtype, HBM) for shape, dtype in saved]
    if plan.entry:
        outputs.append(((rows, width), LOW, HBM))
    ahead = [(width, columns[name]) for name in plan.ahead]
    ahead += [(width // 2, columns[name]) for name in plan.lines]
    outputs += [(shape, LOW, HBM) for shape in ahead]
    outputs += [((width, columns[name]), LOW, HBM) for name in plan.kept]
    qkv_shape, o_shape, lse_shape, heads_shape = saved[:4]
    scratch = [VMEM((joint, rows), LOW), VMEM((rows, attn), LOW), VMEM((attn, rows), LOW)]
    scratch += [VMEM(*pair) for pair in saved[:3] + saved[4:]]
    if plan.entry:
        scratch.append(VMEM((rows, width), LOW))
    scratch += [
        VMEM((slots, PAD), LOW),
        VMEM((PAD, slots), LOW),
        VMEM((size + 16, slots), LOW),
        VMEM((size, slots), LOW),
        VMEM((2, slots, tile), FULL),
        VMEM((2, 8, tile), FULL),
    ]
    scratch += round_buffers(rows, width) + round_buffers(rows, width)
    scratch += [VMEM((16, slots), LOW), VMEM((16, joint), FULL)]
    scratch += [VMEM(value.shape, value.dtype) for value in params]
    scratch += [VMEM((width, columns[name]), LOW) for name in NAMES]
    scratch += [VMEM(shape, LOW) for shape in ahead]
    results = run(
        functools.partial(layer_kernel, plan, last, size, tile),
        "forward_layer",
        ident,
        inputs,
        outputs,
        scratch,
        2 * (count - 1) + 2 * ROUND_COPIES + 2 * count * len(plan.kept + plan.ahead + plan.lines),
        10 + 2 * len(plan.kept + plan.ahead + plan.lines) + len(plan.held) + len(params),
        sizes,
        58,
        2 * rows * width * (2 * hidden + attn + joint) + 4 * slots * slots * 256,
    )
    stream, following = results[:2]
    kept = results[2 : 11 if plan.entry else 10]
    rest = iter(results[2 + len(kept) :])
    for name in plan.ahead:
        gathered[name, plan.layer + 1] = next(rest)
    for name in plan.lines:
        gathered[name, plan.layer + 1, 0] = next(rest)
    for name in plan.kept:
        gathered[name, plan.layer] = next(rest)
    return stream, following, kept


class SmallSums:
    def __init__(self, mover, rows, held, got):
        self.mover, self.rows, self.held, self.got = mover, rows, held, got
        self.stage = 0
        mate, far = tp_peers()
        self.peers = [
            dict(tp=mate),
            dict(tp=far),
            dict(shard=1 - mover.shard),
            dict(ctx=mover.flip(2)),
            dict(ctx=mover.flip(1)),
        ]

    def part(self, stage):
        return pl.ds(0, self.rows if stage < 2 else self.held.shape[1])

    def step(self):
        stage, mover = self.stage, self.mover
        if stage:
            mover.take(self.copy)
            at = self.part(stage - 1)
            self.held[stage] = self.held[stage - 1]
            self.held[stage, at, :] = self.held[stage - 1, at, :] + self.got[stage - 1, at, :]
        if stage < len(self.peers):
            at = self.part(stage)
            self.copy = mover.go(
                self.held.at[stage, at], self.got.at[stage, at], **self.peers[stage]
            )
        self.stage = stage + 1

    def value(self):
        return self.held[len(self.peers)]


def key_bias(mover, live_ref, bias):
    capacity = bias.shape[1] // mover.ctx_count
    row = lax.broadcasted_iota(jnp.int32, (16, capacity), 0)
    slot = lax.broadcasted_iota(jnp.int32, (16, capacity), 1)
    for r in range(mover.ctx_count):
        live = live_ref[0, mover.back(r)]
        value = jnp.where((row == 0) & (slot >= live), NEG_LARGE, 0.0)
        bias[:, r * capacity : (r + 1) * capacity] = value.astype(LOW)


def pair_columns(rows, width, size, turn):
    shape = (width, rows) if turn else (rows, width)
    given = lax.broadcasted_iota(jnp.int32, shape, 1 if turn else 0)
    column = lax.broadcasted_iota(jnp.int32, shape, 0 if turn else 1)
    head, within = column // (3 * size), column % (3 * size)
    wanted = head * (2 * size) + jnp.where(within < size, within, within - size)
    key = (within >= size) & (within < 2 * size)
    return jnp.where((given == wanted) & ~key, 1.0, 0.0).astype(LOW)


def joint_bias(pair, size, width):
    rows = pair.shape[1]
    spread = jnp.broadcast_to(pair, (16, rows)).astype(LOW)
    return jnp.dot(spread, pair_columns(rows, width, size, False), preferred_element_type=FULL)


def live_rows(value, start, live):
    row = start + lax.broadcasted_iota(jnp.int32, value.shape, 0)
    return jnp.where(row < live, value, 0.0)


def sums_into(sums, first, at, values):
    for index, value in enumerate(values):
        row = first + index
        added = jnp.sum(value, axis=0, keepdims=True)
        width = added.shape[1]
        sums[row : row + 1, 0:width] = (
            added if at.start == 0 else sums[row : row + 1, 0:width] + added
        )


def back_kernel(plan, size, tile, mover, ins, outs, work):
    ins, outs, work = iter(ins), iter(outs), iter(work)
    source = next(ins)
    x_ref = None if plan.last else next(ins)
    live_ref, far_gain2, far_gain1 = [next(ins) for _ in range(3)]
    far = [next(ins) for _ in range(14)]
    late_far = next(ins) if plan.late else None
    others = [(next(ins), next(ins)) for _ in range(plan.others)]
    stream, following = next(outs), next(outs)
    grad_outs = {name: next(outs) for name in NAMES if plan.inside and (name != "qkv" or plan.final)}
    mid_out = next(outs) if plan.inside and not plan.final else None
    late_out = next(outs) if plan.late else None
    split = local = totals = None
    if plan.joined:
        totals = next(outs)
    else:
        split, local = next(outs), next(outs)
    wholes = {} if plan.inside else {name: next(outs) for name in NAMES}
    near = [next(work) for _ in range(14)]
    slope, w_down, w_up, middle, hidden, second, w_out, heads, qkv, o_ref, lse, first, w_qkv, before = near
    grad = next(work) if plan.last else source
    pre_grad, attn_grad, parts, grads, nat = [next(work) for _ in range(5)]
    attend_work = [next(work) for _ in range(10)]
    one_work, two_work = [next(work) for _ in range(5)], [next(work) for _ in range(5)]
    rows, width = source.shape
    reduces = {}
    if plan.inside:
        pairs = {
            "down": (grad, hidden),
            "up": (second, pre_grad),
            "out": (attn_grad, heads),
            "qkv": (first, nat),
        }
        for name in ("down", "up", "out", "qkv"):
            buffers = [next(work) for _ in range(4)]
            reduces[name] = Reduce(mover, buffers, grad_outs.get(name), *pairs[name])
    late = None
    if plan.late:
        late_mid, late_line = next(work), next(work)
        late = Reduce(mover, (late_mid, None, late_mid, late_line), late_out, None, None)
    bias, gain2_ref, gain1_ref = [next(work) for _ in range(3)]
    if plan.joined:
        split, local = next(work), next(work)
        early_held, early_got, late_held, late_got = [next(work) for _ in range(4)]
        tops = 8 * (plan.others + 1)
        early = SmallSums(mover, tops, early_held, early_got)
        final = SmallSums(mover, 8, late_held, late_got)
        everything = [(split, local)] + others

    greet(mover, plan.inside)
    gain_loads = [mover.stay(far_gain2, gain2_ref), mover.stay(far_gain1, gain1_ref)]
    one = Round(mover, rows, attn_grad, one_work)
    two = Round(mover, rows, following, two_work)
    if plan.final:
        far[13] = far[13].at[two.rows(two.own)]
    load = {index: mover.stay(far[index], near[index]) for index in (0, 1, 2)}
    late_load = mover.stay(late_far, late_mid) if late else None
    if plan.last:
        chunk = rows // 5 if rows % 80 == 0 else rows

        def mask_step(i, carry):
            at = pl.ds(pl.multiple_of(i * chunk, 16), chunk)
            value = source[at, :].astype(FULL)
            grad[at, :] = live_rows(value, i * chunk, live_ref[0, mover.ctx]).astype(LOW)
            return carry

        lax.fori_loop(0, rows // chunk, mask_step, 0)
    key_bias(mover, live_ref, bias)
    mover.near(*gain_loads)
    gain2, gain1 = [
        ref[...].astype(FULL)[plan.layer : plan.layer + 1] for ref in (gain2_ref, gain1_ref)
    ]
    split[...] = jnp.zeros_like(split)
    local[...] = jnp.zeros_like(local)
    split[5:6, 0:width] = jnp.sum(
        grad[one.rows(one.own), :].astype(FULL), axis=0, keepdims=True
    )
    hidden_width = slope.shape[1]

    def mlp_part(start):
        at = one.rows(start)
        pre = jnp.dot(grad[at, :], w_down[...], preferred_element_type=FULL)
        low = (pre * slope[at, :].astype(FULL)).astype(LOW)
        pre_grad[at, :] = low
        local[0:1, 0:hidden_width] += jnp.sum(low.astype(FULL), axis=0, keepdims=True)
        return dot(low, w_up[...], ((1,), (1,)))

    def to_attn(at, value):
        if plan.last:
            above = grad[one.rows(one.own + at.start, at.size), :].astype(FULL)
        else:
            above = x_ref[at]
        _, normed, inverse = normalize(middle[at], 1.0, 0.0)
        result = above + normalize_back(value, normed, inverse, gain2)
        stream[at] = result
        low = result.astype(LOW)
        sums_into(split, 2, at, (value * normed, value, low.astype(FULL)))
        return low

    def reduce(name):
        if name in reduces:
            reduces[name].begin_blocks()

    def own(name):
        if name in reduces:
            reduces[name].own()

    def first_step(name):
        if name in reduces:
            reduces[name].fold_blocks(3)
            reduces[name].send_first()

    def second_step(name):
        if name in reduces:
            reduces[name].fold_blocks(2)
            reduces[name].send_third()

    def rest(name):
        if name in reduces:
            reduces[name].fold_blocks(1)
            reduces[name].send_second()
            reduces[name].fold_blocks(0)

    def begin_early():
        if plan.joined:
            early_held[0] = jnp.zeros(early_held.shape[1:], FULL)
            for layer, (some, more) in enumerate(everything):
                first_row = 0 if layer else 2
                for row in range(first_row, 6):
                    at = row * len(everything) + layer
                    early_held[0, at : at + 1, :] = some[row : row + 1, :]
                for row in range(2 if layer else 1):
                    at = tops + row * len(everything) + layer
                    early_held[0, at : at + 1, :] = more[row : row + 1, :]

    def early_step():
        if plan.joined:
            early.step()

    def start_down():
        mover.near(load[3], load[4])
        reduce("down")
        if late:
            late.send_third()

    if late:
        mover.near(late_load)
        late.send_first()
        late.send_second()
    mover.near(load[0], load[1], load[2])
    for index in range(3, len(far)):
        load[index] = mover.stay(far[index], near[index])
    one.eager(mlp_part, to_attn, start_down)
    mover.near(load[5])
    reduce("up")
    one.have()
    mover.near(load[6])
    turned_product(attn_grad, w_out, None, parts)

    def waiting():
        begin_early()
        early_step()
        own("down")
        first_step("down")
        mover.near(load[7])
        reduce("out")
        own("out")

    def ready():
        own("up")
        mover.near(load[8], load[9], load[10])

    def between(turn):
        if turn == 0:
            early_step()
        if turn == 3:
            second_step("down")
            first_step("up")

    attend_back_part(
        size,
        tile,
        mover,
        parts,
        bias,
        qkv,
        o_ref,
        lse,
        grads,
        attend_work,
        ready,
        waiting,
        lambda: rest("down"),
        between,
    )
    early_step()
    nat[...] = turned(grads[...])
    pairs_width = nat.shape[1] // 3 * 2
    picked = jnp.dot(
        nat[...], pair_columns(pairs_width, nat.shape[1], size, True), preferred_element_type=FULL
    )
    local[1:2, 0:pairs_width] = jnp.sum(picked, axis=0, keepdims=True)
    mover.near(*[load[index] for index in range(11, len(far))])

    def qkv_part(start):
        return dot(nat[two.rows(start), :], w_qkv[...], ((1,), (1,)))

    def to_following(at, value):
        row = before[at, :].astype(FULL)
        _, normed, inverse = normalize(row, 1.0, 0.0)
        result = stream[at] + normalize_back(value, normed, inverse, gain1)
        stream[at] = result
        low = result.astype(LOW)
        sums_into(split, 0, at, (value * normed, value))
        return low

    def meanwhile():
        if not plan.final:
            reduce("qkv")
        own("qkv")
        second_step("up")
        first_step("out")
        early_step()

    def halfway():
        if plan.final:
            first_step("qkv")

    if plan.final:
        reduce("qkv")
    two.eager(qkv_part, to_following, meanwhile, halfway)
    if plan.joined:
        late_held[0, 0:8, :] = jnp.zeros((8, late_held.shape[2]), FULL)
        late_held[0, 0:2, :] = split[0:2, :]
        late_held[0, 8:16, :] = local[...]
        final.step()
        final.step()
    two.have_mate_own()
    two.have_other()
    if plan.joined:
        final.step()
        early_step()
    second_step("out")
    if plan.final:
        second_step("qkv")
    if plan.joined:
        final.step()
    for name in ("up", "out") + (("qkv",) if plan.final else ()):
        rest(name)
    if plan.inside and not plan.final:
        reduces["qkv"].fold_blocks(3, 2, 1, 0)
        mover.stay(reduces["qkv"].mid, mid_out)
    two.have_mate_other()
    if plan.joined:
        final.step()
    for name in ("down", "up", "out"):
        if name in reduces:
            reduces[name].done()
    if late:
        late.done()
    if plan.inside and plan.final:
        reduces["qkv"].done()
    if plan.joined:
        final.step()
        early.step()
        totals[...] = early.value()
        last_value = final.value()
        for row in range(2):
            at = row * len(everything)
            totals[at : at + 1, :] = last_value[row : row + 1, :]
        at = tops + len(everything)
        totals[at : at + 1, :] = last_value[9:10, :]
    if not plan.inside:
        for name, (lhs, rhs) in {
            "down": (grad, hidden),
            "up": (second, pre_grad),
            "out": (attn_grad, heads),
            "qkv": (first, nat),
        }.items():
            full = Reduce(mover, (wholes[name],) * 4, None, lhs, rhs)
            full.compute(wholes[name], 0)
    mover.settle()


def gather_outputs_kernel(layers, *refs):
    count = layers * len(NAMES)
    parts, token_grads, mixed, totals = refs[:count], refs[count], refs[count + 1], refs[count + 2]
    outs, work = refs[count + 3 : count + 17], refs[count + 17 : -2]
    into, out_of = refs[-2:]
    coming, going = [], []
    pairs = [(mixed, work[4], outs[4].at[0])]
    for index in range(len(NAMES)):
        for layer in range(layers):
            pairs.append(
                (parts[index * layers + layer], work[index].at[layer], outs[index].at[layer])
            )
    for i, (source, stage, _) in enumerate(pairs):
        coming.append(pltpu.make_async_copy(source, stage, into.at[i]))
        coming[-1].start()
    outs[5][0] = token_grads[...].astype(FULL)
    for row, out in enumerate(outs[6:12]):
        out[...] = totals[row * layers : (row + 1) * layers, 0 : out.shape[1]]
    for row, out in enumerate(outs[12:14]):
        row = row + 8
        out[...] = totals[row * layers : (row + 1) * layers, 0 : out.shape[1]]
    for i, (_, stage, target) in enumerate(pairs):
        coming[i].wait()
        going.append(pltpu.make_async_copy(stage, target, out_of.at[i]))
        going[-1].start()
    for copy in going:
        copy.wait()


def gather_outputs(done, token_grads, mixed, totals, layers, widths):
    rows, width = token_grads.shape
    parts = [done[name, layer] for name in NAMES for layer in range(layers)]
    hbm, whole = pl.BlockSpec(memory_space=HBM), lambda shape: pl.BlockSpec(
        shape, lambda i: (0,) * len(shape)
    )
    shapes = [(layers,) + done[name, 0].shape for name in NAMES] + [(1, rows, width)] * 2
    types = [FULL] * 4 + [LOW, FULL]
    small = [(layers, width)] * 6 + [(layers, count) for count in widths]
    copies = len(parts) + 1
    return pl.pallas_call(
        functools.partial(gather_outputs_kernel, layers),
        grid=(1,),
        in_specs=[hbm] * len(parts) + [whole(token_grads.shape), hbm, whole(totals.shape)],
        out_specs=[hbm] * 5 + [whole(shape) for shape in shapes[5:] + small],
        out_shape=[jax.ShapeDtypeStruct(*pair) for pair in zip(shapes, types)]
        + [jax.ShapeDtypeStruct(shape, FULL) for shape in small],
        scratch_shapes=[VMEM(shape, FULL) for shape in shapes[:4]]
        + [VMEM((rows, width), LOW)]
        + [pltpu.SemaphoreType.DMA((copies,)), pltpu.SemaphoreType.DMA((copies,))],
        compiler_params=pltpu.CompilerParams(vmem_limit_bytes=60 * 2**20),
        name="gather_outputs",
    )(*parts, token_grads, mixed, totals)


class BackPlan:
    def __init__(self, layer, layers, inside):
        self.inside, self.layer = inside, layer
        self.last, self.final = layer == layers - 1, layer == 0
        self.late = inside and not self.last
        self.joined = inside and self.final
        self.others = layers - 1 if self.joined else 0


def back_layer(source, x, live, gain2, gain1, saved, late, others, plan, size, sizes, ident):
    rows, width = source.shape
    count = sizes[0]
    slope, w_down, w_up = saved[:3]
    hidden, joint, attn = slope.shape[1], saved[12].shape[1], saved[6].shape[1]
    slots, span = count * rows, rows // 4
    tile = 512 if slots % 512 == 0 else PAD
    wide = max(width, hidden, joint)
    half = width // 2
    block = half // count
    columns = {"qkv": joint, "out": attn, "up": hidden, "down": hidden}
    inputs = [(source, VMEM)] + ([] if plan.last else [(x, VMEM)])
    inputs += [(live, SMEM), (gain2, HBM), (gain1, HBM)]
    inputs += [(value, HBM) for value in saved]
    if plan.late:
        inputs.append((late, HBM))
    for pair in others[: plan.others]:
        inputs += [(value, VMEM) for value in pair]
    outputs = [((span, width), FULL, VMEM), ((rows, width), LOW, VMEM)]
    names = [name for name in NAMES if plan.inside and (name != "qkv" or plan.final)]
    outputs += [((block, columns[name]), FULL, VMEM) for name in names]
    if plan.inside and not plan.final:
        outputs.append(((half, joint), LOW, HBM))
    if plan.late:
        outputs.append(((block, joint), FULL, VMEM))
    depth = 8 * (plan.others + 1)
    if plan.joined:
        outputs.append(((depth + 8, wide), FULL, VMEM))
    else:
        outputs += [((8, wide), FULL, VMEM)] * 2
    if not plan.inside:
        outputs += [((width, columns[name]), LOW, VMEM) for name in NAMES]
    scratch = [VMEM(value.shape, value.dtype) for value in saved]
    scratch[13] = VMEM((span, width), saved[13].dtype)
    if plan.last:
        scratch.append(VMEM((rows, width), LOW))
    scratch += [
        VMEM((rows, hidden), LOW),
        VMEM((rows, width), LOW),
        VMEM((attn, rows), LOW),
        VMEM((joint, rows), LOW),
        VMEM((rows, joint), LOW),
    ]
    scratch += attend_back_buffers(size, count, rows)
    scratch += round_buffers(rows, width) + round_buffers(rows, width)
    if plan.inside:
        for name in ("down", "up", "out", "qkv"):
            scratch += reduce_buffers(half, columns[name], count)
    if plan.late:
        scratch += [VMEM((half, joint), LOW), VMEM((count - 1, block, joint), LOW)]
    scratch.append(VMEM((16, slots), LOW))
    scratch += [VMEM(value.shape, value.dtype) for value in (gain2, gain1)]
    assert 2 * (plan.others + 1) <= 8
    if plan.joined:
        scratch += [VMEM((8, wide), FULL)] * 2
        scratch += [
            VMEM((6, depth + 8, wide), FULL),
            VMEM((5, depth + 8, wide), FULL),
            VMEM((6, 16, wide), FULL),
            VMEM((5, 16, wide), FULL),
        ]
    results = run(
        functools.partial(back_kernel, plan, size, tile),
        "back_layer",
        ident,
        inputs,
        outputs,
        scratch,
        3 * (count - 1) + 2 * ROUND_COPIES + 8 * count + 10 + count,
        len(saved) + 4,
        sizes,
        58,
        6 * rows * width * (2 * hidden + attn + joint) + 10 * slots * slots * 256,
    )
    return results[:2], names, results[2:]


def shards(
    tokens,
    block_tokens,
    ln1_gain,
    ln1_bias,
    w_qkv,
    b_qv,
    w_out,
    b_out,
    ln2_gain,
    ln2_bias,
    w_up,
    b_up,
    w_down,
    b_down,
    cotangent,
):
    images, capacity, width = tokens.shape
    assert images == 1
    layers = w_qkv.shape[0]
    size = HEAD_DIM
    ctx_count = lax.axis_size("ctx")
    ctx_place = lax.axis_index("ctx")
    joint_width = w_qkv.shape[2]
    heads = joint_width // (3 * size)
    assert heads == ctx_count
    attn_width = heads * size
    hidden_width = w_up.shape[2]
    weights = {"qkv": w_qkv, "out": w_out, "up": w_up, "down": w_down}
    sizes = (ctx_count, lax.axis_size("shard"))
    inside = sizes == (4, 2)
    gathered = {}
    if not inside:
        for name, value in weights.items():
            for layer in range(layers):
                gathered[name, layer] = gather_weight(value[layer])[0]
    source, stream = tokens[0], None
    saved = []
    for layer in range(layers):
        last = layer == layers - 1
        result, following, kept = forward_layer(
            source,
            stream,
            block_tokens,
            (b_out, ln2_gain, ln2_bias, b_down, ln1_gain, ln1_bias, b_up, b_qv),
            gathered,
            weights,
            Plan(layer, last, inside),
            last,
            size,
            sizes,
            1 + layer,
        )
        before = stream if layer else source
        first = source if layer else kept[8]
        saved.append((before, first) + tuple(kept[:8]))
        source, stream = following, result
    mixed = source

    done, packs = {}, {}
    source, stream, late = cotangent[0], None, None
    for layer in reversed(range(layers)):
        before, first, qkv, head_out, lse, heads_low, middle, second, hidden, slope = saved[layer]
        plan = BackPlan(layer, layers, inside)
        whole = {name: gathered[name, layer] for name in NAMES}
        near = [slope, whole["down"], whole["up"], middle, hidden, second, whole["out"]]
        near += [heads_low, qkv, head_out, lse, first, whole["qkv"], before]
        others = [packs[key] for key in sorted(packs)]
        (stream, source), names, rest = back_layer(
            source, stream, block_tokens, ln2_gain, ln1_gain, near, late, others, plan, size, sizes, 1 + layers + layer
        )
        rest = iter(rest)
        for name in names:
            done[name, layer] = next(rest)
        if plan.inside and not plan.final:
            late = next(rest)
        if plan.late:
            done["qkv", layer + 1] = next(rest)
        if plan.joined:
            totals = next(rest)
        else:
            packs[layer] = (next(rest), next(rest))
        if not inside:
            for name in NAMES:
                value = next(rest)
                done[name, layer] = scatter_weight(
                    lambda start, count, value=value: rows_of(value, start, count).astype(FULL),
                    width,
                )
    if not inside:
        split = total_over(("tp",), jnp.stack([packs[l][0] for l in range(layers)], axis=1))
        local = jnp.stack([packs[l][1] for l in range(layers)], axis=1)
        totals = total_over(("shard", "ctx"), jnp.concatenate([split, local[:2]]))
        totals = totals.reshape(10 * layers, -1)
    pairs = b_qv.shape[1]
    outs = gather_outputs(done, source, mixed, totals, layers, (hidden_width, pairs))
    g_qkv, g_out, g_up, g_down, mixed, token_grads = outs[:6]
    g_ln1_gain, g_ln1_bias, g_ln2_gain, g_ln2_bias, g_b_out, g_b_down, g_b_up, g_b_qv = outs[6:]
    return (
        mixed,
        token_grads,
        g_ln1_gain,
        g_ln1_bias,
        g_qkv,
        g_b_qv,
        g_out,
        g_b_out,
        g_ln2_gain,
        g_ln2_bias,
        g_up,
        g_b_up,
        g_down,
        g_b_down,
    )


def solution(mesh):
    split_rows = P(None, ("shard", "ctx"), "tp")
    split_tokens = P("shard", "ctx", None)
    return jax.shard_map(
        shards,
        mesh=mesh,
        in_specs=(
            split_tokens,
            P("shard", None),
            P(),
            P(),
            split_rows,
            P(None, "tp"),
            split_rows,
            P(),
            P(),
            P(),
            split_rows,
            P(None, "tp"),
            split_rows,
            P(),
            split_tokens,
        ),
        out_specs=(
            split_tokens,
            split_tokens,
            P(),
            P(),
            split_rows,
            P(None, "tp"),
            split_rows,
            P(),
            P(),
            P(),
            split_rows,
            P(None, "tp"),
            split_rows,
            P(),
        ),
        check_vma=False,
    )
```

```python
import functools
import math

import jax
import jax.numpy as jnp
from jax import lax
from jax.experimental import pallas as pl
from jax.experimental.pallas import tpu as pltpu
from jax.sharding import PartitionSpec as P

HEAD_DIM = 64
EPSILON = 1e-06
NEG_LARGE = -1e30
LOW = jnp.bfloat16
FULL = jnp.float32
PAD = 128
MESH = pl.DeviceIdType.MESH
VMEM = pltpu.VMEM
HBM = pltpu.HBM
SMEM = pltpu.SMEM


def bits_of(axis):
    size = lax.axis_size(axis)
    assert size & (size - 1) == 0
    return [1 << i for i in range(size.bit_length() - 1)]


def swap(value, axis, bit):
    size = lax.axis_size(axis)
    return lax.ppermute(value, axis, [(i, i ^ bit) for i in range(size)])


def side_of(axis, bit):
    return (lax.axis_index(axis) // bit) % 2


def rows_of(value, start, count, axis=0):
    return lax.dynamic_slice_in_dim(value, start, count, axis)


def halve(axis, bits, partial, total):
    offset, span, received = jnp.int32(0), total, []

    def summed(start, count):
        value = partial(start, count)
        for got, base in received:
            value = value + rows_of(got, start - base, count).astype(FULL)
        return value

    for bit in bits:
        half = span // 2
        side = side_of(axis, bit)
        got = swap(summed(offset + (1 - side) * half, half).astype(LOW), axis, bit)
        offset = offset + side * half
        received.append((got, offset))
        span = half
    return summed(offset, span)


def double(axis, bits, value):
    for bit in bits:
        got = swap(value, axis, bit)
        first = side_of(axis, bit) == 0
        value = jnp.concatenate(
            [jnp.where(first, value, got), jnp.where(first, got, value)], axis=0
        )
    return value


def total_over(axes, value):
    for axis in axes:
        for bit in bits_of(axis):
            value = value + swap(value, axis, bit)
    return value


def ring(value, by):
    count = lax.axis_size("ctx")
    return lax.ppermute(value, "ctx", [(i, (i + by) % count) for i in range(count)])


def gather_weight(piece):
    count = lax.axis_size("ctx")
    place = lax.axis_index("ctx")
    ways = lax.axis_size("shard")
    blocks = [piece] + [ring(piece, by) for by in range(1, count)]
    whole = jnp.zeros((ways * count,) + piece.shape, piece.dtype)
    me = lax.axis_index("shard")
    for by, block in enumerate(blocks):
        at = (place - by) % count
        held = [(jnp.int32(0), block)]
        for bit in bits_of("shard"):
            held = held + [(other ^ bit, swap(value, "shard", bit)) for other, value in held]
        for other, value in held:
            whole = lax.dynamic_update_index_in_dim(whole, value, (me ^ other) * count + at, 0)
    return whole.reshape((ways * count * piece.shape[0],) + piece.shape[1:]), blocks[-1]


def scatter_weight(partial, total):
    count = lax.axis_size("ctx")
    place = lax.axis_index("ctx")
    mine = halve("shard", bits_of("shard")[::-1], partial, total).astype(LOW)
    mine = mine.reshape((count, mine.shape[0] // count) + mine.shape[1:])
    value = lax.dynamic_index_in_dim(mine, place, 0, False).astype(FULL)
    for by in range(1, count):
        given = lax.dynamic_index_in_dim(mine, (place + by) % count, 0, False)
        value = value + ring(given, by).astype(FULL)
    return value


def dot(left, right, contract):
    return lax.dot_general(
        left, right, ((contract[0], contract[1]), ((), ())), preferred_element_type=FULL
    )


def turned(value):
    return value.astype(FULL).T.astype(LOW)


def normalize(rows, gain, shift):
    row_mean = jnp.mean(rows, axis=-1, keepdims=True)
    centred = rows - row_mean
    inverse = lax.rsqrt(jnp.mean(centred * centred, axis=-1, keepdims=True) + EPSILON)
    normed = centred * inverse
    return (normed * gain + shift, normed, inverse)


def normalize_back(grad_out, normed, inverse, gain):
    scaled = grad_out * gain
    mean_grad = jnp.mean(scaled, axis=-1, keepdims=True)
    mean_cross = jnp.mean(scaled * normed, axis=-1, keepdims=True)
    return inverse * (scaled - mean_grad - normed * mean_cross)


def gelu_pair(value):
    spread = 0.5 * (1.0 + lax.erf(value * (0.5**0.5)))
    slope = spread + value * jnp.exp(-0.5 * value * value) * (1.0 / math.sqrt(2.0 * math.pi))
    return (value * spread).astype(LOW), slope.astype(LOW)


class Mover:
    def __init__(self, sizes, send, recv, local):
        self.ctx_count, self.shard_count = sizes
        self.send, self.recv, self.local = send, recv, local
        self.copies, self.here = [], []
        self.arrived = set()
        self.landed = set()
        self.ctx = lax.axis_index("ctx")
        self.shard = lax.axis_index("shard")

    def go(self, source, target, **device):
        index = len(self.copies)
        assert index < self.send.shape[0]
        copy = pltpu.make_async_remote_copy(
            src_ref=source,
            dst_ref=target,
            send_sem=self.send.at[index],
            recv_sem=self.recv.at[index],
            device_id=device,
            device_id_type=MESH,
        )
        copy.start()
        self.copies.append(copy)
        return index

    def stay(self, source, target):
        index = len(self.here)
        assert index < self.local.shape[0]
        copy = pltpu.make_async_copy(source, target, self.local.at[index])
        copy.start()
        self.here.append(copy)
        return index

    def near(self, *indices):
        for index in indices:
            if index not in self.landed:
                self.landed.add(index)
                self.here[index].wait()

    def take(self, index):
        if index not in self.arrived:
            self.arrived.add(index)
            self.copies[index].wait_recv()

    def flip(self, bits):
        place = self.ctx
        if bits & 1:
            place = place + 1 - 2 * lax.rem(self.ctx, 2)
        if bits & 2:
            place = place + 2 - 4 * (self.ctx // 2)
        return place

    def on(self, by):
        return lax.rem(self.ctx + by, self.ctx_count)

    def back(self, by):
        return lax.rem(self.ctx + self.ctx_count - by, self.ctx_count)

    def settle(self):
        for index, copy in enumerate(self.copies):
            self.take(index)
            copy.wait_send()
        self.near(*range(len(self.here)))


class Gather:
    def __init__(self, mover, source, target, across=True):
        self.mover, self.source, self.target, self.across = mover, source, target, across
        self.over = []

    def start_line(self):
        mover = self.mover
        mine, there = self.source, self.block(mover.ctx)
        self.far = mover.go(mine, there, ctx=mover.flip(2))
        self.close = mover.go(mine, there, ctx=mover.flip(1))

    def start_over(self):
        mover = self.mover
        mine, there = self.source, self.block(mover.ctx)
        if self.across:
            self.over.append(mover.go(mine, there, shard=1 - mover.shard))
        self.own = mover.stay(mine, there)

    def block(self, ctx):
        mover = self.mover
        rows = self.source.shape[0]
        start = ctx * rows
        if self.across:
            start = start + mover.shard * mover.ctx_count * rows
        return self.target.at[pl.ds(pl.multiple_of(start, rows), rows)]

    def pass_on(self, stage):
        mover = self.mover
        if stage == 1:
            mover.take(self.far)
            rows = self.block(mover.flip(2))
            self.passed = mover.go(rows, rows, ctx=mover.flip(1))
        elif stage == 2:
            mover.take(self.close)
            rows = self.block(mover.flip(1))
        else:
            mover.take(self.passed)
            rows = self.block(mover.flip(3))
        if self.across:
            self.over.append(mover.go(rows, rows, shard=1 - mover.shard))

    def have(self):
        for copy in self.over:
            self.mover.take(copy)
        self.mover.near(self.own)


class Across:
    def __init__(self, mover, source, target):
        rows = source.shape[0]
        there = target.at[pl.ds(pl.multiple_of(mover.shard * rows, rows), rows)]
        self.mover = mover
        self.copy = mover.go(source, there, shard=1 - mover.shard)
        self.own = mover.stay(source, there)

    def have(self):
        self.mover.take(self.copy)
        self.mover.near(self.own)


class Reduce:
    def __init__(self, mover, buffers, out, lhs, rhs):
        self.mover, self.out, self.lhs, self.rhs = mover, out, lhs, rhs
        self.give, self.got, self.mid, self.line = buffers
        self.half = self.give.shape[0]
        self.block = self.half // mover.ctx_count

    def compute(self, target, shard):
        chunk = min(256, self.half)

        def step(i, carry):
            at = pl.ds(pl.multiple_of(shard * self.half + i * chunk, chunk), chunk)
            here = pl.ds(pl.multiple_of(i * chunk, chunk), chunk)
            target[here, :] = dot(self.lhs[:, at], self.rhs[...], ((0,), (0,))).astype(LOW)
            return carry

        lax.fori_loop(0, self.half // chunk, step, 0)

    def begin_blocks(self):
        mover = self.mover
        self.blocks = {}
        for bits in (3, 2, 1, 0):
            ctx = mover.flip(bits)
            at = pl.ds(pl.multiple_of(ctx * self.block, self.block), self.block)
            start = pl.multiple_of((1 - mover.shard) * self.half + ctx * self.block, self.block)
            lhs = self.lhs[:, pl.ds(start, self.block)]
            self.give[at, :] = dot(lhs, self.rhs[...], ((0,), (0,))).astype(LOW)
            self.blocks[bits] = mover.go(
                self.give.at[at], self.got.at[at], shard=1 - mover.shard
            )

    def own(self):
        self.compute(self.mid, self.mover.shard)

    def fold_blocks(self, *which):
        mover = self.mover
        for bits in which:
            mover.take(self.blocks[bits])
            ctx = mover.flip(bits)
            at = pl.ds(pl.multiple_of(ctx * self.block, self.block), self.block)
            self.mid[at, :] = (
                self.mid[at, :].astype(FULL) + self.got[at, :].astype(FULL)
            ).astype(LOW)

    def rows(self, ctx):
        return self.mid.at[pl.ds(pl.multiple_of(ctx * self.block, self.block), self.block)]

    def send_first(self):
        mover = self.mover
        self.first = mover.go(self.rows(mover.flip(3)), self.line.at[1], ctx=mover.flip(1))

    def send_second(self):
        mover = self.mover
        self.second = mover.go(self.rows(mover.flip(1)), self.line.at[0], ctx=mover.flip(1))

    def send_third(self):
        mover = self.mover
        mover.take(self.first)
        rows = self.rows(mover.flip(2))
        rows[...] = (rows[...].astype(FULL) + self.line[1].astype(FULL)).astype(LOW)
        self.third = mover.go(rows, self.line.at[2], ctx=mover.flip(2))

    def done(self):
        self.mover.take(self.second)
        self.mover.take(self.third)
        value = self.rows(self.mover.ctx)[...].astype(FULL)
        self.out[...] = value + self.line[0].astype(FULL) + self.line[2].astype(FULL)


def reduce_buffers(half, width, count):
    return [
        VMEM((half, width), LOW),
        VMEM((half, width), LOW),
        VMEM((half, width), LOW),
        VMEM((count - 1, half // count, width), LOW),
    ]


def greet(mover, shard):
    barrier = pltpu.get_barrier_semaphore()
    peers = [dict(ctx=mover.on(by)) for by in range(1, mover.ctx_count)]
    peers += [dict(tp=peer) for peer in tp_peers()]
    if shard:
        peers.append(dict(shard=1 - mover.shard))
    for peer in peers:
        pl.semaphore_signal(barrier, inc=1, device_id=peer, device_id_type=MESH)
    pl.semaphore_wait(barrier, len(peers))


def tp_peers():
    place = lax.axis_index("tp")
    core, far = lax.rem(place, 2), place // 2
    return place + 1 - 2 * core, place + 2 - 4 * far


def run(kernel, name, ident, inputs, outputs, scratch, remote, local, sizes, vmem, flops):
    n_in, n_out, n_scratch = len(inputs), len(outputs), len(scratch)

    def body(*refs):
        ins, outs = refs[:n_in], refs[n_in : n_in + n_out]
        work = refs[n_in + n_out :]
        mover = Mover(sizes, *work[n_scratch:])
        kernel(mover, ins, outs, work[:n_scratch])

    return pl.pallas_call(
        body,
        in_specs=[pl.BlockSpec(memory_space=space) for _, space in inputs],
        out_specs=[pl.BlockSpec(memory_space=space) for _, _, space in outputs],
        out_shape=[jax.ShapeDtypeStruct(shape, dtype) for shape, dtype, _ in outputs],
        scratch_shapes=list(scratch)
        + [
            pltpu.SemaphoreType.DMA((remote,)),
            pltpu.SemaphoreType.DMA((remote,)),
            pltpu.SemaphoreType.DMA((local,)),
        ],
        compiler_params=pltpu.CompilerParams(
            collective_id=ident, has_side_effects=True, vmem_limit_bytes=vmem * 2**20
        ),
        cost_estimate=pl.CostEstimate(flops=flops, bytes_accessed=2**24, transcendentals=0),
        name=name,
    )(*[value for value, _ in inputs])


def order_of(block, count):
    return (block + count - 1) % count


def tiles_of(count, capacity, tile):
    ends = [-(-(p + 1) * capacity // tile) for p in range(count)]
    return list(zip([0] + ends[:-1], ends))


def tile_at(t, tile):
    return pl.ds(pl.multiple_of(t * tile, tile), tile)


def turned_product(left, right, bias, target):
    value = jnp.dot(left[...], right[...], preferred_element_type=FULL)
    if bias is not None:
        value = value + bias[0:1, :]
    target[...] = turned(value.astype(LOW))


def head_rows(ref, head, width):
    return ref.at[pl.ds(pl.multiple_of(head * width, 16), width)]


def attend_part(size, tile, mover, joint, bias, heads, qkv, o_ref, lse, work, after_send, begun, between):
    k_ref, q_ref, v_ref, low_ref, score_ref, top_ref = work
    count, width, capacity = qkv.shape
    slots = count * capacity
    sent = [None] + [
        mover.go(head_rows(joint, mover.on(by), width), qkv.at[by], ctx=mover.on(by))
        for by in range(1, count)
    ]
    after_send()
    qkv[0] = head_rows(joint, mover.ctx, width)[...]
    q_ref[size:PAD, :] = jnp.concatenate(
        [jnp.ones((16, slots), LOW), jnp.zeros((PAD - size - 16, slots), LOW)], axis=0
    )

    v_ref[size : size + 16, :] = jnp.ones((16, slots), LOW)

    def prepare(r):
        here = slice(r * capacity, (r + 1) * capacity)
        p = order_of(r, count)
        q_ref[0:size, p * capacity : (p + 1) * capacity] = (
            qkv[r, 0:size, :] * (size**-0.5)
        ).astype(LOW)
        v_ref[0:size, here] = qkv[r, 2 * size : 3 * size, :]
        keys = jnp.concatenate(
            [qkv[r, size : 2 * size, :], bias[:, here], jnp.zeros((PAD - size - 16, capacity), LOW)],
            axis=0,
        )
        k_ref[here, :] = turned(keys)

    prepare(0)
    for by in range(1, count):
        mover.take(sent[by])
        prepare(by)

    begun()
    last = slots // tile - 1
    assert last % 2 == 1

    def phase(t, now, following, then):
        at, ahead = tile_at(t, tile), tile_at(following, tile)
        top = top_ref[now, 0:1, :]
        summed = jnp.zeros((size + 16, tile), FULL)
        new_top = jnp.full((1, tile), NEG_LARGE, FULL)
        for r in range(count):
            here = slice(r * capacity, (r + 1) * capacity)
            scores = jnp.dot(k_ref[here, :], q_ref[:, ahead], preferred_element_type=FULL)
            score_ref[then, here, :] = scores
            new_top = jnp.maximum(new_top, jnp.max(scores, axis=0, keepdims=True))
            weights = jnp.exp(score_ref[now, here, :] - top)
            summed = summed + jnp.dot(
                v_ref[:, here], weights.astype(LOW), preferred_element_type=FULL
            )
        top_ref[then] = jnp.broadcast_to(new_top, (8, tile))
        total = summed[size : size + 1]
        out = summed[0:size] / total
        o_ref[:, at] = out
        low_ref[:, at] = out.astype(LOW)
        lse[:, at] = jnp.broadcast_to(top + jnp.log(total), (8, tile))

    def step(i, carry):
        phase(2 * i, 0, 2 * i + 1, 1)
        phase(2 * i + 1, 1, jnp.minimum(2 * i + 2, last), 0)
        return carry

    scores = jnp.dot(k_ref[...], q_ref[:, 0:tile], preferred_element_type=FULL)
    score_ref[0] = scores
    top_ref[0] = jnp.broadcast_to(jnp.max(scores, axis=0, keepdims=True), (8, tile))
    arriving = []
    for p, (low, high) in enumerate(tiles_of(count, capacity, 2 * tile)):
        lax.fori_loop(low, high, step, 0)
        done = low_ref.at[:, p * capacity : (p + 1) * capacity]
        if p < count - 1:
            there = head_rows(heads, mover.ctx, size)
            arriving.append(mover.go(done, there, ctx=mover.back(p + 1)))
        else:
            head_rows(heads, mover.ctx, size)[...] = low_ref[:, p * capacity : (p + 1) * capacity]
        between(p + 1)
    for copy in arriving:
        mover.take(copy)


def below(row, ones):
    width = row.shape[1]
    high = row.astype(LOW).astype(FULL)
    middle = (row - high).astype(LOW).astype(FULL)
    low = row - high - middle
    lead = jnp.full((1, width), 1.0 if ones else 0.0, FULL)
    rest = jnp.zeros((PAD // 2 - 4, width), FULL)
    return jnp.concatenate([lead, high, middle, low, rest], axis=0).astype(LOW)


def attend_back_part(size, tile, mover, parts, bias, qkv, o_ref, lse, grads, work, ready, waiting, begun, between):
    k_ref, v_ref, q_ref, do_ref, nat_ref, dq_ref, dk_ref, dv_ref, got, back = work
    count, width, capacity = qkv.shape
    slots = count * capacity
    sent = [None] + [
        mover.go(head_rows(parts, mover.on(by), size), got.at[by], ctx=mover.on(by))
        for by in range(1, count)
    ]
    got[0] = head_rows(parts, mover.ctx, size)[...]
    waiting()
    ready()
    q_ref[size:PAD, :] = below(lse[0:1, :], True)
    dq_ref[...] = jnp.zeros_like(dq_ref)
    off = (lax.broadcasted_iota(jnp.int32, (16, capacity), 0) + 2) // 3
    taken = jnp.where(off == 1, -1.0, 0.0).astype(LOW)
    pad = jnp.zeros((PAD - size - 16, capacity), LOW)
    for r in range(count):
        here = slice(r * capacity, (r + 1) * capacity)
        k_ref[here, :] = turned(
            jnp.concatenate([qkv[r, size : 2 * size, :], bias[:, here] + taken, pad], axis=0)
        )
        v_ref[here, :] = turned(
            jnp.concatenate([qkv[r, 2 * size : 3 * size, :], taken, pad], axis=0)
        )
    for r in range(count):
        if r:
            mover.take(sent[r])
        p = order_of(r, count)
        at = slice(p * capacity, (p + 1) * capacity)
        scaled = (qkv[r, 0:size, :] * (size**-0.5)).astype(LOW)
        dout = got[r]
        q_ref[0:size, at] = scaled
        do_ref[0:size, at] = dout
        nat_ref[at, :] = turned(jnp.concatenate([scaled, dout], axis=0))
        delta = jnp.sum(dout.astype(FULL) * o_ref[:, at], axis=0, keepdims=True)
        do_ref[size:PAD, at] = below(delta, False)

    begun()
    tiles = tiles_of(count, capacity, tile)
    arriving = []
    mine = head_rows(grads, mover.ctx, width)
    for turn, r in enumerate(list(range(1, count)) + [0]):
        here = slice(r * capacity, (r + 1) * capacity)
        dk_ref[...] = jnp.zeros_like(dk_ref)
        dv_ref[...] = jnp.zeros_like(dv_ref)

        def step(t, carry, r=r, here=here):
            at = tile_at(t, tile)
            scores = jnp.dot(k_ref[here, :], q_ref[:, at], preferred_element_type=FULL)
            chance = jnp.exp(scores)
            chance_grad = jnp.dot(v_ref[here, :], do_ref[:, at], preferred_element_type=FULL)
            score_grad = (chance * chance_grad).astype(LOW)
            dq_ref[:, at] += jnp.dot(
                qkv[r, size : 2 * size, :], score_grad, preferred_element_type=FULL
            )
            dk_ref[...] += jnp.dot(score_grad, nat_ref[at, :], preferred_element_type=FULL)
            dv_ref[...] += jnp.dot(
                chance.astype(LOW), nat_ref[at, :], preferred_element_type=FULL
            )
            return carry

        if r:
            lax.fori_loop(0, tiles[-1][1], step, 0)
        else:
            for p, (low, high) in enumerate(tiles):
                lax.fori_loop(low, high, step, 0)
                at = slice(p * capacity, (p + 1) * capacity)
                value = (dq_ref[:, at] * (size**-0.5)).astype(LOW)
                if p < count - 1:
                    back[p + 1, 0:size, :] = value
                    arriving.append(
                        mover.go(
                            back.at[p + 1, 0:size], mine.at[0:size], ctx=mover.back(p + 1)
                        )
                    )
                else:
                    mine[0:size, :] = value
        keys = dk_ref[...].T[0:size].astype(LOW)
        values = dv_ref[...].T[size : 2 * size].astype(LOW)
        if r:
            back[r, size : 2 * size, :] = keys
            back[r, 2 * size : 3 * size, :] = values
            arriving.append(
                mover.go(
                    back.at[r, size : 3 * size], mine.at[size : 3 * size], ctx=mover.back(r)
                )
            )
        else:
            mine[size : 2 * size, :] = keys
            mine[2 * size : 3 * size, :] = values
        between(turn)
    for copy in arriving:
        mover.take(copy)


def attend_back_buffers(size, count, capacity):
    slots = count * capacity
    return [
        VMEM((slots, PAD), LOW),
        VMEM((slots, PAD), LOW),
        VMEM((PAD, slots), LOW),
        VMEM((PAD, slots), LOW),
        VMEM((slots, PAD), LOW),
        VMEM((size, slots), FULL),
        VMEM((capacity, PAD), FULL),
        VMEM((capacity, PAD), FULL),
        VMEM((count, size, capacity), LOW),
        VMEM((count, 3 * size, capacity), LOW),
    ]


class Round:
    def __init__(self, mover, rows, full, buffers):
        place = lax.axis_index("tp")
        core, far = lax.rem(place, 2), place // 2
        self.mover, self.full = mover, full
        self.give, self.ra, self.passing, self.rb, self.keep = buffers
        self.span = rows // 4
        self.half = self.span // 2
        self.mate, self.far = tp_peers()

        def quarter(c, f):
            return (c * 2 + f) * self.span

        self.own, self.other = quarter(core, far), quarter(core, 1 - far)
        self.mate_own, self.mate_other = quarter(1 - core, far), quarter(1 - core, 1 - far)

    def rows(self, start, count=None):
        return pl.ds(pl.multiple_of(start, 16), count or self.span)

    def hand(self, slot, value):
        self.give[slot] = value.astype(LOW)
        return self.mover.go(self.give.at[slot], self.ra.at[slot], tp=self.mate)

    def onward(self, value, index):
        self.mover.take(index)
        self.passing[...] = (value + self.ra[1].astype(FULL)).astype(LOW)
        return [
            self.mover.go(self.passing.at[at], self.rb.at[at], tp=self.far)
            for at in (pl.ds(0, self.half), pl.ds(self.half, self.half))
        ]

    def close(self, far_copies, index, finish, halfway=None):
        self.mover.take(index)
        self.keep[...] += self.ra[0].astype(FULL)
        self.to_far, self.to_mate = [], []
        for c in range(2):
            at = pl.ds(c * self.half, self.half)
            self.mover.take(far_copies[c])
            low = finish(at, self.keep[at] + self.rb[at].astype(FULL))
            mine = self.full.at[self.rows(self.own + c * self.half, self.half)]
            mine[...] = low
            self.to_far.append(self.mover.go(mine, mine, tp=self.far))
            self.to_mate.append(self.mover.go(mine, mine, tp=self.mate))
            if halfway and c == 0:
                halfway()

    def eager(self, make, finish, meanwhile=None, halfway=None):
        first = self.hand(1, make(self.mate_other))
        copies = self.onward(make(self.other), first)
        second = self.hand(0, make(self.mate_own))
        self.keep[...] = make(self.own)
        if meanwhile:
            meanwhile()
        self.close(copies, second, finish, halfway)

    def after(self, before, make, finish, meanwhile, between):
        before.have_mate_own()
        second = self.hand(0, make(self.mate_own))
        self.keep[...] = make(self.own)
        before.have_other()
        between()
        value = make(self.other)
        before.have_mate_other()
        first = self.hand(1, make(self.mate_other))
        copies = self.onward(value, first)
        meanwhile()
        self.close(copies, second, finish)

    def have_mate_own(self):
        for copy in self.to_mate:
            self.mover.take(copy)

    def have_other(self):
        self.passed = []
        for c in range(2):
            self.mover.take(self.to_far[c])
            rows = self.full.at[self.rows(self.other + c * self.half, self.half)]
            self.passed.append(self.mover.go(rows, rows, tp=self.mate))

    def have_mate_other(self):
        for copy in self.passed:
            self.mover.take(copy)

    def have(self):
        self.have_mate_own()
        self.have_other()
        self.have_mate_other()


ROUND_COPIES = 10


def round_buffers(rows, width):
    span = rows // 4
    return [
        VMEM((2, span, width), LOW),
        VMEM((2, span, width), LOW),
        VMEM((span, width), LOW),
        VMEM((span, width), LOW),
        VMEM((span, width), FULL),
    ]


NAMES = ("qkv", "out", "up", "down")


def layer_kernel(plan, last, size, tile, mover, ins, outs, work):
    ins, outs, work = iter(ins), iter(outs), iter(work)
    source = next(ins)
    x_ref = None if plan.entry else next(ins)
    live_ref = next(ins)
    far_params = [next(ins) for _ in range(8)]
    stream, following = next(outs), next(outs)
    far_qkv, far_o, far_lse, far_heads, far_middle, far_second, far_hidden, far_slope = [
        next(outs) for _ in range(8)
    ]
    far_first = next(outs) if plan.entry else None
    joint, nat, heads, qkv, o_ref, lse, middle, second, hidden, slope = [
        next(work) for _ in range(10)
    ]
    first = next(work) if plan.entry else source
    attend_work = [next(work) for _ in range(6)]
    one_work, two_work = [next(work) for _ in range(5)], [next(work) for _ in range(5)]
    rows = source.shape[0]
    bias, qkv_bias = next(work), next(work)
    params = [next(work) for _ in range(8)]
    whole = {name: next(work) for name in NAMES}
    gathers, loads = {}, {}
    for name in plan.held:
        loads[name] = (next(ins), whole[name])
    half_refs = {name: next(ins) for name in plan.halves}
    for name in plan.own:
        gathers[name, 0] = Gather(mover, next(ins).at[plan.layer], whole[name])
    kept_ahead = {name: next(outs) for name in plan.ahead + plan.lines}
    for name in plan.ahead + plan.lines:
        gathers[name, 1] = Gather(
            mover, next(ins).at[plan.layer + 1], next(work), name in plan.ahead
        )
    kept = {name: next(outs) for name in plan.kept}

    greet(mover, bool(gathers))
    halves = {name: Across(mover, half_refs[name], whole[name]) for name in plan.halves}
    if plan.entry:
        gathers_first = [key for key in [("qkv", 0)] if key in gathers]
        for key in gathers_first:
            gathers[key].start_line()
            gathers[key].start_over()
    param_loads = [mover.stay(there, here) for there, here in zip(far_params, params)]
    waiting_loads = dict(loads)
    loads = {}

    def load(names):
        for name in names:
            if name in waiting_loads and name not in loads:
                loads[name] = mover.stay(*waiting_loads[name])

    load(["qkv"])

    def have(name):
        if name in waiting_loads:
            mover.near(loads[name])
            load(NAMES)
        else:
            (halves[name] if name in halves else gathers[name, 0]).have()
            mover.stay(whole[name], kept[name])
        return whole[name]

    def begin(keys):
        for key in keys:
            if key in gathers:
                gathers[key].start_line()

    def begin_over(keys):
        for key in keys:
            if key in gathers:
                gathers[key].start_over()

    def pass_on(keys, stage):
        for key in keys:
            if key in gathers:
                gathers[key].pass_on(stage)

    def pass_all(keys):
        for stage in (1, 2, 3):
            pass_on(keys, stage)

    mover.near(*param_loads)
    layer, after = plan.layer, min(plan.layer + 1, params[0].shape[0] - 1)

    def row(index, layer=layer):
        return params[index][...].astype(FULL)[layer : layer + 1]

    b_out, gain2, shift2, b_down, b_up = row(0), row(1), row(2), row(3), row(6)
    gain1, shift1, gain0, shift0 = row(4, after), row(5, after), row(4), row(5)
    qkv_bias[...] = joint_bias(row(7), size, joint.shape[0])
    key_bias(mover, live_ref, bias)
    ahead, lines = [("qkv", 1)], [("out", 1), ("up", 1)]
    one = Round(mover, rows, second, one_work)
    two = Round(mover, rows, following, two_work)
    if plan.entry:
        chunk = rows // 5 if rows % 80 == 0 else rows

        def norm_step(i, carry):
            at = pl.ds(pl.multiple_of(i * chunk, 16), chunk)
            value = normalize(source[at, :].astype(FULL), gain0, shift0)[0]
            first[at, :] = value.astype(LOW)
            return carry

        lax.fori_loop(0, rows // chunk, norm_step, 0)
        mover.stay(first, far_first)
        pass_all([("qkv", 0)])
        begin([("out", 0), ("up", 0)])
        begin_over([("out", 0), ("up", 0), ("down", 0)] + ahead + lines)
        turned_product(first, have("qkv"), qkv_bias, joint)
    else:
        turned_product(first, have("qkv"), qkv_bias, joint)

    def after_send():
        if plan.entry:
            pass_all([("out", 0), ("up", 0)])
        else:
            for name in plan.own:
                gathers[name, 0].start_over()

    def begun():
        begin([("down", 0)])

    def between(p):
        if p > 2:
            pass_on([("down", 0)], p - 2)
        if p == 4:
            if not plan.entry:
                begin_over(ahead + lines)
            begin(ahead)

    attend_part(
        size, tile, mover, joint, bias, heads, qkv, o_ref, lse, attend_work, after_send, begun, between
    )
    nat[...] = turned(heads[...])
    w_out = have("out")

    def out_part(start):
        return dot(nat[one.rows(start), :], w_out[...], ((1,), (1,)))

    def to_second(at, value):
        if plan.entry:
            before = source[one.rows(one.own + at.start, at.size), :].astype(FULL)
        else:
            before = x_ref[at]
        value = before + value + b_out
        middle[at] = value
        return normalize(value, gain2, shift2)[0].astype(LOW)

    def meanwhile():
        mover.stay(qkv, far_qkv)
        mover.stay(o_ref, far_o)
        mover.stay(lse, far_lse)
        mover.stay(nat, far_heads)
        pass_on([("down", 0)], 3)

    one.eager(out_part, to_second, meanwhile, lambda: pass_on(ahead, 1))
    pass_on(ahead, 2)
    begin(lines)
    w_up, w_down = have("up"), have("down")

    def mlp_part(start):
        at = two.rows(start)
        pre = jnp.dot(second[at, :], w_up[...], preferred_element_type=FULL) + b_up
        low, low_slope = gelu_pair(pre)
        hidden[at, :] = low
        slope[at, :] = low_slope
        return dot(low, w_down[...], ((1,), (1,)))

    def to_following(at, value):
        value = middle[at] + value + b_down
        stream[at] = value
        if last:
            return live_rows(value, two.own + at.start, live_ref[0, mover.ctx]).astype(LOW)
        return normalize(value, gain1, shift1)[0].astype(LOW)

    def meanwhile():
        mover.stay(middle, far_middle)
        mover.stay(second, far_second)
        mover.stay(hidden, far_hidden)
        mover.stay(slope, far_slope)
        pass_on(lines, 1)

    two.after(one, mlp_part, to_following, meanwhile, lambda: pass_on(ahead, 3))
    two.have()
    pass_on(lines, 2)
    pass_on(lines, 3)
    for name in plan.ahead + plan.lines:
        gathers[name, 1].have()
        mover.stay(gathers[name, 1].target, kept_ahead[name])
    mover.settle()


class Plan:
    def __init__(self, layer, last, inside):
        self.layer, self.entry = layer, layer == 0
        self.own = (NAMES if layer == 0 else ("down",)) if inside else ()
        self.halves = ("out", "up") if inside and layer else ()
        self.ahead = ("qkv",) if inside and not last else ()
        self.lines = ("out", "up") if inside and not last else ()
        self.kept = self.own + self.halves
        self.held = tuple(name for name in NAMES if name not in self.kept)


def forward_layer(source, x, live, params, gathered, weights, plan, last, size, sizes, ident):
    rows, width = source.shape
    count = sizes[0]
    joint, hidden = weights["qkv"].shape[2], weights["up"].shape[2]
    heads = joint // (3 * size)
    attn, slots, span = heads * size, count * rows, rows // 4
    tile = 256 if slots % 256 == 0 else PAD
    columns = {"qkv": joint, "out": attn, "up": hidden, "down": hidden}
    inputs = [(source, VMEM)] + ([] if plan.entry else [(x, VMEM)])
    inputs += [(live, SMEM)] + [(value, HBM) for value in params]
    inputs += [(gathered[name, plan.layer], HBM) for name in plan.held]
    inputs += [(gathered[name, plan.layer, 0], HBM) for name in plan.halves]
    inputs += [(weights[name], HBM) for name in plan.own + plan.ahead + plan.lines]
    saved = [
        ((count, 3 * size, rows), LOW),
        ((size, slots), FULL),
        ((8, slots), FULL),
        ((rows, attn), LOW),
        ((span, width), FULL),
        ((rows, width), LOW),
        ((rows, hidden), LOW),
        ((rows, hidden), LOW),
    ]
    outputs = [((span, width), FULL, VMEM), ((rows, width), LOW, VMEM)]
    outputs += [(shape, dtype, HBM) for shape, dtype in saved]
    if plan.entry:
        outputs.append(((rows, width), LOW, HBM))
    ahead = [(width, columns[name]) for name in plan.ahead]
    ahead += [(width // 2, columns[name]) for name in plan.lines]
    outputs += [(shape, LOW, HBM) for shape in ahead]
    outputs += [((width, columns[name]), LOW, HBM) for name in plan.kept]
    qkv_shape, o_shape, lse_shape, heads_shape = saved[:4]
    scratch = [VMEM((joint, rows), LOW), VMEM((rows, attn), LOW), VMEM((attn, rows), LOW)]
    scratch += [VMEM(*pair) for pair in saved[:3] + saved[4:]]
    if plan.entry:
        scratch.append(VMEM((rows, width), LOW))
    scratch += [
        VMEM((slots, PAD), LOW),
        VMEM((PAD, slots), LOW),
        VMEM((size + 16, slots), LOW),
        VMEM((size, slots), LOW),
        VMEM((2, slots, tile), FULL),
        VMEM((2, 8, tile), FULL),
    ]
    scratch += round_buffers(rows, width) + round_buffers(rows, width)
    scratch += [VMEM((16, slots), LOW), VMEM((16, joint), FULL)]
    scratch += [VMEM(value.shape, value.dtype) for value in params]
    scratch += [VMEM((width, columns[name]), LOW) for name in NAMES]
    scratch += [VMEM(shape, LOW) for shape in ahead]
    results = run(
        functools.partial(layer_kernel, plan, last, size, tile),
        "forward_layer",
        ident,
        inputs,
        outputs,
        scratch,
        2 * (count - 1) + 2 * ROUND_COPIES + 2 * count * len(plan.kept + plan.ahead + plan.lines),
        10 + 2 * len(plan.kept + plan.ahead + plan.lines) + len(plan.held) + len(params),
        sizes,
        58,
        2 * rows * width * (2 * hidden + attn + joint) + 4 * slots * slots * 256,
    )
    stream, following = results[:2]
    kept = results[2 : 11 if plan.entry else 10]
    rest = iter(results[2 + len(kept) :])
    for name in plan.ahead:
        gathered[name, plan.layer + 1] = next(rest)
    for name in plan.lines:
        gathered[name, plan.layer + 1, 0] = next(rest)
    for name in plan.kept:
        gathered[name, plan.layer] = next(rest)
    return stream, following, kept


class SmallSums:
    def __init__(self, mover, rows, held, got, shared=None):
        self.mover, self.rows, self.held, self.got = mover, rows, held, got
        self.shared = shared or rows
        self.stage = 0
        mate, far = tp_peers()
        self.peers = [
            dict(tp=mate),
            dict(tp=far),
            dict(shard=1 - mover.shard),
            dict(ctx=mover.flip(2)),
            dict(ctx=mover.flip(1)),
        ]

    def part(self, stage):
        return pl.ds(0, self.rows if stage < 2 else self.held.shape[1])

    def step(self):
        stage, mover = self.stage, self.mover
        if stage:
            mover.take(self.copy)
            at = self.part(stage - 1)
            self.held[stage] = self.held[stage - 1]
            more = self.got[stage - 1, at, :]
            if stage < 3 and self.shared < self.rows:
                row = lax.broadcasted_iota(jnp.int32, more.shape, 0)
                more = jnp.where(row < self.shared, more, 0.0)
            self.held[stage, at, :] = self.held[stage - 1, at, :] + more
        if stage < len(self.peers):
            at = self.part(stage)
            self.copy = mover.go(
                self.held.at[stage, at], self.got.at[stage, at], **self.peers[stage]
            )
        self.stage = stage + 1

    def value(self):
        return self.held[len(self.peers)]


def key_bias(mover, live_ref, bias):
    capacity = bias.shape[1] // mover.ctx_count
    row = lax.broadcasted_iota(jnp.int32, (16, capacity), 0)
    slot = lax.broadcasted_iota(jnp.int32, (16, capacity), 1)
    for r in range(mover.ctx_count):
        live = live_ref[0, mover.back(r)]
        value = jnp.where((row == 0) & (slot >= live), NEG_LARGE, 0.0)
        bias[:, r * capacity : (r + 1) * capacity] = value.astype(LOW)


def pair_columns(rows, width, size, turn):
    shape = (width, rows) if turn else (rows, width)
    given = lax.broadcasted_iota(jnp.int32, shape, 1 if turn else 0)
    column = lax.broadcasted_iota(jnp.int32, shape, 0 if turn else 1)
    head, within = column // (3 * size), column % (3 * size)
    wanted = head * (2 * size) + jnp.where(within < size, within, within - size)
    key = (within >= size) & (within < 2 * size)
    return jnp.where((given == wanted) & ~key, 1.0, 0.0).astype(LOW)


def joint_bias(pair, size, width):
    rows = pair.shape[1]
    spread = jnp.broadcast_to(pair, (16, rows)).astype(LOW)
    return jnp.dot(spread, pair_columns(rows, width, size, False), preferred_element_type=FULL)


def live_rows(value, start, live):
    row = start + lax.broadcasted_iota(jnp.int32, value.shape, 0)
    return jnp.where(row < live, value, 0.0)


def sums_into(sums, first, at, values):
    for index, value in enumerate(values):
        row = first + index
        added = jnp.sum(value, axis=0, keepdims=True)
        width = added.shape[1]
        sums[row : row + 1, 0:width] = (
            added if at.start == 0 else sums[row : row + 1, 0:width] + added
        )


def back_kernel(plan, size, tile, mover, ins, outs, work):
    ins, outs, work = iter(ins), iter(outs), iter(work)
    source = next(ins)
    x_ref = None if plan.last else next(ins)
    live_ref, far_gain2, far_gain1 = [next(ins) for _ in range(3)]
    far = [next(ins) for _ in range(14)]
    late_far = next(ins) if plan.late else None
    others = [(next(ins), next(ins)) for _ in range(plan.others)]
    stream, following = next(outs), next(outs)
    grad_outs = {name: next(outs) for name in NAMES if plan.inside and (name != "qkv" or plan.final)}
    mid_out = next(outs) if plan.inside and not plan.final else None
    late_out = next(outs) if plan.late else None
    split = local = totals = None
    if plan.joined:
        totals = next(outs)
    else:
        split, local = next(outs), next(outs)
    wholes = {} if plan.inside else {name: next(outs) for name in NAMES}
    near = [next(work) for _ in range(14)]
    slope, w_down, w_up, middle, hidden, second, w_out, heads, qkv, o_ref, lse, first, w_qkv, before = near
    grad = next(work) if plan.last else source
    pre_grad, attn_grad, parts, grads, nat = [next(work) for _ in range(5)]
    attend_work = [next(work) for _ in range(10)]
    one_work, two_work = [next(work) for _ in range(5)], [next(work) for _ in range(5)]
    rows, width = source.shape
    reduces = {}
    if plan.inside:
        pairs = {
            "down": (grad, hidden),
            "up": (second, pre_grad),
            "out": (attn_grad, heads),
            "qkv": (first, nat),
        }
        for name in ("down", "up", "out", "qkv"):
            buffers = [next(work) for _ in range(4)]
            reduces[name] = Reduce(mover, buffers, grad_outs.get(name), *pairs[name])
    late = None
    if plan.late:
        late_mid, late_line = next(work), next(work)
        late = Reduce(mover, (late_mid, None, late_mid, late_line), late_out, None, None)
    bias, gain2_ref, gain1_ref = [next(work) for _ in range(3)]
    if plan.joined:
        split, local = next(work), next(work)
        early_held, early_got, late_held, late_got = [next(work) for _ in range(4)]
        tops = 8 * (plan.others + 1)
        early = SmallSums(mover, tops, early_held, early_got)
        final = SmallSums(mover, 8, late_held, late_got, 2)
        everything = [(split, local)] + others

    greet(mover, plan.inside)
    gain_loads = [mover.stay(far_gain2, gain2_ref), mover.stay(far_gain1, gain1_ref)]
    one = Round(mover, rows, attn_grad, one_work)
    two = Round(mover, rows, following, two_work)
    if plan.final:
        far[13] = far[13].at[two.rows(two.own)]
    load = {index: mover.stay(far[index], near[index]) for index in (0, 1, 2)}
    late_load = mover.stay(late_far, late_mid) if late else None
    if plan.last:
        chunk = rows // 5 if rows % 80 == 0 else rows

        def mask_step(i, carry):
            at = pl.ds(pl.multiple_of(i * chunk, 16), chunk)
            value = source[at, :].astype(FULL)
            grad[at, :] = live_rows(value, i * chunk, live_ref[0, mover.ctx]).astype(LOW)
            return carry

        lax.fori_loop(0, rows // chunk, mask_step, 0)
    key_bias(mover, live_ref, bias)
    mover.near(*gain_loads)
    gain2, gain1 = [
        ref[...].astype(FULL)[plan.layer : plan.layer + 1] for ref in (gain2_ref, gain1_ref)
    ]
    split[...] = jnp.zeros_like(split)
    local[...] = jnp.zeros_like(local)
    split[5:6, 0:width] = jnp.sum(
        grad[one.rows(one.own), :].astype(FULL), axis=0, keepdims=True
    )
    hidden_width = slope.shape[1]

    def mlp_part(start):
        at = one.rows(start)
        pre = jnp.dot(grad[at, :], w_down[...], preferred_element_type=FULL)
        low = (pre * slope[at, :].astype(FULL)).astype(LOW)
        pre_grad[at, :] = low
        local[0:1, 0:hidden_width] += jnp.sum(low.astype(FULL), axis=0, keepdims=True)
        return dot(low, w_up[...], ((1,), (1,)))

    def to_attn(at, value):
        if plan.last:
            above = grad[one.rows(one.own + at.start, at.size), :].astype(FULL)
        else:
            above = x_ref[at]
        _, normed, inverse = normalize(middle[at], 1.0, 0.0)
        result = above + normalize_back(value, normed, inverse, gain2)
        stream[at] = result
        low = result.astype(LOW)
        sums_into(split, 2, at, (value * normed, value, low.astype(FULL)))
        return low

    def reduce(name):
        if name in reduces:
            reduces[name].begin_blocks()

    def own(name):
        if name in reduces:
            reduces[name].own()

    def first_step(name):
        if name in reduces:
            reduces[name].fold_blocks(3)
            reduces[name].send_first()

    def second_step(name):
        if name in reduces:
            reduces[name].fold_blocks(2)
            reduces[name].send_third()

    def rest(name):
        if name in reduces:
            reduces[name].fold_blocks(1)
            reduces[name].send_second()
            reduces[name].fold_blocks(0)

    def begin_early():
        if plan.joined:
            early_held[0] = jnp.zeros(early_held.shape[1:], FULL)
            for layer, (some, more) in enumerate(everything):
                first_row = 0 if layer else 2
                for row in range(first_row, 6):
                    at = row * len(everything) + layer
                    early_held[0, at : at + 1, :] = some[row : row + 1, :]
                for row in range(2 if layer else 1):
                    at = tops + row * len(everything) + layer
                    early_held[0, at : at + 1, :] = more[row : row + 1, :]

    def early_step():
        if plan.joined:
            early.step()

    def start_down():
        mover.near(load[3], load[4])
        reduce("down")
        if late:
            late.send_third()

    if late:
        mover.near(late_load)
        late.send_first()
        late.send_second()
    mover.near(load[0], load[1], load[2])
    for index in range(3, len(far)):
        load[index] = mover.stay(far[index], near[index])
    one.eager(mlp_part, to_attn, start_down)
    mover.near(load[5])
    reduce("up")
    one.have()
    mover.near(load[6])
    turned_product(attn_grad, w_out, None, parts)

    def waiting():
        begin_early()
        early_step()
        own("down")
        first_step("down")
        mover.near(load[7])
        reduce("out")
        own("out")

    def ready():
        own("up")
        mover.near(load[8], load[9], load[10])

    def between(turn):
        if turn == 0:
            early_step()
        if turn == 3:
            second_step("down")
            first_step("up")
            rest("down")

    attend_back_part(
        size,
        tile,
        mover,
        parts,
        bias,
        qkv,
        o_ref,
        lse,
        grads,
        attend_work,
        ready,
        waiting,
        lambda: None,
        between,
    )
    early_step()
    nat[...] = turned(grads[...])
    pairs_width = nat.shape[1] // 3 * 2
    picked = jnp.dot(
        nat[...], pair_columns(pairs_width, nat.shape[1], size, True), preferred_element_type=FULL
    )
    local[1:2, 0:pairs_width] = jnp.sum(picked, axis=0, keepdims=True)
    mover.near(*[load[index] for index in range(11, len(far))])

    def qkv_part(start):
        return dot(nat[two.rows(start), :], w_qkv[...], ((1,), (1,)))

    def to_following(at, value):
        row = before[at, :].astype(FULL)
        _, normed, inverse = normalize(row, 1.0, 0.0)
        result = stream[at] + normalize_back(value, normed, inverse, gain1)
        stream[at] = result
        low = result.astype(LOW)
        sums_into(split, 0, at, (value * normed, value))
        return low

    def meanwhile():
        if not plan.final:
            reduce("qkv")
        own("qkv")
        second_step("up")
        first_step("out")
        rest("up")
        early_step()

    def halfway():
        if plan.final:
            first_step("qkv")

    if plan.final:
        reduce("qkv")
    two.eager(qkv_part, to_following, meanwhile, halfway)
    if plan.joined:
        late_held[0, 0:8, :] = jnp.zeros((8, late_held.shape[2]), FULL)
        late_held[0, 0:2, :] = split[0:2, :]
        late_held[0, 2:3, :] = local[1:2, :]
        final.step()
        final.step()
    two.have_mate_own()
    two.have_other()
    if plan.joined:
        final.step()
        early_step()
    second_step("out")
    rest("out")
    if plan.joined:
        final.step()
    if plan.inside:
        last = reduces["qkv"]
        if plan.final:
            second_step("qkv")
            rest("qkv")
        else:
            last.fold_blocks(3, 2, 1, 0)
            mover.stay(last.mid, mid_out)
    two.have_mate_other()
    if plan.joined:
        final.step()
    for name in ("down", "up", "out"):
        if name in reduces:
            reduces[name].done()
    if late:
        late.done()
    if plan.inside and plan.final:
        reduces["qkv"].done()
    if plan.joined:
        final.step()
        early.step()
        totals[...] = early.value()
        last_value = final.value()
        for row in range(2):
            at = row * len(everything)
            totals[at : at + 1, :] = last_value[row : row + 1, :]
        at = tops + len(everything)
        totals[at : at + 1, :] = last_value[2:3, :]
    if not plan.inside:
        for name, (lhs, rhs) in {
            "down": (grad, hidden),
            "up": (second, pre_grad),
            "out": (attn_grad, heads),
            "qkv": (first, nat),
        }.items():
            full = Reduce(mover, (wholes[name],) * 4, None, lhs, rhs)
            full.compute(wholes[name], 0)
    mover.settle()


def gather_outputs_kernel(layers, *refs):
    count = layers * len(NAMES)
    parts, token_grads, mixed, totals = refs[:count], refs[count], refs[count + 1], refs[count + 2]
    outs, work = refs[count + 3 : count + 17], refs[count + 17 : -2]
    into, out_of = refs[-2:]
    coming, going = [], []
    pairs = [(mixed, work[4], outs[4].at[0])]
    for index in range(len(NAMES)):
        for layer in range(layers):
            pairs.append(
                (parts[index * layers + layer], work[index].at[layer], outs[index].at[layer])
            )
    for i, (source, stage, _) in enumerate(pairs):
        coming.append(pltpu.make_async_copy(source, stage, into.at[i]))
        coming[-1].start()
    outs[5][0] = token_grads[...].astype(FULL)
    for row, out in enumerate(outs[6:12]):
        out[...] = totals[row * layers : (row + 1) * layers, 0 : out.shape[1]]
    for row, out in enumerate(outs[12:14]):
        row = row + 8
        out[...] = totals[row * layers : (row + 1) * layers, 0 : out.shape[1]]
    for i, (_, stage, target) in enumerate(pairs):
        coming[i].wait()
        going.append(pltpu.make_async_copy(stage, target, out_of.at[i]))
        going[-1].start()
    for copy in going:
        copy.wait()


def gather_outputs(done, token_grads, mixed, totals, layers, widths):
    rows, width = token_grads.shape
    parts = [done[name, layer] for name in NAMES for layer in range(layers)]
    hbm, whole = pl.BlockSpec(memory_space=HBM), lambda shape: pl.BlockSpec(
        shape, lambda i: (0,) * len(shape)
    )
    shapes = [(layers,) + done[name, 0].shape for name in NAMES] + [(1, rows, width)] * 2
    types = [FULL] * 4 + [LOW, FULL]
    small = [(layers, width)] * 6 + [(layers, count) for count in widths]
    copies = len(parts) + 1
    return pl.pallas_call(
        functools.partial(gather_outputs_kernel, layers),
        grid=(1,),
        in_specs=[hbm] * len(parts) + [whole(token_grads.shape), hbm, whole(totals.shape)],
        out_specs=[hbm] * 5 + [whole(shape) for shape in shapes[5:] + small],
        out_shape=[jax.ShapeDtypeStruct(*pair) for pair in zip(shapes, types)]
        + [jax.ShapeDtypeStruct(shape, FULL) for shape in small],
        scratch_shapes=[VMEM(shape, FULL) for shape in shapes[:4]]
        + [VMEM((rows, width), LOW)]
        + [pltpu.SemaphoreType.DMA((copies,)), pltpu.SemaphoreType.DMA((copies,))],
        compiler_params=pltpu.CompilerParams(vmem_limit_bytes=60 * 2**20),
        name="gather_outputs",
    )(*parts, token_grads, mixed, totals)


class BackPlan:
    def __init__(self, layer, layers, inside):
        self.inside, self.layer = inside, layer
        self.last, self.final = layer == layers - 1, layer == 0
        self.late = inside and not self.last
        self.joined = inside and self.final
        self.others = layers - 1 if self.joined else 0


def back_layer(source, x, live, gain2, gain1, saved, late, others, plan, size, sizes, ident):
    rows, width = source.shape
    count = sizes[0]
    slope, w_down, w_up = saved[:3]
    hidden, joint, attn = slope.shape[1], saved[12].shape[1], saved[6].shape[1]
    slots, span = count * rows, rows // 4
    tile = 512 if slots % 512 == 0 else PAD
    wide = max(width, hidden, joint)
    half = width // 2
    block = half // count
    columns = {"qkv": joint, "out": attn, "up": hidden, "down": hidden}
    inputs = [(source, VMEM)] + ([] if plan.last else [(x, VMEM)])
    inputs += [(live, SMEM), (gain2, HBM), (gain1, HBM)]
    inputs += [(value, HBM) for value in saved]
    if plan.late:
        inputs.append((late, HBM))
    for pair in others[: plan.others]:
        inputs += [(value, VMEM) for value in pair]
    outputs = [((span, width), FULL, VMEM), ((rows, width), LOW, VMEM)]
    names = [name for name in NAMES if plan.inside and (name != "qkv" or plan.final)]
    outputs += [((block, columns[name]), FULL, VMEM) for name in names]
    if plan.inside and not plan.final:
        outputs.append(((half, joint), LOW, HBM))
    if plan.late:
        outputs.append(((block, joint), FULL, VMEM))
    depth = 8 * (plan.others + 1)
    if plan.joined:
        outputs.append(((depth + 8, wide), FULL, VMEM))
    else:
        outputs += [((8, wide), FULL, VMEM)] * 2
    if not plan.inside:
        outputs += [((width, columns[name]), LOW, VMEM) for name in NAMES]
    scratch = [VMEM(value.shape, value.dtype) for value in saved]
    scratch[13] = VMEM((span, width), saved[13].dtype)
    if plan.last:
        scratch.append(VMEM((rows, width), LOW))
    scratch += [
        VMEM((rows, hidden), LOW),
        VMEM((rows, width), LOW),
        VMEM((attn, rows), LOW),
        VMEM((joint, rows), LOW),
        VMEM((rows, joint), LOW),
    ]
    scratch += attend_back_buffers(size, count, rows)
    scratch += round_buffers(rows, width) + round_buffers(rows, width)
    if plan.inside:
        for name in ("down", "up", "out", "qkv"):
            scratch += reduce_buffers(half, columns[name], count)
    if plan.late:
        scratch += [VMEM((half, joint), LOW), VMEM((count - 1, block, joint), LOW)]
    scratch.append(VMEM((16, slots), LOW))
    scratch += [VMEM(value.shape, value.dtype) for value in (gain2, gain1)]
    assert 2 * (plan.others + 1) <= 8
    if plan.joined:
        scratch += [VMEM((8, wide), FULL)] * 2
        scratch += [
            VMEM((6, depth + 8, wide), FULL),
            VMEM((5, depth + 8, wide), FULL),
            VMEM((6, 8, wide), FULL),
            VMEM((5, 8, wide), FULL),
        ]
    results = run(
        functools.partial(back_kernel, plan, size, tile),
        "back_layer",
        ident,
        inputs,
        outputs,
        scratch,
        3 * (count - 1) + 2 * ROUND_COPIES + 8 * count + 10 + count,
        len(saved) + 4,
        sizes,
        58,
        6 * rows * width * (2 * hidden + attn + joint) + 10 * slots * slots * 256,
    )
    return results[:2], names, results[2:]


def shards(
    tokens,
    block_tokens,
    ln1_gain,
    ln1_bias,
    w_qkv,
    b_qv,
    w_out,
    b_out,
    ln2_gain,
    ln2_bias,
    w_up,
    b_up,
    w_down,
    b_down,
    cotangent,
):
    images, capacity, width = tokens.shape
    assert images == 1
    layers = w_qkv.shape[0]
    size = HEAD_DIM
    ctx_count = lax.axis_size("ctx")
    ctx_place = lax.axis_index("ctx")
    joint_width = w_qkv.shape[2]
    heads = joint_width // (3 * size)
    assert heads == ctx_count
    attn_width = heads * size
    hidden_width = w_up.shape[2]
    weights = {"qkv": w_qkv, "out": w_out, "up": w_up, "down": w_down}
    sizes = (ctx_count, lax.axis_size("shard"))
    inside = sizes == (4, 2)
    gathered = {}
    if not inside:
        for name, value in weights.items():
            for layer in range(layers):
                gathered[name, layer] = gather_weight(value[layer])[0]
    source, stream = tokens[0], None
    saved = []
    for layer in range(layers):
        last = layer == layers - 1
        result, following, kept = forward_layer(
            source,
            stream,
            block_tokens,
            (b_out, ln2_gain, ln2_bias, b_down, ln1_gain, ln1_bias, b_up, b_qv),
            gathered,
            weights,
            Plan(layer, last, inside),
            last,
            size,
            sizes,
            1 + layer,
        )
        before = stream if layer else source
        first = source if layer else kept[8]
        saved.append((before, first) + tuple(kept[:8]))
        source, stream = following, result
    mixed = source

    done, packs = {}, {}
    source, stream, late = cotangent[0], None, None
    for layer in reversed(range(layers)):
        before, first, qkv, head_out, lse, heads_low, middle, second, hidden, slope = saved[layer]
        plan = BackPlan(layer, layers, inside)
        whole = {name: gathered[name, layer] for name in NAMES}
        near = [slope, whole["down"], whole["up"], middle, hidden, second, whole["out"]]
        near += [heads_low, qkv, head_out, lse, first, whole["qkv"], before]
        others = [packs[key] for key in sorted(packs)]
        (stream, source), names, rest = back_layer(
            source, stream, block_tokens, ln2_gain, ln1_gain, near, late, others, plan, size, sizes, 1 + layers + layer
        )
        rest = iter(rest)
        for name in names:
            done[name, layer] = next(rest)
        if plan.inside and not plan.final:
            late = next(rest)
        if plan.late:
            done["qkv", layer + 1] = next(rest)
        if plan.joined:
            totals = next(rest)
        else:
            packs[layer] = (next(rest), next(rest))
        if not inside:
            for name in NAMES:
                value = next(rest)
                done[name, layer] = scatter_weight(
                    lambda start, count, value=value: rows_of(value, start, count).astype(FULL),
                    width,
                )
    if not inside:
        split = total_over(("tp",), jnp.stack([packs[l][0] for l in range(layers)], axis=1))
        local = jnp.stack([packs[l][1] for l in range(layers)], axis=1)
        totals = total_over(("shard", "ctx"), jnp.concatenate([split, local[:2]]))
        totals = totals.reshape(10 * layers, -1)
    pairs = b_qv.shape[1]
    outs = gather_outputs(done, source, mixed, totals, layers, (hidden_width, pairs))
    g_qkv, g_out, g_up, g_down, mixed, token_grads = outs[:6]
    g_ln1_gain, g_ln1_bias, g_ln2_gain, g_ln2_bias, g_b_out, g_b_down, g_b_up, g_b_qv = outs[6:]
    return (
        mixed,
        token_grads,
        g_ln1_gain,
        g_ln1_bias,
        g_qkv,
        g_b_qv,
        g_out,
        g_b_out,
        g_ln2_gain,
        g_ln2_bias,
        g_up,
        g_b_up,
        g_down,
        g_b_down,
    )


def solution(mesh):
    split_rows = P(None, ("shard", "ctx"), "tp")
    split_tokens = P("shard", "ctx", None)
    return jax.shard_map(
        shards,
        mesh=mesh,
        in_specs=(
            split_tokens,
            P("shard", None),
            P(),
            P(),
            split_rows,
            P(None, "tp"),
            split_rows,
            P(),
            P(),
            P(),
            split_rows,
            P(None, "tp"),
            split_rows,
            P(),
            split_tokens,
        ),
        out_specs=(
            split_tokens,
            split_tokens,
            P(),
            P(),
            split_rows,
            P(None, "tp"),
            split_rows,
            P(),
            P(),
            P(),
            split_rows,
            P(None, "tp"),
            split_rows,
            P(),
        ),
        check_vma=False,
    )
```
